32 devices in a mesh: section: 4 (over y, x), seq: 8 (over z, core).
Axes of the slice: x: 2, y: 2, z: 4, core: 2. Of those that a mesh axis runs over, the one named last changes fastest.
Arguments:
- embeds: bfloat16 [4, 1024, 768], P(None, 'seq'), may hold values from -6 to 6
- row_lengths: int32 [4, 4], replicated, may hold values from 1 to 1021, as said below
- qkv_weight: bfloat16 [2, 768, 2304], P(None, 'seq'), may hold values from -0.21875 to 0.21875
- out_weight: bfloat16 [2, 768, 768], P(None, 'seq'), may hold values from -0.21875 to 0.21875
- up_weight: bfloat16 [2, 768, 3072], P(None, 'seq'), may hold values from -0.21875 to 0.21875
- down_weight: bfloat16 [2, 3072, 768], P(None, 'seq'), may hold values from -0.109375 to 0.109375
- model_gains: bfloat16 [2, 3, 768], P(None, None, 'seq'), may hold values from 0.5 to 1.5
- model_biases: bfloat16 [2, 6, 768], P(None, None, 'seq'), may hold values from -1.796875 to 1.796875
- hidden_gains: bfloat16 [2, 3072], P(None, 'seq'), may hold values from 0.5 to 1.5
- hidden_biases: bfloat16 [2, 2, 3072], P(None, None, 'seq'), may hold values from -1.796875 to 1.796875
- cotangent: bfloat16 [4, 1024, 768], P(None, 'seq'), may hold values from -6 to 6
Outputs:
- sublayer_outputs: bfloat16 [4, 4, 1024, 768], P('section', None, 'seq')
- sublayer_grads: bfloat16 [4, 4, 1024, 768], P('section', None, 'seq')
- qkv_grad: float32 [2, 768, 2304], P(None, 'seq')
- out_grad: float32 [2, 768, 768], P(None, 'seq')
- up_grad: float32 [2, 768, 3072], P(None, 'seq')
- down_grad: float32 [2, 3072, 768], P(None, 'seq')
- model_gains_grad: float32 [2, 3, 768], P(None, None, 'seq')
- model_biases_grad: float32 [2, 6, 768], P(None, None, 'seq')
- hidden_gains_grad: float32 [2, 3072], P(None, 'seq')
- hidden_biases_grad: float32 [2, 2, 3072], P(None, None, 'seq')
- pattern_means: float32 [2, 5], replicated
The draws below stay inside these ranges and needn't reach their ends.
Inputs may be any that keep to these rules, and one draw needn't show every extreme that they name: `row_lengths`: in every micro-batch the 4 lengths sum to 1024; in one micro-batch the first row holds all but 4 - 1 of its tokens.
All inputs are finite; a program needn't handle non-finite values.
Results may differ from the reference program's by a relative error of at most 0.019.
Values may be sent and summed in bfloat16 or wider, within the bound.
A program may use at most 320 MiB of HBM per device.

```python
import jax
import jax.numpy as jnp
from jax import lax

D = 768
HEADS = 12
HEAD_DIM = 64
FF = 3072
LAYERS = 2
MICRO = 4
ROWS = 4
GROUP = 1024
N_SECTION = 4


def draw_row_lengths(key, part):
    key = jax.random.fold_in(key, 11)
    batch_keys = jax.random.split(key, MICRO + 1)

    def one_batch(batch_key):
        cut_points = jnp.sort(jax.random.permutation(batch_key, GROUP - 1)[:ROWS - 1] + 1).astype(jnp.int32)
        boundaries = jnp.concatenate([jnp.zeros((1,), jnp.int32), cut_points, jnp.full((1,), GROUP, jnp.int32)])
        return boundaries[1:] - boundaries[:-1]
    lengths = jax.vmap(one_batch)(batch_keys[:MICRO])
    spanning_batch = jax.random.randint(batch_keys[MICRO], (), 0, MICRO)
    spanning_rows = jnp.concatenate([jnp.full((1,), GROUP - ROWS + 1, jnp.int32), jnp.ones((ROWS - 1,), jnp.int32)])
    lengths = jnp.where(jnp.arange(MICRO)[:, None] == spanning_batch, spanning_rows[None, :], lengths)
    return lengths.astype(jnp.int32)


def steps_of(stream_key, extent, pieces, least, top_value):
    def one(position, shards_of):
        draws = jax.random.uniform(jax.random.fold_in(jax.random.fold_in(stream_key, 6), position), (shards_of,), jnp.float32, least / len(pieces), top_value / len(pieces))
        return jnp.repeat(jnp.exp(draws), extent[position] // shards_of).reshape((-1,) + (1,) * (len(extent) - position - 1))

    loudness = one(*pieces[0])
    for cut in pieces[1:]:
        loudness = loudness * one(*cut)
    return loudness


def bell_draw(key, shape, deviation, limit, cuts=(), kind=jnp.bfloat16):
    entries = deviation * jax.random.normal(key, shape, jnp.float32)
    if cuts:
        entries = entries * steps_of(key, shape, cuts, -0.22, 0.18)
    return jnp.clip(entries, -limit, limit).astype(kind)


def setup_inputs(seed: int = 0) -> dict:
    key_list = jax.random.split(jax.random.key(seed), 12)
    embeds = bell_draw(key_list[0], (MICRO, GROUP, D), 1.0, 6.0, ((1, 8),))
    row_lengths = draw_row_lengths(jax.random.fold_in(key_list[11], 71), 0)
    qkv_weight = bell_draw(key_list[2], (LAYERS, D, 3 * D), D ** -0.5, 0.21875, ((1, 8),))
    out_weight = bell_draw(key_list[3], (LAYERS, D, D), D ** -0.5, 0.21875, ((1, 8),))
    up_weight = bell_draw(key_list[4], (LAYERS, D, FF), D ** -0.5, 0.21875, ((1, 8),))
    down_weight = bell_draw(key_list[5], (LAYERS, FF, D), FF ** -0.5, 0.109375, ((1, 8),))
    model_gains = jnp.clip(1.0 + 0.1 * jax.random.normal(key_list[6], (LAYERS, 3, D), jnp.float32), 0.5, 1.5).astype(jnp.bfloat16)
    model_biases = bell_draw(key_list[7], (LAYERS, 6, D), 0.3, 1.796875, ((2, 8),))
    hidden_gains = jnp.clip(1.0 + 0.1 * jax.random.normal(key_list[8], (LAYERS, FF), jnp.float32), 0.5, 1.5).astype(jnp.bfloat16)
    hidden_biases = bell_draw(key_list[9], (LAYERS, 2, FF), 0.3, 1.796875, ((2, 8),))
    cotangent = bell_draw(key_list[10], (MICRO, GROUP, D), 1.0, 6.0, ((1, 8),))
    return {"embeds": embeds, "row_lengths": row_lengths, "qkv_weight": qkv_weight, "out_weight": out_weight, "up_weight": up_weight, "down_weight": down_weight, "model_gains": model_gains, "model_biases": model_biases, "hidden_gains": hidden_gains, "hidden_biases": hidden_biases, "cotangent": cotangent}


WIDTHS = (2048, 4096, 8192, 16384, 32768)
RATIOS = (1, 2, 4, 6, 12)
EPSILON = 1e-05
PRECISE = lax.Precision.HIGHEST

@jax.custom_vjp
def low(v):
    return lax.optimization_barrier(v.astype(jnp.bfloat16)).astype(jnp.float32)

@jax.custom_vjp
def low_back(v):
    return v

def low_keep(v):
    return (low(v), None)

def low_pass(kept, grad):
    return (grad,)

def back_keep(v):
    return (v, None)

def back_low(kept, grad):
    return (low(grad),)
low.defvjp(low_keep, low_pass)
low_back.defvjp(back_keep, back_low)

def norm_rows(inputs, gain_row, offset):
    center = inputs - lax.optimization_barrier(jnp.mean(inputs, -1, keepdims=True))
    spread = lax.optimization_barrier(jnp.mean(center * center, -1, keepdims=True))
    return center * lax.rsqrt(spread + EPSILON) * gain_row + offset

def place_rows(lengths, token_index):
    row_ends = jnp.cumsum(lengths)
    passed = token_index[:, None] >= row_ends[None, :]
    row_ids = lax.optimization_barrier(jnp.sum(passed.astype(jnp.int32), 1))
    offsets = token_index - lax.optimization_barrier(jnp.sum(jnp.where(passed, lengths[None, :], 0), 1))
    return (row_ids, offsets)

def query_chosen(query_pos):
    head_ids = jnp.arange(HEADS, dtype=jnp.int32)
    chosen = []
    for seg_width, seg_ratio in zip(WIDTHS, RATIOS):
        query_pick = query_pos % seg_width % seg_ratio
        chosen.append(query_pick[None, :] == (head_ids % seg_ratio)[:, None])
    return chosen

def pattern_masks(query_rows, query_pos, key_rows, key_pos):
    head_ids = jnp.arange(HEADS, dtype=jnp.int32)
    common = (query_rows[:, None] == key_rows[None, :]) & (key_pos[None, :] <= query_pos[:, None])
    allow_list = []
    for seg_width, seg_ratio in zip(WIDTHS, RATIOS):
        residue = head_ids % seg_ratio
        query_ok = (query_pos % seg_width % seg_ratio)[None, :] == residue[:, None]
        key_ok = (key_pos % seg_width % seg_ratio)[None, :] == residue[:, None]
        inside = common & ((query_pos // seg_width)[:, None] == (key_pos // seg_width)[None, :])
        allow_list.append(inside[None] & query_ok[:, :, None] & key_ok[:, None, :])
    return allow_list

def block_rows(total_rows):
    step_rows = min(total_rows, 512)
    if total_rows % step_rows != 0:
        step_rows = total_rows
    return step_rows

def attention_layer(inputs, lengths, qkv_matrix, out_matrix, norm_gains, norm_biases):
    group_rows = inputs.shape[0]
    hidden = low(norm_rows(inputs, norm_gains[0], norm_biases[0]))
    bias_row = jnp.concatenate([jnp.zeros_like(norm_biases[3]), jnp.zeros_like(norm_biases[3]), norm_biases[3]])
    projected = low(low_back(jnp.dot(hidden, qkv_matrix, precision=PRECISE) + bias_row))
    queries = projected[:, :D].reshape(group_rows, HEADS, HEAD_DIM)
    all_keys = projected[:, D:2 * D].reshape(group_rows, HEADS, HEAD_DIM)
    all_values = projected[:, 2 * D:].reshape(group_rows, HEADS, HEAD_DIM)
    key_rows, key_pos = place_rows(lengths, jnp.arange(group_rows, dtype=jnp.int32))
    step_rows = block_rows(group_rows)

    def one_block(block_start):
        query_block = lax.dynamic_slice_in_dim(queries, block_start, step_rows, 0)
        query_rows = lax.dynamic_slice_in_dim(key_rows, block_start, step_rows, 0)
        query_pos = lax.dynamic_slice_in_dim(key_pos, block_start, step_rows, 0)
        product = jnp.einsum('qhe,khe->hqk', query_block, all_keys, precision=PRECISE)
        scores = low_back(HEAD_DIM ** (-0.5) * product)
        allow_list = pattern_masks(query_rows, query_pos, key_rows, key_pos)
        chosen = query_chosen(query_pos)
        counts = allow_list[0].astype(jnp.float32)
        for allowed in allow_list[1:]:
            counts = counts + allowed.astype(jnp.float32)
        raised = jnp.exp(scores)
        weighted = counts * raised
        totals = lax.optimization_barrier(jnp.sum(weighted, -1))
        attended = jnp.einsum('hqk,khe->qhe', low(weighted), all_values, precision=PRECISE) / jnp.transpose(totals)[:, :, None]
        log_terms = []
        for allowed, pick_row in zip(allow_list, chosen):
            pattern_sum = lax.optimization_barrier(jnp.sum(jnp.where(allowed, raised, 0.0), -1))
            log_terms.append(jnp.sum(jnp.where(pick_row, jnp.log(jnp.where(pick_row, pattern_sum, 1.0)), 0.0)))
        return (attended, jnp.stack(log_terms))
    attended, log_terms = lax.map(jax.checkpoint(one_block), jnp.arange(0, group_rows, step_rows, dtype=jnp.int32))
    attended = low_back(attended.reshape(group_rows, D))
    inner_norm = low(norm_rows(attended, norm_gains[1], norm_biases[1]))
    branch = low_back(jnp.dot(inner_norm, out_matrix, precision=PRECISE) + norm_biases[4])
    return (inputs + branch, lax.optimization_barrier(jnp.sum(log_terms, 0)))

def feed_layer(inputs, up_matrix, down_matrix, norm_gains, norm_biases, hidden_gain, hidden_bias):
    hidden = low(norm_rows(inputs, norm_gains[2], norm_biases[2]))
    upward = low_back(jnp.dot(hidden, up_matrix, precision=PRECISE) + hidden_bias[0])
    inner_norm = low(norm_rows(jax.nn.gelu(upward, approximate=False), hidden_gain, hidden_bias[1]))
    branch = low_back(jnp.dot(inner_norm, down_matrix, precision=PRECISE) + norm_biases[5])
    return inputs + branch

def reference(embeds, row_lengths, qkv_weight, out_weight, up_weight, down_weight, model_gains, model_biases, hidden_gains, hidden_biases, cotangent):
    weights = tuple((stacked.astype(jnp.float32) for stacked in (qkv_weight, out_weight, up_weight, down_weight, model_gains, model_biases, hidden_gains, hidden_biases)))
    base = embeds.astype(jnp.float32)
    probes = jnp.zeros((MICRO, N_SECTION, GROUP, D), jnp.float32)

    def forward(base_in, probe_in, weight_in):

        def one_batch(items):
            stream, lengths, probe = items
            outputs = []
            terms = []
            for section_id in range(N_SECTION):
                layer_id = section_id // 2
                stream = stream + probe[section_id]
                if section_id % 2 == 0:
                    result, log_terms = attention_layer(stream, lengths, weight_in[0][layer_id], weight_in[1][layer_id], weight_in[4][layer_id], weight_in[5][layer_id])
                    terms.append(log_terms)
                else:
                    result = feed_layer(stream, weight_in[2][layer_id], weight_in[3][layer_id], weight_in[4][layer_id], weight_in[5][layer_id], weight_in[6][layer_id], weight_in[7][layer_id])
                stream = low(low_back(result))
                outputs.append(stream)
            return (stream, jnp.stack(outputs), jnp.stack(terms))
        final, outputs, terms = lax.map(one_batch, (base_in, row_lengths, probe_in))
        return (final, (outputs, terms))
    final, pullback, aux = jax.vjp(forward, base, probes, weights, has_aux=True)
    outputs, terms = aux
    unused_base, probe_grads, weight_grads = pullback(cotangent.astype(jnp.float32))

    def positions_of(lengths):
        return place_rows(lengths, jnp.arange(GROUP, dtype=jnp.int32))[1]
    all_pos = jax.vmap(positions_of)(row_lengths).reshape(-1)
    counts = jnp.stack([jnp.sum(pick_row.astype(jnp.float32)) for pick_row in query_chosen(all_pos)])
    pattern_means = lax.optimization_barrier(jnp.sum(terms, 0)) / counts[None, :]
    sublayer_outputs = jnp.transpose(outputs, (1, 0, 2, 3)).astype(jnp.bfloat16)
    sublayer_grads = jnp.transpose(probe_grads, (1, 0, 2, 3)).astype(jnp.bfloat16)
    return (sublayer_outputs, sublayer_grads, weight_grads[0], weight_grads[1], weight_grads[2], weight_grads[3], weight_grads[4], weight_grads[5], weight_grads[6], weight_grads[7], pattern_means)
```

```python
import jax
import jax.numpy as jnp
from jax import lax
from jax.experimental import pallas as pl
from jax.experimental.pallas import tpu as pltpu
from jax.sharding import PartitionSpec as P

D = 768
HEADS = 12
HEAD_DIM = 64
FF = 3072


WIDTHS = (2048, 4096, 8192, 16384, 32768)
RATIOS = (1, 2, 4, 6, 12)
EPSILON = 1e-05


def passed_along(value, axis, steps):
    count = lax.axis_size(axis)
    initial, last = (max(0, -steps), min(count, count - steps))
    return lax.ppermute(value, axis, [(source, source + steps) for source in range(initial, last)])


def norm_rows(inputs, gain_row, offset):
    center = inputs - jnp.mean(inputs, -1, keepdims=True)
    spread = jnp.mean(center * center, -1, keepdims=True)
    return center * lax.rsqrt(spread + EPSILON) * gain_row + offset


def place_rows(lengths, token_index):
    row_ends = jnp.cumsum(lengths)
    passed = token_index[:, None] >= row_ends[None, :]
    row_ids = jnp.sum(passed.astype(jnp.int32), 1)
    offsets = token_index - jnp.sum(jnp.where(passed, lengths[None, :], 0), 1)
    return (row_ids, offsets)


def query_chosen(query_pos):
    head_ids = jnp.arange(HEADS, dtype=jnp.int32)
    chosen = []
    for seg_width, seg_ratio in zip(WIDTHS, RATIOS):
        query_pick = query_pos % seg_width % seg_ratio
        chosen.append(query_pick[None, :] == (head_ids % seg_ratio)[:, None])
    return chosen


def pattern_allow(query_rows, query_pos, key_rows, key_pos):
    widths = jnp.array(WIDTHS, jnp.int32)[:, None]
    ratios = jnp.array(RATIOS, jnp.int32)[:, None]
    residue = jnp.arange(HEADS, dtype=jnp.int32)[None, :] % ratios
    query_mod = query_pos[None, :] % widths % ratios
    key_mod = key_pos[None, :] % widths % ratios
    query_ok = query_mod[:, None, :] == residue[:, :, None]
    key_ok = key_mod[:, None, :] == residue[:, :, None]
    common = (query_rows[:, None] == key_rows[None, :]) & (key_pos[None, :] <= query_pos[:, None])
    inside = common[None] & (
        (query_pos[None, :] // widths)[:, :, None] == (key_pos[None, :] // widths)[:, None, :]
    )
    return inside[:, None] & query_ok[:, :, :, None] & key_ok[:, :, None, :]


def block_rows(total_rows):
    step_rows = min(total_rows, 512)
    return step_rows


def split_heads(matrix):
    return matrix.reshape(matrix.shape[0], HEADS, HEAD_DIM)


def pair_terms(query_block, keys_block, query_rows, query_pos, key_rows, key_pos):
    scores = jnp.einsum(
        "qhe,khe->hqk", query_block, keys_block, preferred_element_type=jnp.float32
    ) * HEAD_DIM ** (-0.5)
    allowed = pattern_allow(query_rows, query_pos, key_rows, key_pos)
    counts = jnp.sum(allowed.astype(jnp.float32), 0)
    raised = jnp.exp(scores)
    return (raised, counts * raised, allowed)


def project_tokens(inputs, qkv_matrix, norm_gains, norm_biases):
    hidden = norm_rows(inputs, norm_gains[0], norm_biases[0]).astype(jnp.bfloat16)
    bias_row = jnp.concatenate(
        [jnp.zeros_like(norm_biases[3]), jnp.zeros_like(norm_biases[3]), norm_biases[3]]
    )
    projected = (jnp.dot(hidden, qkv_matrix, preferred_element_type=jnp.float32) + bias_row).astype(
        jnp.bfloat16
    )
    return (hidden, projected)


def attention_forward(section_in, projected, whole_keys, lengths, params, seq_index):
    out_matrix, norm_gains, norm_biases = (params[1], params[4], params[5])
    tok_rows = section_in.shape[0]
    inputs = section_in.astype(jnp.float32)
    queries = split_heads(projected[:, :D])
    query_rows, query_pos = place_rows(
        lengths, seq_index * tok_rows + jnp.arange(tok_rows, dtype=jnp.int32)
    )
    group_rows = whole_keys.shape[0]
    step_rows = block_rows(group_rows)

    def one_block(running, block_start):
        totals, pattern_sums, accumulated = running
        kv_block = lax.dynamic_slice_in_dim(whole_keys, block_start, step_rows, 0)
        key_rows, key_pos = place_rows(
            lengths, block_start + jnp.arange(step_rows, dtype=jnp.int32)
        )
        raised, weighted, allowed = pair_terms(
            queries, split_heads(kv_block[:, :D]), query_rows, query_pos, key_rows, key_pos
        )
        totals = totals + jnp.sum(weighted, -1)
        pattern_sums = pattern_sums + jnp.sum(jnp.where(allowed, raised[None], 0.0), -1)
        accumulated = accumulated + jnp.einsum(
            "hqk,khe->hqe",
            weighted.astype(jnp.bfloat16),
            split_heads(kv_block[:, D:]),
            preferred_element_type=jnp.float32,
        )
        return ((totals, pattern_sums, accumulated), None)

    start_sums = (
        jnp.zeros((HEADS, tok_rows), jnp.float32),
        jnp.zeros((len(WIDTHS), HEADS, tok_rows), jnp.float32),
        jnp.zeros((HEADS, tok_rows, HEAD_DIM), jnp.float32),
    )
    folded, unused = lax.scan(
        one_block, start_sums, jnp.arange(0, group_rows, step_rows, dtype=jnp.int32)
    )
    totals, pattern_sums, accumulated = folded
    attended = jnp.transpose(accumulated / totals[:, :, None], (1, 0, 2)).reshape(tok_rows, D)
    inner_norm = norm_rows(attended, norm_gains[1], norm_biases[1]).astype(jnp.bfloat16)
    branch = jnp.dot(inner_norm, out_matrix, preferred_element_type=jnp.float32) + norm_biases[4]
    section_out = (inputs + branch).astype(jnp.bfloat16)
    chosen = query_chosen(query_pos)
    log_terms = jnp.stack(
        [
            jnp.sum(
                jnp.where(pick_row, jnp.log(jnp.where(pick_row, pattern_sums[number], 1.0)), 0.0)
            )
            for number, pick_row in enumerate(chosen)
        ]
    )
    pick_counts = jnp.stack([jnp.sum(pick_row.astype(jnp.float32)) for pick_row in chosen])
    return (section_out, attended, totals, log_terms, pick_counts)


def feed_forward(section_in, params):
    up_matrix, down_matrix, norm_gains, norm_biases, hidden_gain, hidden_bias = (
        params[2],
        params[3],
        params[4],
        params[5],
        params[6],
        params[7],
    )
    tok_rows = section_in.shape[0]
    inputs = section_in.astype(jnp.float32)
    hidden = norm_rows(inputs, norm_gains[2], norm_biases[2]).astype(jnp.bfloat16)
    upward = jnp.dot(hidden, up_matrix, preferred_element_type=jnp.float32) + hidden_bias[0]
    inner_norm = norm_rows(
        jax.nn.gelu(upward, approximate=False), hidden_gain, hidden_bias[1]
    ).astype(jnp.bfloat16)
    branch = jnp.dot(inner_norm, down_matrix, preferred_element_type=jnp.float32) + norm_biases[5]
    section_out = (inputs + branch).astype(jnp.bfloat16)
    empty_terms = jnp.zeros((len(WIDTHS),), jnp.float32)
    return (
        section_out,
        jnp.zeros((tok_rows, D), jnp.float32),
        jnp.zeros((HEADS, tok_rows), jnp.float32),
        empty_terms,
        empty_terms,
    )


def attention_middle(
    section_in, grad_out, attended, totals, lengths, all_keys, projected, params, seq_index
):
    out_matrix, norm_gains, norm_biases = (params[1], params[4], params[5])
    scale_factor = HEAD_DIM ** (-0.5)
    tok_rows = section_in.shape[0]
    queries = split_heads(projected[:, :D])
    query_rows, query_pos = place_rows(
        lengths, seq_index * tok_rows + jnp.arange(tok_rows, dtype=jnp.int32)
    )
    inner_norm = norm_rows(attended, norm_gains[1], norm_biases[1]).astype(jnp.bfloat16)
    out_step = jnp.einsum("td,tf->df", inner_norm, grad_out, preferred_element_type=jnp.float32)
    inner_grad = jnp.einsum("tf,df->td", grad_out, out_matrix, preferred_element_type=jnp.float32)
    unused, inner_back = jax.vjp(norm_rows, attended, norm_gains[1], norm_biases[1])
    attended_grad, inner_gain_grad, inner_bias_grad = inner_back(inner_grad)
    low_attended = attended_grad.astype(jnp.bfloat16)
    head_grad = split_heads(low_attended)
    row_dots = jnp.einsum("qhe,qhe->hq", head_grad.astype(jnp.float32), split_heads(attended))
    scaled_grad = head_grad.astype(jnp.float32) / jnp.transpose(totals)[:, :, None]
    group_rows = all_keys.shape[0]
    step_rows = block_rows(group_rows)

    def grad_block(query_grad, block_start):
        kv_block = lax.dynamic_slice_in_dim(all_keys, block_start, step_rows, 0)
        keys_block = split_heads(kv_block[:, :D])
        values_block = split_heads(kv_block[:, D:])
        key_rows, key_pos = place_rows(
            lengths, block_start + jnp.arange(step_rows, dtype=jnp.int32)
        )
        raised, weighted, allowed = pair_terms(
            queries, keys_block, query_rows, query_pos, key_rows, key_pos
        )
        prob_grad = jnp.einsum(
            "qhe,khe->hqk", head_grad, values_block, preferred_element_type=jnp.float32
        )
        score_grad = (weighted / totals[:, :, None] * (prob_grad - row_dots[:, :, None])).astype(
            jnp.bfloat16
        )
        query_grad = (
            query_grad
            + jnp.einsum("hqk,khe->qhe", score_grad, keys_block, preferred_element_type=jnp.float32)
            * scale_factor
        )
        key_grad = (
            jnp.einsum("hqk,qhe->khe", score_grad, queries, preferred_element_type=jnp.float32)
            * scale_factor
        )
        value_grad = jnp.einsum(
            "hqk,qhe->khe",
            weighted.astype(jnp.bfloat16),
            scaled_grad,
            preferred_element_type=jnp.float32,
        )
        block_grad = jnp.concatenate(
            [key_grad.reshape(step_rows, D), value_grad.reshape(step_rows, D)], 1
        )
        return (query_grad, block_grad)

    query_grad, block_grads = lax.scan(
        grad_block,
        jnp.zeros((tok_rows, HEADS, HEAD_DIM), jnp.float32),
        jnp.arange(0, group_rows, step_rows, dtype=jnp.int32),
    )
    block_grads = block_grads.reshape(group_rows, 2 * D)
    return (
        query_grad.reshape(tok_rows, D),
        low_attended,
        row_dots,
        block_grads,
        out_step,
        inner_gain_grad,
        inner_bias_grad,
    )


def attention_finish(section_in, grad_out, middle, extra, params, grad_sums):
    qkv_matrix, norm_gains, norm_biases = (params[0], params[4], params[5])
    inputs = section_in.astype(jnp.float32)
    grad_float = grad_out.astype(jnp.float32)
    hidden = norm_rows(inputs, norm_gains[0], norm_biases[0]).astype(jnp.bfloat16)
    query_grad, low_attended, row_dots, block_grads, out_step, inner_gain_grad, inner_bias_grad = (
        middle
    )
    own_grads = extra[0]
    proj_grad = jnp.concatenate([query_grad, own_grads], 1).astype(jnp.bfloat16)
    qkv_step = jnp.einsum("td,tf->df", hidden, proj_grad, preferred_element_type=jnp.float32)
    value_bias_sums = jnp.sum(proj_grad[:, 2 * D :].astype(jnp.float32), 0)
    hidden_grad = jnp.einsum("tf,df->td", proj_grad, qkv_matrix, preferred_element_type=jnp.float32)
    unused_first, first_back = jax.vjp(norm_rows, inputs, norm_gains[0], norm_biases[0])
    input_grad, first_gain_grad, first_bias_grad = first_back(hidden_grad)
    qkv_sum, out_sum, up_sum, down_sum, gain_sum, bias_sum, hgain_sum, hbias_sum = grad_sums
    gain_sum = gain_sum.at[0].add(first_gain_grad).at[1].add(inner_gain_grad)
    bias_sum = (
        bias_sum.at[0]
        .add(first_bias_grad)
        .at[1]
        .add(inner_bias_grad)
        .at[3]
        .add(value_bias_sums)
        .at[4]
        .add(jnp.sum(grad_float, 0))
    )
    return (
        grad_float + input_grad,
        (
            qkv_sum + qkv_step,
            out_sum + out_step,
            up_sum,
            down_sum,
            gain_sum,
            bias_sum,
            hgain_sum,
            hbias_sum,
        ),
    )


def feed_backward(section_in, grad_out, params, grad_sums):
    up_matrix, down_matrix, norm_gains, norm_biases, hidden_gain, hidden_bias = (
        params[2],
        params[3],
        params[4],
        params[5],
        params[6],
        params[7],
    )
    inputs = section_in.astype(jnp.float32)
    grad_float = grad_out.astype(jnp.float32)
    hidden = norm_rows(inputs, norm_gains[2], norm_biases[2]).astype(jnp.bfloat16)
    upward = jnp.dot(hidden, up_matrix, preferred_element_type=jnp.float32) + hidden_bias[0]

    def inner_rows(upward_in, gain_row, bias_row):
        return norm_rows(jax.nn.gelu(upward_in, approximate=False), gain_row, bias_row)

    inner_value, inner_back = jax.vjp(inner_rows, upward, hidden_gain, hidden_bias[1])
    inner_norm = inner_value.astype(jnp.bfloat16)
    down_step = jnp.einsum("tf,td->fd", inner_norm, grad_out, preferred_element_type=jnp.float32)
    inner_grad = jnp.einsum("td,fd->tf", grad_out, down_matrix, preferred_element_type=jnp.float32)
    upward_grad, hgain_step, hbias_step = inner_back(inner_grad)
    low_upward = upward_grad.astype(jnp.bfloat16)
    up_step = jnp.einsum("td,tf->df", hidden, low_upward, preferred_element_type=jnp.float32)
    hidden_grad = jnp.einsum("tf,df->td", low_upward, up_matrix, preferred_element_type=jnp.float32)
    unused, first_back = jax.vjp(norm_rows, inputs, norm_gains[2], norm_biases[2])
    input_grad, first_gain_grad, first_bias_grad = first_back(hidden_grad)
    qkv_sum, out_sum, up_sum, down_sum, gain_sum, bias_sum, hgain_sum, hbias_sum = grad_sums
    gain_sum = gain_sum.at[2].add(first_gain_grad)
    bias_sum = bias_sum.at[2].add(first_bias_grad).at[5].add(jnp.sum(grad_float, 0))
    hbias_sum = (
        hbias_sum.at[0].add(jnp.sum(low_upward.astype(jnp.float32), 0)).at[1].add(hbias_step)
    )
    return (
        grad_float + input_grad,
        (
            qkv_sum,
            out_sum,
            up_sum + up_step,
            down_sum + down_step,
            gain_sum,
            bias_sum,
            hgain_sum + hgain_step,
            hbias_sum,
        ),
    )


def keep_slot(store, fresh, slot_id, in_range):
    previous = lax.dynamic_index_in_dim(store, slot_id, 0, False)
    return lax.dynamic_update_index_in_dim(store, jnp.where(in_range, fresh, previous), slot_id, 0)


def body(
    embeds,
    row_lengths,
    qkv_weight,
    out_weight,
    up_weight,
    down_weight,
    model_gains,
    model_biases,
    hidden_gains,
    hidden_biases,
    cotangent,
):
    section_id = lax.axis_index("section")
    seq_index = lax.axis_index("seq")
    section_count = lax.axis_size("section")
    micro_count = embeds.shape[0]
    tok_rows = embeds.shape[1]
    group_rows = tok_rows * lax.axis_size("seq")
    layer_id = section_id // 2
    attends = section_id % 2 == 0
    bias_count = model_biases.shape[1]

    def pick_layer(stacked):
        return lax.dynamic_index_in_dim(stacked, layer_id, 0, False)

    gathered = (
        lax.all_gather(pick_layer(qkv_weight), "seq", axis=0, tiled=True),
        lax.all_gather(pick_layer(out_weight), "seq", axis=0, tiled=True),
        lax.all_gather(pick_layer(up_weight), "seq", axis=0, tiled=True),
        lax.all_gather(pick_layer(down_weight), "seq", axis=0, tiled=True),
        lax.all_gather(pick_layer(model_gains), "seq", axis=1, tiled=True),
        lax.all_gather(pick_layer(model_biases), "seq", axis=1, tiled=True),
        lax.all_gather(pick_layer(hidden_gains), "seq", axis=0, tiled=True),
        lax.all_gather(pick_layer(hidden_biases), "seq", axis=1, tiled=True),
    )
    params = tuple(gathered[:4]) + tuple((vector.astype(jnp.float32) for vector in gathered[4:]))
    whole_shape = (0,)

    def make_projected(section_in):
        return project_tokens(section_in.astype(jnp.float32), params[0], params[4], params[5])[1]

    def skip_projected(section_in):
        return jnp.zeros((tok_rows, 3 * D), jnp.bfloat16)

    def run_attention(section_in, projected, whole_keys, lengths):
        return attention_forward(section_in, projected, whole_keys, lengths, params, seq_index)

    def run_feed(section_in, projected, whole_keys, lengths):
        return feed_forward(section_in, params)

    def forward_tick(running, tick_id):
        (
            incoming,
            kept_inputs,
            kept_attended,
            kept_totals,
            kept_whole,
            outputs,
            log_sums,
            pick_sums,
        ) = running
        micro_id = tick_id - section_id
        in_range = (micro_id >= 0) & (micro_id < micro_count)
        slot_id = jnp.clip(micro_id, 0, micro_count - 1)
        lengths = lax.dynamic_index_in_dim(row_lengths, slot_id, 0, False)
        section_in = jnp.where(
            section_id == 0, lax.dynamic_index_in_dim(embeds, slot_id, 0, False), incoming
        )
        projected = lax.cond(attends, make_projected, skip_projected, section_in)
        whole_keys = lax.all_gather(projected[:, D:], "seq", axis=0, tiled=True)
        section_out, attended, totals, log_terms, pick_counts = lax.cond(
            attends, run_attention, run_feed, section_in, projected, whole_keys, lengths
        )
        kept_inputs = keep_slot(kept_inputs, section_in, slot_id, in_range)
        kept_attended = keep_slot(kept_attended, attended, slot_id, in_range)
        kept_totals = keep_slot(kept_totals, totals, slot_id, in_range)
        outputs = keep_slot(outputs, section_out, slot_id, in_range)
        log_sums = log_sums + jnp.where(in_range, log_terms, 0.0)
        pick_sums = pick_sums + jnp.where(in_range, pick_counts, 0.0)
        incoming = passed_along(section_out, "section", 1)
        return (
            (
                incoming,
                kept_inputs,
                kept_attended,
                kept_totals,
                kept_whole,
                outputs,
                log_sums,
                pick_sums,
            ),
            None,
        )

    forward_start = (
        jnp.zeros((tok_rows, D), jnp.bfloat16),
        jnp.zeros((micro_count, tok_rows, D), jnp.bfloat16),
        jnp.zeros((micro_count, tok_rows, D), jnp.float32),
        jnp.zeros((micro_count, HEADS, tok_rows), jnp.float32),
        jnp.zeros((micro_count,) + whole_shape, jnp.bfloat16),
        jnp.zeros((micro_count, tok_rows, D), jnp.bfloat16),
        jnp.zeros((len(WIDTHS),), jnp.float32),
        jnp.zeros((len(WIDTHS),), jnp.float32),
    )
    ticks = jnp.arange(micro_count + section_count - 1, dtype=jnp.int32)
    forward_end, unused = lax.scan(forward_tick, forward_start, ticks)
    unused_in, kept_inputs, kept_attended, kept_totals, kept_whole, outputs, log_sums, pick_sums = (
        forward_end
    )
    block_shape = (group_rows, 2 * D)

    def middle_attention(section_in, grad_out, attended, totals, lengths, all_keys, projected):
        return attention_middle(
            section_in, grad_out, attended, totals, lengths, all_keys, projected, params, seq_index
        )

    def middle_feed(section_in, grad_out, attended, totals, lengths, all_keys, projected):
        return (
            jnp.zeros((tok_rows, D), jnp.float32),
            jnp.zeros((tok_rows, D), jnp.bfloat16),
            jnp.zeros((HEADS, tok_rows), jnp.float32),
            jnp.zeros(block_shape, jnp.float32),
            jnp.zeros((D, D), jnp.float32),
            jnp.zeros((D,), jnp.float32),
            jnp.zeros((D,), jnp.float32),
        )

    def finish_attention(section_in, grad_out, projected, middle, extra, lengths, grad_sums):
        return attention_finish(section_in, grad_out, middle, extra, params, grad_sums)

    def finish_feed(section_in, grad_out, projected, middle, extra, lengths, grad_sums):
        return feed_backward(section_in, grad_out, params, grad_sums)

    def backward_tick(running, tick_id):
        incoming, grad_sums, input_grads = running
        micro_id = micro_count - 1 - tick_id + (section_count - 1 - section_id)
        in_range = (micro_id >= 0) & (micro_id < micro_count)
        slot_id = jnp.clip(micro_id, 0, micro_count - 1)
        from_next = jnp.where(
            section_id == section_count - 1,
            lax.dynamic_index_in_dim(cotangent, slot_id, 0, False),
            incoming,
        )
        grad_out = jnp.where(in_range, from_next, jnp.zeros_like(from_next))
        section_in = lax.dynamic_index_in_dim(kept_inputs, slot_id, 0, False)
        attended = lax.dynamic_index_in_dim(kept_attended, slot_id, 0, False)
        totals = lax.dynamic_index_in_dim(kept_totals, slot_id, 0, False)
        lengths = lax.dynamic_index_in_dim(row_lengths, slot_id, 0, False)
        projected = lax.cond(attends, make_projected, skip_projected, section_in)
        all_keys = lax.all_gather(projected[:, D:], "seq", axis=0, tiled=True)
        middle = lax.cond(
            attends,
            middle_attention,
            middle_feed,
            section_in,
            grad_out,
            attended,
            totals,
            lengths,
            all_keys,
            projected,
        )
        extra = (lax.psum_scatter(middle[3], "seq", scatter_dimension=0, tiled=True),)
        section_grad, grad_sums = lax.cond(
            attends,
            finish_attention,
            finish_feed,
            section_in,
            grad_out,
            projected,
            middle,
            extra,
            lengths,
            grad_sums,
        )
        low_grad = section_grad.astype(jnp.bfloat16)
        input_grads = keep_slot(input_grads, low_grad, slot_id, in_range)
        incoming = passed_along(low_grad, "section", -1)
        return ((incoming, grad_sums, input_grads), None)

    grad_start = (
        jnp.zeros((D, 3 * D), jnp.float32),
        jnp.zeros((D, D), jnp.float32),
        jnp.zeros((D, FF), jnp.float32),
        jnp.zeros((FF, D), jnp.float32),
        jnp.zeros((3, D), jnp.float32),
        jnp.zeros((bias_count, D), jnp.float32),
        jnp.zeros((FF,), jnp.float32),
        jnp.zeros((2, FF), jnp.float32),
    )
    backward_start = (
        jnp.zeros((tok_rows, D), jnp.bfloat16),
        grad_start,
        jnp.zeros((micro_count, tok_rows, D), jnp.bfloat16),
    )
    backward_end, unused_back = lax.scan(backward_tick, backward_start, ticks)
    unused_grad, grad_sums, input_grads = backward_end
    shards = (
        lax.psum_scatter(grad_sums[0], "seq", scatter_dimension=0, tiled=True),
        lax.psum_scatter(grad_sums[1], "seq", scatter_dimension=0, tiled=True),
        lax.psum_scatter(grad_sums[2], "seq", scatter_dimension=0, tiled=True),
        lax.psum_scatter(grad_sums[3], "seq", scatter_dimension=0, tiled=True),
        lax.psum_scatter(grad_sums[4], "seq", scatter_dimension=1, tiled=True),
        lax.psum_scatter(grad_sums[5], "seq", scatter_dimension=1, tiled=True),
        lax.psum_scatter(grad_sums[6], "seq", scatter_dimension=0, tiled=True),
        lax.psum_scatter(grad_sums[7], "seq", scatter_dimension=1, tiled=True),
    )
    sources = (
        qkv_weight,
        out_weight,
        up_weight,
        down_weight,
        model_gains,
        model_biases,
        hidden_gains,
        hidden_biases,
    )
    placed = tuple(
        (
            lax.dynamic_update_index_in_dim(
                jnp.zeros(source.shape, jnp.float32), shard, layer_id, 0
            )
            for shard, source in zip(shards, sources)
        )
    )
    summed = (
        lax.psum(placed[0].astype(jnp.bfloat16), "section").astype(jnp.float32),
        lax.psum(placed[1].astype(jnp.bfloat16), "section").astype(jnp.float32),
        lax.psum(placed[2].astype(jnp.bfloat16), "section").astype(jnp.float32),
        lax.psum(placed[3].astype(jnp.bfloat16), "section").astype(jnp.float32),
        lax.psum(placed[4].astype(jnp.bfloat16), "section").astype(jnp.float32),
        lax.psum(placed[5].astype(jnp.bfloat16), "section").astype(jnp.float32),
        lax.psum(placed[6].astype(jnp.bfloat16), "section").astype(jnp.float32),
        lax.psum(placed[7].astype(jnp.bfloat16), "section").astype(jnp.float32),
    )
    layer_count = qkv_weight.shape[0]
    layer_terms = lax.dynamic_update_index_in_dim(
        jnp.zeros((layer_count, len(WIDTHS)), jnp.float32), log_sums, layer_id, 0
    )
    layer_picks = lax.dynamic_update_index_in_dim(
        jnp.zeros((layer_count, len(WIDTHS)), jnp.float32), pick_sums, layer_id, 0
    )
    log_totals, pick_totals = lax.psum((layer_terms, layer_picks), ("section", "seq"))
    pattern_means = log_totals / pick_totals
    return (
        outputs[None],
        input_grads[None],
        summed[0],
        summed[1],
        summed[2],
        summed[3],
        summed[4],
        summed[5],
        summed[6],
        summed[7],
        pattern_means,
    )


BF16 = jnp.bfloat16
F32 = jnp.float32
PAIRS = HEADS // 2
OWNERS = (0, 2, 3, 4, 5, 6)
TOKENS = 128
PAIR_LANES = 128
QUERY_STEP = 256
MODEL_ROWS = 9
VEC_ROWS = 16
VMEM_BYTES = 60 * 1024 * 1024
SCALE = HEAD_DIM ** (-0.5)


def mul(left, right):
    return lax.dot_general(left, right, (((1,), (0,)), ((), ())), preferred_element_type=F32)


def mul_nt(left, right):
    return lax.dot_general(left, right, (((1,), (1,)), ((), ())), preferred_element_type=F32)


def mul_tn(left, right):
    return lax.dot_general(left, right, (((0,), (0,)), ((), ())), preferred_element_type=F32)


def standardize(values):
    center = values - jnp.mean(values, -1, keepdims=True)
    rstd = lax.rsqrt(jnp.mean(center * center, -1, keepdims=True) + EPSILON)
    return (center * rstd, rstd)


def norm_back(unit, rstd, unit_grad):
    first = jnp.mean(unit_grad, -1, keepdims=True)
    second = jnp.mean(unit_grad * unit, -1, keepdims=True)
    return rstd * (unit_grad - first - unit * second)


def remote(source, target, send_sem, recv_sem, axis, peer):
    return pltpu.make_async_remote_copy(
        src_ref=source,
        dst_ref=target,
        send_sem=send_sem,
        recv_sem=recv_sem,
        device_id={axis: peer},
        device_id_type=pl.DeviceIdType.MESH,
    )


def greet(axis, peers):
    barrier = pltpu.get_barrier_semaphore()
    for peer in peers:
        pl.semaphore_signal(
            barrier, inc=1, device_id={axis: peer}, device_id_type=pl.DeviceIdType.MESH
        )
    pl.semaphore_wait(barrier, len(peers))


def seq_peers(me, count):
    return [lax.rem(me + step, count) for step in range(1, count)]


def plane_peers(me):
    return [
        me,
        me + 1 - 2 * lax.rem(me, 2),
        lax.rem(me + 2, 4),
        3 - me,
    ]


def rows_of(block, size=TOKENS):
    return pl.ds(pl.multiple_of(block * size, size), size)


def attention_forward_kernel(
    x_ref,
    w_ref,
    vec_ref,
    u_ref,
    out_ref,
    qkv_ref,
    att_ref,
    pair_att_ref,
    pair_total_ref,
    log_ref,
    send,
    att_send,
    att_recv,
    send_sem,
    recv_sem,
    att_send_sem,
    att_recv_sem,
):
    me = lax.axis_index("seq")
    count = 8
    greet("seq", seq_peers(me, count))
    inputs = x_ref[...].astype(F32)
    unit, unused = standardize(inputs)
    hidden = (unit * vec_ref[0:1, :] + vec_ref[3:4, :]).astype(BF16)
    for block in range(3):
        part = mul(hidden, w_ref[:, block * D : (block + 1) * D])
        if block == 2:
            part = part + vec_ref[6:7, :]
        part = part.astype(BF16)
        for pair in range(PAIRS):
            send[pair, :, block * PAIR_LANES : (block + 1) * PAIR_LANES] = part[
                :, pair * PAIR_LANES : (pair + 1) * PAIR_LANES
            ]

    def out_copy(pair):
        return remote(
            send.at[pair],
            qkv_ref.at[rows_of(me)],
            send_sem.at[pair],
            recv_sem.at[me],
            "seq",
            OWNERS[pair],
        )

    for pair, owner in enumerate(OWNERS):

        @pl.when(me != owner)
        def _():
            out_copy(pair).start()

        @pl.when(me == owner)
        def _():
            qkv_ref[rows_of(me), :] = send[pair]

    is_owner = (me != 1) & (me != 7)
    my_pair = jnp.where(me == 0, 0, me - 1)
    my_pair = jnp.where(my_pair > PAIRS - 1, PAIRS - 1, my_pair)
    log_ref[...] = jnp.zeros_like(log_ref)

    def back_copy(target):
        return remote(
            att_send.at[pl.ds(target * TOKENS, TOKENS)],
            att_recv.at[my_pair],
            att_send_sem.at[target],
            att_recv_sem.at[my_pair],
            "seq",
            target,
        )

    @pl.when(is_owner)
    def _():
        lane = lax.broadcasted_iota(jnp.int32, (QUERY_STEP, PAIR_LANES), 1)
        first_half = lane < HEAD_DIM
        for step in range(count * TOKENS // QUERY_STEP):
            for source in (2 * step, 2 * step + 1):

                @pl.when(me != source)
                def _():
                    remote(
                        send.at[0],
                        qkv_ref.at[pl.ds(source * TOKENS, TOKENS)],
                        send_sem.at[0],
                        recv_sem.at[source],
                        "seq",
                        source,
                    ).wait_recv()

            start = step * QUERY_STEP
            keys_end = start + QUERY_STEP
            rows = slice(start, keys_end)
            query = qkv_ref[rows, 0:PAIR_LANES] * jnp.asarray(SCALE, BF16)
            keys = qkv_ref[0:keys_end, PAIR_LANES : 2 * PAIR_LANES]
            values = qkv_ref[0:keys_end, 2 * PAIR_LANES : 3 * PAIR_LANES]
            causal = lax.broadcasted_iota(jnp.int32, (QUERY_STEP, keys_end), 1) <= (
                start + lax.broadcasted_iota(jnp.int32, (QUERY_STEP, keys_end), 0)
            )
            sums = []
            totals = []
            logs = jnp.zeros((1, PAIR_LANES), F32)
            for head in range(2):
                mine = first_half if head == 0 else ~first_half
                own_query = jnp.where(mine, query, jnp.zeros_like(query))
                scores = mul_nt(own_query, keys)
                raised = jnp.where(causal, jnp.exp(scores), 0.0)
                pick_query = u_ref[head, rows, :]
                pick_keys = u_ref[head, 0:keys_end, :]
                counts = mul_nt(pick_query, pick_keys)
                weighted = (raised * counts).astype(BF16)
                sums.append(mul(weighted, values))
                pattern = mul(raised.astype(BF16), pick_keys)
                picked = pick_query.astype(F32)
                totals.append(jnp.sum(pattern * picked, -1, keepdims=True))
                chosen = picked > 0.5
                logs = logs + jnp.sum(
                    jnp.where(chosen, jnp.log(jnp.where(chosen, pattern, 1.0)), 0.0),
                    0,
                    keepdims=True,
                )
            log_ref[0:1, :] += logs
            total = jnp.where(first_half, totals[0], totals[1])
            attended = jnp.where(first_half, sums[0], sums[1]) / total
            pair_att_ref[rows, :] = attended
            pair_total_ref[rows, :] = total
            att_send[rows, :] = attended.astype(BF16)
            for target in (2 * step, 2 * step + 1):

                @pl.when(me != target)
                def _():
                    back_copy(target).start()

                @pl.when(me == target)
                def _():
                    att_recv[my_pair] = att_send[target * TOKENS : (target + 1) * TOKENS, :]

    for pair, owner in enumerate(OWNERS):

        @pl.when(me != owner)
        def _():
            remote(
                att_send.at[pl.ds(0, TOKENS)],
                att_recv.at[pair],
                att_send_sem.at[0],
                att_recv_sem.at[pair],
                "seq",
                owner,
            ).wait_recv()

        att_ref[:, pair * PAIR_LANES : (pair + 1) * PAIR_LANES] = att_recv[pair]
    inner_unit, unused = standardize(att_ref[...].astype(F32))
    inner = (inner_unit * vec_ref[1:2, :] + vec_ref[4:5, :]).astype(BF16)
    branch = mul(inner, w_ref[:, 3 * D : 4 * D]) + vec_ref[7:8, :]
    out_ref[...] = (inputs + branch).astype(BF16)
    for pair, owner in enumerate(OWNERS):

        @pl.when(me != owner)
        def _():
            out_copy(pair).wait_send()

    @pl.when(is_owner)
    def _():
        for target in range(count):

            @pl.when(me != target)
            def _():
                back_copy(target).wait_send()


def attention_backward_kernel(
    g_ref,
    x_ref,
    att_ref,
    w_ref,
    vec_ref,
    u_ref,
    qkv_ref,
    pair_att_ref,
    pair_total_ref,
    gx_ref,
    grad_ref,
    do_send,
    do_recv,
    key_sum,
    value_sum,
    d_send,
    d_recv,
    d_proj,
    vec_rows,
    send_sem,
    recv_sem,
    back_send_sem,
    back_recv_sem,
):
    me = lax.axis_index("seq")
    count = 8
    greet("seq", seq_peers(me, count))
    grad = g_ref[...]
    inner_unit, inner_rstd = standardize(att_ref[...].astype(F32))
    inner_grad = mul_nt(grad, w_ref[:, 3 * D : 4 * D])
    att_grad = norm_back(inner_unit, inner_rstd, inner_grad * vec_ref[1:2, :]).astype(BF16)
    for pair in range(PAIRS):
        do_send[pair] = att_grad[:, pair * PAIR_LANES : (pair + 1) * PAIR_LANES]

    def out_copy(pair):
        return remote(
            do_send.at[pair],
            do_recv.at[rows_of(me)],
            send_sem.at[pair],
            recv_sem.at[me],
            "seq",
            OWNERS[pair],
        )

    for pair, owner in enumerate(OWNERS):

        @pl.when(me != owner)
        def _():
            out_copy(pair).start()

        @pl.when(me == owner)
        def _():
            do_recv[rows_of(me), :] = do_send[pair]

    vec_rows[...] = jnp.zeros_like(vec_rows)
    vec_rows[1:2, :] = jnp.sum(inner_grad * inner_unit, 0, keepdims=True)
    vec_rows[4:5, :] = jnp.sum(inner_grad, 0, keepdims=True)
    vec_rows[7:8, :] = jnp.sum(grad.astype(F32), 0, keepdims=True)
    inner = (inner_unit * vec_ref[1:2, :] + vec_ref[4:5, :]).astype(BF16)
    grad_ref[:, 3 * D : 4 * D] = mul_tn(inner, grad).astype(BF16)

    is_owner = (me != 1) & (me != 7)
    my_pair = jnp.where(me == 0, 0, me - 1)
    my_pair = jnp.where(my_pair > PAIRS - 1, PAIRS - 1, my_pair)

    def back_copy(target):
        return remote(
            d_send.at[pl.ds(target * TOKENS, TOKENS)],
            d_recv.at[my_pair],
            back_send_sem.at[target],
            back_recv_sem.at[my_pair],
            "seq",
            target,
        )

    @pl.when(is_owner)
    def _():
        for source in range(count):

            @pl.when(me != source)
            def _():
                remote(
                    do_send.at[0],
                    do_recv.at[pl.ds(source * TOKENS, TOKENS)],
                    send_sem.at[0],
                    recv_sem.at[source],
                    "seq",
                    source,
                ).wait_recv()

        key_sum[...] = jnp.zeros_like(key_sum)
        value_sum[...] = jnp.zeros_like(value_sum)
        lane = lax.broadcasted_iota(jnp.int32, (QUERY_STEP, PAIR_LANES), 1)
        first_half = lane < HEAD_DIM
        for step in reversed(range(count * TOKENS // QUERY_STEP)):
            start = step * QUERY_STEP
            keys_end = start + QUERY_STEP
            rows = slice(start, keys_end)
            plain_query = qkv_ref[rows, 0:PAIR_LANES]
            query = plain_query * jnp.asarray(SCALE, BF16)
            keys = qkv_ref[0:keys_end, PAIR_LANES : 2 * PAIR_LANES]
            values = qkv_ref[0:keys_end, 2 * PAIR_LANES : 3 * PAIR_LANES]
            causal = lax.broadcasted_iota(jnp.int32, (QUERY_STEP, keys_end), 1) <= (
                start + lax.broadcasted_iota(jnp.int32, (QUERY_STEP, keys_end), 0)
            )
            head_grad = do_recv[rows, :]
            inverse = 1.0 / pair_total_ref[rows, :]
            head_float = head_grad.astype(F32)
            products = head_float * pair_att_ref[rows, :]
            scaled = (head_float * inverse).astype(BF16)
            key_lanes = lax.broadcasted_iota(jnp.int32, (keys_end, PAIR_LANES), 1) < HEAD_DIM
            query_parts = []
            key_parts = []
            value_parts = []
            for head in range(2):
                mine = first_half if head == 0 else ~first_half
                own_query = jnp.where(mine, query, jnp.zeros_like(query))
                own_grad = jnp.where(mine, head_grad, jnp.zeros_like(head_grad))
                delta = jnp.sum(jnp.where(mine, products, 0.0), -1, keepdims=True)
                own_inverse = jnp.max(jnp.where(mine, inverse, 0.0), -1, keepdims=True)
                counts = mul_nt(u_ref[head, rows, :], u_ref[head, 0:keys_end, :])
                scores = mul_nt(own_query, keys)
                weighted = jnp.where(causal, jnp.exp(scores) * counts, 0.0)
                prob_grad = mul_nt(own_grad, values)
                score_grad = (weighted * own_inverse * (prob_grad - delta)).astype(BF16)
                query_parts.append(mul(score_grad, keys))
                key_parts.append(mul_tn(score_grad, plain_query))
                value_parts.append(mul_tn(weighted.astype(BF16), scaled))
            key_sum[0:keys_end, :] += jnp.where(key_lanes, key_parts[0], key_parts[1])
            value_sum[0:keys_end, :] += jnp.where(key_lanes, value_parts[0], value_parts[1])
            query_grad = jnp.where(first_half, query_parts[0], query_parts[1]) * SCALE
            d_send[rows, 0:PAIR_LANES] = query_grad.astype(BF16)
            d_send[rows, PAIR_LANES : 2 * PAIR_LANES] = (key_sum[rows, :] * SCALE).astype(BF16)
            d_send[rows, 2 * PAIR_LANES : 3 * PAIR_LANES] = value_sum[rows, :].astype(BF16)
            for target in (2 * step, 2 * step + 1):

                @pl.when(me != target)
                def _():
                    back_copy(target).start()

                @pl.when(me == target)
                def _():
                    d_recv[my_pair] = d_send[target * TOKENS : (target + 1) * TOKENS, :]

    unit, rstd = standardize(x_ref[...].astype(F32))
    hidden = (unit * vec_ref[0:1, :] + vec_ref[3:4, :]).astype(BF16)
    for pair, owner in enumerate(OWNERS):

        @pl.when(me != owner)
        def _():
            remote(
                d_send.at[pl.ds(0, TOKENS)],
                d_recv.at[pair],
                back_send_sem.at[0],
                back_recv_sem.at[pair],
                "seq",
                owner,
            ).wait_recv()

        for block in range(3):
            d_proj[:, block * D + pair * PAIR_LANES : block * D + (pair + 1) * PAIR_LANES] = d_recv[
                pair, :, block * PAIR_LANES : (block + 1) * PAIR_LANES
            ]
    hidden_grad = mul_nt(d_proj[...], w_ref[:, 0 : 3 * D])
    input_grad = norm_back(unit, rstd, hidden_grad * vec_ref[0:1, :])
    gx_ref[...] = (grad.astype(F32) + input_grad).astype(BF16)
    vec_rows[0:1, :] = jnp.sum(hidden_grad * unit, 0, keepdims=True)
    vec_rows[3:4, :] = jnp.sum(hidden_grad, 0, keepdims=True)
    vec_rows[6:7, :] = jnp.sum(d_proj[:, 2 * D : 3 * D].astype(F32), 0, keepdims=True)
    for block in range(3):
        grad_ref[:, block * D : (block + 1) * D] = mul_tn(
            hidden, d_proj[:, block * D : (block + 1) * D]
        ).astype(BF16)
    grad_ref[:, 4 * D : 4 * D + PAIR_LANES] = vec_rows[...].T.astype(BF16)
    for pair, owner in enumerate(OWNERS):

        @pl.when(me != owner)
        def _():
            out_copy(pair).wait_send()

    @pl.when(is_owner)
    def _():
        for target in range(count):

            @pl.when(me != target)
            def _():
                back_copy(target).wait_send()


def gelu_parts(values):
    below = 0.5 * (1.0 + lax.erf(values * (0.5**0.5)))
    return (values * below, below)


def share_stats(columns, send, recv, send_sem, recv_sem, peers):
    send[...] = columns.T[0:8, :]
    recv[0] = send[...]
    copies = [
        remote(send, recv.at[k], send_sem.at[k], recv_sem.at[k], "section", peers[k])
        for k in range(1, 4)
    ]
    for copy in copies:
        copy.start()
    return copies


def two_columns(first, second):
    lane = lax.broadcasted_iota(jnp.int32, (first.shape[0], PAIR_LANES), 1)
    return jnp.where(lane == 0, first, jnp.where(lane == 1, second, 0.0))


def slot_rows(k):
    return slice(k * TOKENS, (k + 1) * TOKENS)


def feed_forward_kernel(
    x_ref,
    w_ref,
    vec_ref,
    out_ref,
    hid_ref,
    up_ref,
    stat_ref,
    active,
    columns,
    stat_rows,
    part_send,
    part_recv,
    stat_send,
    stat_recv,
    hid_send_sem,
    hid_recv_sem,
    stat_send_sem,
    stat_recv_sem,
    part_send_sem,
    part_recv_sem,
):
    me = lax.axis_index("section")
    peers = plane_peers(me)
    greet("section", peers[1:])
    inputs = x_ref[...].astype(F32)
    unit, unused = standardize(inputs)
    hid_ref[slot_rows(0), :] = (unit * vec_ref[2:3, :] + vec_ref[5:6, :]).astype(BF16)
    hidden_copies = [
        remote(
            hid_ref.at[pl.ds(0, TOKENS)],
            hid_ref.at[pl.ds(k * TOKENS, TOKENS)],
            hid_send_sem.at[k],
            hid_recv_sem.at[k],
            "section",
            peers[k],
        )
        for k in range(1, 4)
    ]
    for copy in hidden_copies:
        copy.start()
    for k in range(4):
        if k > 0:
            hidden_copies[k - 1].wait_recv()
        upward = mul(hid_ref[slot_rows(k), :], w_ref[:, 0:D]) + vec_ref[10:11, :]
        up_ref[slot_rows(k), :] = upward
        values, unused = gelu_parts(upward)
        active[slot_rows(k), :] = values
        mean = jnp.mean(values, -1, keepdims=True)
        center = values - mean
        columns[slot_rows(k), :] = two_columns(mean, jnp.sum(center * center, -1, keepdims=True))
    stat_copies = share_stats(
        columns[...], stat_send, stat_recv, stat_send_sem, stat_recv_sem, peers
    )
    for copy in stat_copies:
        copy.wait_recv()
    stat_rows[...] = jnp.zeros_like(stat_rows)
    for k in range(4):
        means = [stat_recv[source, 0:1, slot_rows(k ^ source)] for source in range(4)]
        squares = [stat_recv[source, 1:2, slot_rows(k ^ source)] for source in range(4)]
        mean = (means[0] + means[1] + means[2] + means[3]) * 0.25
        spread = squares[0] + squares[1] + squares[2] + squares[3]
        for each in means:
            spread = spread + D * (each - mean) * (each - mean)
        stat_rows[0:1, slot_rows(k)] = mean
        stat_rows[1:2, slot_rows(k)] = lax.rsqrt(spread * (1.0 / FF) + EPSILON)
    stat_ref[...] = stat_rows[...].T
    branch = None
    part_copies = []
    for k in (1, 2, 3, 0):
        both = stat_ref[slot_rows(k), :]
        inner = (
            (active[slot_rows(k), :] - both[:, 0:1]) * both[:, 1:2] * vec_ref[9:10, :]
            + vec_ref[11:12, :]
        ).astype(BF16)
        part = mul(inner, w_ref[:, D : 2 * D])
        if k == 0:
            branch = part
        else:
            part_send[k] = part.astype(BF16)
            part_copies.append(
                remote(
                    part_send.at[k],
                    part_recv.at[k],
                    part_send_sem.at[k],
                    part_recv_sem.at[k],
                    "section",
                    peers[k],
                )
            )
            part_copies[-1].start()
    for k in range(1, 4):
        part_copies[k - 1].wait_recv()
        branch = branch + part_recv[k].astype(F32)
    out_ref[...] = (inputs + branch + vec_ref[8:9, :]).astype(BF16)
    for copy in hidden_copies + stat_copies + part_copies:
        copy.wait_send()


def feed_backward_kernel(
    g_ref,
    x_ref,
    hid_ref,
    up_ref,
    stat_ref,
    w_ref,
    vec_ref,
    gx_ref,
    grad_ref,
    grads,
    units,
    slopes,
    unit_grads,
    inners,
    lows,
    columns,
    stat_rows,
    part_send,
    part_recv,
    stat_send,
    stat_recv,
    vec_rows,
    g_send_sem,
    g_recv_sem,
    stat_send_sem,
    stat_recv_sem,
    part_send_sem,
    part_recv_sem,
):
    me = lax.axis_index("section")
    peers = plane_peers(me)
    greet("section", peers[1:])
    grads[slot_rows(0), :] = g_ref[...]
    grad_copies = [
        remote(
            grads.at[pl.ds(0, TOKENS)],
            grads.at[pl.ds(k * TOKENS, TOKENS)],
            g_send_sem.at[k],
            g_recv_sem.at[k],
            "section",
            peers[k],
        )
        for k in range(1, 4)
    ]
    for copy in grad_copies:
        copy.start()
    gain_sum = jnp.zeros((1, D), F32)
    bias_sum = jnp.zeros((1, D), F32)
    for k in range(4):
        both = stat_ref[slot_rows(k), :]
        upward = up_ref[slot_rows(k), :]
        values, below = gelu_parts(upward)
        slopes[slot_rows(k), :] = below + upward * (
            jnp.exp(-0.5 * upward * upward) * (0.5 / 3.141592653589793) ** 0.5
        )
        unit = (values - both[:, 0:1]) * both[:, 1:2]
        units[slot_rows(k), :] = unit
        inners[slot_rows(k), :] = (unit * vec_ref[9:10, :] + vec_ref[11:12, :]).astype(BF16)
        if k > 0:
            grad_copies[k - 1].wait_recv()
        inner_grad = mul_nt(grads[slot_rows(k), :], w_ref[:, D : 2 * D])
        gain_sum = gain_sum + jnp.sum(inner_grad * unit, 0, keepdims=True)
        bias_sum = bias_sum + jnp.sum(inner_grad, 0, keepdims=True)
        unit_grad = inner_grad * vec_ref[9:10, :]
        unit_grads[slot_rows(k), :] = unit_grad
        columns[slot_rows(k), :] = two_columns(
            jnp.sum(unit_grad, -1, keepdims=True), jnp.sum(unit_grad * unit, -1, keepdims=True)
        )
    stat_copies = share_stats(
        columns[...], stat_send, stat_recv, stat_send_sem, stat_recv_sem, peers
    )
    vec_rows[...] = jnp.zeros_like(vec_rows)
    vec_rows[9:10, :] = gain_sum
    vec_rows[11:12, :] = bias_sum
    grad_ref[:, D : 2 * D] = mul_tn(inners[...], grads[...]).astype(BF16)
    for copy in stat_copies:
        copy.wait_recv()
    stat_rows[...] = jnp.zeros_like(stat_rows)
    for k in range(4):
        for line in range(2):
            parts = [stat_recv[source, line : line + 1, slot_rows(k ^ source)] for source in range(4)]
            stat_rows[line : line + 1, slot_rows(k)] = (
                parts[0] + parts[1] + parts[2] + parts[3]
            ) * (1.0 / FF)
    columns[...] = stat_rows[...].T
    hidden_grad = None
    low_sum = jnp.zeros((1, D), F32)
    part_copies = []
    for k in (1, 2, 3, 0):
        rstd = stat_ref[slot_rows(k), :][:, 1:2]
        both = columns[slot_rows(k), :]
        low = (
            rstd
            * (unit_grads[slot_rows(k), :] - both[:, 0:1] - units[slot_rows(k), :] * both[:, 1:2])
            * slopes[slot_rows(k), :]
        ).astype(BF16)
        lows[slot_rows(k), :] = low
        low_sum = low_sum + jnp.sum(low.astype(F32), 0, keepdims=True)
        part = mul_nt(low, w_ref[:, 0:D])
        if k == 0:
            hidden_grad = part
        else:
            part_send[k] = part.astype(BF16)
            part_copies.append(
                remote(
                    part_send.at[k],
                    part_recv.at[k],
                    part_send_sem.at[k],
                    part_recv_sem.at[k],
                    "section",
                    peers[k],
                )
            )
            part_copies[-1].start()
    vec_rows[10:11, :] = low_sum
    grad_ref[:, 0:D] = mul_tn(hid_ref[...], lows[...]).astype(BF16)
    unit, rstd = standardize(x_ref[...].astype(F32))
    for k in range(1, 4):
        part_copies[k - 1].wait_recv()
        hidden_grad = hidden_grad + part_recv[k].astype(F32)
    grad = g_ref[...].astype(F32)
    gx_ref[...] = (grad + norm_back(unit, rstd, hidden_grad * vec_ref[2:3, :])).astype(BF16)
    vec_rows[2:3, :] = jnp.sum(hidden_grad * unit, 0, keepdims=True)
    vec_rows[5:6, :] = jnp.sum(hidden_grad, 0, keepdims=True)
    vec_rows[8:9, :] = jnp.sum(grad, 0, keepdims=True)
    grad_ref[:, 2 * D : 2 * D + PAIR_LANES] = vec_rows[...].T.astype(BF16)
    for copy in grad_copies + stat_copies + part_copies:
        copy.wait_send()


def shaped(shape, kind):
    return jax.ShapeDtypeStruct(shape, kind)


def call_kernel(kernel, name, number, outs, scratch, args, flops):
    vmem = pl.BlockSpec(memory_space=pltpu.VMEM)
    return pl.pallas_call(
        kernel,
        name=name,
        out_shape=outs,
        in_specs=[vmem] * len(args),
        out_specs=[vmem] * len(outs),
        scratch_shapes=scratch,
        compiler_params=pltpu.CompilerParams(
            collective_id=number, has_side_effects=True, vmem_limit_bytes=VMEM_BYTES
        ),
        cost_estimate=pl.CostEstimate(flops=flops, bytes_accessed=60_000_000, transcendentals=0),
    )(*args)


def run_attention(number, x, w, vec, picks):
    dma = pltpu.SemaphoreType.DMA
    group = 8 * TOKENS
    return call_kernel(
        attention_forward_kernel,
        "attention_forward",
        number,
        [
            shaped((TOKENS, D), BF16),
            shaped((group, 3 * PAIR_LANES), BF16),
            shaped((TOKENS, D), BF16),
            shaped((group, PAIR_LANES), F32),
            shaped((group, PAIR_LANES), F32),
            shaped((8, PAIR_LANES), F32),
        ],
        [
            pltpu.VMEM((PAIRS, TOKENS, 3 * PAIR_LANES), BF16),
            pltpu.VMEM((group, PAIR_LANES), BF16),
            pltpu.VMEM((PAIRS, TOKENS, PAIR_LANES), BF16),
            dma((PAIRS,)),
            dma((8,)),
            dma((8,)),
            dma((PAIRS,)),
        ],
        (x, w, vec, picks),
        10**9,
    )


def run_attention_back(number, grad, x, att, w, vec, picks, qkv, pair_att, pair_total):
    dma = pltpu.SemaphoreType.DMA
    group = 8 * TOKENS
    return call_kernel(
        attention_backward_kernel,
        "attention_backward",
        number,
        [shaped((TOKENS, D), BF16), shaped((D, 4 * D + PAIR_LANES), BF16)],
        [
            pltpu.VMEM((PAIRS, TOKENS, PAIR_LANES), BF16),
            pltpu.VMEM((group, PAIR_LANES), BF16),
            pltpu.VMEM((group, PAIR_LANES), F32),
            pltpu.VMEM((group, PAIR_LANES), F32),
            pltpu.VMEM((group, 3 * PAIR_LANES), BF16),
            pltpu.VMEM((PAIRS, TOKENS, 3 * PAIR_LANES), BF16),
            pltpu.VMEM((TOKENS, 3 * D), BF16),
            pltpu.VMEM((PAIR_LANES, D), F32),
            dma((PAIRS,)),
            dma((8,)),
            dma((8,)),
            dma((PAIRS,)),
        ],
        (grad, x, att, w, vec, picks, qkv, pair_att, pair_total),
        2 * 10**9,
    )


def run_feed(number, x, w, vec):
    dma = pltpu.SemaphoreType.DMA
    wide = 4 * TOKENS
    return call_kernel(
        feed_forward_kernel,
        "feed_forward",
        number,
        [
            shaped((TOKENS, D), BF16),
            shaped((wide, D), BF16),
            shaped((wide, D), F32),
            shaped((wide, PAIR_LANES), F32),
        ],
        [
            pltpu.VMEM((wide, D), F32),
            pltpu.VMEM((wide, PAIR_LANES), F32),
            pltpu.VMEM((PAIR_LANES, wide), F32),
            pltpu.VMEM((4, TOKENS, D), BF16),
            pltpu.VMEM((4, TOKENS, D), BF16),
            pltpu.VMEM((8, wide), F32),
            pltpu.VMEM((4, 8, wide), F32),
        ]
        + [dma((4,))] * 6,
        (x, w, vec),
        10**9,
    )


def run_feed_back(number, grad, x, hid, upward, stat, w, vec):
    dma = pltpu.SemaphoreType.DMA
    wide = 4 * TOKENS
    return call_kernel(
        feed_backward_kernel,
        "feed_backward",
        number,
        [shaped((TOKENS, D), BF16), shaped((D, 2 * D + PAIR_LANES), BF16)],
        [
            pltpu.VMEM((wide, D), BF16),
            pltpu.VMEM((wide, D), F32),
            pltpu.VMEM((wide, D), F32),
            pltpu.VMEM((wide, D), F32),
            pltpu.VMEM((wide, D), BF16),
            pltpu.VMEM((wide, D), BF16),
            pltpu.VMEM((wide, PAIR_LANES), F32),
            pltpu.VMEM((PAIR_LANES, wide), F32),
            pltpu.VMEM((4, TOKENS, D), BF16),
            pltpu.VMEM((4, TOKENS, D), BF16),
            pltpu.VMEM((8, wide), F32),
            pltpu.VMEM((4, 8, wide), F32),
            pltpu.VMEM((PAIR_LANES, D), F32),
        ]
        + [dma((4,))] * 6,
        (grad, x, hid, upward, stat, w, vec),
        2 * 10**9,
    )


def pattern_picks(lengths, my_pair):
    tokens = jnp.arange(8 * TOKENS, dtype=jnp.int32)
    row_ids, pos = place_rows(lengths, tokens)
    lane = jnp.arange(PAIR_LANES, dtype=jnp.int32)
    number, row = (lane // 4, lane % 4)
    ratio = jnp.where(number < 5, jnp.array(RATIOS + (1, 1, 1), jnp.int32)[jnp.minimum(number, 7)], 1)
    heads = 2 * my_pair + jnp.arange(2, dtype=jnp.int32)
    same = (row_ids[:, None] == row[None, :]) & (number < 5)[None, :]
    fits = (pos[:, None] % ratio[None, :])[None] == (heads[:, None] % ratio[None, :])[:, None, :]
    return (same[None] & fits).astype(BF16)


def quick_body(
    embeds,
    row_lengths,
    qkv_weight,
    out_weight,
    up_weight,
    down_weight,
    model_gains,
    model_biases,
    hidden_gains,
    hidden_biases,
    cotangent,
):
    section = lax.axis_index("section")
    seq = lax.axis_index("seq")
    layers = qkv_weight.shape[0]
    depth = qkv_weight.shape[1]
    piece = FF // 4 // 8

    def of_section(stacked, axis):
        return lax.dynamic_index_in_dim(stacked, section, axis, False)

    hidden_vecs = jnp.concatenate([hidden_gains[:, None], hidden_biases], 1)
    hidden_vecs = of_section(hidden_vecs.reshape(layers, 3, 4, piece), 2)
    small = jnp.concatenate(
        [model_gains, model_biases, hidden_vecs, jnp.zeros((layers, 4, depth), BF16)], 1
    )
    small = lax.all_gather(small, "seq", axis=0, tiled=False)
    vecs = jnp.transpose(small, (1, 2, 0, 3)).reshape(layers, VEC_ROWS, D).astype(F32)
    attention_weights = []
    feed_weights = []
    for layer in range(layers):
        rows = jnp.concatenate([qkv_weight[layer], out_weight[layer]], 1)
        rows = of_section(rows.reshape(4, depth // 4, 4 * D), 0)
        attention_weights.append(lax.all_gather(rows, ("seq", "section"), axis=0, tiled=True))
        up_rows = of_section(up_weight[layer].reshape(depth, 8, 4, piece), 2).reshape(depth, D)
        down_rows = of_section(down_weight[layer].reshape(4, piece, D), 0)
        rows = jnp.concatenate([up_rows, down_rows], 1)
        feed_weights.append(lax.all_gather(rows, "seq", axis=0, tiled=True))
    is_owner = (seq != 1) & (seq != 7)
    my_pair = jnp.clip(jnp.where(seq == 0, 0, seq - 1), 0, PAIRS - 1)
    picks = pattern_picks(lax.dynamic_index_in_dim(row_lengths, section, 0, False), my_pair)
    stream = lax.dynamic_index_in_dim(embeds, section, 0, False)
    grad = lax.dynamic_index_in_dim(cotangent, section, 0, False)
    outputs = []
    kept = []
    log_rows = []
    for layer in range(layers):
        vec = vecs[layer]
        into_attention = stream
        stream, qkv, att, pair_att, pair_total, logs = run_attention(
            10 + layer, stream, attention_weights[layer], vec, picks
        )
        outputs.append(stream)
        log_rows.append(logs[0])
        into_feed = stream
        stream, hid, upward, stat = run_feed(20 + layer, stream, feed_weights[layer], vec)
        outputs.append(stream)
        kept.append((into_attention, att, qkv, pair_att, pair_total, into_feed, hid, upward, stat))
    sublayer_outputs = lax.all_to_all(jnp.stack(outputs), "section", 0, 0, tiled=True)
    pick_rows = jnp.where(is_owner, jnp.sum(picks.astype(F32), (0, 1)), 0.0)
    lines = jnp.stack(log_rows + [pick_rows])[:, :20].reshape(layers + 1, 5, 4).sum(-1)
    lines = lax.psum(lines, ("section", "seq"))
    pattern_means = lines[:layers] / lines[layers:]
    grads = [None] * (2 * layers)
    attention_shards = [None] * layers
    feed_shards = [None] * layers
    for layer in reversed(range(layers)):
        vec = vecs[layer]
        into_attention, att, qkv, pair_att, pair_total, into_feed, hid, upward, stat = kept[layer]
        grad, step = run_feed_back(
            30 + layer, grad, into_feed, hid, upward, stat, feed_weights[layer], vec
        )
        grads[2 * layer + 1] = grad
        shard = lax.psum_scatter(step, "seq", scatter_dimension=0, tiled=True)
        feed_shards[layer] = lax.all_gather(shard, "section", axis=0, tiled=False)
        grad, step = run_attention_back(
            40 + layer,
            grad,
            into_attention,
            att,
            attention_weights[layer],
            vec,
            picks,
            qkv,
            pair_att,
            pair_total,
        )
        grads[2 * layer] = grad
        shard = lax.psum_scatter(step, ("seq", "section"), scatter_dimension=0, tiled=True)
        attention_shards[layer] = lax.all_gather(shard, "section", axis=0, tiled=True)
    sublayer_grads = lax.all_to_all(jnp.stack(grads), "section", 0, 0, tiled=True)
    attention_all = jnp.stack(attention_shards).astype(F32)
    feed_all = jnp.stack(feed_shards).astype(F32)
    qkv_grad = attention_all[:, :, : 3 * D]
    out_grad = attention_all[:, :, 3 * D : 4 * D]
    model_vecs = attention_all[:, :, 4 * D : 4 * D + MODEL_ROWS] + jnp.sum(
        feed_all[:, :, :, 2 * D : 2 * D + MODEL_ROWS], 1
    )
    model_vecs = jnp.transpose(model_vecs, (0, 2, 1))
    up_grad = feed_all[:, :, :, :D].reshape(layers, 4, depth, 8, piece)
    up_grad = jnp.transpose(up_grad, (0, 2, 3, 1, 4)).reshape(layers, depth, FF)
    down_grad = feed_all[:, :, :, D : 2 * D].reshape(layers, 4 * piece, D)
    hidden_rows = feed_all[:, :, :, 2 * D + MODEL_ROWS : 2 * D + MODEL_ROWS + 3]
    hidden_rows = jnp.transpose(hidden_rows, (0, 3, 1, 2)).reshape(layers, 3, 4 * piece)
    return (
        sublayer_outputs[None],
        sublayer_grads[None],
        qkv_grad,
        out_grad,
        up_grad,
        down_grad,
        model_vecs[:, 0:3],
        model_vecs[:, 3:9],
        hidden_rows[:, 0],
        hidden_rows[:, 1:3],
        pattern_means,
    )


def fits_quick(mesh):
    return mesh.shape["section"] == 4 and mesh.shape["seq"] == 8


def solution(mesh):
    return jax.shard_map(
        quick_body if fits_quick(mesh) else body,
        mesh=mesh,
        in_specs=(
            P(None, "seq", None),
            P(),
            P(None, "seq", None),
            P(None, "seq", None),
            P(None, "seq", None),
            P(None, "seq", None),
            P(None, None, "seq"),
            P(None, None, "seq"),
            P(None, "seq"),
            P(None, None, "seq"),
            P(None, "seq", None),
        ),
        out_specs=(
            P("section", None, "seq", None),
            P("section", None, "seq", None),
            P(None, "seq", None),
            P(None, "seq", None),
            P(None, "seq", None),
            P(None, "seq", None),
            P(None, None, "seq"),
            P(None, None, "seq"),
            P(None, "seq"),
            P(None, None, "seq"),
            P(),
        ),
        check_vma=False,
    )
```

```python
import jax
import jax.numpy as jnp
from jax import lax
from jax.experimental import pallas as pl
from jax.experimental.pallas import tpu as pltpu
from jax.sharding import PartitionSpec as P

D = 768
HEADS = 12
HEAD_DIM = 64
FF = 3072


WIDTHS = (2048, 4096, 8192, 16384, 32768)
RATIOS = (1, 2, 4, 6, 12)
EPSILON = 1e-05


def passed_along(value, axis, steps):
    count = lax.axis_size(axis)
    initial, last = (max(0, -steps), min(count, count - steps))
    return lax.ppermute(value, axis, [(source, source + steps) for source in range(initial, last)])


def norm_rows(inputs, gain_row, offset):
    center = inputs - jnp.mean(inputs, -1, keepdims=True)
    spread = jnp.mean(center * center, -1, keepdims=True)
    return center * lax.rsqrt(spread + EPSILON) * gain_row + offset


def place_rows(lengths, token_index):
    row_ends = jnp.cumsum(lengths)
    passed = token_index[:, None] >= row_ends[None, :]
    row_ids = jnp.sum(passed.astype(jnp.int32), 1)
    offsets = token_index - jnp.sum(jnp.where(passed, lengths[None, :], 0), 1)
    return (row_ids, offsets)


def query_chosen(query_pos):
    head_ids = jnp.arange(HEADS, dtype=jnp.int32)
    chosen = []
    for seg_width, seg_ratio in zip(WIDTHS, RATIOS):
        query_pick = query_pos % seg_width % seg_ratio
        chosen.append(query_pick[None, :] == (head_ids % seg_ratio)[:, None])
    return chosen


def pattern_allow(query_rows, query_pos, key_rows, key_pos):
    widths = jnp.array(WIDTHS, jnp.int32)[:, None]
    ratios = jnp.array(RATIOS, jnp.int32)[:, None]
    residue = jnp.arange(HEADS, dtype=jnp.int32)[None, :] % ratios
    query_mod = query_pos[None, :] % widths % ratios
    key_mod = key_pos[None, :] % widths % ratios
    query_ok = query_mod[:, None, :] == residue[:, :, None]
    key_ok = key_mod[:, None, :] == residue[:, :, None]
    common = (query_rows[:, None] == key_rows[None, :]) & (key_pos[None, :] <= query_pos[:, None])
    inside = common[None] & (
        (query_pos[None, :] // widths)[:, :, None] == (key_pos[None, :] // widths)[:, None, :]
    )
    return inside[:, None] & query_ok[:, :, :, None] & key_ok[:, :, None, :]


def block_rows(total_rows):
    step_rows = min(total_rows, 512)
    return step_rows


def split_heads(matrix):
    return matrix.reshape(matrix.shape[0], HEADS, HEAD_DIM)


def pair_terms(query_block, keys_block, query_rows, query_pos, key_rows, key_pos):
    scores = jnp.einsum(
        "qhe,khe->hqk", query_block, keys_block, preferred_element_type=jnp.float32
    ) * HEAD_DIM ** (-0.5)
    allowed = pattern_allow(query_rows, query_pos, key_rows, key_pos)
    counts = jnp.sum(allowed.astype(jnp.float32), 0)
    raised = jnp.exp(scores)
    return (raised, counts * raised, allowed)


def project_tokens(inputs, qkv_matrix, norm_gains, norm_biases):
    hidden = norm_rows(inputs, norm_gains[0], norm_biases[0]).astype(jnp.bfloat16)
    bias_row = jnp.concatenate(
        [jnp.zeros_like(norm_biases[3]), jnp.zeros_like(norm_biases[3]), norm_biases[3]]
    )
    projected = (jnp.dot(hidden, qkv_matrix, preferred_element_type=jnp.float32) + bias_row).astype(
        jnp.bfloat16
    )
    return (hidden, projected)


def attention_forward(section_in, projected, whole_keys, lengths, params, seq_index):
    out_matrix, norm_gains, norm_biases = (params[1], params[4], params[5])
    tok_rows = section_in.shape[0]
    inputs = section_in.astype(jnp.float32)
    queries = split_heads(projected[:, :D])
    query_rows, query_pos = place_rows(
        lengths, seq_index * tok_rows + jnp.arange(tok_rows, dtype=jnp.int32)
    )
    group_rows = whole_keys.shape[0]
    step_rows = block_rows(group_rows)

    def one_block(running, block_start):
        totals, pattern_sums, accumulated = running
        kv_block = lax.dynamic_slice_in_dim(whole_keys, block_start, step_rows, 0)
        key_rows, key_pos = place_rows(
            lengths, block_start + jnp.arange(step_rows, dtype=jnp.int32)
        )
        raised, weighted, allowed = pair_terms(
            queries, split_heads(kv_block[:, :D]), query_rows, query_pos, key_rows, key_pos
        )
        totals = totals + jnp.sum(weighted, -1)
        pattern_sums = pattern_sums + jnp.sum(jnp.where(allowed, raised[None], 0.0), -1)
        accumulated = accumulated + jnp.einsum(
            "hqk,khe->hqe",
            weighted.astype(jnp.bfloat16),
            split_heads(kv_block[:, D:]),
            preferred_element_type=jnp.float32,
        )
        return ((totals, pattern_sums, accumulated), None)

    start_sums = (
        jnp.zeros((HEADS, tok_rows), jnp.float32),
        jnp.zeros((len(WIDTHS), HEADS, tok_rows), jnp.float32),
        jnp.zeros((HEADS, tok_rows, HEAD_DIM), jnp.float32),
    )
    folded, unused = lax.scan(
        one_block, start_sums, jnp.arange(0, group_rows, step_rows, dtype=jnp.int32)
    )
    totals, pattern_sums, accumulated = folded
    attended = jnp.transpose(accumulated / totals[:, :, None], (1, 0, 2)).reshape(tok_rows, D)
    inner_norm = norm_rows(attended, norm_gains[1], norm_biases[1]).astype(jnp.bfloat16)
    branch = jnp.dot(inner_norm, out_matrix, preferred_element_type=jnp.float32) + norm_biases[4]
    section_out = (inputs + branch).astype(jnp.bfloat16)
    chosen = query_chosen(query_pos)
    log_terms = jnp.stack(
        [
            jnp.sum(
                jnp.where(pick_row, jnp.log(jnp.where(pick_row, pattern_sums[number], 1.0)), 0.0)
            )
            for number, pick_row in enumerate(chosen)
        ]
    )
    pick_counts = jnp.stack([jnp.sum(pick_row.astype(jnp.float32)) for pick_row in chosen])
    return (section_out, attended, totals, log_terms, pick_counts)


def feed_forward(section_in, params):
    up_matrix, down_matrix, norm_gains, norm_biases, hidden_gain, hidden_bias = (
        params[2],
        params[3],
        params[4],
        params[5],
        params[6],
        params[7],
    )
    tok_rows = section_in.shape[0]
    inputs = section_in.astype(jnp.float32)
    hidden = norm_rows(inputs, norm_gains[2], norm_biases[2]).astype(jnp.bfloat16)
    upward = jnp.dot(hidden, up_matrix, preferred_element_type=jnp.float32) + hidden_bias[0]
    inner_norm = norm_rows(
        jax.nn.gelu(upward, approximate=False), hidden_gain, hidden_bias[1]
    ).astype(jnp.bfloat16)
    branch = jnp.dot(inner_norm, down_matrix, preferred_element_type=jnp.float32) + norm_biases[5]
    section_out = (inputs + branch).astype(jnp.bfloat16)
    empty_terms = jnp.zeros((len(WIDTHS),), jnp.float32)
    return (
        section_out,
        jnp.zeros((tok_rows, D), jnp.float32),
        jnp.zeros((HEADS, tok_rows), jnp.float32),
        empty_terms,
        empty_terms,
    )


def attention_middle(
    section_in, grad_out, attended, totals, lengths, all_keys, projected, params, seq_index
):
    out_matrix, norm_gains, norm_biases = (params[1], params[4], params[5])
    scale_factor = HEAD_DIM ** (-0.5)
    tok_rows = section_in.shape[0]
    queries = split_heads(projected[:, :D])
    query_rows, query_pos = place_rows(
        lengths, seq_index * tok_rows + jnp.arange(tok_rows, dtype=jnp.int32)
    )
    inner_norm = norm_rows(attended, norm_gains[1], norm_biases[1]).astype(jnp.bfloat16)
    out_step = jnp.einsum("td,tf->df", inner_norm, grad_out, preferred_element_type=jnp.float32)
    inner_grad = jnp.einsum("tf,df->td", grad_out, out_matrix, preferred_element_type=jnp.float32)
    unused, inner_back = jax.vjp(norm_rows, attended, norm_gains[1], norm_biases[1])
    attended_grad, inner_gain_grad, inner_bias_grad = inner_back(inner_grad)
    low_attended = attended_grad.astype(jnp.bfloat16)
    head_grad = split_heads(low_attended)
    row_dots = jnp.einsum("qhe,qhe->hq", head_grad.astype(jnp.float32), split_heads(attended))
    scaled_grad = head_grad.astype(jnp.float32) / jnp.transpose(totals)[:, :, None]
    group_rows = all_keys.shape[0]
    step_rows = block_rows(group_rows)

    def grad_block(query_grad, block_start):
        kv_block = lax.dynamic_slice_in_dim(all_keys, block_start, step_rows, 0)
        keys_block = split_heads(kv_block[:, :D])
        values_block = split_heads(kv_block[:, D:])
        key_rows, key_pos = place_rows(
            lengths, block_start + jnp.arange(step_rows, dtype=jnp.int32)
        )
        raised, weighted, allowed = pair_terms(
            queries, keys_block, query_rows, query_pos, key_rows, key_pos
        )
        prob_grad = jnp.einsum(
            "qhe,khe->hqk", head_grad, values_block, preferred_element_type=jnp.float32
        )
        score_grad = (weighted / totals[:, :, None] * (prob_grad - row_dots[:, :, None])).astype(
            jnp.bfloat16
        )
        query_grad = (
            query_grad
            + jnp.einsum("hqk,khe->qhe", score_grad, keys_block, preferred_element_type=jnp.float32)
            * scale_factor
        )
        key_grad = (
            jnp.einsum("hqk,qhe->khe", score_grad, queries, preferred_element_type=jnp.float32)
            * scale_factor
        )
        value_grad = jnp.einsum(
            "hqk,qhe->khe",
            weighted.astype(jnp.bfloat16),
            scaled_grad,
            preferred_element_type=jnp.float32,
        )
        block_grad = jnp.concatenate(
            [key_grad.reshape(step_rows, D), value_grad.reshape(step_rows, D)], 1
        )
        return (query_grad, block_grad)

    query_grad, block_grads = lax.scan(
        grad_block,
        jnp.zeros((tok_rows, HEADS, HEAD_DIM), jnp.float32),
        jnp.arange(0, group_rows, step_rows, dtype=jnp.int32),
    )
    block_grads = block_grads.reshape(group_rows, 2 * D)
    return (
        query_grad.reshape(tok_rows, D),
        low_attended,
        row_dots,
        block_grads,
        out_step,
        inner_gain_grad,
        inner_bias_grad,
    )


def attention_finish(section_in, grad_out, middle, extra, params, grad_sums):
    qkv_matrix, norm_gains, norm_biases = (params[0], params[4], params[5])
    inputs = section_in.astype(jnp.float32)
    grad_float = grad_out.astype(jnp.float32)
    hidden = norm_rows(inputs, norm_gains[0], norm_biases[0]).astype(jnp.bfloat16)
    query_grad, low_attended, row_dots, block_grads, out_step, inner_gain_grad, inner_bias_grad = (
        middle
    )
    own_grads = extra[0]
    proj_grad = jnp.concatenate([query_grad, own_grads], 1).astype(jnp.bfloat16)
    qkv_step = jnp.einsum("td,tf->df", hidden, proj_grad, preferred_element_type=jnp.float32)
    value_bias_sums = jnp.sum(proj_grad[:, 2 * D :].astype(jnp.float32), 0)
    hidden_grad = jnp.einsum("tf,df->td", proj_grad, qkv_matrix, preferred_element_type=jnp.float32)
    unused_first, first_back = jax.vjp(norm_rows, inputs, norm_gains[0], norm_biases[0])
    input_grad, first_gain_grad, first_bias_grad = first_back(hidden_grad)
    qkv_sum, out_sum, up_sum, down_sum, gain_sum, bias_sum, hgain_sum, hbias_sum = grad_sums
    gain_sum = gain_sum.at[0].add(first_gain_grad).at[1].add(inner_gain_grad)
    bias_sum = (
        bias_sum.at[0]
        .add(first_bias_grad)
        .at[1]
        .add(inner_bias_grad)
        .at[3]
        .add(value_bias_sums)
        .at[4]
        .add(jnp.sum(grad_float, 0))
    )
    return (
        grad_float + input_grad,
        (
            qkv_sum + qkv_step,
            out_sum + out_step,
            up_sum,
            down_sum,
            gain_sum,
            bias_sum,
            hgain_sum,
            hbias_sum,
        ),
    )


def feed_backward(section_in, grad_out, params, grad_sums):
    up_matrix, down_matrix, norm_gains, norm_biases, hidden_gain, hidden_bias = (
        params[2],
        params[3],
        params[4],
        params[5],
        params[6],
        params[7],
    )
    inputs = section_in.astype(jnp.float32)
    grad_float = grad_out.astype(jnp.float32)
    hidden = norm_rows(inputs, norm_gains[2], norm_biases[2]).astype(jnp.bfloat16)
    upward = jnp.dot(hidden, up_matrix, preferred_element_type=jnp.float32) + hidden_bias[0]

    def inner_rows(upward_in, gain_row, bias_row):
        return norm_rows(jax.nn.gelu(upward_in, approximate=False), gain_row, bias_row)

    inner_value, inner_back = jax.vjp(inner_rows, upward, hidden_gain, hidden_bias[1])
    inner_norm = inner_value.astype(jnp.bfloat16)
    down_step = jnp.einsum("tf,td->fd", inner_norm, grad_out, preferred_element_type=jnp.float32)
    inner_grad = jnp.einsum("td,fd->tf", grad_out, down_matrix, preferred_element_type=jnp.float32)
    upward_grad, hgain_step, hbias_step = inner_back(inner_grad)
    low_upward = upward_grad.astype(jnp.bfloat16)
    up_step = jnp.einsum("td,tf->df", hidden, low_upward, preferred_element_type=jnp.float32)
    hidden_grad = jnp.einsum("tf,df->td", low_upward, up_matrix, preferred_element_type=jnp.float32)
    unused, first_back = jax.vjp(norm_rows, inputs, norm_gains[2], norm_biases[2])
    input_grad, first_gain_grad, first_bias_grad = first_back(hidden_grad)
    qkv_sum, out_sum, up_sum, down_sum, gain_sum, bias_sum, hgain_sum, hbias_sum = grad_sums
    gain_sum = gain_sum.at[2].add(first_gain_grad)
    bias_sum = bias_sum.at[2].add(first_bias_grad).at[5].add(jnp.sum(grad_float, 0))
    hbias_sum = (
        hbias_sum.at[0].add(jnp.sum(low_upward.astype(jnp.float32), 0)).at[1].add(hbias_step)
    )
    return (
        grad_float + input_grad,
        (
            qkv_sum,
            out_sum,
            up_sum + up_step,
            down_sum + down_step,
            gain_sum,
            bias_sum,
            hgain_sum + hgain_step,
            hbias_sum,
        ),
    )


def keep_slot(store, fresh, slot_id, in_range):
    previous = lax.dynamic_index_in_dim(store, slot_id, 0, False)
    return lax.dynamic_update_index_in_dim(store, jnp.where(in_range, fresh, previous), slot_id, 0)


def body(
    embeds,
    row_lengths,
    qkv_weight,
    out_weight,
    up_weight,
    down_weight,
    model_gains,
    model_biases,
    hidden_gains,
    hidden_biases,
    cotangent,
):
    section_id = lax.axis_index("section")
    seq_index = lax.axis_index("seq")
    section_count = lax.axis_size("section")
    micro_count = embeds.shape[0]
    tok_rows = embeds.shape[1]
    group_rows = tok_rows * lax.axis_size("seq")
    layer_id = section_id // 2
    attends = section_id % 2 == 0
    bias_count = model_biases.shape[1]

    def pick_layer(stacked):
        return lax.dynamic_index_in_dim(stacked, layer_id, 0, False)

    gathered = (
        lax.all_gather(pick_layer(qkv_weight), "seq", axis=0, tiled=True),
        lax.all_gather(pick_layer(out_weight), "seq", axis=0, tiled=True),
        lax.all_gather(pick_layer(up_weight), "seq", axis=0, tiled=True),
        lax.all_gather(pick_layer(down_weight), "seq", axis=0, tiled=True),
        lax.all_gather(pick_layer(model_gains), "seq", axis=1, tiled=True),
        lax.all_gather(pick_layer(model_biases), "seq", axis=1, tiled=True),
        lax.all_gather(pick_layer(hidden_gains), "seq", axis=0, tiled=True),
        lax.all_gather(pick_layer(hidden_biases), "seq", axis=1, tiled=True),
    )
    params = tuple(gathered[:4]) + tuple((vector.astype(jnp.float32) for vector in gathered[4:]))
    whole_shape = (0,)

    def make_projected(section_in):
        return project_tokens(section_in.astype(jnp.float32), params[0], params[4], params[5])[1]

    def skip_projected(section_in):
        return jnp.zeros((tok_rows, 3 * D), jnp.bfloat16)

    def run_attention(section_in, projected, whole_keys, lengths):
        return attention_forward(section_in, projected, whole_keys, lengths, params, seq_index)

    def run_feed(section_in, projected, whole_keys, lengths):
        return feed_forward(section_in, params)

    def forward_tick(running, tick_id):
        (
            incoming,
            kept_inputs,
            kept_attended,
            kept_totals,
            kept_whole,
            outputs,
            log_sums,
            pick_sums,
        ) = running
        micro_id = tick_id - section_id
        in_range = (micro_id >= 0) & (micro_id < micro_count)
        slot_id = jnp.clip(micro_id, 0, micro_count - 1)
        lengths = lax.dynamic_index_in_dim(row_lengths, slot_id, 0, False)
        section_in = jnp.where(
            section_id == 0, lax.dynamic_index_in_dim(embeds, slot_id, 0, False), incoming
        )
        projected = lax.cond(attends, make_projected, skip_projected, section_in)
        whole_keys = lax.all_gather(projected[:, D:], "seq", axis=0, tiled=True)
        section_out, attended, totals, log_terms, pick_counts = lax.cond(
            attends, run_attention, run_feed, section_in, projected, whole_keys, lengths
        )
        kept_inputs = keep_slot(kept_inputs, section_in, slot_id, in_range)
        kept_attended = keep_slot(kept_attended, attended, slot_id, in_range)
        kept_totals = keep_slot(kept_totals, totals, slot_id, in_range)
        outputs = keep_slot(outputs, section_out, slot_id, in_range)
        log_sums = log_sums + jnp.where(in_range, log_terms, 0.0)
        pick_sums = pick_sums + jnp.where(in_range, pick_counts, 0.0)
        incoming = passed_along(section_out, "section", 1)
        return (
            (
                incoming,
                kept_inputs,
                kept_attended,
                kept_totals,
                kept_whole,
                outputs,
                log_sums,
                pick_sums,
            ),
            None,
        )

    forward_start = (
        jnp.zeros((tok_rows, D), jnp.bfloat16),
        jnp.zeros((micro_count, tok_rows, D), jnp.bfloat16),
        jnp.zeros((micro_count, tok_rows, D), jnp.float32),
        jnp.zeros((micro_count, HEADS, tok_rows), jnp.float32),
        jnp.zeros((micro_count,) + whole_shape, jnp.bfloat16),
        jnp.zeros((micro_count, tok_rows, D), jnp.bfloat16),
        jnp.zeros((len(WIDTHS),), jnp.float32),
        jnp.zeros((len(WIDTHS),), jnp.float32),
    )
    ticks = jnp.arange(micro_count + section_count - 1, dtype=jnp.int32)
    forward_end, unused = lax.scan(forward_tick, forward_start, ticks)
    unused_in, kept_inputs, kept_attended, kept_totals, kept_whole, outputs, log_sums, pick_sums = (
        forward_end
    )
    block_shape = (group_rows, 2 * D)

    def middle_attention(section_in, grad_out, attended, totals, lengths, all_keys, projected):
        return attention_middle(
            section_in, grad_out, attended, totals, lengths, all_keys, projected, params, seq_index
        )

    def middle_feed(section_in, grad_out, attended, totals, lengths, all_keys, projected):
        return (
            jnp.zeros((tok_rows, D), jnp.float32),
            jnp.zeros((tok_rows, D), jnp.bfloat16),
            jnp.zeros((HEADS, tok_rows), jnp.float32),
            jnp.zeros(block_shape, jnp.float32),
            jnp.zeros((D, D), jnp.float32),
            jnp.zeros((D,), jnp.float32),
            jnp.zeros((D,), jnp.float32),
        )

    def finish_attention(section_in, grad_out, projected, middle, extra, lengths, grad_sums):
        return attention_finish(section_in, grad_out, middle, extra, params, grad_sums)

    def finish_feed(section_in, grad_out, projected, middle, extra, lengths, grad_sums):
        return feed_backward(section_in, grad_out, params, grad_sums)

    def backward_tick(running, tick_id):
        incoming, grad_sums, input_grads = running
        micro_id = micro_count - 1 - tick_id + (section_count - 1 - section_id)
        in_range = (micro_id >= 0) & (micro_id < micro_count)
        slot_id = jnp.clip(micro_id, 0, micro_count - 1)
        from_next = jnp.where(
            section_id == section_count - 1,
            lax.dynamic_index_in_dim(cotangent, slot_id, 0, False),
            incoming,
        )
        grad_out = jnp.where(in_range, from_next, jnp.zeros_like(from_next))
        section_in = lax.dynamic_index_in_dim(kept_inputs, slot_id, 0, False)
        attended = lax.dynamic_index_in_dim(kept_attended, slot_id, 0, False)
        totals = lax.dynamic_index_in_dim(kept_totals, slot_id, 0, False)
        lengths = lax.dynamic_index_in_dim(row_lengths, slot_id, 0, False)
        projected = lax.cond(attends, make_projected, skip_projected, section_in)
        all_keys = lax.all_gather(projected[:, D:], "seq", axis=0, tiled=True)
        middle = lax.cond(
            attends,
            middle_attention,
            middle_feed,
            section_in,
            grad_out,
            attended,
            totals,
            lengths,
            all_keys,
            projected,
        )
        extra = (lax.psum_scatter(middle[3], "seq", scatter_dimension=0, tiled=True),)
        section_grad, grad_sums = lax.cond(
            attends,
            finish_attention,
            finish_feed,
            section_in,
            grad_out,
            projected,
            middle,
            extra,
            lengths,
            grad_sums,
        )
        low_grad = section_grad.astype(jnp.bfloat16)
        input_grads = keep_slot(input_grads, low_grad, slot_id, in_range)
        incoming = passed_along(low_grad, "section", -1)
        return ((incoming, grad_sums, input_grads), None)

    grad_start = (
        jnp.zeros((D, 3 * D), jnp.float32),
        jnp.zeros((D, D), jnp.float32),
        jnp.zeros((D, FF), jnp.float32),
        jnp.zeros((FF, D), jnp.float32),
        jnp.zeros((3, D), jnp.float32),
        jnp.zeros((bias_count, D), jnp.float32),
        jnp.zeros((FF,), jnp.float32),
        jnp.zeros((2, FF), jnp.float32),
    )
    backward_start = (
        jnp.zeros((tok_rows, D), jnp.bfloat16),
        grad_start,
        jnp.zeros((micro_count, tok_rows, D), jnp.bfloat16),
    )
    backward_end, unused_back = lax.scan(backward_tick, backward_start, ticks)
    unused_grad, grad_sums, input_grads = backward_end
    shards = (
        lax.psum_scatter(grad_sums[0], "seq", scatter_dimension=0, tiled=True),
        lax.psum_scatter(grad_sums[1], "seq", scatter_dimension=0, tiled=True),
        lax.psum_scatter(grad_sums[2], "seq", scatter_dimension=0, tiled=True),
        lax.psum_scatter(grad_sums[3], "seq", scatter_dimension=0, tiled=True),
        lax.psum_scatter(grad_sums[4], "seq", scatter_dimension=1, tiled=True),
        lax.psum_scatter(grad_sums[5], "seq", scatter_dimension=1, tiled=True),
        lax.psum_scatter(grad_sums[6], "seq", scatter_dimension=0, tiled=True),
        lax.psum_scatter(grad_sums[7], "seq", scatter_dimension=1, tiled=True),
    )
    sources = (
        qkv_weight,
        out_weight,
        up_weight,
        down_weight,
        model_gains,
        model_biases,
        hidden_gains,
        hidden_biases,
    )
    placed = tuple(
        (
            lax.dynamic_update_index_in_dim(
                jnp.zeros(source.shape, jnp.float32), shard, layer_id, 0
            )
            for shard, source in zip(shards, sources)
        )
    )
    summed = (
        lax.psum(placed[0].astype(jnp.bfloat16), "section").astype(jnp.float32),
        lax.psum(placed[1].astype(jnp.bfloat16), "section").astype(jnp.float32),
        lax.psum(placed[2].astype(jnp.bfloat16), "section").astype(jnp.float32),
        lax.psum(placed[3].astype(jnp.bfloat16), "section").astype(jnp.float32),
        lax.psum(placed[4].astype(jnp.bfloat16), "section").astype(jnp.float32),
        lax.psum(placed[5].astype(jnp.bfloat16), "section").astype(jnp.float32),
        lax.psum(placed[6].astype(jnp.bfloat16), "section").astype(jnp.float32),
        lax.psum(placed[7].astype(jnp.bfloat16), "section").astype(jnp.float32),
    )
    layer_count = qkv_weight.shape[0]
    layer_terms = lax.dynamic_update_index_in_dim(
        jnp.zeros((layer_count, len(WIDTHS)), jnp.float32), log_sums, layer_id, 0
    )
    layer_picks = lax.dynamic_update_index_in_dim(
        jnp.zeros((layer_count, len(WIDTHS)), jnp.float32), pick_sums, layer_id, 0
    )
    log_totals, pick_totals = lax.psum((layer_terms, layer_picks), ("section", "seq"))
    pattern_means = log_totals / pick_totals
    return (
        outputs[None],
        input_grads[None],
        summed[0],
        summed[1],
        summed[2],
        summed[3],
        summed[4],
        summed[5],
        summed[6],
        summed[7],
        pattern_means,
    )


BF16 = jnp.bfloat16
F32 = jnp.float32
PAIRS = HEADS // 2
OWNERS = (0, 2, 3, 4, 5, 6)
TOKENS = 128
PAIR_LANES = 128
QUERY_STEP = 256
VEC_ROWS = 16
KERNEL_VMEM_BYTES = 62 * 1024 * 1024
SCALE = HEAD_DIM ** (-0.5)


def mul(left, right):
    return lax.dot_general(left, right, (((1,), (0,)), ((), ())), preferred_element_type=F32)


def mul_nt(left, right):
    return lax.dot_general(left, right, (((1,), (1,)), ((), ())), preferred_element_type=F32)


def mul_tn(left, right):
    return lax.dot_general(left, right, (((0,), (0,)), ((), ())), preferred_element_type=F32)


def standardize(values):
    center = values - jnp.mean(values, -1, keepdims=True)
    rstd = lax.rsqrt(jnp.mean(center * center, -1, keepdims=True) + EPSILON)
    return (center * rstd, rstd)


def norm_back(unit, rstd, unit_grad):
    first = jnp.mean(unit_grad, -1, keepdims=True)
    second = jnp.mean(unit_grad * unit, -1, keepdims=True)
    return rstd * (unit_grad - first - unit * second)


def remote(source, target, send_sem, recv_sem, axis, peer):
    return pltpu.make_async_remote_copy(
        src_ref=source,
        dst_ref=target,
        send_sem=send_sem,
        recv_sem=recv_sem,
        device_id={axis: peer},
        device_id_type=pl.DeviceIdType.MESH,
    )


def greet(axis, peers):
    barrier = pltpu.get_barrier_semaphore()
    for peer in peers:
        pl.semaphore_signal(
            barrier, inc=1, device_id={axis: peer}, device_id_type=pl.DeviceIdType.MESH
        )
    pl.semaphore_wait(barrier, len(peers))


def seq_peers(me, count):
    return [lax.rem(me + step, count) for step in range(1, count)]


def plane_peers(me):
    return [
        me,
        me + 1 - 2 * lax.rem(me, 2),
        lax.rem(me + 2, 4),
        3 - me,
    ]


def rows_of(block, size=TOKENS):
    return pl.ds(pl.multiple_of(block * size, size), size)


def gelu_parts(values):
    below = 0.5 * (1.0 + lax.erf(values * (0.5**0.5)))
    return (values * below, below)


def share_stats(columns, send, recv, send_sem, recv_sem, peers):
    send[...] = columns.T[0:8, :]
    recv[0] = send[...]
    copies = [
        remote(send, recv.at[k], send_sem.at[k], recv_sem.at[k], "section", peers[k])
        for k in range(1, 4)
    ]
    for copy in copies:
        copy.start()
    return copies


def two_columns(first, second):
    lane = lax.broadcasted_iota(jnp.int32, (first.shape[0], PAIR_LANES), 1)
    return jnp.where(lane == 0, first, jnp.where(lane == 1, second, 0.0))


def slot_rows(k):
    return slice(k * TOKENS, (k + 1) * TOKENS)


def shaped(shape, kind):
    return jax.ShapeDtypeStruct(shape, kind)


class Named:
    def __init__(self, groups, refs):
        names = [name for group in groups for name in group]
        for name, ref in zip(names, refs, strict=True):
            setattr(self, name, ref)


GROUP_TOKENS = 8 * TOKENS
WIDE = 4 * TOKENS
SHARD = D // 8
FORE_VMEM = dict(embeds=0, gains=0, biases=0, hgains=0, hbiases=0)
FORE_ANY = dict(qkv_w=0, out_w=0, up_w=0, down_w=0)
FORE_OUT = dict(
    sub=((4, TOKENS, D), BF16, True),
    streams=((4, TOKENS, D), BF16, True),
    att=((2, TOKENS, D), BF16, True),
    vecs=((2, VEC_ROWS, D), F32, True),
    picks=((2, GROUP_TOKENS, PAIR_LANES), BF16, True),
    logs=((8, PAIR_LANES), F32, True),
    wa_out=((2, 4, 4, 2, SHARD, D), BF16, False),
    wf_out=((2, 2, 4, 2, SHARD, D), BF16, False),
    qkv_out=((2, 3, GROUP_TOKENS, PAIR_LANES), BF16, False),
    pa_out=((2, GROUP_TOKENS, PAIR_LANES), F32, False),
    pt_out=((2, GROUP_TOKENS, PAIR_LANES), F32, False),
    hid_out=((2, WIDE, D), BF16, False),
    up_out=((2, WIDE, D), F32, False),
    stat_out=((2, WIDE, PAIR_LANES), F32, False),
)
FORE_SCRATCH = dict(
    wa=((2, 4, 4, 2, SHARD, D), BF16),
    wf=((2, 2, 4, 2, SHARD, D), BF16),
    qkv=((2, 3, GROUP_TOKENS, PAIR_LANES), BF16),
    pa=((2, GROUP_TOKENS, PAIR_LANES), F32),
    pt=((2, GROUP_TOKENS, PAIR_LANES), F32),
    hid=((2, WIDE, D), BF16),
    up=((2, WIDE, D), F32),
    stat=((2, WIDE, PAIR_LANES), F32),
    raw_up=((2, SHARD, FF), BF16),
    small_src=((2, 32, PAIR_LANES), BF16),
    small=((8, 2, 32, PAIR_LANES), BF16),
    hidden=((WIDE, D), BF16),
    proj_send=((4, PAIRS, TOKENS, PAIR_LANES), BF16),
    send=((PAIRS, 3, TOKENS, PAIR_LANES), BF16),
    att_send=((GROUP_TOKENS, PAIR_LANES), BF16),
    att_recv=((2, PAIRS, TOKENS, PAIR_LANES), BF16),
    active=((WIDE, D), F32),
    columns=((WIDE, PAIR_LANES), F32),
    stat_rows=((PAIR_LANES, WIDE), F32),
    part_send=((4, TOKENS, D), BF16),
    part_recv=((2, 4, TOKENS, D), BF16),
    stat_send=((8, WIDE), F32),
    stat_recv=((2, 4, 8, WIDE), F32),
)
FORE_SEMS = dict(
    load_sem=(2, 3),
    store_sem=(2, 8),
    small_s=(8,),
    small_r=(8,),
    az_s=(2, 4),
    az_r=(2, 4),
    asib_s=(2,),
    asib_r=(2,),
    axy_s=(2, 4),
    axy_r=(2, 4),
    axs_s=(2, 4),
    axs_r=(2, 4),
    fz_s=(2, 2, 4),
    fz_r=(2, 2, 4),
    fsib_s=(2, 2),
    fsib_r=(2, 2),
    wide_s=(4, PAIRS),
    wide_r=(3, 8),
    qkv_s=(PAIRS,),
    qkv_r=(8,),
    att_s=(2, 8),
    att_r=(2, PAIRS),
    hid_s=(2, 4),
    hid_r=(2, 4),
    stat_s=(2, 4),
    stat_r=(2, 4),
    part_s=(2, 4),
    part_r=(2, 4),
    sub_s=(4,),
    sub_r=(4,),
)


def square(ref):
    return ref[...].reshape(D, D)


def remote_both(source, target, send_sem, recv_sem, section, seq):
    return pltpu.make_async_remote_copy(
        src_ref=source,
        dst_ref=target,
        send_sem=send_sem,
        recv_sem=recv_sem,
        device_id=(section, seq),
        device_id_type=pl.DeviceIdType.MESH,
    )


def make_picks(lengths_ref, section, my_pair, picks_ref):
    tokens = lax.broadcasted_iota(jnp.int32, (GROUP_TOKENS, PAIR_LANES), 0)
    lane = lax.broadcasted_iota(jnp.int32, (GROUP_TOKENS, PAIR_LANES), 1)
    row_id = jnp.zeros_like(tokens)
    first = jnp.zeros_like(tokens)
    end = 0
    for row in range(lengths_ref.shape[1]):
        end = end + lengths_ref[section, row]
        passed = tokens >= end
        row_id = row_id + jnp.where(passed, 1, 0)
        first = jnp.where(passed, end, first)
    pos = (tokens - first).astype(F32)
    number = lax.shift_right_logical(lane, 2)
    row = lane - 4 * number
    ratio = jnp.zeros(lane.shape, F32)
    for i, each in enumerate(RATIOS):
        ratio = jnp.where(number == i, float(each), ratio)
    valid = ratio > 0.5
    ratio = jnp.where(valid, ratio, 1.0)

    def residue(values):
        return values - ratio * jnp.floor((values + 0.5) / ratio)

    residues = residue(pos)
    for head in range(2):
        wanted = residue(jnp.full(lane.shape, 2 * my_pair + head, jnp.int32).astype(F32))
        fits = valid & (row == row_id) & (jnp.abs(residues - wanted) < 0.5)
        picks_ref[head] = jnp.where(fits, 1.0, 0.0).astype(BF16)


def forward_kernel(lengths, *refs):
    b = Named([FORE_VMEM, FORE_ANY, FORE_OUT, FORE_SCRATCH, FORE_SEMS], refs)
    me = lax.axis_index("seq")
    section = lax.axis_index("section")
    peers = plane_peers(section)
    core = lax.rem(me, 2)
    chip = lax.div(me, 2)
    sibling = me + 1 - 2 * core
    is_owner = (me != 1) & (me != 7)
    my_pair = jnp.where(me == 0, 0, me - 1)
    my_pair = jnp.where(my_pair > PAIRS - 1, PAIRS - 1, my_pair)

    barrier = pltpu.get_barrier_semaphore()
    for other in range(4):
        for j in range(8):

            @pl.when((section != other) | (me != j))
            def _():
                pl.semaphore_signal(
                    barrier, inc=1, device_id=(other, j), device_id_type=pl.DeviceIdType.MESH
                )

    def load_block(layer):
        target = b.wa.at[layer, section, chip, core]

        def from_qkv():
            return pltpu.make_async_copy(
                b.qkv_w.at[layer, :, pl.ds(pl.multiple_of(lax.rem(section, 3) * D, D), D)],
                target,
                b.load_sem.at[layer, 0],
            )

        def from_out():
            return pltpu.make_async_copy(b.out_w.at[layer], target, b.load_sem.at[layer, 0])

        return from_qkv, from_out

    def load_up(layer):
        return pltpu.make_async_copy(b.up_w.at[layer], b.raw_up.at[layer], b.load_sem.at[layer, 1])

    def load_down(layer):
        return pltpu.make_async_copy(
            b.down_w.at[layer, pl.ds(pl.multiple_of(section * SHARD, SHARD), SHARD)],
            b.wf.at[layer, 1, chip, core],
            b.load_sem.at[layer, 2],
        )

    for layer in range(2):
        from_qkv, from_out = load_block(layer)

        @pl.when(section != 3)
        def _():
            from_qkv().start()

        @pl.when(section == 3)
        def _():
            from_out().start()

        load_up(layer).start()
        load_down(layer).start()

    def pick_up(layer):
        load_up(layer).wait()
        load_down(layer).wait()
        raw = b.raw_up[layer]
        for s in range(4):

            @pl.when(section == s)
            def _():
                b.wf[layer, 0, chip, core] = jnp.concatenate(
                    [
                        raw[:, (4 * j + s) * SHARD : (4 * j + s + 1) * SHARD].astype(F32)
                        for j in range(8)
                    ],
                    1,
                ).astype(BF16)

    def block_z(layer, step):
        target = lax.rem(chip + step, 4)
        return remote(
            b.wa.at[layer, section, chip, core],
            b.wa.at[layer, section, chip, core],
            b.az_s.at[layer, step],
            b.az_r.at[layer, step],
            "seq",
            2 * target + core,
        )

    def block_z_wait(layer):
        for step in range(1, 4):
            source = lax.rem(chip + 4 - step, 4)
            remote(
                b.wa.at[layer, section, source, core],
                b.wa.at[layer, section, source, core],
                b.az_s.at[layer, step],
                b.az_r.at[layer, step],
                "seq",
                2 * source + core,
            ).wait_recv()

    def plane_view(layer, slot, side):
        return b.wa.at[layer, slot, :, side]

    def block_sibling(layer, side):
        view = plane_view(layer, section, side)
        return remote(view, view, b.asib_s.at[layer], b.asib_r.at[layer], "seq", sibling)

    def block_plane(layer, k, slot):
        view = plane_view(layer, slot, core)
        return remote(view, view, b.axy_s.at[layer, k], b.axy_r.at[layer, k], "section", peers[k])

    def block_across(layer, k, side):
        view = plane_view(layer, peers[k], side)
        return remote(view, view, b.axs_s.at[layer, k], b.axs_r.at[layer, k], "seq", sibling)

    def feed_z(layer, which, step):
        target = lax.rem(chip + step, 4)
        return remote(
            b.wf.at[layer, which, chip, core],
            b.wf.at[layer, which, chip, core],
            b.fz_s.at[layer, which, step],
            b.fz_r.at[layer, which, step],
            "seq",
            2 * target + core,
        )

    def feed_z_start(layer, which):
        for step in range(1, 4):
            feed_z(layer, which, step).start()

    def feed_sibling(layer, which, side):
        view = b.wf.at[layer, which, :, side]
        return remote(
            view, view, b.fsib_s.at[layer, which], b.fsib_r.at[layer, which], "seq", sibling
        )

    def feed_z_pass(layer, which):
        for step in range(1, 4):
            source = lax.rem(chip + 4 - step, 4)
            remote(
                b.wf.at[layer, which, source, core],
                b.wf.at[layer, which, source, core],
                b.fz_s.at[layer, which, step],
                b.fz_r.at[layer, which, step],
                "seq",
                2 * source + core,
            ).wait_recv()
        feed_sibling(layer, which, core).start()

    def block_z_start(layer):
        from_qkv, from_out = load_block(layer)

        @pl.when(section != 3)
        def _():
            from_qkv().wait()

        @pl.when(section == 3)
        def _():
            from_out().wait()

        for step in range(1, 4):
            block_z(layer, step).start()

    for layer in range(2):
        gains = b.gains[layer].astype(F32)
        biases = b.biases[layer].astype(F32)
        hidden_gain = b.hgains[layer : layer + 1, :].astype(F32)
        hidden_bias = b.hbiases[layer].astype(F32)
        lines = [gains, biases]
        for each in (hidden_gain, hidden_bias[0:1, :], hidden_bias[1:2, :]):
            for s in range(4):
                lines.append(each[:, s * SHARD : (s + 1) * SHARD])
        lines.append(jnp.zeros((11, SHARD), F32))
        packed = jnp.concatenate(lines, 0)
        packed = jnp.concatenate([packed, jnp.zeros((32, PAIR_LANES - SHARD), F32)], 1)
        b.small_src[layer] = packed.astype(BF16)
    b.small[me] = b.small_src[...]
    pl.semaphore_wait(barrier, 31)

    def small_copy(step):
        return remote(
            b.small_src,
            b.small.at[me],
            b.small_s.at[step],
            b.small_r.at[step],
            "seq",
            lax.rem(me + step, 8),
        )

    for step in range(1, 8):
        small_copy(step).start()
    block_z_start(0)
    make_picks(lengths, section, my_pair, b.picks)
    pick_up(0)
    for step in range(1, 8):
        source = lax.rem(me + 8 - step, 8)
        remote(
            b.small_src,
            b.small.at[source],
            b.small_s.at[step],
            b.small_r.at[step],
            "seq",
            source,
        ).wait_recv()
    for layer in range(2):
        pieces = []
        for j in range(8):
            block = b.small[j, layer].astype(F32)
            lines = [block[0:9]]
            for third in range(3):
                line = jnp.zeros((1, PAIR_LANES), F32)
                for s in range(4):
                    at = 9 + 4 * third + s
                    line = line + jnp.where(section == s, block[at : at + 1], 0.0)
                lines.append(line)
            lines.append(jnp.zeros((4, PAIR_LANES), F32))
            pieces.append(jnp.concatenate(lines, 0)[:, 0:SHARD])
        b.vecs[layer] = jnp.concatenate(pieces, 1)
    b.logs[...] = jnp.zeros_like(b.logs)

    def send_sub(number):
        @pl.when(section != number)
        def _():
            sub_copy(number).start()

        @pl.when(section == number)
        def _():
            b.sub[section] = b.streams[number]

    def sub_copy(number):
        return remote(
            b.streams.at[number],
            b.sub.at[section],
            b.sub_s.at[number],
            b.sub_r.at[section],
            "section",
            number,
        )

    def back_copy(layer, target):
        return remote(
            b.att_send.at[pl.ds(target * TOKENS, TOKENS)],
            b.att_recv.at[layer, my_pair],
            b.att_s.at[layer, target],
            b.att_r.at[layer, my_pair],
            "seq",
            target,
        )

    def attend(layer):
        lane = lax.broadcasted_iota(jnp.int32, (QUERY_STEP, PAIR_LANES), 1)
        first_half = lane < HEAD_DIM
        for step in range(GROUP_TOKENS // QUERY_STEP):
            start = step * QUERY_STEP
            keys_end = start + QUERY_STEP
            rows = slice(start, keys_end)
            query = b.qkv[layer, 0, rows, :] * jnp.asarray(SCALE, BF16)
            keys = b.qkv[layer, 1, 0:keys_end, :]
            values = b.qkv[layer, 2, 0:keys_end, :]
            causal = lax.broadcasted_iota(jnp.int32, (QUERY_STEP, keys_end), 1) <= (
                start + lax.broadcasted_iota(jnp.int32, (QUERY_STEP, keys_end), 0)
            )
            sums = []
            totals = []
            logs = jnp.zeros((1, PAIR_LANES), F32)
            picked_sum = jnp.zeros((1, PAIR_LANES), F32)
            for head in range(2):
                mine = first_half if head == 0 else ~first_half
                own_query = jnp.where(mine, query, jnp.zeros_like(query))
                scores = mul_nt(own_query, keys)
                raised = jnp.where(causal, jnp.exp(scores), 0.0)
                pick_query = b.picks[head, rows, :]
                pick_keys = b.picks[head, 0:keys_end, :]
                counts = mul_nt(pick_query, pick_keys)
                weighted = (raised * counts).astype(BF16)
                sums.append(mul(weighted, values))
                pattern = mul(raised.astype(BF16), pick_keys)
                picked = pick_query.astype(F32)
                totals.append(jnp.sum(pattern * picked, -1, keepdims=True))
                chosen = picked > 0.5
                logs = logs + jnp.sum(
                    jnp.where(chosen, jnp.log(jnp.where(chosen, pattern, 1.0)), 0.0),
                    0,
                    keepdims=True,
                )
                picked_sum = picked_sum + jnp.sum(picked, 0, keepdims=True)
            b.logs[layer : layer + 1, :] += logs
            if layer == 0:
                b.logs[2:3, :] += picked_sum
            total = jnp.where(first_half, totals[0], totals[1])
            attended = jnp.where(first_half, sums[0], sums[1]) / total
            b.pa[layer, rows, :] = attended
            b.pt[layer, rows, :] = total
            b.att_send[rows, :] = attended.astype(BF16)
            for target in (2 * step, 2 * step + 1):

                @pl.when(me != target)
                def _():
                    back_copy(layer, target).start()

                @pl.when(me == target)
                def _():
                    b.att_recv[layer, my_pair] = b.att_send[
                        target * TOKENS : (target + 1) * TOKENS, :
                    ]

    def attention_end(layer, inputs):
        vec = b.vecs.at[layer]
        for pair, owner in enumerate(OWNERS):

            @pl.when(me != owner)
            def _():
                remote(
                    b.att_send.at[pl.ds(0, TOKENS)],
                    b.att_recv.at[layer, pair],
                    b.att_s.at[layer, 0],
                    b.att_r.at[layer, pair],
                    "seq",
                    owner,
                ).wait_recv()

            b.att[layer, :, pair * PAIR_LANES : (pair + 1) * PAIR_LANES] = b.att_recv[layer, pair]
        inner_unit, unused = standardize(b.att[layer].astype(F32))
        inner = (inner_unit * vec[1:2, :] + vec[4:5, :]).astype(BF16)
        branch = mul(inner, square(b.wa.at[layer, 3])) + vec[7:8, :]
        b.streams[2 * layer] = (inputs + branch).astype(BF16)
        send_sub(2 * layer)

        @pl.when(is_owner)
        def _():
            for target in range(8):

                @pl.when(me != target)
                def _():
                    back_copy(layer, target).wait_send()

    def feed(layer, waiting, resting):
        vec = b.vecs.at[layer]
        inputs = b.streams[2 * layer].astype(F32)
        unit, unused = standardize(inputs)
        b.hid[layer, slot_rows(0), :] = (unit * vec[2:3, :] + vec[5:6, :]).astype(BF16)
        hidden_copies = [
            remote(
                b.hid.at[layer, pl.ds(0, TOKENS)],
                b.hid.at[layer, pl.ds(k * TOKENS, TOKENS)],
                b.hid_s.at[layer, k],
                b.hid_r.at[layer, k],
                "section",
                peers[k],
            )
            for k in range(1, 4)
        ]
        for copy in hidden_copies:
            copy.start()
        waiting()
        feed_sibling(layer, 0, 1 - core).wait_recv()
        for k in range(4):
            if k > 0:
                hidden_copies[k - 1].wait_recv()
            upward = mul(b.hid[layer, slot_rows(k), :], square(b.wf.at[layer, 0])) + vec[10:11, :]
            b.up[layer, slot_rows(k), :] = upward
            values, unused = gelu_parts(upward)
            b.active[slot_rows(k), :] = values
            mean = jnp.mean(values, -1, keepdims=True)
            center = values - mean
            b.columns[slot_rows(k), :] = two_columns(
                mean, jnp.sum(center * center, -1, keepdims=True)
            )
        stat_copies = share_stats(
            b.columns[...],
            b.stat_send,
            b.stat_recv.at[layer],
            b.stat_s.at[layer],
            b.stat_r.at[layer],
            peers,
        )
        resting()
        for copy in stat_copies:
            copy.wait_recv()
        b.stat_rows[...] = jnp.zeros((PAIR_LANES, WIDE), F32)
        for k in range(4):
            means = [b.stat_recv[layer, other, 0:1, slot_rows(k ^ other)] for other in range(4)]
            squares = [b.stat_recv[layer, other, 1:2, slot_rows(k ^ other)] for other in range(4)]
            mean = (means[0] + means[1] + means[2] + means[3]) * 0.25
            spread = squares[0] + squares[1] + squares[2] + squares[3]
            for each in means:
                spread = spread + D * (each - mean) * (each - mean)
            b.stat_rows[0:1, slot_rows(k)] = mean
            b.stat_rows[1:2, slot_rows(k)] = lax.rsqrt(spread * (1.0 / FF) + EPSILON)
        b.stat[layer] = b.stat_rows[...].T
        feed_sibling(layer, 1, 1 - core).wait_recv()
        branch = None
        part_copies = []
        for k in (1, 2, 3, 0):
            both = b.stat[layer, slot_rows(k), :]
            inner = (
                (b.active[slot_rows(k), :] - both[:, 0:1]) * both[:, 1:2] * vec[9:10, :]
                + vec[11:12, :]
            ).astype(BF16)
            part = mul(inner, square(b.wf.at[layer, 1]))
            if k == 0:
                branch = part
            else:
                b.part_send[k] = part.astype(BF16)
                part_copies.append(
                    remote(
                        b.part_send.at[k],
                        b.part_recv.at[layer, k],
                        b.part_s.at[layer, k],
                        b.part_r.at[layer, k],
                        "section",
                        peers[k],
                    )
                )
                part_copies[-1].start()
        for k in range(1, 4):
            part_copies[k - 1].wait_recv()
            branch = branch + b.part_recv[layer, k].astype(F32)
        b.streams[2 * layer + 1] = (inputs + branch + vec[8:9, :]).astype(BF16)
        send_sub(2 * layer + 1)
        for copy in hidden_copies + stat_copies + part_copies:
            copy.wait_send()

    def stores(layer, chosen):
        pairs = (
            (b.wa, b.wa_out),
            (b.wf, b.wf_out),
            (b.qkv, b.qkv_out),
            (b.pa, b.pa_out),
            (b.pt, b.pt_out),
            (b.hid, b.hid_out),
            (b.up, b.up_out),
            (b.stat, b.stat_out),
        )
        return [
            pltpu.make_async_copy(source.at[layer], target.at[layer], b.store_sem.at[layer, i])
            for i, (source, target) in enumerate(pairs)
            if i in chosen
        ]

    first = b.vecs.at[0]
    for micro in range(4):
        unit, unused = standardize(b.embeds[micro].astype(F32))
        b.hidden[slot_rows(micro), :] = (unit * first[0:1, :] + first[3:4, :]).astype(BF16)
    block_z_wait(0)
    block_sibling(0, core).start()

    @pl.when(section == 3)
    def _():
        for k in range(1, 4):
            block_plane(0, k, section).start()

    feed_z_start(0, 0)
    block_sibling(0, 1 - core).wait_recv()

    def wide_copy(micro, pair):
        return remote_both(
            b.proj_send.at[micro, pair],
            b.qkv.at[0, lax.rem(section, 3), rows_of(me)],
            b.wide_s.at[micro, pair],
            b.wide_r.at[lax.rem(section, 3), me],
            micro,
            OWNERS[pair],
        )

    @pl.when(section != 3)
    def _():
        bias = jnp.where(section == 2, first[6:7, :], 0.0)
        for micro in range(4):
            part = mul(b.hidden[slot_rows(micro), :], square(b.wa.at[0, section])) + bias
            part = part.astype(BF16)
            for pair, owner in enumerate(OWNERS):
                b.proj_send[micro, pair] = part[:, pair * PAIR_LANES : (pair + 1) * PAIR_LANES]
                local = (section == micro) & (me == owner)

                @pl.when(~local)
                def _():
                    wide_copy(micro, pair).start()

                @pl.when(local)
                def _():
                    b.qkv[0, section, rows_of(me), :] = b.proj_send[micro, pair]

    @pl.when(is_owner)
    def _():
        for block in range(3):
            for source in range(8):

                @pl.when((section != block) | (me != source))
                def _():
                    remote_both(
                        b.proj_send.at[0, 0],
                        b.qkv.at[0, block, pl.ds(source * TOKENS, TOKENS)],
                        b.wide_s.at[0, 0],
                        b.wide_r.at[block, source],
                        block,
                        source,
                    ).wait_recv()

    feed_z_start(0, 1)

    @pl.when(is_owner)
    def _():
        attend(0)

    feed_z_pass(0, 0)
    for k in range(1, 4):

        @pl.when(peers[k] == 3)
        def _():
            block_plane(0, k, peers[k]).wait_recv()
            block_across(0, k, core).start()

    block_z_start(1)
    for k in range(1, 4):

        @pl.when(peers[k] == 3)
        def _():
            block_across(0, k, 1 - core).wait_recv()

    attention_end(0, b.embeds[section].astype(F32))

    @pl.when(section != 3)
    def _():
        for micro in range(4):
            for pair, owner in enumerate(OWNERS):

                @pl.when((section != micro) | (me != owner))
                def _():
                    wide_copy(micro, pair).wait_send()

    def waiting():
        feed_z_pass(0, 1)
        pick_up(1)

    def resting():
        block_z_wait(1)
        block_sibling(1, core).start()
        for k in range(1, 4):
            block_plane(1, k, section).start()
        feed_z_start(1, 0)

    feed(0, waiting, resting)
    for copy in stores(0, range(2, 8)):
        copy.start()

    second = b.vecs.at[1]
    inputs = b.streams[1].astype(F32)
    unit, unused = standardize(inputs)
    own_hidden = (unit * second[0:1, :] + second[3:4, :]).astype(BF16)
    block_sibling(1, 1 - core).wait_recv()
    for k in range(1, 4):
        block_plane(1, k, peers[k]).wait_recv()
        block_across(1, k, core).start()
    for k in range(1, 4):
        block_across(1, k, 1 - core).wait_recv()
    for block in range(3):
        part = mul(own_hidden, square(b.wa.at[1, block]))
        if block == 2:
            part = part + second[6:7, :]
        part = part.astype(BF16)
        for pair in range(PAIRS):
            b.send[pair, block] = part[:, pair * PAIR_LANES : (pair + 1) * PAIR_LANES]

    def out_copy(pair):
        return remote(
            b.send.at[pair],
            b.qkv.at[1, :, rows_of(me)],
            b.qkv_s.at[pair],
            b.qkv_r.at[me],
            "seq",
            OWNERS[pair],
        )

    for pair, owner in enumerate(OWNERS):

        @pl.when(me != owner)
        def _():
            out_copy(pair).start()

        @pl.when(me == owner)
        def _():
            b.qkv[1, :, rows_of(me), :] = b.send[pair]

    @pl.when(is_owner)
    def _():
        for source in range(8):

            @pl.when(me != source)
            def _():
                remote(
                    b.send.at[0],
                    b.qkv.at[1, :, pl.ds(source * TOKENS, TOKENS)],
                    b.qkv_s.at[0],
                    b.qkv_r.at[source],
                    "seq",
                    source,
                ).wait_recv()

    feed_z_start(1, 1)

    @pl.when(section != 3)
    def _():
        for k in range(1, 4):
            block_plane(0, k, section).start()

    @pl.when(is_owner)
    def _():
        attend(1)

    feed_z_pass(1, 0)
    attention_end(1, inputs)
    for pair, owner in enumerate(OWNERS):

        @pl.when(me != owner)
        def _():
            out_copy(pair).wait_send()

    def waiting_last():
        feed_z_pass(1, 1)
        for k in range(1, 4):

            @pl.when(peers[k] != 3)
            def _():
                block_plane(0, k, peers[k]).wait_recv()
                block_across(0, k, core).start()

    def resting_last():
        for copy in stores(1, (0, 2, 3, 4)):
            copy.start()
        for k in range(1, 4):

            @pl.when(peers[k] != 3)
            def _():
                block_across(0, k, 1 - core).wait_recv()

        for copy in stores(0, (0, 1)):
            copy.start()

    feed(1, waiting_last, resting_last)
    for copy in stores(1, (1, 5, 6, 7)):
        copy.start()
    for source in range(4):

        @pl.when(section != source)
        def _():
            remote(
                b.streams.at[0],
                b.sub.at[source],
                b.sub_s.at[0],
                b.sub_r.at[source],
                "section",
                source,
            ).wait_recv()

    for number in range(4):

        @pl.when(section != number)
        def _():
            sub_copy(number).wait_send()

    for step in range(1, 8):
        small_copy(step).wait_send()
    for layer in range(2):
        block_sibling(layer, core).wait_send()
        for step in range(1, 4):
            block_z(layer, step).wait_send()
            for which in range(2):
                feed_z(layer, which, step).wait_send()
        for which in range(2):
            feed_sibling(layer, which, core).wait_send()
        for k in range(1, 4):
            block_plane(layer, k, section).wait_send()
            block_across(layer, k, core).wait_send()
        for copy in stores(layer, range(8)):
            copy.wait()


def run_forward(number, lengths, near, far):
    vmem = pl.BlockSpec(memory_space=pltpu.VMEM)
    anywhere = pl.BlockSpec(memory_space=pl.ANY)
    return pl.pallas_call(
        forward_kernel,
        name="forward",
        out_shape=[shaped(out[0], out[1]) for out in FORE_OUT.values()],
        in_specs=[pl.BlockSpec(memory_space=pltpu.SMEM)]
        + [vmem] * len(FORE_VMEM)
        + [anywhere] * len(FORE_ANY),
        out_specs=[vmem if out[2] else anywhere for out in FORE_OUT.values()],
        scratch_shapes=[pltpu.VMEM(item[0], item[1]) for item in FORE_SCRATCH.values()]
        + [pltpu.SemaphoreType.DMA(item) for item in FORE_SEMS.values()],
        compiler_params=pltpu.CompilerParams(
            collective_id=number, has_side_effects=True, vmem_limit_bytes=KERNEL_VMEM_BYTES
        ),
        cost_estimate=pl.CostEstimate(
            flops=10**10, bytes_accessed=100_000_000, transcendentals=0
        ),
    )(lengths, *near, *far)


BACK_VMEM = dict(cotangent=0, embeds=0, x_in=0, att=0, vecs=0, picks=0, logs=0)
BACK_ANY = dict(
    wa_in=0, wf_in=0, qkv_in=0, pa_in=0, pt_in=0, hid_in=0, up_in=0, stat_in=0
)
BACK_OUT = dict(
    sub=((4, TOKENS, D), BF16, True),
    qkv_out=((2, SHARD, 3 * D), F32, False),
    out_out=((2, SHARD, D), F32, False),
    up_out=((2, SHARD, FF), F32, False),
    down_out=((2, 4 * SHARD, D), F32, False),
    gain_out=((2, 3, SHARD), F32, True),
    bias_out=((2, 6, SHARD), F32, True),
    hidden_out=((2, 3, 4 * SHARD), F32, True),
    means_out=((2, 5), F32, True),
)
BACK_SCRATCH = dict(
    wa=((4, 4, 2, SHARD, D), BF16),
    wf=((2, 4, 2, SHARD, D), BF16),
    qkv=((3, GROUP_TOKENS, PAIR_LANES), BF16),
    pa=((GROUP_TOKENS, PAIR_LANES), F32),
    pt=((GROUP_TOKENS, PAIR_LANES), F32),
    hid=((WIDE, D), BF16),
    up=((WIDE, D), F32),
    stat=((WIDE, PAIR_LANES), F32),
    streams=((4, TOKENS, D), BF16),
    grads=((WIDE, D), BF16),
    units=((WIDE, D), F32),
    unit_grads=((WIDE, D), F32),
    inners=((WIDE, D), BF16),
    lows=((WIDE, D), BF16),
    columns=((WIDE, PAIR_LANES), F32),
    stat_rows=((PAIR_LANES, WIDE), F32),
    part_send=((4, TOKENS, D), BF16),
    part_recv=((4, TOKENS, D), BF16),
    stat_send=((8, WIDE), F32),
    stat_recv=((4, 8, WIDE), F32),
    do_send=((PAIRS, TOKENS, PAIR_LANES), BF16),
    do_recv=((GROUP_TOKENS, PAIR_LANES), BF16),
    key_sum=((GROUP_TOKENS, PAIR_LANES), F32),
    value_sum=((GROUP_TOKENS, PAIR_LANES), F32),
    d_send=((GROUP_TOKENS, 3 * PAIR_LANES), BF16),
    d_recv=((PAIRS, TOKENS, 3 * PAIR_LANES), BF16),
    left_src=((2, TOKENS, D), BF16),
    right_src=((4, TOKENS, D), BF16),
    left=((WIDE, D), BF16),
    right=((WIDE, D), BF16),
    vec_rows=((2, PAIR_LANES, D), F32),
    prod_f=((4, 2, 4, SHARD, D), BF16),
    prod_a=((2, 2, 4, SHARD, D + PAIR_LANES), BF16),
    pair_f=((4, 4, SHARD, D), BF16),
    pair_a=((2, 4, SHARD, D + PAIR_LANES), BF16),
    line_f=((4, 3, SHARD, D), BF16),
    line_a=((2, 3, SHARD, D + PAIR_LANES), BF16),
    all_f=((4, 4, SHARD, D), BF16),
    all_a=((2, 4, SHARD, D + PAIR_LANES), BF16),
    stage_a=((SHARD, 4 * D), F32),
    stage_u=((SHARD, FF), F32),
    stage_d=((4 * SHARD, D), F32),
    log_line=((8, 8, PAIR_LANES), F32),
    log_plane=((4, 8, PAIR_LANES), F32),
)
BACK_SEMS = dict(
    load_sem=(16,),
    store_sem=(4,),
    g_s=(2, 4),
    g_r=(2, 4),
    stat_s=(2, 4),
    stat_r=(2, 4),
    part_s=(2, 4),
    part_r=(2, 4),
    do_s=(2, PAIRS),
    do_r=(2, 8),
    d_s=(2, 8),
    d_r=(2, PAIRS),
    left_s=(2, 4),
    left_r=(2, 4),
    right_s=(2, 4),
    right_r=(2, 4),
    sub_s=(4,),
    sub_r=(4,),
    pair_s=(6,),
    pair_r=(6,),
    line_s=(6, 3),
    line_r=(6, 3),
    all_s=(6, 4),
    all_r=(6, 4),
    log_s=(8,),
    log_r=(8,),
    log_plane_s=(4,),
    log_plane_r=(4,),
)


def backward_kernel(*refs):
    b = Named([BACK_VMEM, BACK_ANY, BACK_OUT, BACK_SCRATCH, BACK_SEMS], refs)
    me = lax.axis_index("seq")
    section = lax.axis_index("section")
    peers = plane_peers(section)
    core = lax.rem(me, 2)
    chip = lax.div(me, 2)
    sibling = me + 1 - 2 * core
    is_owner = (me != 1) & (me != 7)
    my_pair = jnp.where(me == 0, 0, me - 1)
    my_pair = jnp.where(my_pair > PAIRS - 1, PAIRS - 1, my_pair)

    barrier = pltpu.get_barrier_semaphore()
    for peer in seq_peers(me, 8):
        pl.semaphore_signal(
            barrier, inc=1, device_id={"seq": peer}, device_id_type=pl.DeviceIdType.MESH
        )
    for peer in peers[1:]:
        pl.semaphore_signal(
            barrier, inc=1, device_id={"section": peer}, device_id_type=pl.DeviceIdType.MESH
        )

    def loads(layer, first, pairs):
        return [
            pltpu.make_async_copy(
                source.at[layer], target, b.load_sem.at[8 * layer + first + number]
            )
            for number, (source, target) in enumerate(pairs)
        ]

    def feed_loads(layer):
        pairs = ((b.wf_in, b.wf), (b.hid_in, b.hid), (b.up_in, b.up), (b.stat_in, b.stat))
        return loads(layer, 0, pairs)

    def attention_loads(layer):
        pairs = ((b.wa_in, b.wa), (b.qkv_in, b.qkv), (b.pa_in, b.pa), (b.pt_in, b.pt))
        return loads(layer, 4, pairs)

    for copy in feed_loads(1) + attention_loads(1):
        copy.start()
    b.log_line[me] = b.logs[...]
    pl.semaphore_wait(barrier, 10)

    def log_copy(step):
        return remote(
            b.logs,
            b.log_line.at[me],
            b.log_s.at[step],
            b.log_r.at[step],
            "seq",
            lax.rem(me + step, 8),
        )

    def log_plane_copy(k, slot):
        return remote(
            b.log_plane.at[slot],
            b.log_plane.at[slot],
            b.log_plane_s.at[k],
            b.log_plane_r.at[k],
            "section",
            peers[k],
        )

    def sum_logs():
        for step in range(1, 8):
            source = lax.rem(me + 8 - step, 8)
            remote(
                b.logs,
                b.log_line.at[source],
                b.log_s.at[step],
                b.log_r.at[step],
                "seq",
                source,
            ).wait_recv()
        total = b.log_line[0]
        for j in range(1, 8):
            total = total + b.log_line[j]
        b.log_plane[section] = total
        for k in range(1, 4):
            log_plane_copy(k, section).start()

    def finish_logs():
        for k in range(1, 4):
            log_plane_copy(k, peers[k]).wait_recv()
        total = b.log_plane[0]
        for other in range(1, 4):
            total = total + b.log_plane[other]
        lane = lax.broadcasted_iota(jnp.int32, (8, PAIR_LANES), 1)
        number = lax.shift_right_logical(lane, 2)
        lines = jnp.zeros((8, PAIR_LANES), F32)
        for i in range(5):
            part = jnp.sum(jnp.where(number == i, total, 0.0), -1, keepdims=True)
            lines = lines + jnp.where(lane == i, part, 0.0)
        means = lines[0:2, :] / jnp.where(lane[0:2, :] < 5, lines[2:3, :], 1.0)
        b.means_out[...] = means[:, 0:5]
        for step in range(1, 8):
            log_copy(step).wait_send()
        for k in range(1, 4):
            log_plane_copy(k, section).wait_send()

    for step in range(1, 8):
        log_copy(step).start()

    def matrix(number):
        layer, which = divmod(number, 3)
        if which == 2:
            return (b.prod_a, b.pair_a, b.line_a, b.all_a, layer, D + PAIR_LANES)
        return (b.prod_f, b.pair_f, b.line_f, b.all_f, 2 * layer + which, D)

    def store_product(number, value):
        prod, unused_pair, unused_line, unused_all, i, unused_width = matrix(number)
        for j in range(8):
            prod[i, j % 2, j // 2, :, 0:D] = value[j * SHARD : (j + 1) * SHARD, :].astype(BF16)

    def pair_copy(number):
        prod, pair, unused_line, unused_all, i, unused_width = matrix(number)
        return remote(
            prod.at[i, 1 - core],
            pair.at[i],
            b.pair_s.at[number],
            b.pair_r.at[number],
            "seq",
            sibling,
        )

    def line_copy(number, step):
        prod, unused_pair, line, unused_all, i, unused_width = matrix(number)
        target = lax.rem(chip + step, 4)
        return remote(
            prod.at[i, core, target],
            line.at[i, step - 1],
            b.line_s.at[number, step - 1],
            b.line_r.at[number, step - 1],
            "seq",
            2 * target + core,
        )

    def all_copy(number, k, slot):
        unused_prod, unused_pair, unused_line, whole, i, unused_width = matrix(number)
        return remote(
            whole.at[i, slot],
            whole.at[i, slot],
            b.all_s.at[number, k],
            b.all_r.at[number, k],
            "section",
            peers[k],
        )

    def sum_pair(number):
        prod, pair, unused_line, unused_all, i, unused_width = matrix(number)
        pair_copy(number).wait_recv()
        for block in range(4):
            prod[i, core, block] = (
                prod[i, core, block].astype(F32) + pair[i, block].astype(F32)
            ).astype(BF16)
        for step in range(1, 4):
            line_copy(number, step).start()

    def sum_line(number):
        prod, unused_pair, line, whole, i, unused_width = matrix(number)
        total = prod[i, core, chip].astype(F32)
        for step in range(1, 4):
            line_copy(number, step).wait_recv()
            total = total + line[i, step - 1].astype(F32)
        whole[i, section] = total.astype(BF16)
        for k in range(1, 4):
            all_copy(number, k, section).start()

    def store_copies(number):
        layer, which = divmod(number, 3)
        if which == 2:
            return [
                pltpu.make_async_copy(
                    b.stage_a.at[:, pl.ds(0, 3 * D)], b.qkv_out.at[1 - layer], b.store_sem.at[0]
                ),
                pltpu.make_async_copy(
                    b.stage_a.at[:, pl.ds(3 * D, D)], b.out_out.at[1 - layer], b.store_sem.at[1]
                ),
            ]
        if which == 0:
            return [pltpu.make_async_copy(b.stage_u, b.up_out.at[1 - layer], b.store_sem.at[2])]
        return [pltpu.make_async_copy(b.stage_d, b.down_out.at[1 - layer], b.store_sem.at[3])]

    def finish(number):
        unused_prod, unused_pair, unused_line, whole, i, unused_width = matrix(number)
        layer, which = divmod(number, 3)
        for k in range(1, 4):
            all_copy(number, k, peers[k]).wait_recv()
        if layer == 1:
            for copy in store_copies(number - 3):
                copy.wait()
        if which == 1:
            for source in range(4):
                b.stage_d[source * SHARD : (source + 1) * SHARD, :] = whole[i, source].astype(F32)
        elif which == 0:
            for j in range(8):
                b.stage_u[:, j * 4 * SHARD : (j + 1) * 4 * SHARD] = jnp.concatenate(
                    [
                        whole[i, source, :, j * SHARD : (j + 1) * SHARD].astype(F32)
                        for source in range(4)
                    ],
                    1,
                )
        else:
            for source in range(4):
                b.stage_a[:, source * D : (source + 1) * D] = whole[i, source, :, 0:D].astype(F32)
            lines = []
            for source in range(4):
                tail = whole[i, source, :, D : D + PAIR_LANES].astype(F32)
                tail = jnp.concatenate([tail, jnp.zeros((PAIR_LANES - SHARD, PAIR_LANES), F32)], 0)
                lines.append(tail.T)
            model = lines[0] + lines[1] + lines[2] + lines[3]
            b.gain_out[1 - layer] = model[0:3, 0:SHARD]
            b.bias_out[1 - layer] = model[3:9, 0:SHARD]
            b.hidden_out[1 - layer] = jnp.concatenate([each[9:12, 0:SHARD] for each in lines], 1)
        for copy in store_copies(number):
            copy.start()

    def sub_copy(number):
        return remote(
            b.streams.at[number],
            b.sub.at[section],
            b.sub_s.at[number],
            b.sub_r.at[section],
            "section",
            number,
        )

    def send_sub(number):
        @pl.when(section != number)
        def _():
            sub_copy(number).start()

        @pl.when(section == number)
        def _():
            b.sub[section] = b.streams[number]

    def feed_phase(layer, grad_ref, x_ref, early, middle, late):
        phase = 1 - layer
        vec = b.vecs.at[layer]
        rows = b.vec_rows.at[layer]
        up_number = 3 * phase
        down_number = 3 * phase + 1
        b.grads[slot_rows(0), :] = grad_ref[...]
        grad_copies = [
            remote(
                b.grads.at[pl.ds(0, TOKENS)],
                b.grads.at[pl.ds(k * TOKENS, TOKENS)],
                b.g_s.at[phase, k],
                b.g_r.at[phase, k],
                "section",
                peers[k],
            )
            for k in range(1, 4)
        ]
        for copy in grad_copies:
            copy.start()
        rows[...] = jnp.zeros((PAIR_LANES, D), F32)
        early()
        for copy in feed_loads(layer):
            copy.wait()
        gain_sum = jnp.zeros((1, D), F32)
        bias_sum = jnp.zeros((1, D), F32)
        for k in range(4):
            both = b.stat[slot_rows(k), :]
            upward = b.up[slot_rows(k), :]
            values, below = gelu_parts(upward)
            b.up[slot_rows(k), :] = below + upward * (
                jnp.exp(-0.5 * upward * upward) * (0.5 / 3.141592653589793) ** 0.5
            )
            unit = (values - both[:, 0:1]) * both[:, 1:2]
            b.units[slot_rows(k), :] = unit
            b.inners[slot_rows(k), :] = (unit * vec[9:10, :] + vec[11:12, :]).astype(BF16)
            if k > 0:
                grad_copies[k - 1].wait_recv()
            inner_grad = mul_nt(b.grads[slot_rows(k), :], square(b.wf.at[1]))
            gain_sum = gain_sum + jnp.sum(inner_grad * unit, 0, keepdims=True)
            bias_sum = bias_sum + jnp.sum(inner_grad, 0, keepdims=True)
            unit_grad = inner_grad * vec[9:10, :]
            b.unit_grads[slot_rows(k), :] = unit_grad
            b.columns[slot_rows(k), :] = two_columns(
                jnp.sum(unit_grad, -1, keepdims=True), jnp.sum(unit_grad * unit, -1, keepdims=True)
            )
        stat_copies = share_stats(
            b.columns[...],
            b.stat_send,
            b.stat_recv,
            b.stat_s.at[phase],
            b.stat_r.at[phase],
            peers,
        )
        rows[9:10, :] = gain_sum
        rows[11:12, :] = bias_sum
        store_product(down_number, mul_tn(b.inners[...], b.grads[...]))
        pair_copy(down_number).start()
        middle()
        for copy in stat_copies:
            copy.wait_recv()
        b.stat_rows[...] = jnp.zeros((PAIR_LANES, WIDE), F32)
        for k in range(4):
            for line in range(2):
                parts = [
                    b.stat_recv[source, line : line + 1, slot_rows(k ^ source)]
                    for source in range(4)
                ]
                b.stat_rows[line : line + 1, slot_rows(k)] = (
                    parts[0] + parts[1] + parts[2] + parts[3]
                ) * (1.0 / FF)
        b.columns[...] = b.stat_rows[...].T
        hidden_grad = None
        low_sum = jnp.zeros((1, D), F32)
        part_copies = []
        for k in (1, 2, 3, 0):
            rstd = b.stat[slot_rows(k), :][:, 1:2]
            both = b.columns[slot_rows(k), :]
            low = (
                rstd
                * (
                    b.unit_grads[slot_rows(k), :]
                    - both[:, 0:1]
                    - b.units[slot_rows(k), :] * both[:, 1:2]
                )
                * b.up[slot_rows(k), :]
            ).astype(BF16)
            b.lows[slot_rows(k), :] = low
            low_sum = low_sum + jnp.sum(low.astype(F32), 0, keepdims=True)
            part = mul_nt(low, square(b.wf.at[0]))
            if k == 0:
                hidden_grad = part
            else:
                b.part_send[k] = part.astype(BF16)
                part_copies.append(
                    remote(
                        b.part_send.at[k],
                        b.part_recv.at[k],
                        b.part_s.at[phase, k],
                        b.part_r.at[phase, k],
                        "section",
                        peers[k],
                    )
                )
                part_copies[-1].start()
        rows[10:11, :] = low_sum
        store_product(up_number, mul_tn(b.hid[...], b.lows[...]))
        pair_copy(up_number).start()
        unit, rstd = standardize(x_ref[...].astype(F32))
        for k in range(1, 4):
            part_copies[k - 1].wait_recv()
            hidden_grad = hidden_grad + b.part_recv[k].astype(F32)
        grad = grad_ref[...].astype(F32)
        number = 2 * layer + 1
        b.streams[number] = (
            grad + norm_back(unit, rstd, hidden_grad * vec[2:3, :])
        ).astype(BF16)
        rows[2:3, :] = jnp.sum(hidden_grad * unit, 0, keepdims=True)
        rows[5:6, :] = jnp.sum(hidden_grad, 0, keepdims=True)
        rows[8:9, :] = jnp.sum(grad, 0, keepdims=True)
        for copy in grad_copies + stat_copies + part_copies:
            copy.wait_send()
        late()

    def attention_phase(layer, grad_ref, x_ref, att_ref, before, inside, after):
        phase = 1 - layer
        vec = b.vecs.at[layer]
        rows = b.vec_rows.at[layer]
        grad = grad_ref[...]
        inner_unit, inner_rstd = standardize(att_ref[...].astype(F32))
        attention_ready = attention_loads(layer)
        attention_ready[0].wait()
        inner_grad = mul_nt(grad, square(b.wa.at[3]))
        att_grad = norm_back(inner_unit, inner_rstd, inner_grad * vec[1:2, :]).astype(BF16)
        for pair in range(PAIRS):
            b.do_send[pair] = att_grad[:, pair * PAIR_LANES : (pair + 1) * PAIR_LANES]

        def out_copy(pair):
            return remote(
                b.do_send.at[pair],
                b.do_recv.at[rows_of(me)],
                b.do_s.at[phase, pair],
                b.do_r.at[phase, me],
                "seq",
                OWNERS[pair],
            )

        for pair, owner in enumerate(OWNERS):

            @pl.when(me != owner)
            def _():
                out_copy(pair).start()

            @pl.when(me == owner)
            def _():
                b.do_recv[rows_of(me), :] = b.do_send[pair]

        def left_copy(k):
            return remote(
                b.left_src.at[lax.div(peers[k], 3)],
                b.left.at[pl.ds(k * TOKENS, TOKENS)],
                b.left_s.at[phase, k],
                b.left_r.at[phase, k],
                "section",
                peers[k],
            )

        def right_copy(k):
            return remote(
                b.right_src.at[peers[k]],
                b.right.at[pl.ds(k * TOKENS, TOKENS)],
                b.right_s.at[phase, k],
                b.right_r.at[phase, k],
                "section",
                peers[k],
            )

        unit, rstd = standardize(x_ref[...].astype(F32))
        b.left_src[0] = (unit * vec[0:1, :] + vec[3:4, :]).astype(BF16)
        b.left_src[1] = (inner_unit * vec[1:2, :] + vec[4:5, :]).astype(BF16)
        b.right_src[3] = grad
        for k in range(1, 4):
            left_copy(k).start()

            @pl.when(peers[k] == 3)
            def _():
                right_copy(k).start()

        b.left[slot_rows(0), :] = b.left_src[lax.div(section, 3)]
        rows[1:2, :] = jnp.sum(inner_grad * inner_unit, 0, keepdims=True)
        rows[4:5, :] = jnp.sum(inner_grad, 0, keepdims=True)
        rows[7:8, :] = jnp.sum(grad.astype(F32), 0, keepdims=True)
        for copy in attention_ready[1:]:
            copy.wait()

        def back_copy(target):
            return remote(
                b.d_send.at[pl.ds(target * TOKENS, TOKENS)],
                b.d_recv.at[my_pair],
                b.d_s.at[phase, target],
                b.d_r.at[phase, my_pair],
                "seq",
                target,
            )

        @pl.when(is_owner)
        def _():
            for source in range(8):

                @pl.when(me != source)
                def _():
                    remote(
                        b.do_send.at[0],
                        b.do_recv.at[pl.ds(source * TOKENS, TOKENS)],
                        b.do_s.at[phase, 0],
                        b.do_r.at[phase, source],
                        "seq",
                        source,
                    ).wait_recv()

        before()

        @pl.when(is_owner)
        def _():
            b.key_sum[...] = jnp.zeros((GROUP_TOKENS, PAIR_LANES), F32)
            b.value_sum[...] = jnp.zeros((GROUP_TOKENS, PAIR_LANES), F32)
            lane = lax.broadcasted_iota(jnp.int32, (QUERY_STEP, PAIR_LANES), 1)
            first_half = lane < HEAD_DIM
            for step in reversed(range(GROUP_TOKENS // QUERY_STEP)):
                start = step * QUERY_STEP
                keys_end = start + QUERY_STEP
                block = slice(start, keys_end)
                plain_query = b.qkv[0, block, :]
                query = plain_query * jnp.asarray(SCALE, BF16)
                keys = b.qkv[1, 0:keys_end, :]
                values = b.qkv[2, 0:keys_end, :]
                causal = lax.broadcasted_iota(jnp.int32, (QUERY_STEP, keys_end), 1) <= (
                    start + lax.broadcasted_iota(jnp.int32, (QUERY_STEP, keys_end), 0)
                )
                head_grad = b.do_recv[block, :]
                inverse = 1.0 / b.pt[block, :]
                head_float = head_grad.astype(F32)
                products = head_float * b.pa[block, :]
                scaled = (head_float * inverse).astype(BF16)
                key_lanes = lax.broadcasted_iota(jnp.int32, (keys_end, PAIR_LANES), 1) < HEAD_DIM
                query_parts = []
                key_parts = []
                value_parts = []
                for head in range(2):
                    mine = first_half if head == 0 else ~first_half
                    own_query = jnp.where(mine, query, jnp.zeros_like(query))
                    own_grad = jnp.where(mine, head_grad, jnp.zeros_like(head_grad))
                    delta = jnp.sum(jnp.where(mine, products, 0.0), -1, keepdims=True)
                    own_inverse = jnp.max(jnp.where(mine, inverse, 0.0), -1, keepdims=True)
                    counts = mul_nt(b.picks[head, block, :], b.picks[head, 0:keys_end, :])
                    scores = mul_nt(own_query, keys)
                    weighted = jnp.where(causal, jnp.exp(scores) * counts, 0.0)
                    prob_grad = mul_nt(own_grad, values)
                    score_grad = (weighted * own_inverse * (prob_grad - delta)).astype(BF16)
                    query_parts.append(mul(score_grad, keys))
                    key_parts.append(mul_tn(score_grad, plain_query))
                    value_parts.append(mul_tn(weighted.astype(BF16), scaled))
                b.key_sum[0:keys_end, :] += jnp.where(key_lanes, key_parts[0], key_parts[1])
                b.value_sum[0:keys_end, :] += jnp.where(key_lanes, value_parts[0], value_parts[1])
                query_grad = jnp.where(first_half, query_parts[0], query_parts[1]) * SCALE
                b.d_send[block, 0:PAIR_LANES] = query_grad.astype(BF16)
                b.d_send[block, PAIR_LANES : 2 * PAIR_LANES] = (
                    b.key_sum[block, :] * SCALE
                ).astype(BF16)
                b.d_send[block, 2 * PAIR_LANES : 3 * PAIR_LANES] = b.value_sum[block, :].astype(
                    BF16
                )
                for target in (2 * step, 2 * step + 1):

                    @pl.when(me != target)
                    def _():
                        back_copy(target).start()

                    @pl.when(me == target)
                    def _():
                        b.d_recv[my_pair] = b.d_send[target * TOKENS : (target + 1) * TOKENS, :]

        inside()
        for pair, owner in enumerate(OWNERS):

            @pl.when(me != owner)
            def _():
                remote(
                    b.d_send.at[pl.ds(0, TOKENS)],
                    b.d_recv.at[pair],
                    b.d_s.at[phase, 0],
                    b.d_r.at[phase, pair],
                    "seq",
                    owner,
                ).wait_recv()

            for third in range(3):
                b.right_src[third, :, pair * PAIR_LANES : (pair + 1) * PAIR_LANES] = b.d_recv[
                    pair, :, third * PAIR_LANES : (third + 1) * PAIR_LANES
                ]
        for k in range(1, 4):

            @pl.when(peers[k] != 3)
            def _():
                right_copy(k).start()

        b.right[slot_rows(0), :] = b.right_src[section]
        hidden_grad = mul_nt(b.right_src[0], square(b.wa.at[0]))
        for third in range(1, 3):
            hidden_grad = hidden_grad + mul_nt(b.right_src[third], square(b.wa.at[third]))
        b.streams[2 * layer] = (
            grad.astype(F32) + norm_back(unit, rstd, hidden_grad * vec[0:1, :])
        ).astype(BF16)
        rows[0:1, :] = jnp.sum(hidden_grad * unit, 0, keepdims=True)
        rows[3:4, :] = jnp.sum(hidden_grad, 0, keepdims=True)
        rows[6:7, :] = jnp.sum(b.right_src[2].astype(F32), 0, keepdims=True)
        for k in range(1, 4):
            left_copy(k).wait_recv()
        after()

        def weights_part():
            for k in range(1, 4):
                right_copy(k).wait_recv()
            number = 3 * phase + 2
            store_product(number, mul_tn(b.left[...], b.right[...]))
            tail = rows[...].T.astype(BF16)
            for j in range(8):
                b.prod_a[phase, j % 2, j // 2, :, D : D + PAIR_LANES] = tail[
                    j * SHARD : (j + 1) * SHARD, :
                ]
            pair_copy(number).start()
            for k in range(1, 4):
                left_copy(k).wait_send()
                right_copy(k).wait_send()
            for pair, owner in enumerate(OWNERS):

                @pl.when(me != owner)
                def _():
                    out_copy(pair).wait_send()

            @pl.when(is_owner)
            def _():
                for target in range(8):

                    @pl.when(me != target)
                    def _():
                        back_copy(target).wait_send()

        return weights_part

    def nothing():
        pass

    UP1, DOWN1, ATT1, UP0, DOWN0, ATT0 = range(6)

    def next_feed():
        for copy in feed_loads(0):
            copy.start()

    feed_phase(1, b.cotangent.at[section], b.x_in.at[2], nothing, nothing, next_feed)
    send_sub(3)
    deferred = attention_phase(
        1,
        b.streams.at[3],
        b.x_in.at[1],
        b.att.at[1],
        lambda: sum_pair(DOWN1),
        lambda: sum_pair(UP1),
        lambda: [copy.start() for copy in attention_loads(0)],
    )
    send_sub(2)

    def early():
        deferred()
        sum_line(DOWN1)
        sum_logs()

    def late():
        sum_line(UP1)
        finish(DOWN1)

    feed_phase(0, b.streams.at[2], b.x_in.at[0], early, lambda: sum_pair(ATT1), late)
    send_sub(1)

    def before():
        sum_pair(DOWN0)
        sum_line(ATT1)

    def inside():
        sum_pair(UP0)
        finish(UP1)
        finish_logs()

    deferred = attention_phase(
        0, b.streams.at[1], b.embeds.at[section], b.att.at[0], before, inside, nothing)
    send_sub(0)
    deferred()
    sum_line(DOWN0)
    sum_pair(ATT0)
    sum_line(UP0)
    finish(ATT1)
    finish(DOWN0)
    finish(UP0)
    sum_line(ATT0)
    finish(ATT0)
    for source in range(4):

        @pl.when(section != source)
        def _():
            remote(
                b.streams.at[0],
                b.sub.at[source],
                b.sub_s.at[0],
                b.sub_r.at[source],
                "section",
                source,
            ).wait_recv()

    for number in range(4):

        @pl.when(section != number)
        def _():
            sub_copy(number).wait_send()

    for number in range(6):
        pair_copy(number).wait_send()
        for step in range(1, 4):
            line_copy(number, step).wait_send()
        for k in range(1, 4):
            all_copy(number, k, section).wait_send()
    for number in (UP0, DOWN0, ATT0):
        for copy in store_copies(number):
            copy.wait()


def run_backward(number, near, far):
    vmem = pl.BlockSpec(memory_space=pltpu.VMEM)
    anywhere = pl.BlockSpec(memory_space=pl.ANY)
    return pl.pallas_call(
        backward_kernel,
        name="backward",
        out_shape=[shaped(out[0], out[1]) for out in BACK_OUT.values()],
        in_specs=[vmem] * len(BACK_VMEM) + [anywhere] * len(BACK_ANY),
        out_specs=[vmem if out[2] else anywhere for out in BACK_OUT.values()],
        scratch_shapes=[pltpu.VMEM(item[0], item[1]) for item in BACK_SCRATCH.values()]
        + [pltpu.SemaphoreType.DMA(item) for item in BACK_SEMS.values()],
        compiler_params=pltpu.CompilerParams(
            collective_id=number, has_side_effects=True, vmem_limit_bytes=KERNEL_VMEM_BYTES
        ),
        cost_estimate=pl.CostEstimate(
            flops=10**10, bytes_accessed=100_000_000, transcendentals=0
        ),
    )(*near, *far)


def quick_body(
    embeds,
    row_lengths,
    qkv_weight,
    out_weight,
    up_weight,
    down_weight,
    model_gains,
    model_biases,
    hidden_gains,
    hidden_biases,
    cotangent,
):
    fore = Named(
        [FORE_OUT],
        run_forward(
            10,
            row_lengths,
            (embeds, model_gains, model_biases, hidden_gains, hidden_biases),
            (qkv_weight, out_weight, up_weight, down_weight),
        ),
    )
    back = Named(
        [BACK_OUT],
        run_backward(
            20,
            (cotangent, embeds, fore.streams, fore.att, fore.vecs, fore.picks, fore.logs),
            (
                fore.wa_out,
                fore.wf_out,
                fore.qkv_out,
                fore.pa_out,
                fore.pt_out,
                fore.hid_out,
                fore.up_out,
                fore.stat_out,
            ),
        ),
    )
    return (
        fore.sub[None],
        back.sub[None],
        back.qkv_out,
        back.out_out,
        back.up_out,
        back.down_out,
        back.gain_out,
        back.bias_out,
        back.hidden_out[:, 0],
        back.hidden_out[:, 1:3],
        back.means_out,
    )


def fits_quick(mesh):
    return mesh.shape["section"] == 4 and mesh.shape["seq"] == 8


def solution(mesh):
    return jax.shard_map(
        quick_body if fits_quick(mesh) else body,
        mesh=mesh,
        in_specs=(
            P(None, "seq", None),
            P(),
            P(None, "seq", None),
            P(None, "seq", None),
            P(None, "seq", None),
            P(None, "seq", None),
            P(None, None, "seq"),
            P(None, None, "seq"),
            P(None, "seq"),
            P(None, None, "seq"),
            P(None, "seq", None),
        ),
        out_specs=(
            P("section", None, "seq", None),
            P("section", None, "seq", None),
            P(None, "seq", None),
            P(None, "seq", None),
            P(None, "seq", None),
            P(None, "seq", None),
            P(None, None, "seq"),
            P(None, None, "seq"),
            P(None, "seq"),
            P(None, None, "seq"),
            P(),
        ),
        check_vma=False,
    )
```

```python
import jax
import jax.numpy as jnp
from jax import lax
from jax.experimental import pallas as pl
from jax.experimental.pallas import tpu as pltpu
from jax.sharding import PartitionSpec as P

D = 768
HEADS = 12
HEAD_DIM = 64
FF = 3072


WIDTHS = (2048, 4096, 8192, 16384, 32768)
RATIOS = (1, 2, 4, 6, 12)
EPSILON = 1e-05


def passed_along(value, axis, steps):
    count = lax.axis_size(axis)
    initial, last = (max(0, -steps), min(count, count - steps))
    return lax.ppermute(value, axis, [(source, source + steps) for source in range(initial, last)])


def norm_rows(inputs, gain_row, offset):
    center = inputs - jnp.mean(inputs, -1, keepdims=True)
    spread = jnp.mean(center * center, -1, keepdims=True)
    return center * lax.rsqrt(spread + EPSILON) * gain_row + offset


def place_rows(lengths, token_index):
    row_ends = jnp.cumsum(lengths)
    passed = token_index[:, None] >= row_ends[None, :]
    row_ids = jnp.sum(passed.astype(jnp.int32), 1)
    offsets = token_index - jnp.sum(jnp.where(passed, lengths[None, :], 0), 1)
    return (row_ids, offsets)


def query_chosen(query_pos):
    head_ids = jnp.arange(HEADS, dtype=jnp.int32)
    chosen = []
    for seg_width, seg_ratio in zip(WIDTHS, RATIOS):
        query_pick = query_pos % seg_width % seg_ratio
        chosen.append(query_pick[None, :] == (head_ids % seg_ratio)[:, None])
    return chosen


def pattern_allow(query_rows, query_pos, key_rows, key_pos):
    widths = jnp.array(WIDTHS, jnp.int32)[:, None]
    ratios = jnp.array(RATIOS, jnp.int32)[:, None]
    residue = jnp.arange(HEADS, dtype=jnp.int32)[None, :] % ratios
    query_mod = query_pos[None, :] % widths % ratios
    key_mod = key_pos[None, :] % widths % ratios
    query_ok = query_mod[:, None, :] == residue[:, :, None]
    key_ok = key_mod[:, None, :] == residue[:, :, None]
    common = (query_rows[:, None] == key_rows[None, :]) & (key_pos[None, :] <= query_pos[:, None])
    inside = common[None] & (
        (query_pos[None, :] // widths)[:, :, None] == (key_pos[None, :] // widths)[:, None, :]
    )
    return inside[:, None] & query_ok[:, :, :, None] & key_ok[:, :, None, :]


def block_rows(total_rows):
    step_rows = min(total_rows, 512)
    return step_rows


def split_heads(matrix):
    return matrix.reshape(matrix.shape[0], HEADS, HEAD_DIM)


def pair_terms(query_block, keys_block, query_rows, query_pos, key_rows, key_pos):
    scores = jnp.einsum(
        "qhe,khe->hqk", query_block, keys_block, preferred_element_type=jnp.float32
    ) * HEAD_DIM ** (-0.5)
    allowed = pattern_allow(query_rows, query_pos, key_rows, key_pos)
    counts = jnp.sum(allowed.astype(jnp.float32), 0)
    raised = jnp.exp(scores)
    return (raised, counts * raised, allowed)


def project_tokens(inputs, qkv_matrix, norm_gains, norm_biases):
    hidden = norm_rows(inputs, norm_gains[0], norm_biases[0]).astype(jnp.bfloat16)
    bias_row = jnp.concatenate(
        [jnp.zeros_like(norm_biases[3]), jnp.zeros_like(norm_biases[3]), norm_biases[3]]
    )
    projected = (jnp.dot(hidden, qkv_matrix, preferred_element_type=jnp.float32) + bias_row).astype(
        jnp.bfloat16
    )
    return (hidden, projected)


def attention_forward(section_in, projected, whole_keys, lengths, params, seq_index):
    out_matrix, norm_gains, norm_biases = (params[1], params[4], params[5])
    tok_rows = section_in.shape[0]
    inputs = section_in.astype(jnp.float32)
    queries = split_heads(projected[:, :D])
    query_rows, query_pos = place_rows(
        lengths, seq_index * tok_rows + jnp.arange(tok_rows, dtype=jnp.int32)
    )
    group_rows = whole_keys.shape[0]
    step_rows = block_rows(group_rows)

    def one_block(running, block_start):
        totals, pattern_sums, accumulated = running
        kv_block = lax.dynamic_slice_in_dim(whole_keys, block_start, step_rows, 0)
        key_rows, key_pos = place_rows(
            lengths, block_start + jnp.arange(step_rows, dtype=jnp.int32)
        )
        raised, weighted, allowed = pair_terms(
            queries, split_heads(kv_block[:, :D]), query_rows, query_pos, key_rows, key_pos
        )
        totals = totals + jnp.sum(weighted, -1)
        pattern_sums = pattern_sums + jnp.sum(jnp.where(allowed, raised[None], 0.0), -1)
        accumulated = accumulated + jnp.einsum(
            "hqk,khe->hqe",
            weighted.astype(jnp.bfloat16),
            split_heads(kv_block[:, D:]),
            preferred_element_type=jnp.float32,
        )
        return ((totals, pattern_sums, accumulated), None)

    start_sums = (
        jnp.zeros((HEADS, tok_rows), jnp.float32),
        jnp.zeros((len(WIDTHS), HEADS, tok_rows), jnp.float32),
        jnp.zeros((HEADS, tok_rows, HEAD_DIM), jnp.float32),
    )
    folded, unused = lax.scan(
        one_block, start_sums, jnp.arange(0, group_rows, step_rows, dtype=jnp.int32)
    )
    totals, pattern_sums, accumulated = folded
    attended = jnp.transpose(accumulated / totals[:, :, None], (1, 0, 2)).reshape(tok_rows, D)
    inner_norm = norm_rows(attended, norm_gains[1], norm_biases[1]).astype(jnp.bfloat16)
    branch = jnp.dot(inner_norm, out_matrix, preferred_element_type=jnp.float32) + norm_biases[4]
    section_out = (inputs + branch).astype(jnp.bfloat16)
    chosen = query_chosen(query_pos)
    log_terms = jnp.stack(
        [
            jnp.sum(
                jnp.where(pick_row, jnp.log(jnp.where(pick_row, pattern_sums[number], 1.0)), 0.0)
            )
            for number, pick_row in enumerate(chosen)
        ]
    )
    pick_counts = jnp.stack([jnp.sum(pick_row.astype(jnp.float32)) for pick_row in chosen])
    return (section_out, attended, totals, log_terms, pick_counts)


def feed_forward(section_in, params):
    up_matrix, down_matrix, norm_gains, norm_biases, hidden_gain, hidden_bias = (
        params[2],
        params[3],
        params[4],
        params[5],
        params[6],
        params[7],
    )
    tok_rows = section_in.shape[0]
    inputs = section_in.astype(jnp.float32)
    hidden = norm_rows(inputs, norm_gains[2], norm_biases[2]).astype(jnp.bfloat16)
    upward = jnp.dot(hidden, up_matrix, preferred_element_type=jnp.float32) + hidden_bias[0]
    inner_norm = norm_rows(
        jax.nn.gelu(upward, approximate=False), hidden_gain, hidden_bias[1]
    ).astype(jnp.bfloat16)
    branch = jnp.dot(inner_norm, down_matrix, preferred_element_type=jnp.float32) + norm_biases[5]
    section_out = (inputs + branch).astype(jnp.bfloat16)
    empty_terms = jnp.zeros((len(WIDTHS),), jnp.float32)
    return (
        section_out,
        jnp.zeros((tok_rows, D), jnp.float32),
        jnp.zeros((HEADS, tok_rows), jnp.float32),
        empty_terms,
        empty_terms,
    )


def attention_middle(
    section_in, grad_out, attended, totals, lengths, all_keys, projected, params, seq_index
):
    out_matrix, norm_gains, norm_biases = (params[1], params[4], params[5])
    scale_factor = HEAD_DIM ** (-0.5)
    tok_rows = section_in.shape[0]
    queries = split_heads(projected[:, :D])
    query_rows, query_pos = place_rows(
        lengths, seq_index * tok_rows + jnp.arange(tok_rows, dtype=jnp.int32)
    )
    inner_norm = norm_rows(attended, norm_gains[1], norm_biases[1]).astype(jnp.bfloat16)
    out_step = jnp.einsum("td,tf->df", inner_norm, grad_out, preferred_element_type=jnp.float32)
    inner_grad = jnp.einsum("tf,df->td", grad_out, out_matrix, preferred_element_type=jnp.float32)
    unused, inner_back = jax.vjp(norm_rows, attended, norm_gains[1], norm_biases[1])
    attended_grad, inner_gain_grad, inner_bias_grad = inner_back(inner_grad)
    low_attended = attended_grad.astype(jnp.bfloat16)
    head_grad = split_heads(low_attended)
    row_dots = jnp.einsum("qhe,qhe->hq", head_grad.astype(jnp.float32), split_heads(attended))
    scaled_grad = head_grad.astype(jnp.float32) / jnp.transpose(totals)[:, :, None]
    group_rows = all_keys.shape[0]
    step_rows = block_rows(group_rows)

    def grad_block(query_grad, block_start):
        kv_block = lax.dynamic_slice_in_dim(all_keys, block_start, step_rows, 0)
        keys_block = split_heads(kv_block[:, :D])
        values_block = split_heads(kv_block[:, D:])
        key_rows, key_pos = place_rows(
            lengths, block_start + jnp.arange(step_rows, dtype=jnp.int32)
        )
        raised, weighted, allowed = pair_terms(
            queries, keys_block, query_rows, query_pos, key_rows, key_pos
        )
        prob_grad = jnp.einsum(
            "qhe,khe->hqk", head_grad, values_block, preferred_element_type=jnp.float32
        )
        score_grad = (weighted / totals[:, :, None] * (prob_grad - row_dots[:, :, None])).astype(
            jnp.bfloat16
        )
        query_grad = (
            query_grad
            + jnp.einsum("hqk,khe->qhe", score_grad, keys_block, preferred_element_type=jnp.float32)
            * scale_factor
        )
        key_grad = (
            jnp.einsum("hqk,qhe->khe", score_grad, queries, preferred_element_type=jnp.float32)
            * scale_factor
        )
        value_grad = jnp.einsum(
            "hqk,qhe->khe",
            weighted.astype(jnp.bfloat16),
            scaled_grad,
            preferred_element_type=jnp.float32,
        )
        block_grad = jnp.concatenate(
            [key_grad.reshape(step_rows, D), value_grad.reshape(step_rows, D)], 1
        )
        return (query_grad, block_grad)

    query_grad, block_grads = lax.scan(
        grad_block,
        jnp.zeros((tok_rows, HEADS, HEAD_DIM), jnp.float32),
        jnp.arange(0, group_rows, step_rows, dtype=jnp.int32),
    )
    block_grads = block_grads.reshape(group_rows, 2 * D)
    return (
        query_grad.reshape(tok_rows, D),
        low_attended,
        row_dots,
        block_grads,
        out_step,
        inner_gain_grad,
        inner_bias_grad,
    )


def attention_finish(section_in, grad_out, middle, extra, params, grad_sums):
    qkv_matrix, norm_gains, norm_biases = (params[0], params[4], params[5])
    inputs = section_in.astype(jnp.float32)
    grad_float = grad_out.astype(jnp.float32)
    hidden = norm_rows(inputs, norm_gains[0], norm_biases[0]).astype(jnp.bfloat16)
    query_grad, low_attended, row_dots, block_grads, out_step, inner_gain_grad, inner_bias_grad = (
        middle
    )
    own_grads = extra[0]
    proj_grad = jnp.concatenate([query_grad, own_grads], 1).astype(jnp.bfloat16)
    qkv_step = jnp.einsum("td,tf->df", hidden, proj_grad, preferred_element_type=jnp.float32)
    value_bias_sums = jnp.sum(proj_grad[:, 2 * D :].astype(jnp.float32), 0)
    hidden_grad = jnp.einsum("tf,df->td", proj_grad, qkv_matrix, preferred_element_type=jnp.float32)
    unused_first, first_back = jax.vjp(norm_rows, inputs, norm_gains[0], norm_biases[0])
    input_grad, first_gain_grad, first_bias_grad = first_back(hidden_grad)
    qkv_sum, out_sum, up_sum, down_sum, gain_sum, bias_sum, hgain_sum, hbias_sum = grad_sums
    gain_sum = gain_sum.at[0].add(first_gain_grad).at[1].add(inner_gain_grad)
    bias_sum = (
        bias_sum.at[0]
        .add(first_bias_grad)
        .at[1]
        .add(inner_bias_grad)
        .at[3]
        .add(value_bias_sums)
        .at[4]
        .add(jnp.sum(grad_float, 0))
    )
    return (
        grad_float + input_grad,
        (
            qkv_sum + qkv_step,
            out_sum + out_step,
            up_sum,
            down_sum,
            gain_sum,
            bias_sum,
            hgain_sum,
            hbias_sum,
        ),
    )


def feed_backward(section_in, grad_out, params, grad_sums):
    up_matrix, down_matrix, norm_gains, norm_biases, hidden_gain, hidden_bias = (
        params[2],
        params[3],
        params[4],
        params[5],
        params[6],
        params[7],
    )
    inputs = section_in.astype(jnp.float32)
    grad_float = grad_out.astype(jnp.float32)
    hidden = norm_rows(inputs, norm_gains[2], norm_biases[2]).astype(jnp.bfloat16)
    upward = jnp.dot(hidden, up_matrix, preferred_element_type=jnp.float32) + hidden_bias[0]

    def inner_rows(upward_in, gain_row, bias_row):
        return norm_rows(jax.nn.gelu(upward_in, approximate=False), gain_row, bias_row)

    inner_value, inner_back = jax.vjp(inner_rows, upward, hidden_gain, hidden_bias[1])
    inner_norm = inner_value.astype(jnp.bfloat16)
    down_step = jnp.einsum("tf,td->fd", inner_norm, grad_out, preferred_element_type=jnp.float32)
    inner_grad = jnp.einsum("td,fd->tf", grad_out, down_matrix, preferred_element_type=jnp.float32)
    upward_grad, hgain_step, hbias_step = inner_back(inner_grad)
    low_upward = upward_grad.astype(jnp.bfloat16)
    up_step = jnp.einsum("td,tf->df", hidden, low_upward, preferred_element_type=jnp.float32)
    hidden_grad = jnp.einsum("tf,df->td", low_upward, up_matrix, preferred_element_type=jnp.float32)
    unused, first_back = jax.vjp(norm_rows, inputs, norm_gains[2], norm_biases[2])
    input_grad, first_gain_grad, first_bias_grad = first_back(hidden_grad)
    qkv_sum, out_sum, up_sum, down_sum, gain_sum, bias_sum, hgain_sum, hbias_sum = grad_sums
    gain_sum = gain_sum.at[2].add(first_gain_grad)
    bias_sum = bias_sum.at[2].add(first_bias_grad).at[5].add(jnp.sum(grad_float, 0))
    hbias_sum = (
        hbias_sum.at[0].add(jnp.sum(low_upward.astype(jnp.float32), 0)).at[1].add(hbias_step)
    )
    return (
        grad_float + input_grad,
        (
            qkv_sum,
            out_sum,
            up_sum + up_step,
            down_sum + down_step,
            gain_sum,
            bias_sum,
            hgain_sum + hgain_step,
            hbias_sum,
        ),
    )


def keep_slot(store, fresh, slot_id, in_range):
    previous = lax.dynamic_index_in_dim(store, slot_id, 0, False)
    return lax.dynamic_update_index_in_dim(store, jnp.where(in_range, fresh, previous), slot_id, 0)


def body(
    embeds,
    row_lengths,
    qkv_weight,
    out_weight,
    up_weight,
    down_weight,
    model_gains,
    model_biases,
    hidden_gains,
    hidden_biases,
    cotangent,
):
    section_id = lax.axis_index("section")
    seq_index = lax.axis_index("seq")
    section_count = lax.axis_size("section")
    micro_count = embeds.shape[0]
    tok_rows = embeds.shape[1]
    group_rows = tok_rows * lax.axis_size("seq")
    layer_id = section_id // 2
    attends = section_id % 2 == 0
    bias_count = model_biases.shape[1]

    def pick_layer(stacked):
        return lax.dynamic_index_in_dim(stacked, layer_id, 0, False)

    gathered = (
        lax.all_gather(pick_layer(qkv_weight), "seq", axis=0, tiled=True),
        lax.all_gather(pick_layer(out_weight), "seq", axis=0, tiled=True),
        lax.all_gather(pick_layer(up_weight), "seq", axis=0, tiled=True),
        lax.all_gather(pick_layer(down_weight), "seq", axis=0, tiled=True),
        lax.all_gather(pick_layer(model_gains), "seq", axis=1, tiled=True),
        lax.all_gather(pick_layer(model_biases), "seq", axis=1, tiled=True),
        lax.all_gather(pick_layer(hidden_gains), "seq", axis=0, tiled=True),
        lax.all_gather(pick_layer(hidden_biases), "seq", axis=1, tiled=True),
    )
    params = tuple(gathered[:4]) + tuple((vector.astype(jnp.float32) for vector in gathered[4:]))
    whole_shape = (0,)

    def make_projected(section_in):
        return project_tokens(section_in.astype(jnp.float32), params[0], params[4], params[5])[1]

    def skip_projected(section_in):
        return jnp.zeros((tok_rows, 3 * D), jnp.bfloat16)

    def run_attention(section_in, projected, whole_keys, lengths):
        return attention_forward(section_in, projected, whole_keys, lengths, params, seq_index)

    def run_feed(section_in, projected, whole_keys, lengths):
        return feed_forward(section_in, params)

    def forward_tick(running, tick_id):
        (
            incoming,
            kept_inputs,
            kept_attended,
            kept_totals,
            kept_whole,
            outputs,
            log_sums,
            pick_sums,
        ) = running
        micro_id = tick_id - section_id
        in_range = (micro_id >= 0) & (micro_id < micro_count)
        slot_id = jnp.clip(micro_id, 0, micro_count - 1)
        lengths = lax.dynamic_index_in_dim(row_lengths, slot_id, 0, False)
        section_in = jnp.where(
            section_id == 0, lax.dynamic_index_in_dim(embeds, slot_id, 0, False), incoming
        )
        projected = lax.cond(attends, make_projected, skip_projected, section_in)
        whole_keys = lax.all_gather(projected[:, D:], "seq", axis=0, tiled=True)
        section_out, attended, totals, log_terms, pick_counts = lax.cond(
            attends, run_attention, run_feed, section_in, projected, whole_keys, lengths
        )
        kept_inputs = keep_slot(kept_inputs, section_in, slot_id, in_range)
        kept_attended = keep_slot(kept_attended, attended, slot_id, in_range)
        kept_totals = keep_slot(kept_totals, totals, slot_id, in_range)
        outputs = keep_slot(outputs, section_out, slot_id, in_range)
        log_sums = log_sums + jnp.where(in_range, log_terms, 0.0)
        pick_sums = pick_sums + jnp.where(in_range, pick_counts, 0.0)
        incoming = passed_along(section_out, "section", 1)
        return (
            (
                incoming,
                kept_inputs,
                kept_attended,
                kept_totals,
                kept_whole,
                outputs,
                log_sums,
                pick_sums,
            ),
            None,
        )

    forward_start = (
        jnp.zeros((tok_rows, D), jnp.bfloat16),
        jnp.zeros((micro_count, tok_rows, D), jnp.bfloat16),
        jnp.zeros((micro_count, tok_rows, D), jnp.float32),
        jnp.zeros((micro_count, HEADS, tok_rows), jnp.float32),
        jnp.zeros((micro_count,) + whole_shape, jnp.bfloat16),
        jnp.zeros((micro_count, tok_rows, D), jnp.bfloat16),
        jnp.zeros((len(WIDTHS),), jnp.float32),
        jnp.zeros((len(WIDTHS),), jnp.float32),
    )
    ticks = jnp.arange(micro_count + section_count - 1, dtype=jnp.int32)
    forward_end, unused = lax.scan(forward_tick, forward_start, ticks)
    unused_in, kept_inputs, kept_attended, kept_totals, kept_whole, outputs, log_sums, pick_sums = (
        forward_end
    )
    block_shape = (group_rows, 2 * D)

    def middle_attention(section_in, grad_out, attended, totals, lengths, all_keys, projected):
        return attention_middle(
            section_in, grad_out, attended, totals, lengths, all_keys, projected, params, seq_index
        )

    def middle_feed(section_in, grad_out, attended, totals, lengths, all_keys, projected):
        return (
            jnp.zeros((tok_rows, D), jnp.float32),
            jnp.zeros((tok_rows, D), jnp.bfloat16),
            jnp.zeros((HEADS, tok_rows), jnp.float32),
            jnp.zeros(block_shape, jnp.float32),
            jnp.zeros((D, D), jnp.float32),
            jnp.zeros((D,), jnp.float32),
            jnp.zeros((D,), jnp.float32),
        )

    def finish_attention(section_in, grad_out, projected, middle, extra, lengths, grad_sums):
        return attention_finish(section_in, grad_out, middle, extra, params, grad_sums)

    def finish_feed(section_in, grad_out, projected, middle, extra, lengths, grad_sums):
        return feed_backward(section_in, grad_out, params, grad_sums)

    def backward_tick(running, tick_id):
        incoming, grad_sums, input_grads = running
        micro_id = micro_count - 1 - tick_id + (section_count - 1 - section_id)
        in_range = (micro_id >= 0) & (micro_id < micro_count)
        slot_id = jnp.clip(micro_id, 0, micro_count - 1)
        from_next = jnp.where(
            section_id == section_count - 1,
            lax.dynamic_index_in_dim(cotangent, slot_id, 0, False),
            incoming,
        )
        grad_out = jnp.where(in_range, from_next, jnp.zeros_like(from_next))
        section_in = lax.dynamic_index_in_dim(kept_inputs, slot_id, 0, False)
        attended = lax.dynamic_index_in_dim(kept_attended, slot_id, 0, False)
        totals = lax.dynamic_index_in_dim(kept_totals, slot_id, 0, False)
        lengths = lax.dynamic_index_in_dim(row_lengths, slot_id, 0, False)
        projected = lax.cond(attends, make_projected, skip_projected, section_in)
        all_keys = lax.all_gather(projected[:, D:], "seq", axis=0, tiled=True)
        middle = lax.cond(
            attends,
            middle_attention,
            middle_feed,
            section_in,
            grad_out,
            attended,
            totals,
            lengths,
            all_keys,
            projected,
        )
        extra = (lax.psum_scatter(middle[3], "seq", scatter_dimension=0, tiled=True),)
        section_grad, grad_sums = lax.cond(
            attends,
            finish_attention,
            finish_feed,
            section_in,
            grad_out,
            projected,
            middle,
            extra,
            lengths,
            grad_sums,
        )
        low_grad = section_grad.astype(jnp.bfloat16)
        input_grads = keep_slot(input_grads, low_grad, slot_id, in_range)
        incoming = passed_along(low_grad, "section", -1)
        return ((incoming, grad_sums, input_grads), None)

    grad_start = (
        jnp.zeros((D, 3 * D), jnp.float32),
        jnp.zeros((D, D), jnp.float32),
        jnp.zeros((D, FF), jnp.float32),
        jnp.zeros((FF, D), jnp.float32),
        jnp.zeros((3, D), jnp.float32),
        jnp.zeros((bias_count, D), jnp.float32),
        jnp.zeros((FF,), jnp.float32),
        jnp.zeros((2, FF), jnp.float32),
    )
    backward_start = (
        jnp.zeros((tok_rows, D), jnp.bfloat16),
        grad_start,
        jnp.zeros((micro_count, tok_rows, D), jnp.bfloat16),
    )
    backward_end, unused_back = lax.scan(backward_tick, backward_start, ticks)
    unused_grad, grad_sums, input_grads = backward_end
    shards = (
        lax.psum_scatter(grad_sums[0], "seq", scatter_dimension=0, tiled=True),
        lax.psum_scatter(grad_sums[1], "seq", scatter_dimension=0, tiled=True),
        lax.psum_scatter(grad_sums[2], "seq", scatter_dimension=0, tiled=True),
        lax.psum_scatter(grad_sums[3], "seq", scatter_dimension=0, tiled=True),
        lax.psum_scatter(grad_sums[4], "seq", scatter_dimension=1, tiled=True),
        lax.psum_scatter(grad_sums[5], "seq", scatter_dimension=1, tiled=True),
        lax.psum_scatter(grad_sums[6], "seq", scatter_dimension=0, tiled=True),
        lax.psum_scatter(grad_sums[7], "seq", scatter_dimension=1, tiled=True),
    )
    sources = (
        qkv_weight,
        out_weight,
        up_weight,
        down_weight,
        model_gains,
        model_biases,
        hidden_gains,
        hidden_biases,
    )
    placed = tuple(
        (
            lax.dynamic_update_index_in_dim(
                jnp.zeros(source.shape, jnp.float32), shard, layer_id, 0
            )
            for shard, source in zip(shards, sources)
        )
    )
    summed = (
        lax.psum(placed[0].astype(jnp.bfloat16), "section").astype(jnp.float32),
        lax.psum(placed[1].astype(jnp.bfloat16), "section").astype(jnp.float32),
        lax.psum(placed[2].astype(jnp.bfloat16), "section").astype(jnp.float32),
        lax.psum(placed[3].astype(jnp.bfloat16), "section").astype(jnp.float32),
        lax.psum(placed[4].astype(jnp.bfloat16), "section").astype(jnp.float32),
        lax.psum(placed[5].astype(jnp.bfloat16), "section").astype(jnp.float32),
        lax.psum(placed[6].astype(jnp.bfloat16), "section").astype(jnp.float32),
        lax.psum(placed[7].astype(jnp.bfloat16), "section").astype(jnp.float32),
    )
    layer_count = qkv_weight.shape[0]
    layer_terms = lax.dynamic_update_index_in_dim(
        jnp.zeros((layer_count, len(WIDTHS)), jnp.float32), log_sums, layer_id, 0
    )
    layer_picks = lax.dynamic_update_index_in_dim(
        jnp.zeros((layer_count, len(WIDTHS)), jnp.float32), pick_sums, layer_id, 0
    )
    log_totals, pick_totals = lax.psum((layer_terms, layer_picks), ("section", "seq"))
    pattern_means = log_totals / pick_totals
    return (
        outputs[None],
        input_grads[None],
        summed[0],
        summed[1],
        summed[2],
        summed[3],
        summed[4],
        summed[5],
        summed[6],
        summed[7],
        pattern_means,
    )


BF16 = jnp.bfloat16
F32 = jnp.float32
PAIRS = HEADS // 2
OWNERS = (0, 2, 3, 4, 5, 6)
TOKENS = 128
PAIR_LANES = 128
QUERY_STEP = 256
VEC_ROWS = 16
KERNEL_VMEM_BYTES = 62 * 1024 * 1024
SCALE = HEAD_DIM ** (-0.5)


def mul(left, right):
    return lax.dot_general(left, right, (((1,), (0,)), ((), ())), preferred_element_type=F32)


def mul_nt(left, right):
    return lax.dot_general(left, right, (((1,), (1,)), ((), ())), preferred_element_type=F32)


def mul_tn(left, right):
    return lax.dot_general(left, right, (((0,), (0,)), ((), ())), preferred_element_type=F32)


def standardize(values):
    center = values - jnp.mean(values, -1, keepdims=True)
    rstd = lax.rsqrt(jnp.mean(center * center, -1, keepdims=True) + EPSILON)
    return (center * rstd, rstd)


def norm_back(unit, rstd, unit_grad):
    first = jnp.mean(unit_grad, -1, keepdims=True)
    second = jnp.mean(unit_grad * unit, -1, keepdims=True)
    return rstd * (unit_grad - first - unit * second)


def remote(source, target, send_sem, recv_sem, axis, peer):
    return pltpu.make_async_remote_copy(
        src_ref=source,
        dst_ref=target,
        send_sem=send_sem,
        recv_sem=recv_sem,
        device_id={axis: peer},
        device_id_type=pl.DeviceIdType.MESH,
    )


def greet(axis, peers):
    barrier = pltpu.get_barrier_semaphore()
    for peer in peers:
        pl.semaphore_signal(
            barrier, inc=1, device_id={axis: peer}, device_id_type=pl.DeviceIdType.MESH
        )
    pl.semaphore_wait(barrier, len(peers))


def seq_peers(me, count):
    return [lax.rem(me + step, count) for step in range(1, count)]


def plane_peers(me):
    return [
        me,
        me + 1 - 2 * lax.rem(me, 2),
        lax.rem(me + 2, 4),
        3 - me,
    ]


def rows_of(block, size=TOKENS):
    return pl.ds(pl.multiple_of(block * size, size), size)


def gelu_parts(values):
    below = 0.5 * (1.0 + lax.erf(values * (0.5**0.5)))
    return (values * below, below)


def share_stats(columns, send, recv, send_sem, recv_sem, peers):
    send[...] = columns.T[0:8, :]
    recv[0] = send[...]
    copies = [
        remote(send, recv.at[k], send_sem.at[k], recv_sem.at[k], "section", peers[k])
        for k in range(1, 4)
    ]
    for copy in copies:
        copy.start()
    return copies


def two_columns(first, second):
    lane = lax.broadcasted_iota(jnp.int32, (first.shape[0], PAIR_LANES), 1)
    return jnp.where(lane == 0, first, jnp.where(lane == 1, second, 0.0))


def slot_rows(k):
    return slice(k * TOKENS, (k + 1) * TOKENS)


def shaped(shape, kind):
    return jax.ShapeDtypeStruct(shape, kind)


class Named:
    def __init__(self, groups, refs):
        names = [name for group in groups for name in group]
        for name, ref in zip(names, refs, strict=True):
            setattr(self, name, ref)


GROUP_TOKENS = 8 * TOKENS
WIDE = 4 * TOKENS
SHARD = D // 8


def square(ref):
    return ref[...].reshape(D, D)


def remote_both(source, target, send_sem, recv_sem, section, seq):
    return pltpu.make_async_remote_copy(
        src_ref=source,
        dst_ref=target,
        send_sem=send_sem,
        recv_sem=recv_sem,
        device_id=(section, seq),
        device_id_type=pl.DeviceIdType.MESH,
    )


def greet_all(barrier, section, me):
    for other in range(4):
        for j in range(8):

            @pl.when((section != other) | (me != j))
            def _():
                pl.semaphore_signal(
                    barrier, inc=1, device_id=(other, j), device_id_type=pl.DeviceIdType.MESH
                )


class Place:
    def __init__(self):
        self.me = lax.axis_index("seq")
        self.section = lax.axis_index("section")
        self.peers = plane_peers(self.section)
        self.core = lax.rem(self.me, 2)
        self.chip = lax.div(self.me, 2)
        self.high = lax.div(self.chip, 2)
        self.low = lax.rem(self.chip, 2)
        self.sibling = self.me + 1 - 2 * self.core
        self.across = 2 * (2 * (1 - self.high) + self.low) + self.core
        self.next = 2 * (2 * self.high + 1 - self.low) + self.core
        self.is_owner = (self.me != 1) & (self.me != 7)
        pair = jnp.where(self.me == 0, 0, self.me - 1)
        self.my_pair = jnp.where(pair > PAIRS - 1, PAIRS - 1, pair)


class LineGather:
    def __init__(self, place, base, far_sems, near_sems, core_sems):
        self.place = place
        self.base = base
        self.far_sems = far_sems
        self.near_sems = near_sems
        self.core_sems = core_sems

    def far(self, high):
        p = self.place
        view = self.base.at[high, p.low, p.core]
        return remote(view, view, self.far_sems[0], self.far_sems[1], "seq", p.across)

    def near(self, low):
        p = self.place
        view = self.base.at[:, low, p.core]
        return remote(view, view, self.near_sems[0], self.near_sems[1], "seq", p.next)

    def cores(self, core):
        p = self.place
        view = self.base.at[:, :, core]
        return remote(view, view, self.core_sems[0], self.core_sems[1], "seq", p.sibling)

    def start(self):
        self.far(self.place.high).start()

    def pass_line(self):
        self.far(1 - self.place.high).wait_recv()
        self.near(self.place.low).start()

    def pass_core(self):
        self.near(1 - self.place.low).wait_recv()
        self.cores(self.place.core).start()

    def ready(self):
        self.cores(1 - self.place.core).wait_recv()

    def drain(self):
        self.far(self.place.high).wait_send()
        self.near(self.place.low).wait_send()
        self.cores(self.place.core).wait_send()


FORE_VMEM = dict(gains=0, biases=0, hgains=0, hbiases=0)
FORE_ANY = dict(embeds_in=0, qkv_w=0, out_w=0, up_w=0, down_w=0)
FORE_OUT = dict(
    sub=((4, TOKENS, D), BF16, True),
    streams_out=((4, TOKENS, D), BF16, False),
    att_out=((2, TOKENS, D), BF16, False),
    vecs=((2, VEC_ROWS, D), F32, True),
    picks_out=((2, GROUP_TOKENS, PAIR_LANES), BF16, False),
    logs=((8, PAIR_LANES), F32, True),
    wa_out=((2, 4, 2, 2, 2, SHARD, D), BF16, False),
    wf_out=((2, 2, 2, 2, 2, SHARD, D), BF16, False),
    qkv_out=((2, 3, GROUP_TOKENS, PAIR_LANES), BF16, False),
    pa_out=((2, GROUP_TOKENS, PAIR_LANES), F32, False),
    pt_out=((2, GROUP_TOKENS, PAIR_LANES), F32, False),
    hid_out=((2, WIDE, D), BF16, False),
    up_out=((2, WIDE, D), F32, False),
    stat_out=((2, WIDE, PAIR_LANES), F32, False),
    left_out=((2, WIDE, D), BF16, False),
)
FORE_SCRATCH = dict(
    embeds=((4, TOKENS, D), BF16),
    streams=((4, TOKENS, D), BF16),
    att=((2, TOKENS, D), BF16),
    picks=((2, GROUP_TOKENS, PAIR_LANES), BF16),
    wa=((2, 4, 2, 2, 2, SHARD, D), BF16),
    wf=((2, 2, 2, 2, 2, SHARD, D), BF16),
    qkv=((2, 3, GROUP_TOKENS, PAIR_LANES), BF16),
    pa=((2, GROUP_TOKENS, PAIR_LANES), F32),
    pt=((2, GROUP_TOKENS, PAIR_LANES), F32),
    hid=((2, WIDE, D), BF16),
    up=((2, WIDE, D), F32),
    stat=((2, WIDE, PAIR_LANES), F32),
    left=((2, WIDE, D), BF16),
    raw_up=((2, SHARD, FF), BF16),
    small_src=((2, 32, PAIR_LANES), BF16),
    small=((8, 2, 32, PAIR_LANES), BF16),
    inner=((TOKENS, D), BF16),
    proj_send=((4, PAIRS, TOKENS, PAIR_LANES), BF16),
    att_send=((GROUP_TOKENS, PAIR_LANES), BF16),
    att_recv=((2, PAIRS, TOKENS, PAIR_LANES), BF16),
    active=((WIDE, D), F32),
    columns=((WIDE, PAIR_LANES), F32),
    stat_rows=((PAIR_LANES, WIDE), F32),
    part_send=((4, TOKENS, D), BF16),
    part_recv=((2, 4, TOKENS, D), BF16),
    stat_send=((8, WIDE), F32),
    stat_recv=((2, 4, 8, WIDE), F32),
)
FORE_SEMS = dict(
    load_sem=(2, 3),
    embeds_sem=(4,),
    store_sem=(2, 13),
    small_s=(8,),
    small_r=(8,),
    az_s=(4,),
    az_r=(4,),
    line_s=(6, 3),
    line_r=(6, 3),
    axy_s=(2, 4),
    axy_r=(2, 4),
    axs_s=(2, 4),
    axs_r=(2, 4),
    left_s=(4,),
    left_r=(4,),
    inner_s=(4,),
    inner_r=(4,),
    wide_s=(2, 4, PAIRS),
    wide_r=(2, 3, 8),
    att_s=(2, 8),
    att_r=(2, PAIRS),
    hid_s=(2, 4),
    hid_r=(2, 4),
    stat_s=(2, 4),
    stat_r=(2, 4),
    part_s=(2, 4),
    part_r=(2, 4),
    sub_s=(4,),
    sub_r=(4,),
)


def make_picks(lengths_ref, section, my_pair, picks_ref):
    tokens = lax.broadcasted_iota(jnp.int32, (GROUP_TOKENS, PAIR_LANES), 0)
    lane = lax.broadcasted_iota(jnp.int32, (GROUP_TOKENS, PAIR_LANES), 1)
    row_id = jnp.zeros_like(tokens)
    first = jnp.zeros_like(tokens)
    end = 0
    for row in range(lengths_ref.shape[1]):
        end = end + lengths_ref[section, row]
        passed = tokens >= end
        row_id = row_id + jnp.where(passed, 1, 0)
        first = jnp.where(passed, end, first)
    pos = (tokens - first).astype(F32)
    number = lax.shift_right_logical(lane, 2)
    row = lane - 4 * number
    ratio = jnp.zeros(lane.shape, F32)
    for i, each in enumerate(RATIOS):
        ratio = jnp.where(number == i, float(each), ratio)
    valid = ratio > 0.5
    ratio = jnp.where(valid, ratio, 1.0)

    def residue(values):
        return values - ratio * jnp.floor((values + 0.5) / ratio)

    residues = residue(pos)
    for head in range(2):
        wanted = residue(jnp.full(lane.shape, 2 * my_pair + head, jnp.int32).astype(F32))
        fits = valid & (row == row_id) & (jnp.abs(residues - wanted) < 0.5)
        picks_ref[head] = jnp.where(fits, 1.0, 0.0).astype(BF16)


def forward_kernel(lengths, *refs):
    b = Named([FORE_VMEM, FORE_ANY, FORE_OUT, FORE_SCRATCH, FORE_SEMS], refs)
    p = Place()
    me, section, peers, core = (p.me, p.section, p.peers, p.core)
    chip, high, low = (p.chip, p.high, p.low)

    barrier = pltpu.get_barrier_semaphore()
    greet_all(barrier, section, me)

    def block_from_qkv(layer):
        return pltpu.make_async_copy(
            b.qkv_w.at[layer, :, pl.ds(pl.multiple_of(lax.rem(section, 3) * D, D), D)],
            b.wa.at[layer, section, high, low, core],
            b.load_sem.at[layer, 0],
        )

    def block_from_out(layer):
        return pltpu.make_async_copy(
            b.out_w.at[layer], b.wa.at[layer, section, high, low, core], b.load_sem.at[layer, 0]
        )

    def load_up(layer):
        return pltpu.make_async_copy(b.up_w.at[layer], b.raw_up.at[layer], b.load_sem.at[layer, 1])

    def load_down(layer):
        return pltpu.make_async_copy(
            b.down_w.at[layer, pl.ds(pl.multiple_of(section * SHARD, SHARD), SHARD)],
            b.wf.at[layer, 1, high, low, core],
            b.load_sem.at[layer, 2],
        )

    def load_embeds(k):
        return pltpu.make_async_copy(
            b.embeds_in.at[peers[k]], b.embeds.at[k], b.embeds_sem.at[k]
        )

    for layer in range(2):

        @pl.when(section != 3)
        def _():
            block_from_qkv(layer).start()

        @pl.when(section == 3)
        def _():
            block_from_out(layer).start()

        if layer == 0:
            for k in range(4):
                load_embeds(k).start()
        load_up(layer).start()
        load_down(layer).start()

    def block_loaded(layer):
        @pl.when(section != 3)
        def _():
            block_from_qkv(layer).wait()

        @pl.when(section == 3)
        def _():
            block_from_out(layer).wait()

    def pick_up(layer):
        load_up(layer).wait()
        load_down(layer).wait()
        raw = b.raw_up[layer]
        for s in range(4):

            @pl.when(section == s)
            def _():
                b.wf[layer, 0, high, low, core] = jnp.concatenate(
                    [
                        raw[:, (4 * j + s) * SHARD : (4 * j + s + 1) * SHARD].astype(F32)
                        for j in range(8)
                    ],
                    1,
                ).astype(BF16)

    def line_gather(number, base):
        pairs = [(b.line_s.at[number, i], b.line_r.at[number, i]) for i in range(3)]
        return LineGather(p, base, *pairs)

    block = [line_gather(layer, b.wa.at[layer, section]) for layer in range(2)]
    feed_lines = [
        [line_gather(2 + 2 * layer + which, b.wf.at[layer, which]) for which in range(2)]
        for layer in range(2)
    ]

    def first_z(step, source):
        view = b.wa.at[0, section, lax.div(source, 2), lax.rem(source, 2), core]
        return remote(
            view,
            view,
            b.az_s.at[step],
            b.az_r.at[step],
            "seq",
            2 * lax.rem(chip + step, 4) + core,
        )

    def block_plane(layer, k, slot):
        view = b.wa.at[layer, slot, :, :, core]
        return remote(view, view, b.axy_s.at[layer, k], b.axy_r.at[layer, k], "section", peers[k])

    def block_across(layer, k, side):
        view = b.wa.at[layer, peers[k], :, :, side]
        return remote(view, view, b.axs_s.at[layer, k], b.axs_r.at[layer, k], "seq", p.sibling)

    for layer in range(2):
        gains = b.gains[layer].astype(F32)
        biases = b.biases[layer].astype(F32)
        hidden_gain = b.hgains[layer : layer + 1, :].astype(F32)
        hidden_bias = b.hbiases[layer].astype(F32)
        lines = [gains, biases]
        for each in (hidden_gain, hidden_bias[0:1, :], hidden_bias[1:2, :]):
            for s in range(4):
                lines.append(each[:, s * SHARD : (s + 1) * SHARD])
        lines.append(jnp.zeros((11, SHARD), F32))
        packed = jnp.concatenate(lines, 0)
        packed = jnp.concatenate([packed, jnp.zeros((32, PAIR_LANES - SHARD), F32)], 1)
        b.small_src[layer] = packed.astype(BF16)
    b.small[me] = b.small_src[...]
    make_picks(lengths, section, p.my_pair, b.picks)
    b.logs[...] = jnp.zeros_like(b.logs)
    block_loaded(0)
    pl.semaphore_wait(barrier, 31)

    def small_copy(step):
        return remote(
            b.small_src,
            b.small.at[me],
            b.small_s.at[step],
            b.small_r.at[step],
            "seq",
            lax.rem(me + step, 8),
        )

    for step in range(1, 8):
        small_copy(step).start()
    for step in range(1, 4):
        first_z(step, chip).start()
    pick_up(0)
    for step in range(1, 8):
        source = lax.rem(me + 8 - step, 8)
        remote(
            b.small_src,
            b.small.at[source],
            b.small_s.at[step],
            b.small_r.at[step],
            "seq",
            source,
        ).wait_recv()
    for layer in range(2):
        pieces = []
        for j in range(8):
            small = b.small[j, layer].astype(F32)
            lines = [small[0:9]]
            for third in range(3):
                line = jnp.zeros((1, PAIR_LANES), F32)
                for s in range(4):
                    at = 9 + 4 * third + s
                    line = line + jnp.where(section == s, small[at : at + 1], 0.0)
                lines.append(line)
            lines.append(jnp.zeros((4, PAIR_LANES), F32))
            pieces.append(jnp.concatenate(lines, 0)[:, 0:SHARD])
        b.vecs[layer] = jnp.concatenate(pieces, 1)

    def stores(layer, chosen):
        pairs = (
            (b.wf.at[layer], b.wf_out.at[layer]),
            (b.qkv.at[layer], b.qkv_out.at[layer]),
            (b.pa.at[layer], b.pa_out.at[layer]),
            (b.pt.at[layer], b.pt_out.at[layer]),
            (b.hid.at[layer], b.hid_out.at[layer]),
            (b.up.at[layer], b.up_out.at[layer]),
            (b.stat.at[layer], b.stat_out.at[layer]),
            (b.left.at[layer], b.left_out.at[layer]),
            (b.att.at[layer], b.att_out.at[layer]),
            (b.streams.at[pl.ds(2 * layer, 2)], b.streams_out.at[pl.ds(2 * layer, 2)]),
            (b.picks.at[layer], b.picks_out.at[layer]),
        )
        return [
            pltpu.make_async_copy(source, target, b.store_sem.at[layer, i])
            for i, (source, target) in enumerate(pairs)
            if i in chosen
        ]

    def store_block(layer, slot, number):
        return pltpu.make_async_copy(
            b.wa.at[layer, slot], b.wa_out.at[layer, slot], b.store_sem.at[layer, number]
        )

    def wide_copy(layer, k, pair):
        return remote_both(
            b.proj_send.at[k, pair],
            b.qkv.at[layer, lax.rem(section, 3), rows_of(me)],
            b.wide_s.at[layer, k, pair],
            b.wide_r.at[layer, lax.rem(section, 3), me],
            peers[k],
            OWNERS[pair],
        )

    def project(layer, arrive):
        vec = b.vecs.at[layer]

        @pl.when(section != 3)
        def _():
            bias = jnp.where(section == 2, vec[6:7, :], 0.0)
            for k in range(4):
                if k > 0:
                    arrive(k)
                part = mul(b.left[layer, slot_rows(k), :], square(b.wa.at[layer, section])) + bias
                part = part.astype(BF16)
                for pair, owner in enumerate(OWNERS):
                    b.proj_send[k, pair] = part[:, pair * PAIR_LANES : (pair + 1) * PAIR_LANES]
                    if k > 0:
                        wide_copy(layer, k, pair).start()
                    else:

                        @pl.when(me != owner)
                        def _():
                            wide_copy(layer, k, pair).start()

                        @pl.when(me == owner)
                        def _():
                            b.qkv[layer, section, rows_of(me), :] = b.proj_send[k, pair]

    def wait_projected(layer):
        @pl.when(p.is_owner)
        def _():
            for third in range(3):
                for source in range(8):

                    @pl.when((section != third) | (me != source))
                    def _():
                        remote_both(
                            b.proj_send.at[0, 0],
                            b.qkv.at[layer, third, pl.ds(source * TOKENS, TOKENS)],
                            b.wide_s.at[layer, 0, 0],
                            b.wide_r.at[layer, third, source],
                            third,
                            source,
                        ).wait_recv()

        @pl.when(section != 3)
        def _():
            for k in range(4):
                for pair, owner in enumerate(OWNERS):
                    if k > 0:
                        wide_copy(layer, k, pair).wait_send()
                    else:

                        @pl.when(me != owner)
                        def _():
                            wide_copy(layer, k, pair).wait_send()

    def back_copy(layer, target):
        return remote(
            b.att_send.at[pl.ds(target * TOKENS, TOKENS)],
            b.att_recv.at[layer, p.my_pair],
            b.att_s.at[layer, target],
            b.att_r.at[layer, p.my_pair],
            "seq",
            target,
        )

    def attend(layer):
        lane = lax.broadcasted_iota(jnp.int32, (QUERY_STEP, PAIR_LANES), 1)
        first_half = lane < HEAD_DIM
        for step in range(GROUP_TOKENS // QUERY_STEP):
            start = step * QUERY_STEP
            keys_end = start + QUERY_STEP
            rows = slice(start, keys_end)
            query = b.qkv[layer, 0, rows, :] * jnp.asarray(SCALE, BF16)
            keys = b.qkv[layer, 1, 0:keys_end, :]
            values = b.qkv[layer, 2, 0:keys_end, :]
            causal = lax.broadcasted_iota(jnp.int32, (QUERY_STEP, keys_end), 1) <= (
                start + lax.broadcasted_iota(jnp.int32, (QUERY_STEP, keys_end), 0)
            )
            sums = []
            totals = []
            logs = jnp.zeros((1, PAIR_LANES), F32)
            picked_sum = jnp.zeros((1, PAIR_LANES), F32)
            for head in range(2):
                mine = first_half if head == 0 else ~first_half
                own_query = jnp.where(mine, query, jnp.zeros_like(query))
                scores = mul_nt(own_query, keys)
                raised = jnp.where(causal, jnp.exp(scores), 0.0)
                pick_query = b.picks[head, rows, :]
                pick_keys = b.picks[head, 0:keys_end, :]
                counts = mul_nt(pick_query, pick_keys)
                weighted = (raised * counts).astype(BF16)
                sums.append(mul(weighted, values))
                pattern = mul(raised.astype(BF16), pick_keys)
                picked = pick_query.astype(F32)
                totals.append(jnp.sum(pattern * picked, -1, keepdims=True))
                chosen = picked > 0.5
                logs = logs + jnp.sum(
                    jnp.where(chosen, jnp.log(jnp.where(chosen, pattern, 1.0)), 0.0),
                    0,
                    keepdims=True,
                )
                picked_sum = picked_sum + jnp.sum(picked, 0, keepdims=True)
            b.logs[layer : layer + 1, :] += logs
            if layer == 0:
                b.logs[2:3, :] += picked_sum
            total = jnp.where(first_half, totals[0], totals[1])
            attended = jnp.where(first_half, sums[0], sums[1]) / total
            b.pa[layer, rows, :] = attended
            b.pt[layer, rows, :] = total
            b.att_send[rows, :] = attended.astype(BF16)
            for target in (2 * step, 2 * step + 1):

                @pl.when(me != target)
                def _():
                    back_copy(layer, target).start()

                @pl.when(me == target)
                def _():
                    b.att_recv[layer, p.my_pair] = b.att_send[
                        target * TOKENS : (target + 1) * TOKENS, :
                    ]

    def attention_rest(layer, inputs_ref, after):
        vec = b.vecs.at[layer]
        wait_projected(layer)
        feed_lines[layer][0].start()
        after()

        @pl.when(p.is_owner)
        def _():
            attend(layer)

        feed_lines[layer][0].pass_line()
        for k in range(1, 4):

            @pl.when(peers[k] == 3)
            def _():
                block_plane(layer, k, peers[k]).wait_recv()
                block_across(layer, k, core).start()

        for pair, owner in enumerate(OWNERS):

            @pl.when(me != owner)
            def _():
                remote(
                    b.att_send.at[pl.ds(0, TOKENS)],
                    b.att_recv.at[layer, pair],
                    b.att_s.at[layer, 0],
                    b.att_r.at[layer, pair],
                    "seq",
                    owner,
                ).wait_recv()

            b.att[layer, :, pair * PAIR_LANES : (pair + 1) * PAIR_LANES] = b.att_recv[layer, pair]
        inner_unit, unused = standardize(b.att[layer].astype(F32))
        inner = (inner_unit * vec[1:2, :] + vec[4:5, :]).astype(BF16)
        if layer == 0:
            b.inner[...] = inner
        for k in range(1, 4):

            @pl.when(peers[k] == 3)
            def _():
                block_across(layer, k, 1 - core).wait_recv()

        branch = mul(inner, square(b.wa.at[layer, 3])) + vec[7:8, :]
        b.streams[2 * layer] = (inputs_ref[...].astype(F32) + branch).astype(BF16)

    def attention_drain(layer):
        @pl.when(p.is_owner)
        def _():
            for target in range(8):

                @pl.when(me != target)
                def _():
                    back_copy(layer, target).wait_send()

    def feed(layer, resting, parting):
        vec = b.vecs.at[layer]
        inputs = b.streams[2 * layer].astype(F32)
        unit, unused = standardize(inputs)
        b.hid[layer, slot_rows(0), :] = (unit * vec[2:3, :] + vec[5:6, :]).astype(BF16)
        hidden_copies = [
            remote(
                b.hid.at[layer, pl.ds(0, TOKENS)],
                b.hid.at[layer, pl.ds(k * TOKENS, TOKENS)],
                b.hid_s.at[layer, k],
                b.hid_r.at[layer, k],
                "section",
                peers[k],
            )
            for k in range(1, 4)
        ]
        for copy in hidden_copies:
            copy.start()
        up_line, down_line = feed_lines[layer]
        up_line.pass_core()
        down_line.start()
        up_line.ready()
        for k in range(4):
            if k > 0:
                hidden_copies[k - 1].wait_recv()
            upward = mul(b.hid[layer, slot_rows(k), :], square(b.wf.at[layer, 0])) + vec[10:11, :]
            b.up[layer, slot_rows(k), :] = upward
            values, unused = gelu_parts(upward)
            b.active[slot_rows(k), :] = values
            mean = jnp.mean(values, -1, keepdims=True)
            center = values - mean
            b.columns[slot_rows(k), :] = two_columns(
                mean, jnp.sum(center * center, -1, keepdims=True)
            )
            if k == 0:
                down_line.pass_line()
        stat_copies = share_stats(
            b.columns[...],
            b.stat_send,
            b.stat_recv.at[layer],
            b.stat_s.at[layer],
            b.stat_r.at[layer],
            peers,
        )
        down_line.pass_core()
        resting()
        for copy in stat_copies:
            copy.wait_recv()
        b.stat_rows[...] = jnp.zeros((PAIR_LANES, WIDE), F32)
        for k in range(4):
            means = [b.stat_recv[layer, other, 0:1, slot_rows(k ^ other)] for other in range(4)]
            squares = [b.stat_recv[layer, other, 1:2, slot_rows(k ^ other)] for other in range(4)]
            mean = (means[0] + means[1] + means[2] + means[3]) * 0.25
            spread = squares[0] + squares[1] + squares[2] + squares[3]
            for each in means:
                spread = spread + D * (each - mean) * (each - mean)
            b.stat_rows[0:1, slot_rows(k)] = mean
            b.stat_rows[1:2, slot_rows(k)] = lax.rsqrt(spread * (1.0 / FF) + EPSILON)
        b.stat[layer] = b.stat_rows[...].T
        down_line.ready()
        branch = None
        part_copies = []
        for k in (3, 1, 2, 0):
            both = b.stat[layer, slot_rows(k), :]
            inner = (
                (b.active[slot_rows(k), :] - both[:, 0:1]) * both[:, 1:2] * vec[9:10, :]
                + vec[11:12, :]
            ).astype(BF16)
            part = mul(inner, square(b.wf.at[layer, 1]))
            if k == 0:
                branch = part
            else:
                b.part_send[k] = part.astype(BF16)
                part_copies.append(
                    remote(
                        b.part_send.at[k],
                        b.part_recv.at[layer, k],
                        b.part_s.at[layer, k],
                        b.part_r.at[layer, k],
                        "section",
                        peers[k],
                    )
                )
                part_copies[-1].start()
        parting()
        for k, copy in zip((3, 1, 2), part_copies):
            copy.wait_recv()
            branch = branch + b.part_recv[layer, k].astype(F32)
        b.streams[2 * layer + 1] = (inputs + branch + vec[8:9, :]).astype(BF16)
        for copy in hidden_copies + stat_copies + part_copies:
            copy.wait_send()

    def sub_away(number):
        return remote(
            b.streams.at[number],
            b.sub.at[section],
            b.sub_s.at[number],
            b.sub_r.at[section],
            "section",
            number,
        )

    def sub_own(number):
        return pltpu.make_async_copy(
            b.streams.at[number], b.sub.at[section], b.sub_s.at[number]
        )

    def send_sub(number):
        @pl.when(section != number)
        def _():
            sub_away(number).start()

        @pl.when(section == number)
        def _():
            sub_own(number).start()

    for k in range(4):
        load_embeds(k).wait()

        @pl.when(section != 3)
        def _():
            unit, unused = standardize(b.embeds[k].astype(F32))
            b.left[0, slot_rows(k), :] = (
                unit * b.vecs[0, 0:1, :] + b.vecs[0, 3:4, :]
            ).astype(BF16)
    pick_up(1)
    for step in range(1, 4):
        first_z(step, lax.rem(chip + 4 - step, 4)).wait_recv()
    block[0].cores(core).start()

    @pl.when(section == 3)
    def _():
        for k in range(1, 4):
            block_plane(0, k, section).start()

    block[0].ready()
    project(0, lambda k: None)

    attention_rest(0, b.embeds.at[0], lambda: None)

    def resting_first():
        block_loaded(1)
        block[1].start()

    def parting_first():
        attention_drain(0)
        block[1].pass_line()

    feed(0, resting_first, parting_first)

    second = b.vecs.at[1]
    unit, unused = standardize(b.streams[1].astype(F32))
    b.left[1, slot_rows(0), :] = (unit * second[0:1, :] + second[3:4, :]).astype(BF16)

    def left_copy(k):
        return remote(
            b.left.at[1, pl.ds(0, TOKENS)],
            b.left.at[1, pl.ds(k * TOKENS, TOKENS)],
            b.left_s.at[k],
            b.left_r.at[k],
            "section",
            peers[k],
        )

    for k in (3, 1, 2):

        @pl.when(peers[k] != 3)
        def _():
            left_copy(k).start()

    for copy in stores(0, (0, 1, 2, 3, 4, 5, 6, 8, 9, 10)):
        copy.start()
    block[1].pass_core()
    for k in range(1, 4):

        @pl.when(peers[k] != 3)
        def _():
            left_copy(k).wait_send()

    @pl.when(section == 3)
    def _():
        for k in range(1, 4):
            block_plane(1, k, section).start()

    block[1].ready()
    project(1, lambda k: left_copy(k).wait_recv())

    def inner_copy(k):
        return remote(
            b.inner,
            b.left.at[0, pl.ds(k * TOKENS, TOKENS)],
            b.inner_s.at[k],
            b.inner_r.at[k],
            "section",
            peers[k],
        )

    def after_second():
        for k in range(1, 4):

            @pl.when(peers[k] == 3)
            def _():
                inner_copy(k).start()

        @pl.when(section == 3)
        def _():
            b.left[0, slot_rows(0), :] = b.inner[...]

        send_sub(0)
        send_sub(1)

    attention_rest(1, b.streams.at[1], after_second)

    def parting_second():
        for copy in stores(1, (0, 1, 2, 3, 4, 5, 6, 7, 8, 10)):
            copy.start()

        @pl.when(section == 3)
        def _():
            for k in range(1, 4):
                inner_copy(k).wait_recv()

        for copy in stores(0, (7,)):
            copy.start()
        for layer in range(2):
            store_block(layer, section, 11).start()

            @pl.when(section != 3)
            def _():
                store_block(layer, 3, 12).start()

        attention_drain(1)

    feed(1, lambda: None, parting_second)
    for copy in stores(1, (9,)):
        copy.start()
    for step in range(1, 8):
        small_copy(step).wait_send()
    for step in range(1, 4):
        first_z(step, chip).wait_send()
    block[0].cores(core).wait_send()
    block[1].drain()
    for layer in range(2):
        for line in feed_lines[layer]:
            line.drain()
    for layer in range(2):
        for k in range(1, 4):

            @pl.when(section == 3)
            def _():
                block_plane(layer, k, section).wait_send()

            @pl.when(peers[k] == 3)
            def _():
                block_across(layer, k, core).wait_send()

    for k in range(1, 4):

        @pl.when(peers[k] == 3)
        def _():
            inner_copy(k).wait_send()

    for number in range(2):

        @pl.when(section != number)
        def _():
            sub_away(number).wait_send()

        @pl.when(section == number)
        def _():
            sub_own(number).wait()

    @pl.when(section < 2)
    def _():
        for k in range(1, 4):
            remote(
                b.streams.at[0],
                b.sub.at[peers[k]],
                b.sub_s.at[0],
                b.sub_r.at[peers[k]],
                "section",
                peers[k],
            ).wait_recv()

    for layer in range(2):
        for copy in stores(layer, range(11)):
            copy.wait()
    for layer in range(2):
        store_block(layer, section, 11).wait()

        @pl.when(section != 3)
        def _():
            store_block(layer, 3, 12).wait()


BACK_VMEM = dict(vecs=0, logs=0)
BACK_ANY = dict(
    cotangent_in=0,
    embeds_in=0,
    streams_in=0,
    att_in=0,
    picks_in=0,
    wa_in=0,
    wf_in=0,
    qkv_in=0,
    pa_in=0,
    pt_in=0,
    hid_in=0,
    up_in=0,
    stat_in=0,
    left_in=0,
)
BACK_OUT = dict(
    sub_f=((4, TOKENS, D), BF16, True),
    sub_g=((4, TOKENS, D), BF16, True),
    all_m=((6, 4, SHARD, D), BF16, True),
    all_v=((2, 4, SHARD, PAIR_LANES), BF16, True),
    log_total=((8, PAIR_LANES), F32, True),
)
BACK_SCRATCH = dict(
    wa=((2, 2, 2, 2, 2, SHARD, D), BF16),
    wf=((2, 2, 2, 2, SHARD, D), BF16),
    qkv=((3, GROUP_TOKENS, PAIR_LANES), BF16),
    pa=((GROUP_TOKENS, PAIR_LANES), F32),
    pt=((GROUP_TOKENS, PAIR_LANES), F32),
    hid=((WIDE, D), BF16),
    up=((WIDE, D), F32),
    stat=((WIDE, PAIR_LANES), F32),
    xs=((5, TOKENS, D), BF16),
    att=((2, TOKENS, D), BF16),
    picks=((2, GROUP_TOKENS, PAIR_LANES), BF16),
    cot=((TOKENS, D), BF16),
    streams=((4, TOKENS, D), BF16),
    grads=((WIDE, D), BF16),
    units=((WIDE, D), F32),
    unit_grads=((WIDE, D), F32),
    inners=((WIDE, D), BF16),
    lows=((WIDE, D), BF16),
    columns=((WIDE, PAIR_LANES), F32),
    stat_rows=((PAIR_LANES, WIDE), F32),
    part_send=((4, TOKENS, D), BF16),
    part_recv=((4, TOKENS, D), BF16),
    stat_send=((8, WIDE), F32),
    stat_recv=((4, 8, WIDE), F32),
    do_send=((PAIRS, TOKENS, PAIR_LANES), BF16),
    do_recv=((GROUP_TOKENS, PAIR_LANES), BF16),
    key_sum=((GROUP_TOKENS, PAIR_LANES), F32),
    value_sum=((GROUP_TOKENS, PAIR_LANES), F32),
    d_send=((3, GROUP_TOKENS, PAIR_LANES), BF16),
    d_recv=((2, 4, PAIRS, TOKENS, PAIR_LANES), BF16),
    left_src=((TOKENS, D), BF16),
    right_src=((TOKENS, D), BF16),
    left=((2, WIDE, D), BF16),
    right=((2, WIDE, D), BF16),
    vec_rows=((2, PAIR_LANES, D), F32),
    hidden_grad=((TOKENS, D), F32),
    prod=((6, 2, 2, 2, SHARD, D), BF16),
    prod_v=((2, 2, 2, 2, SHARD, PAIR_LANES), BF16),
    pair=((6, 2, 2, SHARD, D), BF16),
    pair_v=((2, 2, 2, SHARD, PAIR_LANES), BF16),
    near=((6, 2, SHARD, D), BF16),
    near_v=((2, 2, SHARD, PAIR_LANES), BF16),
    far=((6, SHARD, D), BF16),
    far_v=((2, SHARD, PAIR_LANES), BF16),
    done=((6, SHARD, D), BF16),
    done_v=((2, SHARD, PAIR_LANES), BF16),
    log_line=((8, 8, PAIR_LANES), F32),
    log_plane=((4, 8, PAIR_LANES), F32),
)
BACK_SEMS = dict(
    load_sem=(24,),
    block_sem=(2, 2),
    left_sem=(2,),
    g_s=(2, 4),
    g_r=(2, 4),
    stat_s=(2, 4),
    stat_r=(2, 4),
    part_s=(2, 4),
    part_r=(2, 4),
    do_s=(2, PAIRS),
    do_r=(2, 8),
    d_s=(2, 3, 8),
    d_r=(2, 4, PAIRS),
    left_s=(2, 4),
    left_r=(2, 4),
    right_s=(2, 4),
    right_r=(2, 4),
    back_s=(2, 4),
    back_r=(2, 4),
    subf_s=(4,),
    subf_r=(4,),
    subg_s=(4,),
    subg_r=(4,),
    own_sem=(2,),
    pair_s=(8,),
    pair_r=(8,),
    near_s=(8,),
    near_r=(8,),
    far_s=(8,),
    far_r=(8,),
    all_s=(8, 4),
    all_r=(8, 4),
    log_s=(8,),
    log_r=(8,),
    log_plane_s=(4,),
    log_plane_r=(4,),
)


def backward_kernel(*refs):
    b = Named([BACK_VMEM, BACK_ANY, BACK_OUT, BACK_SCRATCH, BACK_SEMS], refs)
    p = Place()
    me, section, peers, core = (p.me, p.section, p.peers, p.core)
    high, low = (p.high, p.low)

    barrier = pltpu.get_barrier_semaphore()
    greet_all(barrier, section, me)

    def loads(first, pairs):
        return [
            pltpu.make_async_copy(source, target, b.load_sem.at[first + number])
            for number, (source, target) in enumerate(pairs)
        ]

    def feed_loads(layer):
        pairs = (
            (b.hid_in.at[layer], b.hid),
            (b.up_in.at[layer], b.up),
            (b.stat_in.at[layer], b.stat),
            (b.wf_in.at[layer], b.wf),
        )
        return loads(4 * layer, pairs)

    def attention_loads(layer):
        pairs = (
            (b.qkv_in.at[layer], b.qkv),
            (b.pa_in.at[layer], b.pa),
            (b.pt_in.at[layer], b.pt),
        )
        return loads(8 + 3 * layer, pairs)

    def common_loads():
        pairs = (
            (b.cotangent_in.at[section], b.cot),
            (b.embeds_in.at[section], b.xs.at[0]),
            (b.streams_in, b.xs.at[pl.ds(1, 4)]),
            (b.att_in, b.att),
            (b.picks_in, b.picks),
        )
        return loads(14, pairs)

    def block_load(layer, number):
        slot = 3 if number == 1 else section
        return pltpu.make_async_copy(
            b.wa_in.at[layer, slot], b.wa.at[layer, number], b.block_sem.at[layer, number]
        )

    def left_load(layer):
        return pltpu.make_async_copy(b.left_in.at[layer], b.left.at[layer], b.left_sem.at[layer])

    common = common_loads()
    common[0].start()
    for copy in feed_loads(1):
        copy.start()
    for layer in (1, 0):
        for number in (1, 0):
            block_load(layer, number).start()

    @pl.when(section != 3)
    def _():
        left_load(1).start()

    left_load(0).start()

    for copy in common[1:] + attention_loads(1):
        copy.start()
    b.log_line[me] = b.logs[...]
    common[0].wait()
    b.grads[slot_rows(0), :] = b.cot[...]
    pl.semaphore_wait(barrier, 31)

    def log_copy(step):
        return remote(
            b.logs,
            b.log_line.at[me],
            b.log_s.at[step],
            b.log_r.at[step],
            "seq",
            lax.rem(me + step, 8),
        )

    def log_plane_copy(k, slot):
        return remote(
            b.log_plane.at[slot],
            b.log_plane.at[slot],
            b.log_plane_s.at[k],
            b.log_plane_r.at[k],
            "section",
            peers[k],
        )

    def start_logs():
        for step in range(1, 8):
            log_copy(step).start()

    def sum_logs():
        for step in range(1, 8):
            source = lax.rem(me + 8 - step, 8)
            remote(
                b.logs,
                b.log_line.at[source],
                b.log_s.at[step],
                b.log_r.at[step],
                "seq",
                source,
            ).wait_recv()
        total = b.log_line[0]
        for j in range(1, 8):
            total = total + b.log_line[j]
        b.log_plane[section] = total
        for k in range(1, 4):
            log_plane_copy(k, section).start()

    def finish_logs():
        for k in range(1, 4):
            log_plane_copy(k, peers[k]).wait_recv()
        total = b.log_plane[0]
        for other in range(1, 4):
            total = total + b.log_plane[other]
        b.log_total[...] = total
        for step in range(1, 8):
            log_copy(step).wait_send()
        for k in range(1, 4):
            log_plane_copy(k, section).wait_send()

    class Matrix:
        def __init__(self, number):
            self.number = number
            if number < 6:
                self.i = number
                refs = (b.prod, b.pair, b.near, b.far, b.done, b.all_m)
            else:
                self.i = number - 6
                refs = (b.prod_v, b.pair_v, b.near_v, b.far_v, b.done_v, b.all_v)
            self.prod, self.pair, self.near, self.far, self.done, self.all = refs

        def store(self, value):
            for j in range(8):
                self.prod[self.i, j % 2, j // 4, j // 2 % 2] = value[
                    j * SHARD : (j + 1) * SHARD, :
                ].astype(BF16)

        def pair_copy(self):
            n = self.number
            return remote(
                self.prod.at[self.i, 1 - core],
                self.pair.at[self.i],
                b.pair_s.at[n],
                b.pair_r.at[n],
                "seq",
                p.sibling,
            )

        def near_copy(self):
            n = self.number
            return remote(
                self.prod.at[self.i, core, :, 1 - low],
                self.near.at[self.i],
                b.near_s.at[n],
                b.near_r.at[n],
                "seq",
                p.next,
            )

        def far_copy(self):
            n = self.number
            return remote(
                self.prod.at[self.i, core, 1 - high, low],
                self.far.at[self.i],
                b.far_s.at[n],
                b.far_r.at[n],
                "seq",
                p.across,
            )

        def all_copy(self, k, slot):
            n = self.number
            return remote(
                self.done.at[self.i],
                self.all.at[self.i, slot],
                b.all_s.at[n, k],
                b.all_r.at[n, k],
                "section",
                peers[k],
            )

        def own_copy(self):
            return pltpu.make_async_copy(
                self.done.at[self.i], self.all.at[self.i, section], b.all_s.at[self.number, 0]
            )

        def step_near(self):
            self.pair_copy().wait_recv()
            i = self.i
            for h in range(2):
                for l in range(2):
                    self.prod[i, core, h, l] = (
                        self.prod[i, core, h, l].astype(F32) + self.pair[i, h, l].astype(F32)
                    ).astype(BF16)
            self.near_copy().start()

        def step_far(self):
            self.near_copy().wait_recv()
            i = self.i
            for h in range(2):
                self.prod[i, core, h, low] = (
                    self.prod[i, core, h, low].astype(F32) + self.near[i, h].astype(F32)
                ).astype(BF16)
            self.far_copy().start()

        def step_plane(self):
            self.far_copy().wait_recv()
            i = self.i
            self.done[i] = (
                self.prod[i, core, high, low].astype(F32) + self.far[i].astype(F32)
            ).astype(BF16)
            for k in (3, 1, 2):
                self.all_copy(k, section).start()
            self.own_copy().start()

        def step_end(self):
            for k in range(1, 4):
                self.all_copy(k, peers[k]).wait_recv()
                self.all_copy(k, section).wait_send()
            self.own_copy().wait()
            self.pair_copy().wait_send()
            self.near_copy().wait_send()
            self.far_copy().wait_send()

    matrices = [Matrix(number) for number in range(8)]
    up1, down1, att1, up0, down0, att0, vec1, vec0 = matrices

    def sub_copies(number, forward):
        source = b.xs.at[pl.ds(1, 4)] if forward else b.streams
        target = b.sub_f if forward else b.sub_g
        send_sem = b.subf_s if forward else b.subg_s
        recv_sem = b.subf_r if forward else b.subg_r

        def away():
            return remote(
                source.at[number],
                target.at[section],
                send_sem.at[number],
                recv_sem.at[section],
                "section",
                number,
            )

        def own():
            return pltpu.make_async_copy(
                source.at[number], target.at[section], b.own_sem.at[0 if forward else 1]
            )

        return away, own

    def send_sub(number, forward):
        @pl.when(section != number)
        def _():
            sub_copies(number, forward)[0]().start()

        @pl.when(section == number)
        def _():
            sub_copies(number, forward)[1]().start()

    def drain_sub(number, forward):
        @pl.when(section != number)
        def _():
            sub_copies(number, forward)[0]().wait_send()

        @pl.when(section == number)
        def _():
            sub_copies(number, forward)[1]().wait()

    def receive_sub(source, forward):
        target = b.sub_f if forward else b.sub_g

        @pl.when(section != source)
        def _():
            remote(
                b.streams.at[0],
                target.at[source],
                (b.subf_s if forward else b.subg_s).at[0],
                (b.subf_r if forward else b.subg_r).at[source],
                "section",
                source,
            ).wait_recv()

    def feed_phase(layer, grad_ref, x_ref, hooks):
        phase = 1 - layer
        vec = b.vecs.at[layer]
        rows = b.vec_rows.at[layer]
        up_matrix = matrices[3 * phase]
        down_matrix = matrices[3 * phase + 1]
        early, middle, parting, late = hooks
        if layer == 0:
            b.grads[slot_rows(0), :] = grad_ref[...]
        grad_copies = [
            remote(
                b.grads.at[pl.ds(0, TOKENS)],
                b.grads.at[pl.ds(k * TOKENS, TOKENS)],
                b.g_s.at[phase, k],
                b.g_r.at[phase, k],
                "section",
                peers[k],
            )
            for k in range(1, 4)
        ]
        for k in (3, 1, 2):
            grad_copies[k - 1].start()
        rows[...] = jnp.zeros((PAIR_LANES, D), F32)
        early()
        feed_ready = feed_loads(layer)
        for copy in feed_ready[:3]:
            copy.wait()
        for k in range(4):
            both = b.stat[slot_rows(k), :]
            upward = b.up[slot_rows(k), :]
            values, below = gelu_parts(upward)
            b.up[slot_rows(k), :] = below + upward * (
                jnp.exp(-0.5 * upward * upward) * (0.5 / 3.141592653589793) ** 0.5
            )
            unit = (values - both[:, 0:1]) * both[:, 1:2]
            b.units[slot_rows(k), :] = unit
            b.inners[slot_rows(k), :] = (unit * vec[9:10, :] + vec[11:12, :]).astype(BF16)
        feed_ready[3].wait()
        gain_sum = jnp.zeros((1, D), F32)
        bias_sum = jnp.zeros((1, D), F32)
        for k in range(4):
            if k > 0:
                grad_copies[k - 1].wait_recv()
            unit = b.units[slot_rows(k), :]
            inner_grad = mul_nt(b.grads[slot_rows(k), :], square(b.wf.at[1]))
            gain_sum = gain_sum + jnp.sum(inner_grad * unit, 0, keepdims=True)
            bias_sum = bias_sum + jnp.sum(inner_grad, 0, keepdims=True)
            unit_grad = inner_grad * vec[9:10, :]
            b.unit_grads[slot_rows(k), :] = unit_grad
            b.columns[slot_rows(k), :] = two_columns(
                jnp.sum(unit_grad, -1, keepdims=True), jnp.sum(unit_grad * unit, -1, keepdims=True)
            )
        stat_copies = share_stats(
            b.columns[...],
            b.stat_send,
            b.stat_recv,
            b.stat_s.at[phase],
            b.stat_r.at[phase],
            peers,
        )
        rows[9:10, :] = gain_sum
        rows[11:12, :] = bias_sum
        down_matrix.store(mul_tn(b.inners[...], b.grads[...]))
        down_matrix.pair_copy().start()
        middle()
        for copy in stat_copies:
            copy.wait_recv()
        b.stat_rows[...] = jnp.zeros((PAIR_LANES, WIDE), F32)
        for k in range(4):
            for line in range(2):
                parts = [
                    b.stat_recv[other, line : line + 1, slot_rows(k ^ other)]
                    for other in range(4)
                ]
                b.stat_rows[line : line + 1, slot_rows(k)] = (
                    parts[0] + parts[1] + parts[2] + parts[3]
                ) * (1.0 / FF)
        b.columns[...] = b.stat_rows[...].T
        hidden_grad = None
        low_sum = jnp.zeros((1, D), F32)
        part_copies = []
        for k in (3, 1, 2, 0):
            rstd = b.stat[slot_rows(k), :][:, 1:2]
            both = b.columns[slot_rows(k), :]
            lowered = (
                rstd
                * (
                    b.unit_grads[slot_rows(k), :]
                    - both[:, 0:1]
                    - b.units[slot_rows(k), :] * both[:, 1:2]
                )
                * b.up[slot_rows(k), :]
            ).astype(BF16)
            b.lows[slot_rows(k), :] = lowered
            low_sum = low_sum + jnp.sum(lowered.astype(F32), 0, keepdims=True)
            part = mul_nt(lowered, square(b.wf.at[0]))
            if k == 0:
                hidden_grad = part
            else:
                b.part_send[k] = part.astype(BF16)
                part_copies.append(
                    remote(
                        b.part_send.at[k],
                        b.part_recv.at[k],
                        b.part_s.at[phase, k],
                        b.part_r.at[phase, k],
                        "section",
                        peers[k],
                    )
                )
                part_copies[-1].start()
        rows[10:11, :] = low_sum
        up_matrix.store(mul_tn(b.hid[...], b.lows[...]))
        up_matrix.pair_copy().start()
        unit, rstd = standardize(x_ref[...].astype(F32))
        parting()
        for k, copy in zip((3, 1, 2), part_copies):
            copy.wait_recv()
            hidden_grad = hidden_grad + b.part_recv[k].astype(F32)
        grad = grad_ref[...].astype(F32)
        number = 2 * layer + 1
        b.streams[number] = (
            grad + norm_back(unit, rstd, hidden_grad * vec[2:3, :])
        ).astype(BF16)
        rows[2:3, :] = jnp.sum(hidden_grad * unit, 0, keepdims=True)
        rows[5:6, :] = jnp.sum(hidden_grad, 0, keepdims=True)
        rows[8:9, :] = jnp.sum(grad, 0, keepdims=True)
        for copy in grad_copies + stat_copies + part_copies:
            copy.wait_send()
        late()

    def attention_phase(layer, grad_ref, x_ref, att_ref, hooks):
        phase = 1 - layer
        vec = b.vecs.at[layer]
        rows = b.vec_rows.at[layer]
        before, inside, after, during = hooks
        grad = grad_ref[...]
        inner_unit, inner_rstd = standardize(att_ref[...].astype(F32))
        block_load(layer, 1).wait()
        inner_grad = mul_nt(grad, square(b.wa.at[layer, 1]))
        att_grad = norm_back(inner_unit, inner_rstd, inner_grad * vec[1:2, :]).astype(BF16)
        for pair in range(PAIRS):
            b.do_send[pair] = att_grad[:, pair * PAIR_LANES : (pair + 1) * PAIR_LANES]

        def out_copy(pair):
            return remote(
                b.do_send.at[pair],
                b.do_recv.at[rows_of(me)],
                b.do_s.at[phase, pair],
                b.do_r.at[phase, me],
                "seq",
                OWNERS[pair],
            )

        for pair, owner in enumerate(OWNERS):

            @pl.when(me != owner)
            def _():
                out_copy(pair).start()

            @pl.when(me == owner)
            def _():
                b.do_recv[rows_of(me), :] = b.do_send[pair]

        def left_copy(k):
            return remote(
                b.left_src,
                b.left.at[layer, pl.ds(k * TOKENS, TOKENS)],
                b.left_s.at[phase, k],
                b.left_r.at[phase, k],
                "section",
                peers[k],
            )

        def right_copy(k):
            return remote(
                b.right_src,
                b.right.at[layer, pl.ds(k * TOKENS, TOKENS)],
                b.right_s.at[phase, k],
                b.right_r.at[phase, k],
                "section",
                peers[k],
            )

        unit, rstd = standardize(x_ref[...].astype(F32))
        b.left_src[...] = (inner_unit * vec[1:2, :] + vec[4:5, :]).astype(BF16)
        b.right_src[...] = grad
        for k in range(1, 4):

            @pl.when(peers[k] == 3)
            def _():
                right_copy(k).start()
                if layer == 1:
                    left_copy(k).start()

        if layer == 1:

            @pl.when(section == 3)
            def _():
                b.left[layer, slot_rows(0), :] = b.left_src[...]

        rows[1:2, :] = jnp.sum(inner_grad * inner_unit, 0, keepdims=True)
        rows[4:5, :] = jnp.sum(inner_grad, 0, keepdims=True)
        rows[7:8, :] = jnp.sum(grad.astype(F32), 0, keepdims=True)
        for copy in attention_loads(layer):
            copy.wait()

        def back_copy(third, target):
            return remote_both(
                b.d_send.at[third, pl.ds(target * TOKENS, TOKENS)],
                b.d_recv.at[layer, section, p.my_pair],
                b.d_s.at[phase, third, target],
                b.d_r.at[phase, section, p.my_pair],
                third,
                target,
            )

        @pl.when(p.is_owner)
        def _():
            for source in range(8):

                @pl.when(me != source)
                def _():
                    remote(
                        b.do_send.at[0],
                        b.do_recv.at[pl.ds(source * TOKENS, TOKENS)],
                        b.do_s.at[phase, 0],
                        b.do_r.at[phase, source],
                        "seq",
                        source,
                    ).wait_recv()

        before()

        @pl.when(p.is_owner)
        def _():
            b.key_sum[...] = jnp.zeros((GROUP_TOKENS, PAIR_LANES), F32)
            b.value_sum[...] = jnp.zeros((GROUP_TOKENS, PAIR_LANES), F32)
            lane = lax.broadcasted_iota(jnp.int32, (QUERY_STEP, PAIR_LANES), 1)
            first_half = lane < HEAD_DIM
            for step in reversed(range(GROUP_TOKENS // QUERY_STEP)):
                start = step * QUERY_STEP
                keys_end = start + QUERY_STEP
                block = slice(start, keys_end)
                plain_query = b.qkv[0, block, :]
                query = plain_query * jnp.asarray(SCALE, BF16)
                keys = b.qkv[1, 0:keys_end, :]
                values = b.qkv[2, 0:keys_end, :]
                causal = lax.broadcasted_iota(jnp.int32, (QUERY_STEP, keys_end), 1) <= (
                    start + lax.broadcasted_iota(jnp.int32, (QUERY_STEP, keys_end), 0)
                )
                head_grad = b.do_recv[block, :]
                inverse = 1.0 / b.pt[block, :]
                head_float = head_grad.astype(F32)
                products = head_float * b.pa[block, :]
                scaled = (head_float * inverse).astype(BF16)
                key_lanes = lax.broadcasted_iota(jnp.int32, (keys_end, PAIR_LANES), 1) < HEAD_DIM
                query_parts = []
                key_parts = []
                value_parts = []
                for head in range(2):
                    mine = first_half if head == 0 else ~first_half
                    own_query = jnp.where(mine, query, jnp.zeros_like(query))
                    own_grad = jnp.where(mine, head_grad, jnp.zeros_like(head_grad))
                    delta = jnp.sum(jnp.where(mine, products, 0.0), -1, keepdims=True)
                    own_inverse = jnp.max(jnp.where(mine, inverse, 0.0), -1, keepdims=True)
                    counts = mul_nt(b.picks[head, block, :], b.picks[head, 0:keys_end, :])
                    scores = mul_nt(own_query, keys)
                    weighted = jnp.where(causal, jnp.exp(scores) * counts, 0.0)
                    prob_grad = mul_nt(own_grad, values)
                    score_grad = (weighted * own_inverse * (prob_grad - delta)).astype(BF16)
                    query_parts.append(mul(score_grad, keys))
                    key_parts.append(mul_tn(score_grad, plain_query))
                    value_parts.append(mul_tn(weighted.astype(BF16), scaled))
                b.key_sum[0:keys_end, :] += jnp.where(key_lanes, key_parts[0], key_parts[1])
                b.value_sum[0:keys_end, :] += jnp.where(key_lanes, value_parts[0], value_parts[1])
                query_grad = jnp.where(first_half, query_parts[0], query_parts[1]) * SCALE
                b.d_send[0, block, :] = query_grad.astype(BF16)
                b.d_send[1, block, :] = (b.key_sum[block, :] * SCALE).astype(BF16)
                b.d_send[2, block, :] = b.value_sum[block, :].astype(BF16)
                for third in range(3):
                    for target in (2 * step, 2 * step + 1):
                        away = (section != third) | (me != target)

                        @pl.when(away)
                        def _():
                            back_copy(third, target).start()

                        @pl.when(~away)
                        def _():
                            b.d_recv[layer, section, p.my_pair] = b.d_send[
                                third, target * TOKENS : (target + 1) * TOKENS, :
                            ]

        inside()
        after()
        block_load(layer, 0).wait()

        def part_copy(k):
            return remote(
                b.part_send.at[k],
                b.part_recv.at[k],
                b.back_s.at[phase, k],
                b.back_r.at[phase, k],
                "section",
                peers[k],
            )

        @pl.when(section != 3)
        def _():
            if layer == 1:
                left_load(layer).wait()
            for k in (0, 2, 1, 3):
                for pair, owner in enumerate(OWNERS):
                    away = me != owner if k == 0 else True

                    @pl.when(away)
                    def _():
                        remote_both(
                            b.d_send.at[0, pl.ds(0, TOKENS)],
                            b.d_recv.at[layer, peers[k], pair],
                            b.d_s.at[phase, 0, 0],
                            b.d_r.at[phase, peers[k], pair],
                            peers[k],
                            owner,
                        ).wait_recv()

                    b.right[layer, slot_rows(k), pair * PAIR_LANES : (pair + 1) * PAIR_LANES] = (
                        b.d_recv[layer, peers[k], pair]
                    )
                part = mul_nt(b.right[layer, slot_rows(k), :], square(b.wa.at[layer, 0]))
                if k == 0:
                    b.hidden_grad[...] = part
                else:
                    b.part_send[k] = part.astype(BF16)
                    part_copy(k).start()

        @pl.when(section == 3)
        def _():
            b.right[layer, slot_rows(0), :] = b.right_src[...]
            b.hidden_grad[...] = jnp.zeros((TOKENS, D), F32)
            for k in range(1, 4):
                right_copy(k).wait_recv()
                if layer == 1:
                    left_copy(k).wait_recv()

        if layer == 0:
            left_load(layer).wait()
        matrix = matrices[3 * phase + 2]
        matrix.store(mul_tn(b.left[layer], b.right[layer]))
        matrix.pair_copy().start()
        value_sum = jnp.sum(b.right[layer].astype(F32), 0, keepdims=True)
        rows[6:7, :] = jnp.where(section == 2, value_sum, 0.0)
        during()
        for k in (3, 1, 2):

            @pl.when(peers[k] != 3)
            def _():
                part_copy(k).wait_recv()
                b.hidden_grad[...] += b.part_recv[k].astype(F32)

        hidden_grad = b.hidden_grad[...]
        b.streams[2 * layer] = (
            grad.astype(F32) + norm_back(unit, rstd, hidden_grad * vec[0:1, :])
        ).astype(BF16)
        rows[0:1, :] = jnp.sum(hidden_grad * unit, 0, keepdims=True)
        rows[3:4, :] = jnp.sum(hidden_grad, 0, keepdims=True)

        def drain():
            @pl.when(section != 3)
            def _():
                for k in range(1, 4):
                    part_copy(k).wait_send()

            for k in range(1, 4):

                @pl.when(peers[k] == 3)
                def _():
                    right_copy(k).wait_send()
                    if layer == 1:
                        left_copy(k).wait_send()

            for pair, owner in enumerate(OWNERS):

                @pl.when(me != owner)
                def _():
                    out_copy(pair).wait_send()

            @pl.when(p.is_owner)
            def _():
                for third in range(3):
                    for target in range(8):

                        @pl.when((section != third) | (me != target))
                        def _():
                            back_copy(third, target).wait_send()

        return drain

    def nothing():
        pass

    def middle_first():
        for copy in common[1:]:
            copy.wait()

    def late_first():
        for copy in feed_loads(0):
            copy.start()

    feed_phase(
        1,
        b.cot,
        b.xs.at[3],
        (start_logs, middle_first, down1.step_near, late_first),
    )

    def before_first():
        down1.step_far()
        send_sub(2, True)

    def during_first():
        up1.step_far()
        sum_logs()

    drain_first = attention_phase(
        1,
        b.streams.at[3],
        b.xs.at[2],
        b.att.at[1],
        (before_first, down1.step_plane, up1.step_near, during_first),
    )

    def early_second():
        vec1.store(b.vec_rows[1].T)
        vec1.pair_copy().start()
        drain_first()
        for copy in attention_loads(0):
            copy.start()
        att1.step_near()

    def middle_second():
        att1.step_far()
        vec1.step_near()
        up1.step_plane()

    def parting_second():
        down0.step_near()
        vec1.step_far()

    feed_phase(
        0,
        b.streams.at[2],
        b.xs.at[1],
        (early_second, middle_second, parting_second, nothing),
    )

    def before_second():
        down0.step_far()
        send_sub(3, True)

    def inside_second():
        att1.step_plane()
        vec1.step_plane()
        down0.step_plane()
        for number in (2, 1):
            send_sub(number, False)

        @pl.when(section == 3)
        def _():
            for k in range(4):
                b.sub_g[peers[k]] = b.right[1, slot_rows(k), :]

        finish_logs()

    def during_second():
        att0.step_near()
        up0.step_far()

    drain_second = attention_phase(
        0,
        b.streams.at[1],
        b.xs.at[0],
        b.att.at[0],
        (before_second, inside_second, up0.step_near, during_second),
    )
    vec0.store(b.vec_rows[0].T)
    vec0.pair_copy().start()
    att0.step_far()
    send_sub(0, False)
    vec0.step_near()
    up0.step_plane()
    vec0.step_far()
    att0.step_plane()
    vec0.step_plane()
    drain_second()
    for matrix in matrices:
        matrix.step_end()
    for number in range(3):
        drain_sub(number, False)

    @pl.when(section != 3)
    def _():
        for source in range(4):
            receive_sub(source, False)

    drain_sub(2, True)
    drain_sub(3, True)

    @pl.when(section >= 2)
    def _():
        for source in range(4):
            receive_sub(source, True)


def finish_kernel(
    all_m,
    all_v,
    sub_a,
    sub_f,
    sub_g,
    log_total,
    outputs_ref,
    grads_ref,
    qkv_ref,
    out_ref,
    up_ref,
    down_ref,
    gains_ref,
    biases_ref,
    hgains_ref,
    hbiases_ref,
    means_ref,
):
    outputs_ref[...] = jnp.where(lax.axis_index("section") >= 2, sub_f[...], sub_a[...])
    grads_ref[...] = sub_g[...]
    for layer in range(2):
        up_i = 3 * (1 - layer)
        down_i = up_i + 1
        for source in range(4):
            down_ref[layer, source * SHARD : (source + 1) * SHARD, :] = all_m[
                down_i, source
            ].astype(F32)
        for j in range(8):
            up_ref[layer, :, j * 4 * SHARD : (j + 1) * 4 * SHARD] = jnp.concatenate(
                [
                    all_m[up_i, source, :, j * SHARD : (j + 1) * SHARD].astype(F32)
                    for source in range(4)
                ],
                1,
            )
        lines = []
        for source in range(4):
            block = all_m[up_i + 2, source].astype(F32)
            if source < 3:
                qkv_ref[layer, :, source * D : (source + 1) * D] = block
            else:
                out_ref[layer] = block
            tail = all_v[1 - layer, source].astype(F32)
            tail = jnp.concatenate([tail, jnp.zeros((PAIR_LANES - SHARD, PAIR_LANES), F32)], 0)
            lines.append(tail.T)
        model = lines[0] + lines[1] + lines[2] + lines[3]
        gains_ref[layer] = model[0:3, 0:SHARD]
        biases_ref[layer] = model[3:9, 0:SHARD]
        hidden = jnp.concatenate([each[9:12, 0:SHARD] for each in lines], 1)
        hgains_ref[layer : layer + 1, :] = hidden[0:1, :]
        hbiases_ref[layer] = hidden[1:3, :]
    lane = lax.broadcasted_iota(jnp.int32, (8, PAIR_LANES), 1)
    number = lax.shift_right_logical(lane, 2)
    sums = jnp.zeros((8, PAIR_LANES), F32)
    for i in range(5):
        part = jnp.sum(jnp.where(number == i, log_total[...], 0.0), -1, keepdims=True)
        sums = sums + jnp.where(lane == i, part, 0.0)
    means = sums[0:2, :] / jnp.where(lane[0:2, :] < 5, sums[2:3, :], 1.0)
    means_ref[...] = means[:, 0:5]


def run_remote(kernel, number, lengths, near, far, outs, scratch, sems):
    vmem = pl.BlockSpec(memory_space=pltpu.VMEM)
    anywhere = pl.BlockSpec(memory_space=pl.ANY)
    smem = pl.BlockSpec(memory_space=pltpu.SMEM)
    return pl.pallas_call(
        kernel,
        out_shape=[shaped(out[0], out[1]) for out in outs.values()],
        in_specs=[smem] * len(lengths) + [vmem] * len(near) + [anywhere] * len(far),
        out_specs=[vmem if out[2] else anywhere for out in outs.values()],
        scratch_shapes=[pltpu.VMEM(item[0], item[1]) for item in scratch.values()]
        + [pltpu.SemaphoreType.DMA(item) for item in sems.values()],
        compiler_params=pltpu.CompilerParams(
            collective_id=number, has_side_effects=True, vmem_limit_bytes=KERNEL_VMEM_BYTES
        ),
        cost_estimate=pl.CostEstimate(
            flops=10**10, bytes_accessed=100_000_000, transcendentals=0
        ),
    )(*lengths, *near, *far)


def run_finish(*args):
    vmem = pl.BlockSpec(memory_space=pltpu.VMEM)
    outs = [
        shaped((4, TOKENS, D), BF16),
        shaped((4, TOKENS, D), BF16),
        shaped((2, SHARD, 3 * D), F32),
        shaped((2, SHARD, D), F32),
        shaped((2, SHARD, FF), F32),
        shaped((2, 4 * SHARD, D), F32),
        shaped((2, 3, SHARD), F32),
        shaped((2, 6, SHARD), F32),
        shaped((2, 4 * SHARD), F32),
        shaped((2, 2, 4 * SHARD), F32),
        shaped((2, 5), F32),
    ]
    return pl.pallas_call(
        finish_kernel,
        out_shape=outs,
        in_specs=[vmem] * len(args),
        out_specs=[vmem] * len(outs),
        compiler_params=pltpu.CompilerParams(vmem_limit_bytes=KERNEL_VMEM_BYTES),
    )(*args)


def quick_body(
    embeds,
    row_lengths,
    qkv_weight,
    out_weight,
    up_weight,
    down_weight,
    model_gains,
    model_biases,
    hidden_gains,
    hidden_biases,
    cotangent,
):
    fore = Named(
        [FORE_OUT],
        run_remote(
            forward_kernel,
            10,
            (row_lengths,),
            (model_gains, model_biases, hidden_gains, hidden_biases),
            (embeds, qkv_weight, out_weight, up_weight, down_weight),
            FORE_OUT,
            FORE_SCRATCH,
            FORE_SEMS,
        ),
    )
    back = Named(
        [BACK_OUT],
        run_remote(
            backward_kernel,
            20,
            (),
            (fore.vecs, fore.logs),
            (
                cotangent,
                embeds,
                fore.streams_out,
                fore.att_out,
                fore.picks_out,
                fore.wa_out,
                fore.wf_out,
                fore.qkv_out,
                fore.pa_out,
                fore.pt_out,
                fore.hid_out,
                fore.up_out,
                fore.stat_out,
                fore.left_out,
            ),
            BACK_OUT,
            BACK_SCRATCH,
            BACK_SEMS,
        ),
    )
    results = run_finish(
        back.all_m, back.all_v, fore.sub, back.sub_f, back.sub_g, back.log_total
    )
    return (results[0][None], results[1][None]) + tuple(results[2:])


def fits_quick(mesh):
    return mesh.shape["section"] == 4 and mesh.shape["seq"] == 8


def solution(mesh):
    return jax.shard_map(
        quick_body if fits_quick(mesh) else body,
        mesh=mesh,
        in_specs=(
            P(None, "seq", None),
            P(),
            P(None, "seq", None),
            P(None, "seq", None),
            P(None, "seq", None),
            P(None, "seq", None),
            P(None, None, "seq"),
            P(None, None, "seq"),
            P(None, "seq"),
            P(None, None, "seq"),
            P(None, "seq", None),
        ),
        out_specs=(
            P("section", None, "seq", None),
            P("section", None, "seq", None),
            P(None, "seq", None),
            P(None, "seq", None),
            P(None, "seq", None),
            P(None, "seq", None),
            P(None, None, "seq"),
            P(None, None, "seq"),
            P(None, "seq"),
            P(None, None, "seq"),
            P(),
        ),
        check_vma=False,
    )
```

```python
import jax
import jax.numpy as jnp
from jax import lax
from jax.experimental import pallas as pl
from jax.experimental.pallas import tpu as pltpu
from jax.sharding import PartitionSpec as P

D = 768
HEADS = 12
HEAD_DIM = 64
FF = 3072


WIDTHS = (2048, 4096, 8192, 16384, 32768)
RATIOS = (1, 2, 4, 6, 12)
EPSILON = 1e-05


def passed_along(value, axis, steps):
    count = lax.axis_size(axis)
    initial, last = (max(0, -steps), min(count, count - steps))
    return lax.ppermute(value, axis, [(source, source + steps) for source in range(initial, last)])


def norm_rows(inputs, gain_row, offset):
    center = inputs - jnp.mean(inputs, -1, keepdims=True)
    spread = jnp.mean(center * center, -1, keepdims=True)
    return center * lax.rsqrt(spread + EPSILON) * gain_row + offset


def place_rows(lengths, token_index):
    row_ends = jnp.cumsum(lengths)
    passed = token_index[:, None] >= row_ends[None, :]
    row_ids = jnp.sum(passed.astype(jnp.int32), 1)
    offsets = token_index - jnp.sum(jnp.where(passed, lengths[None, :], 0), 1)
    return (row_ids, offsets)


def query_chosen(query_pos):
    head_ids = jnp.arange(HEADS, dtype=jnp.int32)
    chosen = []
    for seg_width, seg_ratio in zip(WIDTHS, RATIOS):
        query_pick = query_pos % seg_width % seg_ratio
        chosen.append(query_pick[None, :] == (head_ids % seg_ratio)[:, None])
    return chosen


def pattern_allow(query_rows, query_pos, key_rows, key_pos):
    widths = jnp.array(WIDTHS, jnp.int32)[:, None]
    ratios = jnp.array(RATIOS, jnp.int32)[:, None]
    residue = jnp.arange(HEADS, dtype=jnp.int32)[None, :] % ratios
    query_mod = query_pos[None, :] % widths % ratios
    key_mod = key_pos[None, :] % widths % ratios
    query_ok = query_mod[:, None, :] == residue[:, :, None]
    key_ok = key_mod[:, None, :] == residue[:, :, None]
    common = (query_rows[:, None] == key_rows[None, :]) & (key_pos[None, :] <= query_pos[:, None])
    inside = common[None] & (
        (query_pos[None, :] // widths)[:, :, None] == (key_pos[None, :] // widths)[:, None, :]
    )
    return inside[:, None] & query_ok[:, :, :, None] & key_ok[:, :, None, :]


def block_rows(total_rows):
    step_rows = min(total_rows, 512)
    return step_rows


def split_heads(matrix):
    return matrix.reshape(matrix.shape[0], HEADS, HEAD_DIM)


def pair_terms(query_block, keys_block, query_rows, query_pos, key_rows, key_pos):
    scores = jnp.einsum(
        "qhe,khe->hqk", query_block, keys_block, preferred_element_type=jnp.float32
    ) * HEAD_DIM ** (-0.5)
    allowed = pattern_allow(query_rows, query_pos, key_rows, key_pos)
    counts = jnp.sum(allowed.astype(jnp.float32), 0)
    raised = jnp.exp(scores)
    return (raised, counts * raised, allowed)


def project_tokens(inputs, qkv_matrix, norm_gains, norm_biases):
    hidden = norm_rows(inputs, norm_gains[0], norm_biases[0]).astype(jnp.bfloat16)
    bias_row = jnp.concatenate(
        [jnp.zeros_like(norm_biases[3]), jnp.zeros_like(norm_biases[3]), norm_biases[3]]
    )
    projected = (jnp.dot(hidden, qkv_matrix, preferred_element_type=jnp.float32) + bias_row).astype(
        jnp.bfloat16
    )
    return (hidden, projected)


def attention_forward(section_in, projected, whole_keys, lengths, params, seq_index):
    out_matrix, norm_gains, norm_biases = (params[1], params[4], params[5])
    tok_rows = section_in.shape[0]
    inputs = section_in.astype(jnp.float32)
    queries = split_heads(projected[:, :D])
    query_rows, query_pos = place_rows(
        lengths, seq_index * tok_rows + jnp.arange(tok_rows, dtype=jnp.int32)
    )
    group_rows = whole_keys.shape[0]
    step_rows = block_rows(group_rows)

    def one_block(running, block_start):
        totals, pattern_sums, accumulated = running
        kv_block = lax.dynamic_slice_in_dim(whole_keys, block_start, step_rows, 0)
        key_rows, key_pos = place_rows(
            lengths, block_start + jnp.arange(step_rows, dtype=jnp.int32)
        )
        raised, weighted, allowed = pair_terms(
            queries, split_heads(kv_block[:, :D]), query_rows, query_pos, key_rows, key_pos
        )
        totals = totals + jnp.sum(weighted, -1)
        pattern_sums = pattern_sums + jnp.sum(jnp.where(allowed, raised[None], 0.0), -1)
        accumulated = accumulated + jnp.einsum(
            "hqk,khe->hqe",
            weighted.astype(jnp.bfloat16),
            split_heads(kv_block[:, D:]),
            preferred_element_type=jnp.float32,
        )
        return ((totals, pattern_sums, accumulated), None)

    start_sums = (
        jnp.zeros((HEADS, tok_rows), jnp.float32),
        jnp.zeros((len(WIDTHS), HEADS, tok_rows), jnp.float32),
        jnp.zeros((HEADS, tok_rows, HEAD_DIM), jnp.float32),
    )
    folded, unused = lax.scan(
        one_block, start_sums, jnp.arange(0, group_rows, step_rows, dtype=jnp.int32)
    )
    totals, pattern_sums, accumulated = folded
    attended = jnp.transpose(accumulated / totals[:, :, None], (1, 0, 2)).reshape(tok_rows, D)
    inner_norm = norm_rows(attended, norm_gains[1], norm_biases[1]).astype(jnp.bfloat16)
    branch = jnp.dot(inner_norm, out_matrix, preferred_element_type=jnp.float32) + norm_biases[4]
    section_out = (inputs + branch).astype(jnp.bfloat16)
    chosen = query_chosen(query_pos)
    log_terms = jnp.stack(
        [
            jnp.sum(
                jnp.where(pick_row, jnp.log(jnp.where(pick_row, pattern_sums[number], 1.0)), 0.0)
            )
            for number, pick_row in enumerate(chosen)
        ]
    )
    pick_counts = jnp.stack([jnp.sum(pick_row.astype(jnp.float32)) for pick_row in chosen])
    return (section_out, attended, totals, log_terms, pick_counts)


def feed_forward(section_in, params):
    up_matrix, down_matrix, norm_gains, norm_biases, hidden_gain, hidden_bias = (
        params[2],
        params[3],
        params[4],
        params[5],
        params[6],
        params[7],
    )
    tok_rows = section_in.shape[0]
    inputs = section_in.astype(jnp.float32)
    hidden = norm_rows(inputs, norm_gains[2], norm_biases[2]).astype(jnp.bfloat16)
    upward = jnp.dot(hidden, up_matrix, preferred_element_type=jnp.float32) + hidden_bias[0]
    inner_norm = norm_rows(
        jax.nn.gelu(upward, approximate=False), hidden_gain, hidden_bias[1]
    ).astype(jnp.bfloat16)
    branch = jnp.dot(inner_norm, down_matrix, preferred_element_type=jnp.float32) + norm_biases[5]
    section_out = (inputs + branch).astype(jnp.bfloat16)
    empty_terms = jnp.zeros((len(WIDTHS),), jnp.float32)
    return (
        section_out,
        jnp.zeros((tok_rows, D), jnp.float32),
        jnp.zeros((HEADS, tok_rows), jnp.float32),
        empty_terms,
        empty_terms,
    )


def attention_middle(
    section_in, grad_out, attended, totals, lengths, all_keys, projected, params, seq_index
):
    out_matrix, norm_gains, norm_biases = (params[1], params[4], params[5])
    scale_factor = HEAD_DIM ** (-0.5)
    tok_rows = section_in.shape[0]
    queries = split_heads(projected[:, :D])
    query_rows, query_pos = place_rows(
        lengths, seq_index * tok_rows + jnp.arange(tok_rows, dtype=jnp.int32)
    )
    inner_norm = norm_rows(attended, norm_gains[1], norm_biases[1]).astype(jnp.bfloat16)
    out_step = jnp.einsum("td,tf->df", inner_norm, grad_out, preferred_element_type=jnp.float32)
    inner_grad = jnp.einsum("tf,df->td", grad_out, out_matrix, preferred_element_type=jnp.float32)
    unused, inner_back = jax.vjp(norm_rows, attended, norm_gains[1], norm_biases[1])
    attended_grad, inner_gain_grad, inner_bias_grad = inner_back(inner_grad)
    low_attended = attended_grad.astype(jnp.bfloat16)
    head_grad = split_heads(low_attended)
    row_dots = jnp.einsum("qhe,qhe->hq", head_grad.astype(jnp.float32), split_heads(attended))
    scaled_grad = head_grad.astype(jnp.float32) / jnp.transpose(totals)[:, :, None]
    group_rows = all_keys.shape[0]
    step_rows = block_rows(group_rows)

    def grad_block(query_grad, block_start):
        kv_block = lax.dynamic_slice_in_dim(all_keys, block_start, step_rows, 0)
        keys_block = split_heads(kv_block[:, :D])
        values_block = split_heads(kv_block[:, D:])
        key_rows, key_pos = place_rows(
            lengths, block_start + jnp.arange(step_rows, dtype=jnp.int32)
        )
        raised, weighted, allowed = pair_terms(
            queries, keys_block, query_rows, query_pos, key_rows, key_pos
        )
        prob_grad = jnp.einsum(
            "qhe,khe->hqk", head_grad, values_block, preferred_element_type=jnp.float32
        )
        score_grad = (weighted / totals[:, :, None] * (prob_grad - row_dots[:, :, None])).astype(
            jnp.bfloat16
        )
        query_grad = (
            query_grad
            + jnp.einsum("hqk,khe->qhe", score_grad, keys_block, preferred_element_type=jnp.float32)
            * scale_factor
        )
        key_grad = (
            jnp.einsum("hqk,qhe->khe", score_grad, queries, preferred_element_type=jnp.float32)
            * scale_factor
        )
        value_grad = jnp.einsum(
            "hqk,qhe->khe",
            weighted.astype(jnp.bfloat16),
            scaled_grad,
            preferred_element_type=jnp.float32,
        )
        block_grad = jnp.concatenate(
            [key_grad.reshape(step_rows, D), value_grad.reshape(step_rows, D)], 1
        )
        return (query_grad, block_grad)

    query_grad, block_grads = lax.scan(
        grad_block,
        jnp.zeros((tok_rows, HEADS, HEAD_DIM), jnp.float32),
        jnp.arange(0, group_rows, step_rows, dtype=jnp.int32),
    )
    block_grads = block_grads.reshape(group_rows, 2 * D)
    return (
        query_grad.reshape(tok_rows, D),
        low_attended,
        row_dots,
        block_grads,
        out_step,
        inner_gain_grad,
        inner_bias_grad,
    )


def attention_finish(section_in, grad_out, middle, extra, params, grad_sums):
    qkv_matrix, norm_gains, norm_biases = (params[0], params[4], params[5])
    inputs = section_in.astype(jnp.float32)
    grad_float = grad_out.astype(jnp.float32)
    hidden = norm_rows(inputs, norm_gains[0], norm_biases[0]).astype(jnp.bfloat16)
    query_grad, low_attended, row_dots, block_grads, out_step, inner_gain_grad, inner_bias_grad = (
        middle
    )
    own_grads = extra[0]
    proj_grad = jnp.concatenate([query_grad, own_grads], 1).astype(jnp.bfloat16)
    qkv_step = jnp.einsum("td,tf->df", hidden, proj_grad, preferred_element_type=jnp.float32)
    value_bias_sums = jnp.sum(proj_grad[:, 2 * D :].astype(jnp.float32), 0)
    hidden_grad = jnp.einsum("tf,df->td", proj_grad, qkv_matrix, preferred_element_type=jnp.float32)
    unused_first, first_back = jax.vjp(norm_rows, inputs, norm_gains[0], norm_biases[0])
    input_grad, first_gain_grad, first_bias_grad = first_back(hidden_grad)
    qkv_sum, out_sum, up_sum, down_sum, gain_sum, bias_sum, hgain_sum, hbias_sum = grad_sums
    gain_sum = gain_sum.at[0].add(first_gain_grad).at[1].add(inner_gain_grad)
    bias_sum = (
        bias_sum.at[0]
        .add(first_bias_grad)
        .at[1]
        .add(inner_bias_grad)
        .at[3]
        .add(value_bias_sums)
        .at[4]
        .add(jnp.sum(grad_float, 0))
    )
    return (
        grad_float + input_grad,
        (
            qkv_sum + qkv_step,
            out_sum + out_step,
            up_sum,
            down_sum,
            gain_sum,
            bias_sum,
            hgain_sum,
            hbias_sum,
        ),
    )


def feed_backward(section_in, grad_out, params, grad_sums):
    up_matrix, down_matrix, norm_gains, norm_biases, hidden_gain, hidden_bias = (
        params[2],
        params[3],
        params[4],
        params[5],
        params[6],
        params[7],
    )
    inputs = section_in.astype(jnp.float32)
    grad_float = grad_out.astype(jnp.float32)
    hidden = norm_rows(inputs, norm_gains[2], norm_biases[2]).astype(jnp.bfloat16)
    upward = jnp.dot(hidden, up_matrix, preferred_element_type=jnp.float32) + hidden_bias[0]

    def inner_rows(upward_in, gain_row, bias_row):
        return norm_rows(jax.nn.gelu(upward_in, approximate=False), gain_row, bias_row)

    inner_value, inner_back = jax.vjp(inner_rows, upward, hidden_gain, hidden_bias[1])
    inner_norm = inner_value.astype(jnp.bfloat16)
    down_step = jnp.einsum("tf,td->fd", inner_norm, grad_out, preferred_element_type=jnp.float32)
    inner_grad = jnp.einsum("td,fd->tf", grad_out, down_matrix, preferred_element_type=jnp.float32)
    upward_grad, hgain_step, hbias_step = inner_back(inner_grad)
    low_upward = upward_grad.astype(jnp.bfloat16)
    up_step = jnp.einsum("td,tf->df", hidden, low_upward, preferred_element_type=jnp.float32)
    hidden_grad = jnp.einsum("tf,df->td", low_upward, up_matrix, preferred_element_type=jnp.float32)
    unused, first_back = jax.vjp(norm_rows, inputs, norm_gains[2], norm_biases[2])
    input_grad, first_gain_grad, first_bias_grad = first_back(hidden_grad)
    qkv_sum, out_sum, up_sum, down_sum, gain_sum, bias_sum, hgain_sum, hbias_sum = grad_sums
    gain_sum = gain_sum.at[2].add(first_gain_grad)
    bias_sum = bias_sum.at[2].add(first_bias_grad).at[5].add(jnp.sum(grad_float, 0))
    hbias_sum = (
        hbias_sum.at[0].add(jnp.sum(low_upward.astype(jnp.float32), 0)).at[1].add(hbias_step)
    )
    return (
        grad_float + input_grad,
        (
            qkv_sum,
            out_sum,
            up_sum + up_step,
            down_sum + down_step,
            gain_sum,
            bias_sum,
            hgain_sum + hgain_step,
            hbias_sum,
        ),
    )


def keep_slot(store, fresh, slot_id, in_range):
    previous = lax.dynamic_index_in_dim(store, slot_id, 0, False)
    return lax.dynamic_update_index_in_dim(store, jnp.where(in_range, fresh, previous), slot_id, 0)


def body(
    embeds,
    row_lengths,
    qkv_weight,
    out_weight,
    up_weight,
    down_weight,
    model_gains,
    model_biases,
    hidden_gains,
    hidden_biases,
    cotangent,
):
    section_id = lax.axis_index("section")
    seq_index = lax.axis_index("seq")
    section_count = lax.axis_size("section")
    micro_count = embeds.shape[0]
    tok_rows = embeds.shape[1]
    group_rows = tok_rows * lax.axis_size("seq")
    layer_id = section_id // 2
    attends = section_id % 2 == 0
    bias_count = model_biases.shape[1]

    def pick_layer(stacked):
        return lax.dynamic_index_in_dim(stacked, layer_id, 0, False)

    gathered = (
        lax.all_gather(pick_layer(qkv_weight), "seq", axis=0, tiled=True),
        lax.all_gather(pick_layer(out_weight), "seq", axis=0, tiled=True),
        lax.all_gather(pick_layer(up_weight), "seq", axis=0, tiled=True),
        lax.all_gather(pick_layer(down_weight), "seq", axis=0, tiled=True),
        lax.all_gather(pick_layer(model_gains), "seq", axis=1, tiled=True),
        lax.all_gather(pick_layer(model_biases), "seq", axis=1, tiled=True),
        lax.all_gather(pick_layer(hidden_gains), "seq", axis=0, tiled=True),
        lax.all_gather(pick_layer(hidden_biases), "seq", axis=1, tiled=True),
    )
    params = tuple(gathered[:4]) + tuple((vector.astype(jnp.float32) for vector in gathered[4:]))
    whole_shape = (0,)

    def make_projected(section_in):
        return project_tokens(section_in.astype(jnp.float32), params[0], params[4], params[5])[1]

    def skip_projected(section_in):
        return jnp.zeros((tok_rows, 3 * D), jnp.bfloat16)

    def run_attention(section_in, projected, whole_keys, lengths):
        return attention_forward(section_in, projected, whole_keys, lengths, params, seq_index)

    def run_feed(section_in, projected, whole_keys, lengths):
        return feed_forward(section_in, params)

    def forward_tick(running, tick_id):
        (
            incoming,
            kept_inputs,
            kept_attended,
            kept_totals,
            kept_whole,
            outputs,
            log_sums,
            pick_sums,
        ) = running
        micro_id = tick_id - section_id
        in_range = (micro_id >= 0) & (micro_id < micro_count)
        slot_id = jnp.clip(micro_id, 0, micro_count - 1)
        lengths = lax.dynamic_index_in_dim(row_lengths, slot_id, 0, False)
        section_in = jnp.where(
            section_id == 0, lax.dynamic_index_in_dim(embeds, slot_id, 0, False), incoming
        )
        projected = lax.cond(attends, make_projected, skip_projected, section_in)
        whole_keys = lax.all_gather(projected[:, D:], "seq", axis=0, tiled=True)
        section_out, attended, totals, log_terms, pick_counts = lax.cond(
            attends, run_attention, run_feed, section_in, projected, whole_keys, lengths
        )
        kept_inputs = keep_slot(kept_inputs, section_in, slot_id, in_range)
        kept_attended = keep_slot(kept_attended, attended, slot_id, in_range)
        kept_totals = keep_slot(kept_totals, totals, slot_id, in_range)
        outputs = keep_slot(outputs, section_out, slot_id, in_range)
        log_sums = log_sums + jnp.where(in_range, log_terms, 0.0)
        pick_sums = pick_sums + jnp.where(in_range, pick_counts, 0.0)
        incoming = passed_along(section_out, "section", 1)
        return (
            (
                incoming,
                kept_inputs,
                kept_attended,
                kept_totals,
                kept_whole,
                outputs,
                log_sums,
                pick_sums,
            ),
            None,
        )

    forward_start = (
        jnp.zeros((tok_rows, D), jnp.bfloat16),
        jnp.zeros((micro_count, tok_rows, D), jnp.bfloat16),
        jnp.zeros((micro_count, tok_rows, D), jnp.float32),
        jnp.zeros((micro_count, HEADS, tok_rows), jnp.float32),
        jnp.zeros((micro_count,) + whole_shape, jnp.bfloat16),
        jnp.zeros((micro_count, tok_rows, D), jnp.bfloat16),
        jnp.zeros((len(WIDTHS),), jnp.float32),
        jnp.zeros((len(WIDTHS),), jnp.float32),
    )
    ticks = jnp.arange(micro_count + section_count - 1, dtype=jnp.int32)
    forward_end, unused = lax.scan(forward_tick, forward_start, ticks)
    unused_in, kept_inputs, kept_attended, kept_totals, kept_whole, outputs, log_sums, pick_sums = (
        forward_end
    )
    block_shape = (group_rows, 2 * D)

    def middle_attention(section_in, grad_out, attended, totals, lengths, all_keys, projected):
        return attention_middle(
            section_in, grad_out, attended, totals, lengths, all_keys, projected, params, seq_index
        )

    def middle_feed(section_in, grad_out, attended, totals, lengths, all_keys, projected):
        return (
            jnp.zeros((tok_rows, D), jnp.float32),
            jnp.zeros((tok_rows, D), jnp.bfloat16),
            jnp.zeros((HEADS, tok_rows), jnp.float32),
            jnp.zeros(block_shape, jnp.float32),
            jnp.zeros((D, D), jnp.float32),
            jnp.zeros((D,), jnp.float32),
            jnp.zeros((D,), jnp.float32),
        )

    def finish_attention(section_in, grad_out, projected, middle, extra, lengths, grad_sums):
        return attention_finish(section_in, grad_out, middle, extra, params, grad_sums)

    def finish_feed(section_in, grad_out, projected, middle, extra, lengths, grad_sums):
        return feed_backward(section_in, grad_out, params, grad_sums)

    def backward_tick(running, tick_id):
        incoming, grad_sums, input_grads = running
        micro_id = micro_count - 1 - tick_id + (section_count - 1 - section_id)
        in_range = (micro_id >= 0) & (micro_id < micro_count)
        slot_id = jnp.clip(micro_id, 0, micro_count - 1)
        from_next = jnp.where(
            section_id == section_count - 1,
            lax.dynamic_index_in_dim(cotangent, slot_id, 0, False),
            incoming,
        )
        grad_out = jnp.where(in_range, from_next, jnp.zeros_like(from_next))
        section_in = lax.dynamic_index_in_dim(kept_inputs, slot_id, 0, False)
        attended = lax.dynamic_index_in_dim(kept_attended, slot_id, 0, False)
        totals = lax.dynamic_index_in_dim(kept_totals, slot_id, 0, False)
        lengths = lax.dynamic_index_in_dim(row_lengths, slot_id, 0, False)
        projected = lax.cond(attends, make_projected, skip_projected, section_in)
        all_keys = lax.all_gather(projected[:, D:], "seq", axis=0, tiled=True)
        middle = lax.cond(
            attends,
            middle_attention,
            middle_feed,
            section_in,
            grad_out,
            attended,
            totals,
            lengths,
            all_keys,
            projected,
        )
        extra = (lax.psum_scatter(middle[3], "seq", scatter_dimension=0, tiled=True),)
        section_grad, grad_sums = lax.cond(
            attends,
            finish_attention,
            finish_feed,
            section_in,
            grad_out,
            projected,
            middle,
            extra,
            lengths,
            grad_sums,
        )
        low_grad = section_grad.astype(jnp.bfloat16)
        input_grads = keep_slot(input_grads, low_grad, slot_id, in_range)
        incoming = passed_along(low_grad, "section", -1)
        return ((incoming, grad_sums, input_grads), None)

    grad_start = (
        jnp.zeros((D, 3 * D), jnp.float32),
        jnp.zeros((D, D), jnp.float32),
        jnp.zeros((D, FF), jnp.float32),
        jnp.zeros((FF, D), jnp.float32),
        jnp.zeros((3, D), jnp.float32),
        jnp.zeros((bias_count, D), jnp.float32),
        jnp.zeros((FF,), jnp.float32),
        jnp.zeros((2, FF), jnp.float32),
    )
    backward_start = (
        jnp.zeros((tok_rows, D), jnp.bfloat16),
        grad_start,
        jnp.zeros((micro_count, tok_rows, D), jnp.bfloat16),
    )
    backward_end, unused_back = lax.scan(backward_tick, backward_start, ticks)
    unused_grad, grad_sums, input_grads = backward_end
    shards = (
        lax.psum_scatter(grad_sums[0], "seq", scatter_dimension=0, tiled=True),
        lax.psum_scatter(grad_sums[1], "seq", scatter_dimension=0, tiled=True),
        lax.psum_scatter(grad_sums[2], "seq", scatter_dimension=0, tiled=True),
        lax.psum_scatter(grad_sums[3], "seq", scatter_dimension=0, tiled=True),
        lax.psum_scatter(grad_sums[4], "seq", scatter_dimension=1, tiled=True),
        lax.psum_scatter(grad_sums[5], "seq", scatter_dimension=1, tiled=True),
        lax.psum_scatter(grad_sums[6], "seq", scatter_dimension=0, tiled=True),
        lax.psum_scatter(grad_sums[7], "seq", scatter_dimension=1, tiled=True),
    )
    sources = (
        qkv_weight,
        out_weight,
        up_weight,
        down_weight,
        model_gains,
        model_biases,
        hidden_gains,
        hidden_biases,
    )
    placed = tuple(
        (
            lax.dynamic_update_index_in_dim(
                jnp.zeros(source.shape, jnp.float32), shard, layer_id, 0
            )
            for shard, source in zip(shards, sources)
        )
    )
    summed = (
        lax.psum(placed[0].astype(jnp.bfloat16), "section").astype(jnp.float32),
        lax.psum(placed[1].astype(jnp.bfloat16), "section").astype(jnp.float32),
        lax.psum(placed[2].astype(jnp.bfloat16), "section").astype(jnp.float32),
        lax.psum(placed[3].astype(jnp.bfloat16), "section").astype(jnp.float32),
        lax.psum(placed[4].astype(jnp.bfloat16), "section").astype(jnp.float32),
        lax.psum(placed[5].astype(jnp.bfloat16), "section").astype(jnp.float32),
        lax.psum(placed[6].astype(jnp.bfloat16), "section").astype(jnp.float32),
        lax.psum(placed[7].astype(jnp.bfloat16), "section").astype(jnp.float32),
    )
    layer_count = qkv_weight.shape[0]
    layer_terms = lax.dynamic_update_index_in_dim(
        jnp.zeros((layer_count, len(WIDTHS)), jnp.float32), log_sums, layer_id, 0
    )
    layer_picks = lax.dynamic_update_index_in_dim(
        jnp.zeros((layer_count, len(WIDTHS)), jnp.float32), pick_sums, layer_id, 0
    )
    log_totals, pick_totals = lax.psum((layer_terms, layer_picks), ("section", "seq"))
    pattern_means = log_totals / pick_totals
    return (
        outputs[None],
        input_grads[None],
        summed[0],
        summed[1],
        summed[2],
        summed[3],
        summed[4],
        summed[5],
        summed[6],
        summed[7],
        pattern_means,
    )


BF16 = jnp.bfloat16
F32 = jnp.float32
PAIRS = HEADS // 2
OWNERS = (0, 2, 3, 4, 5, 6)
TOKENS = 128
PAIR_LANES = 128
QUERY_STEP = 256
VEC_ROWS = 16
KERNEL_VMEM_BYTES = 62 * 1024 * 1024
SCALE = HEAD_DIM ** (-0.5)


def mul(left, right):
    return lax.dot_general(left, right, (((1,), (0,)), ((), ())), preferred_element_type=F32)


def mul_nt(left, right):
    return lax.dot_general(left, right, (((1,), (1,)), ((), ())), preferred_element_type=F32)


def mul_tn(left, right):
    return lax.dot_general(left, right, (((0,), (0,)), ((), ())), preferred_element_type=F32)


def standardize(values):
    center = values - jnp.mean(values, -1, keepdims=True)
    rstd = lax.rsqrt(jnp.mean(center * center, -1, keepdims=True) + EPSILON)
    return (center * rstd, rstd)


def norm_back(unit, rstd, unit_grad):
    first = jnp.mean(unit_grad, -1, keepdims=True)
    second = jnp.mean(unit_grad * unit, -1, keepdims=True)
    return rstd * (unit_grad - first - unit * second)


def remote(source, target, send_sem, recv_sem, axis, peer):
    return pltpu.make_async_remote_copy(
        src_ref=source,
        dst_ref=target,
        send_sem=send_sem,
        recv_sem=recv_sem,
        device_id={axis: peer},
        device_id_type=pl.DeviceIdType.MESH,
    )


def greet(axis, peers):
    barrier = pltpu.get_barrier_semaphore()
    for peer in peers:
        pl.semaphore_signal(
            barrier, inc=1, device_id={axis: peer}, device_id_type=pl.DeviceIdType.MESH
        )
    pl.semaphore_wait(barrier, len(peers))


def seq_peers(me, count):
    return [lax.rem(me + step, count) for step in range(1, count)]


def plane_peers(me):
    return [
        me,
        me + 1 - 2 * lax.rem(me, 2),
        lax.rem(me + 2, 4),
        3 - me,
    ]


def rows_of(block, size=TOKENS):
    return pl.ds(pl.multiple_of(block * size, size), size)


def gelu_parts(values):
    below = 0.5 * (1.0 + lax.erf(values * (0.5**0.5)))
    return (values * below, below)


def share_stats(columns, send, recv, send_sem, recv_sem, peers):
    send[...] = columns.T[0:8, :]
    recv[0] = send[...]
    copies = [
        remote(send, recv.at[k], send_sem.at[k], recv_sem.at[k], "section", peers[k])
        for k in range(1, 4)
    ]
    for copy in copies:
        copy.start()
    return copies


def two_columns(first, second):
    lane = lax.broadcasted_iota(jnp.int32, (first.shape[0], PAIR_LANES), 1)
    return jnp.where(lane == 0, first, jnp.where(lane == 1, second, 0.0))


def slot_rows(k):
    return slice(k * TOKENS, (k + 1) * TOKENS)


def shaped(shape, kind):
    return jax.ShapeDtypeStruct(shape, kind)


class Named:
    def __init__(self, groups, refs):
        names = [name for group in groups for name in group]
        for name, ref in zip(names, refs, strict=True):
            setattr(self, name, ref)


GROUP_TOKENS = 8 * TOKENS
WIDE = 4 * TOKENS
SHARD = D // 8


def square(ref):
    return ref[...].reshape(D, D)


def remote_both(source, target, send_sem, recv_sem, section, seq):
    return pltpu.make_async_remote_copy(
        src_ref=source,
        dst_ref=target,
        send_sem=send_sem,
        recv_sem=recv_sem,
        device_id=(section, seq),
        device_id_type=pl.DeviceIdType.MESH,
    )


def greet_all(barrier, section, me):
    for other in range(4):
        for j in range(8):

            @pl.when((section != other) | (me != j))
            def _():
                pl.semaphore_signal(
                    barrier, inc=1, device_id=(other, j), device_id_type=pl.DeviceIdType.MESH
                )


class Place:
    def __init__(self):
        self.me = lax.axis_index("seq")
        self.section = lax.axis_index("section")
        self.peers = plane_peers(self.section)
        self.core = lax.rem(self.me, 2)
        self.chip = lax.div(self.me, 2)
        self.high = lax.div(self.chip, 2)
        self.low = lax.rem(self.chip, 2)
        self.sibling = self.me + 1 - 2 * self.core
        self.across = 2 * (2 * (1 - self.high) + self.low) + self.core
        self.next = 2 * (2 * self.high + 1 - self.low) + self.core
        self.is_owner = (self.me != 1) & (self.me != 7)
        pair = jnp.where(self.me == 0, 0, self.me - 1)
        self.my_pair = jnp.where(pair > PAIRS - 1, PAIRS - 1, pair)


class LineGather:
    def __init__(self, place, base, far_sems, near_sems, core_sems):
        self.place = place
        self.base = base
        self.far_sems = far_sems
        self.near_sems = near_sems
        self.core_sems = core_sems

    def far(self, high):
        p = self.place
        view = self.base.at[high, p.low, p.core]
        return remote(view, view, self.far_sems[0], self.far_sems[1], "seq", p.across)

    def near(self, low):
        p = self.place
        view = self.base.at[:, low, p.core]
        return remote(view, view, self.near_sems[0], self.near_sems[1], "seq", p.next)

    def cores(self, core):
        p = self.place
        view = self.base.at[:, :, core]
        return remote(view, view, self.core_sems[0], self.core_sems[1], "seq", p.sibling)

    def start(self):
        self.far(self.place.high).start()

    def pass_line(self):
        self.far(1 - self.place.high).wait_recv()
        self.near(self.place.low).start()

    def pass_core(self):
        self.near(1 - self.place.low).wait_recv()
        self.cores(self.place.core).start()

    def ready(self):
        self.cores(1 - self.place.core).wait_recv()

    def drain(self):
        self.far(self.place.high).wait_send()
        self.near(self.place.low).wait_send()
        self.cores(self.place.core).wait_send()


FORE_VMEM = dict(model=0, hgains=0, hbiases=0)
FORE_ANY = dict(embeds_in=0, qkv_w=0, out_w=0, up_w=0, down_w=0)
FORE_OUT = dict(
    sub_out=((4, TOKENS, D), BF16, False),
    streams_out=((3, TOKENS, D), BF16, False),
    att_out=((2, TOKENS, D), BF16, False),
    vecs_out=((2, VEC_ROWS, D), F32, False),
    picks_out=((2, GROUP_TOKENS, PAIR_LANES), BF16, False),
    logs_out=((8, PAIR_LANES), F32, False),
    wa_out=((2, 4, 2, 2, 2, SHARD, D), BF16, False),
    wf_out=((2, 2, 2, 2, 2, SHARD, D), BF16, False),
    qkv_out=((2, 3, GROUP_TOKENS, PAIR_LANES), BF16, False),
    pa_out=((2, GROUP_TOKENS, PAIR_LANES), F32, False),
    pt_out=((2, GROUP_TOKENS, PAIR_LANES), F32, False),
    hid_out=((2, WIDE, D), BF16, False),
    up_out=((2, WIDE, D), F32, False),
    stat_out=((2, WIDE, PAIR_LANES), F32, False),
    left_out=((2, WIDE, D), BF16, False),
)
FORE_SCRATCH = dict(
    embeds=((4, TOKENS, D), BF16),
    streams=((3, TOKENS, D), BF16),
    att=((2, TOKENS, D), BF16),
    picks=((2, GROUP_TOKENS, PAIR_LANES), BF16),
    wa=((2, 4, 2, 2, 2, SHARD, D), BF16),
    wf=((2, 2, 2, 2, 2, SHARD, D), BF16),
    qkv=((2, 3, GROUP_TOKENS, PAIR_LANES), BF16),
    pa=((2, GROUP_TOKENS, PAIR_LANES), F32),
    pt=((2, GROUP_TOKENS, PAIR_LANES), F32),
    hid=((2, WIDE, D), BF16),
    up=((2, WIDE, D), F32),
    stat=((2, WIDE, PAIR_LANES), F32),
    left=((2, WIDE, D), BF16),
    raw_up=((2, SHARD, FF), BF16),
    small_src=((2, 32, PAIR_LANES), BF16),
    small=((8, 2, 32, PAIR_LANES), BF16),
    inner=((TOKENS, D), BF16),
    vecs=((2, VEC_ROWS, D), F32),
    logs=((8, PAIR_LANES), F32),
    sub=((4, TOKENS, D), BF16),
    proj_send=((4, PAIRS, TOKENS, PAIR_LANES), BF16),
    att_send=((GROUP_TOKENS, PAIR_LANES), BF16),
    att_recv=((2, PAIRS, TOKENS, PAIR_LANES), BF16),
    active=((WIDE, D), F32),
    columns=((WIDE, PAIR_LANES), F32),
    stat_rows=((PAIR_LANES, WIDE), F32),
    part_send=((4, TOKENS, D), BF16),
    part_recv=((2, 4, TOKENS, D), BF16),
    stat_send=((8, WIDE), F32),
    stat_recv=((2, 4, 8, WIDE), F32),
)
FORE_SEMS = dict(
    load_sem=(2, 3),
    embeds_sem=(4,),
    store_sem=(2, 15),
    small_s=(8,),
    small_r=(8,),
    az_s=(4,),
    az_r=(4,),
    line_s=(6, 3),
    line_r=(6, 3),
    axy_s=(2, 4),
    axy_r=(2, 4),
    axs_s=(2, 4),
    axs_r=(2, 4),
    left_s=(4,),
    left_r=(4,),
    inner_s=(4,),
    inner_r=(4,),
    wide_s=(2, 4, PAIRS),
    wide_r=(2, 3, 8),
    att_s=(2, 8),
    att_r=(2, PAIRS),
    hid_s=(2, 4),
    hid_r=(2, 4),
    stat_s=(2, 4),
    stat_r=(2, 4),
    part_s=(2, 4),
    part_r=(2, 4),
    sub_s=(4,),
    sub_r=(4,),
)


def make_picks(lengths_ref, section, my_pair, picks_ref):
    tokens = lax.broadcasted_iota(jnp.int32, (GROUP_TOKENS, PAIR_LANES), 0)
    lane = lax.broadcasted_iota(jnp.int32, (GROUP_TOKENS, PAIR_LANES), 1)
    row_id = jnp.zeros_like(tokens)
    first = jnp.zeros_like(tokens)
    end = 0
    for row in range(lengths_ref.shape[1]):
        end = end + lengths_ref[section, row]
        passed = tokens >= end
        row_id = row_id + jnp.where(passed, 1, 0)
        first = jnp.where(passed, end, first)
    pos = (tokens - first).astype(F32)
    number = lax.shift_right_logical(lane, 2)
    row = lane - 4 * number
    ratio = jnp.zeros(lane.shape, F32)
    for i, each in enumerate(RATIOS):
        ratio = jnp.where(number == i, float(each), ratio)
    valid = ratio > 0.5
    ratio = jnp.where(valid, ratio, 1.0)

    def residue(values):
        return values - ratio * jnp.floor((values + 0.5) / ratio)

    residues = residue(pos)
    for head in range(2):
        wanted = residue(jnp.full(lane.shape, 2 * my_pair + head, jnp.int32).astype(F32))
        fits = valid & (row == row_id) & (jnp.abs(residues - wanted) < 0.5)
        picks_ref[head] = jnp.where(fits, 1.0, 0.0).astype(BF16)


def forward_kernel(lengths, *refs):
    b = Named([FORE_VMEM, FORE_ANY, FORE_OUT, FORE_SCRATCH, FORE_SEMS], refs)
    p = Place()
    me, section, peers, core = (p.me, p.section, p.peers, p.core)
    chip, high, low = (p.chip, p.high, p.low)

    barrier = pltpu.get_barrier_semaphore()
    greet_all(barrier, section, me)

    def block_from_qkv(layer):
        return pltpu.make_async_copy(
            b.qkv_w.at[layer, :, pl.ds(pl.multiple_of(lax.rem(section, 3) * D, D), D)],
            b.wa.at[layer, section, high, low, core],
            b.load_sem.at[layer, 0],
        )

    def block_from_out(layer):
        return pltpu.make_async_copy(
            b.out_w.at[layer], b.wa.at[layer, section, high, low, core], b.load_sem.at[layer, 0]
        )

    def load_up(layer):
        return pltpu.make_async_copy(b.up_w.at[layer], b.raw_up.at[layer], b.load_sem.at[layer, 1])

    def load_down(layer):
        return pltpu.make_async_copy(
            b.down_w.at[layer, pl.ds(pl.multiple_of(section * SHARD, SHARD), SHARD)],
            b.wf.at[layer, 1, high, low, core],
            b.load_sem.at[layer, 2],
        )

    def load_embeds(k):
        return pltpu.make_async_copy(
            b.embeds_in.at[peers[k]], b.embeds.at[k], b.embeds_sem.at[k]
        )

    for layer in range(2):

        @pl.when(section != 3)
        def _():
            block_from_qkv(layer).start()

        @pl.when(section == 3)
        def _():
            block_from_out(layer).start()

        if layer == 0:
            for k in range(4):
                load_embeds(k).start()
        load_up(layer).start()
        load_down(layer).start()

    def block_loaded(layer):
        @pl.when(section != 3)
        def _():
            block_from_qkv(layer).wait()

        @pl.when(section == 3)
        def _():
            block_from_out(layer).wait()

    def pick_up(layer):
        load_up(layer).wait()
        load_down(layer).wait()
        raw = b.raw_up[layer]
        for s in range(4):

            @pl.when(section == s)
            def _():
                b.wf[layer, 0, high, low, core] = jnp.concatenate(
                    [
                        raw[:, (4 * j + s) * SHARD : (4 * j + s + 1) * SHARD].astype(F32)
                        for j in range(8)
                    ],
                    1,
                ).astype(BF16)

    def line_gather(number, base):
        pairs = [(b.line_s.at[number, i], b.line_r.at[number, i]) for i in range(3)]
        return LineGather(p, base, *pairs)

    block = [line_gather(layer, b.wa.at[layer, section]) for layer in range(2)]
    feed_lines = [
        [line_gather(2 + 2 * layer + which, b.wf.at[layer, which]) for which in range(2)]
        for layer in range(2)
    ]

    def first_z(step, source):
        view = b.wa.at[0, section, lax.div(source, 2), lax.rem(source, 2), core]
        return remote(
            view,
            view,
            b.az_s.at[step],
            b.az_r.at[step],
            "seq",
            2 * lax.rem(chip + step, 4) + core,
        )

    def block_plane(layer, k, slot):
        view = b.wa.at[layer, slot, :, :, core]
        return remote(view, view, b.axy_s.at[layer, k], b.axy_r.at[layer, k], "section", peers[k])

    def block_across(layer, k, side):
        view = b.wa.at[layer, peers[k], :, :, side]
        return remote(view, view, b.axs_s.at[layer, k], b.axs_r.at[layer, k], "seq", p.sibling)

    for layer in range(2):
        model = b.model[layer].astype(F32)
        hidden_gain = b.hgains[layer : layer + 1, :].astype(F32)
        hidden_bias = b.hbiases[layer].astype(F32)
        lines = [model]
        for each in (hidden_gain, hidden_bias[0:1, :], hidden_bias[1:2, :]):
            for s in range(4):
                lines.append(each[:, s * SHARD : (s + 1) * SHARD])
        lines.append(jnp.zeros((11, SHARD), F32))
        packed = jnp.concatenate(lines, 0)
        packed = jnp.concatenate([packed, jnp.zeros((32, PAIR_LANES - SHARD), F32)], 1)
        b.small_src[layer] = packed.astype(BF16)
    b.small[me] = b.small_src[...]
    make_picks(lengths, section, p.my_pair, b.picks)
    b.logs[...] = jnp.zeros_like(b.logs)
    block_loaded(0)
    pl.semaphore_wait(barrier, 31)

    def small_copy(step):
        return remote(
            b.small_src,
            b.small.at[me],
            b.small_s.at[step],
            b.small_r.at[step],
            "seq",
            lax.rem(me + step, 8),
        )

    for step in range(1, 8):
        small_copy(step).start()
    for step in range(1, 4):
        first_z(step, chip).start()
    pick_up(0)
    for step in range(1, 8):
        source = lax.rem(me + 8 - step, 8)
        remote(
            b.small_src,
            b.small.at[source],
            b.small_s.at[step],
            b.small_r.at[step],
            "seq",
            source,
        ).wait_recv()
    for layer in range(2):
        pieces = []
        for j in range(8):
            small = b.small[j, layer].astype(F32)
            lines = [small[0:9]]
            for third in range(3):
                line = jnp.zeros((1, PAIR_LANES), F32)
                for s in range(4):
                    at = 9 + 4 * third + s
                    line = line + jnp.where(section == s, small[at : at + 1], 0.0)
                lines.append(line)
            lines.append(jnp.zeros((4, PAIR_LANES), F32))
            pieces.append(jnp.concatenate(lines, 0)[:, 0:SHARD])
        b.vecs[layer] = jnp.concatenate(pieces, 1)

    def stores(layer, chosen):
        pairs = (
            (b.wf.at[layer, 1], b.wf_out.at[layer, 1]),
            (b.qkv.at[layer], b.qkv_out.at[layer]),
            (b.pa.at[layer], b.pa_out.at[layer]),
            (b.pt.at[layer], b.pt_out.at[layer]),
            (b.hid.at[layer], b.hid_out.at[layer]),
            (b.up.at[layer], b.up_out.at[layer]),
            (b.stat.at[layer], b.stat_out.at[layer]),
            (b.left.at[layer], b.left_out.at[layer]),
            (b.att.at[layer], b.att_out.at[layer]),
            (b.streams.at[pl.ds(2 * layer, 2 - layer)], b.streams_out.at[pl.ds(2 * layer, 2 - layer)]),
            (b.picks.at[layer], b.picks_out.at[layer]),
            (b.wf.at[layer, 0], b.wf_out.at[layer, 0]),
            (b.vecs.at[layer], b.vecs_out.at[layer]),
        )
        return [
            pltpu.make_async_copy(source, target, b.store_sem.at[layer, i])
            for i, (source, target) in enumerate(pairs)
            if i in chosen
        ]

    def store_block(layer, slot, number):
        return pltpu.make_async_copy(
            b.wa.at[layer, slot], b.wa_out.at[layer, slot], b.store_sem.at[layer, number]
        )

    def store_logs():
        return pltpu.make_async_copy(b.logs, b.logs_out, b.embeds_sem.at[1])

    def wide_copy(layer, k, pair):
        return remote_both(
            b.proj_send.at[k, pair],
            b.qkv.at[layer, lax.rem(section, 3), rows_of(me)],
            b.wide_s.at[layer, k, pair],
            b.wide_r.at[layer, lax.rem(section, 3), me],
            peers[k],
            OWNERS[pair],
        )

    def project(layer, arrive):
        vec = b.vecs.at[layer]

        @pl.when(section != 3)
        def _():
            bias = jnp.where(section == 2, vec[6:7, :], 0.0)
            for k in (3, 1, 2, 0) if layer == 0 else (0, 1, 2, 3):
                if k > 0:
                    arrive(k)
                part = mul(b.left[layer, slot_rows(k), :], square(b.wa.at[layer, section])) + bias
                part = part.astype(BF16)
                for pair in (5, 0, 3, 2, 4, 1):
                    owner = OWNERS[pair]
                    b.proj_send[k, pair] = part[:, pair * PAIR_LANES : (pair + 1) * PAIR_LANES]
                    if k > 0:
                        wide_copy(layer, k, pair).start()
                    else:

                        @pl.when(me != owner)
                        def _():
                            wide_copy(layer, k, pair).start()

                        @pl.when(me == owner)
                        def _():
                            b.qkv[layer, section, rows_of(me), :] = b.proj_send[k, pair]

    def wait_projected(layer):
        @pl.when(p.is_owner)
        def _():
            for third in range(3):
                for source in range(8):

                    @pl.when((section != third) | (me != source))
                    def _():
                        remote_both(
                            b.proj_send.at[0, 0],
                            b.qkv.at[layer, third, pl.ds(source * TOKENS, TOKENS)],
                            b.wide_s.at[layer, 0, 0],
                            b.wide_r.at[layer, third, source],
                            third,
                            source,
                        ).wait_recv()

        @pl.when(section != 3)
        def _():
            for k in range(4):
                for pair, owner in enumerate(OWNERS):
                    if k > 0:
                        wide_copy(layer, k, pair).wait_send()
                    else:

                        @pl.when(me != owner)
                        def _():
                            wide_copy(layer, k, pair).wait_send()

    def back_copy(layer, target):
        return remote(
            b.att_send.at[pl.ds(target * TOKENS, TOKENS)],
            b.att_recv.at[layer, p.my_pair],
            b.att_s.at[layer, target],
            b.att_r.at[layer, p.my_pair],
            "seq",
            target,
        )

    def attend(layer):
        lane = lax.broadcasted_iota(jnp.int32, (QUERY_STEP, PAIR_LANES), 1)
        first_half = lane < HEAD_DIM
        for step in range(GROUP_TOKENS // QUERY_STEP):
            start = step * QUERY_STEP
            keys_end = start + QUERY_STEP
            rows = slice(start, keys_end)
            query = b.qkv[layer, 0, rows, :] * jnp.asarray(SCALE, BF16)
            keys = b.qkv[layer, 1, 0:keys_end, :]
            values = b.qkv[layer, 2, 0:keys_end, :]
            causal = lax.broadcasted_iota(jnp.int32, (QUERY_STEP, keys_end), 1) <= (
                start + lax.broadcasted_iota(jnp.int32, (QUERY_STEP, keys_end), 0)
            )
            sums = []
            totals = []
            logs = jnp.zeros((1, PAIR_LANES), F32)
            picked_sum = jnp.zeros((1, PAIR_LANES), F32)
            for head in range(2):
                mine = first_half if head == 0 else ~first_half
                own_query = jnp.where(mine, query, jnp.zeros_like(query))
                scores = mul_nt(own_query, keys)
                raised = jnp.where(causal, jnp.exp(scores), 0.0)
                pick_query = b.picks[head, rows, :]
                pick_keys = b.picks[head, 0:keys_end, :]
                counts = mul_nt(pick_query, pick_keys)
                weighted = (raised * counts).astype(BF16)
                sums.append(mul(weighted, values))
                pattern = mul(raised.astype(BF16), pick_keys)
                picked = pick_query.astype(F32)
                totals.append(jnp.sum(pattern * picked, -1, keepdims=True))
                chosen = picked > 0.5
                logs = logs + jnp.sum(
                    jnp.where(chosen, jnp.log(jnp.where(chosen, pattern, 1.0)), 0.0),
                    0,
                    keepdims=True,
                )
                picked_sum = picked_sum + jnp.sum(picked, 0, keepdims=True)
            b.logs[layer : layer + 1, :] += logs
            if layer == 0:
                b.logs[2:3, :] += picked_sum
            total = jnp.where(first_half, totals[0], totals[1])
            attended = jnp.where(first_half, sums[0], sums[1]) / total
            b.pa[layer, rows, :] = attended
            b.pt[layer, rows, :] = total
            b.att_send[rows, :] = attended.astype(BF16)
            for target in (2 * step, 2 * step + 1):

                @pl.when(me != target)
                def _():
                    back_copy(layer, target).start()

                @pl.when(me == target)
                def _():
                    b.att_recv[layer, p.my_pair] = b.att_send[
                        target * TOKENS : (target + 1) * TOKENS, :
                    ]

    def attention_rest(layer, inputs_ref, after):
        vec = b.vecs.at[layer]
        wait_projected(layer)
        feed_lines[layer][0].start()
        after()

        @pl.when(p.is_owner)
        def _():
            attend(layer)

        feed_lines[layer][0].pass_line()
        for k in range(1, 4):

            @pl.when(peers[k] == 3)
            def _():
                block_plane(layer, k, peers[k]).wait_recv()
                block_across(layer, k, core).start()

        for pair, owner in enumerate(OWNERS):

            @pl.when(me != owner)
            def _():
                remote(
                    b.att_send.at[pl.ds(0, TOKENS)],
                    b.att_recv.at[layer, pair],
                    b.att_s.at[layer, 0],
                    b.att_r.at[layer, pair],
                    "seq",
                    owner,
                ).wait_recv()

            b.att[layer, :, pair * PAIR_LANES : (pair + 1) * PAIR_LANES] = b.att_recv[layer, pair]
        inner_unit, unused = standardize(b.att[layer].astype(F32))
        inner = (inner_unit * vec[1:2, :] + vec[4:5, :]).astype(BF16)
        if layer == 0:
            b.inner[...] = inner
        for k in range(1, 4):

            @pl.when(peers[k] == 3)
            def _():
                block_across(layer, k, 1 - core).wait_recv()

        branch = mul(inner, square(b.wa.at[layer, 3])) + vec[7:8, :]
        b.streams[2 * layer] = (inputs_ref[...].astype(F32) + branch).astype(BF16)

    def attention_drain(layer):
        @pl.when(p.is_owner)
        def _():
            for target in range(8):

                @pl.when(me != target)
                def _():
                    back_copy(layer, target).wait_send()

    def feed(layer, resting, parting):
        vec = b.vecs.at[layer]
        inputs = b.streams[2 * layer].astype(F32)
        unit, unused = standardize(inputs)
        b.hid[layer, slot_rows(0), :] = (unit * vec[2:3, :] + vec[5:6, :]).astype(BF16)
        hidden_copies = [
            remote(
                b.hid.at[layer, pl.ds(0, TOKENS)],
                b.hid.at[layer, pl.ds(k * TOKENS, TOKENS)],
                b.hid_s.at[layer, k],
                b.hid_r.at[layer, k],
                "section",
                peers[k],
            )
            for k in range(1, 4)
        ]
        for copy in hidden_copies:
            copy.start()
        up_line, down_line = feed_lines[layer]
        down_line.start()
        up_line.pass_core()
        up_line.ready()
        for k in range(4):
            if k > 0:
                hidden_copies[k - 1].wait_recv()
            upward = mul(b.hid[layer, slot_rows(k), :], square(b.wf.at[layer, 0])) + vec[10:11, :]
            b.up[layer, slot_rows(k), :] = upward
            values, unused = gelu_parts(upward)
            b.active[slot_rows(k), :] = values
            mean = jnp.mean(values, -1, keepdims=True)
            center = values - mean
            b.columns[slot_rows(k), :] = two_columns(
                mean, jnp.sum(center * center, -1, keepdims=True)
            )
            if k == 0:
                down_line.pass_line()
        stat_copies = share_stats(
            b.columns[...],
            b.stat_send,
            b.stat_recv.at[layer],
            b.stat_s.at[layer],
            b.stat_r.at[layer],
            peers,
        )
        down_line.pass_core()
        resting()
        for copy in stat_copies:
            copy.wait_recv()
        b.stat_rows[...] = jnp.zeros((PAIR_LANES, WIDE), F32)
        for k in range(4):
            means = [b.stat_recv[layer, other, 0:1, slot_rows(k ^ other)] for other in range(4)]
            squares = [b.stat_recv[layer, other, 1:2, slot_rows(k ^ other)] for other in range(4)]
            mean = (means[0] + means[1] + means[2] + means[3]) * 0.25
            spread = squares[0] + squares[1] + squares[2] + squares[3]
            for each in means:
                spread = spread + D * (each - mean) * (each - mean)
            b.stat_rows[0:1, slot_rows(k)] = mean
            b.stat_rows[1:2, slot_rows(k)] = lax.rsqrt(spread * (1.0 / FF) + EPSILON)
        b.stat[layer] = b.stat_rows[...].T
        down_line.ready()
        if layer == 1:
            parting()
            for copy in hidden_copies + stat_copies:
                copy.wait_send()
            return
        branch = None
        part_copies = []
        for k in (3, 1, 2, 0):
            both = b.stat[layer, slot_rows(k), :]
            inner = (
                (b.active[slot_rows(k), :] - both[:, 0:1]) * both[:, 1:2] * vec[9:10, :]
                + vec[11:12, :]
            ).astype(BF16)
            part = mul(inner, square(b.wf.at[layer, 1]))
            if k == 0:
                branch = part
            else:
                b.part_send[k] = part.astype(BF16)
                part_copies.append(
                    remote(
                        b.part_send.at[k],
                        b.part_recv.at[layer, k],
                        b.part_s.at[layer, k],
                        b.part_r.at[layer, k],
                        "section",
                        peers[k],
                    )
                )
                part_copies[-1].start()
        parting()
        for k, copy in zip((3, 1, 2), part_copies):
            copy.wait_recv()
            branch = branch + b.part_recv[layer, k].astype(F32)
        b.streams[2 * layer + 1] = (inputs + branch + vec[8:9, :]).astype(BF16)
        for copy in hidden_copies + stat_copies + part_copies:
            copy.wait_send()

    def sub_away(number):
        return remote(
            b.streams.at[number],
            b.sub.at[section],
            b.sub_s.at[number],
            b.sub_r.at[section],
            "section",
            number,
        )

    def sub_own(number):
        return pltpu.make_async_copy(
            b.streams.at[number], b.sub.at[section], b.sub_s.at[number]
        )

    def send_sub(number):
        @pl.when(section != number)
        def _():
            sub_away(number).start()

        @pl.when(section == number)
        def _():
            sub_own(number).start()

    def sub_drain():
        for number in range(2):

            @pl.when(section != number)
            def _():
                sub_away(number).wait_send()

            @pl.when(section == number)
            def _():
                sub_own(number).wait()

        @pl.when(section < 2)
        def _():
            for k in range(1, 4):
                remote(
                    b.streams.at[0],
                    b.sub.at[peers[k]],
                    b.sub_s.at[0],
                    b.sub_r.at[peers[k]],
                    "section",
                    peers[k],
                ).wait_recv()

    def sub_store():
        return pltpu.make_async_copy(b.sub, b.sub_out, b.embeds_sem.at[0])

    for k in range(4):
        load_embeds(k).wait()

        @pl.when(section != 3)
        def _():
            unit, unused = standardize(b.embeds[k].astype(F32))
            b.left[0, slot_rows(k), :] = (
                unit * b.vecs[0, 0:1, :] + b.vecs[0, 3:4, :]
            ).astype(BF16)
    pick_up(1)
    for step in range(1, 4):
        first_z(step, lax.rem(chip + 4 - step, 4)).wait_recv()
    block[0].cores(core).start()

    @pl.when(section == 3)
    def _():
        for k in range(1, 4):
            block_plane(0, k, section).start()

    block[0].ready()
    project(0, lambda k: None)

    attention_rest(0, b.embeds.at[0], lambda: None)

    def resting_first():
        block_loaded(1)
        block[1].start()

    def parting_first():
        attention_drain(0)
        block[1].pass_line()

    feed(0, resting_first, parting_first)

    second = b.vecs.at[1]
    unit, unused = standardize(b.streams[1].astype(F32))
    b.left[1, slot_rows(0), :] = (unit * second[0:1, :] + second[3:4, :]).astype(BF16)

    def left_copy(k):
        return remote(
            b.left.at[1, pl.ds(0, TOKENS)],
            b.left.at[1, pl.ds(k * TOKENS, TOKENS)],
            b.left_s.at[k],
            b.left_r.at[k],
            "section",
            peers[k],
        )

    for k in (3, 1, 2):

        @pl.when(peers[k] != 3)
        def _():
            left_copy(k).start()

    for copy in stores(0, (0, 1, 2, 3, 4, 5, 6, 8, 9, 10, 11, 12)):
        copy.start()
    block[1].pass_core()
    for k in range(1, 4):

        @pl.when(peers[k] != 3)
        def _():
            left_copy(k).wait_send()

    @pl.when(section == 3)
    def _():
        for k in range(1, 4):
            block_plane(1, k, section).start()

    block[1].ready()
    project(1, lambda k: left_copy(k).wait_recv())

    def inner_copy(k):
        return remote(
            b.inner,
            b.left.at[0, pl.ds(k * TOKENS, TOKENS)],
            b.inner_s.at[k],
            b.inner_r.at[k],
            "section",
            peers[k],
        )

    def after_second():
        for k in range(1, 4):

            @pl.when(peers[k] == 3)
            def _():
                inner_copy(k).start()

        @pl.when(section == 3)
        def _():
            b.left[0, slot_rows(0), :] = b.inner[...]

        send_sub(0)
        send_sub(1)

    attention_rest(1, b.streams.at[1], after_second)

    def parting_second():
        for copy in stores(1, (0, 6)):
            copy.start()

        attention_drain(1)

    def resting_second():
        for copy in stores(1, (4, 5, 1, 2, 3, 7, 8, 9, 10, 11, 12)):
            copy.start()
        store_logs().start()
        for layer in range(2):
            store_block(layer, section, 13).start()

            @pl.when(section != 3)
            def _():
                store_block(layer, 3, 14).start()

        @pl.when(section == 3)
        def _():
            for k in range(1, 4):
                inner_copy(k).wait_recv()

        for copy in stores(0, (7,)):
            copy.start()
        sub_drain()
        sub_store().start()

    feed(1, resting_second, parting_second)
    for step in range(1, 8):
        small_copy(step).wait_send()
    for step in range(1, 4):
        first_z(step, chip).wait_send()
    block[0].cores(core).wait_send()
    block[1].drain()
    for layer in range(2):
        for line in feed_lines[layer]:
            line.drain()
    for layer in range(2):
        for k in range(1, 4):

            @pl.when(section == 3)
            def _():
                block_plane(layer, k, section).wait_send()

            @pl.when(peers[k] == 3)
            def _():
                block_across(layer, k, core).wait_send()

    for k in range(1, 4):

        @pl.when(peers[k] == 3)
        def _():
            inner_copy(k).wait_send()

    for layer in range(2):
        for copy in stores(layer, range(13)):
            copy.wait()
    sub_store().wait()
    store_logs().wait()
    for layer in range(2):
        store_block(layer, section, 13).wait()

        @pl.when(section != 3)
        def _():
            store_block(layer, 3, 14).wait()


BACK_VMEM = dict()
BACK_ANY = dict(
    vecs_in=0,
    logs_in=0,
    cotangent_in=0,
    embeds_in=0,
    streams_in=0,
    att_in=0,
    picks_in=0,
    wa_in=0,
    wf_in=0,
    qkv_in=0,
    pa_in=0,
    pt_in=0,
    hid_in=0,
    up_in=0,
    stat_in=0,
    left_in=0,
)
BACK_OUT = dict(
    sub_f_out=((4, TOKENS, D), BF16, False),
    sub_g_out=((4, TOKENS, D), BF16, False),
    all_m_out=((6, 4, SHARD, D), BF16, False),
    all_v_out=((2, 4, SHARD, PAIR_LANES), BF16, False),
    log_total=((8, PAIR_LANES), F32, True),
)
BACK_SCRATCH = dict(
    wa=((2, 2, 2, 2, 2, SHARD, D), BF16),
    wf=((2, 2, 2, 2, SHARD, D), BF16),
    qkv=((3, GROUP_TOKENS, PAIR_LANES), BF16),
    pa=((GROUP_TOKENS, PAIR_LANES), F32),
    pt=((GROUP_TOKENS, PAIR_LANES), F32),
    hid=((WIDE, D), BF16),
    up=((WIDE, D), F32),
    stat=((WIDE, PAIR_LANES), F32),
    xs=((5, TOKENS, D), BF16),
    att=((2, TOKENS, D), BF16),
    picks=((2, GROUP_TOKENS, PAIR_LANES), BF16),
    vecs=((2, VEC_ROWS, D), F32),
    logs=((8, PAIR_LANES), F32),
    last_send=((4, TOKENS, D), BF16),
    last_recv=((4, TOKENS, D), BF16),
    last=((TOKENS, D), F32),
    streams=((4, TOKENS, D), BF16),
    grads=((WIDE, D), BF16),
    units=((WIDE, D), F32),
    unit_grads=((WIDE, D), F32),
    inners=((WIDE, D), BF16),
    lows=((WIDE, D), BF16),
    columns=((WIDE, PAIR_LANES), F32),
    stat_rows=((PAIR_LANES, WIDE), F32),
    part_send=((4, TOKENS, D), BF16),
    part_recv=((4, TOKENS, D), BF16),
    stat_send=((8, WIDE), F32),
    stat_recv=((4, 8, WIDE), F32),
    do_send=((PAIRS, TOKENS, PAIR_LANES), BF16),
    do_recv=((GROUP_TOKENS, PAIR_LANES), BF16),
    key_sum=((GROUP_TOKENS, PAIR_LANES), F32),
    value_sum=((GROUP_TOKENS, PAIR_LANES), F32),
    d_send=((3, GROUP_TOKENS, PAIR_LANES), BF16),
    d_recv=((2, 4, PAIRS, TOKENS, PAIR_LANES), BF16),
    left_src=((TOKENS, D), BF16),
    right_src=((TOKENS, D), BF16),
    left=((2, WIDE, D), BF16),
    right=((2, WIDE, D), BF16),
    vec_rows=((2, PAIR_LANES, D), F32),
    hidden_grad=((TOKENS, D), F32),
    prod=((6, 2, 2, 2, SHARD, D), BF16),
    prod_v=((2, 2, 2, 2, SHARD, PAIR_LANES), BF16),
    pair=((6, 2, 2, SHARD, D), BF16),
    pair_v=((2, 2, 2, SHARD, PAIR_LANES), BF16),
    near=((6, 2, SHARD, D), BF16),
    near_v=((2, 2, SHARD, PAIR_LANES), BF16),
    far=((6, SHARD, D), BF16),
    far_v=((2, SHARD, PAIR_LANES), BF16),
    done=((6, SHARD, D), BF16),
    done_v=((2, SHARD, PAIR_LANES), BF16),
    sub_f=((4, TOKENS, D), BF16),
    sub_g=((4, TOKENS, D), BF16),
    all_m=((6, 4, SHARD, D), BF16),
    all_v=((2, 4, SHARD, PAIR_LANES), BF16),
    log_line=((8, 8, PAIR_LANES), F32),
    log_plane=((4, 8, PAIR_LANES), F32),
)
BACK_SEMS = dict(
    load_sem=(24,),
    block_sem=(2, 2),
    left_sem=(2,),
    g_s=(2, 4),
    g_r=(2, 4),
    stat_s=(2, 4),
    stat_r=(2, 4),
    part_s=(2, 4),
    part_r=(2, 4),
    do_s=(2, PAIRS),
    do_r=(2, 8),
    d_s=(2, 3, 8),
    d_r=(2, 4, PAIRS),
    left_s=(2, 4),
    left_r=(2, 4),
    right_s=(2, 4),
    right_r=(2, 4),
    back_s=(2, 4),
    back_r=(2, 4),
    subf_s=(4,),
    subf_r=(4,),
    subg_s=(4,),
    subg_r=(4,),
    own_sem=(2,),
    last_s=(4,),
    last_r=(4,),
    cot_sem=(4,),
    out_sem=(10,),
    pair_s=(8,),
    pair_r=(8,),
    near_s=(8,),
    near_r=(8,),
    far_s=(8,),
    far_r=(8,),
    all_s=(8, 4),
    all_r=(8, 4),
    log_s=(8,),
    log_r=(8,),
    log_plane_s=(4,),
    log_plane_r=(4,),
)


def backward_kernel(*refs):
    b = Named([BACK_VMEM, BACK_ANY, BACK_OUT, BACK_SCRATCH, BACK_SEMS], refs)
    p = Place()
    me, section, peers, core = (p.me, p.section, p.peers, p.core)
    high, low = (p.high, p.low)

    barrier = pltpu.get_barrier_semaphore()
    greet_all(barrier, section, me)

    def loads(first, pairs):
        return [
            pltpu.make_async_copy(source, target, b.load_sem.at[first + number])
            for number, (source, target) in enumerate(pairs)
        ]

    def feed_loads(layer):
        pairs = (
            (b.stat_in.at[layer], b.stat),
            (b.up_in.at[layer], b.up),
            (b.vecs_in.at[layer], b.vecs.at[layer]),
            (b.wf_in.at[layer], b.wf),
            (b.hid_in.at[layer], b.hid),
        )
        return loads(5 * layer, pairs)

    def attention_loads(layer):
        pairs = (
            (b.qkv_in.at[layer], b.qkv),
            (b.pa_in.at[layer], b.pa),
            (b.pt_in.at[layer], b.pt),
        )
        return loads(10 + 3 * layer, pairs)

    def common_loads():
        pairs = (
            (b.logs_in, b.logs),
            (b.embeds_in.at[section], b.xs.at[0]),
            (b.streams_in, b.xs.at[pl.ds(1, 3)]),
            (b.att_in, b.att),
            (b.picks_in, b.picks),
        )
        return loads(16, pairs)

    def block_load(layer, number):
        slot = 3 if number == 1 else section
        return pltpu.make_async_copy(
            b.wa_in.at[layer, slot], b.wa.at[layer, number], b.block_sem.at[layer, number]
        )

    def left_load(layer):
        return pltpu.make_async_copy(b.left_in.at[layer], b.left.at[layer], b.left_sem.at[layer])

    def cotangent_load(k):
        return pltpu.make_async_copy(
            b.cotangent_in.at[peers[k]], b.grads.at[pl.ds(k * TOKENS, TOKENS)], b.cot_sem.at[k]
        )

    for copy in feed_loads(1):
        copy.start()
    for k in range(4):
        cotangent_load(k).start()
    common = common_loads()
    for layer in (1, 0):
        for number in (1, 0):
            block_load(layer, number).start()

    @pl.when(section != 3)
    def _():
        left_load(1).start()

    left_load(0).start()

    for copy in common + attention_loads(1):
        copy.start()
    pl.semaphore_wait(barrier, 31)

    def log_copy(step):
        return remote(
            b.logs,
            b.log_line.at[me],
            b.log_s.at[step],
            b.log_r.at[step],
            "seq",
            lax.rem(me + step, 8),
        )

    def log_plane_copy(k, slot):
        return remote(
            b.log_plane.at[slot],
            b.log_plane.at[slot],
            b.log_plane_s.at[k],
            b.log_plane_r.at[k],
            "section",
            peers[k],
        )

    def start_logs():
        common[0].wait()
        b.log_line[me] = b.logs[...]
        for step in range(1, 8):
            log_copy(step).start()

    def sum_logs():
        for step in range(1, 8):
            source = lax.rem(me + 8 - step, 8)
            remote(
                b.logs,
                b.log_line.at[source],
                b.log_s.at[step],
                b.log_r.at[step],
                "seq",
                source,
            ).wait_recv()
        total = b.log_line[0]
        for j in range(1, 8):
            total = total + b.log_line[j]
        b.log_plane[section] = total
        for k in range(1, 4):
            log_plane_copy(k, section).start()

    def finish_logs():
        for k in range(1, 4):
            log_plane_copy(k, peers[k]).wait_recv()
        total = b.log_plane[0]
        for other in range(1, 4):
            total = total + b.log_plane[other]
        b.log_total[...] = total
        for step in range(1, 8):
            log_copy(step).wait_send()
        for k in range(1, 4):
            log_plane_copy(k, section).wait_send()

    class Matrix:
        def __init__(self, number):
            self.number = number
            self.direct = number > 4
            self.turn = (1, 2) if number % 2 else (2, 1)
            if number < 6:
                self.i = number
                refs = (b.prod, b.pair, b.near, b.far, b.done, b.all_m, b.all_m_out)
            else:
                self.i = number - 6
                refs = (b.prod_v, b.pair_v, b.near_v, b.far_v, b.done_v, b.all_v, b.all_v_out)
            self.prod, self.pair, self.near, self.far, self.done, self.all, self.out = refs

        def store(self, value):
            for j in range(8):
                self.prod[self.i, j % 2, j // 4, j // 2 % 2] = value[
                    j * SHARD : (j + 1) * SHARD, :
                ].astype(BF16)

        def pair_copy(self):
            n = self.number
            return remote(
                self.prod.at[self.i, 1 - core],
                self.pair.at[self.i],
                b.pair_s.at[n],
                b.pair_r.at[n],
                "seq",
                p.sibling,
            )

        def near_copy(self):
            n = self.number
            return remote(
                self.prod.at[self.i, core, :, 1 - low],
                self.near.at[self.i],
                b.near_s.at[n],
                b.near_r.at[n],
                "seq",
                p.next,
            )

        def far_copy(self):
            n = self.number
            return remote(
                self.prod.at[self.i, core, 1 - high, low],
                self.far.at[self.i],
                b.far_s.at[n],
                b.far_r.at[n],
                "seq",
                p.across,
            )

        def all_copy(self, k, slot):
            n = self.number
            return remote(
                self.done.at[self.i],
                self.all.at[self.i, slot],
                b.all_s.at[n, k],
                b.all_r.at[n, k],
                "section",
                peers[k],
            )

        def own_copy(self):
            return pltpu.make_async_copy(
                self.done.at[self.i], self.all.at[self.i, section], b.all_s.at[self.number, 0]
            )

        def out_copy(self):
            return pltpu.make_async_copy(
                self.all.at[self.i], self.out.at[self.i], b.out_sem.at[self.number]
            )

        def step_near(self):
            self.pair_copy().wait_recv()
            i = self.i
            for h in range(2):
                for l in range(2):
                    self.prod[i, core, h, l] = (
                        self.prod[i, core, h, l].astype(F32) + self.pair[i, h, l].astype(F32)
                    ).astype(BF16)
            self.near_copy().start()

        def step_far(self):
            self.near_copy().wait_recv()
            i = self.i
            for h in range(2):
                self.prod[i, core, h, low] = (
                    self.prod[i, core, h, low].astype(F32) + self.near[i, h].astype(F32)
                ).astype(BF16)
            self.far_copy().start()

        def step_plane(self):
            self.far_copy().wait_recv()
            i = self.i
            self.done[i] = (
                self.prod[i, core, high, low].astype(F32) + self.far[i].astype(F32)
            ).astype(BF16)
            for k in (3, 1, 2) if self.direct else (1, 2):
                self.all_copy(k, section).start()
            self.own_copy().start()

        def turn_copy(self):
            n = self.number
            first, second = self.turn
            view = self.all.at[self.i, peers[first]]
            return remote(
                view, view, b.all_s.at[n, 3], b.all_r.at[n, 3], "section", peers[second]
            )

        def step_pass(self):
            first = self.turn[0]
            self.all_copy(first, peers[first]).wait_recv()
            self.turn_copy().start()

        def step_end(self):
            for k in range(1, 4):
                if self.direct or k != self.turn[0]:
                    self.all_copy(k, peers[k]).wait_recv()
                if self.direct or k != 3:
                    self.all_copy(k, section).wait_send()
                else:
                    self.turn_copy().wait_send()
            self.own_copy().wait()
            self.out_copy().start()
            self.pair_copy().wait_send()
            self.near_copy().wait_send()
            self.far_copy().wait_send()

    matrices = [Matrix(number) for number in range(8)]
    up1, down1, att1, up0, down0, att0, vec1, vec0 = matrices

    def sub_copies(number, forward):
        source = b.xs.at[pl.ds(1, 4)] if forward else b.streams
        target = b.sub_f if forward else b.sub_g
        send_sem = b.subf_s if forward else b.subg_s
        recv_sem = b.subf_r if forward else b.subg_r

        def away():
            return remote(
                source.at[number],
                target.at[section],
                send_sem.at[number],
                recv_sem.at[section],
                "section",
                number,
            )

        def own():
            return pltpu.make_async_copy(
                source.at[number], target.at[section], b.own_sem.at[0 if forward else 1]
            )

        return away, own

    def send_sub(number, forward):
        @pl.when(section != number)
        def _():
            sub_copies(number, forward)[0]().start()

        @pl.when(section == number)
        def _():
            sub_copies(number, forward)[1]().start()

    def drain_sub(number, forward):
        @pl.when(section != number)
        def _():
            sub_copies(number, forward)[0]().wait_send()

        @pl.when(section == number)
        def _():
            sub_copies(number, forward)[1]().wait()

    def receive_sub(source, forward):
        target = b.sub_f if forward else b.sub_g

        @pl.when(section != source)
        def _():
            remote(
                b.streams.at[0],
                target.at[source],
                (b.subf_s if forward else b.subg_s).at[0],
                (b.subf_r if forward else b.subg_r).at[source],
                "section",
                source,
            ).wait_recv()

    def last_copy(k):
        return remote(
            b.last_send.at[k],
            b.last_recv.at[k],
            b.last_s.at[k],
            b.last_r.at[k],
            "section",
            peers[k],
        )

    def start_last():
        for k in (3, 1, 2, 0):
            part = mul(b.inners[slot_rows(k), :], square(b.wf.at[1]))
            if k == 0:
                b.last[...] = part
            else:
                b.last_send[k] = part.astype(BF16)
                last_copy(k).start()

    def finish_last():
        total = b.xs[3].astype(F32) + b.last[...] + b.vecs[1, 8:9, :]
        for k in range(1, 4):
            last_copy(k).wait_recv()
            total = total + b.last_recv[k].astype(F32)
        b.xs[4] = total.astype(BF16)
        for k in range(1, 4):
            last_copy(k).wait_send()

    def feed_phase(layer, grad_ref, x_ref, hooks):
        phase = 1 - layer
        vec = b.vecs.at[layer]
        rows = b.vec_rows.at[layer]
        up_matrix = matrices[3 * phase]
        down_matrix = matrices[3 * phase + 1]
        early, middle, parting, late = hooks
        if layer == 0:
            b.grads[slot_rows(0), :] = grad_ref[...]
        grad_copies = [] if layer == 1 else [
            remote(
                b.grads.at[pl.ds(0, TOKENS)],
                b.grads.at[pl.ds(k * TOKENS, TOKENS)],
                b.g_s.at[phase, k],
                b.g_r.at[phase, k],
                "section",
                peers[k],
            )
            for k in range(1, 4)
        ]
        if layer == 0:
            for k in (3, 1, 2):
                grad_copies[k - 1].start()
        rows[...] = jnp.zeros((PAIR_LANES, D), F32)
        early()
        feed_ready = feed_loads(layer)
        for copy in feed_ready[:3]:
            copy.wait()
        for k in range(4):
            both = b.stat[slot_rows(k), :]
            upward = b.up[slot_rows(k), :]
            values, below = gelu_parts(upward)
            b.up[slot_rows(k), :] = below + upward * (
                jnp.exp(-0.5 * upward * upward) * (0.5 / 3.141592653589793) ** 0.5
            )
            unit = (values - both[:, 0:1]) * both[:, 1:2]
            b.units[slot_rows(k), :] = unit
            b.inners[slot_rows(k), :] = (unit * vec[9:10, :] + vec[11:12, :]).astype(BF16)
        feed_ready[3].wait()
        gain_sum = jnp.zeros((1, D), F32)
        bias_sum = jnp.zeros((1, D), F32)
        for k in range(4):
            if layer == 1:
                cotangent_load(k).wait()
            elif k > 0:
                grad_copies[k - 1].wait_recv()
            unit = b.units[slot_rows(k), :]
            inner_grad = mul_nt(b.grads[slot_rows(k), :], square(b.wf.at[1]))
            gain_sum = gain_sum + jnp.sum(inner_grad * unit, 0, keepdims=True)
            bias_sum = bias_sum + jnp.sum(inner_grad, 0, keepdims=True)
            unit_grad = inner_grad * vec[9:10, :]
            b.unit_grads[slot_rows(k), :] = unit_grad
            b.columns[slot_rows(k), :] = two_columns(
                jnp.sum(unit_grad, -1, keepdims=True), jnp.sum(unit_grad * unit, -1, keepdims=True)
            )
        stat_copies = share_stats(
            b.columns[...],
            b.stat_send,
            b.stat_recv,
            b.stat_s.at[phase],
            b.stat_r.at[phase],
            peers,
        )
        rows[9:10, :] = gain_sum
        rows[11:12, :] = bias_sum
        down_matrix.store(mul_tn(b.inners[...], b.grads[...]))
        down_matrix.pair_copy().start()
        middle()
        for copy in stat_copies:
            copy.wait_recv()
        b.stat_rows[...] = jnp.zeros((PAIR_LANES, WIDE), F32)
        for k in range(4):
            for line in range(2):
                parts = [
                    b.stat_recv[other, line : line + 1, slot_rows(k ^ other)]
                    for other in range(4)
                ]
                b.stat_rows[line : line + 1, slot_rows(k)] = (
                    parts[0] + parts[1] + parts[2] + parts[3]
                ) * (1.0 / FF)
        b.columns[...] = b.stat_rows[...].T
        hidden_grad = None
        low_sum = jnp.zeros((1, D), F32)
        part_copies = []
        for k in (3, 1, 2, 0):
            rstd = b.stat[slot_rows(k), :][:, 1:2]
            both = b.columns[slot_rows(k), :]
            lowered = (
                rstd
                * (
                    b.unit_grads[slot_rows(k), :]
                    - both[:, 0:1]
                    - b.units[slot_rows(k), :] * both[:, 1:2]
                )
                * b.up[slot_rows(k), :]
            ).astype(BF16)
            b.lows[slot_rows(k), :] = lowered
            low_sum = low_sum + jnp.sum(lowered.astype(F32), 0, keepdims=True)
            part = mul_nt(lowered, square(b.wf.at[0]))
            if k == 0:
                hidden_grad = part
            else:
                b.part_send[k] = part.astype(BF16)
                part_copies.append(
                    remote(
                        b.part_send.at[k],
                        b.part_recv.at[k],
                        b.part_s.at[phase, k],
                        b.part_r.at[phase, k],
                        "section",
                        peers[k],
                    )
                )
                part_copies[-1].start()
        rows[10:11, :] = low_sum
        feed_ready[4].wait()
        up_matrix.store(mul_tn(b.hid[...], b.lows[...]))
        up_matrix.pair_copy().start()
        unit, rstd = standardize(x_ref[...].astype(F32))
        parting()
        for k, copy in zip((3, 1, 2), part_copies):
            copy.wait_recv()
            hidden_grad = hidden_grad + b.part_recv[k].astype(F32)
        grad = grad_ref[...].astype(F32)
        number = 2 * layer + 1
        b.streams[number] = (
            grad + norm_back(unit, rstd, hidden_grad * vec[2:3, :])
        ).astype(BF16)
        rows[2:3, :] = jnp.sum(hidden_grad * unit, 0, keepdims=True)
        rows[5:6, :] = jnp.sum(hidden_grad, 0, keepdims=True)
        rows[8:9, :] = jnp.sum(grad, 0, keepdims=True)
        for copy in grad_copies + stat_copies + part_copies:
            copy.wait_send()
        late()

    def attention_phase(layer, grad_ref, x_ref, att_ref, hooks):
        phase = 1 - layer
        vec = b.vecs.at[layer]
        rows = b.vec_rows.at[layer]
        before, inside, after, during = hooks
        grad = grad_ref[...]
        inner_unit, inner_rstd = standardize(att_ref[...].astype(F32))
        block_load(layer, 1).wait()
        inner_grad = mul_nt(grad, square(b.wa.at[layer, 1]))
        att_grad = norm_back(inner_unit, inner_rstd, inner_grad * vec[1:2, :]).astype(BF16)
        for pair in range(PAIRS):
            b.do_send[pair] = att_grad[:, pair * PAIR_LANES : (pair + 1) * PAIR_LANES]

        def out_copy(pair):
            return remote(
                b.do_send.at[pair],
                b.do_recv.at[rows_of(me)],
                b.do_s.at[phase, pair],
                b.do_r.at[phase, me],
                "seq",
                OWNERS[pair],
            )

        for pair, owner in enumerate(OWNERS):

            @pl.when(me != owner)
            def _():
                out_copy(pair).start()

            @pl.when(me == owner)
            def _():
                b.do_recv[rows_of(me), :] = b.do_send[pair]

        def left_copy(k):
            return remote(
                b.left_src,
                b.left.at[layer, pl.ds(k * TOKENS, TOKENS)],
                b.left_s.at[phase, k],
                b.left_r.at[phase, k],
                "section",
                peers[k],
            )

        def right_copy(k):
            return remote(
                b.right_src,
                b.right.at[layer, pl.ds(k * TOKENS, TOKENS)],
                b.right_s.at[phase, k],
                b.right_r.at[phase, k],
                "section",
                peers[k],
            )

        unit, rstd = standardize(x_ref[...].astype(F32))
        b.left_src[...] = (inner_unit * vec[1:2, :] + vec[4:5, :]).astype(BF16)
        b.right_src[...] = grad
        for k in range(1, 4):

            @pl.when(peers[k] == 3)
            def _():
                right_copy(k).start()
                if layer == 1:
                    left_copy(k).start()

        if layer == 1:

            @pl.when(section == 3)
            def _():
                b.left[layer, slot_rows(0), :] = b.left_src[...]

        rows[1:2, :] = jnp.sum(inner_grad * inner_unit, 0, keepdims=True)
        rows[4:5, :] = jnp.sum(inner_grad, 0, keepdims=True)
        rows[7:8, :] = jnp.sum(grad.astype(F32), 0, keepdims=True)
        for copy in attention_loads(layer):
            copy.wait()

        def back_copy(third, target):
            return remote_both(
                b.d_send.at[third, pl.ds(target * TOKENS, TOKENS)],
                b.d_recv.at[layer, section, p.my_pair],
                b.d_s.at[phase, third, target],
                b.d_r.at[phase, section, p.my_pair],
                third,
                target,
            )

        @pl.when(p.is_owner)
        def _():
            for source in range(8):

                @pl.when(me != source)
                def _():
                    remote(
                        b.do_send.at[0],
                        b.do_recv.at[pl.ds(source * TOKENS, TOKENS)],
                        b.do_s.at[phase, 0],
                        b.do_r.at[phase, source],
                        "seq",
                        source,
                    ).wait_recv()

        before()

        @pl.when(p.is_owner)
        def _():
            b.key_sum[...] = jnp.zeros((GROUP_TOKENS, PAIR_LANES), F32)
            b.value_sum[...] = jnp.zeros((GROUP_TOKENS, PAIR_LANES), F32)
            lane = lax.broadcasted_iota(jnp.int32, (QUERY_STEP, PAIR_LANES), 1)
            first_half = lane < HEAD_DIM
            for step in reversed(range(GROUP_TOKENS // QUERY_STEP)):
                start = step * QUERY_STEP
                keys_end = start + QUERY_STEP
                block = slice(start, keys_end)
                plain_query = b.qkv[0, block, :]
                query = plain_query * jnp.asarray(SCALE, BF16)
                keys = b.qkv[1, 0:keys_end, :]
                values = b.qkv[2, 0:keys_end, :]
                causal = lax.broadcasted_iota(jnp.int32, (QUERY_STEP, keys_end), 1) <= (
                    start + lax.broadcasted_iota(jnp.int32, (QUERY_STEP, keys_end), 0)
                )
                head_grad = b.do_recv[block, :]
                inverse = 1.0 / b.pt[block, :]
                head_float = head_grad.astype(F32)
                products = head_float * b.pa[block, :]
                scaled = (head_float * inverse).astype(BF16)
                key_lanes = lax.broadcasted_iota(jnp.int32, (keys_end, PAIR_LANES), 1) < HEAD_DIM
                query_parts = []
                key_parts = []
                value_parts = []
                for head in range(2):
                    mine = first_half if head == 0 else ~first_half
                    own_query = jnp.where(mine, query, jnp.zeros_like(query))
                    own_grad = jnp.where(mine, head_grad, jnp.zeros_like(head_grad))
                    delta = jnp.sum(jnp.where(mine, products, 0.0), -1, keepdims=True)
                    own_inverse = jnp.max(jnp.where(mine, inverse, 0.0), -1, keepdims=True)
                    counts = mul_nt(b.picks[head, block, :], b.picks[head, 0:keys_end, :])
                    scores = mul_nt(own_query, keys)
                    weighted = jnp.where(causal, jnp.exp(scores) * counts, 0.0)
                    prob_grad = mul_nt(own_grad, values)
                    score_grad = (weighted * own_inverse * (prob_grad - delta)).astype(BF16)
                    query_parts.append(mul(score_grad, keys))
                    key_parts.append(mul_tn(score_grad, plain_query))
                    value_parts.append(mul_tn(weighted.astype(BF16), scaled))
                b.key_sum[0:keys_end, :] += jnp.where(key_lanes, key_parts[0], key_parts[1])
                b.value_sum[0:keys_end, :] += jnp.where(key_lanes, value_parts[0], value_parts[1])
                query_grad = jnp.where(first_half, query_parts[0], query_parts[1]) * SCALE
                b.d_send[0, block, :] = query_grad.astype(BF16)
                b.d_send[1, block, :] = (b.key_sum[block, :] * SCALE).astype(BF16)
                b.d_send[2, block, :] = b.value_sum[block, :].astype(BF16)
                for third in range(3):
                    for target in (2 * step, 2 * step + 1):
                        away = (section != third) | (me != target)

                        @pl.when(away)
                        def _():
                            back_copy(third, target).start()

                        @pl.when(~away)
                        def _():
                            b.d_recv[layer, section, p.my_pair] = b.d_send[
                                third, target * TOKENS : (target + 1) * TOKENS, :
                            ]

        inside()
        after()
        block_load(layer, 0).wait()

        def part_copy(k):
            return remote(
                b.part_send.at[k],
                b.part_recv.at[k],
                b.back_s.at[phase, k],
                b.back_r.at[phase, k],
                "section",
                peers[k],
            )

        @pl.when(section != 3)
        def _():
            if layer == 1:
                left_load(layer).wait()
            for k in (3, 2, 1, 0):
                for pair, owner in enumerate(OWNERS):
                    away = me != owner if k == 0 else True

                    @pl.when(away)
                    def _():
                        remote_both(
                            b.d_send.at[0, pl.ds(0, TOKENS)],
                            b.d_recv.at[layer, peers[k], pair],
                            b.d_s.at[phase, 0, 0],
                            b.d_r.at[phase, peers[k], pair],
                            peers[k],
                            owner,
                        ).wait_recv()

                    b.right[layer, slot_rows(k), pair * PAIR_LANES : (pair + 1) * PAIR_LANES] = (
                        b.d_recv[layer, peers[k], pair]
                    )
                part = mul_nt(b.right[layer, slot_rows(k), :], square(b.wa.at[layer, 0]))
                if k == 0:
                    b.hidden_grad[...] = part
                else:
                    b.part_send[k] = part.astype(BF16)
                    part_copy(k).start()

        @pl.when(section == 3)
        def _():
            b.right[layer, slot_rows(0), :] = b.right_src[...]
            b.hidden_grad[...] = jnp.zeros((TOKENS, D), F32)
            for k in range(1, 4):
                right_copy(k).wait_recv()
                if layer == 1:
                    left_copy(k).wait_recv()

        if layer == 0:
            left_load(layer).wait()
        matrix = matrices[3 * phase + 2]
        matrix.store(mul_tn(b.left[layer], b.right[layer]))
        matrix.pair_copy().start()
        value_sum = jnp.sum(b.right[layer].astype(F32), 0, keepdims=True)
        rows[6:7, :] = jnp.where(section == 2, value_sum, 0.0)
        during()
        for k in (3, 1, 2):

            @pl.when(peers[k] != 3)
            def _():
                part_copy(k).wait_recv()
                b.hidden_grad[...] += b.part_recv[k].astype(F32)

        hidden_grad = b.hidden_grad[...]
        b.streams[2 * layer] = (
            grad.astype(F32) + norm_back(unit, rstd, hidden_grad * vec[0:1, :])
        ).astype(BF16)
        rows[0:1, :] = jnp.sum(hidden_grad * unit, 0, keepdims=True)
        rows[3:4, :] = jnp.sum(hidden_grad, 0, keepdims=True)

        def drain():
            @pl.when(section != 3)
            def _():
                for k in range(1, 4):
                    part_copy(k).wait_send()

            for k in range(1, 4):

                @pl.when(peers[k] == 3)
                def _():
                    right_copy(k).wait_send()
                    if layer == 1:
                        left_copy(k).wait_send()

            for pair, owner in enumerate(OWNERS):

                @pl.when(me != owner)
                def _():
                    out_copy(pair).wait_send()

            @pl.when(p.is_owner)
            def _():
                for third in range(3):
                    for target in range(8):

                        @pl.when((section != third) | (me != target))
                        def _():
                            back_copy(third, target).wait_send()

        return drain

    def nothing():
        pass

    def middle_first():
        start_logs()
        for copy in common[1:]:
            copy.wait()

    def late_first():
        start_last()
        for copy in feed_loads(0):
            copy.start()

    feed_phase(
        1,
        b.grads.at[pl.ds(0, TOKENS)],
        b.xs.at[3],
        (nothing, middle_first, down1.step_near, late_first),
    )

    def before_first():
        down1.step_far()
        send_sub(2, True)

    def during_first():
        up1.step_far()
        down1.step_pass()
        finish_last()
        sum_logs()

    drain_first = attention_phase(
        1,
        b.streams.at[3],
        b.xs.at[2],
        b.att.at[1],
        (before_first, down1.step_plane, up1.step_near, during_first),
    )

    def early_second():
        vec1.store(b.vec_rows[1].T)
        vec1.pair_copy().start()
        drain_first()
        for copy in attention_loads(0):
            copy.start()
        att1.step_near()

    def middle_second():
        att1.step_far()
        vec1.step_near()
        up1.step_plane()

    def parting_second():
        down0.step_near()
        vec1.step_far()
        up1.step_pass()

    feed_phase(
        0,
        b.streams.at[2],
        b.xs.at[1],
        (early_second, middle_second, parting_second, nothing),
    )

    def before_second():
        down0.step_far()
        send_sub(3, True)

    def inside_second():
        att1.step_plane()
        vec1.step_plane()
        down0.step_plane()
        for number in (2, 1):
            send_sub(number, False)

        @pl.when(section == 3)
        def _():
            for k in range(4):
                b.sub_g[peers[k]] = b.right[1, slot_rows(k), :]

        finish_logs()

    def during_second():
        att0.step_near()
        att1.step_pass()
        down0.step_pass()
        up0.step_far()

    drain_second = attention_phase(
        0,
        b.streams.at[1],
        b.xs.at[0],
        b.att.at[0],
        (before_second, inside_second, up0.step_near, during_second),
    )
    vec0.store(b.vec_rows[0].T)
    vec0.pair_copy().start()
    att0.step_far()
    send_sub(0, False)
    vec0.step_near()
    up0.step_plane()
    vec0.step_far()
    up0.step_pass()
    att0.step_plane()
    vec0.step_plane()
    drain_second()
    for matrix in (up1, down1, att1, vec1, down0, up0, vec0, att0):
        matrix.step_end()
    for number in range(3):
        drain_sub(number, False)

    @pl.when(section != 3)
    def _():
        for source in range(4):
            receive_sub(source, False)

    sub_stores = [
        pltpu.make_async_copy(b.sub_f, b.sub_f_out, b.out_sem.at[8]),
        pltpu.make_async_copy(b.sub_g, b.sub_g_out, b.out_sem.at[9]),
    ]
    sub_stores[1].start()
    drain_sub(2, True)
    drain_sub(3, True)

    @pl.when(section >= 2)
    def _():
        for source in range(4):
            receive_sub(source, True)

    sub_stores[0].start()
    for copy in sub_stores + [matrix.out_copy() for matrix in matrices]:
        copy.wait()


FINISH_IN = dict(all_m=0, all_v=0, sub_a=0, sub_f=0, sub_g=0, log_total=0)
FINISH_OUT = dict(
    outputs=((1, 4, TOKENS, D), BF16, False),
    grads=((1, 4, TOKENS, D), BF16, False),
    qkv=((2, SHARD, 3 * D), F32, False),
    out=((2, SHARD, D), F32, False),
    up=((2, SHARD, FF), F32, False),
    down=((2, 4 * SHARD, D), F32, False),
    gains=((2, 3, SHARD), F32, True),
    biases=((2, 6, SHARD), F32, True),
    hgains=((2, 4 * SHARD), F32, True),
    hbiases=((2, 2, 4 * SHARD), F32, True),
    means=((2, 5), F32, True),
)
FINISH_SCRATCH = dict(
    matrix=((6, 4, SHARD, D), BF16),
    vectors=((2, 4, SHARD, PAIR_LANES), BF16),
    wide=((2, SHARD, 4 * D), F32),
    tall=((2, 4 * SHARD, D), F32),
    spread=((2, SHARD, FF), F32),
    first=((4, TOKENS, D), BF16),
    second=((4, TOKENS, D), BF16),
)
FINISH_SEMS = dict(load_sem=(9,), store_sem=(10,))


def finish_kernel(*refs):
    b = Named([FINISH_IN, FINISH_OUT, FINISH_SCRATCH, FINISH_SEMS], refs)
    section = lax.axis_index("section")
    loads = [
        pltpu.make_async_copy(b.all_m.at[i], b.matrix.at[i], b.load_sem.at[i]) for i in range(6)
    ] + [pltpu.make_async_copy(b.all_v, b.vectors, b.load_sem.at[6])]
    for copy in loads:
        copy.start()

    def outputs_from(source):
        return pltpu.make_async_copy(source, b.first, b.load_sem.at[7])

    @pl.when(section >= 2)
    def _():
        outputs_from(b.sub_f).start()

    @pl.when(section < 2)
    def _():
        outputs_from(b.sub_a).start()

    grads_load = pltpu.make_async_copy(b.sub_g, b.second, b.load_sem.at[8])
    grads_load.start()
    stores = []

    def store(source, target, number):
        copy = pltpu.make_async_copy(source, target, b.store_sem.at[number])
        copy.start()
        stores.append(copy)

    for layer in (1, 0):
        up_i = 3 * (1 - layer)
        loads[up_i].wait()
        for j in range(8):
            b.spread[layer, :, j * 4 * SHARD : (j + 1) * 4 * SHARD] = jnp.concatenate(
                [
                    b.matrix[up_i, source, :, j * SHARD : (j + 1) * SHARD].astype(F32)
                    for source in range(4)
                ],
                1,
            )
        store(b.spread.at[layer], b.up.at[layer], 4 * layer)
        loads[up_i + 1].wait()
        for source in range(4):
            b.tall[layer, source * SHARD : (source + 1) * SHARD, :] = b.matrix[
                up_i + 1, source
            ].astype(F32)
        store(b.tall.at[layer], b.down.at[layer], 4 * layer + 1)
        loads[up_i + 2].wait()
        for source in range(4):
            b.wide[layer, :, source * D : (source + 1) * D] = b.matrix[up_i + 2, source].astype(
                F32
            )
        store(b.wide.at[layer, :, pl.ds(0, 3 * D)], b.qkv.at[layer], 4 * layer + 2)
        store(b.wide.at[layer, :, pl.ds(3 * D, D)], b.out.at[layer], 4 * layer + 3)
    outputs_from(b.sub_a).wait()
    store(b.first, b.outputs.at[0], 8)
    grads_load.wait()
    store(b.second, b.grads.at[0], 9)
    loads[6].wait()
    for layer in range(2):
        lines = []
        for source in range(4):
            tail = b.vectors[1 - layer, source].astype(F32)
            tail = jnp.concatenate([tail, jnp.zeros((PAIR_LANES - SHARD, PAIR_LANES), F32)], 0)
            lines.append(tail.T)
        model = lines[0] + lines[1] + lines[2] + lines[3]
        b.gains[layer] = model[0:3, 0:SHARD]
        b.biases[layer] = model[3:9, 0:SHARD]
        hidden = jnp.concatenate([each[9:12, 0:SHARD] for each in lines], 1)
        b.hgains[layer : layer + 1, :] = hidden[0:1, :]
        b.hbiases[layer] = hidden[1:3, :]
    lane = lax.broadcasted_iota(jnp.int32, (8, PAIR_LANES), 1)
    number = lax.shift_right_logical(lane, 2)
    sums = jnp.zeros((8, PAIR_LANES), F32)
    for i in range(5):
        part = jnp.sum(jnp.where(number == i, b.log_total[...], 0.0), -1, keepdims=True)
        sums = sums + jnp.where(lane == i, part, 0.0)
    means = sums[0:2, :] / jnp.where(lane[0:2, :] < 5, sums[2:3, :], 1.0)
    b.means[...] = means[:, 0:5]
    for copy in stores:
        copy.wait()


def run_remote(kernel, number, lengths, near, far, outs, scratch, sems):
    vmem = pl.BlockSpec(memory_space=pltpu.VMEM)
    anywhere = pl.BlockSpec(memory_space=pl.ANY)
    smem = pl.BlockSpec(memory_space=pltpu.SMEM)
    return pl.pallas_call(
        kernel,
        out_shape=[shaped(out[0], out[1]) for out in outs.values()],
        in_specs=[smem] * len(lengths) + [vmem] * len(near) + [anywhere] * len(far),
        out_specs=[vmem if out[2] else anywhere for out in outs.values()],
        scratch_shapes=[pltpu.VMEM(item[0], item[1]) for item in scratch.values()]
        + [pltpu.SemaphoreType.DMA(item) for item in sems.values()],
        compiler_params=pltpu.CompilerParams(
            collective_id=number, has_side_effects=True, vmem_limit_bytes=KERNEL_VMEM_BYTES
        ),
        cost_estimate=pl.CostEstimate(
            flops=10**10, bytes_accessed=100_000_000, transcendentals=0
        ),
    )(*lengths, *near, *far)


def run_finish(log_total, *far):
    vmem = pl.BlockSpec(memory_space=pltpu.VMEM)
    anywhere = pl.BlockSpec(memory_space=pl.ANY)
    return pl.pallas_call(
        finish_kernel,
        out_shape=[shaped(out[0], out[1]) for out in FINISH_OUT.values()],
        in_specs=[anywhere] * len(far) + [vmem],
        out_specs=[vmem if out[2] else anywhere for out in FINISH_OUT.values()],
        scratch_shapes=[pltpu.VMEM(item[0], item[1]) for item in FINISH_SCRATCH.values()]
        + [pltpu.SemaphoreType.DMA(item) for item in FINISH_SEMS.values()],
        compiler_params=pltpu.CompilerParams(vmem_limit_bytes=KERNEL_VMEM_BYTES),
    )(*far, log_total)


def quick_body(
    embeds,
    row_lengths,
    qkv_weight,
    out_weight,
    up_weight,
    down_weight,
    model_gains,
    model_biases,
    hidden_gains,
    hidden_biases,
    cotangent,
):
    fore = Named(
        [FORE_OUT],
        run_remote(
            forward_kernel,
            10,
            (row_lengths,),
            (jnp.concatenate([model_gains, model_biases], 1), hidden_gains, hidden_biases),
            (embeds, qkv_weight, out_weight, up_weight, down_weight),
            FORE_OUT,
            FORE_SCRATCH,
            FORE_SEMS,
        ),
    )
    back = Named(
        [BACK_OUT],
        run_remote(
            backward_kernel,
            20,
            (),
            (),
            (
                fore.vecs_out,
                fore.logs_out,
                cotangent,
                embeds,
                fore.streams_out,
                fore.att_out,
                fore.picks_out,
                fore.wa_out,
                fore.wf_out,
                fore.qkv_out,
                fore.pa_out,
                fore.pt_out,
                fore.hid_out,
                fore.up_out,
                fore.stat_out,
                fore.left_out,
            ),
            BACK_OUT,
            BACK_SCRATCH,
            BACK_SEMS,
        ),
    )
    return tuple(
        run_finish(
            back.log_total,
            back.all_m_out,
            back.all_v_out,
            fore.sub_out,
            back.sub_f_out,
            back.sub_g_out,
        )
    )


def fits_quick(mesh):
    return mesh.shape["section"] == 4 and mesh.shape["seq"] == 8


def solution(mesh):
    return jax.shard_map(
        quick_body if fits_quick(mesh) else body,
        mesh=mesh,
        in_specs=(
            P(None, "seq", None),
            P(),
            P(None, "seq", None),
            P(None, "seq", None),
            P(None, "seq", None),
            P(None, "seq", None),
            P(None, None, "seq"),
            P(None, None, "seq"),
            P(None, "seq"),
            P(None, None, "seq"),
            P(None, "seq", None),
        ),
        out_specs=(
            P("section", None, "seq", None),
            P("section", None, "seq", None),
            P(None, "seq", None),
            P(None, "seq", None),
            P(None, "seq", None),
            P(None, "seq", None),
            P(None, None, "seq"),
            P(None, None, "seq"),
            P(None, "seq"),
            P(None, None, "seq"),
            P(),
        ),
        check_vma=False,
    )
```

```python
import jax
import jax.numpy as jnp
from jax import lax
from jax.experimental import pallas as pl
from jax.experimental.pallas import tpu as pltpu
from jax.sharding import PartitionSpec as P

D = 768
HEADS = 12
HEAD_DIM = 64
FF = 3072


WIDTHS = (2048, 4096, 8192, 16384, 32768)
RATIOS = (1, 2, 4, 6, 12)
EPSILON = 1e-05


def passed_along(value, axis, steps):
    count = lax.axis_size(axis)
    initial, last = (max(0, -steps), min(count, count - steps))
    return lax.ppermute(value, axis, [(source, source + steps) for source in range(initial, last)])


def norm_rows(inputs, gain_row, offset):
    center = inputs - jnp.mean(inputs, -1, keepdims=True)
    spread = jnp.mean(center * center, -1, keepdims=True)
    return center * lax.rsqrt(spread + EPSILON) * gain_row + offset


def place_rows(lengths, token_index):
    row_ends = jnp.cumsum(lengths)
    passed = token_index[:, None] >= row_ends[None, :]
    row_ids = jnp.sum(passed.astype(jnp.int32), 1)
    offsets = token_index - jnp.sum(jnp.where(passed, lengths[None, :], 0), 1)
    return (row_ids, offsets)


def query_chosen(query_pos):
    head_ids = jnp.arange(HEADS, dtype=jnp.int32)
    chosen = []
    for seg_width, seg_ratio in zip(WIDTHS, RATIOS):
        query_pick = query_pos % seg_width % seg_ratio
        chosen.append(query_pick[None, :] == (head_ids % seg_ratio)[:, None])
    return chosen


def pattern_allow(query_rows, query_pos, key_rows, key_pos):
    widths = jnp.array(WIDTHS, jnp.int32)[:, None]
    ratios = jnp.array(RATIOS, jnp.int32)[:, None]
    residue = jnp.arange(HEADS, dtype=jnp.int32)[None, :] % ratios
    query_mod = query_pos[None, :] % widths % ratios
    key_mod = key_pos[None, :] % widths % ratios
    query_ok = query_mod[:, None, :] == residue[:, :, None]
    key_ok = key_mod[:, None, :] == residue[:, :, None]
    common = (query_rows[:, None] == key_rows[None, :]) & (key_pos[None, :] <= query_pos[:, None])
    inside = common[None] & (
        (query_pos[None, :] // widths)[:, :, None] == (key_pos[None, :] // widths)[:, None, :]
    )
    return inside[:, None] & query_ok[:, :, :, None] & key_ok[:, :, None, :]


def block_rows(total_rows):
    step_rows = min(total_rows, 512)
    return step_rows


def split_heads(matrix):
    return matrix.reshape(matrix.shape[0], HEADS, HEAD_DIM)


def pair_terms(query_block, keys_block, query_rows, query_pos, key_rows, key_pos):
    scores = jnp.einsum(
        "qhe,khe->hqk", query_block, keys_block, preferred_element_type=jnp.float32
    ) * HEAD_DIM ** (-0.5)
    allowed = pattern_allow(query_rows, query_pos, key_rows, key_pos)
    counts = jnp.sum(allowed.astype(jnp.float32), 0)
    raised = jnp.exp(scores)
    return (raised, counts * raised, allowed)


def project_tokens(inputs, qkv_matrix, norm_gains, norm_biases):
    hidden = norm_rows(inputs, norm_gains[0], norm_biases[0]).astype(jnp.bfloat16)
    bias_row = jnp.concatenate(
        [jnp.zeros_like(norm_biases[3]), jnp.zeros_like(norm_biases[3]), norm_biases[3]]
    )
    projected = (jnp.dot(hidden, qkv_matrix, preferred_element_type=jnp.float32) + bias_row).astype(
        jnp.bfloat16
    )
    return (hidden, projected)


def attention_forward(section_in, projected, whole_keys, lengths, params, seq_index):
    out_matrix, norm_gains, norm_biases = (params[1], params[4], params[5])
    tok_rows = section_in.shape[0]
    inputs = section_in.astype(jnp.float32)
    queries = split_heads(projected[:, :D])
    query_rows, query_pos = place_rows(
        lengths, seq_index * tok_rows + jnp.arange(tok_rows, dtype=jnp.int32)
    )
    group_rows = whole_keys.shape[0]
    step_rows = block_rows(group_rows)

    def one_block(running, block_start):
        totals, pattern_sums, accumulated = running
        kv_block = lax.dynamic_slice_in_dim(whole_keys, block_start, step_rows, 0)
        key_rows, key_pos = place_rows(
            lengths, block_start + jnp.arange(step_rows, dtype=jnp.int32)
        )
        raised, weighted, allowed = pair_terms(
            queries, split_heads(kv_block[:, :D]), query_rows, query_pos, key_rows, key_pos
        )
        totals = totals + jnp.sum(weighted, -1)
        pattern_sums = pattern_sums + jnp.sum(jnp.where(allowed, raised[None], 0.0), -1)
        accumulated = accumulated + jnp.einsum(
            "hqk,khe->hqe",
            weighted.astype(jnp.bfloat16),
            split_heads(kv_block[:, D:]),
            preferred_element_type=jnp.float32,
        )
        return ((totals, pattern_sums, accumulated), None)

    start_sums = (
        jnp.zeros((HEADS, tok_rows), jnp.float32),
        jnp.zeros((len(WIDTHS), HEADS, tok_rows), jnp.float32),
        jnp.zeros((HEADS, tok_rows, HEAD_DIM), jnp.float32),
    )
    folded, unused = lax.scan(
        one_block, start_sums, jnp.arange(0, group_rows, step_rows, dtype=jnp.int32)
    )
    totals, pattern_sums, accumulated = folded
    attended = jnp.transpose(accumulated / totals[:, :, None], (1, 0, 2)).reshape(tok_rows, D)
    inner_norm = norm_rows(attended, norm_gains[1], norm_biases[1]).astype(jnp.bfloat16)
    branch = jnp.dot(inner_norm, out_matrix, preferred_element_type=jnp.float32) + norm_biases[4]
    section_out = (inputs + branch).astype(jnp.bfloat16)
    chosen = query_chosen(query_pos)
    log_terms = jnp.stack(
        [
            jnp.sum(
                jnp.where(pick_row, jnp.log(jnp.where(pick_row, pattern_sums[number], 1.0)), 0.0)
            )
            for number, pick_row in enumerate(chosen)
        ]
    )
    pick_counts = jnp.stack([jnp.sum(pick_row.astype(jnp.float32)) for pick_row in chosen])
    return (section_out, attended, totals, log_terms, pick_counts)


def feed_forward(section_in, params):
    up_matrix, down_matrix, norm_gains, norm_biases, hidden_gain, hidden_bias = (
        params[2],
        params[3],
        params[4],
        params[5],
        params[6],
        params[7],
    )
    tok_rows = section_in.shape[0]
    inputs = section_in.astype(jnp.float32)
    hidden = norm_rows(inputs, norm_gains[2], norm_biases[2]).astype(jnp.bfloat16)
    upward = jnp.dot(hidden, up_matrix, preferred_element_type=jnp.float32) + hidden_bias[0]
    inner_norm = norm_rows(
        jax.nn.gelu(upward, approximate=False), hidden_gain, hidden_bias[1]
    ).astype(jnp.bfloat16)
    branch = jnp.dot(inner_norm, down_matrix, preferred_element_type=jnp.float32) + norm_biases[5]
    section_out = (inputs + branch).astype(jnp.bfloat16)
    empty_terms = jnp.zeros((len(WIDTHS),), jnp.float32)
    return (
        section_out,
        jnp.zeros((tok_rows, D), jnp.float32),
        jnp.zeros((HEADS, tok_rows), jnp.float32),
        empty_terms,
        empty_terms,
    )


def attention_middle(
    section_in, grad_out, attended, totals, lengths, all_keys, projected, params, seq_index
):
    out_matrix, norm_gains, norm_biases = (params[1], params[4], params[5])
    scale_factor = HEAD_DIM ** (-0.5)
    tok_rows = section_in.shape[0]
    queries = split_heads(projected[:, :D])
    query_rows, query_pos = place_rows(
        lengths, seq_index * tok_rows + jnp.arange(tok_rows, dtype=jnp.int32)
    )
    inner_norm = norm_rows(attended, norm_gains[1], norm_biases[1]).astype(jnp.bfloat16)
    out_step = jnp.einsum("td,tf->df", inner_norm, grad_out, preferred_element_type=jnp.float32)
    inner_grad = jnp.einsum("tf,df->td", grad_out, out_matrix, preferred_element_type=jnp.float32)
    unused, inner_back = jax.vjp(norm_rows, attended, norm_gains[1], norm_biases[1])
    attended_grad, inner_gain_grad, inner_bias_grad = inner_back(inner_grad)
    low_attended = attended_grad.astype(jnp.bfloat16)
    head_grad = split_heads(low_attended)
    row_dots = jnp.einsum("qhe,qhe->hq", head_grad.astype(jnp.float32), split_heads(attended))
    scaled_grad = head_grad.astype(jnp.float32) / jnp.transpose(totals)[:, :, None]
    group_rows = all_keys.shape[0]
    step_rows = block_rows(group_rows)

    def grad_block(query_grad, block_start):
        kv_block = lax.dynamic_slice_in_dim(all_keys, block_start, step_rows, 0)
        keys_block = split_heads(kv_block[:, :D])
        values_block = split_heads(kv_block[:, D:])
        key_rows, key_pos = place_rows(
            lengths, block_start + jnp.arange(step_rows, dtype=jnp.int32)
        )
        raised, weighted, allowed = pair_terms(
            queries, keys_block, query_rows, query_pos, key_rows, key_pos
        )
        prob_grad = jnp.einsum(
            "qhe,khe->hqk", head_grad, values_block, preferred_element_type=jnp.float32
        )
        score_grad = (weighted / totals[:, :, None] * (prob_grad - row_dots[:, :, None])).astype(
            jnp.bfloat16
        )
        query_grad = (
            query_grad
            + jnp.einsum("hqk,khe->qhe", score_grad, keys_block, preferred_element_type=jnp.float32)
            * scale_factor
        )
        key_grad = (
            jnp.einsum("hqk,qhe->khe", score_grad, queries, preferred_element_type=jnp.float32)
            * scale_factor
        )
        value_grad = jnp.einsum(
            "hqk,qhe->khe",
            weighted.astype(jnp.bfloat16),
            scaled_grad,
            preferred_element_type=jnp.float32,
        )
        block_grad = jnp.concatenate(
            [key_grad.reshape(step_rows, D), value_grad.reshape(step_rows, D)], 1
        )
        return (query_grad, block_grad)

    query_grad, block_grads = lax.scan(
        grad_block,
        jnp.zeros((tok_rows, HEADS, HEAD_DIM), jnp.float32),
        jnp.arange(0, group_rows, step_rows, dtype=jnp.int32),
    )
    block_grads = block_grads.reshape(group_rows, 2 * D)
    return (
        query_grad.reshape(tok_rows, D),
        low_attended,
        row_dots,
        block_grads,
        out_step,
        inner_gain_grad,
        inner_bias_grad,
    )


def attention_finish(section_in, grad_out, middle, extra, params, grad_sums):
    qkv_matrix, norm_gains, norm_biases = (params[0], params[4], params[5])
    inputs = section_in.astype(jnp.float32)
    grad_float = grad_out.astype(jnp.float32)
    hidden = norm_rows(inputs, norm_gains[0], norm_biases[0]).astype(jnp.bfloat16)
    query_grad, low_attended, row_dots, block_grads, out_step, inner_gain_grad, inner_bias_grad = (
        middle
    )
    own_grads = extra[0]
    proj_grad = jnp.concatenate([query_grad, own_grads], 1).astype(jnp.bfloat16)
    qkv_step = jnp.einsum("td,tf->df", hidden, proj_grad, preferred_element_type=jnp.float32)
    value_bias_sums = jnp.sum(proj_grad[:, 2 * D :].astype(jnp.float32), 0)
    hidden_grad = jnp.einsum("tf,df->td", proj_grad, qkv_matrix, preferred_element_type=jnp.float32)
    unused_first, first_back = jax.vjp(norm_rows, inputs, norm_gains[0], norm_biases[0])
    input_grad, first_gain_grad, first_bias_grad = first_back(hidden_grad)
    qkv_sum, out_sum, up_sum, down_sum, gain_sum, bias_sum, hgain_sum, hbias_sum = grad_sums
    gain_sum = gain_sum.at[0].add(first_gain_grad).at[1].add(inner_gain_grad)
    bias_sum = (
        bias_sum.at[0]
        .add(first_bias_grad)
        .at[1]
        .add(inner_bias_grad)
        .at[3]
        .add(value_bias_sums)
        .at[4]
        .add(jnp.sum(grad_float, 0))
    )
    return (
        grad_float + input_grad,
        (
            qkv_sum + qkv_step,
            out_sum + out_step,
            up_sum,
            down_sum,
            gain_sum,
            bias_sum,
            hgain_sum,
            hbias_sum,
        ),
    )


def feed_backward(section_in, grad_out, params, grad_sums):
    up_matrix, down_matrix, norm_gains, norm_biases, hidden_gain, hidden_bias = (
        params[2],
        params[3],
        params[4],
        params[5],
        params[6],
        params[7],
    )
    inputs = section_in.astype(jnp.float32)
    grad_float = grad_out.astype(jnp.float32)
    hidden = norm_rows(inputs, norm_gains[2], norm_biases[2]).astype(jnp.bfloat16)
    upward = jnp.dot(hidden, up_matrix, preferred_element_type=jnp.float32) + hidden_bias[0]

    def inner_rows(upward_in, gain_row, bias_row):
        return norm_rows(jax.nn.gelu(upward_in, approximate=False), gain_row, bias_row)

    inner_value, inner_back = jax.vjp(inner_rows, upward, hidden_gain, hidden_bias[1])
    inner_norm = inner_value.astype(jnp.bfloat16)
    down_step = jnp.einsum("tf,td->fd", inner_norm, grad_out, preferred_element_type=jnp.float32)
    inner_grad = jnp.einsum("td,fd->tf", grad_out, down_matrix, preferred_element_type=jnp.float32)
    upward_grad, hgain_step, hbias_step = inner_back(inner_grad)
    low_upward = upward_grad.astype(jnp.bfloat16)
    up_step = jnp.einsum("td,tf->df", hidden, low_upward, preferred_element_type=jnp.float32)
    hidden_grad = jnp.einsum("tf,df->td", low_upward, up_matrix, preferred_element_type=jnp.float32)
    unused, first_back = jax.vjp(norm_rows, inputs, norm_gains[2], norm_biases[2])
    input_grad, first_gain_grad, first_bias_grad = first_back(hidden_grad)
    qkv_sum, out_sum, up_sum, down_sum, gain_sum, bias_sum, hgain_sum, hbias_sum = grad_sums
    gain_sum = gain_sum.at[2].add(first_gain_grad)
    bias_sum = bias_sum.at[2].add(first_bias_grad).at[5].add(jnp.sum(grad_float, 0))
    hbias_sum = (
        hbias_sum.at[0].add(jnp.sum(low_upward.astype(jnp.float32), 0)).at[1].add(hbias_step)
    )
    return (
        grad_float + input_grad,
        (
            qkv_sum,
            out_sum,
            up_sum + up_step,
            down_sum + down_step,
            gain_sum,
            bias_sum,
            hgain_sum + hgain_step,
            hbias_sum,
        ),
    )


def keep_slot(store, fresh, slot_id, in_range):
    previous = lax.dynamic_index_in_dim(store, slot_id, 0, False)
    return lax.dynamic_update_index_in_dim(store, jnp.where(in_range, fresh, previous), slot_id, 0)


def body(
    embeds,
    row_lengths,
    qkv_weight,
    out_weight,
    up_weight,
    down_weight,
    model_gains,
    model_biases,
    hidden_gains,
    hidden_biases,
    cotangent,
):
    section_id = lax.axis_index("section")
    seq_index = lax.axis_index("seq")
    section_count = lax.axis_size("section")
    micro_count = embeds.shape[0]
    tok_rows = embeds.shape[1]
    group_rows = tok_rows * lax.axis_size("seq")
    layer_id = section_id // 2
    attends = section_id % 2 == 0
    bias_count = model_biases.shape[1]

    def pick_layer(stacked):
        return lax.dynamic_index_in_dim(stacked, layer_id, 0, False)

    gathered = (
        lax.all_gather(pick_layer(qkv_weight), "seq", axis=0, tiled=True),
        lax.all_gather(pick_layer(out_weight), "seq", axis=0, tiled=True),
        lax.all_gather(pick_layer(up_weight), "seq", axis=0, tiled=True),
        lax.all_gather(pick_layer(down_weight), "seq", axis=0, tiled=True),
        lax.all_gather(pick_layer(model_gains), "seq", axis=1, tiled=True),
        lax.all_gather(pick_layer(model_biases), "seq", axis=1, tiled=True),
        lax.all_gather(pick_layer(hidden_gains), "seq", axis=0, tiled=True),
        lax.all_gather(pick_layer(hidden_biases), "seq", axis=1, tiled=True),
    )
    params = tuple(gathered[:4]) + tuple((vector.astype(jnp.float32) for vector in gathered[4:]))
    whole_shape = (0,)

    def make_projected(section_in):
        return project_tokens(section_in.astype(jnp.float32), params[0], params[4], params[5])[1]

    def skip_projected(section_in):
        return jnp.zeros((tok_rows, 3 * D), jnp.bfloat16)

    def run_attention(section_in, projected, whole_keys, lengths):
        return attention_forward(section_in, projected, whole_keys, lengths, params, seq_index)

    def run_feed(section_in, projected, whole_keys, lengths):
        return feed_forward(section_in, params)

    def forward_tick(running, tick_id):
        (
            incoming,
            kept_inputs,
            kept_attended,
            kept_totals,
            kept_whole,
            outputs,
            log_sums,
            pick_sums,
        ) = running
        micro_id = tick_id - section_id
        in_range = (micro_id >= 0) & (micro_id < micro_count)
        slot_id = jnp.clip(micro_id, 0, micro_count - 1)
        lengths = lax.dynamic_index_in_dim(row_lengths, slot_id, 0, False)
        section_in = jnp.where(
            section_id == 0, lax.dynamic_index_in_dim(embeds, slot_id, 0, False), incoming
        )
        projected = lax.cond(attends, make_projected, skip_projected, section_in)
        whole_keys = lax.all_gather(projected[:, D:], "seq", axis=0, tiled=True)
        section_out, attended, totals, log_terms, pick_counts = lax.cond(
            attends, run_attention, run_feed, section_in, projected, whole_keys, lengths
        )
        kept_inputs = keep_slot(kept_inputs, section_in, slot_id, in_range)
        kept_attended = keep_slot(kept_attended, attended, slot_id, in_range)
        kept_totals = keep_slot(kept_totals, totals, slot_id, in_range)
        outputs = keep_slot(outputs, section_out, slot_id, in_range)
        log_sums = log_sums + jnp.where(in_range, log_terms, 0.0)
        pick_sums = pick_sums + jnp.where(in_range, pick_counts, 0.0)
        incoming = passed_along(section_out, "section", 1)
        return (
            (
                incoming,
                kept_inputs,
                kept_attended,
                kept_totals,
                kept_whole,
                outputs,
                log_sums,
                pick_sums,
            ),
            None,
        )

    forward_start = (
        jnp.zeros((tok_rows, D), jnp.bfloat16),
        jnp.zeros((micro_count, tok_rows, D), jnp.bfloat16),
        jnp.zeros((micro_count, tok_rows, D), jnp.float32),
        jnp.zeros((micro_count, HEADS, tok_rows), jnp.float32),
        jnp.zeros((micro_count,) + whole_shape, jnp.bfloat16),
        jnp.zeros((micro_count, tok_rows, D), jnp.bfloat16),
        jnp.zeros((len(WIDTHS),), jnp.float32),
        jnp.zeros((len(WIDTHS),), jnp.float32),
    )
    ticks = jnp.arange(micro_count + section_count - 1, dtype=jnp.int32)
    forward_end, unused = lax.scan(forward_tick, forward_start, ticks)
    unused_in, kept_inputs, kept_attended, kept_totals, kept_whole, outputs, log_sums, pick_sums = (
        forward_end
    )
    block_shape = (group_rows, 2 * D)

    def middle_attention(section_in, grad_out, attended, totals, lengths, all_keys, projected):
        return attention_middle(
            section_in, grad_out, attended, totals, lengths, all_keys, projected, params, seq_index
        )

    def middle_feed(section_in, grad_out, attended, totals, lengths, all_keys, projected):
        return (
            jnp.zeros((tok_rows, D), jnp.float32),
            jnp.zeros((tok_rows, D), jnp.bfloat16),
            jnp.zeros((HEADS, tok_rows), jnp.float32),
            jnp.zeros(block_shape, jnp.float32),
            jnp.zeros((D, D), jnp.float32),
            jnp.zeros((D,), jnp.float32),
            jnp.zeros((D,), jnp.float32),
        )

    def finish_attention(section_in, grad_out, projected, middle, extra, lengths, grad_sums):
        return attention_finish(section_in, grad_out, middle, extra, params, grad_sums)

    def finish_feed(section_in, grad_out, projected, middle, extra, lengths, grad_sums):
        return feed_backward(section_in, grad_out, params, grad_sums)

    def backward_tick(running, tick_id):
        incoming, grad_sums, input_grads = running
        micro_id = micro_count - 1 - tick_id + (section_count - 1 - section_id)
        in_range = (micro_id >= 0) & (micro_id < micro_count)
        slot_id = jnp.clip(micro_id, 0, micro_count - 1)
        from_next = jnp.where(
            section_id == section_count - 1,
            lax.dynamic_index_in_dim(cotangent, slot_id, 0, False),
            incoming,
        )
        grad_out = jnp.where(in_range, from_next, jnp.zeros_like(from_next))
        section_in = lax.dynamic_index_in_dim(kept_inputs, slot_id, 0, False)
        attended = lax.dynamic_index_in_dim(kept_attended, slot_id, 0, False)
        totals = lax.dynamic_index_in_dim(kept_totals, slot_id, 0, False)
        lengths = lax.dynamic_index_in_dim(row_lengths, slot_id, 0, False)
        projected = lax.cond(attends, make_projected, skip_projected, section_in)
        all_keys = lax.all_gather(projected[:, D:], "seq", axis=0, tiled=True)
        middle = lax.cond(
            attends,
            middle_attention,
            middle_feed,
            section_in,
            grad_out,
            attended,
            totals,
            lengths,
            all_keys,
            projected,
        )
        extra = (lax.psum_scatter(middle[3], "seq", scatter_dimension=0, tiled=True),)
        section_grad, grad_sums = lax.cond(
            attends,
            finish_attention,
            finish_feed,
            section_in,
            grad_out,
            projected,
            middle,
            extra,
            lengths,
            grad_sums,
        )
        low_grad = section_grad.astype(jnp.bfloat16)
        input_grads = keep_slot(input_grads, low_grad, slot_id, in_range)
        incoming = passed_along(low_grad, "section", -1)
        return ((incoming, grad_sums, input_grads), None)

    grad_start = (
        jnp.zeros((D, 3 * D), jnp.float32),
        jnp.zeros((D, D), jnp.float32),
        jnp.zeros((D, FF), jnp.float32),
        jnp.zeros((FF, D), jnp.float32),
        jnp.zeros((3, D), jnp.float32),
        jnp.zeros((bias_count, D), jnp.float32),
        jnp.zeros((FF,), jnp.float32),
        jnp.zeros((2, FF), jnp.float32),
    )
    backward_start = (
        jnp.zeros((tok_rows, D), jnp.bfloat16),
        grad_start,
        jnp.zeros((micro_count, tok_rows, D), jnp.bfloat16),
    )
    backward_end, unused_back = lax.scan(backward_tick, backward_start, ticks)
    unused_grad, grad_sums, input_grads = backward_end
    shards = (
        lax.psum_scatter(grad_sums[0], "seq", scatter_dimension=0, tiled=True),
        lax.psum_scatter(grad_sums[1], "seq", scatter_dimension=0, tiled=True),
        lax.psum_scatter(grad_sums[2], "seq", scatter_dimension=0, tiled=True),
        lax.psum_scatter(grad_sums[3], "seq", scatter_dimension=0, tiled=True),
        lax.psum_scatter(grad_sums[4], "seq", scatter_dimension=1, tiled=True),
        lax.psum_scatter(grad_sums[5], "seq", scatter_dimension=1, tiled=True),
        lax.psum_scatter(grad_sums[6], "seq", scatter_dimension=0, tiled=True),
        lax.psum_scatter(grad_sums[7], "seq", scatter_dimension=1, tiled=True),
    )
    sources = (
        qkv_weight,
        out_weight,
        up_weight,
        down_weight,
        model_gains,
        model_biases,
        hidden_gains,
        hidden_biases,
    )
    placed = tuple(
        (
            lax.dynamic_update_index_in_dim(
                jnp.zeros(source.shape, jnp.float32), shard, layer_id, 0
            )
            for shard, source in zip(shards, sources)
        )
    )
    summed = (
        lax.psum(placed[0].astype(jnp.bfloat16), "section").astype(jnp.float32),
        lax.psum(placed[1].astype(jnp.bfloat16), "section").astype(jnp.float32),
        lax.psum(placed[2].astype(jnp.bfloat16), "section").astype(jnp.float32),
        lax.psum(placed[3].astype(jnp.bfloat16), "section").astype(jnp.float32),
        lax.psum(placed[4].astype(jnp.bfloat16), "section").astype(jnp.float32),
        lax.psum(placed[5].astype(jnp.bfloat16), "section").astype(jnp.float32),
        lax.psum(placed[6].astype(jnp.bfloat16), "section").astype(jnp.float32),
        lax.psum(placed[7].astype(jnp.bfloat16), "section").astype(jnp.float32),
    )
    layer_count = qkv_weight.shape[0]
    layer_terms = lax.dynamic_update_index_in_dim(
        jnp.zeros((layer_count, len(WIDTHS)), jnp.float32), log_sums, layer_id, 0
    )
    layer_picks = lax.dynamic_update_index_in_dim(
        jnp.zeros((layer_count, len(WIDTHS)), jnp.float32), pick_sums, layer_id, 0
    )
    log_totals, pick_totals = lax.psum((layer_terms, layer_picks), ("section", "seq"))
    pattern_means = log_totals / pick_totals
    return (
        outputs[None],
        input_grads[None],
        summed[0],
        summed[1],
        summed[2],
        summed[3],
        summed[4],
        summed[5],
        summed[6],
        summed[7],
        pattern_means,
    )


BF16 = jnp.bfloat16
F32 = jnp.float32
PAIRS = HEADS // 2
OWNERS = (0, 2, 3, 4, 5, 6)
TOKENS = 128
PAIR_LANES = 128
QUERY_STEP = 256
VEC_ROWS = 16
KERNEL_VMEM_BYTES = 64 * 1024 * 1024 - 65536
SCALE = HEAD_DIM ** (-0.5)


def mul(left, right):
    return lax.dot_general(left, right, (((1,), (0,)), ((), ())), preferred_element_type=F32)


def mul_nt(left, right):
    return lax.dot_general(left, right, (((1,), (1,)), ((), ())), preferred_element_type=F32)


def mul_tn(left, right):
    return lax.dot_general(left, right, (((0,), (0,)), ((), ())), preferred_element_type=F32)


def standardize(values):
    center = values - jnp.mean(values, -1, keepdims=True)
    rstd = lax.rsqrt(jnp.mean(center * center, -1, keepdims=True) + EPSILON)
    return (center * rstd, rstd)


def norm_back(unit, rstd, unit_grad):
    first = jnp.mean(unit_grad, -1, keepdims=True)
    second = jnp.mean(unit_grad * unit, -1, keepdims=True)
    return rstd * (unit_grad - first - unit * second)


def remote(source, target, send_sem, recv_sem, axis, peer):
    return pltpu.make_async_remote_copy(
        src_ref=source,
        dst_ref=target,
        send_sem=send_sem,
        recv_sem=recv_sem,
        device_id={axis: peer},
        device_id_type=pl.DeviceIdType.MESH,
    )


def greet(axis, peers):
    barrier = pltpu.get_barrier_semaphore()
    for peer in peers:
        pl.semaphore_signal(
            barrier, inc=1, device_id={axis: peer}, device_id_type=pl.DeviceIdType.MESH
        )
    pl.semaphore_wait(barrier, len(peers))


def seq_peers(me, count):
    return [lax.rem(me + step, count) for step in range(1, count)]


def plane_peers(me):
    return [
        me,
        me + 1 - 2 * lax.rem(me, 2),
        lax.rem(me + 2, 4),
        3 - me,
    ]


def rows_of(block, size=TOKENS):
    return pl.ds(pl.multiple_of(block * size, size), size)


def gelu_parts(values):
    below = 0.5 * (1.0 + lax.erf(values * (0.5**0.5)))
    return (values * below, below)


def share_stats(columns, send, recv, send_sem, recv_sem, peers):
    send[...] = columns.T[0:8, :]
    recv[0] = send[...]
    copies = [
        remote(send, recv.at[k], send_sem.at[k], recv_sem.at[k], "section", peers[k])
        for k in range(1, 4)
    ]
    for copy in copies:
        copy.start()
    return copies


def two_columns(first, second):
    lane = lax.broadcasted_iota(jnp.int32, (first.shape[0], PAIR_LANES), 1)
    return jnp.where(lane == 0, first, jnp.where(lane == 1, second, 0.0))


def slot_rows(k):
    return slice(k * TOKENS, (k + 1) * TOKENS)


def shaped(shape, kind):
    return jax.ShapeDtypeStruct(shape, kind)


class Named:
    def __init__(self, groups, refs):
        names = [name for group in groups for name in group]
        for name, ref in zip(names, refs, strict=True):
            setattr(self, name, ref)


GROUP_TOKENS = 8 * TOKENS
WIDE = 4 * TOKENS
SHARD = D // 8


def square(ref):
    return ref[...].reshape(D, D)


def remote_both(source, target, send_sem, recv_sem, section, seq):
    return pltpu.make_async_remote_copy(
        src_ref=source,
        dst_ref=target,
        send_sem=send_sem,
        recv_sem=recv_sem,
        device_id=(section, seq),
        device_id_type=pl.DeviceIdType.MESH,
    )


def greet_all(barrier, section, me):
    for other in range(4):
        for j in range(8):

            @pl.when((section != other) | (me != j))
            def _():
                pl.semaphore_signal(
                    barrier, inc=1, device_id=(other, j), device_id_type=pl.DeviceIdType.MESH
                )


class Place:
    def __init__(self):
        self.me = lax.axis_index("seq")
        self.section = lax.axis_index("section")
        self.peers = plane_peers(self.section)
        self.core = lax.rem(self.me, 2)
        self.chip = lax.div(self.me, 2)
        self.high = lax.div(self.chip, 2)
        self.low = lax.rem(self.chip, 2)
        self.sibling = self.me + 1 - 2 * self.core
        self.across = 2 * (2 * (1 - self.high) + self.low) + self.core
        self.next = 2 * (2 * self.high + 1 - self.low) + self.core
        self.is_owner = (self.me != 1) & (self.me != 7)
        pair = jnp.where(self.me == 0, 0, self.me - 1)
        self.my_pair = jnp.where(pair > PAIRS - 1, PAIRS - 1, pair)


class LineGather:
    def __init__(self, place, base, far_sems, near_sems, core_sems):
        self.place = place
        self.base = base
        self.far_sems = far_sems
        self.near_sems = near_sems
        self.core_sems = core_sems

    def far(self, high):
        p = self.place
        view = self.base.at[high, p.low, p.core]
        return remote(view, view, self.far_sems[0], self.far_sems[1], "seq", p.across)

    def near(self, low):
        p = self.place
        view = self.base.at[:, low, p.core]
        return remote(view, view, self.near_sems[0], self.near_sems[1], "seq", p.next)

    def cores(self, core):
        p = self.place
        view = self.base.at[:, :, core]
        return remote(view, view, self.core_sems[0], self.core_sems[1], "seq", p.sibling)

    def start(self):
        self.far(self.place.high).start()

    def pass_line(self):
        self.far(1 - self.place.high).wait_recv()
        self.near(self.place.low).start()

    def pass_core(self):
        self.near(1 - self.place.low).wait_recv()
        self.cores(self.place.core).start()

    def ready(self):
        self.cores(1 - self.place.core).wait_recv()

    def drain(self):
        self.far(self.place.high).wait_send()
        self.near(self.place.low).wait_send()
        self.cores(self.place.core).wait_send()


BOTH_VMEM = dict(model=0, hgains=0, hbiases=0)
BOTH_ANY = dict(embeds_in=0, qkv_w=0, out_w=0, up_w=0, down_w=0, cotangent_in=0)
BOTH_OUT = dict(
    sub_f_out=((4, TOKENS, D), BF16, False),
    sub_g_out=((4, TOKENS, D), BF16, False),
    all_m_out=((6, 4, SHARD, D), BF16, False),
    all_v_out=((2, 4, SHARD, PAIR_LANES), BF16, False),
    log_total=((8, PAIR_LANES), F32, True),
)
BOTH_SCRATCH = dict(
    embeds=((4, TOKENS, D), BF16),
    att=((2, TOKENS, D), BF16),
    picks=((2, GROUP_TOKENS, PAIR_LANES), BF16),
    wa=((2, 2, 2, 2, 2, SHARD, D), BF16),
    wf=((2, 2, 2, 2, 2, SHARD, D), BF16),
    qkv=((2, 3, GROUP_TOKENS, PAIR_LANES), BF16),
    pa=((2, GROUP_TOKENS, PAIR_LANES), F32),
    pt=((2, GROUP_TOKENS, PAIR_LANES), F32),
    hid=((2, WIDE, D), BF16),
    up=((2, WIDE, D), F32),
    stat=((2, WIDE, PAIR_LANES), F32),
    left=((2, WIDE, D), BF16),
    raw_up=((2, SHARD, FF), BF16),
    small_src=((2, 32, PAIR_LANES), BF16),
    small=((8, 2, 32, PAIR_LANES), BF16),
    inner=((TOKENS, D), BF16),
    vecs=((2, VEC_ROWS, D), F32),
    logs=((8, PAIR_LANES), F32),
    proj_send=((4, PAIRS, TOKENS, PAIR_LANES), BF16),
    att_send=((GROUP_TOKENS, PAIR_LANES), BF16),
    att_recv=((2, PAIRS, TOKENS, PAIR_LANES), BF16),
    columns=((WIDE, PAIR_LANES), F32),
    stat_rows=((PAIR_LANES, WIDE), F32),
    stat_send=((8, WIDE), F32),
    first_recv=((4, TOKENS, D), BF16),
    fstat_recv=((2, 4, 8, WIDE), F32),
    xs=((4, TOKENS, D), BF16),
    last_send=((4, TOKENS, D), BF16),
    last_recv=((4, TOKENS, D), BF16),
    last=((TOKENS, D), F32),
    streams=((4, TOKENS, D), BF16),
    grads=((WIDE, D), BF16),
    units=((WIDE, D), F32),
    unit_grads=((WIDE, D), F32),
    inners=((WIDE, D), BF16),
    lows=((WIDE, D), BF16),
    part_send=((4, TOKENS, D), BF16),
    part_recv=((4, TOKENS, D), BF16),
    stat_recv=((4, 8, WIDE), F32),
    do_send=((PAIRS, TOKENS, PAIR_LANES), BF16),
    do_recv=((GROUP_TOKENS, PAIR_LANES), BF16),
    key_sum=((GROUP_TOKENS, PAIR_LANES), F32),
    value_sum=((GROUP_TOKENS, PAIR_LANES), F32),
    d_send=((3, GROUP_TOKENS, PAIR_LANES), BF16),
    d_recv=((2, 4, PAIRS, TOKENS, PAIR_LANES), BF16),
    left_src=((TOKENS, D), BF16),
    right_src=((TOKENS, D), BF16),
    right=((2, WIDE, D), BF16),
    vec_rows=((2, PAIR_LANES, D), F32),
    hidden_grad=((TOKENS, D), F32),
    prod=((3, 2, 2, 2, SHARD, D), BF16),
    prod_v=((2, 2, 2, 2, SHARD, PAIR_LANES), BF16),
    pair=((6, 2, 2, SHARD, D), BF16),
    pair_v=((2, 2, 2, SHARD, PAIR_LANES), BF16),
    near=((6, 2, SHARD, D), BF16),
    near_v=((2, 2, SHARD, PAIR_LANES), BF16),
    far=((6, SHARD, D), BF16),
    far_v=((2, SHARD, PAIR_LANES), BF16),
    done=((6, SHARD, D), BF16),
    done_v=((2, SHARD, PAIR_LANES), BF16),
    log_line=((8, 8, PAIR_LANES), F32),
    log_plane=((4, 8, PAIR_LANES), F32),
)
BOTH_SEMS = dict(
    load_sem=(2, 3),
    embeds_sem=(4,),
    small_s=(8,),
    small_r=(8,),
    az_s=(4,),
    az_r=(4,),
    line_s=(6, 3),
    line_r=(6, 3),
    axy_s=(2, 4),
    axy_r=(2, 4),
    axs_s=(2, 4),
    axs_r=(2, 4),
    inner_s=(4,),
    inner_r=(4,),
    wide_s=(2, 4, PAIRS),
    wide_r=(2, 3, 8),
    att_s=(2, 8),
    att_r=(2, PAIRS),
    fhid_s=(2, 4),
    fhid_r=(2, 4),
    fstat_s=(2, 4),
    fstat_r=(2, 4),
    fleft_s=(4,),
    fleft_r=(4,),
    first_s=(4,),
    first_r=(4,),
    g_s=(2, 4),
    g_r=(2, 4),
    stat_s=(2, 4),
    stat_r=(2, 4),
    part_s=(2, 4),
    part_r=(2, 4),
    do_s=(2, PAIRS),
    do_r=(2, 8),
    d_s=(2, 3, 8),
    d_r=(2, 4, PAIRS),
    left_s=(2, 4),
    left_r=(2, 4),
    right_s=(2, 4),
    right_r=(2, 4),
    back_s=(2, 4),
    back_r=(2, 4),
    subf_s=(4,),
    subf_r=(4,),
    subg_s=(4,),
    subg_r=(4,),
    own_sem=(2,),
    last_s=(4,),
    last_r=(4,),
    cot_sem=(4,),
    pair_s=(8,),
    pair_r=(8,),
    near_s=(8,),
    near_r=(8,),
    far_s=(8,),
    far_r=(8,),
    all_s=(8, 4),
    all_r=(8, 4),
    log_s=(8,),
    log_r=(8,),
    log_plane_s=(4,),
    log_plane_r=(4,),
    third_sem=(4,),
)


def make_picks(lengths_ref, section, my_pair, picks_ref):
    tokens = lax.broadcasted_iota(jnp.int32, (GROUP_TOKENS, PAIR_LANES), 0)
    lane = lax.broadcasted_iota(jnp.int32, (GROUP_TOKENS, PAIR_LANES), 1)
    row_id = jnp.zeros_like(tokens)
    first = jnp.zeros_like(tokens)
    end = 0
    for row in range(lengths_ref.shape[1]):
        end = end + lengths_ref[section, row]
        passed = tokens >= end
        row_id = row_id + jnp.where(passed, 1, 0)
        first = jnp.where(passed, end, first)
    pos = (tokens - first).astype(F32)
    number = lax.shift_right_logical(lane, 2)
    row = lane - 4 * number
    ratio = jnp.zeros(lane.shape, F32)
    for i, each in enumerate(RATIOS):
        ratio = jnp.where(number == i, float(each), ratio)
    valid = ratio > 0.5
    ratio = jnp.where(valid, ratio, 1.0)

    def residue(values):
        return values - ratio * jnp.floor((values + 0.5) / ratio)

    residues = residue(pos)
    for head in range(2):
        wanted = residue(jnp.full(lane.shape, 2 * my_pair + head, jnp.int32).astype(F32))
        fits = valid & (row == row_id) & (jnp.abs(residues - wanted) < 0.5)
        picks_ref[head] = jnp.where(fits, 1.0, 0.0).astype(BF16)


def both_kernel(lengths, *refs):
    b = Named([BOTH_VMEM, BOTH_ANY, BOTH_OUT, BOTH_SCRATCH, BOTH_SEMS], refs)
    p = Place()
    me, section, peers, core = (p.me, p.section, p.peers, p.core)
    chip, high, low = (p.chip, p.high, p.low)
    out_slot = jnp.where(section == 3, 0, 1)

    barrier = pltpu.get_barrier_semaphore()
    greet_all(barrier, section, me)

    def block_from_qkv(layer):
        return pltpu.make_async_copy(
            b.qkv_w.at[layer, :, pl.ds(pl.multiple_of(lax.rem(section, 3) * D, D), D)],
            b.wa.at[layer, 0, high, low, core],
            b.load_sem.at[layer, 0],
        )

    def block_from_out(layer):
        return pltpu.make_async_copy(
            b.out_w.at[layer], b.wa.at[layer, 0, high, low, core], b.load_sem.at[layer, 0]
        )

    def load_up(layer):
        return pltpu.make_async_copy(b.up_w.at[layer], b.raw_up.at[layer], b.load_sem.at[layer, 1])

    def load_down(layer):
        return pltpu.make_async_copy(
            b.down_w.at[layer, pl.ds(pl.multiple_of(section * SHARD, SHARD), SHARD)],
            b.wf.at[layer, 1, high, low, core],
            b.load_sem.at[layer, 2],
        )

    def load_embeds(k):
        return pltpu.make_async_copy(
            b.embeds_in.at[peers[k]], b.embeds.at[k], b.embeds_sem.at[k]
        )

    for layer in range(2):

        @pl.when(section != 3)
        def _():
            block_from_qkv(layer).start()

        @pl.when(section == 3)
        def _():
            block_from_out(layer).start()

        if layer == 0:
            for k in range(4):
                load_embeds(k).start()
        load_up(layer).start()
        load_down(layer).start()

    def block_loaded(layer):
        @pl.when(section != 3)
        def _():
            block_from_qkv(layer).wait()

        @pl.when(section == 3)
        def _():
            block_from_out(layer).wait()

    def pick_up(layer):
        load_up(layer).wait()
        load_down(layer).wait()
        raw = b.raw_up[layer]
        for s in range(4):

            @pl.when(section == s)
            def _():
                b.wf[layer, 0, high, low, core] = jnp.concatenate(
                    [
                        raw[:, (4 * j + s) * SHARD : (4 * j + s + 1) * SHARD].astype(F32)
                        for j in range(8)
                    ],
                    1,
                ).astype(BF16)

    def line_gather(number, base):
        pairs = [(b.line_s.at[number, i], b.line_r.at[number, i]) for i in range(3)]
        return LineGather(p, base, *pairs)

    block = [line_gather(layer, b.wa.at[layer, 0]) for layer in range(2)]
    feed_lines = [
        [line_gather(2 + 2 * layer + which, b.wf.at[layer, which]) for which in range(2)]
        for layer in range(2)
    ]

    def first_z(step, source):
        view = b.wa.at[0, 0, lax.div(source, 2), lax.rem(source, 2), core]
        return remote(
            view,
            view,
            b.az_s.at[step],
            b.az_r.at[step],
            "seq",
            2 * lax.rem(chip + step, 4) + core,
        )

    def block_plane(layer, k):
        source = b.wa.at[layer, 0, :, :, core]
        target = b.wa.at[layer, 1, :, :, core]
        return remote(source, target, b.axy_s.at[layer, k], b.axy_r.at[layer, k], "section", peers[k])

    def block_across(layer, k, side):
        view = b.wa.at[layer, 1, :, :, side]
        return remote(view, view, b.axs_s.at[layer, k], b.axs_r.at[layer, k], "seq", p.sibling)

    for layer in range(2):
        model = b.model[layer].astype(F32)
        hidden_gain = b.hgains[layer : layer + 1, :].astype(F32)
        hidden_bias = b.hbiases[layer].astype(F32)
        lines = [model]
        for each in (hidden_gain, hidden_bias[0:1, :], hidden_bias[1:2, :]):
            for s in range(4):
                lines.append(each[:, s * SHARD : (s + 1) * SHARD])
        lines.append(jnp.zeros((11, SHARD), F32))
        packed = jnp.concatenate(lines, 0)
        packed = jnp.concatenate([packed, jnp.zeros((32, PAIR_LANES - SHARD), F32)], 1)
        b.small_src[layer] = packed.astype(BF16)
    b.small[me] = b.small_src[...]
    make_picks(lengths, section, p.my_pair, b.picks)
    b.logs[...] = jnp.zeros_like(b.logs)
    block_loaded(0)
    pl.semaphore_wait(barrier, 31)

    def small_copy(step):
        return remote(
            b.small_src,
            b.small.at[me],
            b.small_s.at[step],
            b.small_r.at[step],
            "seq",
            lax.rem(me + step, 8),
        )

    for step in range(1, 8):
        small_copy(step).start()
    for step in range(1, 4):
        first_z(step, chip).start()
    pick_up(0)
    for step in range(1, 8):
        source = lax.rem(me + 8 - step, 8)
        remote(
            b.small_src,
            b.small.at[source],
            b.small_s.at[step],
            b.small_r.at[step],
            "seq",
            source,
        ).wait_recv()
    for layer in range(2):
        pieces = []
        for j in range(8):
            small = b.small[j, layer].astype(F32)
            lines = [small[0:9]]
            for third in range(3):
                line = jnp.zeros((1, PAIR_LANES), F32)
                for s in range(4):
                    at = 9 + 4 * third + s
                    line = line + jnp.where(section == s, small[at : at + 1], 0.0)
                lines.append(line)
            lines.append(jnp.zeros((4, PAIR_LANES), F32))
            pieces.append(jnp.concatenate(lines, 0)[:, 0:SHARD])
        b.vecs[layer] = jnp.concatenate(pieces, 1)

    def wide_copy(layer, k, pair):
        return remote_both(
            b.proj_send.at[k, pair],
            b.qkv.at[layer, lax.rem(section, 3), rows_of(me)],
            b.wide_s.at[layer, k, pair],
            b.wide_r.at[layer, lax.rem(section, 3), me],
            peers[k],
            OWNERS[pair],
        )

    def project(layer, arrive):
        vec = b.vecs.at[layer]

        @pl.when(section != 3)
        def _():
            bias = jnp.where(section == 2, vec[6:7, :], 0.0)
            for k in (3, 1, 2, 0) if layer == 0 else (0, 1, 2, 3):
                if k > 0:
                    arrive(k)
                part = mul(b.left[layer, slot_rows(k), :], square(b.wa.at[layer, 0])) + bias
                part = part.astype(BF16)
                for pair in (5, 0, 3, 2, 4, 1):
                    owner = OWNERS[pair]
                    b.proj_send[k, pair] = part[:, pair * PAIR_LANES : (pair + 1) * PAIR_LANES]
                    if k > 0:
                        wide_copy(layer, k, pair).start()
                    else:

                        @pl.when(me != owner)
                        def _():
                            wide_copy(layer, k, pair).start()

                        @pl.when(me == owner)
                        def _():
                            b.qkv[layer, section, rows_of(me), :] = b.proj_send[k, pair]

    def wait_projected(layer):
        @pl.when(p.is_owner)
        def _():
            for third in range(3):
                for source in range(8):

                    @pl.when((section != third) | (me != source))
                    def _():
                        remote_both(
                            b.proj_send.at[0, 0],
                            b.qkv.at[layer, third, pl.ds(source * TOKENS, TOKENS)],
                            b.wide_s.at[layer, 0, 0],
                            b.wide_r.at[layer, third, source],
                            third,
                            source,
                        ).wait_recv()

        @pl.when(section != 3)
        def _():
            for k in range(4):
                for pair, owner in enumerate(OWNERS):
                    if k > 0:
                        wide_copy(layer, k, pair).wait_send()
                    else:

                        @pl.when(me != owner)
                        def _():
                            wide_copy(layer, k, pair).wait_send()

    def back_copy(layer, target):
        return remote(
            b.att_send.at[pl.ds(target * TOKENS, TOKENS)],
            b.att_recv.at[layer, p.my_pair],
            b.att_s.at[layer, target],
            b.att_r.at[layer, p.my_pair],
            "seq",
            target,
        )

    def attend(layer):
        lane = lax.broadcasted_iota(jnp.int32, (QUERY_STEP, PAIR_LANES), 1)
        first_half = lane < HEAD_DIM
        for step in range(GROUP_TOKENS // QUERY_STEP):
            start = step * QUERY_STEP
            keys_end = start + QUERY_STEP
            rows = slice(start, keys_end)
            query = b.qkv[layer, 0, rows, :] * jnp.asarray(SCALE, BF16)
            keys = b.qkv[layer, 1, 0:keys_end, :]
            values = b.qkv[layer, 2, 0:keys_end, :]
            causal = lax.broadcasted_iota(jnp.int32, (QUERY_STEP, keys_end), 1) <= (
                start + lax.broadcasted_iota(jnp.int32, (QUERY_STEP, keys_end), 0)
            )
            sums = []
            totals = []
            logs = jnp.zeros((1, PAIR_LANES), F32)
            picked_sum = jnp.zeros((1, PAIR_LANES), F32)
            for head in range(2):
                mine = first_half if head == 0 else ~first_half
                own_query = jnp.where(mine, query, jnp.zeros_like(query))
                scores = mul_nt(own_query, keys)
                raised = jnp.where(causal, jnp.exp(scores), 0.0)
                pick_query = b.picks[head, rows, :]
                pick_keys = b.picks[head, 0:keys_end, :]
                counts = mul_nt(pick_query, pick_keys)
                weighted = (raised * counts).astype(BF16)
                sums.append(mul(weighted, values))
                pattern = mul(raised.astype(BF16), pick_keys)
                picked = pick_query.astype(F32)
                totals.append(jnp.sum(pattern * picked, -1, keepdims=True))
                chosen = picked > 0.5
                logs = logs + jnp.sum(
                    jnp.where(chosen, jnp.log(jnp.where(chosen, pattern, 1.0)), 0.0),
                    0,
                    keepdims=True,
                )
                picked_sum = picked_sum + jnp.sum(picked, 0, keepdims=True)
            b.logs[layer : layer + 1, :] += logs
            if layer == 0:
                b.logs[2:3, :] += picked_sum
            total = jnp.where(first_half, totals[0], totals[1])
            attended = jnp.where(first_half, sums[0], sums[1]) / total
            b.pa[layer, rows, :] = attended
            b.pt[layer, rows, :] = total
            b.att_send[rows, :] = attended.astype(BF16)
            for target in (2 * step, 2 * step + 1):

                @pl.when(me != target)
                def _():
                    back_copy(layer, target).start()

                @pl.when(me == target)
                def _():
                    b.att_recv[layer, p.my_pair] = b.att_send[
                        target * TOKENS : (target + 1) * TOKENS, :
                    ]

    def attention_rest(layer, inputs_ref, after):
        vec = b.vecs.at[layer]
        wait_projected(layer)
        feed_lines[layer][0].start()
        after()

        @pl.when(p.is_owner)
        def _():
            attend(layer)

        feed_lines[layer][0].pass_line()
        for k in range(1, 4):

            @pl.when(peers[k] == 3)
            def _():
                block_plane(layer, k).wait_recv()
                block_across(layer, k, core).start()

        for pair, owner in enumerate(OWNERS):

            @pl.when(me != owner)
            def _():
                remote(
                    b.att_send.at[pl.ds(0, TOKENS)],
                    b.att_recv.at[layer, pair],
                    b.att_s.at[layer, 0],
                    b.att_r.at[layer, pair],
                    "seq",
                    owner,
                ).wait_recv()

            b.att[layer, :, pair * PAIR_LANES : (pair + 1) * PAIR_LANES] = b.att_recv[layer, pair]
        inner_unit, unused = standardize(b.att[layer].astype(F32))
        inner = (inner_unit * vec[1:2, :] + vec[4:5, :]).astype(BF16)
        if layer == 0:
            b.inner[...] = inner
        for k in range(1, 4):

            @pl.when(peers[k] == 3)
            def _():
                block_across(layer, k, 1 - core).wait_recv()

        branch = mul(inner, square(b.wa.at[layer, out_slot])) + vec[7:8, :]
        b.xs[2 * layer] = (inputs_ref[...].astype(F32) + branch).astype(BF16)

    def attention_drain(layer):
        @pl.when(p.is_owner)
        def _():
            for target in range(8):

                @pl.when(me != target)
                def _():
                    back_copy(layer, target).wait_send()

    def feed(layer, resting, parting):
        vec = b.vecs.at[layer]
        inputs = b.xs[2 * layer].astype(F32)
        unit, unused = standardize(inputs)
        b.hid[layer, slot_rows(0), :] = (unit * vec[2:3, :] + vec[5:6, :]).astype(BF16)
        hidden_copies = [
            remote(
                b.hid.at[layer, pl.ds(0, TOKENS)],
                b.hid.at[layer, pl.ds(k * TOKENS, TOKENS)],
                b.fhid_s.at[layer, k],
                b.fhid_r.at[layer, k],
                "section",
                peers[k],
            )
            for k in range(1, 4)
        ]
        for copy in hidden_copies:
            copy.start()
        up_line, down_line = feed_lines[layer]
        down_line.start()
        up_line.pass_core()
        down_line.pass_line()
        up_line.ready()
        for k in range(4):
            if k > 0:
                hidden_copies[k - 1].wait_recv()
            upward = mul(b.hid[layer, slot_rows(k), :], square(b.wf.at[layer, 0])) + vec[10:11, :]
            b.up[layer, slot_rows(k), :] = upward
            values, unused = gelu_parts(upward)
            b.units[slot_rows(k), :] = values
            mean = jnp.mean(values, -1, keepdims=True)
            center = values - mean
            b.columns[slot_rows(k), :] = two_columns(
                mean, jnp.sum(center * center, -1, keepdims=True)
            )
        stat_copies = share_stats(
            b.columns[...],
            b.stat_send,
            b.fstat_recv.at[layer],
            b.fstat_s.at[layer],
            b.fstat_r.at[layer],
            peers,
        )
        down_line.pass_core()
        resting()
        for copy in stat_copies:
            copy.wait_recv()
        b.stat_rows[...] = jnp.zeros((PAIR_LANES, WIDE), F32)
        for k in range(4):
            means = [b.fstat_recv[layer, other, 0:1, slot_rows(k ^ other)] for other in range(4)]
            squares = [b.fstat_recv[layer, other, 1:2, slot_rows(k ^ other)] for other in range(4)]
            mean = (means[0] + means[1] + means[2] + means[3]) * 0.25
            spread = squares[0] + squares[1] + squares[2] + squares[3]
            for each in means:
                spread = spread + D * (each - mean) * (each - mean)
            b.stat_rows[0:1, slot_rows(k)] = mean
            b.stat_rows[1:2, slot_rows(k)] = lax.rsqrt(spread * (1.0 / FF) + EPSILON)
        b.stat[layer] = b.stat_rows[...].T
        down_line.ready()
        if layer == 1:
            parting()
            for copy in hidden_copies + stat_copies:
                copy.wait_send()
            return
        branch = None
        part_copies = []
        for k in (3, 1, 2, 0):
            both = b.stat[layer, slot_rows(k), :]
            inner = (
                (b.units[slot_rows(k), :] - both[:, 0:1]) * both[:, 1:2] * vec[9:10, :]
                + vec[11:12, :]
            ).astype(BF16)
            part = mul(inner, square(b.wf.at[layer, 1]))
            if k == 0:
                branch = part
            else:
                b.part_send[k] = part.astype(BF16)
                part_copies.append(
                    remote(
                        b.part_send.at[k],
                        b.first_recv.at[k],
                        b.first_s.at[k],
                        b.first_r.at[k],
                        "section",
                        peers[k],
                    )
                )
                part_copies[-1].start()
        parting()
        for k, copy in zip((3, 1, 2), part_copies):
            copy.wait_recv()
            branch = branch + b.first_recv[k].astype(F32)
        b.xs[2 * layer + 1] = (inputs + branch + vec[8:9, :]).astype(BF16)
        for copy in hidden_copies + stat_copies + part_copies:
            copy.wait_send()

    def sub_copies(number, forward):
        source = b.xs if forward else b.streams
        target = b.sub_f_out if forward else b.sub_g_out
        send_sem = b.subf_s if forward else b.subg_s
        recv_sem = b.subf_r if forward else b.subg_r

        def away():
            return remote(
                source.at[number],
                target.at[section],
                send_sem.at[number],
                recv_sem.at[section],
                "section",
                number,
            )

        def own():
            return pltpu.make_async_copy(
                source.at[number], target.at[section], b.own_sem.at[0 if forward else 1]
            )

        return away, own

    def send_sub(number, forward):
        @pl.when(section != number)
        def _():
            sub_copies(number, forward)[0]().start()

        @pl.when(section == number)
        def _():
            sub_copies(number, forward)[1]().start()

    def drain_sub(number, forward):
        @pl.when(section != number)
        def _():
            sub_copies(number, forward)[0]().wait_send()

        @pl.when(section == number)
        def _():
            sub_copies(number, forward)[1]().wait()

    def receive_sub(source, forward):
        target = b.sub_f_out if forward else b.sub_g_out

        @pl.when(section != source)
        def _():
            remote(
                b.streams.at[0],
                target.at[source],
                (b.subf_s if forward else b.subg_s).at[0],
                (b.subf_r if forward else b.subg_r).at[source],
                "section",
                source,
            ).wait_recv()

    for k in range(4):
        load_embeds(k).wait()

        @pl.when(section != 3)
        def _():
            unit, unused = standardize(b.embeds[k].astype(F32))
            b.left[0, slot_rows(k), :] = (
                unit * b.vecs[0, 0:1, :] + b.vecs[0, 3:4, :]
            ).astype(BF16)
    pick_up(1)
    for step in range(1, 4):
        first_z(step, lax.rem(chip + 4 - step, 4)).wait_recv()
    block[0].cores(core).start()

    @pl.when(section == 3)
    def _():
        for k in range(1, 4):
            block_plane(0, k).start()

    block[0].ready()
    project(0, lambda k: None)

    attention_rest(0, b.embeds.at[0], lambda: None)

    def resting_first():
        block_loaded(1)
        block[1].start()

    def parting_first():
        attention_drain(0)
        block[1].pass_line()

    feed(0, resting_first, parting_first)

    second = b.vecs.at[1]
    unit, unused = standardize(b.xs[1].astype(F32))
    b.left[1, slot_rows(0), :] = (unit * second[0:1, :] + second[3:4, :]).astype(BF16)

    def left_copy(k):
        return remote(
            b.left.at[1, pl.ds(0, TOKENS)],
            b.left.at[1, pl.ds(k * TOKENS, TOKENS)],
            b.fleft_s.at[k],
            b.fleft_r.at[k],
            "section",
            peers[k],
        )

    for k in (3, 1, 2):

        @pl.when(peers[k] != 3)
        def _():
            left_copy(k).start()

    block[1].pass_core()
    for k in range(1, 4):

        @pl.when(peers[k] != 3)
        def _():
            left_copy(k).wait_send()

    @pl.when(section == 3)
    def _():
        for k in range(1, 4):
            block_plane(1, k).start()

    block[1].ready()
    project(1, lambda k: left_copy(k).wait_recv())

    def inner_copy(k):
        return remote(
            b.inner,
            b.left.at[0, pl.ds(k * TOKENS, TOKENS)],
            b.inner_s.at[k],
            b.inner_r.at[k],
            "section",
            peers[k],
        )

    def after_second():
        for k in range(1, 4):

            @pl.when(peers[k] == 3)
            def _():
                inner_copy(k).start()

        @pl.when(section == 3)
        def _():
            b.left[0, slot_rows(0), :] = b.inner[...]

        send_sub(0, True)
        send_sub(1, True)

    attention_rest(1, b.xs.at[1], after_second)

    def resting_second():
        send_sub(2, True)
        for k in range(1, 4):

            @pl.when(peers[k] == 3)
            def _():
                inner_copy(k).wait_send()

        @pl.when(section == 3)
        def _():
            for k in range(1, 4):
                inner_copy(k).wait_recv()

    def parting_second():
        attention_drain(1)

    feed(1, resting_second, parting_second)

    def cotangent_load(k):
        return pltpu.make_async_copy(
            b.cotangent_in.at[peers[k]], b.grads.at[pl.ds(k * TOKENS, TOKENS)], b.cot_sem.at[k]
        )

    for k in range(4):
        cotangent_load(k).start()

    def log_copy(step):
        return remote(
            b.logs,
            b.log_line.at[me],
            b.log_s.at[step],
            b.log_r.at[step],
            "seq",
            lax.rem(me + step, 8),
        )

    def log_plane_copy(k, slot):
        return remote(
            b.log_plane.at[slot],
            b.log_plane.at[slot],
            b.log_plane_s.at[k],
            b.log_plane_r.at[k],
            "section",
            peers[k],
        )

    def start_logs():
        b.log_line[me] = b.logs[...]
        for step in range(1, 8):
            log_copy(step).start()

    def sum_logs():
        for step in range(1, 8):
            source = lax.rem(me + 8 - step, 8)
            remote(
                b.logs,
                b.log_line.at[source],
                b.log_s.at[step],
                b.log_r.at[step],
                "seq",
                source,
            ).wait_recv()
        total = b.log_line[0]
        for j in range(1, 8):
            total = total + b.log_line[j]
        b.log_plane[section] = total
        for k in range(1, 4):
            log_plane_copy(k, section).start()

    def finish_logs():
        for k in range(1, 4):
            log_plane_copy(k, peers[k]).wait_recv()
        total = b.log_plane[0]
        for other in range(1, 4):
            total = total + b.log_plane[other]
        b.log_total[...] = total
        for step in range(1, 8):
            log_copy(step).wait_send()
        for k in range(1, 4):
            log_plane_copy(k, section).wait_send()

    class Matrix:
        def __init__(self, number):
            self.number = number
            self.direct = number > 4
            self.turn = (1, 2) if number % 2 else (2, 1)
            self.j = number % 3 if number < 6 else number - 6
            if number < 6:
                self.i = number
                refs = (b.prod, b.pair, b.near, b.far, b.done, b.all_m_out)
            else:
                self.i = number - 6
                refs = (b.prod_v, b.pair_v, b.near_v, b.far_v, b.done_v, b.all_v_out)
            self.prod, self.pair, self.near, self.far, self.done, self.all = refs

        def store(self, value):
            if 3 <= self.number < 6:
                matrices[self.number - 3].sent()
            for j in range(8):
                self.prod[self.j, j % 2, j // 4, j // 2 % 2] = value[
                    j * SHARD : (j + 1) * SHARD, :
                ].astype(BF16)

        def pair_copy(self):
            n = self.number
            return remote(
                self.prod.at[self.j, 1 - core],
                self.pair.at[self.i],
                b.pair_s.at[n],
                b.pair_r.at[n],
                "seq",
                p.sibling,
            )

        def near_copy(self):
            n = self.number
            return remote(
                self.prod.at[self.j, core, :, 1 - low],
                self.near.at[self.i],
                b.near_s.at[n],
                b.near_r.at[n],
                "seq",
                p.next,
            )

        def far_copy(self):
            n = self.number
            return remote(
                self.prod.at[self.j, core, 1 - high, low],
                self.far.at[self.i],
                b.far_s.at[n],
                b.far_r.at[n],
                "seq",
                p.across,
            )

        def all_copy(self, k, slot):
            n = self.number
            return remote(
                self.done.at[self.i],
                self.all.at[self.i, slot],
                b.all_s.at[n, k],
                b.all_r.at[n, k],
                "section",
                peers[k],
            )

        def own_copy(self):
            return pltpu.make_async_copy(
                self.done.at[self.i], self.all.at[self.i, section], b.all_s.at[self.number, 0]
            )

        def step_near(self):
            self.pair_copy().wait_recv()
            i, at = (self.i, self.j)
            for h in range(2):
                for l in range(2):
                    self.prod[at, core, h, l] = (
                        self.prod[at, core, h, l].astype(F32) + self.pair[i, h, l].astype(F32)
                    ).astype(BF16)
            self.near_copy().start()

        def step_far(self):
            self.near_copy().wait_recv()
            i, at = (self.i, self.j)
            for h in range(2):
                self.prod[at, core, h, low] = (
                    self.prod[at, core, h, low].astype(F32) + self.near[i, h].astype(F32)
                ).astype(BF16)
            self.far_copy().start()

        def step_plane(self):
            self.far_copy().wait_recv()
            i = self.i
            self.done[i] = (
                self.prod[self.j, core, high, low].astype(F32) + self.far[i].astype(F32)
            ).astype(BF16)
            for k in (3, 1, 2) if self.direct else (1, 2):
                self.all_copy(k, section).start()
            self.own_copy().start()

        def turn_copy(self):
            n = self.number
            first, second = self.turn
            view = self.all.at[self.i, peers[first]]
            return remote(
                view, view, b.all_s.at[n, 3], b.all_r.at[n, 3], "section", peers[second]
            )

        def step_pass(self):
            first = self.turn[0]
            self.all_copy(first, peers[first]).wait_recv()
            self.turn_copy().start()

        def step_end(self):
            for k in range(1, 4):
                if self.direct or k != self.turn[0]:
                    self.all_copy(k, peers[k]).wait_recv()
                if self.direct or k != 3:
                    self.all_copy(k, section).wait_send()
                else:
                    self.turn_copy().wait_send()
            self.own_copy().wait()
            if self.number > 2:
                self.sent()

        def sent(self):
            self.pair_copy().wait_send()
            self.near_copy().wait_send()
            self.far_copy().wait_send()

    matrices = [Matrix(number) for number in range(8)]
    up1, down1, att1, up0, down0, att0, vec1, vec0 = matrices

    def last_copy(k):
        return remote(
            b.last_send.at[k],
            b.last_recv.at[k],
            b.last_s.at[k],
            b.last_r.at[k],
            "section",
            peers[k],
        )

    def start_last():
        for k in (3, 1, 2, 0):
            part = mul(b.inners[slot_rows(k), :], square(b.wf.at[1, 1]))
            if k == 0:
                b.last[...] = part
            else:
                b.last_send[k] = part.astype(BF16)
                last_copy(k).start()

    def finish_last():
        total = b.xs[2].astype(F32) + b.last[...] + b.vecs[1, 8:9, :]
        for k in range(1, 4):
            last_copy(k).wait_recv()
            total = total + b.last_recv[k].astype(F32)
        b.xs[3] = total.astype(BF16)
        for k in range(1, 4):
            last_copy(k).wait_send()

    def feed_phase(layer, grad_ref, x_ref, hooks):
        phase = 1 - layer
        vec = b.vecs.at[layer]
        rows = b.vec_rows.at[layer]
        up_matrix = matrices[3 * phase]
        down_matrix = matrices[3 * phase + 1]
        early, middle, parting, late = hooks
        if layer == 0:
            b.grads[slot_rows(0), :] = grad_ref[...]
        grad_copies = [] if layer == 1 else [
            remote(
                b.grads.at[pl.ds(0, TOKENS)],
                b.grads.at[pl.ds(k * TOKENS, TOKENS)],
                b.g_s.at[phase, k],
                b.g_r.at[phase, k],
                "section",
                peers[k],
            )
            for k in range(1, 4)
        ]
        if layer == 0:
            for k in (3, 1, 2):
                grad_copies[k - 1].start()
        rows[...] = jnp.zeros((PAIR_LANES, D), F32)
        early()
        for k in range(4):
            both = b.stat[layer, slot_rows(k), :]
            upward = b.up[layer, slot_rows(k), :]
            values, below = gelu_parts(upward)
            b.up[layer, slot_rows(k), :] = below + upward * (
                jnp.exp(-0.5 * upward * upward) * (0.5 / 3.141592653589793) ** 0.5
            )
            unit = (values - both[:, 0:1]) * both[:, 1:2]
            b.units[slot_rows(k), :] = unit
            b.inners[slot_rows(k), :] = (unit * vec[9:10, :] + vec[11:12, :]).astype(BF16)
        gain_sum = jnp.zeros((1, D), F32)
        bias_sum = jnp.zeros((1, D), F32)
        for k in range(4):
            if layer == 1:
                cotangent_load(k).wait()
            elif k > 0:
                grad_copies[k - 1].wait_recv()
            unit = b.units[slot_rows(k), :]
            inner_grad = mul_nt(b.grads[slot_rows(k), :], square(b.wf.at[layer, 1]))
            gain_sum = gain_sum + jnp.sum(inner_grad * unit, 0, keepdims=True)
            bias_sum = bias_sum + jnp.sum(inner_grad, 0, keepdims=True)
            unit_grad = inner_grad * vec[9:10, :]
            b.unit_grads[slot_rows(k), :] = unit_grad
            b.columns[slot_rows(k), :] = two_columns(
                jnp.sum(unit_grad, -1, keepdims=True), jnp.sum(unit_grad * unit, -1, keepdims=True)
            )
        stat_copies = share_stats(
            b.columns[...],
            b.stat_send,
            b.stat_recv,
            b.stat_s.at[phase],
            b.stat_r.at[phase],
            peers,
        )
        rows[9:10, :] = gain_sum
        rows[11:12, :] = bias_sum
        down_matrix.store(mul_tn(b.inners[...], b.grads[...]))
        down_matrix.pair_copy().start()
        middle()
        for copy in stat_copies:
            copy.wait_recv()
        b.stat_rows[...] = jnp.zeros((PAIR_LANES, WIDE), F32)
        for k in range(4):
            for line in range(2):
                parts = [
                    b.stat_recv[other, line : line + 1, slot_rows(k ^ other)]
                    for other in range(4)
                ]
                b.stat_rows[line : line + 1, slot_rows(k)] = (
                    parts[0] + parts[1] + parts[2] + parts[3]
                ) * (1.0 / FF)
        b.columns[...] = b.stat_rows[...].T
        hidden_grad = None
        low_sum = jnp.zeros((1, D), F32)
        part_copies = []
        for k in (3, 1, 2, 0):
            rstd = b.stat[layer, slot_rows(k), :][:, 1:2]
            both = b.columns[slot_rows(k), :]
            lowered = (
                rstd
                * (
                    b.unit_grads[slot_rows(k), :]
                    - both[:, 0:1]
                    - b.units[slot_rows(k), :] * both[:, 1:2]
                )
                * b.up[layer, slot_rows(k), :]
            ).astype(BF16)
            b.lows[slot_rows(k), :] = lowered
            low_sum = low_sum + jnp.sum(lowered.astype(F32), 0, keepdims=True)
            part = mul_nt(lowered, square(b.wf.at[layer, 0]))
            if k == 0:
                hidden_grad = part
            else:
                b.part_send[k] = part.astype(BF16)
                part_copies.append(
                    remote(
                        b.part_send.at[k],
                        b.part_recv.at[k],
                        b.part_s.at[phase, k],
                        b.part_r.at[phase, k],
                        "section",
                        peers[k],
                    )
                )
                part_copies[-1].start()
        rows[10:11, :] = low_sum
        up_matrix.store(mul_tn(b.hid[layer], b.lows[...]))
        up_matrix.pair_copy().start()
        unit, rstd = standardize(x_ref[...].astype(F32))
        parting()
        for k, copy in zip((3, 1, 2), part_copies):
            copy.wait_recv()
            hidden_grad = hidden_grad + b.part_recv[k].astype(F32)
        grad = grad_ref[...].astype(F32)
        number = 2 * layer + 1
        b.streams[number] = (
            grad + norm_back(unit, rstd, hidden_grad * vec[2:3, :])
        ).astype(BF16)
        rows[2:3, :] = jnp.sum(hidden_grad * unit, 0, keepdims=True)
        rows[5:6, :] = jnp.sum(hidden_grad, 0, keepdims=True)
        rows[8:9, :] = jnp.sum(grad, 0, keepdims=True)
        for copy in grad_copies + stat_copies + part_copies:
            copy.wait_send()
        late()

    def attention_phase(layer, grad_ref, x_ref, att_ref, hooks):
        phase = 1 - layer
        vec = b.vecs.at[layer]
        rows = b.vec_rows.at[layer]
        before, inside, after, during = hooks
        grad = grad_ref[...]
        inner_unit, inner_rstd = standardize(att_ref[...].astype(F32))
        inner_grad = mul_nt(grad, square(b.wa.at[layer, out_slot]))
        att_grad = norm_back(inner_unit, inner_rstd, inner_grad * vec[1:2, :]).astype(BF16)
        for pair in range(PAIRS):
            b.do_send[pair] = att_grad[:, pair * PAIR_LANES : (pair + 1) * PAIR_LANES]

        def out_copy(pair):
            return remote(
                b.do_send.at[pair],
                b.do_recv.at[rows_of(me)],
                b.do_s.at[phase, pair],
                b.do_r.at[phase, me],
                "seq",
                OWNERS[pair],
            )

        for pair, owner in enumerate(OWNERS):

            @pl.when(me != owner)
            def _():
                out_copy(pair).start()

            @pl.when(me == owner)
            def _():
                b.do_recv[rows_of(me), :] = b.do_send[pair]

        def left_copy(k):
            return remote(
                b.left_src,
                b.left.at[layer, pl.ds(k * TOKENS, TOKENS)],
                b.left_s.at[phase, k],
                b.left_r.at[phase, k],
                "section",
                peers[k],
            )

        def right_copy(k):
            return remote(
                b.right_src,
                b.right.at[layer, pl.ds(k * TOKENS, TOKENS)],
                b.right_s.at[phase, k],
                b.right_r.at[phase, k],
                "section",
                peers[k],
            )

        unit, rstd = standardize(x_ref[...].astype(F32))
        b.left_src[...] = (inner_unit * vec[1:2, :] + vec[4:5, :]).astype(BF16)
        b.right_src[...] = grad
        for k in range(1, 4):

            @pl.when(peers[k] == 3)
            def _():
                right_copy(k).start()
                if layer == 1:
                    left_copy(k).start()

        if layer == 1:

            @pl.when(section == 3)
            def _():
                b.left[layer, slot_rows(0), :] = b.left_src[...]

        rows[1:2, :] = jnp.sum(inner_grad * inner_unit, 0, keepdims=True)
        rows[4:5, :] = jnp.sum(inner_grad, 0, keepdims=True)
        rows[7:8, :] = jnp.sum(grad.astype(F32), 0, keepdims=True)

        def back_copy(third, target):
            return remote_both(
                b.d_send.at[third, pl.ds(target * TOKENS, TOKENS)],
                b.d_recv.at[layer, section, p.my_pair],
                b.d_s.at[phase, third, target],
                b.d_r.at[phase, section, p.my_pair],
                third,
                target,
            )

        @pl.when(p.is_owner)
        def _():
            for source in range(8):

                @pl.when(me != source)
                def _():
                    remote(
                        b.do_send.at[0],
                        b.do_recv.at[pl.ds(source * TOKENS, TOKENS)],
                        b.do_s.at[phase, 0],
                        b.do_r.at[phase, source],
                        "seq",
                        source,
                    ).wait_recv()

        before()

        @pl.when(p.is_owner)
        def _():
            b.key_sum[...] = jnp.zeros((GROUP_TOKENS, PAIR_LANES), F32)
            b.value_sum[...] = jnp.zeros((GROUP_TOKENS, PAIR_LANES), F32)
            lane = lax.broadcasted_iota(jnp.int32, (QUERY_STEP, PAIR_LANES), 1)
            first_half = lane < HEAD_DIM
            last_step = GROUP_TOKENS // QUERY_STEP - 1
            for step in (0,) + tuple(range(last_step, 0, -1)):
                start = step * QUERY_STEP
                keys_end = start + QUERY_STEP
                block = slice(start, keys_end)
                plain_query = b.qkv[layer, 0, block, :]
                query = plain_query * jnp.asarray(SCALE, BF16)
                keys = b.qkv[layer, 1, 0:keys_end, :]
                values = b.qkv[layer, 2, 0:keys_end, :]
                causal = lax.broadcasted_iota(jnp.int32, (QUERY_STEP, keys_end), 1) <= (
                    start + lax.broadcasted_iota(jnp.int32, (QUERY_STEP, keys_end), 0)
                )
                head_grad = b.do_recv[block, :]
                inverse = 1.0 / b.pt[layer, block, :]
                head_float = head_grad.astype(F32)
                products = head_float * b.pa[layer, block, :]
                scaled = (head_float * inverse).astype(BF16)
                key_lanes = lax.broadcasted_iota(jnp.int32, (keys_end, PAIR_LANES), 1) < HEAD_DIM
                query_parts = []
                key_parts = []
                value_parts = []
                for head in range(2):
                    mine = first_half if head == 0 else ~first_half
                    own_query = jnp.where(mine, query, jnp.zeros_like(query))
                    own_grad = jnp.where(mine, head_grad, jnp.zeros_like(head_grad))
                    delta = jnp.sum(jnp.where(mine, products, 0.0), -1, keepdims=True)
                    own_inverse = jnp.max(jnp.where(mine, inverse, 0.0), -1, keepdims=True)
                    counts = mul_nt(b.picks[head, block, :], b.picks[head, 0:keys_end, :])
                    scores = mul_nt(own_query, keys)
                    weighted = jnp.where(causal, jnp.exp(scores) * counts, 0.0)
                    prob_grad = mul_nt(own_grad, values)
                    score_grad = (weighted * own_inverse * (prob_grad - delta)).astype(BF16)
                    query_parts.append(mul(score_grad, keys))
                    key_parts.append(mul_tn(score_grad, plain_query))
                    value_parts.append(mul_tn(weighted.astype(BF16), scaled))
                b.key_sum[0:keys_end, :] += jnp.where(key_lanes, key_parts[0], key_parts[1])
                b.value_sum[0:keys_end, :] += jnp.where(key_lanes, value_parts[0], value_parts[1])
                query_grad = jnp.where(first_half, query_parts[0], query_parts[1]) * SCALE
                b.d_send[0, block, :] = query_grad.astype(BF16)
                ready = [(0, step)]
                if step > 0:
                    ready = [(0, step), (1, step), (2, step)]
                if step == 1:
                    ready = [(1, 0), (2, 0)] + ready
                for third, part in ready:
                    part_rows = slice(part * QUERY_STEP, (part + 1) * QUERY_STEP)
                    if third == 1:
                        b.d_send[1, part_rows, :] = (b.key_sum[part_rows, :] * SCALE).astype(BF16)
                    if third == 2:
                        b.d_send[2, part_rows, :] = b.value_sum[part_rows, :].astype(BF16)
                    for target in (2 * part, 2 * part + 1):
                        away = (section != third) | (me != target)

                        @pl.when(away)
                        def _():
                            back_copy(third, target).start()

                        @pl.when(~away)
                        def _():
                            b.d_recv[layer, section, p.my_pair] = b.d_send[
                                third, target * TOKENS : (target + 1) * TOKENS, :
                            ]

        inside()
        after()

        def part_copy(k):
            return remote(
                b.part_send.at[k],
                b.part_recv.at[k],
                b.back_s.at[phase, k],
                b.back_r.at[phase, k],
                "section",
                peers[k],
            )

        @pl.when(section != 3)
        def _():
            for k in (3, 2, 1, 0):
                for pair, owner in enumerate(OWNERS):
                    away = me != owner if k == 0 else True

                    @pl.when(away)
                    def _():
                        remote_both(
                            b.d_send.at[0, pl.ds(0, TOKENS)],
                            b.d_recv.at[layer, peers[k], pair],
                            b.d_s.at[phase, 0, 0],
                            b.d_r.at[phase, peers[k], pair],
                            peers[k],
                            owner,
                        ).wait_recv()

                    b.right[layer, slot_rows(k), pair * PAIR_LANES : (pair + 1) * PAIR_LANES] = (
                        b.d_recv[layer, peers[k], pair]
                    )
                part = mul_nt(b.right[layer, slot_rows(k), :], square(b.wa.at[layer, 0]))
                if k == 0:
                    b.hidden_grad[...] = part
                else:
                    b.part_send[k] = part.astype(BF16)
                    part_copy(k).start()

        @pl.when(section == 3)
        def _():
            b.right[layer, slot_rows(0), :] = b.right_src[...]
            b.hidden_grad[...] = jnp.zeros((TOKENS, D), F32)
            for k in range(1, 4):
                right_copy(k).wait_recv()
                if layer == 1:
                    left_copy(k).wait_recv()

        matrix = matrices[3 * phase + 2]
        matrix.store(mul_tn(b.left[layer], b.right[layer]))
        matrix.pair_copy().start()
        value_sum = jnp.sum(b.right[layer].astype(F32), 0, keepdims=True)
        rows[6:7, :] = jnp.where(section == 2, value_sum, 0.0)
        during()
        for k in (3, 1, 2):

            @pl.when(peers[k] != 3)
            def _():
                part_copy(k).wait_recv()
                b.hidden_grad[...] += b.part_recv[k].astype(F32)

        hidden_grad = b.hidden_grad[...]
        b.streams[2 * layer] = (
            grad.astype(F32) + norm_back(unit, rstd, hidden_grad * vec[0:1, :])
        ).astype(BF16)
        rows[0:1, :] = jnp.sum(hidden_grad * unit, 0, keepdims=True)
        rows[3:4, :] = jnp.sum(hidden_grad, 0, keepdims=True)

        def drain():
            @pl.when(section != 3)
            def _():
                for k in range(1, 4):
                    part_copy(k).wait_send()

            for k in range(1, 4):

                @pl.when(peers[k] == 3)
                def _():
                    right_copy(k).wait_send()
                    if layer == 1:
                        left_copy(k).wait_send()

            for pair, owner in enumerate(OWNERS):

                @pl.when(me != owner)
                def _():
                    out_copy(pair).wait_send()

            @pl.when(p.is_owner)
            def _():
                for third in range(3):
                    for target in range(8):

                        @pl.when((section != third) | (me != target))
                        def _():
                            back_copy(third, target).wait_send()

        return drain

    def nothing():
        pass

    def middle_first():
        start_logs()

    def late_first():
        start_last()

    feed_phase(
        1,
        b.grads.at[pl.ds(0, TOKENS)],
        b.xs.at[2],
        (nothing, middle_first, down1.step_near, late_first),
    )

    def third_out(k):
        return pltpu.make_async_copy(
            b.right.at[1, pl.ds(k * TOKENS, TOKENS)], b.sub_g_out.at[peers[k]], b.third_sem.at[k]
        )

    def before_first():
        down1.step_far()

    def during_first():
        up1.step_far()
        down1.step_pass()
        finish_last()
        sum_logs()

    drain_first = attention_phase(
        1,
        b.streams.at[3],
        b.xs.at[1],
        b.att.at[1],
        (before_first, down1.step_plane, up1.step_near, during_first),
    )

    def early_second():
        vec1.store(b.vec_rows[1].T)
        vec1.pair_copy().start()
        drain_first()
        att1.step_near()

    def middle_second():
        att1.step_far()
        vec1.step_near()
        up1.step_plane()
        down0.step_near()

    def parting_second():
        down0.step_far()
        vec1.step_far()
        up1.step_pass()

    feed_phase(
        0,
        b.streams.at[2],
        b.xs.at[0],
        (early_second, middle_second, parting_second, nothing),
    )

    def before_second():
        up0.step_near()
        send_sub(3, True)

    def inside_second():
        att1.step_plane()
        vec1.step_plane()
        down0.step_plane()
        for number in (2, 1):
            send_sub(number, False)

        @pl.when(section == 3)
        def _():
            for k in range(4):
                third_out(k).start()

        finish_logs()

    def during_second():
        att0.step_near()
        up0.step_far()
        att1.step_pass()
        down0.step_pass()

    drain_second = attention_phase(
        0,
        b.streams.at[1],
        b.embeds.at[0],
        b.att.at[0],
        (before_second, inside_second, nothing, during_second),
    )
    vec0.store(b.vec_rows[0].T)
    vec0.pair_copy().start()
    att0.step_far()
    send_sub(0, False)
    vec0.step_near()
    up0.step_plane()
    vec0.step_far()
    up0.step_pass()
    att0.step_plane()
    vec0.step_plane()
    drain_second()
    for matrix in (up1, down1, att1, vec1, down0, up0, vec0, att0):
        matrix.step_end()
    for number in range(3):
        drain_sub(number, False)

    @pl.when(section != 3)
    def _():
        for source in range(4):
            receive_sub(source, False)

    @pl.when(section == 3)
    def _():
        for k in range(4):
            third_out(k).wait()

    for number in range(4):
        drain_sub(number, True)
        receive_sub(number, True)
    for step in range(1, 8):
        small_copy(step).wait_send()
    for step in range(1, 4):
        first_z(step, chip).wait_send()
    block[0].cores(core).wait_send()
    block[1].drain()
    for layer in range(2):
        for line in feed_lines[layer]:
            line.drain()
        for k in range(1, 4):

            @pl.when(section == 3)
            def _():
                block_plane(layer, k).wait_send()

            @pl.when(peers[k] == 3)
            def _():
                block_across(layer, k, core).wait_send()


FINISH_IN = dict(all_m=0, all_v=0, sub_f=0, sub_g=0, log_total=0)
FINISH_OUT = dict(
    outputs=((1, 4, TOKENS, D), BF16, False),
    grads=((1, 4, TOKENS, D), BF16, False),
    qkv=((2, SHARD, 3 * D), F32, False),
    out=((2, SHARD, D), F32, False),
    up=((2, SHARD, FF), F32, False),
    down=((2, 4 * SHARD, D), F32, False),
    gains=((2, 3, SHARD), F32, True),
    biases=((2, 6, SHARD), F32, True),
    hgains=((2, 4 * SHARD), F32, True),
    hbiases=((2, 2, 4 * SHARD), F32, True),
    means=((2, 5), F32, True),
)
FINISH_SCRATCH = dict(
    matrix=((6, 4, SHARD, D), BF16),
    vectors=((2, 4, SHARD, PAIR_LANES), BF16),
    wide=((2, SHARD, 4 * D), F32),
    tall=((2, 4 * SHARD, D), F32),
    spread=((2, SHARD, FF), F32),
    first=((4, TOKENS, D), BF16),
    second=((4, TOKENS, D), BF16),
)
FINISH_SEMS = dict(load_sem=(9,), store_sem=(10,))


def finish_kernel(*refs):
    b = Named([FINISH_IN, FINISH_OUT, FINISH_SCRATCH, FINISH_SEMS], refs)
    loads = [
        pltpu.make_async_copy(b.all_m.at[i], b.matrix.at[i], b.load_sem.at[i]) for i in range(6)
    ] + [pltpu.make_async_copy(b.all_v, b.vectors, b.load_sem.at[6])]
    for copy in loads:
        copy.start()

    outputs_load = pltpu.make_async_copy(b.sub_f, b.first, b.load_sem.at[7])
    outputs_load.start()
    grads_load = pltpu.make_async_copy(b.sub_g, b.second, b.load_sem.at[8])
    grads_load.start()
    stores = []

    def store(source, target, number):
        copy = pltpu.make_async_copy(source, target, b.store_sem.at[number])
        copy.start()
        stores.append(copy)

    for layer in (1, 0):
        up_i = 3 * (1 - layer)
        loads[up_i].wait()
        for j in range(8):
            b.spread[layer, :, j * 4 * SHARD : (j + 1) * 4 * SHARD] = jnp.concatenate(
                [
                    b.matrix[up_i, source, :, j * SHARD : (j + 1) * SHARD].astype(F32)
                    for source in range(4)
                ],
                1,
            )
        store(b.spread.at[layer], b.up.at[layer], 4 * layer)
        loads[up_i + 1].wait()
        for source in range(4):
            b.tall[layer, source * SHARD : (source + 1) * SHARD, :] = b.matrix[
                up_i + 1, source
            ].astype(F32)
        store(b.tall.at[layer], b.down.at[layer], 4 * layer + 1)
        loads[up_i + 2].wait()
        for source in range(4):
            b.wide[layer, :, source * D : (source + 1) * D] = b.matrix[up_i + 2, source].astype(
                F32
            )
        store(b.wide.at[layer, :, pl.ds(0, 3 * D)], b.qkv.at[layer], 4 * layer + 2)
        store(b.wide.at[layer, :, pl.ds(3 * D, D)], b.out.at[layer], 4 * layer + 3)
    outputs_load.wait()
    store(b.first, b.outputs.at[0], 8)
    grads_load.wait()
    store(b.second, b.grads.at[0], 9)
    loads[6].wait()
    for layer in range(2):
        lines = []
        for source in range(4):
            tail = b.vectors[1 - layer, source].astype(F32)
            tail = jnp.concatenate([tail, jnp.zeros((PAIR_LANES - SHARD, PAIR_LANES), F32)], 0)
            lines.append(tail.T)
        model = lines[0] + lines[1] + lines[2] + lines[3]
        b.gains[layer] = model[0:3, 0:SHARD]
        b.biases[layer] = model[3:9, 0:SHARD]
        hidden = jnp.concatenate([each[9:12, 0:SHARD] for each in lines], 1)
        b.hgains[layer : layer + 1, :] = hidden[0:1, :]
        b.hbiases[layer] = hidden[1:3, :]
    lane = lax.broadcasted_iota(jnp.int32, (8, PAIR_LANES), 1)
    number = lax.shift_right_logical(lane, 2)
    sums = jnp.zeros((8, PAIR_LANES), F32)
    for i in range(5):
        part = jnp.sum(jnp.where(number == i, b.log_total[...], 0.0), -1, keepdims=True)
        sums = sums + jnp.where(lane == i, part, 0.0)
    means = sums[0:2, :] / jnp.where(lane[0:2, :] < 5, sums[2:3, :], 1.0)
    b.means[...] = means[:, 0:5]
    for copy in stores:
        copy.wait()


def run_remote(kernel, number, lengths, near, far, outs, scratch, sems):
    vmem = pl.BlockSpec(memory_space=pltpu.VMEM)
    anywhere = pl.BlockSpec(memory_space=pl.ANY)
    smem = pl.BlockSpec(memory_space=pltpu.SMEM)
    return pl.pallas_call(
        kernel,
        out_shape=[shaped(out[0], out[1]) for out in outs.values()],
        in_specs=[smem] * len(lengths) + [vmem] * len(near) + [anywhere] * len(far),
        out_specs=[vmem if out[2] else anywhere for out in outs.values()],
        scratch_shapes=[pltpu.VMEM(item[0], item[1]) for item in scratch.values()]
        + [pltpu.SemaphoreType.DMA(item) for item in sems.values()],
        compiler_params=pltpu.CompilerParams(
            collective_id=number, has_side_effects=True, vmem_limit_bytes=KERNEL_VMEM_BYTES
        ),
        cost_estimate=pl.CostEstimate(
            flops=10**10, bytes_accessed=100_000_000, transcendentals=0
        ),
    )(*lengths, *near, *far)


def run_finish(log_total, *far):
    vmem = pl.BlockSpec(memory_space=pltpu.VMEM)
    anywhere = pl.BlockSpec(memory_space=pl.ANY)
    return pl.pallas_call(
        finish_kernel,
        out_shape=[shaped(out[0], out[1]) for out in FINISH_OUT.values()],
        in_specs=[anywhere] * len(far) + [vmem],
        out_specs=[vmem if out[2] else anywhere for out in FINISH_OUT.values()],
        scratch_shapes=[pltpu.VMEM(item[0], item[1]) for item in FINISH_SCRATCH.values()]
        + [pltpu.SemaphoreType.DMA(item) for item in FINISH_SEMS.values()],
        compiler_params=pltpu.CompilerParams(vmem_limit_bytes=KERNEL_VMEM_BYTES),
    )(*far, log_total)


def quick_body(
    embeds,
    row_lengths,
    qkv_weight,
    out_weight,
    up_weight,
    down_weight,
    model_gains,
    model_biases,
    hidden_gains,
    hidden_biases,
    cotangent,
):
    both = Named(
        [BOTH_OUT],
        run_remote(
            both_kernel,
            10,
            (row_lengths,),
            (jnp.concatenate([model_gains, model_biases], 1), hidden_gains, hidden_biases),
            (embeds, qkv_weight, out_weight, up_weight, down_weight, cotangent),
            BOTH_OUT,
            BOTH_SCRATCH,
            BOTH_SEMS,
        ),
    )
    return tuple(
        run_finish(
            both.log_total,
            both.all_m_out,
            both.all_v_out,
            both.sub_f_out,
            both.sub_g_out,
        )
    )


def fits_quick(mesh):
    return mesh.shape["section"] == 4 and mesh.shape["seq"] == 8


def solution(mesh):
    return jax.shard_map(
        quick_body if fits_quick(mesh) else body,
        mesh=mesh,
        in_specs=(
            P(None, "seq", None),
            P(),
            P(None, "seq", None),
            P(None, "seq", None),
            P(None, "seq", None),
            P(None, "seq", None),
            P(None, None, "seq"),
            P(None, None, "seq"),
            P(None, "seq"),
            P(None, None, "seq"),
            P(None, "seq", None),
        ),
        out_specs=(
            P("section", None, "seq", None),
            P("section", None, "seq", None),
            P(None, "seq", None),
            P(None, "seq", None),
            P(None, "seq", None),
            P(None, "seq", None),
            P(None, None, "seq"),
            P(None, None, "seq"),
            P(None, "seq"),
            P(None, None, "seq"),
            P(),
        ),
        check_vma=False,
    )
```

```python
import jax
import jax.numpy as jnp
from jax import lax
from jax.experimental import pallas as pl
from jax.experimental.pallas import tpu as pltpu
from jax.sharding import PartitionSpec as P

D = 768
HEADS = 12
HEAD_DIM = 64
FF = 3072


WIDTHS = (2048, 4096, 8192, 16384, 32768)
RATIOS = (1, 2, 4, 6, 12)
EPSILON = 1e-05


def passed_along(value, axis, steps):
    count = lax.axis_size(axis)
    initial, last = (max(0, -steps), min(count, count - steps))
    return lax.ppermute(value, axis, [(source, source + steps) for source in range(initial, last)])


def norm_rows(inputs, gain_row, offset):
    center = inputs - jnp.mean(inputs, -1, keepdims=True)
    spread = jnp.mean(center * center, -1, keepdims=True)
    return center * lax.rsqrt(spread + EPSILON) * gain_row + offset


def place_rows(lengths, token_index):
    row_ends = jnp.cumsum(lengths)
    passed = token_index[:, None] >= row_ends[None, :]
    row_ids = jnp.sum(passed.astype(jnp.int32), 1)
    offsets = token_index - jnp.sum(jnp.where(passed, lengths[None, :], 0), 1)
    return (row_ids, offsets)


def query_chosen(query_pos):
    head_ids = jnp.arange(HEADS, dtype=jnp.int32)
    chosen = []
    for seg_width, seg_ratio in zip(WIDTHS, RATIOS):
        query_pick = query_pos % seg_width % seg_ratio
        chosen.append(query_pick[None, :] == (head_ids % seg_ratio)[:, None])
    return chosen


def pattern_allow(query_rows, query_pos, key_rows, key_pos):
    widths = jnp.array(WIDTHS, jnp.int32)[:, None]
    ratios = jnp.array(RATIOS, jnp.int32)[:, None]
    residue = jnp.arange(HEADS, dtype=jnp.int32)[None, :] % ratios
    query_mod = query_pos[None, :] % widths % ratios
    key_mod = key_pos[None, :] % widths % ratios
    query_ok = query_mod[:, None, :] == residue[:, :, None]
    key_ok = key_mod[:, None, :] == residue[:, :, None]
    common = (query_rows[:, None] == key_rows[None, :]) & (key_pos[None, :] <= query_pos[:, None])
    inside = common[None] & (
        (query_pos[None, :] // widths)[:, :, None] == (key_pos[None, :] // widths)[:, None, :]
    )
    return inside[:, None] & query_ok[:, :, :, None] & key_ok[:, :, None, :]


def block_rows(total_rows):
    step_rows = min(total_rows, 512)
    return step_rows


def split_heads(matrix):
    return matrix.reshape(matrix.shape[0], HEADS, HEAD_DIM)


def pair_terms(query_block, keys_block, query_rows, query_pos, key_rows, key_pos):
    scores = jnp.einsum(
        "qhe,khe->hqk", query_block, keys_block, preferred_element_type=jnp.float32
    ) * HEAD_DIM ** (-0.5)
    allowed = pattern_allow(query_rows, query_pos, key_rows, key_pos)
    counts = jnp.sum(allowed.astype(jnp.float32), 0)
    raised = jnp.exp(scores)
    return (raised, counts * raised, allowed)


def project_tokens(inputs, qkv_matrix, norm_gains, norm_biases):
    hidden = norm_rows(inputs, norm_gains[0], norm_biases[0]).astype(jnp.bfloat16)
    bias_row = jnp.concatenate(
        [jnp.zeros_like(norm_biases[3]), jnp.zeros_like(norm_biases[3]), norm_biases[3]]
    )
    projected = (jnp.dot(hidden, qkv_matrix, preferred_element_type=jnp.float32) + bias_row).astype(
        jnp.bfloat16
    )
    return (hidden, projected)


def attention_forward(section_in, projected, whole_keys, lengths, params, seq_index):
    out_matrix, norm_gains, norm_biases = (params[1], params[4], params[5])
    tok_rows = section_in.shape[0]
    inputs = section_in.astype(jnp.float32)
    queries = split_heads(projected[:, :D])
    query_rows, query_pos = place_rows(
        lengths, seq_index * tok_rows + jnp.arange(tok_rows, dtype=jnp.int32)
    )
    group_rows = whole_keys.shape[0]
    step_rows = block_rows(group_rows)

    def one_block(running, block_start):
        totals, pattern_sums, accumulated = running
        kv_block = lax.dynamic_slice_in_dim(whole_keys, block_start, step_rows, 0)
        key_rows, key_pos = place_rows(
            lengths, block_start + jnp.arange(step_rows, dtype=jnp.int32)
        )
        raised, weighted, allowed = pair_terms(
            queries, split_heads(kv_block[:, :D]), query_rows, query_pos, key_rows, key_pos
        )
        totals = totals + jnp.sum(weighted, -1)
        pattern_sums = pattern_sums + jnp.sum(jnp.where(allowed, raised[None], 0.0), -1)
        accumulated = accumulated + jnp.einsum(
            "hqk,khe->hqe",
            weighted.astype(jnp.bfloat16),
            split_heads(kv_block[:, D:]),
            preferred_element_type=jnp.float32,
        )
        return ((totals, pattern_sums, accumulated), None)

    start_sums = (
        jnp.zeros((HEADS, tok_rows), jnp.float32),
        jnp.zeros((len(WIDTHS), HEADS, tok_rows), jnp.float32),
        jnp.zeros((HEADS, tok_rows, HEAD_DIM), jnp.float32),
    )
    folded, unused = lax.scan(
        one_block, start_sums, jnp.arange(0, group_rows, step_rows, dtype=jnp.int32)
    )
    totals, pattern_sums, accumulated = folded
    attended = jnp.transpose(accumulated / totals[:, :, None], (1, 0, 2)).reshape(tok_rows, D)
    inner_norm = norm_rows(attended, norm_gains[1], norm_biases[1]).astype(jnp.bfloat16)
    branch = jnp.dot(inner_norm, out_matrix, preferred_element_type=jnp.float32) + norm_biases[4]
    section_out = (inputs + branch).astype(jnp.bfloat16)
    chosen = query_chosen(query_pos)
    log_terms = jnp.stack(
        [
            jnp.sum(
                jnp.where(pick_row, jnp.log(jnp.where(pick_row, pattern_sums[number], 1.0)), 0.0)
            )
            for number, pick_row in enumerate(chosen)
        ]
    )
    pick_counts = jnp.stack([jnp.sum(pick_row.astype(jnp.float32)) for pick_row in chosen])
    return (section_out, attended, totals, log_terms, pick_counts)


def feed_forward(section_in, params):
    up_matrix, down_matrix, norm_gains, norm_biases, hidden_gain, hidden_bias = (
        params[2],
        params[3],
        params[4],
        params[5],
        params[6],
        params[7],
    )
    tok_rows = section_in.shape[0]
    inputs = section_in.astype(jnp.float32)
    hidden = norm_rows(inputs, norm_gains[2], norm_biases[2]).astype(jnp.bfloat16)
    upward = jnp.dot(hidden, up_matrix, preferred_element_type=jnp.float32) + hidden_bias[0]
    inner_norm = norm_rows(
        jax.nn.gelu(upward, approximate=False), hidden_gain, hidden_bias[1]
    ).astype(jnp.bfloat16)
    branch = jnp.dot(inner_norm, down_matrix, preferred_element_type=jnp.float32) + norm_biases[5]
    section_out = (inputs + branch).astype(jnp.bfloat16)
    empty_terms = jnp.zeros((len(WIDTHS),), jnp.float32)
    return (
        section_out,
        jnp.zeros((tok_rows, D), jnp.float32),
        jnp.zeros((HEADS, tok_rows), jnp.float32),
        empty_terms,
        empty_terms,
    )


def attention_middle(
    section_in, grad_out, attended, totals, lengths, all_keys, projected, params, seq_index
):
    out_matrix, norm_gains, norm_biases = (params[1], params[4], params[5])
    scale_factor = HEAD_DIM ** (-0.5)
    tok_rows = section_in.shape[0]
    queries = split_heads(projected[:, :D])
    query_rows, query_pos = place_rows(
        lengths, seq_index * tok_rows + jnp.arange(tok_rows, dtype=jnp.int32)
    )
    inner_norm = norm_rows(attended, norm_gains[1], norm_biases[1]).astype(jnp.bfloat16)
    out_step = jnp.einsum("td,tf->df", inner_norm, grad_out, preferred_element_type=jnp.float32)
    inner_grad = jnp.einsum("tf,df->td", grad_out, out_matrix, preferred_element_type=jnp.float32)
    unused, inner_back = jax.vjp(norm_rows, attended, norm_gains[1], norm_biases[1])
    attended_grad, inner_gain_grad, inner_bias_grad = inner_back(inner_grad)
    low_attended = attended_grad.astype(jnp.bfloat16)
    head_grad = split_heads(low_attended)
    row_dots = jnp.einsum("qhe,qhe->hq", head_grad.astype(jnp.float32), split_heads(attended))
    scaled_grad = head_grad.astype(jnp.float32) / jnp.transpose(totals)[:, :, None]
    group_rows = all_keys.shape[0]
    step_rows = block_rows(group_rows)

    def grad_block(query_grad, block_start):
        kv_block = lax.dynamic_slice_in_dim(all_keys, block_start, step_rows, 0)
        keys_block = split_heads(kv_block[:, :D])
        values_block = split_heads(kv_block[:, D:])
        key_rows, key_pos = place_rows(
            lengths, block_start + jnp.arange(step_rows, dtype=jnp.int32)
        )
        raised, weighted, allowed = pair_terms(
            queries, keys_block, query_rows, query_pos, key_rows, key_pos
        )
        prob_grad = jnp.einsum(
            "qhe,khe->hqk", head_grad, values_block, preferred_element_type=jnp.float32
        )
        score_grad = (weighted / totals[:, :, None] * (prob_grad - row_dots[:, :, None])).astype(
            jnp.bfloat16
        )
        query_grad = (
            query_grad
            + jnp.einsum("hqk,khe->qhe", score_grad, keys_block, preferred_element_type=jnp.float32)
            * scale_factor
        )
        key_grad = (
            jnp.einsum("hqk,qhe->khe", score_grad, queries, preferred_element_type=jnp.float32)
            * scale_factor
        )
        value_grad = jnp.einsum(
            "hqk,qhe->khe",
            weighted.astype(jnp.bfloat16),
            scaled_grad,
            preferred_element_type=jnp.float32,
        )
        block_grad = jnp.concatenate(
            [key_grad.reshape(step_rows, D), value_grad.reshape(step_rows, D)], 1
        )
        return (query_grad, block_grad)

    query_grad, block_grads = lax.scan(
        grad_block,
        jnp.zeros((tok_rows, HEADS, HEAD_DIM), jnp.float32),
        jnp.arange(0, group_rows, step_rows, dtype=jnp.int32),
    )
    block_grads = block_grads.reshape(group_rows, 2 * D)
    return (
        query_grad.reshape(tok_rows, D),
        low_attended,
        row_dots,
        block_grads,
        out_step,
        inner_gain_grad,
        inner_bias_grad,
    )


def attention_finish(section_in, grad_out, middle, extra, params, grad_sums):
    qkv_matrix, norm_gains, norm_biases = (params[0], params[4], params[5])
    inputs = section_in.astype(jnp.float32)
    grad_float = grad_out.astype(jnp.float32)
    hidden = norm_rows(inputs, norm_gains[0], norm_biases[0]).astype(jnp.bfloat16)
    query_grad, low_attended, row_dots, block_grads, out_step, inner_gain_grad, inner_bias_grad = (
        middle
    )
    own_grads = extra[0]
    proj_grad = jnp.concatenate([query_grad, own_grads], 1).astype(jnp.bfloat16)
    qkv_step = jnp.einsum("td,tf->df", hidden, proj_grad, preferred_element_type=jnp.float32)
    value_bias_sums = jnp.sum(proj_grad[:, 2 * D :].astype(jnp.float32), 0)
    hidden_grad = jnp.einsum("tf,df->td", proj_grad, qkv_matrix, preferred_element_type=jnp.float32)
    unused_first, first_back = jax.vjp(norm_rows, inputs, norm_gains[0], norm_biases[0])
    input_grad, first_gain_grad, first_bias_grad = first_back(hidden_grad)
    qkv_sum, out_sum, up_sum, down_sum, gain_sum, bias_sum, hgain_sum, hbias_sum = grad_sums
    gain_sum = gain_sum.at[0].add(first_gain_grad).at[1].add(inner_gain_grad)
    bias_sum = (
        bias_sum.at[0]
        .add(first_bias_grad)
        .at[1]
        .add(inner_bias_grad)
        .at[3]
        .add(value_bias_sums)
        .at[4]
        .add(jnp.sum(grad_float, 0))
    )
    return (
        grad_float + input_grad,
        (
            qkv_sum + qkv_step,
            out_sum + out_step,
            up_sum,
            down_sum,
            gain_sum,
            bias_sum,
            hgain_sum,
            hbias_sum,
        ),
    )


def feed_backward(section_in, grad_out, params, grad_sums):
    up_matrix, down_matrix, norm_gains, norm_biases, hidden_gain, hidden_bias = (
        params[2],
        params[3],
        params[4],
        params[5],
        params[6],
        params[7],
    )
    inputs = section_in.astype(jnp.float32)
    grad_float = grad_out.astype(jnp.float32)
    hidden = norm_rows(inputs, norm_gains[2], norm_biases[2]).astype(jnp.bfloat16)
    upward = jnp.dot(hidden, up_matrix, preferred_element_type=jnp.float32) + hidden_bias[0]

    def inner_rows(upward_in, gain_row, bias_row):
        return norm_rows(jax.nn.gelu(upward_in, approximate=False), gain_row, bias_row)

    inner_value, inner_back = jax.vjp(inner_rows, upward, hidden_gain, hidden_bias[1])
    inner_norm = inner_value.astype(jnp.bfloat16)
    down_step = jnp.einsum("tf,td->fd", inner_norm, grad_out, preferred_element_type=jnp.float32)
    inner_grad = jnp.einsum("td,fd->tf", grad_out, down_matrix, preferred_element_type=jnp.float32)
    upward_grad, hgain_step, hbias_step = inner_back(inner_grad)
    low_upward = upward_grad.astype(jnp.bfloat16)
    up_step = jnp.einsum("td,tf->df", hidden, low_upward, preferred_element_type=jnp.float32)
    hidden_grad = jnp.einsum("tf,df->td", low_upward, up_matrix, preferred_element_type=jnp.float32)
    unused, first_back = jax.vjp(norm_rows, inputs, norm_gains[2], norm_biases[2])
    input_grad, first_gain_grad, first_bias_grad = first_back(hidden_grad)
    qkv_sum, out_sum, up_sum, down_sum, gain_sum, bias_sum, hgain_sum, hbias_sum = grad_sums
    gain_sum = gain_sum.at[2].add(first_gain_grad)
    bias_sum = bias_sum.at[2].add(first_bias_grad).at[5].add(jnp.sum(grad_float, 0))
    hbias_sum = (
        hbias_sum.at[0].add(jnp.sum(low_upward.astype(jnp.float32), 0)).at[1].add(hbias_step)
    )
    return (
        grad_float + input_grad,
        (
            qkv_sum,
            out_sum,
            up_sum + up_step,
            down_sum + down_step,
            gain_sum,
            bias_sum,
            hgain_sum + hgain_step,
            hbias_sum,
        ),
    )


def keep_slot(store, fresh, slot_id, in_range):
    previous = lax.dynamic_index_in_dim(store, slot_id, 0, False)
    return lax.dynamic_update_index_in_dim(store, jnp.where(in_range, fresh, previous), slot_id, 0)


def body(
    embeds,
    row_lengths,
    qkv_weight,
    out_weight,
    up_weight,
    down_weight,
    model_gains,
    model_biases,
    hidden_gains,
    hidden_biases,
    cotangent,
):
    section_id = lax.axis_index("section")
    seq_index = lax.axis_index("seq")
    section_count = lax.axis_size("section")
    micro_count = embeds.shape[0]
    tok_rows = embeds.shape[1]
    group_rows = tok_rows * lax.axis_size("seq")
    layer_id = section_id // 2
    attends = section_id % 2 == 0
    bias_count = model_biases.shape[1]

    def pick_layer(stacked):
        return lax.dynamic_index_in_dim(stacked, layer_id, 0, False)

    gathered = (
        lax.all_gather(pick_layer(qkv_weight), "seq", axis=0, tiled=True),
        lax.all_gather(pick_layer(out_weight), "seq", axis=0, tiled=True),
        lax.all_gather(pick_layer(up_weight), "seq", axis=0, tiled=True),
        lax.all_gather(pick_layer(down_weight), "seq", axis=0, tiled=True),
        lax.all_gather(pick_layer(model_gains), "seq", axis=1, tiled=True),
        lax.all_gather(pick_layer(model_biases), "seq", axis=1, tiled=True),
        lax.all_gather(pick_layer(hidden_gains), "seq", axis=0, tiled=True),
        lax.all_gather(pick_layer(hidden_biases), "seq", axis=1, tiled=True),
    )
    params = tuple(gathered[:4]) + tuple((vector.astype(jnp.float32) for vector in gathered[4:]))
    whole_shape = (0,)

    def make_projected(section_in):
        return project_tokens(section_in.astype(jnp.float32), params[0], params[4], params[5])[1]

    def skip_projected(section_in):
        return jnp.zeros((tok_rows, 3 * D), jnp.bfloat16)

    def run_attention(section_in, projected, whole_keys, lengths):
        return attention_forward(section_in, projected, whole_keys, lengths, params, seq_index)

    def run_feed(section_in, projected, whole_keys, lengths):
        return feed_forward(section_in, params)

    def forward_tick(running, tick_id):
        (
            incoming,
            kept_inputs,
            kept_attended,
            kept_totals,
            kept_whole,
            outputs,
            log_sums,
            pick_sums,
        ) = running
        micro_id = tick_id - section_id
        in_range = (micro_id >= 0) & (micro_id < micro_count)
        slot_id = jnp.clip(micro_id, 0, micro_count - 1)
        lengths = lax.dynamic_index_in_dim(row_lengths, slot_id, 0, False)
        section_in = jnp.where(
            section_id == 0, lax.dynamic_index_in_dim(embeds, slot_id, 0, False), incoming
        )
        projected = lax.cond(attends, make_projected, skip_projected, section_in)
        whole_keys = lax.all_gather(projected[:, D:], "seq", axis=0, tiled=True)
        section_out, attended, totals, log_terms, pick_counts = lax.cond(
            attends, run_attention, run_feed, section_in, projected, whole_keys, lengths
        )
        kept_inputs = keep_slot(kept_inputs, section_in, slot_id, in_range)
        kept_attended = keep_slot(kept_attended, attended, slot_id, in_range)
        kept_totals = keep_slot(kept_totals, totals, slot_id, in_range)
        outputs = keep_slot(outputs, section_out, slot_id, in_range)
        log_sums = log_sums + jnp.where(in_range, log_terms, 0.0)
        pick_sums = pick_sums + jnp.where(in_range, pick_counts, 0.0)
        incoming = passed_along(section_out, "section", 1)
        return (
            (
                incoming,
                kept_inputs,
                kept_attended,
                kept_totals,
                kept_whole,
                outputs,
                log_sums,
                pick_sums,
            ),
            None,
        )

    forward_start = (
        jnp.zeros((tok_rows, D), jnp.bfloat16),
        jnp.zeros((micro_count, tok_rows, D), jnp.bfloat16),
        jnp.zeros((micro_count, tok_rows, D), jnp.float32),
        jnp.zeros((micro_count, HEADS, tok_rows), jnp.float32),
        jnp.zeros((micro_count,) + whole_shape, jnp.bfloat16),
        jnp.zeros((micro_count, tok_rows, D), jnp.bfloat16),
        jnp.zeros((len(WIDTHS),), jnp.float32),
        jnp.zeros((len(WIDTHS),), jnp.float32),
    )
    ticks = jnp.arange(micro_count + section_count - 1, dtype=jnp.int32)
    forward_end, unused = lax.scan(forward_tick, forward_start, ticks)
    unused_in, kept_inputs, kept_attended, kept_totals, kept_whole, outputs, log_sums, pick_sums = (
        forward_end
    )
    block_shape = (group_rows, 2 * D)

    def middle_attention(section_in, grad_out, attended, totals, lengths, all_keys, projected):
        return attention_middle(
            section_in, grad_out, attended, totals, lengths, all_keys, projected, params, seq_index
        )

    def middle_feed(section_in, grad_out, attended, totals, lengths, all_keys, projected):
        return (
            jnp.zeros((tok_rows, D), jnp.float32),
            jnp.zeros((tok_rows, D), jnp.bfloat16),
            jnp.zeros((HEADS, tok_rows), jnp.float32),
            jnp.zeros(block_shape, jnp.float32),
            jnp.zeros((D, D), jnp.float32),
            jnp.zeros((D,), jnp.float32),
            jnp.zeros((D,), jnp.float32),
        )

    def finish_attention(section_in, grad_out, projected, middle, extra, lengths, grad_sums):
        return attention_finish(section_in, grad_out, middle, extra, params, grad_sums)

    def finish_feed(section_in, grad_out, projected, middle, extra, lengths, grad_sums):
        return feed_backward(section_in, grad_out, params, grad_sums)

    def backward_tick(running, tick_id):
        incoming, grad_sums, input_grads = running
        micro_id = micro_count - 1 - tick_id + (section_count - 1 - section_id)
        in_range = (micro_id >= 0) & (micro_id < micro_count)
        slot_id = jnp.clip(micro_id, 0, micro_count - 1)
        from_next = jnp.where(
            section_id == section_count - 1,
            lax.dynamic_index_in_dim(cotangent, slot_id, 0, False),
            incoming,
        )
        grad_out = jnp.where(in_range, from_next, jnp.zeros_like(from_next))
        section_in = lax.dynamic_index_in_dim(kept_inputs, slot_id, 0, False)
        attended = lax.dynamic_index_in_dim(kept_attended, slot_id, 0, False)
        totals = lax.dynamic_index_in_dim(kept_totals, slot_id, 0, False)
        lengths = lax.dynamic_index_in_dim(row_lengths, slot_id, 0, False)
        projected = lax.cond(attends, make_projected, skip_projected, section_in)
        all_keys = lax.all_gather(projected[:, D:], "seq", axis=0, tiled=True)
        middle = lax.cond(
            attends,
            middle_attention,
            middle_feed,
            section_in,
            grad_out,
            attended,
            totals,
            lengths,
            all_keys,
            projected,
        )
        extra = (lax.psum_scatter(middle[3], "seq", scatter_dimension=0, tiled=True),)
        section_grad, grad_sums = lax.cond(
            attends,
            finish_attention,
            finish_feed,
            section_in,
            grad_out,
            projected,
            middle,
            extra,
            lengths,
            grad_sums,
        )
        low_grad = section_grad.astype(jnp.bfloat16)
        input_grads = keep_slot(input_grads, low_grad, slot_id, in_range)
        incoming = passed_along(low_grad, "section", -1)
        return ((incoming, grad_sums, input_grads), None)

    grad_start = (
        jnp.zeros((D, 3 * D), jnp.float32),
        jnp.zeros((D, D), jnp.float32),
        jnp.zeros((D, FF), jnp.float32),
        jnp.zeros((FF, D), jnp.float32),
        jnp.zeros((3, D), jnp.float32),
        jnp.zeros((bias_count, D), jnp.float32),
        jnp.zeros((FF,), jnp.float32),
        jnp.zeros((2, FF), jnp.float32),
    )
    backward_start = (
        jnp.zeros((tok_rows, D), jnp.bfloat16),
        grad_start,
        jnp.zeros((micro_count, tok_rows, D), jnp.bfloat16),
    )
    backward_end, unused_back = lax.scan(backward_tick, backward_start, ticks)
    unused_grad, grad_sums, input_grads = backward_end
    shards = (
        lax.psum_scatter(grad_sums[0], "seq", scatter_dimension=0, tiled=True),
        lax.psum_scatter(grad_sums[1], "seq", scatter_dimension=0, tiled=True),
        lax.psum_scatter(grad_sums[2], "seq", scatter_dimension=0, tiled=True),
        lax.psum_scatter(grad_sums[3], "seq", scatter_dimension=0, tiled=True),
        lax.psum_scatter(grad_sums[4], "seq", scatter_dimension=1, tiled=True),
        lax.psum_scatter(grad_sums[5], "seq", scatter_dimension=1, tiled=True),
        lax.psum_scatter(grad_sums[6], "seq", scatter_dimension=0, tiled=True),
        lax.psum_scatter(grad_sums[7], "seq", scatter_dimension=1, tiled=True),
    )
    sources = (
        qkv_weight,
        out_weight,
        up_weight,
        down_weight,
        model_gains,
        model_biases,
        hidden_gains,
        hidden_biases,
    )
    placed = tuple(
        (
            lax.dynamic_update_index_in_dim(
                jnp.zeros(source.shape, jnp.float32), shard, layer_id, 0
            )
            for shard, source in zip(shards, sources)
        )
    )
    summed = (
        lax.psum(placed[0].astype(jnp.bfloat16), "section").astype(jnp.float32),
        lax.psum(placed[1].astype(jnp.bfloat16), "section").astype(jnp.float32),
        lax.psum(placed[2].astype(jnp.bfloat16), "section").astype(jnp.float32),
        lax.psum(placed[3].astype(jnp.bfloat16), "section").astype(jnp.float32),
        lax.psum(placed[4].astype(jnp.bfloat16), "section").astype(jnp.float32),
        lax.psum(placed[5].astype(jnp.bfloat16), "section").astype(jnp.float32),
        lax.psum(placed[6].astype(jnp.bfloat16), "section").astype(jnp.float32),
        lax.psum(placed[7].astype(jnp.bfloat16), "section").astype(jnp.float32),
    )
    layer_count = qkv_weight.shape[0]
    layer_terms = lax.dynamic_update_index_in_dim(
        jnp.zeros((layer_count, len(WIDTHS)), jnp.float32), log_sums, layer_id, 0
    )
    layer_picks = lax.dynamic_update_index_in_dim(
        jnp.zeros((layer_count, len(WIDTHS)), jnp.float32), pick_sums, layer_id, 0
    )
    log_totals, pick_totals = lax.psum((layer_terms, layer_picks), ("section", "seq"))
    pattern_means = log_totals / pick_totals
    return (
        outputs[None],
        input_grads[None],
        summed[0],
        summed[1],
        summed[2],
        summed[3],
        summed[4],
        summed[5],
        summed[6],
        summed[7],
        pattern_means,
    )


BF16 = jnp.bfloat16
F32 = jnp.float32
PAIRS = HEADS // 2
OWNERS = (0, 2, 3, 4, 5, 6)
TOKENS = 128
PAIR_LANES = 128
QUERY_STEP = 256
VEC_ROWS = 16
KERNEL_VMEM_BYTES = 64 * 1024 * 1024 - 65536
SCALE = HEAD_DIM ** (-0.5)


def mul(left, right):
    return lax.dot_general(left, right, (((1,), (0,)), ((), ())), preferred_element_type=F32)


def mul_nt(left, right):
    return lax.dot_general(left, right, (((1,), (1,)), ((), ())), preferred_element_type=F32)


def mul_tn(left, right):
    return lax.dot_general(left, right, (((0,), (0,)), ((), ())), preferred_element_type=F32)


def standardize(values):
    center = values - jnp.mean(values, -1, keepdims=True)
    rstd = lax.rsqrt(jnp.mean(center * center, -1, keepdims=True) + EPSILON)
    return (center * rstd, rstd)


def norm_back(unit, rstd, unit_grad):
    first = jnp.mean(unit_grad, -1, keepdims=True)
    second = jnp.mean(unit_grad * unit, -1, keepdims=True)
    return rstd * (unit_grad - first - unit * second)


def remote(source, target, send_sem, recv_sem, axis, peer):
    return pltpu.make_async_remote_copy(
        src_ref=source,
        dst_ref=target,
        send_sem=send_sem,
        recv_sem=recv_sem,
        device_id={axis: peer},
        device_id_type=pl.DeviceIdType.MESH,
    )


def greet(axis, peers):
    barrier = pltpu.get_barrier_semaphore()
    for peer in peers:
        pl.semaphore_signal(
            barrier, inc=1, device_id={axis: peer}, device_id_type=pl.DeviceIdType.MESH
        )
    pl.semaphore_wait(barrier, len(peers))


def seq_peers(me, count):
    return [lax.rem(me + step, count) for step in range(1, count)]


def plane_peers(me):
    return [
        me,
        me + 1 - 2 * lax.rem(me, 2),
        lax.rem(me + 2, 4),
        3 - me,
    ]


def rows_of(block, size=TOKENS):
    return pl.ds(pl.multiple_of(block * size, size), size)


def gelu_parts(values):
    below = 0.5 * (1.0 + lax.erf(values * (0.5**0.5)))
    return (values * below, below)


def share_stats(columns, send, recv, send_sem, recv_sem, peers):
    send[...] = columns.T[0:8, :]
    recv[0] = send[...]
    copies = [
        remote(send, recv.at[k], send_sem.at[k], recv_sem.at[k], "section", peers[k])
        for k in range(1, 4)
    ]
    for copy in copies:
        copy.start()
    return copies


def two_columns(first, second):
    lane = lax.broadcasted_iota(jnp.int32, (first.shape[0], PAIR_LANES), 1)
    return jnp.where(lane == 0, first, jnp.where(lane == 1, second, 0.0))


def slot_rows(k):
    return slice(k * TOKENS, (k + 1) * TOKENS)


def shaped(shape, kind):
    return jax.ShapeDtypeStruct(shape, kind)


class Named:
    def __init__(self, groups, refs):
        names = [name for group in groups for name in group]
        for name, ref in zip(names, refs, strict=True):
            setattr(self, name, ref)


GROUP_TOKENS = 8 * TOKENS
WIDE = 4 * TOKENS
SHARD = D // 8


def square(ref):
    return ref[...].reshape(D, D)


def remote_both(source, target, send_sem, recv_sem, section, seq):
    return pltpu.make_async_remote_copy(
        src_ref=source,
        dst_ref=target,
        send_sem=send_sem,
        recv_sem=recv_sem,
        device_id=(section, seq),
        device_id_type=pl.DeviceIdType.MESH,
    )


def greet_all(barrier, section, me):
    for other in range(4):
        for j in range(8):

            @pl.when((section != other) | (me != j))
            def _():
                pl.semaphore_signal(
                    barrier, inc=1, device_id=(other, j), device_id_type=pl.DeviceIdType.MESH
                )


class Place:
    def __init__(self):
        self.me = lax.axis_index("seq")
        self.section = lax.axis_index("section")
        self.peers = plane_peers(self.section)
        self.core = lax.rem(self.me, 2)
        self.chip = lax.div(self.me, 2)
        self.high = lax.div(self.chip, 2)
        self.low = lax.rem(self.chip, 2)
        self.sibling = self.me + 1 - 2 * self.core
        self.across = 2 * (2 * (1 - self.high) + self.low) + self.core
        self.next = 2 * (2 * self.high + 1 - self.low) + self.core
        self.is_owner = (self.me != 1) & (self.me != 7)
        pair = jnp.where(self.me == 0, 0, self.me - 1)
        self.my_pair = jnp.where(pair > PAIRS - 1, PAIRS - 1, pair)


class LineGather:
    def __init__(self, place, base, far_sems, near_sems, core_sems):
        self.place = place
        self.base = base
        self.far_sems = far_sems
        self.near_sems = near_sems
        self.core_sems = core_sems

    def far(self, high):
        p = self.place
        view = self.base.at[high, p.low, p.core]
        return remote(view, view, self.far_sems[0], self.far_sems[1], "seq", p.across)

    def near(self, low):
        p = self.place
        view = self.base.at[:, low, p.core]
        return remote(view, view, self.near_sems[0], self.near_sems[1], "seq", p.next)

    def cores(self, core):
        p = self.place
        view = self.base.at[:, :, core]
        return remote(view, view, self.core_sems[0], self.core_sems[1], "seq", p.sibling)

    def start(self):
        self.far(self.place.high).start()

    def pass_line(self):
        self.far(1 - self.place.high).wait_recv()
        self.near(self.place.low).start()

    def pass_core(self):
        self.near(1 - self.place.low).wait_recv()
        self.cores(self.place.core).start()

    def ready(self):
        self.cores(1 - self.place.core).wait_recv()

    def drain(self):
        self.far(self.place.high).wait_send()
        self.near(self.place.low).wait_send()
        self.cores(self.place.core).wait_send()


BOTH_VMEM = dict(model=0, hgains=0, hbiases=0)
BOTH_ANY = dict(embeds_in=0, qkv_w=0, out_w=0, up_w=0, down_w=0, cotangent_in=0)
BOTH_OUT = dict(
    sub_f_out=((4, TOKENS, D), BF16, False),
    sub_g_out=((4, TOKENS, D), BF16, False),
    all_m_out=((6, 4, SHARD, D), BF16, False),
    all_v_out=((2, 4, SHARD, PAIR_LANES), BF16, False),
    log_total=((8, PAIR_LANES), F32, True),
)
BOTH_SCRATCH = dict(
    embeds=((4, TOKENS, D), BF16),
    att=((2, TOKENS, D), BF16),
    picks=((2, GROUP_TOKENS, PAIR_LANES), BF16),
    wa=((2, 2, 2, 2, 2, SHARD, D), BF16),
    wf=((2, 2, 2, 2, 2, SHARD, D), BF16),
    qkv=((2, 3, GROUP_TOKENS, PAIR_LANES), BF16),
    pa=((2, GROUP_TOKENS, PAIR_LANES), F32),
    pt=((2, GROUP_TOKENS, PAIR_LANES), F32),
    hid=((2, WIDE, D), BF16),
    up=((2, WIDE, D), F32),
    stat=((2, WIDE, PAIR_LANES), F32),
    left=((2, WIDE, D), BF16),
    raw_up=((2, SHARD, FF), BF16),
    small_src=((2, 32, PAIR_LANES), BF16),
    small=((8, 2, 32, PAIR_LANES), BF16),
    inner=((TOKENS, D), BF16),
    vecs=((2, VEC_ROWS, D), F32),
    logs=((8, PAIR_LANES), F32),
    proj_send=((4, PAIRS, TOKENS, PAIR_LANES), BF16),
    att_send=((GROUP_TOKENS, PAIR_LANES), BF16),
    att_recv=((2, PAIRS, TOKENS, PAIR_LANES), BF16),
    columns=((WIDE, PAIR_LANES), F32),
    stat_rows=((PAIR_LANES, WIDE), F32),
    stat_send=((8, WIDE), F32),
    first_recv=((4, TOKENS, D), BF16),
    fstat_recv=((2, 4, 8, WIDE), F32),
    xs=((4, TOKENS, D), BF16),
    last_send=((4, TOKENS, D), BF16),
    last_recv=((4, TOKENS, D), BF16),
    last=((TOKENS, D), F32),
    streams=((4, TOKENS, D), BF16),
    grads=((WIDE, D), BF16),
    units=((WIDE, D), F32),
    unit_grads=((WIDE, D), F32),
    inners=((WIDE, D), BF16),
    lows=((WIDE, D), BF16),
    part_send=((4, TOKENS, D), BF16),
    part_recv=((4, TOKENS, D), BF16),
    stat_recv=((4, 8, WIDE), F32),
    do_send=((PAIRS, TOKENS, PAIR_LANES), BF16),
    do_recv=((GROUP_TOKENS, PAIR_LANES), BF16),
    key_sum=((GROUP_TOKENS, PAIR_LANES), F32),
    value_sum=((GROUP_TOKENS, PAIR_LANES), F32),
    d_send=((3, GROUP_TOKENS, PAIR_LANES), BF16),
    d_recv=((2, 4, PAIRS, TOKENS, PAIR_LANES), BF16),
    left_src=((TOKENS, D), BF16),
    right_src=((TOKENS, D), BF16),
    right=((2, WIDE, D), BF16),
    vec_rows=((2, PAIR_LANES, D), F32),
    hidden_grad=((TOKENS, D), F32),
    prod=((3, 2, 2, 2, SHARD, D), BF16),
    prod_v=((2, 2, 2, 2, SHARD, PAIR_LANES), BF16),
    pair=((6, 2, 2, SHARD, D), BF16),
    pair_v=((2, 2, 2, SHARD, PAIR_LANES), BF16),
    near=((6, 2, SHARD, D), BF16),
    near_v=((2, 2, SHARD, PAIR_LANES), BF16),
    far=((6, SHARD, D), BF16),
    far_v=((2, SHARD, PAIR_LANES), BF16),
    done=((6, SHARD, D), BF16),
    done_v=((2, SHARD, PAIR_LANES), BF16),
    log_line=((8, 8, PAIR_LANES), F32),
    log_plane=((4, 8, PAIR_LANES), F32),
)
BOTH_SEMS = dict(
    load_sem=(2, 3),
    embeds_sem=(4,),
    small_s=(8,),
    small_r=(8,),
    az_s=(4,),
    az_r=(4,),
    line_s=(6, 3),
    line_r=(6, 3),
    axy_s=(2, 4),
    axy_r=(2, 4),
    axs_s=(2, 4),
    axs_r=(2, 4),
    inner_s=(4,),
    inner_r=(4,),
    wide_s=(2, 4, PAIRS),
    wide_r=(2, 3, 8),
    att_s=(2, 8),
    att_r=(2, PAIRS),
    fhid_s=(2, 4),
    fhid_r=(2, 4),
    fstat_s=(2, 4),
    fstat_r=(2, 4),
    fleft_s=(4,),
    fleft_r=(4,),
    first_s=(4,),
    first_r=(4,),
    g_s=(2, 4),
    g_r=(2, 4),
    stat_s=(2, 4),
    stat_r=(2, 4),
    part_s=(2, 4),
    part_r=(2, 4),
    do_s=(2, PAIRS),
    do_r=(2, 8),
    d_s=(2, 3, 8),
    d_r=(2, 4, PAIRS),
    left_s=(2, 4),
    left_r=(2, 4),
    right_s=(2, 4),
    right_r=(2, 4),
    back_s=(2, 4),
    back_r=(2, 4),
    subf_s=(4,),
    subf_r=(4,),
    subg_s=(4,),
    subg_r=(4,),
    own_sem=(2,),
    last_s=(4,),
    last_r=(4,),
    cot_sem=(4,),
    pair_s=(8,),
    pair_r=(8,),
    near_s=(8,),
    near_r=(8,),
    far_s=(8,),
    far_r=(8,),
    all_s=(8, 4),
    all_r=(8, 4),
    log_s=(8,),
    log_r=(8,),
    log_plane_s=(4,),
    log_plane_r=(4,),
    third_sem=(4,),
)


def make_picks(lengths_ref, section, my_pair, picks_ref):
    tokens = lax.broadcasted_iota(jnp.int32, (GROUP_TOKENS, PAIR_LANES), 0)
    lane = lax.broadcasted_iota(jnp.int32, (GROUP_TOKENS, PAIR_LANES), 1)
    row_id = jnp.zeros_like(tokens)
    first = jnp.zeros_like(tokens)
    end = 0
    for row in range(lengths_ref.shape[1]):
        end = end + lengths_ref[section, row]
        passed = tokens >= end
        row_id = row_id + jnp.where(passed, 1, 0)
        first = jnp.where(passed, end, first)
    pos = (tokens - first).astype(F32)
    number = lax.shift_right_logical(lane, 2)
    row = lane - 4 * number
    ratio = jnp.zeros(lane.shape, F32)
    for i, each in enumerate(RATIOS):
        ratio = jnp.where(number == i, float(each), ratio)
    valid = ratio > 0.5
    ratio = jnp.where(valid, ratio, 1.0)

    def residue(values):
        return values - ratio * jnp.floor((values + 0.5) / ratio)

    residues = residue(pos)
    for head in range(2):
        wanted = residue(jnp.full(lane.shape, 2 * my_pair + head, jnp.int32).astype(F32))
        fits = valid & (row == row_id) & (jnp.abs(residues - wanted) < 0.5)
        picks_ref[head] = jnp.where(fits, 1.0, 0.0).astype(BF16)


def both_kernel(lengths, *refs):
    b = Named([BOTH_VMEM, BOTH_ANY, BOTH_OUT, BOTH_SCRATCH, BOTH_SEMS], refs)
    p = Place()
    me, section, peers, core = (p.me, p.section, p.peers, p.core)
    chip, high, low = (p.chip, p.high, p.low)
    out_slot = jnp.where(section == 3, 0, 1)

    barrier = pltpu.get_barrier_semaphore()
    greet_all(barrier, section, me)

    def block_from_qkv(layer):
        return pltpu.make_async_copy(
            b.qkv_w.at[layer, :, pl.ds(pl.multiple_of(lax.rem(section, 3) * D, D), D)],
            b.wa.at[layer, 0, high, low, core],
            b.load_sem.at[layer, 0],
        )

    def block_from_out(layer):
        return pltpu.make_async_copy(
            b.out_w.at[layer], b.wa.at[layer, 0, high, low, core], b.load_sem.at[layer, 0]
        )

    def load_up(layer):
        return pltpu.make_async_copy(b.up_w.at[layer], b.raw_up.at[layer], b.load_sem.at[layer, 1])

    def load_down(layer):
        return pltpu.make_async_copy(
            b.down_w.at[layer, pl.ds(pl.multiple_of(section * SHARD, SHARD), SHARD)],
            b.wf.at[layer, 1, high, low, core],
            b.load_sem.at[layer, 2],
        )

    def load_embeds(k):
        return pltpu.make_async_copy(
            b.embeds_in.at[peers[k]], b.embeds.at[k], b.embeds_sem.at[k]
        )

    for layer in range(2):

        @pl.when(section != 3)
        def _():
            block_from_qkv(layer).start()

        @pl.when(section == 3)
        def _():
            block_from_out(layer).start()

        if layer == 0:
            for k in range(4):
                load_embeds(k).start()
        load_up(layer).start()
        load_down(layer).start()

    def block_loaded(layer):
        @pl.when(section != 3)
        def _():
            block_from_qkv(layer).wait()

        @pl.when(section == 3)
        def _():
            block_from_out(layer).wait()

    def pick_up(layer):
        load_up(layer).wait()
        load_down(layer).wait()
        raw = b.raw_up[layer]
        for s in range(4):

            @pl.when(section == s)
            def _():
                b.wf[layer, 0, high, low, core] = jnp.concatenate(
                    [
                        raw[:, (4 * j + s) * SHARD : (4 * j + s + 1) * SHARD].astype(F32)
                        for j in range(8)
                    ],
                    1,
                ).astype(BF16)

    def line_gather(number, base):
        pairs = [(b.line_s.at[number, i], b.line_r.at[number, i]) for i in range(3)]
        return LineGather(p, base, *pairs)

    block = [line_gather(layer, b.wa.at[layer, 0]) for layer in range(2)]
    feed_lines = [
        [line_gather(2 + 2 * layer + which, b.wf.at[layer, which]) for which in range(2)]
        for layer in range(2)
    ]

    def first_z(step, source):
        view = b.wa.at[0, 0, lax.div(source, 2), lax.rem(source, 2), core]
        return remote(
            view,
            view,
            b.az_s.at[step],
            b.az_r.at[step],
            "seq",
            2 * lax.rem(chip + step, 4) + core,
        )

    def block_plane(layer, k):
        source = b.wa.at[layer, 0, :, :, core]
        target = b.wa.at[layer, 1, :, :, core]
        return remote(source, target, b.axy_s.at[layer, k], b.axy_r.at[layer, k], "section", peers[k])

    def block_across(layer, k, side):
        view = b.wa.at[layer, 1, :, :, side]
        return remote(view, view, b.axs_s.at[layer, k], b.axs_r.at[layer, k], "seq", p.sibling)

    for layer in range(2):
        model = b.model[layer].astype(F32)
        hidden_gain = b.hgains[layer : layer + 1, :].astype(F32)
        hidden_bias = b.hbiases[layer].astype(F32)
        lines = [model]
        for each in (hidden_gain, hidden_bias[0:1, :], hidden_bias[1:2, :]):
            for s in range(4):
                lines.append(each[:, s * SHARD : (s + 1) * SHARD])
        lines.append(jnp.zeros((11, SHARD), F32))
        packed = jnp.concatenate(lines, 0)
        packed = jnp.concatenate([packed, jnp.zeros((32, PAIR_LANES - SHARD), F32)], 1)
        b.small_src[layer] = packed.astype(BF16)
    b.small[me] = b.small_src[...]
    make_picks(lengths, section, p.my_pair, b.picks)
    b.logs[...] = jnp.zeros_like(b.logs)
    block_loaded(0)
    pl.semaphore_wait(barrier, 31)

    def small_copy(step):
        return remote(
            b.small_src,
            b.small.at[me],
            b.small_s.at[step],
            b.small_r.at[step],
            "seq",
            lax.rem(me + step, 8),
        )

    for step in range(1, 8):
        small_copy(step).start()
    for step in range(1, 4):
        first_z(step, chip).start()
    pick_up(0)
    for step in range(1, 8):
        source = lax.rem(me + 8 - step, 8)
        remote(
            b.small_src,
            b.small.at[source],
            b.small_s.at[step],
            b.small_r.at[step],
            "seq",
            source,
        ).wait_recv()
    for layer in range(2):
        pieces = []
        for j in range(8):
            small = b.small[j, layer].astype(F32)
            lines = [small[0:9]]
            for third in range(3):
                line = jnp.zeros((1, PAIR_LANES), F32)
                for s in range(4):
                    at = 9 + 4 * third + s
                    line = line + jnp.where(section == s, small[at : at + 1], 0.0)
                lines.append(line)
            lines.append(jnp.zeros((4, PAIR_LANES), F32))
            pieces.append(jnp.concatenate(lines, 0)[:, 0:SHARD])
        b.vecs[layer] = jnp.concatenate(pieces, 1)

    def owner_of(pair):
        return jnp.where(pair == 0, 0, pair + 1)

    def wide_turned(layer, k, step):
        pair = lax.rem(me + step, PAIRS)
        return (
            remote_both(
                b.proj_send.at[k, pair],
                b.qkv.at[layer, lax.rem(section, 3), rows_of(me)],
                b.wide_s.at[layer, k, pair],
                b.wide_r.at[layer, lax.rem(section, 3), me],
                peers[k],
                owner_of(pair),
            ),
            owner_of(pair),
        )

    def wide_copy(layer, k, pair):
        return remote_both(
            b.proj_send.at[k, pair],
            b.qkv.at[layer, lax.rem(section, 3), rows_of(me)],
            b.wide_s.at[layer, k, pair],
            b.wide_r.at[layer, lax.rem(section, 3), me],
            peers[k],
            OWNERS[pair],
        )

    def project(layer, arrive):
        vec = b.vecs.at[layer]

        @pl.when(section != 3)
        def _():
            bias = jnp.where(section == 2, vec[6:7, :], 0.0)
            for k in (3, 1, 2, 0) if layer == 0 else (0, 1, 2, 3):
                if k > 0:
                    arrive(k)
                part = mul(b.left[layer, slot_rows(k), :], square(b.wa.at[layer, 0])) + bias
                part = part.astype(BF16)
                for pair in range(PAIRS):
                    b.proj_send[k, pair] = part[:, pair * PAIR_LANES : (pair + 1) * PAIR_LANES]
                for step in range(PAIRS):
                    if k > 0:
                        wide_turned(layer, k, step)[0].start()
                    else:
                        owner = wide_turned(layer, k, step)[1]

                        @pl.when(me != owner)
                        def _():
                            wide_turned(layer, k, step)[0].start()

                if k == 0:

                    @pl.when(p.is_owner)
                    def _():
                        b.qkv[layer, section, rows_of(me), :] = b.proj_send[0, p.my_pair]

    def wait_projected(layer):
        @pl.when(p.is_owner)
        def _():
            for third in range(3):
                for source in range(8):

                    @pl.when((section != third) | (me != source))
                    def _():
                        remote_both(
                            b.proj_send.at[0, 0],
                            b.qkv.at[layer, third, pl.ds(source * TOKENS, TOKENS)],
                            b.wide_s.at[layer, 0, 0],
                            b.wide_r.at[layer, third, source],
                            third,
                            source,
                        ).wait_recv()

        @pl.when(section != 3)
        def _():
            for k in range(4):
                for pair, owner in enumerate(OWNERS):
                    if k > 0:
                        wide_copy(layer, k, pair).wait_send()
                    else:

                        @pl.when(me != owner)
                        def _():
                            wide_copy(layer, k, pair).wait_send()

    def back_copy(layer, target):
        return remote(
            b.att_send.at[pl.ds(target * TOKENS, TOKENS)],
            b.att_recv.at[layer, p.my_pair],
            b.att_s.at[layer, target],
            b.att_r.at[layer, p.my_pair],
            "seq",
            target,
        )

    def attend(layer):
        lane = lax.broadcasted_iota(jnp.int32, (QUERY_STEP, PAIR_LANES), 1)
        first_half = lane < HEAD_DIM
        for step in range(GROUP_TOKENS // QUERY_STEP):
            start = step * QUERY_STEP
            keys_end = start + QUERY_STEP
            rows = slice(start, keys_end)
            query = b.qkv[layer, 0, rows, :] * jnp.asarray(SCALE, BF16)
            keys = b.qkv[layer, 1, 0:keys_end, :]
            values = b.qkv[layer, 2, 0:keys_end, :]
            causal = lax.broadcasted_iota(jnp.int32, (QUERY_STEP, keys_end), 1) <= (
                start + lax.broadcasted_iota(jnp.int32, (QUERY_STEP, keys_end), 0)
            )
            sums = []
            totals = []
            logs = jnp.zeros((1, PAIR_LANES), F32)
            picked_sum = jnp.zeros((1, PAIR_LANES), F32)
            for head in range(2):
                mine = first_half if head == 0 else ~first_half
                own_query = jnp.where(mine, query, jnp.zeros_like(query))
                scores = mul_nt(own_query, keys)
                raised = jnp.where(causal, jnp.exp(scores), 0.0)
                pick_query = b.picks[head, rows, :]
                pick_keys = b.picks[head, 0:keys_end, :]
                counts = mul_nt(pick_query, pick_keys)
                weighted = (raised * counts).astype(BF16)
                sums.append(mul(weighted, values))
                pattern = mul(raised.astype(BF16), pick_keys)
                picked = pick_query.astype(F32)
                totals.append(jnp.sum(pattern * picked, -1, keepdims=True))
                chosen = picked > 0.5
                logs = logs + jnp.sum(
                    jnp.where(chosen, jnp.log(jnp.where(chosen, pattern, 1.0)), 0.0),
                    0,
                    keepdims=True,
                )
                picked_sum = picked_sum + jnp.sum(picked, 0, keepdims=True)
            b.logs[layer : layer + 1, :] += logs
            if layer == 0:
                b.logs[2:3, :] += picked_sum
            total = jnp.where(first_half, totals[0], totals[1])
            attended = jnp.where(first_half, sums[0], sums[1]) / total
            b.pa[layer, rows, :] = attended
            b.pt[layer, rows, :] = total
            b.att_send[rows, :] = attended.astype(BF16)
            for target in (2 * step, 2 * step + 1):

                @pl.when(me != target)
                def _():
                    back_copy(layer, target).start()

                @pl.when(me == target)
                def _():
                    b.att_recv[layer, p.my_pair] = b.att_send[
                        target * TOKENS : (target + 1) * TOKENS, :
                    ]

    def attention_rest(layer, inputs_ref, after):
        vec = b.vecs.at[layer]
        wait_projected(layer)
        feed_lines[layer][0].start()
        after()

        @pl.when(p.is_owner)
        def _():
            attend(layer)

        feed_lines[layer][0].pass_line()
        for k in range(1, 4):

            @pl.when(peers[k] == 3)
            def _():
                block_plane(layer, k).wait_recv()
                block_across(layer, k, core).start()

        for pair, owner in enumerate(OWNERS):

            @pl.when(me != owner)
            def _():
                remote(
                    b.att_send.at[pl.ds(0, TOKENS)],
                    b.att_recv.at[layer, pair],
                    b.att_s.at[layer, 0],
                    b.att_r.at[layer, pair],
                    "seq",
                    owner,
                ).wait_recv()

            b.att[layer, :, pair * PAIR_LANES : (pair + 1) * PAIR_LANES] = b.att_recv[layer, pair]
        inner_unit, unused = standardize(b.att[layer].astype(F32))
        inner = (inner_unit * vec[1:2, :] + vec[4:5, :]).astype(BF16)
        if layer == 0:
            b.inner[...] = inner
        for k in range(1, 4):

            @pl.when(peers[k] == 3)
            def _():
                block_across(layer, k, 1 - core).wait_recv()

        branch = mul(inner, square(b.wa.at[layer, out_slot])) + vec[7:8, :]
        b.xs[2 * layer] = (inputs_ref[...].astype(F32) + branch).astype(BF16)

    def attention_drain(layer):
        @pl.when(p.is_owner)
        def _():
            for target in range(8):

                @pl.when(me != target)
                def _():
                    back_copy(layer, target).wait_send()

    def feed(layer, resting, parting):
        vec = b.vecs.at[layer]
        inputs = b.xs[2 * layer].astype(F32)
        unit, unused = standardize(inputs)
        b.hid[layer, slot_rows(0), :] = (unit * vec[2:3, :] + vec[5:6, :]).astype(BF16)
        hidden_copies = [
            remote(
                b.hid.at[layer, pl.ds(0, TOKENS)],
                b.hid.at[layer, pl.ds(k * TOKENS, TOKENS)],
                b.fhid_s.at[layer, k],
                b.fhid_r.at[layer, k],
                "section",
                peers[k],
            )
            for k in range(1, 4)
        ]
        for copy in hidden_copies:
            copy.start()
        up_line, down_line = feed_lines[layer]
        down_line.start()
        up_line.pass_core()
        down_line.pass_line()
        up_line.ready()
        for k in range(4):
            if k > 0:
                hidden_copies[k - 1].wait_recv()
            upward = mul(b.hid[layer, slot_rows(k), :], square(b.wf.at[layer, 0])) + vec[10:11, :]
            b.up[layer, slot_rows(k), :] = upward
            values, unused = gelu_parts(upward)
            b.units[slot_rows(k), :] = values
            mean = jnp.mean(values, -1, keepdims=True)
            center = values - mean
            b.columns[slot_rows(k), :] = two_columns(
                mean, jnp.sum(center * center, -1, keepdims=True)
            )
        stat_copies = share_stats(
            b.columns[...],
            b.stat_send,
            b.fstat_recv.at[layer],
            b.fstat_s.at[layer],
            b.fstat_r.at[layer],
            peers,
        )
        down_line.pass_core()
        resting()
        for copy in stat_copies:
            copy.wait_recv()
        b.stat_rows[...] = jnp.zeros((PAIR_LANES, WIDE), F32)
        for k in range(4):
            means = [b.fstat_recv[layer, other, 0:1, slot_rows(k ^ other)] for other in range(4)]
            squares = [b.fstat_recv[layer, other, 1:2, slot_rows(k ^ other)] for other in range(4)]
            mean = (means[0] + means[1] + means[2] + means[3]) * 0.25
            spread = squares[0] + squares[1] + squares[2] + squares[3]
            for each in means:
                spread = spread + D * (each - mean) * (each - mean)
            b.stat_rows[0:1, slot_rows(k)] = mean
            b.stat_rows[1:2, slot_rows(k)] = lax.rsqrt(spread * (1.0 / FF) + EPSILON)
        b.stat[layer] = b.stat_rows[...].T
        down_line.ready()
        if layer == 1:
            parting()
            for copy in hidden_copies + stat_copies:
                copy.wait_send()
            return
        branch = None
        part_copies = []
        for k in (3, 1, 2, 0):
            both = b.stat[layer, slot_rows(k), :]
            inner = (
                (b.units[slot_rows(k), :] - both[:, 0:1]) * both[:, 1:2] * vec[9:10, :]
                + vec[11:12, :]
            ).astype(BF16)
            part = mul(inner, square(b.wf.at[layer, 1]))
            if k == 0:
                branch = part
            else:
                b.part_send[k] = part.astype(BF16)
                part_copies.append(
                    remote(
                        b.part_send.at[k],
                        b.first_recv.at[k],
                        b.first_s.at[k],
                        b.first_r.at[k],
                        "section",
                        peers[k],
                    )
                )
                part_copies[-1].start()
        parting()
        for k, copy in zip((3, 1, 2), part_copies):
            copy.wait_recv()
            branch = branch + b.first_recv[k].astype(F32)
        b.xs[2 * layer + 1] = (inputs + branch + vec[8:9, :]).astype(BF16)
        for copy in hidden_copies + stat_copies + part_copies:
            copy.wait_send()

    def sub_copies(number, forward):
        source = b.xs if forward else b.streams
        target = b.sub_f_out if forward else b.sub_g_out
        send_sem = b.subf_s if forward else b.subg_s
        recv_sem = b.subf_r if forward else b.subg_r

        def away():
            return remote(
                source.at[number],
                target.at[section],
                send_sem.at[number],
                recv_sem.at[section],
                "section",
                number,
            )

        def own():
            return pltpu.make_async_copy(
                source.at[number], target.at[section], b.own_sem.at[0 if forward else 1]
            )

        return away, own

    def send_sub(number, forward):
        @pl.when(section != number)
        def _():
            sub_copies(number, forward)[0]().start()

        @pl.when(section == number)
        def _():
            sub_copies(number, forward)[1]().start()

    def drain_sub(number, forward):
        @pl.when(section != number)
        def _():
            sub_copies(number, forward)[0]().wait_send()

        @pl.when(section == number)
        def _():
            sub_copies(number, forward)[1]().wait()

    def receive_sub(source, forward):
        target = b.sub_f_out if forward else b.sub_g_out

        @pl.when(section != source)
        def _():
            remote(
                b.streams.at[0],
                target.at[source],
                (b.subf_s if forward else b.subg_s).at[0],
                (b.subf_r if forward else b.subg_r).at[source],
                "section",
                source,
            ).wait_recv()

    for k in range(4):
        load_embeds(k).wait()

        @pl.when(section != 3)
        def _():
            unit, unused = standardize(b.embeds[k].astype(F32))
            b.left[0, slot_rows(k), :] = (
                unit * b.vecs[0, 0:1, :] + b.vecs[0, 3:4, :]
            ).astype(BF16)
    pick_up(1)
    for step in range(1, 4):
        first_z(step, lax.rem(chip + 4 - step, 4)).wait_recv()
    block[0].cores(core).start()

    @pl.when(section == 3)
    def _():
        for k in range(1, 4):
            block_plane(0, k).start()

    block[0].ready()
    project(0, lambda k: None)

    attention_rest(0, b.embeds.at[0], lambda: None)

    def resting_first():
        block_loaded(1)
        block[1].start()

    def parting_first():
        attention_drain(0)
        block[1].pass_line()

    feed(0, resting_first, parting_first)

    second = b.vecs.at[1]
    unit, unused = standardize(b.xs[1].astype(F32))
    b.left[1, slot_rows(0), :] = (unit * second[0:1, :] + second[3:4, :]).astype(BF16)

    def left_copy(k):
        return remote(
            b.left.at[1, pl.ds(0, TOKENS)],
            b.left.at[1, pl.ds(k * TOKENS, TOKENS)],
            b.fleft_s.at[k],
            b.fleft_r.at[k],
            "section",
            peers[k],
        )

    for k in (3, 1, 2):

        @pl.when(peers[k] != 3)
        def _():
            left_copy(k).start()

    block[1].pass_core()
    for k in range(1, 4):

        @pl.when(peers[k] != 3)
        def _():
            left_copy(k).wait_send()

    @pl.when(section == 3)
    def _():
        for k in range(1, 4):
            block_plane(1, k).start()

    block[1].ready()
    project(1, lambda k: left_copy(k).wait_recv())

    def inner_copy(k):
        return remote(
            b.inner,
            b.left.at[0, pl.ds(k * TOKENS, TOKENS)],
            b.inner_s.at[k],
            b.inner_r.at[k],
            "section",
            peers[k],
        )

    def after_second():
        for k in range(1, 4):

            @pl.when(peers[k] == 3)
            def _():
                inner_copy(k).start()

        @pl.when(section == 3)
        def _():
            b.left[0, slot_rows(0), :] = b.inner[...]

        send_sub(0, True)
        send_sub(1, True)

    attention_rest(1, b.xs.at[1], after_second)

    def resting_second():
        send_sub(2, True)
        for k in range(1, 4):

            @pl.when(peers[k] == 3)
            def _():
                inner_copy(k).wait_send()

        @pl.when(section == 3)
        def _():
            for k in range(1, 4):
                inner_copy(k).wait_recv()

    def parting_second():
        attention_drain(1)

    feed(1, resting_second, parting_second)

    def cotangent_load(k):
        return pltpu.make_async_copy(
            b.cotangent_in.at[peers[k]], b.grads.at[pl.ds(k * TOKENS, TOKENS)], b.cot_sem.at[k]
        )

    for k in range(4):
        cotangent_load(k).start()

    def log_copy(step):
        return remote(
            b.logs,
            b.log_line.at[me],
            b.log_s.at[step],
            b.log_r.at[step],
            "seq",
            lax.rem(me + step, 8),
        )

    def log_plane_copy(k, slot):
        return remote(
            b.log_plane.at[slot],
            b.log_plane.at[slot],
            b.log_plane_s.at[k],
            b.log_plane_r.at[k],
            "section",
            peers[k],
        )

    def start_logs():
        b.log_line[me] = b.logs[...]
        for step in range(1, 8):
            log_copy(step).start()

    def sum_logs():
        for step in range(1, 8):
            source = lax.rem(me + 8 - step, 8)
            remote(
                b.logs,
                b.log_line.at[source],
                b.log_s.at[step],
                b.log_r.at[step],
                "seq",
                source,
            ).wait_recv()
        total = b.log_line[0]
        for j in range(1, 8):
            total = total + b.log_line[j]
        b.log_plane[section] = total
        for k in range(1, 4):
            log_plane_copy(k, section).start()

    def finish_logs():
        for k in range(1, 4):
            log_plane_copy(k, peers[k]).wait_recv()
        total = b.log_plane[0]
        for other in range(1, 4):
            total = total + b.log_plane[other]
        b.log_total[...] = total
        for step in range(1, 8):
            log_copy(step).wait_send()
        for k in range(1, 4):
            log_plane_copy(k, section).wait_send()

    class Matrix:
        def __init__(self, number):
            self.number = number
            self.direct = number > 4
            self.turn = (1, 2) if number % 2 else (2, 1)
            self.j = number % 3 if number < 6 else number - 6
            if number < 6:
                self.i = number
                refs = (b.prod, b.pair, b.near, b.far, b.done, b.all_m_out)
            else:
                self.i = number - 6
                refs = (b.prod_v, b.pair_v, b.near_v, b.far_v, b.done_v, b.all_v_out)
            self.prod, self.pair, self.near, self.far, self.done, self.all = refs

        def store(self, value):
            if 3 <= self.number < 6:
                matrices[self.number - 3].sent()
            for j in range(8):
                self.prod[self.j, j % 2, j // 4, j // 2 % 2] = value[
                    j * SHARD : (j + 1) * SHARD, :
                ].astype(BF16)

        def pair_copy(self):
            n = self.number
            return remote(
                self.prod.at[self.j, 1 - core],
                self.pair.at[self.i],
                b.pair_s.at[n],
                b.pair_r.at[n],
                "seq",
                p.sibling,
            )

        def near_copy(self):
            n = self.number
            return remote(
                self.prod.at[self.j, core, :, 1 - low],
                self.near.at[self.i],
                b.near_s.at[n],
                b.near_r.at[n],
                "seq",
                p.next,
            )

        def far_copy(self):
            n = self.number
            return remote(
                self.prod.at[self.j, core, 1 - high, low],
                self.far.at[self.i],
                b.far_s.at[n],
                b.far_r.at[n],
                "seq",
                p.across,
            )

        def all_copy(self, k, slot):
            n = self.number
            return remote(
                self.done.at[self.i],
                self.all.at[self.i, slot],
                b.all_s.at[n, k],
                b.all_r.at[n, k],
                "section",
                peers[k],
            )

        def own_copy(self):
            return pltpu.make_async_copy(
                self.done.at[self.i], self.all.at[self.i, section], b.all_s.at[self.number, 0]
            )

        def step_near(self):
            self.pair_copy().wait_recv()
            i, at = (self.i, self.j)
            for h in range(2):
                for l in range(2):
                    self.prod[at, core, h, l] = (
                        self.prod[at, core, h, l].astype(F32) + self.pair[i, h, l].astype(F32)
                    ).astype(BF16)
            self.near_copy().start()

        def step_far(self):
            self.near_copy().wait_recv()
            i, at = (self.i, self.j)
            for h in range(2):
                self.prod[at, core, h, low] = (
                    self.prod[at, core, h, low].astype(F32) + self.near[i, h].astype(F32)
                ).astype(BF16)
            self.far_copy().start()

        def step_plane(self):
            self.far_copy().wait_recv()
            i = self.i
            self.done[i] = (
                self.prod[self.j, core, high, low].astype(F32) + self.far[i].astype(F32)
            ).astype(BF16)
            for k in (3, 1, 2) if self.direct else (1, 2):
                self.all_copy(k, section).start()
            self.own_copy().start()

        def turn_copy(self):
            n = self.number
            first, second = self.turn
            view = self.all.at[self.i, peers[first]]
            return remote(
                view, view, b.all_s.at[n, 3], b.all_r.at[n, 3], "section", peers[second]
            )

        def step_pass(self):
            first = self.turn[0]
            self.all_copy(first, peers[first]).wait_recv()
            self.turn_copy().start()

        def step_end(self):
            for k in range(1, 4):
                if self.direct or k != self.turn[0]:
                    self.all_copy(k, peers[k]).wait_recv()
                if self.direct or k != 3:
                    self.all_copy(k, section).wait_send()
                else:
                    self.turn_copy().wait_send()
            self.own_copy().wait()
            if self.number > 2:
                self.sent()

        def sent(self):
            self.pair_copy().wait_send()
            self.near_copy().wait_send()
            self.far_copy().wait_send()

    matrices = [Matrix(number) for number in range(8)]
    up1, down1, att1, up0, down0, att0, vec1, vec0 = matrices

    def last_copy(k):
        return remote(
            b.last_send.at[k],
            b.last_recv.at[k],
            b.last_s.at[k],
            b.last_r.at[k],
            "section",
            peers[k],
        )

    def start_last():
        for k in (3, 1, 2, 0):
            part = mul(b.inners[slot_rows(k), :], square(b.wf.at[1, 1]))
            if k == 0:
                b.last[...] = part
            else:
                b.last_send[k] = part.astype(BF16)
                last_copy(k).start()

    def finish_last():
        total = b.xs[2].astype(F32) + b.last[...] + b.vecs[1, 8:9, :]
        for k in range(1, 4):
            last_copy(k).wait_recv()
            total = total + b.last_recv[k].astype(F32)
        b.xs[3] = total.astype(BF16)
        for k in range(1, 4):
            last_copy(k).wait_send()

    def feed_phase(layer, grad_ref, x_ref, hooks):
        phase = 1 - layer
        vec = b.vecs.at[layer]
        rows = b.vec_rows.at[layer]
        up_matrix = matrices[3 * phase]
        down_matrix = matrices[3 * phase + 1]
        early, middle, parting, late = hooks
        if layer == 0:
            b.grads[slot_rows(0), :] = grad_ref[...]
        grad_copies = [] if layer == 1 else [
            remote(
                b.grads.at[pl.ds(0, TOKENS)],
                b.grads.at[pl.ds(k * TOKENS, TOKENS)],
                b.g_s.at[phase, k],
                b.g_r.at[phase, k],
                "section",
                peers[k],
            )
            for k in range(1, 4)
        ]
        if layer == 0:
            for k in (3, 1, 2):
                grad_copies[k - 1].start()
        rows[...] = jnp.zeros((PAIR_LANES, D), F32)
        early()
        for k in range(4):
            both = b.stat[layer, slot_rows(k), :]
            upward = b.up[layer, slot_rows(k), :]
            values, below = gelu_parts(upward)
            b.up[layer, slot_rows(k), :] = below + upward * (
                jnp.exp(-0.5 * upward * upward) * (0.5 / 3.141592653589793) ** 0.5
            )
            unit = (values - both[:, 0:1]) * both[:, 1:2]
            b.units[slot_rows(k), :] = unit
            b.inners[slot_rows(k), :] = (unit * vec[9:10, :] + vec[11:12, :]).astype(BF16)
        gain_sum = jnp.zeros((1, D), F32)
        bias_sum = jnp.zeros((1, D), F32)
        for k in range(4):
            if layer == 1:
                cotangent_load(k).wait()
            elif k > 0:
                if k == 3:
                    att1.step_far()
                    vec1.step_near()
                grad_copies[k - 1].wait_recv()
            unit = b.units[slot_rows(k), :]
            inner_grad = mul_nt(b.grads[slot_rows(k), :], square(b.wf.at[layer, 1]))
            gain_sum = gain_sum + jnp.sum(inner_grad * unit, 0, keepdims=True)
            bias_sum = bias_sum + jnp.sum(inner_grad, 0, keepdims=True)
            unit_grad = inner_grad * vec[9:10, :]
            b.unit_grads[slot_rows(k), :] = unit_grad
            b.columns[slot_rows(k), :] = two_columns(
                jnp.sum(unit_grad, -1, keepdims=True), jnp.sum(unit_grad * unit, -1, keepdims=True)
            )
        stat_copies = share_stats(
            b.columns[...],
            b.stat_send,
            b.stat_recv,
            b.stat_s.at[phase],
            b.stat_r.at[phase],
            peers,
        )
        rows[9:10, :] = gain_sum
        rows[11:12, :] = bias_sum
        down_matrix.store(mul_tn(b.inners[...], b.grads[...]))
        down_matrix.pair_copy().start()
        middle()
        for copy in stat_copies:
            copy.wait_recv()
        b.stat_rows[...] = jnp.zeros((PAIR_LANES, WIDE), F32)
        for k in range(4):
            for line in range(2):
                parts = [
                    b.stat_recv[other, line : line + 1, slot_rows(k ^ other)]
                    for other in range(4)
                ]
                b.stat_rows[line : line + 1, slot_rows(k)] = (
                    parts[0] + parts[1] + parts[2] + parts[3]
                ) * (1.0 / FF)
        b.columns[...] = b.stat_rows[...].T
        hidden_grad = None
        low_sum = jnp.zeros((1, D), F32)
        part_copies = []
        for k in (3, 1, 2, 0):
            rstd = b.stat[layer, slot_rows(k), :][:, 1:2]
            both = b.columns[slot_rows(k), :]
            lowered = (
                rstd
                * (
                    b.unit_grads[slot_rows(k), :]
                    - both[:, 0:1]
                    - b.units[slot_rows(k), :] * both[:, 1:2]
                )
                * b.up[layer, slot_rows(k), :]
            ).astype(BF16)
            b.lows[slot_rows(k), :] = lowered
            low_sum = low_sum + jnp.sum(lowered.astype(F32), 0, keepdims=True)
            part = mul_nt(lowered, square(b.wf.at[layer, 0]))
            if k == 0:
                hidden_grad = part
            else:
                b.part_send[k] = part.astype(BF16)
                part_copies.append(
                    remote(
                        b.part_send.at[k],
                        b.part_recv.at[k],
                        b.part_s.at[phase, k],
                        b.part_r.at[phase, k],
                        "section",
                        peers[k],
                    )
                )
                part_copies[-1].start()
        rows[10:11, :] = low_sum
        up_matrix.store(mul_tn(b.hid[layer], b.lows[...]))
        up_matrix.pair_copy().start()
        unit, rstd = standardize(x_ref[...].astype(F32))
        parting()
        for k, copy in zip((3, 1, 2), part_copies):
            copy.wait_recv()
            hidden_grad = hidden_grad + b.part_recv[k].astype(F32)
        grad = grad_ref[...].astype(F32)
        number = 2 * layer + 1
        b.streams[number] = (
            grad + norm_back(unit, rstd, hidden_grad * vec[2:3, :])
        ).astype(BF16)
        rows[2:3, :] = jnp.sum(hidden_grad * unit, 0, keepdims=True)
        rows[5:6, :] = jnp.sum(hidden_grad, 0, keepdims=True)
        rows[8:9, :] = jnp.sum(grad, 0, keepdims=True)
        for copy in grad_copies + stat_copies + part_copies:
            copy.wait_send()
        late()

    def attention_phase(layer, grad_ref, x_ref, att_ref, hooks):
        phase = 1 - layer
        vec = b.vecs.at[layer]
        rows = b.vec_rows.at[layer]
        before, inside, after, during = hooks
        grad = grad_ref[...]
        inner_unit, inner_rstd = standardize(att_ref[...].astype(F32))
        inner_grad = mul_nt(grad, square(b.wa.at[layer, out_slot]))
        att_grad = norm_back(inner_unit, inner_rstd, inner_grad * vec[1:2, :]).astype(BF16)
        for pair in range(PAIRS):
            b.do_send[pair] = att_grad[:, pair * PAIR_LANES : (pair + 1) * PAIR_LANES]

        def out_copy(pair):
            return remote(
                b.do_send.at[pair],
                b.do_recv.at[rows_of(me)],
                b.do_s.at[phase, pair],
                b.do_r.at[phase, me],
                "seq",
                OWNERS[pair],
            )

        for pair, owner in enumerate(OWNERS):

            @pl.when(me != owner)
            def _():
                out_copy(pair).start()

            @pl.when(me == owner)
            def _():
                b.do_recv[rows_of(me), :] = b.do_send[pair]

        def left_copy(k):
            return remote(
                b.left_src,
                b.left.at[layer, pl.ds(k * TOKENS, TOKENS)],
                b.left_s.at[phase, k],
                b.left_r.at[phase, k],
                "section",
                peers[k],
            )

        def right_copy(k):
            return remote(
                b.right_src,
                b.right.at[layer, pl.ds(k * TOKENS, TOKENS)],
                b.right_s.at[phase, k],
                b.right_r.at[phase, k],
                "section",
                peers[k],
            )

        unit, rstd = standardize(x_ref[...].astype(F32))
        b.left_src[...] = (inner_unit * vec[1:2, :] + vec[4:5, :]).astype(BF16)
        b.right_src[...] = grad
        for k in range(1, 4):

            @pl.when(peers[k] == 3)
            def _():
                right_copy(k).start()
                if layer == 1:
                    left_copy(k).start()

        if layer == 1:

            @pl.when(section == 3)
            def _():
                b.left[layer, slot_rows(0), :] = b.left_src[...]

        rows[1:2, :] = jnp.sum(inner_grad * inner_unit, 0, keepdims=True)
        rows[4:5, :] = jnp.sum(inner_grad, 0, keepdims=True)
        rows[7:8, :] = jnp.sum(grad.astype(F32), 0, keepdims=True)

        def back_copy(third, target):
            return remote_both(
                b.d_send.at[third, pl.ds(target * TOKENS, TOKENS)],
                b.d_recv.at[layer, section, p.my_pair],
                b.d_s.at[phase, third, target],
                b.d_r.at[phase, section, p.my_pair],
                third,
                target,
            )

        @pl.when(p.is_owner)
        def _():
            for source in range(8):

                @pl.when(me != source)
                def _():
                    remote(
                        b.do_send.at[0],
                        b.do_recv.at[pl.ds(source * TOKENS, TOKENS)],
                        b.do_s.at[phase, 0],
                        b.do_r.at[phase, source],
                        "seq",
                        source,
                    ).wait_recv()

        before()

        @pl.when(p.is_owner)
        def _():
            b.key_sum[...] = jnp.zeros((GROUP_TOKENS, PAIR_LANES), F32)
            b.value_sum[...] = jnp.zeros((GROUP_TOKENS, PAIR_LANES), F32)
            lane = lax.broadcasted_iota(jnp.int32, (QUERY_STEP, PAIR_LANES), 1)
            first_half = lane < HEAD_DIM
            last_step = GROUP_TOKENS // QUERY_STEP - 1
            for step in (0,) + tuple(range(last_step, 0, -1)):
                start = step * QUERY_STEP
                keys_end = start + QUERY_STEP
                block = slice(start, keys_end)
                plain_query = b.qkv[layer, 0, block, :]
                query = plain_query * jnp.asarray(SCALE, BF16)
                keys = b.qkv[layer, 1, 0:keys_end, :]
                values = b.qkv[layer, 2, 0:keys_end, :]
                causal = lax.broadcasted_iota(jnp.int32, (QUERY_STEP, keys_end), 1) <= (
                    start + lax.broadcasted_iota(jnp.int32, (QUERY_STEP, keys_end), 0)
                )
                head_grad = b.do_recv[block, :]
                inverse = 1.0 / b.pt[layer, block, :]
                head_float = head_grad.astype(F32)
                products = head_float * b.pa[layer, block, :]
                scaled = (head_float * inverse).astype(BF16)
                key_lanes = lax.broadcasted_iota(jnp.int32, (keys_end, PAIR_LANES), 1) < HEAD_DIM
                query_parts = []
                key_parts = []
                value_parts = []
                for head in range(2):
                    mine = first_half if head == 0 else ~first_half
                    own_query = jnp.where(mine, query, jnp.zeros_like(query))
                    own_grad = jnp.where(mine, head_grad, jnp.zeros_like(head_grad))
                    delta = jnp.sum(jnp.where(mine, products, 0.0), -1, keepdims=True)
                    own_inverse = jnp.max(jnp.where(mine, inverse, 0.0), -1, keepdims=True)
                    counts = mul_nt(b.picks[head, block, :], b.picks[head, 0:keys_end, :])
                    scores = mul_nt(own_query, keys)
                    weighted = jnp.where(causal, jnp.exp(scores) * counts, 0.0)
                    prob_grad = mul_nt(own_grad, values)
                    score_grad = (weighted * own_inverse * (prob_grad - delta)).astype(BF16)
                    query_parts.append(mul(score_grad, keys))
                    key_parts.append(mul_tn(score_grad, plain_query))
                    value_parts.append(mul_tn(weighted.astype(BF16), scaled))
                b.key_sum[0:keys_end, :] += jnp.where(key_lanes, key_parts[0], key_parts[1])
                b.value_sum[0:keys_end, :] += jnp.where(key_lanes, value_parts[0], value_parts[1])
                query_grad = jnp.where(first_half, query_parts[0], query_parts[1]) * SCALE
                b.d_send[0, block, :] = query_grad.astype(BF16)
                ready = [(0, step)]
                if step > 0:
                    ready = [(0, step), (1, step), (2, step)]
                if step == 1:
                    ready = [(1, 0), (2, 0)] + ready
                for third, part in ready:
                    part_rows = slice(part * QUERY_STEP, (part + 1) * QUERY_STEP)
                    if third == 1:
                        b.d_send[1, part_rows, :] = (b.key_sum[part_rows, :] * SCALE).astype(BF16)
                    if third == 2:
                        b.d_send[2, part_rows, :] = b.value_sum[part_rows, :].astype(BF16)
                    for target in (2 * part, 2 * part + 1):
                        away = (section != third) | (me != target)

                        @pl.when(away)
                        def _():
                            back_copy(third, target).start()

                        @pl.when(~away)
                        def _():
                            b.d_recv[layer, section, p.my_pair] = b.d_send[
                                third, target * TOKENS : (target + 1) * TOKENS, :
                            ]

        inside()
        after()

        def part_copy(k):
            return remote(
                b.part_send.at[k],
                b.part_recv.at[k],
                b.back_s.at[phase, k],
                b.back_r.at[phase, k],
                "section",
                peers[k],
            )

        @pl.when(section != 3)
        def _():
            for k in (3, 2, 1, 0):
                for pair, owner in enumerate(OWNERS):
                    away = me != owner if k == 0 else True

                    @pl.when(away)
                    def _():
                        remote_both(
                            b.d_send.at[0, pl.ds(0, TOKENS)],
                            b.d_recv.at[layer, peers[k], pair],
                            b.d_s.at[phase, 0, 0],
                            b.d_r.at[phase, peers[k], pair],
                            peers[k],
                            owner,
                        ).wait_recv()

                    b.right[layer, slot_rows(k), pair * PAIR_LANES : (pair + 1) * PAIR_LANES] = (
                        b.d_recv[layer, peers[k], pair]
                    )
                part = mul_nt(b.right[layer, slot_rows(k), :], square(b.wa.at[layer, 0]))
                if k == 0:
                    b.hidden_grad[...] = part
                else:
                    b.part_send[k] = part.astype(BF16)
                    part_copy(k).start()

        @pl.when(section == 3)
        def _():
            b.right[layer, slot_rows(0), :] = b.right_src[...]
            b.hidden_grad[...] = jnp.zeros((TOKENS, D), F32)
            for k in range(1, 4):
                right_copy(k).wait_recv()
                if layer == 1:
                    left_copy(k).wait_recv()

        matrix = matrices[3 * phase + 2]
        matrix.store(mul_tn(b.left[layer], b.right[layer]))
        matrix.pair_copy().start()
        value_sum = jnp.sum(b.right[layer].astype(F32), 0, keepdims=True)
        rows[6:7, :] = jnp.where(section == 2, value_sum, 0.0)
        during()
        for k in (3, 1, 2):

            @pl.when(peers[k] != 3)
            def _():
                part_copy(k).wait_recv()
                b.hidden_grad[...] += b.part_recv[k].astype(F32)

        hidden_grad = b.hidden_grad[...]
        b.streams[2 * layer] = (
            grad.astype(F32) + norm_back(unit, rstd, hidden_grad * vec[0:1, :])
        ).astype(BF16)
        rows[0:1, :] = jnp.sum(hidden_grad * unit, 0, keepdims=True)
        rows[3:4, :] = jnp.sum(hidden_grad, 0, keepdims=True)

        def drain():
            @pl.when(section != 3)
            def _():
                for k in range(1, 4):
                    part_copy(k).wait_send()

            for k in range(1, 4):

                @pl.when(peers[k] == 3)
                def _():
                    right_copy(k).wait_send()
                    if layer == 1:
                        left_copy(k).wait_send()

            for pair, owner in enumerate(OWNERS):

                @pl.when(me != owner)
                def _():
                    out_copy(pair).wait_send()

            @pl.when(p.is_owner)
            def _():
                for third in range(3):
                    for target in range(8):

                        @pl.when((section != third) | (me != target))
                        def _():
                            back_copy(third, target).wait_send()

        return drain

    def nothing():
        pass

    def middle_first():
        start_logs()

    def late_first():
        start_last()

    feed_phase(
        1,
        b.grads.at[pl.ds(0, TOKENS)],
        b.xs.at[2],
        (nothing, middle_first, down1.step_near, late_first),
    )

    def third_out(k):
        return pltpu.make_async_copy(
            b.right.at[1, pl.ds(k * TOKENS, TOKENS)], b.sub_g_out.at[peers[k]], b.third_sem.at[k]
        )

    def before_first():
        down1.step_far()

    def during_first():
        up1.step_far()
        down1.step_pass()
        finish_last()
        sum_logs()

    drain_first = attention_phase(
        1,
        b.streams.at[3],
        b.xs.at[1],
        b.att.at[1],
        (before_first, down1.step_plane, up1.step_near, during_first),
    )

    def early_second():
        vec1.store(b.vec_rows[1].T)
        vec1.pair_copy().start()
        drain_first()
        att1.step_near()

    def middle_second():
        up1.step_plane()
        down0.step_near()

    def parting_second():
        down0.step_far()

    feed_phase(
        0,
        b.streams.at[2],
        b.xs.at[0],
        (early_second, middle_second, parting_second, nothing),
    )

    def before_second():
        up0.step_near()
        vec1.step_far()
        up1.step_pass()
        send_sub(3, True)

    def inside_second():
        up0.step_far()
        att1.step_plane()
        vec1.step_plane()
        down0.step_plane()
        @pl.when(section == 3)
        def _():
            for k in range(4):
                third_out(k).start()

        finish_logs()

    def during_second():
        att0.step_near()
        att1.step_pass()
        down0.step_pass()

    drain_second = attention_phase(
        0,
        b.streams.at[1],
        b.embeds.at[0],
        b.att.at[0],
        (before_second, inside_second, nothing, during_second),
    )
    vec0.store(b.vec_rows[0].T)
    vec0.pair_copy().start()
    att0.step_far()
    send_sub(0, False)
    vec0.step_near()
    up0.step_plane()
    send_sub(2, False)
    send_sub(1, False)
    att0.step_plane()
    up0.step_pass()
    vec0.step_far()
    vec0.step_plane()
    drain_second()
    for matrix in (up1, down1, att1, vec1, down0, up0, vec0, att0):
        matrix.step_end()
    for number in range(3):
        drain_sub(number, False)

    @pl.when(section != 3)
    def _():
        for source in range(4):
            receive_sub(source, False)

    @pl.when(section == 3)
    def _():
        for k in range(4):
            third_out(k).wait()

    for number in range(4):
        drain_sub(number, True)
        receive_sub(number, True)
    for step in range(1, 8):
        small_copy(step).wait_send()
    for step in range(1, 4):
        first_z(step, chip).wait_send()
    block[0].cores(core).wait_send()
    block[1].drain()
    for layer in range(2):
        for line in feed_lines[layer]:
            line.drain()
        for k in range(1, 4):

            @pl.when(section == 3)
            def _():
                block_plane(layer, k).wait_send()

            @pl.when(peers[k] == 3)
            def _():
                block_across(layer, k, core).wait_send()


FINISH_IN = dict(all_m=0, all_v=0, sub_f=0, sub_g=0, log_total=0)
FINISH_OUT = dict(
    outputs=((1, 4, TOKENS, D), BF16, False),
    grads=((1, 4, TOKENS, D), BF16, False),
    qkv=((2, SHARD, 3 * D), F32, False),
    out=((2, SHARD, D), F32, False),
    up=((2, SHARD, FF), F32, False),
    down=((2, 4 * SHARD, D), F32, False),
    gains=((2, 3, SHARD), F32, True),
    biases=((2, 6, SHARD), F32, True),
    hgains=((2, 4 * SHARD), F32, True),
    hbiases=((2, 2, 4 * SHARD), F32, True),
    means=((2, 5), F32, True),
)
FINISH_SCRATCH = dict(
    matrix=((6, 4, SHARD, D), BF16),
    vectors=((2, 4, SHARD, PAIR_LANES), BF16),
    wide=((2, SHARD, 4 * D), F32),
    tall=((2, 4 * SHARD, D), F32),
    spread=((2, SHARD, FF), F32),
    first=((4, TOKENS, D), BF16),
    second=((4, TOKENS, D), BF16),
)
FINISH_SEMS = dict(load_sem=(9,), store_sem=(10,))


def finish_kernel(*refs):
    b = Named([FINISH_IN, FINISH_OUT, FINISH_SCRATCH, FINISH_SEMS], refs)
    loads = [
        pltpu.make_async_copy(b.all_m.at[i], b.matrix.at[i], b.load_sem.at[i]) for i in range(6)
    ] + [pltpu.make_async_copy(b.all_v, b.vectors, b.load_sem.at[6])]
    for copy in loads:
        copy.start()

    outputs_load = pltpu.make_async_copy(b.sub_f, b.first, b.load_sem.at[7])
    outputs_load.start()
    grads_load = pltpu.make_async_copy(b.sub_g, b.second, b.load_sem.at[8])
    grads_load.start()
    stores = []

    def store(source, target, number):
        copy = pltpu.make_async_copy(source, target, b.store_sem.at[number])
        copy.start()
        stores.append(copy)

    for layer in (1, 0):
        up_i = 3 * (1 - layer)
        loads[up_i].wait()
        for j in range(8):
            b.spread[layer, :, j * 4 * SHARD : (j + 1) * 4 * SHARD] = jnp.concatenate(
                [
                    b.matrix[up_i, source, :, j * SHARD : (j + 1) * SHARD].astype(F32)
                    for source in range(4)
                ],
                1,
            )
        store(b.spread.at[layer], b.up.at[layer], 4 * layer)
        loads[up_i + 1].wait()
        for source in range(4):
            b.tall[layer, source * SHARD : (source + 1) * SHARD, :] = b.matrix[
                up_i + 1, source
            ].astype(F32)
        store(b.tall.at[layer], b.down.at[layer], 4 * layer + 1)
        loads[up_i + 2].wait()
        for source in range(4):
            b.wide[layer, :, source * D : (source + 1) * D] = b.matrix[up_i + 2, source].astype(
                F32
            )
        store(b.wide.at[layer, :, pl.ds(0, 3 * D)], b.qkv.at[layer], 4 * layer + 2)
        store(b.wide.at[layer, :, pl.ds(3 * D, D)], b.out.at[layer], 4 * layer + 3)
    outputs_load.wait()
    store(b.first, b.outputs.at[0], 8)
    grads_load.wait()
    store(b.second, b.grads.at[0], 9)
    loads[6].wait()
    for layer in range(2):
        lines = []
        for source in range(4):
            tail = b.vectors[1 - layer, source].astype(F32)
            tail = jnp.concatenate([tail, jnp.zeros((PAIR_LANES - SHARD, PAIR_LANES), F32)], 0)
            lines.append(tail.T)
        model = lines[0] + lines[1] + lines[2] + lines[3]
        b.gains[layer] = model[0:3, 0:SHARD]
        b.biases[layer] = model[3:9, 0:SHARD]
        hidden = jnp.concatenate([each[9:12, 0:SHARD] for each in lines], 1)
        b.hgains[layer : layer + 1, :] = hidden[0:1, :]
        b.hbiases[layer] = hidden[1:3, :]
    lane = lax.broadcasted_iota(jnp.int32, (8, PAIR_LANES), 1)
    number = lax.shift_right_logical(lane, 2)
    sums = jnp.zeros((8, PAIR_LANES), F32)
    for i in range(5):
        part = jnp.sum(jnp.where(number == i, b.log_total[...], 0.0), -1, keepdims=True)
        sums = sums + jnp.where(lane == i, part, 0.0)
    means = sums[0:2, :] / jnp.where(lane[0:2, :] < 5, sums[2:3, :], 1.0)
    b.means[...] = means[:, 0:5]
    for copy in stores:
        copy.wait()


def run_remote(kernel, number, lengths, near, far, outs, scratch, sems):
    vmem = pl.BlockSpec(memory_space=pltpu.VMEM)
    anywhere = pl.BlockSpec(memory_space=pl.ANY)
    smem = pl.BlockSpec(memory_space=pltpu.SMEM)
    return pl.pallas_call(
        kernel,
        out_shape=[shaped(out[0], out[1]) for out in outs.values()],
        in_specs=[smem] * len(lengths) + [vmem] * len(near) + [anywhere] * len(far),
        out_specs=[vmem if out[2] else anywhere for out in outs.values()],
        scratch_shapes=[pltpu.VMEM(item[0], item[1]) for item in scratch.values()]
        + [pltpu.SemaphoreType.DMA(item) for item in sems.values()],
        compiler_params=pltpu.CompilerParams(
            collective_id=number, has_side_effects=True, vmem_limit_bytes=KERNEL_VMEM_BYTES
        ),
        cost_estimate=pl.CostEstimate(
            flops=10**10, bytes_accessed=100_000_000, transcendentals=0
        ),
    )(*lengths, *near, *far)


def run_finish(log_total, *far):
    vmem = pl.BlockSpec(memory_space=pltpu.VMEM)
    anywhere = pl.BlockSpec(memory_space=pl.ANY)
    return pl.pallas_call(
        finish_kernel,
        out_shape=[shaped(out[0], out[1]) for out in FINISH_OUT.values()],
        in_specs=[anywhere] * len(far) + [vmem],
        out_specs=[vmem if out[2] else anywhere for out in FINISH_OUT.values()],
        scratch_shapes=[pltpu.VMEM(item[0], item[1]) for item in FINISH_SCRATCH.values()]
        + [pltpu.SemaphoreType.DMA(item) for item in FINISH_SEMS.values()],
        compiler_params=pltpu.CompilerParams(vmem_limit_bytes=KERNEL_VMEM_BYTES),
    )(*far, log_total)


def quick_body(
    embeds,
    row_lengths,
    qkv_weight,
    out_weight,
    up_weight,
    down_weight,
    model_gains,
    model_biases,
    hidden_gains,
    hidden_biases,
    cotangent,
):
    both = Named(
        [BOTH_OUT],
        run_remote(
            both_kernel,
            10,
            (row_lengths,),
            (jnp.concatenate([model_gains, model_biases], 1), hidden_gains, hidden_biases),
            (embeds, qkv_weight, out_weight, up_weight, down_weight, cotangent),
            BOTH_OUT,
            BOTH_SCRATCH,
            BOTH_SEMS,
        ),
    )
    return tuple(
        run_finish(
            both.log_total,
            both.all_m_out,
            both.all_v_out,
            both.sub_f_out,
            both.sub_g_out,
        )
    )


def fits_quick(mesh):
    return mesh.shape["section"] == 4 and mesh.shape["seq"] == 8


def solution(mesh):
    return jax.shard_map(
        quick_body if fits_quick(mesh) else body,
        mesh=mesh,
        in_specs=(
            P(None, "seq", None),
            P(),
            P(None, "seq", None),
            P(None, "seq", None),
            P(None, "seq", None),
            P(None, "seq", None),
            P(None, None, "seq"),
            P(None, None, "seq"),
            P(None, "seq"),
            P(None, None, "seq"),
            P(None, "seq", None),
        ),
        out_specs=(
            P("section", None, "seq", None),
            P("section", None, "seq", None),
            P(None, "seq", None),
            P(None, "seq", None),
            P(None, "seq", None),
            P(None, "seq", None),
            P(None, None, "seq"),
            P(None, None, "seq"),
            P(None, "seq"),
            P(None, None, "seq"),
            P(),
        ),
        check_vma=False,
    )
```

```python
import jax
import jax.numpy as jnp
from jax import lax
from jax.experimental import pallas as pl
from jax.experimental.pallas import tpu as pltpu
from jax.sharding import PartitionSpec as P

D = 768
HEADS = 12
HEAD_DIM = 64
FF = 3072


WIDTHS = (2048, 4096, 8192, 16384, 32768)
RATIOS = (1, 2, 4, 6, 12)
EPSILON = 1e-05


def passed_along(value, axis, steps):
    count = lax.axis_size(axis)
    initial, last = (max(0, -steps), min(count, count - steps))
    return lax.ppermute(value, axis, [(source, source + steps) for source in range(initial, last)])


def norm_rows(inputs, gain_row, offset):
    center = inputs - jnp.mean(inputs, -1, keepdims=True)
    spread = jnp.mean(center * center, -1, keepdims=True)
    return center * lax.rsqrt(spread + EPSILON) * gain_row + offset


def place_rows(lengths, token_index):
    row_ends = jnp.cumsum(lengths)
    passed = token_index[:, None] >= row_ends[None, :]
    row_ids = jnp.sum(passed.astype(jnp.int32), 1)
    offsets = token_index - jnp.sum(jnp.where(passed, lengths[None, :], 0), 1)
    return (row_ids, offsets)


def query_chosen(query_pos):
    head_ids = jnp.arange(HEADS, dtype=jnp.int32)
    chosen = []
    for seg_width, seg_ratio in zip(WIDTHS, RATIOS):
        query_pick = query_pos % seg_width % seg_ratio
        chosen.append(query_pick[None, :] == (head_ids % seg_ratio)[:, None])
    return chosen


def pattern_allow(query_rows, query_pos, key_rows, key_pos):
    widths = jnp.array(WIDTHS, jnp.int32)[:, None]
    ratios = jnp.array(RATIOS, jnp.int32)[:, None]
    residue = jnp.arange(HEADS, dtype=jnp.int32)[None, :] % ratios
    query_mod = query_pos[None, :] % widths % ratios
    key_mod = key_pos[None, :] % widths % ratios
    query_ok = query_mod[:, None, :] == residue[:, :, None]
    key_ok = key_mod[:, None, :] == residue[:, :, None]
    common = (query_rows[:, None] == key_rows[None, :]) & (key_pos[None, :] <= query_pos[:, None])
    inside = common[None] & (
        (query_pos[None, :] // widths)[:, :, None] == (key_pos[None, :] // widths)[:, None, :]
    )
    return inside[:, None] & query_ok[:, :, :, None] & key_ok[:, :, None, :]


def block_rows(total_rows):
    step_rows = min(total_rows, 512)
    return step_rows


def split_heads(matrix):
    return matrix.reshape(matrix.shape[0], HEADS, HEAD_DIM)


def pair_terms(query_block, keys_block, query_rows, query_pos, key_rows, key_pos):
    scores = jnp.einsum(
        "qhe,khe->hqk", query_block, keys_block, preferred_element_type=jnp.float32
    ) * HEAD_DIM ** (-0.5)
    allowed = pattern_allow(query_rows, query_pos, key_rows, key_pos)
    counts = jnp.sum(allowed.astype(jnp.float32), 0)
    raised = jnp.exp(scores)
    return (raised, counts * raised, allowed)


def project_tokens(inputs, qkv_matrix, norm_gains, norm_biases):
    hidden = norm_rows(inputs, norm_gains[0], norm_biases[0]).astype(jnp.bfloat16)
    bias_row = jnp.concatenate(
        [jnp.zeros_like(norm_biases[3]), jnp.zeros_like(norm_biases[3]), norm_biases[3]]
    )
    projected = (jnp.dot(hidden, qkv_matrix, preferred_element_type=jnp.float32) + bias_row).astype(
        jnp.bfloat16
    )
    return (hidden, projected)


def attention_forward(section_in, projected, whole_keys, lengths, params, seq_index):
    out_matrix, norm_gains, norm_biases = (params[1], params[4], params[5])
    tok_rows = section_in.shape[0]
    inputs = section_in.astype(jnp.float32)
    queries = split_heads(projected[:, :D])
    query_rows, query_pos = place_rows(
        lengths, seq_index * tok_rows + jnp.arange(tok_rows, dtype=jnp.int32)
    )
    group_rows = whole_keys.shape[0]
    step_rows = block_rows(group_rows)

    def one_block(running, block_start):
        totals, pattern_sums, accumulated = running
        kv_block = lax.dynamic_slice_in_dim(whole_keys, block_start, step_rows, 0)
        key_rows, key_pos = place_rows(
            lengths, block_start + jnp.arange(step_rows, dtype=jnp.int32)
        )
        raised, weighted, allowed = pair_terms(
            queries, split_heads(kv_block[:, :D]), query_rows, query_pos, key_rows, key_pos
        )
        totals = totals + jnp.sum(weighted, -1)
        pattern_sums = pattern_sums + jnp.sum(jnp.where(allowed, raised[None], 0.0), -1)
        accumulated = accumulated + jnp.einsum(
            "hqk,khe->hqe",
            weighted.astype(jnp.bfloat16),
            split_heads(kv_block[:, D:]),
            preferred_element_type=jnp.float32,
        )
        return ((totals, pattern_sums, accumulated), None)

    start_sums = (
        jnp.zeros((HEADS, tok_rows), jnp.float32),
        jnp.zeros((len(WIDTHS), HEADS, tok_rows), jnp.float32),
        jnp.zeros((HEADS, tok_rows, HEAD_DIM), jnp.float32),
    )
    folded, unused = lax.scan(
        one_block, start_sums, jnp.arange(0, group_rows, step_rows, dtype=jnp.int32)
    )
    totals, pattern_sums, accumulated = folded
    attended = jnp.transpose(accumulated / totals[:, :, None], (1, 0, 2)).reshape(tok_rows, D)
    inner_norm = norm_rows(attended, norm_gains[1], norm_biases[1]).astype(jnp.bfloat16)
    branch = jnp.dot(inner_norm, out_matrix, preferred_element_type=jnp.float32) + norm_biases[4]
    section_out = (inputs + branch).astype(jnp.bfloat16)
    chosen = query_chosen(query_pos)
    log_terms = jnp.stack(
        [
            jnp.sum(
                jnp.where(pick_row, jnp.log(jnp.where(pick_row, pattern_sums[number], 1.0)), 0.0)
            )
            for number, pick_row in enumerate(chosen)
        ]
    )
    pick_counts = jnp.stack([jnp.sum(pick_row.astype(jnp.float32)) for pick_row in chosen])
    return (section_out, attended, totals, log_terms, pick_counts)


def feed_forward(section_in, params):
    up_matrix, down_matrix, norm_gains, norm_biases, hidden_gain, hidden_bias = (
        params[2],
        params[3],
        params[4],
        params[5],
        params[6],
        params[7],
    )
    tok_rows = section_in.shape[0]
    inputs = section_in.astype(jnp.float32)
    hidden = norm_rows(inputs, norm_gains[2], norm_biases[2]).astype(jnp.bfloat16)
    upward = jnp.dot(hidden, up_matrix, preferred_element_type=jnp.float32) + hidden_bias[0]
    inner_norm = norm_rows(
        jax.nn.gelu(upward, approximate=False), hidden_gain, hidden_bias[1]
    ).astype(jnp.bfloat16)
    branch = jnp.dot(inner_norm, down_matrix, preferred_element_type=jnp.float32) + norm_biases[5]
    section_out = (inputs + branch).astype(jnp.bfloat16)
    empty_terms = jnp.zeros((len(WIDTHS),), jnp.float32)
    return (
        section_out,
        jnp.zeros((tok_rows, D), jnp.float32),
        jnp.zeros((HEADS, tok_rows), jnp.float32),
        empty_terms,
        empty_terms,
    )


def attention_middle(
    section_in, grad_out, attended, totals, lengths, all_keys, projected, params, seq_index
):
    out_matrix, norm_gains, norm_biases = (params[1], params[4], params[5])
    scale_factor = HEAD_DIM ** (-0.5)
    tok_rows = section_in.shape[0]
    queries = split_heads(projected[:, :D])
    query_rows, query_pos = place_rows(
        lengths, seq_index * tok_rows + jnp.arange(tok_rows, dtype=jnp.int32)
    )
    inner_norm = norm_rows(attended, norm_gains[1], norm_biases[1]).astype(jnp.bfloat16)
    out_step = jnp.einsum("td,tf->df", inner_norm, grad_out, preferred_element_type=jnp.float32)
    inner_grad = jnp.einsum("tf,df->td", grad_out, out_matrix, preferred_element_type=jnp.float32)
    unused, inner_back = jax.vjp(norm_rows, attended, norm_gains[1], norm_biases[1])
    attended_grad, inner_gain_grad, inner_bias_grad = inner_back(inner_grad)
    low_attended = attended_grad.astype(jnp.bfloat16)
    head_grad = split_heads(low_attended)
    row_dots = jnp.einsum("qhe,qhe->hq", head_grad.astype(jnp.float32), split_heads(attended))
    scaled_grad = head_grad.astype(jnp.float32) / jnp.transpose(totals)[:, :, None]
    group_rows = all_keys.shape[0]
    step_rows = block_rows(group_rows)

    def grad_block(query_grad, block_start):
        kv_block = lax.dynamic_slice_in_dim(all_keys, block_start, step_rows, 0)
        keys_block = split_heads(kv_block[:, :D])
        values_block = split_heads(kv_block[:, D:])
        key_rows, key_pos = place_rows(
            lengths, block_start + jnp.arange(step_rows, dtype=jnp.int32)
        )
        raised, weighted, allowed = pair_terms(
            queries, keys_block, query_rows, query_pos, key_rows, key_pos
        )
        prob_grad = jnp.einsum(
            "qhe,khe->hqk", head_grad, values_block, preferred_element_type=jnp.float32
        )
        score_grad = (weighted / totals[:, :, None] * (prob_grad - row_dots[:, :, None])).astype(
            jnp.bfloat16
        )
        query_grad = (
            query_grad
            + jnp.einsum("hqk,khe->qhe", score_grad, keys_block, preferred_element_type=jnp.float32)
            * scale_factor
        )
        key_grad = (
            jnp.einsum("hqk,qhe->khe", score_grad, queries, preferred_element_type=jnp.float32)
            * scale_factor
        )
        value_grad = jnp.einsum(
            "hqk,qhe->khe",
            weighted.astype(jnp.bfloat16),
            scaled_grad,
            preferred_element_type=jnp.float32,
        )
        block_grad = jnp.concatenate(
            [key_grad.reshape(step_rows, D), value_grad.reshape(step_rows, D)], 1
        )
        return (query_grad, block_grad)

    query_grad, block_grads = lax.scan(
        grad_block,
        jnp.zeros((tok_rows, HEADS, HEAD_DIM), jnp.float32),
        jnp.arange(0, group_rows, step_rows, dtype=jnp.int32),
    )
    block_grads = block_grads.reshape(group_rows, 2 * D)
    return (
        query_grad.reshape(tok_rows, D),
        low_attended,
        row_dots,
        block_grads,
        out_step,
        inner_gain_grad,
        inner_bias_grad,
    )


def attention_finish(section_in, grad_out, middle, extra, params, grad_sums):
    qkv_matrix, norm_gains, norm_biases = (params[0], params[4], params[5])
    inputs = section_in.astype(jnp.float32)
    grad_float = grad_out.astype(jnp.float32)
    hidden = norm_rows(inputs, norm_gains[0], norm_biases[0]).astype(jnp.bfloat16)
    query_grad, low_attended, row_dots, block_grads, out_step, inner_gain_grad, inner_bias_grad = (
        middle
    )
    own_grads = extra[0]
    proj_grad = jnp.concatenate([query_grad, own_grads], 1).astype(jnp.bfloat16)
    qkv_step = jnp.einsum("td,tf->df", hidden, proj_grad, preferred_element_type=jnp.float32)
    value_bias_sums = jnp.sum(proj_grad[:, 2 * D :].astype(jnp.float32), 0)
    hidden_grad = jnp.einsum("tf,df->td", proj_grad, qkv_matrix, preferred_element_type=jnp.float32)
    unused_first, first_back = jax.vjp(norm_rows, inputs, norm_gains[0], norm_biases[0])
    input_grad, first_gain_grad, first_bias_grad = first_back(hidden_grad)
    qkv_sum, out_sum, up_sum, down_sum, gain_sum, bias_sum, hgain_sum, hbias_sum = grad_sums
    gain_sum = gain_sum.at[0].add(first_gain_grad).at[1].add(inner_gain_grad)
    bias_sum = (
        bias_sum.at[0]
        .add(first_bias_grad)
        .at[1]
        .add(inner_bias_grad)
        .at[3]
        .add(value_bias_sums)
        .at[4]
        .add(jnp.sum(grad_float, 0))
    )
    return (
        grad_float + input_grad,
        (
            qkv_sum + qkv_step,
            out_sum + out_step,
            up_sum,
            down_sum,
            gain_sum,
            bias_sum,
            hgain_sum,
            hbias_sum,
        ),
    )


def feed_backward(section_in, grad_out, params, grad_sums):
    up_matrix, down_matrix, norm_gains, norm_biases, hidden_gain, hidden_bias = (
        params[2],
        params[3],
        params[4],
        params[5],
        params[6],
        params[7],
    )
    inputs = section_in.astype(jnp.float32)
    grad_float = grad_out.astype(jnp.float32)
    hidden = norm_rows(inputs, norm_gains[2], norm_biases[2]).astype(jnp.bfloat16)
    upward = jnp.dot(hidden, up_matrix, preferred_element_type=jnp.float32) + hidden_bias[0]

    def inner_rows(upward_in, gain_row, bias_row):
        return norm_rows(jax.nn.gelu(upward_in, approximate=False), gain_row, bias_row)

    inner_value, inner_back = jax.vjp(inner_rows, upward, hidden_gain, hidden_bias[1])
    inner_norm = inner_value.astype(jnp.bfloat16)
    down_step = jnp.einsum("tf,td->fd", inner_norm, grad_out, preferred_element_type=jnp.float32)
    inner_grad = jnp.einsum("td,fd->tf", grad_out, down_matrix, preferred_element_type=jnp.float32)
    upward_grad, hgain_step, hbias_step = inner_back(inner_grad)
    low_upward = upward_grad.astype(jnp.bfloat16)
    up_step = jnp.einsum("td,tf->df", hidden, low_upward, preferred_element_type=jnp.float32)
    hidden_grad = jnp.einsum("tf,df->td", low_upward, up_matrix, preferred_element_type=jnp.float32)
    unused, first_back = jax.vjp(norm_rows, inputs, norm_gains[2], norm_biases[2])
    input_grad, first_gain_grad, first_bias_grad = first_back(hidden_grad)
    qkv_sum, out_sum, up_sum, down_sum, gain_sum, bias_sum, hgain_sum, hbias_sum = grad_sums
    gain_sum = gain_sum.at[2].add(first_gain_grad)
    bias_sum = bias_sum.at[2].add(first_bias_grad).at[5].add(jnp.sum(grad_float, 0))
    hbias_sum = (
        hbias_sum.at[0].add(jnp.sum(low_upward.astype(jnp.float32), 0)).at[1].add(hbias_step)
    )
    return (
        grad_float + input_grad,
        (
            qkv_sum,
            out_sum,
            up_sum + up_step,
            down_sum + down_step,
            gain_sum,
            bias_sum,
            hgain_sum + hgain_step,
            hbias_sum,
        ),
    )


def keep_slot(store, fresh, slot_id, in_range):
    previous = lax.dynamic_index_in_dim(store, slot_id, 0, False)
    return lax.dynamic_update_index_in_dim(store, jnp.where(in_range, fresh, previous), slot_id, 0)


def body(
    embeds,
    row_lengths,
    qkv_weight,
    out_weight,
    up_weight,
    down_weight,
    model_gains,
    model_biases,
    hidden_gains,
    hidden_biases,
    cotangent,
):
    section_id = lax.axis_index("section")
    seq_index = lax.axis_index("seq")
    section_count = lax.axis_size("section")
    micro_count = embeds.shape[0]
    tok_rows = embeds.shape[1]
    group_rows = tok_rows * lax.axis_size("seq")
    layer_id = section_id // 2
    attends = section_id % 2 == 0
    bias_count = model_biases.shape[1]

    def pick_layer(stacked):
        return lax.dynamic_index_in_dim(stacked, layer_id, 0, False)

    gathered = (
        lax.all_gather(pick_layer(qkv_weight), "seq", axis=0, tiled=True),
        lax.all_gather(pick_layer(out_weight), "seq", axis=0, tiled=True),
        lax.all_gather(pick_layer(up_weight), "seq", axis=0, tiled=True),
        lax.all_gather(pick_layer(down_weight), "seq", axis=0, tiled=True),
        lax.all_gather(pick_layer(model_gains), "seq", axis=1, tiled=True),
        lax.all_gather(pick_layer(model_biases), "seq", axis=1, tiled=True),
        lax.all_gather(pick_layer(hidden_gains), "seq", axis=0, tiled=True),
        lax.all_gather(pick_layer(hidden_biases), "seq", axis=1, tiled=True),
    )
    params = tuple(gathered[:4]) + tuple((vector.astype(jnp.float32) for vector in gathered[4:]))
    whole_shape = (0,)

    def make_projected(section_in):
        return project_tokens(section_in.astype(jnp.float32), params[0], params[4], params[5])[1]

    def skip_projected(section_in):
        return jnp.zeros((tok_rows, 3 * D), jnp.bfloat16)

    def run_attention(section_in, projected, whole_keys, lengths):
        return attention_forward(section_in, projected, whole_keys, lengths, params, seq_index)

    def run_feed(section_in, projected, whole_keys, lengths):
        return feed_forward(section_in, params)

    def forward_tick(running, tick_id):
        (
            incoming,
            kept_inputs,
            kept_attended,
            kept_totals,
            kept_whole,
            outputs,
            log_sums,
            pick_sums,
        ) = running
        micro_id = tick_id - section_id
        in_range = (micro_id >= 0) & (micro_id < micro_count)
        slot_id = jnp.clip(micro_id, 0, micro_count - 1)
        lengths = lax.dynamic_index_in_dim(row_lengths, slot_id, 0, False)
        section_in = jnp.where(
            section_id == 0, lax.dynamic_index_in_dim(embeds, slot_id, 0, False), incoming
        )
        projected = lax.cond(attends, make_projected, skip_projected, section_in)
        whole_keys = lax.all_gather(projected[:, D:], "seq", axis=0, tiled=True)
        section_out, attended, totals, log_terms, pick_counts = lax.cond(
            attends, run_attention, run_feed, section_in, projected, whole_keys, lengths
        )
        kept_inputs = keep_slot(kept_inputs, section_in, slot_id, in_range)
        kept_attended = keep_slot(kept_attended, attended, slot_id, in_range)
        kept_totals = keep_slot(kept_totals, totals, slot_id, in_range)
        outputs = keep_slot(outputs, section_out, slot_id, in_range)
        log_sums = log_sums + jnp.where(in_range, log_terms, 0.0)
        pick_sums = pick_sums + jnp.where(in_range, pick_counts, 0.0)
        incoming = passed_along(section_out, "section", 1)
        return (
            (
                incoming,
                kept_inputs,
                kept_attended,
                kept_totals,
                kept_whole,
                outputs,
                log_sums,
                pick_sums,
            ),
            None,
        )

    forward_start = (
        jnp.zeros((tok_rows, D), jnp.bfloat16),
        jnp.zeros((micro_count, tok_rows, D), jnp.bfloat16),
        jnp.zeros((micro_count, tok_rows, D), jnp.float32),
        jnp.zeros((micro_count, HEADS, tok_rows), jnp.float32),
        jnp.zeros((micro_count,) + whole_shape, jnp.bfloat16),
        jnp.zeros((micro_count, tok_rows, D), jnp.bfloat16),
        jnp.zeros((len(WIDTHS),), jnp.float32),
        jnp.zeros((len(WIDTHS),), jnp.float32),
    )
    ticks = jnp.arange(micro_count + section_count - 1, dtype=jnp.int32)
    forward_end, unused = lax.scan(forward_tick, forward_start, ticks)
    unused_in, kept_inputs, kept_attended, kept_totals, kept_whole, outputs, log_sums, pick_sums = (
        forward_end
    )
    block_shape = (group_rows, 2 * D)

    def middle_attention(section_in, grad_out, attended, totals, lengths, all_keys, projected):
        return attention_middle(
            section_in, grad_out, attended, totals, lengths, all_keys, projected, params, seq_index
        )

    def middle_feed(section_in, grad_out, attended, totals, lengths, all_keys, projected):
        return (
            jnp.zeros((tok_rows, D), jnp.float32),
            jnp.zeros((tok_rows, D), jnp.bfloat16),
            jnp.zeros((HEADS, tok_rows), jnp.float32),
            jnp.zeros(block_shape, jnp.float32),
            jnp.zeros((D, D), jnp.float32),
            jnp.zeros((D,), jnp.float32),
            jnp.zeros((D,), jnp.float32),
        )

    def finish_attention(section_in, grad_out, projected, middle, extra, lengths, grad_sums):
        return attention_finish(section_in, grad_out, middle, extra, params, grad_sums)

    def finish_feed(section_in, grad_out, projected, middle, extra, lengths, grad_sums):
        return feed_backward(section_in, grad_out, params, grad_sums)

    def backward_tick(running, tick_id):
        incoming, grad_sums, input_grads = running
        micro_id = micro_count - 1 - tick_id + (section_count - 1 - section_id)
        in_range = (micro_id >= 0) & (micro_id < micro_count)
        slot_id = jnp.clip(micro_id, 0, micro_count - 1)
        from_next = jnp.where(
            section_id == section_count - 1,
            lax.dynamic_index_in_dim(cotangent, slot_id, 0, False),
            incoming,
        )
        grad_out = jnp.where(in_range, from_next, jnp.zeros_like(from_next))
        section_in = lax.dynamic_index_in_dim(kept_inputs, slot_id, 0, False)
        attended = lax.dynamic_index_in_dim(kept_attended, slot_id, 0, False)
        totals = lax.dynamic_index_in_dim(kept_totals, slot_id, 0, False)
        lengths = lax.dynamic_index_in_dim(row_lengths, slot_id, 0, False)
        projected = lax.cond(attends, make_projected, skip_projected, section_in)
        all_keys = lax.all_gather(projected[:, D:], "seq", axis=0, tiled=True)
        middle = lax.cond(
            attends,
            middle_attention,
            middle_feed,
            section_in,
            grad_out,
            attended,
            totals,
            lengths,
            all_keys,
            projected,
        )
        extra = (lax.psum_scatter(middle[3], "seq", scatter_dimension=0, tiled=True),)
        section_grad, grad_sums = lax.cond(
            attends,
            finish_attention,
            finish_feed,
            section_in,
            grad_out,
            projected,
            middle,
            extra,
            lengths,
            grad_sums,
        )
        low_grad = section_grad.astype(jnp.bfloat16)
        input_grads = keep_slot(input_grads, low_grad, slot_id, in_range)
        incoming = passed_along(low_grad, "section", -1)
        return ((incoming, grad_sums, input_grads), None)

    grad_start = (
        jnp.zeros((D, 3 * D), jnp.float32),
        jnp.zeros((D, D), jnp.float32),
        jnp.zeros((D, FF), jnp.float32),
        jnp.zeros((FF, D), jnp.float32),
        jnp.zeros((3, D), jnp.float32),
        jnp.zeros((bias_count, D), jnp.float32),
        jnp.zeros((FF,), jnp.float32),
        jnp.zeros((2, FF), jnp.float32),
    )
    backward_start = (
        jnp.zeros((tok_rows, D), jnp.bfloat16),
        grad_start,
        jnp.zeros((micro_count, tok_rows, D), jnp.bfloat16),
    )
    backward_end, unused_back = lax.scan(backward_tick, backward_start, ticks)
    unused_grad, grad_sums, input_grads = backward_end
    shards = (
        lax.psum_scatter(grad_sums[0], "seq", scatter_dimension=0, tiled=True),
        lax.psum_scatter(grad_sums[1], "seq", scatter_dimension=0, tiled=True),
        lax.psum_scatter(grad_sums[2], "seq", scatter_dimension=0, tiled=True),
        lax.psum_scatter(grad_sums[3], "seq", scatter_dimension=0, tiled=True),
        lax.psum_scatter(grad_sums[4], "seq", scatter_dimension=1, tiled=True),
        lax.psum_scatter(grad_sums[5], "seq", scatter_dimension=1, tiled=True),
        lax.psum_scatter(grad_sums[6], "seq", scatter_dimension=0, tiled=True),
        lax.psum_scatter(grad_sums[7], "seq", scatter_dimension=1, tiled=True),
    )
    sources = (
        qkv_weight,
        out_weight,
        up_weight,
        down_weight,
        model_gains,
        model_biases,
        hidden_gains,
        hidden_biases,
    )
    placed = tuple(
        (
            lax.dynamic_update_index_in_dim(
                jnp.zeros(source.shape, jnp.float32), shard, layer_id, 0
            )
            for shard, source in zip(shards, sources)
        )
    )
    summed = (
        lax.psum(placed[0].astype(jnp.bfloat16), "section").astype(jnp.float32),
        lax.psum(placed[1].astype(jnp.bfloat16), "section").astype(jnp.float32),
        lax.psum(placed[2].astype(jnp.bfloat16), "section").astype(jnp.float32),
        lax.psum(placed[3].astype(jnp.bfloat16), "section").astype(jnp.float32),
        lax.psum(placed[4].astype(jnp.bfloat16), "section").astype(jnp.float32),
        lax.psum(placed[5].astype(jnp.bfloat16), "section").astype(jnp.float32),
        lax.psum(placed[6].astype(jnp.bfloat16), "section").astype(jnp.float32),
        lax.psum(placed[7].astype(jnp.bfloat16), "section").astype(jnp.float32),
    )
    layer_count = qkv_weight.shape[0]
    layer_terms = lax.dynamic_update_index_in_dim(
        jnp.zeros((layer_count, len(WIDTHS)), jnp.float32), log_sums, layer_id, 0
    )
    layer_picks = lax.dynamic_update_index_in_dim(
        jnp.zeros((layer_count, len(WIDTHS)), jnp.float32), pick_sums, layer_id, 0
    )
    log_totals, pick_totals = lax.psum((layer_terms, layer_picks), ("section", "seq"))
    pattern_means = log_totals / pick_totals
    return (
        outputs[None],
        input_grads[None],
        summed[0],
        summed[1],
        summed[2],
        summed[3],
        summed[4],
        summed[5],
        summed[6],
        summed[7],
        pattern_means,
    )


BF16 = jnp.bfloat16
F32 = jnp.float32
PAIRS = HEADS // 2
OWNERS = (0, 2, 3, 4, 5, 6)
TOKENS = 128
PAIR_LANES = 128
QUERY_STEP = 256
VEC_ROWS = 16
KERNEL_VMEM_BYTES = 64 * 1024 * 1024 - 65536
SCALE = HEAD_DIM ** (-0.5)


def mul(left, right):
    return lax.dot_general(left, right, (((1,), (0,)), ((), ())), preferred_element_type=F32)


def mul_nt(left, right):
    return lax.dot_general(left, right, (((1,), (1,)), ((), ())), preferred_element_type=F32)


def mul_tn(left, right):
    return lax.dot_general(left, right, (((0,), (0,)), ((), ())), preferred_element_type=F32)


def standardize(values):
    center = values - jnp.mean(values, -1, keepdims=True)
    rstd = lax.rsqrt(jnp.mean(center * center, -1, keepdims=True) + EPSILON)
    return (center * rstd, rstd)


def norm_back(unit, rstd, unit_grad):
    first = jnp.mean(unit_grad, -1, keepdims=True)
    second = jnp.mean(unit_grad * unit, -1, keepdims=True)
    return rstd * (unit_grad - first - unit * second)


def remote(source, target, send_sem, recv_sem, axis, peer):
    return pltpu.make_async_remote_copy(
        src_ref=source,
        dst_ref=target,
        send_sem=send_sem,
        recv_sem=recv_sem,
        device_id={axis: peer},
        device_id_type=pl.DeviceIdType.MESH,
    )


def greet(axis, peers):
    barrier = pltpu.get_barrier_semaphore()
    for peer in peers:
        pl.semaphore_signal(
            barrier, inc=1, device_id={axis: peer}, device_id_type=pl.DeviceIdType.MESH
        )
    pl.semaphore_wait(barrier, len(peers))


def seq_peers(me, count):
    return [lax.rem(me + step, count) for step in range(1, count)]


def plane_peers(me):
    return [
        me,
        me + 1 - 2 * lax.rem(me, 2),
        lax.rem(me + 2, 4),
        3 - me,
    ]


def rows_of(block, size=TOKENS):
    return pl.ds(pl.multiple_of(block * size, size), size)


def gelu_parts(values):
    below = 0.5 * (1.0 + lax.erf(values * (0.5**0.5)))
    return (values * below, below)


def share_stats(columns, send, recv, send_sem, recv_sem, peers):
    send[...] = columns.T[0:8, :]
    recv[0] = send[...]
    copies = [
        remote(send, recv.at[k], send_sem.at[k], recv_sem.at[k], "section", peers[k])
        for k in range(1, 4)
    ]
    for copy in copies:
        copy.start()
    return copies


def two_columns(first, second):
    lane = lax.broadcasted_iota(jnp.int32, (first.shape[0], PAIR_LANES), 1)
    return jnp.where(lane == 0, first, jnp.where(lane == 1, second, 0.0))


def slot_rows(k):
    return slice(k * TOKENS, (k + 1) * TOKENS)


def shaped(shape, kind):
    return jax.ShapeDtypeStruct(shape, kind)


class Named:
    def __init__(self, groups, refs):
        names = [name for group in groups for name in group]
        for name, ref in zip(names, refs, strict=True):
            setattr(self, name, ref)


GROUP_TOKENS = 8 * TOKENS
WIDE = 4 * TOKENS
SHARD = D // 8


def square(ref):
    return ref[...].reshape(D, D)


def remote_both(source, target, send_sem, recv_sem, section, seq):
    return pltpu.make_async_remote_copy(
        src_ref=source,
        dst_ref=target,
        send_sem=send_sem,
        recv_sem=recv_sem,
        device_id=(section, seq),
        device_id_type=pl.DeviceIdType.MESH,
    )


def greet_all(barrier, section, me):
    for other in range(4):
        for j in range(8):

            @pl.when((section != other) | (me != j))
            def _():
                pl.semaphore_signal(
                    barrier, inc=1, device_id=(other, j), device_id_type=pl.DeviceIdType.MESH
                )


class Place:
    def __init__(self):
        self.me = lax.axis_index("seq")
        self.section = lax.axis_index("section")
        self.peers = plane_peers(self.section)
        self.core = lax.rem(self.me, 2)
        self.chip = lax.div(self.me, 2)
        self.high = lax.div(self.chip, 2)
        self.low = lax.rem(self.chip, 2)
        self.sibling = self.me + 1 - 2 * self.core
        self.across = 2 * (2 * (1 - self.high) + self.low) + self.core
        self.next = 2 * (2 * self.high + 1 - self.low) + self.core
        self.is_owner = (self.me != 1) & (self.me != 7)
        pair = jnp.where(self.me == 0, 0, self.me - 1)
        self.my_pair = jnp.where(pair > PAIRS - 1, PAIRS - 1, pair)


class LineGather:
    def __init__(self, place, base, far_sems, near_sems, core_sems):
        self.place = place
        self.base = base
        self.far_sems = far_sems
        self.near_sems = near_sems
        self.core_sems = core_sems

    def far(self, high):
        p = self.place
        view = self.base.at[high, p.low, p.core]
        return remote(view, view, self.far_sems[0], self.far_sems[1], "seq", p.across)

    def near(self, low):
        p = self.place
        view = self.base.at[:, low, p.core]
        return remote(view, view, self.near_sems[0], self.near_sems[1], "seq", p.next)

    def cores(self, core):
        p = self.place
        view = self.base.at[:, :, core]
        return remote(view, view, self.core_sems[0], self.core_sems[1], "seq", p.sibling)

    def start(self):
        self.far(self.place.high).start()

    def pass_line(self):
        self.far(1 - self.place.high).wait_recv()
        self.near(self.place.low).start()

    def pass_core(self):
        self.near(1 - self.place.low).wait_recv()
        self.cores(self.place.core).start()

    def ready(self):
        self.cores(1 - self.place.core).wait_recv()

    def drain(self):
        self.far(self.place.high).wait_send()
        self.near(self.place.low).wait_send()
        self.cores(self.place.core).wait_send()


BOTH_VMEM = dict(model=0, hgains=0, hbiases=0)
BOTH_ANY = dict(embeds_in=0, qkv_w=0, out_w=0, up_w=0, down_w=0, cotangent_in=0)
BOTH_OUT = dict(
    sub_f_out=((4, TOKENS, D), BF16, False),
    sub_g_out=((4, TOKENS, D), BF16, False),
    all_m_out=((6, 4, SHARD, D), BF16, False),
    all_v_out=((2, 4, SHARD, PAIR_LANES), BF16, False),
    log_total=((8, PAIR_LANES), F32, True),
)
BOTH_SCRATCH = dict(
    embeds=((4, TOKENS, D), BF16),
    att=((2, TOKENS, D), BF16),
    picks=((2, GROUP_TOKENS, PAIR_LANES), BF16),
    wa=((2, 2, 2, 2, 2, SHARD, D), BF16),
    wf=((2, 2, 2, 2, 2, SHARD, D), BF16),
    qkv=((2, 3, GROUP_TOKENS, PAIR_LANES), BF16),
    pa=((2, GROUP_TOKENS, PAIR_LANES), F32),
    pt=((2, GROUP_TOKENS, PAIR_LANES), F32),
    hid=((2, WIDE, D), BF16),
    up=((2, WIDE, D), F32),
    stat=((2, WIDE, PAIR_LANES), F32),
    left=((2, WIDE, D), BF16),
    raw_up=((2, SHARD, FF), BF16),
    small_src=((2, 32, PAIR_LANES), BF16),
    small=((8, 2, 32, PAIR_LANES), BF16),
    inner=((TOKENS, D), BF16),
    vecs=((2, VEC_ROWS, D), F32),
    logs=((8, PAIR_LANES), F32),
    proj_send=((4, PAIRS, TOKENS, PAIR_LANES), BF16),
    att_send=((GROUP_TOKENS, PAIR_LANES), BF16),
    att_recv=((2, PAIRS, TOKENS, PAIR_LANES), BF16),
    columns=((WIDE, PAIR_LANES), F32),
    stat_rows=((PAIR_LANES, WIDE), F32),
    stat_send=((8, WIDE), F32),
    first_recv=((4, TOKENS, D), BF16),
    fstat_recv=((2, 4, 8, WIDE), F32),
    xs=((4, TOKENS, D), BF16),
    last_send=((4, TOKENS, D), BF16),
    last_recv=((4, TOKENS, D), BF16),
    last=((TOKENS, D), F32),
    streams=((4, TOKENS, D), BF16),
    grads=((WIDE, D), BF16),
    units=((WIDE, D), F32),
    unit_grads=((WIDE, D), F32),
    inners=((WIDE, D), BF16),
    lows=((WIDE, D), BF16),
    part_send=((4, TOKENS, D), BF16),
    part_recv=((4, TOKENS, D), BF16),
    stat_recv=((4, 8, WIDE), F32),
    do_send=((PAIRS, TOKENS, PAIR_LANES), BF16),
    do_recv=((GROUP_TOKENS, PAIR_LANES), BF16),
    key_sum=((GROUP_TOKENS, PAIR_LANES), F32),
    value_sum=((GROUP_TOKENS, PAIR_LANES), F32),
    d_send=((3, GROUP_TOKENS, PAIR_LANES), BF16),
    d_recv=((2, 4, PAIRS, TOKENS, PAIR_LANES), BF16),
    left_src=((TOKENS, D), BF16),
    right_src=((TOKENS, D), BF16),
    right=((2, WIDE, D), BF16),
    vec_rows=((2, PAIR_LANES, D), F32),
    hidden_grad=((TOKENS, D), F32),
    prod=((3, 2, 2, 2, SHARD, D), BF16),
    prod_v=((2, 2, 2, 2, SHARD, PAIR_LANES), BF16),
    pair=((6, 2, 2, SHARD, D), BF16),
    pair_v=((2, 2, 2, SHARD, PAIR_LANES), BF16),
    near=((6, 2, SHARD, D), BF16),
    near_v=((2, 2, SHARD, PAIR_LANES), BF16),
    far=((6, SHARD, D), BF16),
    far_v=((2, SHARD, PAIR_LANES), BF16),
    done=((6, SHARD, D), BF16),
    done_v=((2, SHARD, PAIR_LANES), BF16),
    line=((3, SHARD, D), BF16),
    log_line=((8, 8, PAIR_LANES), F32),
    log_plane=((4, 8, PAIR_LANES), F32),
)
BOTH_SEMS = dict(
    load_sem=(2, 3),
    embeds_sem=(4,),
    small_s=(8,),
    small_r=(8,),
    az_s=(4,),
    az_r=(4,),
    line_s=(6, 3),
    line_r=(6, 3),
    axy_s=(2, 4),
    axy_r=(2, 4),
    axs_s=(2, 4),
    axs_r=(2, 4),
    inner_s=(4,),
    inner_r=(4,),
    wide_s=(2, 4, PAIRS),
    wide_r=(2, 3, 8),
    att_s=(2, 8),
    att_r=(2, PAIRS),
    fhid_s=(2, 4),
    fhid_r=(2, 4),
    fstat_s=(2, 4),
    fstat_r=(2, 4),
    fleft_s=(4,),
    fleft_r=(4,),
    first_s=(4,),
    first_r=(4,),
    g_s=(2, 4),
    g_r=(2, 4),
    stat_s=(2, 4),
    stat_r=(2, 4),
    part_s=(2, 4),
    part_r=(2, 4),
    do_s=(2, PAIRS),
    do_r=(2, 8),
    d_s=(2, 3, 8),
    d_r=(2, 4, PAIRS),
    left_s=(2, 4),
    left_r=(2, 4),
    right_s=(2, 4),
    right_r=(2, 4),
    back_s=(2, 4),
    back_r=(2, 4),
    subf_s=(4,),
    subf_r=(4,),
    subg_s=(4,),
    subg_r=(4,),
    own_sem=(2,),
    last_s=(4,),
    last_r=(4,),
    cot_sem=(4,),
    pair_s=(8,),
    pair_r=(8,),
    near_s=(8,),
    near_r=(8,),
    far_s=(8,),
    far_r=(8,),
    all_s=(8, 4),
    all_r=(8, 4),
    log_s=(8,),
    log_r=(8,),
    log_plane_s=(4,),
    log_plane_r=(4,),
    third_sem=(4,),
    last_line_s=(4,),
    last_line_r=(4,),
)


def make_picks(lengths_ref, section, my_pair, picks_ref):
    tokens = lax.broadcasted_iota(jnp.int32, (GROUP_TOKENS, PAIR_LANES), 0)
    lane = lax.broadcasted_iota(jnp.int32, (GROUP_TOKENS, PAIR_LANES), 1)
    row_id = jnp.zeros_like(tokens)
    first = jnp.zeros_like(tokens)
    end = 0
    for row in range(lengths_ref.shape[1]):
        end = end + lengths_ref[section, row]
        passed = tokens >= end
        row_id = row_id + jnp.where(passed, 1, 0)
        first = jnp.where(passed, end, first)
    pos = (tokens - first).astype(F32)
    number = lax.shift_right_logical(lane, 2)
    row = lane - 4 * number
    ratio = jnp.zeros(lane.shape, F32)
    for i, each in enumerate(RATIOS):
        ratio = jnp.where(number == i, float(each), ratio)
    valid = ratio > 0.5
    ratio = jnp.where(valid, ratio, 1.0)

    def residue(values):
        return values - ratio * jnp.floor((values + 0.5) / ratio)

    residues = residue(pos)
    for head in range(2):
        wanted = residue(jnp.full(lane.shape, 2 * my_pair + head, jnp.int32).astype(F32))
        fits = valid & (row == row_id) & (jnp.abs(residues - wanted) < 0.5)
        picks_ref[head] = jnp.where(fits, 1.0, 0.0).astype(BF16)


def both_kernel(lengths, *refs):
    b = Named([BOTH_VMEM, BOTH_ANY, BOTH_OUT, BOTH_SCRATCH, BOTH_SEMS], refs)
    p = Place()
    me, section, peers, core = (p.me, p.section, p.peers, p.core)
    chip, high, low = (p.chip, p.high, p.low)
    out_slot = jnp.where(section == 3, 0, 1)

    barrier = pltpu.get_barrier_semaphore()
    greet_all(barrier, section, me)

    def block_from_qkv(layer):
        return pltpu.make_async_copy(
            b.qkv_w.at[layer, :, pl.ds(pl.multiple_of(lax.rem(section, 3) * D, D), D)],
            b.wa.at[layer, 0, high, low, core],
            b.load_sem.at[layer, 0],
        )

    def block_from_out(layer):
        return pltpu.make_async_copy(
            b.out_w.at[layer], b.wa.at[layer, 0, high, low, core], b.load_sem.at[layer, 0]
        )

    def load_up(layer):
        return pltpu.make_async_copy(b.up_w.at[layer], b.raw_up.at[layer], b.load_sem.at[layer, 1])

    def load_down(layer):
        return pltpu.make_async_copy(
            b.down_w.at[layer, pl.ds(pl.multiple_of(section * SHARD, SHARD), SHARD)],
            b.wf.at[layer, 1, high, low, core],
            b.load_sem.at[layer, 2],
        )

    def load_embeds(k):
        return pltpu.make_async_copy(
            b.embeds_in.at[peers[k]], b.embeds.at[k], b.embeds_sem.at[k]
        )

    for layer in range(2):

        @pl.when(section != 3)
        def _():
            block_from_qkv(layer).start()

        @pl.when(section == 3)
        def _():
            block_from_out(layer).start()

        if layer == 0:
            for k in range(4):
                load_embeds(k).start()
        load_up(layer).start()
        load_down(layer).start()

    def block_loaded(layer):
        @pl.when(section != 3)
        def _():
            block_from_qkv(layer).wait()

        @pl.when(section == 3)
        def _():
            block_from_out(layer).wait()

    def pick_up(layer):
        load_up(layer).wait()
        load_down(layer).wait()
        raw = b.raw_up[layer]
        for s in range(4):

            @pl.when(section == s)
            def _():
                b.wf[layer, 0, high, low, core] = jnp.concatenate(
                    [
                        raw[:, (4 * j + s) * SHARD : (4 * j + s + 1) * SHARD].astype(F32)
                        for j in range(8)
                    ],
                    1,
                ).astype(BF16)

    def line_gather(number, base):
        pairs = [(b.line_s.at[number, i], b.line_r.at[number, i]) for i in range(3)]
        return LineGather(p, base, *pairs)

    block = [line_gather(layer, b.wa.at[layer, 0]) for layer in range(2)]
    feed_lines = [
        [line_gather(2 + 2 * layer + which, b.wf.at[layer, which]) for which in range(2)]
        for layer in range(2)
    ]

    def first_z(step, source):
        view = b.wa.at[0, 0, lax.div(source, 2), lax.rem(source, 2), core]
        return remote(
            view,
            view,
            b.az_s.at[step],
            b.az_r.at[step],
            "seq",
            2 * lax.rem(chip + step, 4) + core,
        )

    def block_plane(layer, k):
        source = b.wa.at[layer, 0, :, :, core]
        target = b.wa.at[layer, 1, :, :, core]
        return remote(source, target, b.axy_s.at[layer, k], b.axy_r.at[layer, k], "section", peers[k])

    def block_across(layer, k, side):
        view = b.wa.at[layer, 1, :, :, side]
        return remote(view, view, b.axs_s.at[layer, k], b.axs_r.at[layer, k], "seq", p.sibling)

    for layer in range(2):
        model = b.model[layer].astype(F32)
        hidden_gain = b.hgains[layer : layer + 1, :].astype(F32)
        hidden_bias = b.hbiases[layer].astype(F32)
        lines = [model]
        for each in (hidden_gain, hidden_bias[0:1, :], hidden_bias[1:2, :]):
            for s in range(4):
                lines.append(each[:, s * SHARD : (s + 1) * SHARD])
        lines.append(jnp.zeros((11, SHARD), F32))
        packed = jnp.concatenate(lines, 0)
        packed = jnp.concatenate([packed, jnp.zeros((32, PAIR_LANES - SHARD), F32)], 1)
        b.small_src[layer] = packed.astype(BF16)
    b.small[me] = b.small_src[...]
    make_picks(lengths, section, p.my_pair, b.picks)
    b.logs[...] = jnp.zeros_like(b.logs)
    block_loaded(0)
    pl.semaphore_wait(barrier, 31)

    def small_copy(step):
        return remote(
            b.small_src,
            b.small.at[me],
            b.small_s.at[step],
            b.small_r.at[step],
            "seq",
            lax.rem(me + step, 8),
        )

    for step in range(1, 8):
        small_copy(step).start()
    for step in range(1, 4):
        first_z(step, chip).start()
    pick_up(0)
    for step in range(1, 8):
        source = lax.rem(me + 8 - step, 8)
        remote(
            b.small_src,
            b.small.at[source],
            b.small_s.at[step],
            b.small_r.at[step],
            "seq",
            source,
        ).wait_recv()
    for layer in range(2):
        pieces = []
        for j in range(8):
            small = b.small[j, layer].astype(F32)
            lines = [small[0:9]]
            for third in range(3):
                line = jnp.zeros((1, PAIR_LANES), F32)
                for s in range(4):
                    at = 9 + 4 * third + s
                    line = line + jnp.where(section == s, small[at : at + 1], 0.0)
                lines.append(line)
            lines.append(jnp.zeros((4, PAIR_LANES), F32))
            pieces.append(jnp.concatenate(lines, 0)[:, 0:SHARD])
        b.vecs[layer] = jnp.concatenate(pieces, 1)

    def owner_of(pair):
        return jnp.where(pair == 0, 0, pair + 1)

    def wide_turned(layer, k, step):
        pair = lax.rem(me + step, PAIRS)
        return (
            remote_both(
                b.proj_send.at[k, pair],
                b.qkv.at[layer, lax.rem(section, 3), rows_of(me)],
                b.wide_s.at[layer, k, pair],
                b.wide_r.at[layer, lax.rem(section, 3), me],
                peers[k],
                owner_of(pair),
            ),
            owner_of(pair),
        )

    def wide_copy(layer, k, pair):
        return remote_both(
            b.proj_send.at[k, pair],
            b.qkv.at[layer, lax.rem(section, 3), rows_of(me)],
            b.wide_s.at[layer, k, pair],
            b.wide_r.at[layer, lax.rem(section, 3), me],
            peers[k],
            OWNERS[pair],
        )

    def project(layer, arrive):
        vec = b.vecs.at[layer]

        @pl.when(section != 3)
        def _():
            bias = jnp.where(section == 2, vec[6:7, :], 0.0)
            for k in (3, 1, 2, 0) if layer == 0 else (0, 1, 2, 3):
                if k > 0:
                    arrive(k)
                part = mul(b.left[layer, slot_rows(k), :], square(b.wa.at[layer, 0])) + bias
                part = part.astype(BF16)
                for pair in range(PAIRS):
                    b.proj_send[k, pair] = part[:, pair * PAIR_LANES : (pair + 1) * PAIR_LANES]
                for step in range(PAIRS):
                    if k > 0:
                        wide_turned(layer, k, step)[0].start()
                    else:
                        owner = wide_turned(layer, k, step)[1]

                        @pl.when(me != owner)
                        def _():
                            wide_turned(layer, k, step)[0].start()

                if k == 0:

                    @pl.when(p.is_owner)
                    def _():
                        b.qkv[layer, section, rows_of(me), :] = b.proj_send[0, p.my_pair]

    def wait_projected(layer):
        @pl.when(p.is_owner)
        def _():
            for third in range(3):
                for source in range(8):

                    @pl.when((section != third) | (me != source))
                    def _():
                        remote_both(
                            b.proj_send.at[0, 0],
                            b.qkv.at[layer, third, pl.ds(source * TOKENS, TOKENS)],
                            b.wide_s.at[layer, 0, 0],
                            b.wide_r.at[layer, third, source],
                            third,
                            source,
                        ).wait_recv()

        @pl.when(section != 3)
        def _():
            for k in range(4):
                for pair, owner in enumerate(OWNERS):
                    if k > 0:
                        wide_copy(layer, k, pair).wait_send()
                    else:

                        @pl.when(me != owner)
                        def _():
                            wide_copy(layer, k, pair).wait_send()

    def back_copy(layer, target):
        return remote(
            b.att_send.at[pl.ds(target * TOKENS, TOKENS)],
            b.att_recv.at[layer, p.my_pair],
            b.att_s.at[layer, target],
            b.att_r.at[layer, p.my_pair],
            "seq",
            target,
        )

    def attend(layer):
        lane = lax.broadcasted_iota(jnp.int32, (QUERY_STEP, PAIR_LANES), 1)
        first_half = lane < HEAD_DIM
        for step in range(GROUP_TOKENS // QUERY_STEP):
            start = step * QUERY_STEP
            keys_end = start + QUERY_STEP
            rows = slice(start, keys_end)
            query = b.qkv[layer, 0, rows, :] * jnp.asarray(SCALE, BF16)
            keys = b.qkv[layer, 1, 0:keys_end, :]
            values = b.qkv[layer, 2, 0:keys_end, :]
            causal = lax.broadcasted_iota(jnp.int32, (QUERY_STEP, keys_end), 1) <= (
                start + lax.broadcasted_iota(jnp.int32, (QUERY_STEP, keys_end), 0)
            )
            sums = []
            totals = []
            logs = jnp.zeros((1, PAIR_LANES), F32)
            picked_sum = jnp.zeros((1, PAIR_LANES), F32)
            for head in range(2):
                mine = first_half if head == 0 else ~first_half
                own_query = jnp.where(mine, query, jnp.zeros_like(query))
                scores = mul_nt(own_query, keys)
                raised = jnp.where(causal, jnp.exp(scores), 0.0)
                pick_query = b.picks[head, rows, :]
                pick_keys = b.picks[head, 0:keys_end, :]
                counts = mul_nt(pick_query, pick_keys)
                weighted = (raised * counts).astype(BF16)
                sums.append(mul(weighted, values))
                pattern = mul(raised.astype(BF16), pick_keys)
                picked = pick_query.astype(F32)
                totals.append(jnp.sum(pattern * picked, -1, keepdims=True))
                chosen = picked > 0.5
                logs = logs + jnp.sum(
                    jnp.where(chosen, jnp.log(jnp.where(chosen, pattern, 1.0)), 0.0),
                    0,
                    keepdims=True,
                )
                picked_sum = picked_sum + jnp.sum(picked, 0, keepdims=True)
            b.logs[layer : layer + 1, :] += logs
            if layer == 0:
                b.logs[2:3, :] += picked_sum
            total = jnp.where(first_half, totals[0], totals[1])
            attended = jnp.where(first_half, sums[0], sums[1]) / total
            b.pa[layer, rows, :] = attended
            b.pt[layer, rows, :] = total
            b.att_send[rows, :] = attended.astype(BF16)
            for target in (2 * step, 2 * step + 1):

                @pl.when(me != target)
                def _():
                    back_copy(layer, target).start()

                @pl.when(me == target)
                def _():
                    b.att_recv[layer, p.my_pair] = b.att_send[
                        target * TOKENS : (target + 1) * TOKENS, :
                    ]

    def attention_rest(layer, inputs_ref, after):
        vec = b.vecs.at[layer]
        wait_projected(layer)
        feed_lines[layer][0].start()
        after()

        @pl.when(p.is_owner)
        def _():
            attend(layer)

        feed_lines[layer][0].pass_line()
        for k in range(1, 4):

            @pl.when(peers[k] == 3)
            def _():
                block_plane(layer, k).wait_recv()
                block_across(layer, k, core).start()

        for pair, owner in enumerate(OWNERS):

            @pl.when(me != owner)
            def _():
                remote(
                    b.att_send.at[pl.ds(0, TOKENS)],
                    b.att_recv.at[layer, pair],
                    b.att_s.at[layer, 0],
                    b.att_r.at[layer, pair],
                    "seq",
                    owner,
                ).wait_recv()

            b.att[layer, :, pair * PAIR_LANES : (pair + 1) * PAIR_LANES] = b.att_recv[layer, pair]
        inner_unit, unused = standardize(b.att[layer].astype(F32))
        inner = (inner_unit * vec[1:2, :] + vec[4:5, :]).astype(BF16)
        if layer == 0:
            b.inner[...] = inner
        for k in range(1, 4):

            @pl.when(peers[k] == 3)
            def _():
                block_across(layer, k, 1 - core).wait_recv()

        branch = mul(inner, square(b.wa.at[layer, out_slot])) + vec[7:8, :]
        b.xs[2 * layer] = (inputs_ref[...].astype(F32) + branch).astype(BF16)

    def attention_drain(layer):
        @pl.when(p.is_owner)
        def _():
            for target in range(8):

                @pl.when(me != target)
                def _():
                    back_copy(layer, target).wait_send()

    def feed(layer, resting, parting):
        vec = b.vecs.at[layer]
        inputs = b.xs[2 * layer].astype(F32)
        unit, unused = standardize(inputs)
        b.hid[layer, slot_rows(0), :] = (unit * vec[2:3, :] + vec[5:6, :]).astype(BF16)
        hidden_copies = [
            remote(
                b.hid.at[layer, pl.ds(0, TOKENS)],
                b.hid.at[layer, pl.ds(k * TOKENS, TOKENS)],
                b.fhid_s.at[layer, k],
                b.fhid_r.at[layer, k],
                "section",
                peers[k],
            )
            for k in range(1, 4)
        ]
        for copy in hidden_copies:
            copy.start()
        up_line, down_line = feed_lines[layer]
        down_line.start()
        up_line.pass_core()
        down_line.pass_line()
        up_line.ready()
        for k in range(4):
            if k > 0:
                hidden_copies[k - 1].wait_recv()
            upward = mul(b.hid[layer, slot_rows(k), :], square(b.wf.at[layer, 0])) + vec[10:11, :]
            b.up[layer, slot_rows(k), :] = upward
            values, unused = gelu_parts(upward)
            b.units[slot_rows(k), :] = values
            mean = jnp.mean(values, -1, keepdims=True)
            center = values - mean
            b.columns[slot_rows(k), :] = two_columns(
                mean, jnp.sum(center * center, -1, keepdims=True)
            )
        stat_copies = share_stats(
            b.columns[...],
            b.stat_send,
            b.fstat_recv.at[layer],
            b.fstat_s.at[layer],
            b.fstat_r.at[layer],
            peers,
        )
        down_line.pass_core()
        resting()
        for copy in stat_copies:
            copy.wait_recv()
        b.stat_rows[...] = jnp.zeros((PAIR_LANES, WIDE), F32)
        for k in range(4):
            means = [b.fstat_recv[layer, other, 0:1, slot_rows(k ^ other)] for other in range(4)]
            squares = [b.fstat_recv[layer, other, 1:2, slot_rows(k ^ other)] for other in range(4)]
            mean = (means[0] + means[1] + means[2] + means[3]) * 0.25
            spread = squares[0] + squares[1] + squares[2] + squares[3]
            for each in means:
                spread = spread + D * (each - mean) * (each - mean)
            b.stat_rows[0:1, slot_rows(k)] = mean
            b.stat_rows[1:2, slot_rows(k)] = lax.rsqrt(spread * (1.0 / FF) + EPSILON)
        b.stat[layer] = b.stat_rows[...].T
        down_line.ready()
        if layer == 1:
            parting()
            for copy in hidden_copies + stat_copies:
                copy.wait_send()
            return
        branch = None
        part_copies = []
        for k in (3, 1, 2, 0):
            both = b.stat[layer, slot_rows(k), :]
            inner = (
                (b.units[slot_rows(k), :] - both[:, 0:1]) * both[:, 1:2] * vec[9:10, :]
                + vec[11:12, :]
            ).astype(BF16)
            part = mul(inner, square(b.wf.at[layer, 1]))
            if k == 0:
                branch = part
            else:
                b.part_send[k] = part.astype(BF16)
                part_copies.append(
                    remote(
                        b.part_send.at[k],
                        b.first_recv.at[k],
                        b.first_s.at[k],
                        b.first_r.at[k],
                        "section",
                        peers[k],
                    )
                )
                part_copies[-1].start()
        parting()
        for k, copy in zip((3, 1, 2), part_copies):
            copy.wait_recv()
            branch = branch + b.first_recv[k].astype(F32)
        b.xs[2 * layer + 1] = (inputs + branch + vec[8:9, :]).astype(BF16)
        for copy in hidden_copies + stat_copies + part_copies:
            copy.wait_send()

    def sub_copies(number, forward):
        source = b.xs if forward else b.streams
        target = b.sub_f_out if forward else b.sub_g_out
        send_sem = b.subf_s if forward else b.subg_s
        recv_sem = b.subf_r if forward else b.subg_r

        def away():
            return remote(
                source.at[number],
                target.at[section],
                send_sem.at[number],
                recv_sem.at[section],
                "section",
                number,
            )

        def own():
            return pltpu.make_async_copy(
                source.at[number], target.at[section], b.own_sem.at[0 if forward else 1]
            )

        return away, own

    def send_sub(number, forward):
        @pl.when(section != number)
        def _():
            sub_copies(number, forward)[0]().start()

        @pl.when(section == number)
        def _():
            sub_copies(number, forward)[1]().start()

    def drain_sub(number, forward):
        @pl.when(section != number)
        def _():
            sub_copies(number, forward)[0]().wait_send()

        @pl.when(section == number)
        def _():
            sub_copies(number, forward)[1]().wait()

    def receive_sub(source, forward):
        target = b.sub_f_out if forward else b.sub_g_out

        @pl.when(section != source)
        def _():
            remote(
                b.streams.at[0],
                target.at[source],
                (b.subf_s if forward else b.subg_s).at[0],
                (b.subf_r if forward else b.subg_r).at[source],
                "section",
                source,
            ).wait_recv()

    for k in range(4):
        load_embeds(k).wait()

        @pl.when(section != 3)
        def _():
            unit, unused = standardize(b.embeds[k].astype(F32))
            b.left[0, slot_rows(k), :] = (
                unit * b.vecs[0, 0:1, :] + b.vecs[0, 3:4, :]
            ).astype(BF16)
    pick_up(1)
    for step in range(1, 4):
        first_z(step, lax.rem(chip + 4 - step, 4)).wait_recv()
    block[0].cores(core).start()

    @pl.when(section == 3)
    def _():
        for k in range(1, 4):
            block_plane(0, k).start()

    block[0].ready()
    project(0, lambda k: None)

    attention_rest(0, b.embeds.at[0], lambda: None)

    def resting_first():
        block_loaded(1)
        block[1].start()

    def parting_first():
        attention_drain(0)
        block[1].pass_line()

    feed(0, resting_first, parting_first)

    second = b.vecs.at[1]
    unit, unused = standardize(b.xs[1].astype(F32))
    b.left[1, slot_rows(0), :] = (unit * second[0:1, :] + second[3:4, :]).astype(BF16)

    def left_copy(k):
        return remote(
            b.left.at[1, pl.ds(0, TOKENS)],
            b.left.at[1, pl.ds(k * TOKENS, TOKENS)],
            b.fleft_s.at[k],
            b.fleft_r.at[k],
            "section",
            peers[k],
        )

    for k in (3, 1, 2):

        @pl.when(peers[k] != 3)
        def _():
            left_copy(k).start()

    block[1].pass_core()
    for k in range(1, 4):

        @pl.when(peers[k] != 3)
        def _():
            left_copy(k).wait_send()

    @pl.when(section == 3)
    def _():
        for k in range(1, 4):
            block_plane(1, k).start()

    block[1].ready()
    project(1, lambda k: left_copy(k).wait_recv())

    def inner_copy(k):
        return remote(
            b.inner,
            b.left.at[0, pl.ds(k * TOKENS, TOKENS)],
            b.inner_s.at[k],
            b.inner_r.at[k],
            "section",
            peers[k],
        )

    def after_second():
        for k in range(1, 4):

            @pl.when(peers[k] == 3)
            def _():
                inner_copy(k).start()

        @pl.when(section == 3)
        def _():
            b.left[0, slot_rows(0), :] = b.inner[...]

        send_sub(0, True)
        send_sub(1, True)

    attention_rest(1, b.xs.at[1], after_second)

    def resting_second():
        send_sub(2, True)
        for k in range(1, 4):

            @pl.when(peers[k] == 3)
            def _():
                inner_copy(k).wait_send()

        @pl.when(section == 3)
        def _():
            for k in range(1, 4):
                inner_copy(k).wait_recv()

    def parting_second():
        attention_drain(1)

    feed(1, resting_second, parting_second)

    def cotangent_load(k):
        return pltpu.make_async_copy(
            b.cotangent_in.at[peers[k]], b.grads.at[pl.ds(k * TOKENS, TOKENS)], b.cot_sem.at[k]
        )

    for k in range(4):
        cotangent_load(k).start()

    def log_copy(step):
        return remote(
            b.logs,
            b.log_line.at[me],
            b.log_s.at[step],
            b.log_r.at[step],
            "seq",
            lax.rem(me + step, 8),
        )

    def log_plane_copy(k, slot):
        return remote(
            b.log_plane.at[slot],
            b.log_plane.at[slot],
            b.log_plane_s.at[k],
            b.log_plane_r.at[k],
            "section",
            peers[k],
        )

    def start_logs():
        b.log_line[me] = b.logs[...]
        for step in range(1, 8):
            log_copy(step).start()

    def sum_logs():
        for step in range(1, 8):
            source = lax.rem(me + 8 - step, 8)
            remote(
                b.logs,
                b.log_line.at[source],
                b.log_s.at[step],
                b.log_r.at[step],
                "seq",
                source,
            ).wait_recv()
        total = b.log_line[0]
        for j in range(1, 8):
            total = total + b.log_line[j]
        b.log_plane[section] = total
        for k in range(1, 4):
            log_plane_copy(k, section).start()

    def finish_logs():
        for k in range(1, 4):
            log_plane_copy(k, peers[k]).wait_recv()
        total = b.log_plane[0]
        for other in range(1, 4):
            total = total + b.log_plane[other]
        b.log_total[...] = total
        for step in range(1, 8):
            log_copy(step).wait_send()
        for k in range(1, 4):
            log_plane_copy(k, section).wait_send()

    class Matrix:
        def __init__(self, number):
            self.number = number
            self.direct = number > 4
            self.turn = (1, 2) if number % 2 else (2, 1)
            self.j = number % 3 if number < 6 else number - 6
            if number < 6:
                self.i = number
                refs = (b.prod, b.pair, b.near, b.far, b.done, b.all_m_out)
            else:
                self.i = number - 6
                refs = (b.prod_v, b.pair_v, b.near_v, b.far_v, b.done_v, b.all_v_out)
            self.prod, self.pair, self.near, self.far, self.done, self.all = refs

        def store(self, value):
            if 3 <= self.number < 6:
                matrices[self.number - 3].sent()
            for j in range(8):
                self.prod[self.j, j % 2, j // 4, j // 2 % 2] = value[
                    j * SHARD : (j + 1) * SHARD, :
                ].astype(BF16)

        def pair_copy(self):
            n = self.number
            return remote(
                self.prod.at[self.j, 1 - core],
                self.pair.at[self.i],
                b.pair_s.at[n],
                b.pair_r.at[n],
                "seq",
                p.sibling,
            )

        def near_copy(self):
            n = self.number
            return remote(
                self.prod.at[self.j, core, :, 1 - low],
                self.near.at[self.i],
                b.near_s.at[n],
                b.near_r.at[n],
                "seq",
                p.next,
            )

        def far_copy(self):
            n = self.number
            return remote(
                self.prod.at[self.j, core, 1 - high, low],
                self.far.at[self.i],
                b.far_s.at[n],
                b.far_r.at[n],
                "seq",
                p.across,
            )

        def all_copy(self, k, slot):
            n = self.number
            return remote(
                self.done.at[self.i],
                self.all.at[self.i, slot],
                b.all_s.at[n, k],
                b.all_r.at[n, k],
                "section",
                peers[k],
            )

        def own_copy(self):
            return pltpu.make_async_copy(
                self.done.at[self.i], self.all.at[self.i, section], b.all_s.at[self.number, 0]
            )

        def step_near(self):
            self.pair_copy().wait_recv()
            i, at = (self.i, self.j)
            for h in range(2):
                for l in range(2):
                    self.prod[at, core, h, l] = (
                        self.prod[at, core, h, l].astype(F32) + self.pair[i, h, l].astype(F32)
                    ).astype(BF16)
            self.near_copy().start()

        def line_copy(self, step):
            target = lax.rem(chip + step, 4)
            return remote(
                self.prod.at[self.j, core, lax.div(target, 2), lax.rem(target, 2)],
                b.line.at[step - 1],
                b.last_line_s.at[step],
                b.last_line_r.at[step],
                "seq",
                2 * target + core,
            )

        def step_line(self):
            self.pair_copy().wait_recv()
            i, at = (self.i, self.j)
            for h in range(2):
                for l in range(2):
                    self.prod[at, core, h, l] = (
                        self.prod[at, core, h, l].astype(F32) + self.pair[i, h, l].astype(F32)
                    ).astype(BF16)
            for step in (2, 1, 3):
                self.line_copy(step).start()

        def step_line_plane(self):
            total = self.prod[self.j, core, high, low].astype(F32)
            for step in range(1, 4):
                self.line_copy(step).wait_recv()
                total = total + b.line[step - 1].astype(F32)
            self.done[self.i] = total.astype(BF16)
            for k in (3, 1, 2):
                self.all_copy(k, section).start()
            self.own_copy().start()

        def step_far(self):
            self.near_copy().wait_recv()
            i, at = (self.i, self.j)
            for h in range(2):
                self.prod[at, core, h, low] = (
                    self.prod[at, core, h, low].astype(F32) + self.near[i, h].astype(F32)
                ).astype(BF16)
            self.far_copy().start()

        def step_plane(self):
            self.far_copy().wait_recv()
            i = self.i
            self.done[i] = (
                self.prod[self.j, core, high, low].astype(F32) + self.far[i].astype(F32)
            ).astype(BF16)
            for k in (3, 1, 2) if self.direct else (1, 2):
                self.all_copy(k, section).start()
            self.own_copy().start()

        def turn_copy(self):
            n = self.number
            first, second = self.turn
            view = self.all.at[self.i, peers[first]]
            return remote(
                view, view, b.all_s.at[n, 3], b.all_r.at[n, 3], "section", peers[second]
            )

        def step_pass(self):
            first = self.turn[0]
            self.all_copy(first, peers[first]).wait_recv()
            self.turn_copy().start()

        def step_end(self):
            for k in range(1, 4):
                if self.direct or k != self.turn[0]:
                    self.all_copy(k, peers[k]).wait_recv()
                if self.direct or k != 3:
                    self.all_copy(k, section).wait_send()
                else:
                    self.turn_copy().wait_send()
            self.own_copy().wait()
            if self.number > 2:
                self.sent()

        def sent(self):
            self.pair_copy().wait_send()
            if self.number == 5:
                for step in range(1, 4):
                    self.line_copy(step).wait_send()
                return
            self.near_copy().wait_send()
            self.far_copy().wait_send()

    matrices = [Matrix(number) for number in range(8)]
    up1, down1, att1, up0, down0, att0, vec1, vec0 = matrices

    def last_copy(k):
        return remote(
            b.last_send.at[k],
            b.last_recv.at[k],
            b.last_s.at[k],
            b.last_r.at[k],
            "section",
            peers[k],
        )

    def start_last():
        for k in (3, 1, 2, 0):
            part = mul(b.inners[slot_rows(k), :], square(b.wf.at[1, 1]))
            if k == 0:
                b.last[...] = part
            else:
                b.last_send[k] = part.astype(BF16)
                last_copy(k).start()

    def finish_last():
        total = b.xs[2].astype(F32) + b.last[...] + b.vecs[1, 8:9, :]
        for k in range(1, 4):
            last_copy(k).wait_recv()
            total = total + b.last_recv[k].astype(F32)
        b.xs[3] = total.astype(BF16)
        for k in range(1, 4):
            last_copy(k).wait_send()

    def feed_phase(layer, grad_ref, x_ref, hooks):
        phase = 1 - layer
        vec = b.vecs.at[layer]
        rows = b.vec_rows.at[layer]
        up_matrix = matrices[3 * phase]
        down_matrix = matrices[3 * phase + 1]
        early, middle, parting, late = hooks
        if layer == 0:
            b.grads[slot_rows(0), :] = grad_ref[...]
        grad_copies = [] if layer == 1 else [
            remote(
                b.grads.at[pl.ds(0, TOKENS)],
                b.grads.at[pl.ds(k * TOKENS, TOKENS)],
                b.g_s.at[phase, k],
                b.g_r.at[phase, k],
                "section",
                peers[k],
            )
            for k in range(1, 4)
        ]
        if layer == 0:
            for k in (3, 1, 2):
                grad_copies[k - 1].start()
        rows[...] = jnp.zeros((PAIR_LANES, D), F32)
        early()
        for k in range(4):
            both = b.stat[layer, slot_rows(k), :]
            upward = b.up[layer, slot_rows(k), :]
            values, below = gelu_parts(upward)
            b.up[layer, slot_rows(k), :] = below + upward * (
                jnp.exp(-0.5 * upward * upward) * (0.5 / 3.141592653589793) ** 0.5
            )
            unit = (values - both[:, 0:1]) * both[:, 1:2]
            b.units[slot_rows(k), :] = unit
            b.inners[slot_rows(k), :] = (unit * vec[9:10, :] + vec[11:12, :]).astype(BF16)
        gain_sum = jnp.zeros((1, D), F32)
        bias_sum = jnp.zeros((1, D), F32)
        for k in range(4):
            if layer == 1:
                cotangent_load(k).wait()
            elif k > 0:
                if k == 3:
                    att1.step_far()
                    vec1.step_near()
                grad_copies[k - 1].wait_recv()
            unit = b.units[slot_rows(k), :]
            inner_grad = mul_nt(b.grads[slot_rows(k), :], square(b.wf.at[layer, 1]))
            gain_sum = gain_sum + jnp.sum(inner_grad * unit, 0, keepdims=True)
            bias_sum = bias_sum + jnp.sum(inner_grad, 0, keepdims=True)
            unit_grad = inner_grad * vec[9:10, :]
            b.unit_grads[slot_rows(k), :] = unit_grad
            b.columns[slot_rows(k), :] = two_columns(
                jnp.sum(unit_grad, -1, keepdims=True), jnp.sum(unit_grad * unit, -1, keepdims=True)
            )
        stat_copies = share_stats(
            b.columns[...],
            b.stat_send,
            b.stat_recv,
            b.stat_s.at[phase],
            b.stat_r.at[phase],
            peers,
        )
        rows[9:10, :] = gain_sum
        rows[11:12, :] = bias_sum
        down_matrix.store(mul_tn(b.inners[...], b.grads[...]))
        down_matrix.pair_copy().start()
        middle()
        for copy in stat_copies:
            copy.wait_recv()
        b.stat_rows[...] = jnp.zeros((PAIR_LANES, WIDE), F32)
        for k in range(4):
            for line in range(2):
                parts = [
                    b.stat_recv[other, line : line + 1, slot_rows(k ^ other)]
                    for other in range(4)
                ]
                b.stat_rows[line : line + 1, slot_rows(k)] = (
                    parts[0] + parts[1] + parts[2] + parts[3]
                ) * (1.0 / FF)
        b.columns[...] = b.stat_rows[...].T
        hidden_grad = None
        low_sum = jnp.zeros((1, D), F32)
        part_copies = []
        for k in (3, 1, 2, 0):
            rstd = b.stat[layer, slot_rows(k), :][:, 1:2]
            both = b.columns[slot_rows(k), :]
            lowered = (
                rstd
                * (
                    b.unit_grads[slot_rows(k), :]
                    - both[:, 0:1]
                    - b.units[slot_rows(k), :] * both[:, 1:2]
                )
                * b.up[layer, slot_rows(k), :]
            ).astype(BF16)
            b.lows[slot_rows(k), :] = lowered
            low_sum = low_sum + jnp.sum(lowered.astype(F32), 0, keepdims=True)
            part = mul_nt(lowered, square(b.wf.at[layer, 0]))
            if k == 0:
                hidden_grad = part
            else:
                b.part_send[k] = part.astype(BF16)
                part_copies.append(
                    remote(
                        b.part_send.at[k],
                        b.part_recv.at[k],
                        b.part_s.at[phase, k],
                        b.part_r.at[phase, k],
                        "section",
                        peers[k],
                    )
                )
                part_copies[-1].start()
        rows[10:11, :] = low_sum
        up_matrix.store(mul_tn(b.hid[layer], b.lows[...]))
        up_matrix.pair_copy().start()
        unit, rstd = standardize(x_ref[...].astype(F32))
        parting()
        for k, copy in zip((3, 1, 2), part_copies):
            copy.wait_recv()
            hidden_grad = hidden_grad + b.part_recv[k].astype(F32)
        grad = grad_ref[...].astype(F32)
        number = 2 * layer + 1
        b.streams[number] = (
            grad + norm_back(unit, rstd, hidden_grad * vec[2:3, :])
        ).astype(BF16)
        rows[2:3, :] = jnp.sum(hidden_grad * unit, 0, keepdims=True)
        rows[5:6, :] = jnp.sum(hidden_grad, 0, keepdims=True)
        rows[8:9, :] = jnp.sum(grad, 0, keepdims=True)
        for copy in grad_copies + stat_copies + part_copies:
            copy.wait_send()
        late()

    def attention_phase(layer, grad_ref, x_ref, att_ref, hooks):
        phase = 1 - layer
        vec = b.vecs.at[layer]
        rows = b.vec_rows.at[layer]
        before, inside, after, during = hooks
        grad = grad_ref[...]
        inner_unit, inner_rstd = standardize(att_ref[...].astype(F32))
        inner_grad = mul_nt(grad, square(b.wa.at[layer, out_slot]))
        att_grad = norm_back(inner_unit, inner_rstd, inner_grad * vec[1:2, :]).astype(BF16)
        for pair in range(PAIRS):
            b.do_send[pair] = att_grad[:, pair * PAIR_LANES : (pair + 1) * PAIR_LANES]

        def out_copy(pair):
            return remote(
                b.do_send.at[pair],
                b.do_recv.at[rows_of(me)],
                b.do_s.at[phase, pair],
                b.do_r.at[phase, me],
                "seq",
                OWNERS[pair],
            )

        for pair, owner in enumerate(OWNERS):

            @pl.when(me != owner)
            def _():
                out_copy(pair).start()

            @pl.when(me == owner)
            def _():
                b.do_recv[rows_of(me), :] = b.do_send[pair]

        def left_copy(k):
            return remote(
                b.left_src,
                b.left.at[layer, pl.ds(k * TOKENS, TOKENS)],
                b.left_s.at[phase, k],
                b.left_r.at[phase, k],
                "section",
                peers[k],
            )

        def right_copy(k):
            return remote(
                b.right_src,
                b.right.at[layer, pl.ds(k * TOKENS, TOKENS)],
                b.right_s.at[phase, k],
                b.right_r.at[phase, k],
                "section",
                peers[k],
            )

        unit, rstd = standardize(x_ref[...].astype(F32))
        b.left_src[...] = (inner_unit * vec[1:2, :] + vec[4:5, :]).astype(BF16)
        b.right_src[...] = grad
        for k in range(1, 4):

            @pl.when(peers[k] == 3)
            def _():
                right_copy(k).start()
                if layer == 1:
                    left_copy(k).start()

        if layer == 1:

            @pl.when(section == 3)
            def _():
                b.left[layer, slot_rows(0), :] = b.left_src[...]

        rows[1:2, :] = jnp.sum(inner_grad * inner_unit, 0, keepdims=True)
        rows[4:5, :] = jnp.sum(inner_grad, 0, keepdims=True)
        rows[7:8, :] = jnp.sum(grad.astype(F32), 0, keepdims=True)

        def back_copy(third, target):
            return remote_both(
                b.d_send.at[third, pl.ds(target * TOKENS, TOKENS)],
                b.d_recv.at[layer, section, p.my_pair],
                b.d_s.at[phase, third, target],
                b.d_r.at[phase, section, p.my_pair],
                third,
                target,
            )

        @pl.when(p.is_owner)
        def _():
            for source in range(8):

                @pl.when(me != source)
                def _():
                    remote(
                        b.do_send.at[0],
                        b.do_recv.at[pl.ds(source * TOKENS, TOKENS)],
                        b.do_s.at[phase, 0],
                        b.do_r.at[phase, source],
                        "seq",
                        source,
                    ).wait_recv()

        before()

        @pl.when(p.is_owner)
        def _():
            b.key_sum[...] = jnp.zeros((GROUP_TOKENS, PAIR_LANES), F32)
            b.value_sum[...] = jnp.zeros((GROUP_TOKENS, PAIR_LANES), F32)
            lane = lax.broadcasted_iota(jnp.int32, (QUERY_STEP, PAIR_LANES), 1)
            first_half = lane < HEAD_DIM
            last_step = GROUP_TOKENS // QUERY_STEP - 1
            for step in (0,) + tuple(range(last_step, 0, -1)):
                start = step * QUERY_STEP
                keys_end = start + QUERY_STEP
                block = slice(start, keys_end)
                plain_query = b.qkv[layer, 0, block, :]
                query = plain_query * jnp.asarray(SCALE, BF16)
                keys = b.qkv[layer, 1, 0:keys_end, :]
                values = b.qkv[layer, 2, 0:keys_end, :]
                causal = lax.broadcasted_iota(jnp.int32, (QUERY_STEP, keys_end), 1) <= (
                    start + lax.broadcasted_iota(jnp.int32, (QUERY_STEP, keys_end), 0)
                )
                head_grad = b.do_recv[block, :]
                inverse = 1.0 / b.pt[layer, block, :]
                head_float = head_grad.astype(F32)
                products = head_float * b.pa[layer, block, :]
                scaled = (head_float * inverse).astype(BF16)
                key_lanes = lax.broadcasted_iota(jnp.int32, (keys_end, PAIR_LANES), 1) < HEAD_DIM
                query_parts = []
                key_parts = []
                value_parts = []
                for head in range(2):
                    mine = first_half if head == 0 else ~first_half
                    own_query = jnp.where(mine, query, jnp.zeros_like(query))
                    own_grad = jnp.where(mine, head_grad, jnp.zeros_like(head_grad))
                    delta = jnp.sum(jnp.where(mine, products, 0.0), -1, keepdims=True)
                    own_inverse = jnp.max(jnp.where(mine, inverse, 0.0), -1, keepdims=True)
                    counts = mul_nt(b.picks[head, block, :], b.picks[head, 0:keys_end, :])
                    scores = mul_nt(own_query, keys)
                    weighted = jnp.where(causal, jnp.exp(scores) * counts, 0.0)
                    prob_grad = mul_nt(own_grad, values)
                    score_grad = (weighted * own_inverse * (prob_grad - delta)).astype(BF16)
                    query_parts.append(mul(score_grad, keys))
                    key_parts.append(mul_tn(score_grad, plain_query))
                    value_parts.append(mul_tn(weighted.astype(BF16), scaled))
                b.key_sum[0:keys_end, :] += jnp.where(key_lanes, key_parts[0], key_parts[1])
                b.value_sum[0:keys_end, :] += jnp.where(key_lanes, value_parts[0], value_parts[1])
                query_grad = jnp.where(first_half, query_parts[0], query_parts[1]) * SCALE
                b.d_send[0, block, :] = query_grad.astype(BF16)
                ready = [(0, step)]
                if step > 0:
                    ready = [(0, step), (1, step), (2, step)]
                if step == 1:
                    ready = [(1, 0), (2, 0)] + ready
                for third, part in ready:
                    part_rows = slice(part * QUERY_STEP, (part + 1) * QUERY_STEP)
                    if third == 1:
                        b.d_send[1, part_rows, :] = (b.key_sum[part_rows, :] * SCALE).astype(BF16)
                    if third == 2:
                        b.d_send[2, part_rows, :] = b.value_sum[part_rows, :].astype(BF16)
                    for target in (2 * part, 2 * part + 1):
                        away = (section != third) | (me != target)

                        @pl.when(away)
                        def _():
                            back_copy(third, target).start()

                        @pl.when(~away)
                        def _():
                            b.d_recv[layer, section, p.my_pair] = b.d_send[
                                third, target * TOKENS : (target + 1) * TOKENS, :
                            ]

        inside()
        after()

        def part_copy(k):
            return remote(
                b.part_send.at[k],
                b.part_recv.at[k],
                b.back_s.at[phase, k],
                b.back_r.at[phase, k],
                "section",
                peers[k],
            )

        @pl.when(section != 3)
        def _():
            for k in (3, 2, 1, 0):
                for pair, owner in enumerate(OWNERS):
                    away = me != owner if k == 0 else True

                    @pl.when(away)
                    def _():
                        remote_both(
                            b.d_send.at[0, pl.ds(0, TOKENS)],
                            b.d_recv.at[layer, peers[k], pair],
                            b.d_s.at[phase, 0, 0],
                            b.d_r.at[phase, peers[k], pair],
                            peers[k],
                            owner,
                        ).wait_recv()

                    b.right[layer, slot_rows(k), pair * PAIR_LANES : (pair + 1) * PAIR_LANES] = (
                        b.d_recv[layer, peers[k], pair]
                    )
                part = mul_nt(b.right[layer, slot_rows(k), :], square(b.wa.at[layer, 0]))
                if k == 0:
                    b.hidden_grad[...] = part
                else:
                    b.part_send[k] = part.astype(BF16)
                    part_copy(k).start()

        @pl.when(section == 3)
        def _():
            b.right[layer, slot_rows(0), :] = b.right_src[...]
            b.hidden_grad[...] = jnp.zeros((TOKENS, D), F32)
            for k in range(1, 4):
                right_copy(k).wait_recv()
                if layer == 1:
                    left_copy(k).wait_recv()

        matrix = matrices[3 * phase + 2]
        matrix.store(mul_tn(b.left[layer], b.right[layer]))
        matrix.pair_copy().start()
        value_sum = jnp.sum(b.right[layer].astype(F32), 0, keepdims=True)
        rows[6:7, :] = jnp.where(section == 2, value_sum, 0.0)
        during()
        for k in (3, 1, 2):

            @pl.when(peers[k] != 3)
            def _():
                part_copy(k).wait_recv()
                b.hidden_grad[...] += b.part_recv[k].astype(F32)

        hidden_grad = b.hidden_grad[...]
        b.streams[2 * layer] = (
            grad.astype(F32) + norm_back(unit, rstd, hidden_grad * vec[0:1, :])
        ).astype(BF16)
        rows[0:1, :] = jnp.sum(hidden_grad * unit, 0, keepdims=True)
        rows[3:4, :] = jnp.sum(hidden_grad, 0, keepdims=True)

        def drain():
            @pl.when(section != 3)
            def _():
                for k in range(1, 4):
                    part_copy(k).wait_send()

            for k in range(1, 4):

                @pl.when(peers[k] == 3)
                def _():
                    right_copy(k).wait_send()
                    if layer == 1:
                        left_copy(k).wait_send()

            for pair, owner in enumerate(OWNERS):

                @pl.when(me != owner)
                def _():
                    out_copy(pair).wait_send()

            @pl.when(p.is_owner)
            def _():
                for third in range(3):
                    for target in range(8):

                        @pl.when((section != third) | (me != target))
                        def _():
                            back_copy(third, target).wait_send()

        return drain

    def nothing():
        pass

    def middle_first():
        start_logs()

    def late_first():
        start_last()

    feed_phase(
        1,
        b.grads.at[pl.ds(0, TOKENS)],
        b.xs.at[2],
        (nothing, middle_first, down1.step_near, late_first),
    )

    def third_out(k):
        return pltpu.make_async_copy(
            b.right.at[1, pl.ds(k * TOKENS, TOKENS)], b.sub_g_out.at[peers[k]], b.third_sem.at[k]
        )

    def before_first():
        down1.step_far()

    def during_first():
        up1.step_far()
        down1.step_pass()
        finish_last()
        sum_logs()

    drain_first = attention_phase(
        1,
        b.streams.at[3],
        b.xs.at[1],
        b.att.at[1],
        (before_first, down1.step_plane, up1.step_near, during_first),
    )

    def early_second():
        vec1.store(b.vec_rows[1].T)
        vec1.pair_copy().start()
        drain_first()
        att1.step_near()

    def middle_second():
        up1.step_plane()
        down0.step_near()

    def late_second():
        att1.step_plane()
        send_sub(2, False)
        send_sub(1, False)

    def parting_second():
        down0.step_far()

    feed_phase(
        0,
        b.streams.at[2],
        b.xs.at[0],
        (early_second, middle_second, parting_second, late_second),
    )

    def before_second():
        up0.step_near()
        vec1.step_far()
        up1.step_pass()
        down0.step_plane()
        send_sub(3, True)

    def inside_second():
        up0.step_far()
        att1.step_pass()
        vec1.step_plane()
        down0.step_pass()
        @pl.when(section == 3)
        def _():
            for k in range(4):
                third_out(k).start()

        finish_logs()

    def during_second():
        att0.step_line()
        up0.step_plane()

    drain_second = attention_phase(
        0,
        b.streams.at[1],
        b.embeds.at[0],
        b.att.at[0],
        (before_second, inside_second, nothing, during_second),
    )
    vec0.store(b.vec_rows[0].T)
    vec0.pair_copy().start()
    send_sub(0, False)
    vec0.step_near()
    att0.step_line_plane()
    vec0.step_far()
    up0.step_pass()
    vec0.step_plane()
    drain_second()
    for matrix in (up1, down1, att1, vec1, down0, up0, vec0, att0):
        matrix.step_end()
    for number in range(3):
        drain_sub(number, False)

    @pl.when(section != 3)
    def _():
        for source in range(4):
            receive_sub(source, False)

    @pl.when(section == 3)
    def _():
        for k in range(4):
            third_out(k).wait()

    for number in range(4):
        drain_sub(number, True)
        receive_sub(number, True)
    for step in range(1, 8):
        small_copy(step).wait_send()
    for step in range(1, 4):
        first_z(step, chip).wait_send()
    block[0].cores(core).wait_send()
    block[1].drain()
    for layer in range(2):
        for line in feed_lines[layer]:
            line.drain()
        for k in range(1, 4):

            @pl.when(section == 3)
            def _():
                block_plane(layer, k).wait_send()

            @pl.when(peers[k] == 3)
            def _():
                block_across(layer, k, core).wait_send()


FINISH_IN = dict(all_m=0, all_v=0, sub_f=0, sub_g=0, log_total=0)
FINISH_OUT = dict(
    outputs=((1, 4, TOKENS, D), BF16, False),
    grads=((1, 4, TOKENS, D), BF16, False),
    qkv=((2, SHARD, 3 * D), F32, False),
    out=((2, SHARD, D), F32, False),
    up=((2, SHARD, FF), F32, False),
    down=((2, 4 * SHARD, D), F32, False),
    gains=((2, 3, SHARD), F32, True),
    biases=((2, 6, SHARD), F32, True),
    hgains=((2, 4 * SHARD), F32, True),
    hbiases=((2, 2, 4 * SHARD), F32, True),
    means=((2, 5), F32, True),
)
FINISH_SCRATCH = dict(
    matrix=((6, 4, SHARD, D), BF16),
    vectors=((2, 4, SHARD, PAIR_LANES), BF16),
    wide=((2, SHARD, 4 * D), F32),
    tall=((2, 4 * SHARD, D), F32),
    spread=((2, SHARD, FF), F32),
    first=((4, TOKENS, D), BF16),
    second=((4, TOKENS, D), BF16),
)
FINISH_SEMS = dict(load_sem=(9,), store_sem=(10,))


def finish_kernel(*refs):
    b = Named([FINISH_IN, FINISH_OUT, FINISH_SCRATCH, FINISH_SEMS], refs)
    loads = [
        pltpu.make_async_copy(b.all_m.at[i], b.matrix.at[i], b.load_sem.at[i]) for i in range(6)
    ] + [pltpu.make_async_copy(b.all_v, b.vectors, b.load_sem.at[6])]
    for copy in loads:
        copy.start()

    outputs_load = pltpu.make_async_copy(b.sub_f, b.first, b.load_sem.at[7])
    outputs_load.start()
    grads_load = pltpu.make_async_copy(b.sub_g, b.second, b.load_sem.at[8])
    grads_load.start()
    stores = []

    def store(source, target, number):
        copy = pltpu.make_async_copy(source, target, b.store_sem.at[number])
        copy.start()
        stores.append(copy)

    for layer in (1, 0):
        up_i = 3 * (1 - layer)
        loads[up_i].wait()
        for j in range(8):
            b.spread[layer, :, j * 4 * SHARD : (j + 1) * 4 * SHARD] = jnp.concatenate(
                [
                    b.matrix[up_i, source, :, j * SHARD : (j + 1) * SHARD].astype(F32)
                    for source in range(4)
                ],
                1,
            )
        store(b.spread.at[layer], b.up.at[layer], 4 * layer)
        loads[up_i + 1].wait()
        for source in range(4):
            b.tall[layer, source * SHARD : (source + 1) * SHARD, :] = b.matrix[
                up_i + 1, source
            ].astype(F32)
        store(b.tall.at[layer], b.down.at[layer], 4 * layer + 1)
        loads[up_i + 2].wait()
        for source in range(4):
            b.wide[layer, :, source * D : (source + 1) * D] = b.matrix[up_i + 2, source].astype(
                F32
            )
        store(b.wide.at[layer, :, pl.ds(0, 3 * D)], b.qkv.at[layer], 4 * layer + 2)
        store(b.wide.at[layer, :, pl.ds(3 * D, D)], b.out.at[layer], 4 * layer + 3)
    outputs_load.wait()
    store(b.first, b.outputs.at[0], 8)
    grads_load.wait()
    store(b.second, b.grads.at[0], 9)
    loads[6].wait()
    for layer in range(2):
        lines = []
        for source in range(4):
            tail = b.vectors[1 - layer, source].astype(F32)
            tail = jnp.concatenate([tail, jnp.zeros((PAIR_LANES - SHARD, PAIR_LANES), F32)], 0)
            lines.append(tail.T)
        model = lines[0] + lines[1] + lines[2] + lines[3]
        b.gains[layer] = model[0:3, 0:SHARD]
        b.biases[layer] = model[3:9, 0:SHARD]
        hidden = jnp.concatenate([each[9:12, 0:SHARD] for each in lines], 1)
        b.hgains[layer : layer + 1, :] = hidden[0:1, :]
        b.hbiases[layer] = hidden[1:3, :]
    lane = lax.broadcasted_iota(jnp.int32, (8, PAIR_LANES), 1)
    number = lax.shift_right_logical(lane, 2)
    sums = jnp.zeros((8, PAIR_LANES), F32)
    for i in range(5):
        part = jnp.sum(jnp.where(number == i, b.log_total[...], 0.0), -1, keepdims=True)
        sums = sums + jnp.where(lane == i, part, 0.0)
    means = sums[0:2, :] / jnp.where(lane[0:2, :] < 5, sums[2:3, :], 1.0)
    b.means[...] = means[:, 0:5]
    for copy in stores:
        copy.wait()


def run_remote(kernel, number, lengths, near, far, outs, scratch, sems):
    vmem = pl.BlockSpec(memory_space=pltpu.VMEM)
    anywhere = pl.BlockSpec(memory_space=pl.ANY)
    smem = pl.BlockSpec(memory_space=pltpu.SMEM)
    return pl.pallas_call(
        kernel,
        out_shape=[shaped(out[0], out[1]) for out in outs.values()],
        in_specs=[smem] * len(lengths) + [vmem] * len(near) + [anywhere] * len(far),
        out_specs=[vmem if out[2] else anywhere for out in outs.values()],
        scratch_shapes=[pltpu.VMEM(item[0], item[1]) for item in scratch.values()]
        + [pltpu.SemaphoreType.DMA(item) for item in sems.values()],
        compiler_params=pltpu.CompilerParams(
            collective_id=number, has_side_effects=True, vmem_limit_bytes=KERNEL_VMEM_BYTES
        ),
        cost_estimate=pl.CostEstimate(
            flops=10**10, bytes_accessed=100_000_000, transcendentals=0
        ),
    )(*lengths, *near, *far)


def run_finish(log_total, *far):
    vmem = pl.BlockSpec(memory_space=pltpu.VMEM)
    anywhere = pl.BlockSpec(memory_space=pl.ANY)
    return pl.pallas_call(
        finish_kernel,
        out_shape=[shaped(out[0], out[1]) for out in FINISH_OUT.values()],
        in_specs=[anywhere] * len(far) + [vmem],
        out_specs=[vmem if out[2] else anywhere for out in FINISH_OUT.values()],
        scratch_shapes=[pltpu.VMEM(item[0], item[1]) for item in FINISH_SCRATCH.values()]
        + [pltpu.SemaphoreType.DMA(item) for item in FINISH_SEMS.values()],
        compiler_params=pltpu.CompilerParams(vmem_limit_bytes=KERNEL_VMEM_BYTES),
    )(*far, log_total)


def quick_body(
    embeds,
    row_lengths,
    qkv_weight,
    out_weight,
    up_weight,
    down_weight,
    model_gains,
    model_biases,
    hidden_gains,
    hidden_biases,
    cotangent,
):
    both = Named(
        [BOTH_OUT],
        run_remote(
            both_kernel,
            10,
            (row_lengths,),
            (jnp.concatenate([model_gains, model_biases], 1), hidden_gains, hidden_biases),
            (embeds, qkv_weight, out_weight, up_weight, down_weight, cotangent),
            BOTH_OUT,
            BOTH_SCRATCH,
            BOTH_SEMS,
        ),
    )
    return tuple(
        run_finish(
            both.log_total,
            both.all_m_out,
            both.all_v_out,
            both.sub_f_out,
            both.sub_g_out,
        )
    )


def fits_quick(mesh):
    return mesh.shape["section"] == 4 and mesh.shape["seq"] == 8


def solution(mesh):
    return jax.shard_map(
        quick_body if fits_quick(mesh) else body,
        mesh=mesh,
        in_specs=(
            P(None, "seq", None),
            P(),
            P(None, "seq", None),
            P(None, "seq", None),
            P(None, "seq", None),
            P(None, "seq", None),
            P(None, None, "seq"),
            P(None, None, "seq"),
            P(None, "seq"),
            P(None, None, "seq"),
            P(None, "seq", None),
        ),
        out_specs=(
            P("section", None, "seq", None),
            P("section", None, "seq", None),
            P(None, "seq", None),
            P(None, "seq", None),
            P(None, "seq", None),
            P(None, "seq", None),
            P(None, None, "seq"),
            P(None, None, "seq"),
            P(None, "seq"),
            P(None, None, "seq"),
            P(),
        ),
        check_vma=False,
    )
```

```python
import jax
import jax.numpy as jnp
from jax import lax
from jax.experimental import pallas as pl
from jax.experimental.pallas import tpu as pltpu
from jax.sharding import PartitionSpec as P

D = 768
HEADS = 12
HEAD_DIM = 64
FF = 3072


WIDTHS = (2048, 4096, 8192, 16384, 32768)
RATIOS = (1, 2, 4, 6, 12)
EPSILON = 1e-05


def passed_along(value, axis, steps):
    count = lax.axis_size(axis)
    initial, last = (max(0, -steps), min(count, count - steps))
    return lax.ppermute(value, axis, [(source, source + steps) for source in range(initial, last)])


def norm_rows(inputs, gain_row, offset):
    center = inputs - jnp.mean(inputs, -1, keepdims=True)
    spread = jnp.mean(center * center, -1, keepdims=True)
    return center * lax.rsqrt(spread + EPSILON) * gain_row + offset


def place_rows(lengths, token_index):
    row_ends = jnp.cumsum(lengths)
    passed = token_index[:, None] >= row_ends[None, :]
    row_ids = jnp.sum(passed.astype(jnp.int32), 1)
    offsets = token_index - jnp.sum(jnp.where(passed, lengths[None, :], 0), 1)
    return (row_ids, offsets)


def query_chosen(query_pos):
    head_ids = jnp.arange(HEADS, dtype=jnp.int32)
    chosen = []
    for seg_width, seg_ratio in zip(WIDTHS, RATIOS):
        query_pick = query_pos % seg_width % seg_ratio
        chosen.append(query_pick[None, :] == (head_ids % seg_ratio)[:, None])
    return chosen


def pattern_allow(query_rows, query_pos, key_rows, key_pos):
    widths = jnp.array(WIDTHS, jnp.int32)[:, None]
    ratios = jnp.array(RATIOS, jnp.int32)[:, None]
    residue = jnp.arange(HEADS, dtype=jnp.int32)[None, :] % ratios
    query_mod = query_pos[None, :] % widths % ratios
    key_mod = key_pos[None, :] % widths % ratios
    query_ok = query_mod[:, None, :] == residue[:, :, None]
    key_ok = key_mod[:, None, :] == residue[:, :, None]
    common = (query_rows[:, None] == key_rows[None, :]) & (key_pos[None, :] <= query_pos[:, None])
    inside = common[None] & (
        (query_pos[None, :] // widths)[:, :, None] == (key_pos[None, :] // widths)[:, None, :]
    )
    return inside[:, None] & query_ok[:, :, :, None] & key_ok[:, :, None, :]


def block_rows(total_rows):
    step_rows = min(total_rows, 512)
    return step_rows


def split_heads(matrix):
    return matrix.reshape(matrix.shape[0], HEADS, HEAD_DIM)


def pair_terms(query_block, keys_block, query_rows, query_pos, key_rows, key_pos):
    scores = jnp.einsum(
        "qhe,khe->hqk", query_block, keys_block, preferred_element_type=jnp.float32
    ) * HEAD_DIM ** (-0.5)
    allowed = pattern_allow(query_rows, query_pos, key_rows, key_pos)
    counts = jnp.sum(allowed.astype(jnp.float32), 0)
    raised = jnp.exp(scores)
    return (raised, counts * raised, allowed)


def project_tokens(inputs, qkv_matrix, norm_gains, norm_biases):
    hidden = norm_rows(inputs, norm_gains[0], norm_biases[0]).astype(jnp.bfloat16)
    bias_row = jnp.concatenate(
        [jnp.zeros_like(norm_biases[3]), jnp.zeros_like(norm_biases[3]), norm_biases[3]]
    )
    projected = (jnp.dot(hidden, qkv_matrix, preferred_element_type=jnp.float32) + bias_row).astype(
        jnp.bfloat16
    )
    return (hidden, projected)


def attention_forward(section_in, projected, whole_keys, lengths, params, seq_index):
    out_matrix, norm_gains, norm_biases = (params[1], params[4], params[5])
    tok_rows = section_in.shape[0]
    inputs = section_in.astype(jnp.float32)
    queries = split_heads(projected[:, :D])
    query_rows, query_pos = place_rows(
        lengths, seq_index * tok_rows + jnp.arange(tok_rows, dtype=jnp.int32)
    )
    group_rows = whole_keys.shape[0]
    step_rows = block_rows(group_rows)

    def one_block(running, block_start):
        totals, pattern_sums, accumulated = running
        kv_block = lax.dynamic_slice_in_dim(whole_keys, block_start, step_rows, 0)
        key_rows, key_pos = place_rows(
            lengths, block_start + jnp.arange(step_rows, dtype=jnp.int32)
        )
        raised, weighted, allowed = pair_terms(
            queries, split_heads(kv_block[:, :D]), query_rows, query_pos, key_rows, key_pos
        )
        totals = totals + jnp.sum(weighted, -1)
        pattern_sums = pattern_sums + jnp.sum(jnp.where(allowed, raised[None], 0.0), -1)
        accumulated = accumulated + jnp.einsum(
            "hqk,khe->hqe",
            weighted.astype(jnp.bfloat16),
            split_heads(kv_block[:, D:]),
            preferred_element_type=jnp.float32,
        )
        return ((totals, pattern_sums, accumulated), None)

    start_sums = (
        jnp.zeros((HEADS, tok_rows), jnp.float32),
        jnp.zeros((len(WIDTHS), HEADS, tok_rows), jnp.float32),
        jnp.zeros((HEADS, tok_rows, HEAD_DIM), jnp.float32),
    )
    folded, unused = lax.scan(
        one_block, start_sums, jnp.arange(0, group_rows, step_rows, dtype=jnp.int32)
    )
    totals, pattern_sums, accumulated = folded
    attended = jnp.transpose(accumulated / totals[:, :, None], (1, 0, 2)).reshape(tok_rows, D)
    inner_norm = norm_rows(attended, norm_gains[1], norm_biases[1]).astype(jnp.bfloat16)
    branch = jnp.dot(inner_norm, out_matrix, preferred_element_type=jnp.float32) + norm_biases[4]
    section_out = (inputs + branch).astype(jnp.bfloat16)
    chosen = query_chosen(query_pos)
    log_terms = jnp.stack(
        [
            jnp.sum(
                jnp.where(pick_row, jnp.log(jnp.where(pick_row, pattern_sums[number], 1.0)), 0.0)
            )
            for number, pick_row in enumerate(chosen)
        ]
    )
    pick_counts = jnp.stack([jnp.sum(pick_row.astype(jnp.float32)) for pick_row in chosen])
    return (section_out, attended, totals, log_terms, pick_counts)


def feed_forward(section_in, params):
    up_matrix, down_matrix, norm_gains, norm_biases, hidden_gain, hidden_bias = (
        params[2],
        params[3],
        params[4],
        params[5],
        params[6],
        params[7],
    )
    tok_rows = section_in.shape[0]
    inputs = section_in.astype(jnp.float32)
    hidden = norm_rows(inputs, norm_gains[2], norm_biases[2]).astype(jnp.bfloat16)
    upward = jnp.dot(hidden, up_matrix, preferred_element_type=jnp.float32) + hidden_bias[0]
    inner_norm = norm_rows(
        jax.nn.gelu(upward, approximate=False), hidden_gain, hidden_bias[1]
    ).astype(jnp.bfloat16)
    branch = jnp.dot(inner_norm, down_matrix, preferred_element_type=jnp.float32) + norm_biases[5]
    section_out = (inputs + branch).astype(jnp.bfloat16)
    empty_terms = jnp.zeros((len(WIDTHS),), jnp.float32)
    return (
        section_out,
        jnp.zeros((tok_rows, D), jnp.float32),
        jnp.zeros((HEADS, tok_rows), jnp.float32),
        empty_terms,
        empty_terms,
    )


def attention_middle(
    section_in, grad_out, attended, totals, lengths, all_keys, projected, params, seq_index
):
    out_matrix, norm_gains, norm_biases = (params[1], params[4], params[5])
    scale_factor = HEAD_DIM ** (-0.5)
    tok_rows = section_in.shape[0]
    queries = split_heads(projected[:, :D])
    query_rows, query_pos = place_rows(
        lengths, seq_index * tok_rows + jnp.arange(tok_rows, dtype=jnp.int32)
    )
    inner_norm = norm_rows(attended, norm_gains[1], norm_biases[1]).astype(jnp.bfloat16)
    out_step = jnp.einsum("td,tf->df", inner_norm, grad_out, preferred_element_type=jnp.float32)
    inner_grad = jnp.einsum("tf,df->td", grad_out, out_matrix, preferred_element_type=jnp.float32)
    unused, inner_back = jax.vjp(norm_rows, attended, norm_gains[1], norm_biases[1])
    attended_grad, inner_gain_grad, inner_bias_grad = inner_back(inner_grad)
    low_attended = attended_grad.astype(jnp.bfloat16)
    head_grad = split_heads(low_attended)
    row_dots = jnp.einsum("qhe,qhe->hq", head_grad.astype(jnp.float32), split_heads(attended))
    scaled_grad = head_grad.astype(jnp.float32) / jnp.transpose(totals)[:, :, None]
    group_rows = all_keys.shape[0]
    step_rows = block_rows(group_rows)

    def grad_block(query_grad, block_start):
        kv_block = lax.dynamic_slice_in_dim(all_keys, block_start, step_rows, 0)
        keys_block = split_heads(kv_block[:, :D])
        values_block = split_heads(kv_block[:, D:])
        key_rows, key_pos = place_rows(
            lengths, block_start + jnp.arange(step_rows, dtype=jnp.int32)
        )
        raised, weighted, allowed = pair_terms(
            queries, keys_block, query_rows, query_pos, key_rows, key_pos
        )
        prob_grad = jnp.einsum(
            "qhe,khe->hqk", head_grad, values_block, preferred_element_type=jnp.float32
        )
        score_grad = (weighted / totals[:, :, None] * (prob_grad - row_dots[:, :, None])).astype(
            jnp.bfloat16
        )
        query_grad = (
            query_grad
            + jnp.einsum("hqk,khe->qhe", score_grad, keys_block, preferred_element_type=jnp.float32)
            * scale_factor
        )
        key_grad = (
            jnp.einsum("hqk,qhe->khe", score_grad, queries, preferred_element_type=jnp.float32)
            * scale_factor
        )
        value_grad = jnp.einsum(
            "hqk,qhe->khe",
            weighted.astype(jnp.bfloat16),
            scaled_grad,
            preferred_element_type=jnp.float32,
        )
        block_grad = jnp.concatenate(
            [key_grad.reshape(step_rows, D), value_grad.reshape(step_rows, D)], 1
        )
        return (query_grad, block_grad)

    query_grad, block_grads = lax.scan(
        grad_block,
        jnp.zeros((tok_rows, HEADS, HEAD_DIM), jnp.float32),
        jnp.arange(0, group_rows, step_rows, dtype=jnp.int32),
    )
    block_grads = block_grads.reshape(group_rows, 2 * D)
    return (
        query_grad.reshape(tok_rows, D),
        low_attended,
        row_dots,
        block_grads,
        out_step,
        inner_gain_grad,
        inner_bias_grad,
    )


def attention_finish(section_in, grad_out, middle, extra, params, grad_sums):
    qkv_matrix, norm_gains, norm_biases = (params[0], params[4], params[5])
    inputs = section_in.astype(jnp.float32)
    grad_float = grad_out.astype(jnp.float32)
    hidden = norm_rows(inputs, norm_gains[0], norm_biases[0]).astype(jnp.bfloat16)
    query_grad, low_attended, row_dots, block_grads, out_step, inner_gain_grad, inner_bias_grad = (
        middle
    )
    own_grads = extra[0]
    proj_grad = jnp.concatenate([query_grad, own_grads], 1).astype(jnp.bfloat16)
    qkv_step = jnp.einsum("td,tf->df", hidden, proj_grad, preferred_element_type=jnp.float32)
    value_bias_sums = jnp.sum(proj_grad[:, 2 * D :].astype(jnp.float32), 0)
    hidden_grad = jnp.einsum("tf,df->td", proj_grad, qkv_matrix, preferred_element_type=jnp.float32)
    unused_first, first_back = jax.vjp(norm_rows, inputs, norm_gains[0], norm_biases[0])
    input_grad, first_gain_grad, first_bias_grad = first_back(hidden_grad)
    qkv_sum, out_sum, up_sum, down_sum, gain_sum, bias_sum, hgain_sum, hbias_sum = grad_sums
    gain_sum = gain_sum.at[0].add(first_gain_grad).at[1].add(inner_gain_grad)
    bias_sum = (
        bias_sum.at[0]
        .add(first_bias_grad)
        .at[1]
        .add(inner_bias_grad)
        .at[3]
        .add(value_bias_sums)
        .at[4]
        .add(jnp.sum(grad_float, 0))
    )
    return (
        grad_float + input_grad,
        (
            qkv_sum + qkv_step,
            out_sum + out_step,
            up_sum,
            down_sum,
            gain_sum,
            bias_sum,
            hgain_sum,
            hbias_sum,
        ),
    )


def feed_backward(section_in, grad_out, params, grad_sums):
    up_matrix, down_matrix, norm_gains, norm_biases, hidden_gain, hidden_bias = (
        params[2],
        params[3],
        params[4],
        params[5],
        params[6],
        params[7],
    )
    inputs = section_in.astype(jnp.float32)
    grad_float = grad_out.astype(jnp.float32)
    hidden = norm_rows(inputs, norm_gains[2], norm_biases[2]).astype(jnp.bfloat16)
    upward = jnp.dot(hidden, up_matrix, preferred_element_type=jnp.float32) + hidden_bias[0]

    def inner_rows(upward_in, gain_row, bias_row):
        return norm_rows(jax.nn.gelu(upward_in, approximate=False), gain_row, bias_row)

    inner_value, inner_back = jax.vjp(inner_rows, upward, hidden_gain, hidden_bias[1])
    inner_norm = inner_value.astype(jnp.bfloat16)
    down_step = jnp.einsum("tf,td->fd", inner_norm, grad_out, preferred_element_type=jnp.float32)
    inner_grad = jnp.einsum("td,fd->tf", grad_out, down_matrix, preferred_element_type=jnp.float32)
    upward_grad, hgain_step, hbias_step = inner_back(inner_grad)
    low_upward = upward_grad.astype(jnp.bfloat16)
    up_step = jnp.einsum("td,tf->df", hidden, low_upward, preferred_element_type=jnp.float32)
    hidden_grad = jnp.einsum("tf,df->td", low_upward, up_matrix, preferred_element_type=jnp.float32)
    unused, first_back = jax.vjp(norm_rows, inputs, norm_gains[2], norm_biases[2])
    input_grad, first_gain_grad, first_bias_grad = first_back(hidden_grad)
    qkv_sum, out_sum, up_sum, down_sum, gain_sum, bias_sum, hgain_sum, hbias_sum = grad_sums
    gain_sum = gain_sum.at[2].add(first_gain_grad)
    bias_sum = bias_sum.at[2].add(first_bias_grad).at[5].add(jnp.sum(grad_float, 0))
    hbias_sum = (
        hbias_sum.at[0].add(jnp.sum(low_upward.astype(jnp.float32), 0)).at[1].add(hbias_step)
    )
    return (
        grad_float + input_grad,
        (
            qkv_sum,
            out_sum,
            up_sum + up_step,
            down_sum + down_step,
            gain_sum,
            bias_sum,
            hgain_sum + hgain_step,
            hbias_sum,
        ),
    )


def keep_slot(store, fresh, slot_id, in_range):
    previous = lax.dynamic_index_in_dim(store, slot_id, 0, False)
    return lax.dynamic_update_index_in_dim(store, jnp.where(in_range, fresh, previous), slot_id, 0)


def body(
    embeds,
    row_lengths,
    qkv_weight,
    out_weight,
    up_weight,
    down_weight,
    model_gains,
    model_biases,
    hidden_gains,
    hidden_biases,
    cotangent,
):
    section_id = lax.axis_index("section")
    seq_index = lax.axis_index("seq")
    section_count = lax.axis_size("section")
    micro_count = embeds.shape[0]
    tok_rows = embeds.shape[1]
    group_rows = tok_rows * lax.axis_size("seq")
    layer_id = section_id // 2
    attends = section_id % 2 == 0
    bias_count = model_biases.shape[1]

    def pick_layer(stacked):
        return lax.dynamic_index_in_dim(stacked, layer_id, 0, False)

    gathered = (
        lax.all_gather(pick_layer(qkv_weight), "seq", axis=0, tiled=True),
        lax.all_gather(pick_layer(out_weight), "seq", axis=0, tiled=True),
        lax.all_gather(pick_layer(up_weight), "seq", axis=0, tiled=True),
        lax.all_gather(pick_layer(down_weight), "seq", axis=0, tiled=True),
        lax.all_gather(pick_layer(model_gains), "seq", axis=1, tiled=True),
        lax.all_gather(pick_layer(model_biases), "seq", axis=1, tiled=True),
        lax.all_gather(pick_layer(hidden_gains), "seq", axis=0, tiled=True),
        lax.all_gather(pick_layer(hidden_biases), "seq", axis=1, tiled=True),
    )
    params = tuple(gathered[:4]) + tuple((vector.astype(jnp.float32) for vector in gathered[4:]))
    whole_shape = (0,)

    def make_projected(section_in):
        return project_tokens(section_in.astype(jnp.float32), params[0], params[4], params[5])[1]

    def skip_projected(section_in):
        return jnp.zeros((tok_rows, 3 * D), jnp.bfloat16)

    def run_attention(section_in, projected, whole_keys, lengths):
        return attention_forward(section_in, projected, whole_keys, lengths, params, seq_index)

    def run_feed(section_in, projected, whole_keys, lengths):
        return feed_forward(section_in, params)

    def forward_tick(running, tick_id):
        (
            incoming,
            kept_inputs,
            kept_attended,
            kept_totals,
            kept_whole,
            outputs,
            log_sums,
            pick_sums,
        ) = running
        micro_id = tick_id - section_id
        in_range = (micro_id >= 0) & (micro_id < micro_count)
        slot_id = jnp.clip(micro_id, 0, micro_count - 1)
        lengths = lax.dynamic_index_in_dim(row_lengths, slot_id, 0, False)
        section_in = jnp.where(
            section_id == 0, lax.dynamic_index_in_dim(embeds, slot_id, 0, False), incoming
        )
        projected = lax.cond(attends, make_projected, skip_projected, section_in)
        whole_keys = lax.all_gather(projected[:, D:], "seq", axis=0, tiled=True)
        section_out, attended, totals, log_terms, pick_counts = lax.cond(
            attends, run_attention, run_feed, section_in, projected, whole_keys, lengths
        )
        kept_inputs = keep_slot(kept_inputs, section_in, slot_id, in_range)
        kept_attended = keep_slot(kept_attended, attended, slot_id, in_range)
        kept_totals = keep_slot(kept_totals, totals, slot_id, in_range)
        outputs = keep_slot(outputs, section_out, slot_id, in_range)
        log_sums = log_sums + jnp.where(in_range, log_terms, 0.0)
        pick_sums = pick_sums + jnp.where(in_range, pick_counts, 0.0)
        incoming = passed_along(section_out, "section", 1)
        return (
            (
                incoming,
                kept_inputs,
                kept_attended,
                kept_totals,
                kept_whole,
                outputs,
                log_sums,
                pick_sums,
            ),
            None,
        )

    forward_start = (
        jnp.zeros((tok_rows, D), jnp.bfloat16),
        jnp.zeros((micro_count, tok_rows, D), jnp.bfloat16),
        jnp.zeros((micro_count, tok_rows, D), jnp.float32),
        jnp.zeros((micro_count, HEADS, tok_rows), jnp.float32),
        jnp.zeros((micro_count,) + whole_shape, jnp.bfloat16),
        jnp.zeros((micro_count, tok_rows, D), jnp.bfloat16),
        jnp.zeros((len(WIDTHS),), jnp.float32),
        jnp.zeros((len(WIDTHS),), jnp.float32),
    )
    ticks = jnp.arange(micro_count + section_count - 1, dtype=jnp.int32)
    forward_end, unused = lax.scan(forward_tick, forward_start, ticks)
    unused_in, kept_inputs, kept_attended, kept_totals, kept_whole, outputs, log_sums, pick_sums = (
        forward_end
    )
    block_shape = (group_rows, 2 * D)

    def middle_attention(section_in, grad_out, attended, totals, lengths, all_keys, projected):
        return attention_middle(
            section_in, grad_out, attended, totals, lengths, all_keys, projected, params, seq_index
        )

    def middle_feed(section_in, grad_out, attended, totals, lengths, all_keys, projected):
        return (
            jnp.zeros((tok_rows, D), jnp.float32),
            jnp.zeros((tok_rows, D), jnp.bfloat16),
            jnp.zeros((HEADS, tok_rows), jnp.float32),
            jnp.zeros(block_shape, jnp.float32),
            jnp.zeros((D, D), jnp.float32),
            jnp.zeros((D,), jnp.float32),
            jnp.zeros((D,), jnp.float32),
        )

    def finish_attention(section_in, grad_out, projected, middle, extra, lengths, grad_sums):
        return attention_finish(section_in, grad_out, middle, extra, params, grad_sums)

    def finish_feed(section_in, grad_out, projected, middle, extra, lengths, grad_sums):
        return feed_backward(section_in, grad_out, params, grad_sums)

    def backward_tick(running, tick_id):
        incoming, grad_sums, input_grads = running
        micro_id = micro_count - 1 - tick_id + (section_count - 1 - section_id)
        in_range = (micro_id >= 0) & (micro_id < micro_count)
        slot_id = jnp.clip(micro_id, 0, micro_count - 1)
        from_next = jnp.where(
            section_id == section_count - 1,
            lax.dynamic_index_in_dim(cotangent, slot_id, 0, False),
            incoming,
        )
        grad_out = jnp.where(in_range, from_next, jnp.zeros_like(from_next))
        section_in = lax.dynamic_index_in_dim(kept_inputs, slot_id, 0, False)
        attended = lax.dynamic_index_in_dim(kept_attended, slot_id, 0, False)
        totals = lax.dynamic_index_in_dim(kept_totals, slot_id, 0, False)
        lengths = lax.dynamic_index_in_dim(row_lengths, slot_id, 0, False)
        projected = lax.cond(attends, make_projected, skip_projected, section_in)
        all_keys = lax.all_gather(projected[:, D:], "seq", axis=0, tiled=True)
        middle = lax.cond(
            attends,
            middle_attention,
            middle_feed,
            section_in,
            grad_out,
            attended,
            totals,
            lengths,
            all_keys,
            projected,
        )
        extra = (lax.psum_scatter(middle[3], "seq", scatter_dimension=0, tiled=True),)
        section_grad, grad_sums = lax.cond(
            attends,
            finish_attention,
            finish_feed,
            section_in,
            grad_out,
            projected,
            middle,
            extra,
            lengths,
            grad_sums,
        )
        low_grad = section_grad.astype(jnp.bfloat16)
        input_grads = keep_slot(input_grads, low_grad, slot_id, in_range)
        incoming = passed_along(low_grad, "section", -1)
        return ((incoming, grad_sums, input_grads), None)

    grad_start = (
        jnp.zeros((D, 3 * D), jnp.float32),
        jnp.zeros((D, D), jnp.float32),
        jnp.zeros((D, FF), jnp.float32),
        jnp.zeros((FF, D), jnp.float32),
        jnp.zeros((3, D), jnp.float32),
        jnp.zeros((bias_count, D), jnp.float32),
        jnp.zeros((FF,), jnp.float32),
        jnp.zeros((2, FF), jnp.float32),
    )
    backward_start = (
        jnp.zeros((tok_rows, D), jnp.bfloat16),
        grad_start,
        jnp.zeros((micro_count, tok_rows, D), jnp.bfloat16),
    )
    backward_end, unused_back = lax.scan(backward_tick, backward_start, ticks)
    unused_grad, grad_sums, input_grads = backward_end
    shards = (
        lax.psum_scatter(grad_sums[0], "seq", scatter_dimension=0, tiled=True),
        lax.psum_scatter(grad_sums[1], "seq", scatter_dimension=0, tiled=True),
        lax.psum_scatter(grad_sums[2], "seq", scatter_dimension=0, tiled=True),
        lax.psum_scatter(grad_sums[3], "seq", scatter_dimension=0, tiled=True),
        lax.psum_scatter(grad_sums[4], "seq", scatter_dimension=1, tiled=True),
        lax.psum_scatter(grad_sums[5], "seq", scatter_dimension=1, tiled=True),
        lax.psum_scatter(grad_sums[6], "seq", scatter_dimension=0, tiled=True),
        lax.psum_scatter(grad_sums[7], "seq", scatter_dimension=1, tiled=True),
    )
    sources = (
        qkv_weight,
        out_weight,
        up_weight,
        down_weight,
        model_gains,
        model_biases,
        hidden_gains,
        hidden_biases,
    )
    placed = tuple(
        (
            lax.dynamic_update_index_in_dim(
                jnp.zeros(source.shape, jnp.float32), shard, layer_id, 0
            )
            for shard, source in zip(shards, sources)
        )
    )
    summed = (
        lax.psum(placed[0].astype(jnp.bfloat16), "section").astype(jnp.float32),
        lax.psum(placed[1].astype(jnp.bfloat16), "section").astype(jnp.float32),
        lax.psum(placed[2].astype(jnp.bfloat16), "section").astype(jnp.float32),
        lax.psum(placed[3].astype(jnp.bfloat16), "section").astype(jnp.float32),
        lax.psum(placed[4].astype(jnp.bfloat16), "section").astype(jnp.float32),
        lax.psum(placed[5].astype(jnp.bfloat16), "section").astype(jnp.float32),
        lax.psum(placed[6].astype(jnp.bfloat16), "section").astype(jnp.float32),
        lax.psum(placed[7].astype(jnp.bfloat16), "section").astype(jnp.float32),
    )
    layer_count = qkv_weight.shape[0]
    layer_terms = lax.dynamic_update_index_in_dim(
        jnp.zeros((layer_count, len(WIDTHS)), jnp.float32), log_sums, layer_id, 0
    )
    layer_picks = lax.dynamic_update_index_in_dim(
        jnp.zeros((layer_count, len(WIDTHS)), jnp.float32), pick_sums, layer_id, 0
    )
    log_totals, pick_totals = lax.psum((layer_terms, layer_picks), ("section", "seq"))
    pattern_means = log_totals / pick_totals
    return (
        outputs[None],
        input_grads[None],
        summed[0],
        summed[1],
        summed[2],
        summed[3],
        summed[4],
        summed[5],
        summed[6],
        summed[7],
        pattern_means,
    )


BF16 = jnp.bfloat16
F32 = jnp.float32
PAIRS = HEADS // 2
OWNERS = (0, 2, 3, 4, 5, 6)
TOKENS = 128
PAIR_LANES = 128
QUERY_STEP = 256
VEC_ROWS = 16
KERNEL_VMEM_BYTES = 64 * 1024 * 1024 - 65536
SCALE = HEAD_DIM ** (-0.5)


def mul(left, right):
    return lax.dot_general(left, right, (((1,), (0,)), ((), ())), preferred_element_type=F32)


def mul_nt(left, right):
    return lax.dot_general(left, right, (((1,), (1,)), ((), ())), preferred_element_type=F32)


def mul_tn(left, right):
    return lax.dot_general(left, right, (((0,), (0,)), ((), ())), preferred_element_type=F32)


def standardize(values):
    center = values - jnp.mean(values, -1, keepdims=True)
    rstd = lax.rsqrt(jnp.mean(center * center, -1, keepdims=True) + EPSILON)
    return (center * rstd, rstd)


def norm_back(unit, rstd, unit_grad):
    first = jnp.mean(unit_grad, -1, keepdims=True)
    second = jnp.mean(unit_grad * unit, -1, keepdims=True)
    return rstd * (unit_grad - first - unit * second)


def remote(source, target, send_sem, recv_sem, axis, peer):
    return pltpu.make_async_remote_copy(
        src_ref=source,
        dst_ref=target,
        send_sem=send_sem,
        recv_sem=recv_sem,
        device_id={axis: peer},
        device_id_type=pl.DeviceIdType.MESH,
    )


def greet(axis, peers):
    barrier = pltpu.get_barrier_semaphore()
    for peer in peers:
        pl.semaphore_signal(
            barrier, inc=1, device_id={axis: peer}, device_id_type=pl.DeviceIdType.MESH
        )
    pl.semaphore_wait(barrier, len(peers))


def seq_peers(me, count):
    return [lax.rem(me + step, count) for step in range(1, count)]


def plane_peers(me):
    return [
        me,
        me + 1 - 2 * lax.rem(me, 2),
        lax.rem(me + 2, 4),
        3 - me,
    ]


def rows_of(block, size=TOKENS):
    return pl.ds(pl.multiple_of(block * size, size), size)


def gelu_parts(values):
    below = 0.5 * (1.0 + lax.erf(values * (0.5**0.5)))
    return (values * below, below)


def share_stats(columns, send, recv, send_sem, recv_sem, peers):
    send[...] = columns.T[0:8, :]
    recv[0] = send[...]
    copies = [
        remote(send, recv.at[k], send_sem.at[k], recv_sem.at[k], "section", peers[k])
        for k in range(1, 4)
    ]
    for copy in copies:
        copy.start()
    return copies


def two_columns(first, second):
    lane = lax.broadcasted_iota(jnp.int32, (first.shape[0], PAIR_LANES), 1)
    return jnp.where(lane == 0, first, jnp.where(lane == 1, second, 0.0))


def slot_rows(k):
    return slice(k * TOKENS, (k + 1) * TOKENS)


def shaped(shape, kind):
    return jax.ShapeDtypeStruct(shape, kind)


class Named:
    def __init__(self, groups, refs):
        names = [name for group in groups for name in group]
        for name, ref in zip(names, refs, strict=True):
            setattr(self, name, ref)


GROUP_TOKENS = 8 * TOKENS
WIDE = 4 * TOKENS
SHARD = D // 8


def square(ref):
    return ref[...].reshape(D, D)


def remote_both(source, target, send_sem, recv_sem, section, seq):
    return pltpu.make_async_remote_copy(
        src_ref=source,
        dst_ref=target,
        send_sem=send_sem,
        recv_sem=recv_sem,
        device_id=(section, seq),
        device_id_type=pl.DeviceIdType.MESH,
    )


def greet_all(barrier, section, me):
    for other in range(4):
        for j in range(8):

            @pl.when((section != other) | (me != j))
            def _():
                pl.semaphore_signal(
                    barrier, inc=1, device_id=(other, j), device_id_type=pl.DeviceIdType.MESH
                )


class Place:
    def __init__(self):
        self.me = lax.axis_index("seq")
        self.section = lax.axis_index("section")
        self.peers = plane_peers(self.section)
        self.core = lax.rem(self.me, 2)
        self.chip = lax.div(self.me, 2)
        self.high = lax.div(self.chip, 2)
        self.low = lax.rem(self.chip, 2)
        self.sibling = self.me + 1 - 2 * self.core
        self.across = 2 * (2 * (1 - self.high) + self.low) + self.core
        self.next = 2 * (2 * self.high + 1 - self.low) + self.core
        self.is_owner = (self.me != 1) & (self.me != 7)
        pair = jnp.where(self.me == 0, 0, self.me - 1)
        self.my_pair = jnp.where(pair > PAIRS - 1, PAIRS - 1, pair)


class LineGather:
    def __init__(self, place, base, far_sems, near_sems, core_sems):
        self.place = place
        self.base = base
        self.far_sems = far_sems
        self.near_sems = near_sems
        self.core_sems = core_sems

    def far(self, high):
        p = self.place
        view = self.base.at[high, p.low, p.core]
        return remote(view, view, self.far_sems[0], self.far_sems[1], "seq", p.across)

    def near(self, low):
        p = self.place
        view = self.base.at[:, low, p.core]
        return remote(view, view, self.near_sems[0], self.near_sems[1], "seq", p.next)

    def cores(self, core):
        p = self.place
        view = self.base.at[:, :, core]
        return remote(view, view, self.core_sems[0], self.core_sems[1], "seq", p.sibling)

    def start(self):
        self.far(self.place.high).start()

    def pass_line(self):
        self.far(1 - self.place.high).wait_recv()
        self.near(self.place.low).start()

    def pass_core(self):
        self.near(1 - self.place.low).wait_recv()
        self.cores(self.place.core).start()

    def ready(self):
        self.cores(1 - self.place.core).wait_recv()

    def drain(self):
        self.far(self.place.high).wait_send()
        self.near(self.place.low).wait_send()
        self.cores(self.place.core).wait_send()


BOTH_VMEM = dict(model=0, hgains=0, hbiases=0)
BOTH_ANY = dict(embeds_in=0, qkv_w=0, out_w=0, up_w=0, down_w=0, cotangent_in=0)
BOTH_OUT = dict(
    sub_f_out=((4, TOKENS, D), BF16, False),
    sub_g_out=((4, TOKENS, D), BF16, False),
    all_m_out=((6, 4, SHARD, D), BF16, False),
    all_v_out=((2, 4, SHARD, PAIR_LANES), BF16, False),
    log_total=((8, PAIR_LANES), F32, True),
)
BOTH_SCRATCH = dict(
    embeds=((4, TOKENS, D), BF16),
    att=((2, TOKENS, D), BF16),
    picks=((2, GROUP_TOKENS, PAIR_LANES), BF16),
    wa=((2, 2, 2, 2, 2, SHARD, D), BF16),
    wf=((2, 2, 2, 2, 2, SHARD, D), BF16),
    qkv=((2, 3, GROUP_TOKENS, PAIR_LANES), BF16),
    pa=((2, GROUP_TOKENS, PAIR_LANES), F32),
    pt=((2, GROUP_TOKENS, PAIR_LANES), F32),
    hid=((2, WIDE, D), BF16),
    up=((2, WIDE, D), F32),
    stat=((2, WIDE, PAIR_LANES), F32),
    left=((2, WIDE, D), BF16),
    raw_up=((2, SHARD, FF), BF16),
    small_src=((2, 32, PAIR_LANES), BF16),
    small=((8, 2, 32, PAIR_LANES), BF16),
    inner=((TOKENS, D), BF16),
    vecs=((2, VEC_ROWS, D), F32),
    logs=((8, PAIR_LANES), F32),
    proj_send=((4, PAIRS, TOKENS, PAIR_LANES), BF16),
    att_send=((GROUP_TOKENS, PAIR_LANES), BF16),
    att_recv=((2, PAIRS, TOKENS, PAIR_LANES), BF16),
    columns=((WIDE, PAIR_LANES), F32),
    stat_rows=((PAIR_LANES, WIDE), F32),
    stat_send=((8, WIDE), F32),
    first_recv=((4, TOKENS, D), BF16),
    fstat_recv=((2, 4, 8, WIDE), F32),
    xs=((4, TOKENS, D), BF16),
    last_send=((4, TOKENS, D), BF16),
    last_recv=((4, TOKENS, D), BF16),
    last=((TOKENS, D), F32),
    streams=((4, TOKENS, D), BF16),
    grads=((WIDE, D), BF16),
    units=((WIDE, D), F32),
    unit_grads=((WIDE, D), F32),
    inners=((WIDE, D), BF16),
    lows=((WIDE, D), BF16),
    part_send=((4, TOKENS, D), BF16),
    part_recv=((4, TOKENS, D), BF16),
    stat_recv=((4, 8, WIDE), F32),
    do_send=((PAIRS, TOKENS, PAIR_LANES), BF16),
    do_recv=((GROUP_TOKENS, PAIR_LANES), BF16),
    key_sum=((GROUP_TOKENS, PAIR_LANES), F32),
    value_sum=((GROUP_TOKENS, PAIR_LANES), F32),
    d_send=((3, GROUP_TOKENS, PAIR_LANES), BF16),
    d_recv=((2, 4, PAIRS, TOKENS, PAIR_LANES), BF16),
    left_src=((TOKENS, D), BF16),
    right_src=((TOKENS, D), BF16),
    right=((2, WIDE, D), BF16),
    vec_rows=((2, PAIR_LANES, D), F32),
    hidden_grad=((TOKENS, D), F32),
    prod=((3, 2, 2, 2, SHARD, D), BF16),
    prod_v=((2, 2, 2, 2, SHARD, PAIR_LANES), BF16),
    pair=((6, 2, 2, SHARD, D), BF16),
    pair_v=((2, 2, 2, SHARD, PAIR_LANES), BF16),
    near=((6, 2, SHARD, D), BF16),
    near_v=((2, 2, SHARD, PAIR_LANES), BF16),
    far=((6, SHARD, D), BF16),
    far_v=((2, SHARD, PAIR_LANES), BF16),
    done=((6, SHARD, D), BF16),
    done_v=((2, SHARD, PAIR_LANES), BF16),
    line=((3, SHARD, D), BF16),
    log_line=((8, 8, PAIR_LANES), F32),
    log_plane=((4, 8, PAIR_LANES), F32),
)
BOTH_SEMS = dict(
    load_sem=(2, 3),
    embeds_sem=(4,),
    small_s=(8,),
    small_r=(8,),
    az_s=(4,),
    az_r=(4,),
    line_s=(6, 3),
    line_r=(6, 3),
    axy_s=(2, 4),
    axy_r=(2, 4),
    axs_s=(2, 4),
    axs_r=(2, 4),
    inner_s=(4,),
    inner_r=(4,),
    wide_s=(2, 4, PAIRS),
    wide_r=(2, 3, 8),
    att_s=(2, 8),
    att_r=(2, PAIRS),
    fhid_s=(2, 4),
    fhid_r=(2, 4),
    fstat_s=(2, 4),
    fstat_r=(2, 4),
    fleft_s=(4,),
    fleft_r=(4,),
    first_s=(4,),
    first_r=(4,),
    g_s=(2, 4),
    g_r=(2, 4),
    stat_s=(2, 4),
    stat_r=(2, 4),
    part_s=(2, 4),
    part_r=(2, 4),
    do_s=(2, PAIRS),
    do_r=(2, 8),
    d_s=(2, 3, 8),
    d_r=(2, 4, PAIRS),
    left_s=(2, 4),
    left_r=(2, 4),
    right_s=(2, 4),
    right_r=(2, 4),
    back_s=(2, 4),
    back_r=(2, 4),
    subf_s=(4,),
    subf_r=(4,),
    subg_s=(4,),
    subg_r=(4,),
    own_sem=(2,),
    last_s=(4,),
    last_r=(4,),
    cot_sem=(4,),
    pair_s=(8,),
    pair_r=(8,),
    near_s=(8,),
    near_r=(8,),
    far_s=(8,),
    far_r=(8,),
    all_s=(8, 4),
    all_r=(8, 4),
    log_s=(8,),
    log_r=(8,),
    log_plane_s=(4,),
    log_plane_r=(4,),
    third_sem=(4,),
    last_line_s=(4,),
    last_line_r=(4,),
)


def make_picks(lengths_ref, section, my_pair, picks_ref):
    tokens = lax.broadcasted_iota(jnp.int32, (GROUP_TOKENS, PAIR_LANES), 0)
    lane = lax.broadcasted_iota(jnp.int32, (GROUP_TOKENS, PAIR_LANES), 1)
    row_id = jnp.zeros_like(tokens)
    first = jnp.zeros_like(tokens)
    end = 0
    for row in range(lengths_ref.shape[1]):
        end = end + lengths_ref[section, row]
        passed = tokens >= end
        row_id = row_id + jnp.where(passed, 1, 0)
        first = jnp.where(passed, end, first)
    pos = (tokens - first).astype(F32)
    number = lax.shift_right_logical(lane, 2)
    row = lane - 4 * number
    ratio = jnp.zeros(lane.shape, F32)
    for i, each in enumerate(RATIOS):
        ratio = jnp.where(number == i, float(each), ratio)
    valid = ratio > 0.5
    ratio = jnp.where(valid, ratio, 1.0)

    def residue(values):
        return values - ratio * jnp.floor((values + 0.5) / ratio)

    residues = residue(pos)
    for head in range(2):
        wanted = residue(jnp.full(lane.shape, 2 * my_pair + head, jnp.int32).astype(F32))
        fits = valid & (row == row_id) & (jnp.abs(residues - wanted) < 0.5)
        picks_ref[head] = jnp.where(fits, 1.0, 0.0).astype(BF16)


def both_kernel(lengths, *refs):
    b = Named([BOTH_VMEM, BOTH_ANY, BOTH_OUT, BOTH_SCRATCH, BOTH_SEMS], refs)
    p = Place()
    me, section, peers, core = (p.me, p.section, p.peers, p.core)
    chip, high, low = (p.chip, p.high, p.low)
    out_slot = jnp.where(section == 3, 0, 1)

    barrier = pltpu.get_barrier_semaphore()
    greet_all(barrier, section, me)

    def block_from_qkv(layer):
        return pltpu.make_async_copy(
            b.qkv_w.at[layer, :, pl.ds(pl.multiple_of(lax.rem(section, 3) * D, D), D)],
            b.wa.at[layer, 0, high, low, core],
            b.load_sem.at[layer, 0],
        )

    def block_from_out(layer):
        return pltpu.make_async_copy(
            b.out_w.at[layer], b.wa.at[layer, 0, high, low, core], b.load_sem.at[layer, 0]
        )

    def load_up(layer):
        return pltpu.make_async_copy(b.up_w.at[layer], b.raw_up.at[layer], b.load_sem.at[layer, 1])

    def load_down(layer):
        return pltpu.make_async_copy(
            b.down_w.at[layer, pl.ds(pl.multiple_of(section * SHARD, SHARD), SHARD)],
            b.wf.at[layer, 1, high, low, core],
            b.load_sem.at[layer, 2],
        )

    def load_embeds(k):
        return pltpu.make_async_copy(
            b.embeds_in.at[peers[k]], b.embeds.at[k], b.embeds_sem.at[k]
        )

    for layer in range(2):

        @pl.when(section != 3)
        def _():
            block_from_qkv(layer).start()

        @pl.when(section == 3)
        def _():
            block_from_out(layer).start()

        if layer == 0:
            for k in range(4):
                load_embeds(k).start()
        load_up(layer).start()
        load_down(layer).start()

    def block_loaded(layer):
        @pl.when(section != 3)
        def _():
            block_from_qkv(layer).wait()

        @pl.when(section == 3)
        def _():
            block_from_out(layer).wait()

    def pick_up(layer):
        load_up(layer).wait()
        load_down(layer).wait()
        raw = b.raw_up[layer]
        for s in range(4):

            @pl.when(section == s)
            def _():
                b.wf[layer, 0, high, low, core] = jnp.concatenate(
                    [
                        raw[:, (4 * j + s) * SHARD : (4 * j + s + 1) * SHARD].astype(F32)
                        for j in range(8)
                    ],
                    1,
                ).astype(BF16)

    def line_gather(number, base):
        pairs = [(b.line_s.at[number, i], b.line_r.at[number, i]) for i in range(3)]
        return LineGather(p, base, *pairs)

    block = [line_gather(layer, b.wa.at[layer, 0]) for layer in range(2)]
    feed_lines = [
        [line_gather(2 + 2 * layer + which, b.wf.at[layer, which]) for which in range(2)]
        for layer in range(2)
    ]

    def first_z(step, source):
        view = b.wa.at[0, 0, lax.div(source, 2), lax.rem(source, 2), core]
        return remote(
            view,
            view,
            b.az_s.at[step],
            b.az_r.at[step],
            "seq",
            2 * lax.rem(chip + step, 4) + core,
        )

    def block_plane(layer, k):
        source = b.wa.at[layer, 0, :, :, core]
        target = b.wa.at[layer, 1, :, :, core]
        return remote(source, target, b.axy_s.at[layer, k], b.axy_r.at[layer, k], "section", peers[k])

    def block_across(layer, k, side):
        view = b.wa.at[layer, 1, :, :, side]
        return remote(view, view, b.axs_s.at[layer, k], b.axs_r.at[layer, k], "seq", p.sibling)

    for layer in range(2):
        model = b.model[layer].astype(F32)
        hidden_gain = b.hgains[layer : layer + 1, :].astype(F32)
        hidden_bias = b.hbiases[layer].astype(F32)
        lines = [model]
        for each in (hidden_gain, hidden_bias[0:1, :], hidden_bias[1:2, :]):
            for s in range(4):
                lines.append(each[:, s * SHARD : (s + 1) * SHARD])
        lines.append(jnp.zeros((11, SHARD), F32))
        packed = jnp.concatenate(lines, 0)
        packed = jnp.concatenate([packed, jnp.zeros((32, PAIR_LANES - SHARD), F32)], 1)
        b.small_src[layer] = packed.astype(BF16)
    b.small[me] = b.small_src[...]
    make_picks(lengths, section, p.my_pair, b.picks)
    b.logs[...] = jnp.zeros_like(b.logs)
    block_loaded(0)
    pl.semaphore_wait(barrier, 31)

    def small_copy(step):
        return remote(
            b.small_src,
            b.small.at[me],
            b.small_s.at[step],
            b.small_r.at[step],
            "seq",
            lax.rem(me + step, 8),
        )

    for step in range(1, 8):
        small_copy(step).start()
    for step in range(1, 4):
        first_z(step, chip).start()
    pick_up(0)
    for step in range(1, 8):
        source = lax.rem(me + 8 - step, 8)
        remote(
            b.small_src,
            b.small.at[source],
            b.small_s.at[step],
            b.small_r.at[step],
            "seq",
            source,
        ).wait_recv()
    for layer in range(2):
        pieces = []
        for j in range(8):
            small = b.small[j, layer].astype(F32)
            lines = [small[0:9]]
            for third in range(3):
                line = jnp.zeros((1, PAIR_LANES), F32)
                for s in range(4):
                    at = 9 + 4 * third + s
                    line = line + jnp.where(section == s, small[at : at + 1], 0.0)
                lines.append(line)
            lines.append(jnp.zeros((4, PAIR_LANES), F32))
            pieces.append(jnp.concatenate(lines, 0)[:, 0:SHARD])
        b.vecs[layer] = jnp.concatenate(pieces, 1)

    def owner_of(pair):
        return jnp.where(pair == 0, 0, pair + 1)

    def wide_turned(layer, k, step):
        pair = lax.rem(me + step, PAIRS)
        return (
            remote_both(
                b.proj_send.at[k, pair],
                b.qkv.at[layer, lax.rem(section, 3), rows_of(me)],
                b.wide_s.at[layer, k, pair],
                b.wide_r.at[layer, lax.rem(section, 3), me],
                peers[k],
                owner_of(pair),
            ),
            owner_of(pair),
        )

    def wide_copy(layer, k, pair):
        return remote_both(
            b.proj_send.at[k, pair],
            b.qkv.at[layer, lax.rem(section, 3), rows_of(me)],
            b.wide_s.at[layer, k, pair],
            b.wide_r.at[layer, lax.rem(section, 3), me],
            peers[k],
            OWNERS[pair],
        )

    def project(layer, arrive):
        vec = b.vecs.at[layer]

        @pl.when(section != 3)
        def _():
            bias = jnp.where(section == 2, vec[6:7, :], 0.0)
            for k in (3, 1, 2, 0) if layer == 0 else (0, 1, 2, 3):
                if k > 0:
                    arrive(k)
                part = mul(b.left[layer, slot_rows(k), :], square(b.wa.at[layer, 0])) + bias
                part = part.astype(BF16)
                for pair in range(PAIRS):
                    b.proj_send[k, pair] = part[:, pair * PAIR_LANES : (pair + 1) * PAIR_LANES]
                for step in range(PAIRS):
                    if k > 0:
                        wide_turned(layer, k, step)[0].start()
                    else:
                        owner = wide_turned(layer, k, step)[1]

                        @pl.when(me != owner)
                        def _():
                            wide_turned(layer, k, step)[0].start()

                if k == 0:

                    @pl.when(p.is_owner)
                    def _():
                        b.qkv[layer, section, rows_of(me), :] = b.proj_send[0, p.my_pair]

    def wait_projected(layer):
        @pl.when(p.is_owner)
        def _():
            for third in range(3):
                for source in range(8):

                    @pl.when((section != third) | (me != source))
                    def _():
                        remote_both(
                            b.proj_send.at[0, 0],
                            b.qkv.at[layer, third, pl.ds(source * TOKENS, TOKENS)],
                            b.wide_s.at[layer, 0, 0],
                            b.wide_r.at[layer, third, source],
                            third,
                            source,
                        ).wait_recv()

        @pl.when(section != 3)
        def _():
            for k in range(4):
                for pair, owner in enumerate(OWNERS):
                    if k > 0:
                        wide_copy(layer, k, pair).wait_send()
                    else:

                        @pl.when(me != owner)
                        def _():
                            wide_copy(layer, k, pair).wait_send()

    def back_copy(layer, target):
        return remote(
            b.att_send.at[pl.ds(target * TOKENS, TOKENS)],
            b.att_recv.at[layer, p.my_pair],
            b.att_s.at[layer, target],
            b.att_r.at[layer, p.my_pair],
            "seq",
            target,
        )

    def attend(layer):
        lane = lax.broadcasted_iota(jnp.int32, (QUERY_STEP, PAIR_LANES), 1)
        first_half = lane < HEAD_DIM
        for step in range(GROUP_TOKENS // QUERY_STEP):
            start = step * QUERY_STEP
            keys_end = start + QUERY_STEP
            rows = slice(start, keys_end)
            query = b.qkv[layer, 0, rows, :] * jnp.asarray(SCALE, BF16)
            keys = b.qkv[layer, 1, 0:keys_end, :]
            values = b.qkv[layer, 2, 0:keys_end, :]
            causal = lax.broadcasted_iota(jnp.int32, (QUERY_STEP, keys_end), 1) <= (
                start + lax.broadcasted_iota(jnp.int32, (QUERY_STEP, keys_end), 0)
            )
            sums = []
            totals = []
            logs = jnp.zeros((1, PAIR_LANES), F32)
            picked_sum = jnp.zeros((1, PAIR_LANES), F32)
            for head in range(2):
                mine = first_half if head == 0 else ~first_half
                own_query = jnp.where(mine, query, jnp.zeros_like(query))
                scores = mul_nt(own_query, keys)
                raised = jnp.where(causal, jnp.exp(scores), 0.0)
                pick_query = b.picks[head, rows, :]
                pick_keys = b.picks[head, 0:keys_end, :]
                counts = mul_nt(pick_query, pick_keys)
                weighted = (raised * counts).astype(BF16)
                sums.append(mul(weighted, values))
                pattern = mul(raised.astype(BF16), pick_keys)
                picked = pick_query.astype(F32)
                totals.append(jnp.sum(pattern * picked, -1, keepdims=True))
                chosen = picked > 0.5
                logs = logs + jnp.sum(
                    jnp.where(chosen, jnp.log(jnp.where(chosen, pattern, 1.0)), 0.0),
                    0,
                    keepdims=True,
                )
                picked_sum = picked_sum + jnp.sum(picked, 0, keepdims=True)
            b.logs[layer : layer + 1, :] += logs
            if layer == 0:
                b.logs[2:3, :] += picked_sum
            total = jnp.where(first_half, totals[0], totals[1])
            attended = jnp.where(first_half, sums[0], sums[1]) / total
            b.pa[layer, rows, :] = attended
            b.pt[layer, rows, :] = total
            b.att_send[rows, :] = attended.astype(BF16)
            for target in (2 * step, 2 * step + 1):

                @pl.when(me != target)
                def _():
                    back_copy(layer, target).start()

                @pl.when(me == target)
                def _():
                    b.att_recv[layer, p.my_pair] = b.att_send[
                        target * TOKENS : (target + 1) * TOKENS, :
                    ]

    def attention_rest(layer, inputs_ref, after):
        vec = b.vecs.at[layer]
        wait_projected(layer)
        feed_lines[layer][0].start()
        after()

        @pl.when(p.is_owner)
        def _():
            attend(layer)

        feed_lines[layer][0].pass_line()
        for k in range(1, 4):

            @pl.when(peers[k] == 3)
            def _():
                block_plane(layer, k).wait_recv()
                block_across(layer, k, core).start()

        for pair, owner in enumerate(OWNERS):

            @pl.when(me != owner)
            def _():
                remote(
                    b.att_send.at[pl.ds(0, TOKENS)],
                    b.att_recv.at[layer, pair],
                    b.att_s.at[layer, 0],
                    b.att_r.at[layer, pair],
                    "seq",
                    owner,
                ).wait_recv()

            b.att[layer, :, pair * PAIR_LANES : (pair + 1) * PAIR_LANES] = b.att_recv[layer, pair]
        inner_unit, unused = standardize(b.att[layer].astype(F32))
        inner = (inner_unit * vec[1:2, :] + vec[4:5, :]).astype(BF16)
        if layer == 0:
            b.inner[...] = inner
        for k in range(1, 4):

            @pl.when(peers[k] == 3)
            def _():
                block_across(layer, k, 1 - core).wait_recv()

        branch = mul(inner, square(b.wa.at[layer, out_slot])) + vec[7:8, :]
        b.xs[2 * layer] = (inputs_ref[...].astype(F32) + branch).astype(BF16)

    def attention_drain(layer):
        @pl.when(p.is_owner)
        def _():
            for target in range(8):

                @pl.when(me != target)
                def _():
                    back_copy(layer, target).wait_send()

    def feed(layer, resting, parting):
        vec = b.vecs.at[layer]
        inputs = b.xs[2 * layer].astype(F32)
        unit, unused = standardize(inputs)
        b.hid[layer, slot_rows(0), :] = (unit * vec[2:3, :] + vec[5:6, :]).astype(BF16)
        hidden_copies = [
            remote(
                b.hid.at[layer, pl.ds(0, TOKENS)],
                b.hid.at[layer, pl.ds(k * TOKENS, TOKENS)],
                b.fhid_s.at[layer, k],
                b.fhid_r.at[layer, k],
                "section",
                peers[k],
            )
            for k in range(1, 4)
        ]
        for copy in hidden_copies:
            copy.start()
        up_line, down_line = feed_lines[layer]
        down_line.start()
        up_line.pass_core()
        down_line.pass_line()
        up_line.ready()
        for k in range(4):
            if k > 0:
                hidden_copies[k - 1].wait_recv()
            upward = mul(b.hid[layer, slot_rows(k), :], square(b.wf.at[layer, 0])) + vec[10:11, :]
            b.up[layer, slot_rows(k), :] = upward
            values, unused = gelu_parts(upward)
            b.units[slot_rows(k), :] = values
            mean = jnp.mean(values, -1, keepdims=True)
            center = values - mean
            b.columns[slot_rows(k), :] = two_columns(
                mean, jnp.sum(center * center, -1, keepdims=True)
            )
        stat_copies = share_stats(
            b.columns[...],
            b.stat_send,
            b.fstat_recv.at[layer],
            b.fstat_s.at[layer],
            b.fstat_r.at[layer],
            peers,
        )
        down_line.pass_core()
        resting()
        for copy in stat_copies:
            copy.wait_recv()
        b.stat_rows[...] = jnp.zeros((PAIR_LANES, WIDE), F32)
        for k in range(4):
            means = [b.fstat_recv[layer, other, 0:1, slot_rows(k ^ other)] for other in range(4)]
            squares = [b.fstat_recv[layer, other, 1:2, slot_rows(k ^ other)] for other in range(4)]
            mean = (means[0] + means[1] + means[2] + means[3]) * 0.25
            spread = squares[0] + squares[1] + squares[2] + squares[3]
            for each in means:
                spread = spread + D * (each - mean) * (each - mean)
            b.stat_rows[0:1, slot_rows(k)] = mean
            b.stat_rows[1:2, slot_rows(k)] = lax.rsqrt(spread * (1.0 / FF) + EPSILON)
        b.stat[layer] = b.stat_rows[...].T
        down_line.ready()
        if layer == 1:
            parting()
            for copy in hidden_copies + stat_copies:
                copy.wait_send()
            return
        branch = None
        part_copies = []
        for k in (3, 1, 2, 0):
            both = b.stat[layer, slot_rows(k), :]
            inner = (
                (b.units[slot_rows(k), :] - both[:, 0:1]) * both[:, 1:2] * vec[9:10, :]
                + vec[11:12, :]
            ).astype(BF16)
            part = mul(inner, square(b.wf.at[layer, 1]))
            if k == 0:
                branch = part
            else:
                b.part_send[k] = part.astype(BF16)
                part_copies.append(
                    remote(
                        b.part_send.at[k],
                        b.first_recv.at[k],
                        b.first_s.at[k],
                        b.first_r.at[k],
                        "section",
                        peers[k],
                    )
                )
                part_copies[-1].start()
        parting()
        for k, copy in zip((3, 1, 2), part_copies):
            copy.wait_recv()
            branch = branch + b.first_recv[k].astype(F32)
        b.xs[2 * layer + 1] = (inputs + branch + vec[8:9, :]).astype(BF16)
        for copy in hidden_copies + stat_copies + part_copies:
            copy.wait_send()

    def sub_copies(number, forward):
        source = b.xs if forward else b.streams
        target = b.sub_f_out if forward else b.sub_g_out
        send_sem = b.subf_s if forward else b.subg_s
        recv_sem = b.subf_r if forward else b.subg_r

        def away():
            return remote(
                source.at[number],
                target.at[section],
                send_sem.at[number],
                recv_sem.at[section],
                "section",
                number,
            )

        def own():
            return pltpu.make_async_copy(
                source.at[number], target.at[section], b.own_sem.at[0 if forward else 1]
            )

        return away, own

    def send_sub(number, forward):
        @pl.when(section != number)
        def _():
            sub_copies(number, forward)[0]().start()

        @pl.when(section == number)
        def _():
            sub_copies(number, forward)[1]().start()

    def drain_sub(number, forward):
        @pl.when(section != number)
        def _():
            sub_copies(number, forward)[0]().wait_send()

        @pl.when(section == number)
        def _():
            sub_copies(number, forward)[1]().wait()

    def receive_sub(source, forward):
        target = b.sub_f_out if forward else b.sub_g_out

        @pl.when(section != source)
        def _():
            remote(
                b.streams.at[0],
                target.at[source],
                (b.subf_s if forward else b.subg_s).at[0],
                (b.subf_r if forward else b.subg_r).at[source],
                "section",
                source,
            ).wait_recv()

    for k in range(4):
        load_embeds(k).wait()

        @pl.when(section != 3)
        def _():
            unit, unused = standardize(b.embeds[k].astype(F32))
            b.left[0, slot_rows(k), :] = (
                unit * b.vecs[0, 0:1, :] + b.vecs[0, 3:4, :]
            ).astype(BF16)
    pick_up(1)
    for step in range(1, 4):
        first_z(step, lax.rem(chip + 4 - step, 4)).wait_recv()
    block[0].cores(core).start()

    @pl.when(section == 3)
    def _():
        for k in range(1, 4):
            block_plane(0, k).start()

    block[0].ready()
    project(0, lambda k: None)

    attention_rest(0, b.embeds.at[0], lambda: None)

    def resting_first():
        block_loaded(1)
        block[1].start()

    def parting_first():
        attention_drain(0)
        block[1].pass_line()

    feed(0, resting_first, parting_first)

    second = b.vecs.at[1]
    unit, unused = standardize(b.xs[1].astype(F32))
    b.left[1, slot_rows(0), :] = (unit * second[0:1, :] + second[3:4, :]).astype(BF16)

    def left_copy(k):
        return remote(
            b.left.at[1, pl.ds(0, TOKENS)],
            b.left.at[1, pl.ds(k * TOKENS, TOKENS)],
            b.fleft_s.at[k],
            b.fleft_r.at[k],
            "section",
            peers[k],
        )

    for k in (3, 1, 2):

        @pl.when(peers[k] != 3)
        def _():
            left_copy(k).start()

    block[1].pass_core()
    for k in range(1, 4):

        @pl.when(peers[k] != 3)
        def _():
            left_copy(k).wait_send()

    @pl.when(section == 3)
    def _():
        for k in range(1, 4):
            block_plane(1, k).start()

    block[1].ready()
    project(1, lambda k: left_copy(k).wait_recv())

    def inner_copy(k):
        return remote(
            b.inner,
            b.left.at[0, pl.ds(k * TOKENS, TOKENS)],
            b.inner_s.at[k],
            b.inner_r.at[k],
            "section",
            peers[k],
        )

    def after_second():
        for k in range(1, 4):

            @pl.when(peers[k] == 3)
            def _():
                inner_copy(k).start()

        @pl.when(section == 3)
        def _():
            b.left[0, slot_rows(0), :] = b.inner[...]

        send_sub(0, True)
        send_sub(1, True)

    attention_rest(1, b.xs.at[1], after_second)

    def resting_second():
        send_sub(2, True)
        for k in range(1, 4):

            @pl.when(peers[k] == 3)
            def _():
                inner_copy(k).wait_send()

        @pl.when(section == 3)
        def _():
            for k in range(1, 4):
                inner_copy(k).wait_recv()

    def parting_second():
        attention_drain(1)

    feed(1, resting_second, parting_second)

    def cotangent_load(k):
        return pltpu.make_async_copy(
            b.cotangent_in.at[peers[k]], b.grads.at[pl.ds(k * TOKENS, TOKENS)], b.cot_sem.at[k]
        )

    for k in range(4):
        cotangent_load(k).start()

    def log_copy(step):
        return remote(
            b.logs,
            b.log_line.at[me],
            b.log_s.at[step],
            b.log_r.at[step],
            "seq",
            lax.rem(me + step, 8),
        )

    def log_plane_copy(k, slot):
        return remote(
            b.log_plane.at[slot],
            b.log_plane.at[slot],
            b.log_plane_s.at[k],
            b.log_plane_r.at[k],
            "section",
            peers[k],
        )

    def start_logs():
        b.log_line[me] = b.logs[...]
        for step in range(1, 8):
            log_copy(step).start()

    def sum_logs():
        for step in range(1, 8):
            source = lax.rem(me + 8 - step, 8)
            remote(
                b.logs,
                b.log_line.at[source],
                b.log_s.at[step],
                b.log_r.at[step],
                "seq",
                source,
            ).wait_recv()
        total = b.log_line[0]
        for j in range(1, 8):
            total = total + b.log_line[j]
        b.log_plane[section] = total
        for k in range(1, 4):
            log_plane_copy(k, section).start()

    def finish_logs():
        for k in range(1, 4):
            log_plane_copy(k, peers[k]).wait_recv()
        total = b.log_plane[0]
        for other in range(1, 4):
            total = total + b.log_plane[other]
        b.log_total[...] = total
        for step in range(1, 8):
            log_copy(step).wait_send()
        for k in range(1, 4):
            log_plane_copy(k, section).wait_send()

    class Matrix:
        def __init__(self, number):
            self.number = number
            self.direct = number > 4
            self.turn = (1, 2) if number % 2 else (2, 1)
            self.j = number % 3 if number < 6 else number - 6
            if number < 6:
                self.i = number
                refs = (b.prod, b.pair, b.near, b.far, b.done, b.all_m_out)
            else:
                self.i = number - 6
                refs = (b.prod_v, b.pair_v, b.near_v, b.far_v, b.done_v, b.all_v_out)
            self.prod, self.pair, self.near, self.far, self.done, self.all = refs

        def store(self, value):
            if 3 <= self.number < 6:
                matrices[self.number - 3].sent()
            for j in range(8):
                self.prod[self.j, j % 2, j // 4, j // 2 % 2] = value[
                    j * SHARD : (j + 1) * SHARD, :
                ].astype(BF16)

        def pair_copy(self):
            n = self.number
            return remote(
                self.prod.at[self.j, 1 - core],
                self.pair.at[self.i],
                b.pair_s.at[n],
                b.pair_r.at[n],
                "seq",
                p.sibling,
            )

        def near_copy(self):
            n = self.number
            return remote(
                self.prod.at[self.j, core, :, 1 - low],
                self.near.at[self.i],
                b.near_s.at[n],
                b.near_r.at[n],
                "seq",
                p.next,
            )

        def far_copy(self):
            n = self.number
            return remote(
                self.prod.at[self.j, core, 1 - high, low],
                self.far.at[self.i],
                b.far_s.at[n],
                b.far_r.at[n],
                "seq",
                p.across,
            )

        def all_copy(self, k, slot):
            n = self.number
            return remote(
                self.done.at[self.i],
                self.all.at[self.i, slot],
                b.all_s.at[n, k],
                b.all_r.at[n, k],
                "section",
                peers[k],
            )

        def own_copy(self):
            return pltpu.make_async_copy(
                self.done.at[self.i], self.all.at[self.i, section], b.all_s.at[self.number, 0]
            )

        def step_near(self):
            self.pair_copy().wait_recv()
            i, at = (self.i, self.j)
            for h in range(2):
                for l in range(2):
                    self.prod[at, core, h, l] = (
                        self.prod[at, core, h, l].astype(F32) + self.pair[i, h, l].astype(F32)
                    ).astype(BF16)
            self.near_copy().start()

        def line_copy(self, step):
            target = lax.rem(chip + step, 4)
            return remote(
                self.prod.at[self.j, core, lax.div(target, 2), lax.rem(target, 2)],
                b.line.at[step - 1],
                b.last_line_s.at[step],
                b.last_line_r.at[step],
                "seq",
                2 * target + core,
            )

        def step_line(self):
            self.pair_copy().wait_recv()
            i, at = (self.i, self.j)
            for h in range(2):
                for l in range(2):
                    self.prod[at, core, h, l] = (
                        self.prod[at, core, h, l].astype(F32) + self.pair[i, h, l].astype(F32)
                    ).astype(BF16)
            for step in (2, 1, 3):
                self.line_copy(step).start()

        def step_line_plane(self):
            total = self.prod[self.j, core, high, low].astype(F32)
            for step in range(1, 4):
                self.line_copy(step).wait_recv()
                total = total + b.line[step - 1].astype(F32)
            self.done[self.i] = total.astype(BF16)
            for k in (3, 1, 2):
                self.all_copy(k, section).start()
            self.own_copy().start()

        def step_far(self):
            self.near_copy().wait_recv()
            i, at = (self.i, self.j)
            for h in range(2):
                self.prod[at, core, h, low] = (
                    self.prod[at, core, h, low].astype(F32) + self.near[i, h].astype(F32)
                ).astype(BF16)
            self.far_copy().start()

        def step_plane(self):
            self.far_copy().wait_recv()
            i = self.i
            self.done[i] = (
                self.prod[self.j, core, high, low].astype(F32) + self.far[i].astype(F32)
            ).astype(BF16)
            for k in (3, 1, 2) if self.direct else (1, 2):
                self.all_copy(k, section).start()
            self.own_copy().start()

        def turn_copy(self):
            n = self.number
            first, second = self.turn
            view = self.all.at[self.i, peers[first]]
            return remote(
                view, view, b.all_s.at[n, 3], b.all_r.at[n, 3], "section", peers[second]
            )

        def step_pass(self):
            first = self.turn[0]
            self.all_copy(first, peers[first]).wait_recv()
            self.turn_copy().start()

        def step_end(self):
            for k in range(1, 4):
                if self.direct or k != self.turn[0]:
                    self.all_copy(k, peers[k]).wait_recv()
                if self.direct or k != 3:
                    self.all_copy(k, section).wait_send()
                else:
                    self.turn_copy().wait_send()
            self.own_copy().wait()
            if self.number > 2:
                self.sent()

        def sent(self):
            self.pair_copy().wait_send()
            if self.number == 5:
                for step in range(1, 4):
                    self.line_copy(step).wait_send()
                return
            self.near_copy().wait_send()
            self.far_copy().wait_send()

    matrices = [Matrix(number) for number in range(8)]
    up1, down1, att1, up0, down0, att0, vec1, vec0 = matrices

    def last_copy(k):
        return remote(
            b.last_send.at[k],
            b.last_recv.at[k],
            b.last_s.at[k],
            b.last_r.at[k],
            "section",
            peers[k],
        )

    def start_last():
        for k in (3, 1, 2, 0):
            part = mul(b.inners[slot_rows(k), :], square(b.wf.at[1, 1]))
            if k == 0:
                b.last[...] = part
            else:
                b.last_send[k] = part.astype(BF16)
                last_copy(k).start()

    def finish_last():
        total = b.xs[2].astype(F32) + b.last[...] + b.vecs[1, 8:9, :]
        for k in range(1, 4):
            last_copy(k).wait_recv()
            total = total + b.last_recv[k].astype(F32)
        b.xs[3] = total.astype(BF16)
        for k in range(1, 4):
            last_copy(k).wait_send()

    def feed_phase(layer, grad_ref, x_ref, hooks):
        phase = 1 - layer
        vec = b.vecs.at[layer]
        rows = b.vec_rows.at[layer]
        up_matrix = matrices[3 * phase]
        down_matrix = matrices[3 * phase + 1]
        early, middle, parting, late = hooks
        if layer == 0:
            b.grads[slot_rows(0), :] = grad_ref[...]
        grad_copies = [] if layer == 1 else [
            remote(
                b.grads.at[pl.ds(0, TOKENS)],
                b.grads.at[pl.ds(k * TOKENS, TOKENS)],
                b.g_s.at[phase, k],
                b.g_r.at[phase, k],
                "section",
                peers[k],
            )
            for k in range(1, 4)
        ]
        if layer == 0:
            for k in (3, 1, 2):
                grad_copies[k - 1].start()
        rows[...] = jnp.zeros((PAIR_LANES, D), F32)
        early()
        for k in range(4):
            both = b.stat[layer, slot_rows(k), :]
            upward = b.up[layer, slot_rows(k), :]
            values, below = gelu_parts(upward)
            b.up[layer, slot_rows(k), :] = below + upward * (
                jnp.exp(-0.5 * upward * upward) * (0.5 / 3.141592653589793) ** 0.5
            )
            unit = (values - both[:, 0:1]) * both[:, 1:2]
            b.units[slot_rows(k), :] = unit
            b.inners[slot_rows(k), :] = (unit * vec[9:10, :] + vec[11:12, :]).astype(BF16)
        gain_sum = jnp.zeros((1, D), F32)
        bias_sum = jnp.zeros((1, D), F32)
        for k in range(4):
            if layer == 1:
                cotangent_load(k).wait()
            elif k > 0:
                if k == 3:
                    att1.step_far()
                    vec1.step_near()
                grad_copies[k - 1].wait_recv()
            unit = b.units[slot_rows(k), :]
            inner_grad = mul_nt(b.grads[slot_rows(k), :], square(b.wf.at[layer, 1]))
            gain_sum = gain_sum + jnp.sum(inner_grad * unit, 0, keepdims=True)
            bias_sum = bias_sum + jnp.sum(inner_grad, 0, keepdims=True)
            unit_grad = inner_grad * vec[9:10, :]
            b.unit_grads[slot_rows(k), :] = unit_grad
            b.columns[slot_rows(k), :] = two_columns(
                jnp.sum(unit_grad, -1, keepdims=True), jnp.sum(unit_grad * unit, -1, keepdims=True)
            )
        stat_copies = share_stats(
            b.columns[...],
            b.stat_send,
            b.stat_recv,
            b.stat_s.at[phase],
            b.stat_r.at[phase],
            peers,
        )
        rows[9:10, :] = gain_sum
        rows[11:12, :] = bias_sum
        down_matrix.store(mul_tn(b.inners[...], b.grads[...]))
        down_matrix.pair_copy().start()
        middle()
        for copy in stat_copies:
            copy.wait_recv()
        b.stat_rows[...] = jnp.zeros((PAIR_LANES, WIDE), F32)
        for k in range(4):
            for line in range(2):
                parts = [
                    b.stat_recv[other, line : line + 1, slot_rows(k ^ other)]
                    for other in range(4)
                ]
                b.stat_rows[line : line + 1, slot_rows(k)] = (
                    parts[0] + parts[1] + parts[2] + parts[3]
                ) * (1.0 / FF)
        b.columns[...] = b.stat_rows[...].T
        hidden_grad = None
        low_sum = jnp.zeros((1, D), F32)
        part_copies = []
        for k in (3, 1, 2, 0):
            rstd = b.stat[layer, slot_rows(k), :][:, 1:2]
            both = b.columns[slot_rows(k), :]
            lowered = (
                rstd
                * (
                    b.unit_grads[slot_rows(k), :]
                    - both[:, 0:1]
                    - b.units[slot_rows(k), :] * both[:, 1:2]
                )
                * b.up[layer, slot_rows(k), :]
            ).astype(BF16)
            b.lows[slot_rows(k), :] = lowered
            low_sum = low_sum + jnp.sum(lowered.astype(F32), 0, keepdims=True)
            part = mul_nt(lowered, square(b.wf.at[layer, 0]))
            if k == 0:
                hidden_grad = part
            else:
                b.part_send[k] = part.astype(BF16)
                part_copies.append(
                    remote(
                        b.part_send.at[k],
                        b.part_recv.at[k],
                        b.part_s.at[phase, k],
                        b.part_r.at[phase, k],
                        "section",
                        peers[k],
                    )
                )
                part_copies[-1].start()
        rows[10:11, :] = low_sum
        up_matrix.store(mul_tn(b.hid[layer], b.lows[...]))
        up_matrix.pair_copy().start()
        unit, rstd = standardize(x_ref[...].astype(F32))
        parting()
        for k, copy in zip((3, 1, 2), part_copies):
            copy.wait_recv()
            hidden_grad = hidden_grad + b.part_recv[k].astype(F32)
        grad = grad_ref[...].astype(F32)
        number = 2 * layer + 1
        b.streams[number] = (
            grad + norm_back(unit, rstd, hidden_grad * vec[2:3, :])
        ).astype(BF16)
        rows[2:3, :] = jnp.sum(hidden_grad * unit, 0, keepdims=True)
        rows[5:6, :] = jnp.sum(hidden_grad, 0, keepdims=True)
        rows[8:9, :] = jnp.sum(grad, 0, keepdims=True)
        for copy in grad_copies + stat_copies + part_copies:
            copy.wait_send()
        late()

    def attention_phase(layer, grad_ref, x_ref, att_ref, hooks):
        phase = 1 - layer
        vec = b.vecs.at[layer]
        rows = b.vec_rows.at[layer]
        before, inside, after, during = hooks
        grad = grad_ref[...]
        inner_unit, inner_rstd = standardize(att_ref[...].astype(F32))
        inner_grad = mul_nt(grad, square(b.wa.at[layer, out_slot]))
        att_grad = norm_back(inner_unit, inner_rstd, inner_grad * vec[1:2, :]).astype(BF16)
        for pair in range(PAIRS):
            b.do_send[pair] = att_grad[:, pair * PAIR_LANES : (pair + 1) * PAIR_LANES]

        def out_copy(pair):
            return remote(
                b.do_send.at[pair],
                b.do_recv.at[rows_of(me)],
                b.do_s.at[phase, pair],
                b.do_r.at[phase, me],
                "seq",
                OWNERS[pair],
            )

        for pair, owner in enumerate(OWNERS):

            @pl.when(me != owner)
            def _():
                out_copy(pair).start()

            @pl.when(me == owner)
            def _():
                b.do_recv[rows_of(me), :] = b.do_send[pair]

        def left_copy(k):
            return remote(
                b.left_src,
                b.left.at[layer, pl.ds(k * TOKENS, TOKENS)],
                b.left_s.at[phase, k],
                b.left_r.at[phase, k],
                "section",
                peers[k],
            )

        def right_copy(k):
            return remote(
                b.right_src,
                b.right.at[layer, pl.ds(k * TOKENS, TOKENS)],
                b.right_s.at[phase, k],
                b.right_r.at[phase, k],
                "section",
                peers[k],
            )

        unit, rstd = standardize(x_ref[...].astype(F32))
        if layer == 1:
            start_last()
        b.left_src[...] = (inner_unit * vec[1:2, :] + vec[4:5, :]).astype(BF16)
        b.right_src[...] = grad
        for k in range(1, 4):

            @pl.when(peers[k] == 3)
            def _():
                right_copy(k).start()
                if layer == 1:
                    left_copy(k).start()

        if layer == 1:

            @pl.when(section == 3)
            def _():
                b.left[layer, slot_rows(0), :] = b.left_src[...]

        rows[1:2, :] = jnp.sum(inner_grad * inner_unit, 0, keepdims=True)
        rows[4:5, :] = jnp.sum(inner_grad, 0, keepdims=True)
        rows[7:8, :] = jnp.sum(grad.astype(F32), 0, keepdims=True)

        def back_copy(third, target):
            return remote_both(
                b.d_send.at[third, pl.ds(target * TOKENS, TOKENS)],
                b.d_recv.at[layer, section, p.my_pair],
                b.d_s.at[phase, third, target],
                b.d_r.at[phase, section, p.my_pair],
                third,
                target,
            )

        @pl.when(p.is_owner)
        def _():
            for source in range(8):

                @pl.when(me != source)
                def _():
                    remote(
                        b.do_send.at[0],
                        b.do_recv.at[pl.ds(source * TOKENS, TOKENS)],
                        b.do_s.at[phase, 0],
                        b.do_r.at[phase, source],
                        "seq",
                        source,
                    ).wait_recv()

        before()

        @pl.when(p.is_owner)
        def _():
            b.key_sum[...] = jnp.zeros((GROUP_TOKENS, PAIR_LANES), F32)
            b.value_sum[...] = jnp.zeros((GROUP_TOKENS, PAIR_LANES), F32)
            lane = lax.broadcasted_iota(jnp.int32, (QUERY_STEP, PAIR_LANES), 1)
            first_half = lane < HEAD_DIM
            last_step = GROUP_TOKENS // QUERY_STEP - 1
            for step in (0,) + tuple(range(last_step, 0, -1)):
                start = step * QUERY_STEP
                keys_end = start + QUERY_STEP
                block = slice(start, keys_end)
                plain_query = b.qkv[layer, 0, block, :]
                query = plain_query * jnp.asarray(SCALE, BF16)
                keys = b.qkv[layer, 1, 0:keys_end, :]
                values = b.qkv[layer, 2, 0:keys_end, :]
                causal = lax.broadcasted_iota(jnp.int32, (QUERY_STEP, keys_end), 1) <= (
                    start + lax.broadcasted_iota(jnp.int32, (QUERY_STEP, keys_end), 0)
                )
                head_grad = b.do_recv[block, :]
                inverse = 1.0 / b.pt[layer, block, :]
                head_float = head_grad.astype(F32)
                products = head_float * b.pa[layer, block, :]
                scaled = (head_float * inverse).astype(BF16)
                key_lanes = lax.broadcasted_iota(jnp.int32, (keys_end, PAIR_LANES), 1) < HEAD_DIM
                query_parts = []
                key_parts = []
                value_parts = []
                for head in range(2):
                    mine = first_half if head == 0 else ~first_half
                    own_query = jnp.where(mine, query, jnp.zeros_like(query))
                    own_grad = jnp.where(mine, head_grad, jnp.zeros_like(head_grad))
                    delta = jnp.sum(jnp.where(mine, products, 0.0), -1, keepdims=True)
                    own_inverse = jnp.max(jnp.where(mine, inverse, 0.0), -1, keepdims=True)
                    counts = mul_nt(b.picks[head, block, :], b.picks[head, 0:keys_end, :])
                    scores = mul_nt(own_query, keys)
                    weighted = jnp.where(causal, jnp.exp(scores) * counts, 0.0)
                    prob_grad = mul_nt(own_grad, values)
                    score_grad = (weighted * own_inverse * (prob_grad - delta)).astype(BF16)
                    query_parts.append(mul(score_grad, keys))
                    key_parts.append(mul_tn(score_grad, plain_query))
                    value_parts.append(mul_tn(weighted.astype(BF16), scaled))
                b.key_sum[0:keys_end, :] += jnp.where(key_lanes, key_parts[0], key_parts[1])
                b.value_sum[0:keys_end, :] += jnp.where(key_lanes, value_parts[0], value_parts[1])
                query_grad = jnp.where(first_half, query_parts[0], query_parts[1]) * SCALE
                b.d_send[0, block, :] = query_grad.astype(BF16)
                ready = [(0, step)]
                if step > 0:
                    ready = [(0, step), (1, step), (2, step)]
                if step == 1:
                    ready = [(1, 0), (2, 0)] + ready
                for third, part in ready:
                    part_rows = slice(part * QUERY_STEP, (part + 1) * QUERY_STEP)
                    if third == 1:
                        b.d_send[1, part_rows, :] = (b.key_sum[part_rows, :] * SCALE).astype(BF16)
                    if third == 2:
                        b.d_send[2, part_rows, :] = b.value_sum[part_rows, :].astype(BF16)
                    for target in (2 * part, 2 * part + 1):
                        away = (section != third) | (me != target)

                        @pl.when(away)
                        def _():
                            back_copy(third, target).start()

                        @pl.when(~away)
                        def _():
                            b.d_recv[layer, section, p.my_pair] = b.d_send[
                                third, target * TOKENS : (target + 1) * TOKENS, :
                            ]

        inside()
        after()

        def part_copy(k):
            return remote(
                b.part_send.at[k],
                b.part_recv.at[k],
                b.back_s.at[phase, k],
                b.back_r.at[phase, k],
                "section",
                peers[k],
            )

        @pl.when(section != 3)
        def _():
            for k in (3, 2, 1, 0):
                for pair, owner in enumerate(OWNERS):
                    away = me != owner if k == 0 else True

                    @pl.when(away)
                    def _():
                        remote_both(
                            b.d_send.at[0, pl.ds(0, TOKENS)],
                            b.d_recv.at[layer, peers[k], pair],
                            b.d_s.at[phase, 0, 0],
                            b.d_r.at[phase, peers[k], pair],
                            peers[k],
                            owner,
                        ).wait_recv()

                    b.right[layer, slot_rows(k), pair * PAIR_LANES : (pair + 1) * PAIR_LANES] = (
                        b.d_recv[layer, peers[k], pair]
                    )
                part = mul_nt(b.right[layer, slot_rows(k), :], square(b.wa.at[layer, 0]))
                if k == 0:
                    b.hidden_grad[...] = part
                else:
                    b.part_send[k] = part.astype(BF16)
                    part_copy(k).start()

        @pl.when(section == 3)
        def _():
            b.right[layer, slot_rows(0), :] = b.right_src[...]
            b.hidden_grad[...] = jnp.zeros((TOKENS, D), F32)
            for k in range(1, 4):
                right_copy(k).wait_recv()
                if layer == 1:
                    left_copy(k).wait_recv()

        matrix = matrices[3 * phase + 2]
        matrix.store(mul_tn(b.left[layer], b.right[layer]))
        matrix.pair_copy().start()
        value_sum = jnp.sum(b.right[layer].astype(F32), 0, keepdims=True)
        rows[6:7, :] = jnp.where(section == 2, value_sum, 0.0)
        during()
        for k in (3, 1, 2):

            @pl.when(peers[k] != 3)
            def _():
                part_copy(k).wait_recv()
                b.hidden_grad[...] += b.part_recv[k].astype(F32)

        hidden_grad = b.hidden_grad[...]
        b.streams[2 * layer] = (
            grad.astype(F32) + norm_back(unit, rstd, hidden_grad * vec[0:1, :])
        ).astype(BF16)
        rows[0:1, :] = jnp.sum(hidden_grad * unit, 0, keepdims=True)
        rows[3:4, :] = jnp.sum(hidden_grad, 0, keepdims=True)

        def drain():
            @pl.when(section != 3)
            def _():
                for k in range(1, 4):
                    part_copy(k).wait_send()

            for k in range(1, 4):

                @pl.when(peers[k] == 3)
                def _():
                    right_copy(k).wait_send()
                    if layer == 1:
                        left_copy(k).wait_send()

            for pair, owner in enumerate(OWNERS):

                @pl.when(me != owner)
                def _():
                    out_copy(pair).wait_send()

            @pl.when(p.is_owner)
            def _():
                for third in range(3):
                    for target in range(8):

                        @pl.when((section != third) | (me != target))
                        def _():
                            back_copy(third, target).wait_send()

        return drain

    def nothing():
        pass

    def middle_first():
        start_logs()

    feed_phase(
        1,
        b.grads.at[pl.ds(0, TOKENS)],
        b.xs.at[2],
        (nothing, middle_first, down1.step_near, nothing),
    )

    def third_out(k):
        return pltpu.make_async_copy(
            b.right.at[1, pl.ds(k * TOKENS, TOKENS)], b.sub_g_out.at[peers[k]], b.third_sem.at[k]
        )

    def before_first():
        down1.step_far()

    def during_first():
        up1.step_far()
        down1.step_pass()
        finish_last()
        sum_logs()

    drain_first = attention_phase(
        1,
        b.streams.at[3],
        b.xs.at[1],
        b.att.at[1],
        (before_first, down1.step_plane, up1.step_near, during_first),
    )

    def early_second():
        vec1.store(b.vec_rows[1].T)
        vec1.pair_copy().start()
        drain_first()
        att1.step_near()

    def middle_second():
        up1.step_plane()
        down0.step_near()

    def late_second():
        att1.step_plane()
        send_sub(2, False)
        send_sub(1, False)

    def parting_second():
        down0.step_far()

    feed_phase(
        0,
        b.streams.at[2],
        b.xs.at[0],
        (early_second, middle_second, parting_second, late_second),
    )

    def before_second():
        up0.step_near()
        vec1.step_far()
        up1.step_pass()
        down0.step_plane()
        send_sub(3, True)

    def inside_second():
        up0.step_far()
        att1.step_pass()
        vec1.step_plane()
        down0.step_pass()
        @pl.when(section == 3)
        def _():
            for k in range(4):
                third_out(k).start()

        finish_logs()

    def during_second():
        att0.step_line()
        up0.step_plane()

    drain_second = attention_phase(
        0,
        b.streams.at[1],
        b.embeds.at[0],
        b.att.at[0],
        (before_second, inside_second, nothing, during_second),
    )
    vec0.store(b.vec_rows[0].T)
    vec0.pair_copy().start()
    send_sub(0, False)
    vec0.step_near()
    att0.step_line_plane()
    vec0.step_far()
    up0.step_pass()
    vec0.step_plane()
    drain_second()
    for matrix in (up1, down1, att1, vec1, down0, up0, vec0, att0):
        matrix.step_end()
    for number in range(3):
        drain_sub(number, False)

    @pl.when(section != 3)
    def _():
        for source in range(4):
            receive_sub(source, False)

    @pl.when(section == 3)
    def _():
        for k in range(4):
            third_out(k).wait()

    for number in range(4):
        drain_sub(number, True)
        receive_sub(number, True)
    for step in range(1, 8):
        small_copy(step).wait_send()
    for step in range(1, 4):
        first_z(step, chip).wait_send()
    block[0].cores(core).wait_send()
    block[1].drain()
    for layer in range(2):
        for line in feed_lines[layer]:
            line.drain()
        for k in range(1, 4):

            @pl.when(section == 3)
            def _():
                block_plane(layer, k).wait_send()

            @pl.when(peers[k] == 3)
            def _():
                block_across(layer, k, core).wait_send()


FINISH_IN = dict(all_m=0, all_v=0, sub_f=0, sub_g=0, log_total=0)
FINISH_OUT = dict(
    outputs=((1, 4, TOKENS, D), BF16, False),
    grads=((1, 4, TOKENS, D), BF16, False),
    qkv=((2, SHARD, 3 * D), F32, False),
    out=((2, SHARD, D), F32, False),
    up=((2, SHARD, FF), F32, False),
    down=((2, 4 * SHARD, D), F32, False),
    gains=((2, 3, SHARD), F32, True),
    biases=((2, 6, SHARD), F32, True),
    hgains=((2, 4 * SHARD), F32, True),
    hbiases=((2, 2, 4 * SHARD), F32, True),
    means=((2, 5), F32, True),
)
FINISH_SCRATCH = dict(
    matrix=((6, 4, SHARD, D), BF16),
    vectors=((2, 4, SHARD, PAIR_LANES), BF16),
    wide=((2, SHARD, 4 * D), F32),
    tall=((2, 4 * SHARD, D), F32),
    spread=((2, SHARD, FF), F32),
    first=((4, TOKENS, D), BF16),
    second=((4, TOKENS, D), BF16),
)
FINISH_SEMS = dict(load_sem=(9,), store_sem=(10,))


def finish_kernel(*refs):
    b = Named([FINISH_IN, FINISH_OUT, FINISH_SCRATCH, FINISH_SEMS], refs)
    loads = [
        pltpu.make_async_copy(b.all_m.at[i], b.matrix.at[i], b.load_sem.at[i]) for i in range(6)
    ] + [pltpu.make_async_copy(b.all_v, b.vectors, b.load_sem.at[6])]
    for copy in loads:
        copy.start()

    outputs_load = pltpu.make_async_copy(b.sub_f, b.first, b.load_sem.at[7])
    outputs_load.start()
    grads_load = pltpu.make_async_copy(b.sub_g, b.second, b.load_sem.at[8])
    grads_load.start()
    stores = []

    def store(source, target, number):
        copy = pltpu.make_async_copy(source, target, b.store_sem.at[number])
        copy.start()
        stores.append(copy)

    for layer in (1, 0):
        up_i = 3 * (1 - layer)
        loads[up_i].wait()
        for j in range(8):
            b.spread[layer, :, j * 4 * SHARD : (j + 1) * 4 * SHARD] = jnp.concatenate(
                [
                    b.matrix[up_i, source, :, j * SHARD : (j + 1) * SHARD].astype(F32)
                    for source in range(4)
                ],
                1,
            )
        store(b.spread.at[layer], b.up.at[layer], 4 * layer)
        loads[up_i + 1].wait()
        for source in range(4):
            b.tall[layer, source * SHARD : (source + 1) * SHARD, :] = b.matrix[
                up_i + 1, source
            ].astype(F32)
        store(b.tall.at[layer], b.down.at[layer], 4 * layer + 1)
        loads[up_i + 2].wait()
        for source in range(4):
            b.wide[layer, :, source * D : (source + 1) * D] = b.matrix[up_i + 2, source].astype(
                F32
            )
        store(b.wide.at[layer, :, pl.ds(0, 3 * D)], b.qkv.at[layer], 4 * layer + 2)
        store(b.wide.at[layer, :, pl.ds(3 * D, D)], b.out.at[layer], 4 * layer + 3)
    outputs_load.wait()
    store(b.first, b.outputs.at[0], 8)
    grads_load.wait()
    store(b.second, b.grads.at[0], 9)
    loads[6].wait()
    for layer in range(2):
        lines = []
        for source in range(4):
            tail = b.vectors[1 - layer, source].astype(F32)
            tail = jnp.concatenate([tail, jnp.zeros((PAIR_LANES - SHARD, PAIR_LANES), F32)], 0)
            lines.append(tail.T)
        model = lines[0] + lines[1] + lines[2] + lines[3]
        b.gains[layer] = model[0:3, 0:SHARD]
        b.biases[layer] = model[3:9, 0:SHARD]
        hidden = jnp.concatenate([each[9:12, 0:SHARD] for each in lines], 1)
        b.hgains[layer : layer + 1, :] = hidden[0:1, :]
        b.hbiases[layer] = hidden[1:3, :]
    lane = lax.broadcasted_iota(jnp.int32, (8, PAIR_LANES), 1)
    number = lax.shift_right_logical(lane, 2)
    sums = jnp.zeros((8, PAIR_LANES), F32)
    for i in range(5):
        part = jnp.sum(jnp.where(number == i, b.log_total[...], 0.0), -1, keepdims=True)
        sums = sums + jnp.where(lane == i, part, 0.0)
    means = sums[0:2, :] / jnp.where(lane[0:2, :] < 5, sums[2:3, :], 1.0)
    b.means[...] = means[:, 0:5]
    for copy in stores:
        copy.wait()


def run_remote(kernel, number, lengths, near, far, outs, scratch, sems):
    vmem = pl.BlockSpec(memory_space=pltpu.VMEM)
    anywhere = pl.BlockSpec(memory_space=pl.ANY)
    smem = pl.BlockSpec(memory_space=pltpu.SMEM)
    return pl.pallas_call(
        kernel,
        out_shape=[shaped(out[0], out[1]) for out in outs.values()],
        in_specs=[smem] * len(lengths) + [vmem] * len(near) + [anywhere] * len(far),
        out_specs=[vmem if out[2] else anywhere for out in outs.values()],
        scratch_shapes=[pltpu.VMEM(item[0], item[1]) for item in scratch.values()]
        + [pltpu.SemaphoreType.DMA(item) for item in sems.values()],
        compiler_params=pltpu.CompilerParams(
            collective_id=number, has_side_effects=True, vmem_limit_bytes=KERNEL_VMEM_BYTES
        ),
        cost_estimate=pl.CostEstimate(
            flops=10**10, bytes_accessed=100_000_000, transcendentals=0
        ),
    )(*lengths, *near, *far)


def run_finish(log_total, *far):
    vmem = pl.BlockSpec(memory_space=pltpu.VMEM)
    anywhere = pl.BlockSpec(memory_space=pl.ANY)
    return pl.pallas_call(
        finish_kernel,
        out_shape=[shaped(out[0], out[1]) for out in FINISH_OUT.values()],
        in_specs=[anywhere] * len(far) + [vmem],
        out_specs=[vmem if out[2] else anywhere for out in FINISH_OUT.values()],
        scratch_shapes=[pltpu.VMEM(item[0], item[1]) for item in FINISH_SCRATCH.values()]
        + [pltpu.SemaphoreType.DMA(item) for item in FINISH_SEMS.values()],
        compiler_params=pltpu.CompilerParams(vmem_limit_bytes=KERNEL_VMEM_BYTES),
    )(*far, log_total)


def quick_body(
    embeds,
    row_lengths,
    qkv_weight,
    out_weight,
    up_weight,
    down_weight,
    model_gains,
    model_biases,
    hidden_gains,
    hidden_biases,
    cotangent,
):
    both = Named(
        [BOTH_OUT],
        run_remote(
            both_kernel,
            10,
            (row_lengths,),
            (jnp.concatenate([model_gains, model_biases], 1), hidden_gains, hidden_biases),
            (embeds, qkv_weight, out_weight, up_weight, down_weight, cotangent),
            BOTH_OUT,
            BOTH_SCRATCH,
            BOTH_SEMS,
        ),
    )
    return tuple(
        run_finish(
            both.log_total,
            both.all_m_out,
            both.all_v_out,
            both.sub_f_out,
            both.sub_g_out,
        )
    )


def fits_quick(mesh):
    return mesh.shape["section"] == 4 and mesh.shape["seq"] == 8


def solution(mesh):
    return jax.shard_map(
        quick_body if fits_quick(mesh) else body,
        mesh=mesh,
        in_specs=(
            P(None, "seq", None),
            P(),
            P(None, "seq", None),
            P(None, "seq", None),
            P(None, "seq", None),
            P(None, "seq", None),
            P(None, None, "seq"),
            P(None, None, "seq"),
            P(None, "seq"),
            P(None, None, "seq"),
            P(None, "seq", None),
        ),
        out_specs=(
            P("section", None, "seq", None),
            P("section", None, "seq", None),
            P(None, "seq", None),
            P(None, "seq", None),
            P(None, "seq", None),
            P(None, "seq", None),
            P(None, None, "seq"),
            P(None, None, "seq"),
            P(None, "seq"),
            P(None, None, "seq"),
            P(),
        ),
        check_vma=False,
    )
```

```python
import jax
import jax.numpy as jnp
from jax import lax
from jax.experimental import pallas as pl
from jax.experimental.pallas import tpu as pltpu
from jax.sharding import PartitionSpec as P

D = 768
HEADS = 12
HEAD_DIM = 64
FF = 3072


WIDTHS = (2048, 4096, 8192, 16384, 32768)
RATIOS = (1, 2, 4, 6, 12)
EPSILON = 1e-05


def passed_along(value, axis, steps):
    count = lax.axis_size(axis)
    initial, last = (max(0, -steps), min(count, count - steps))
    return lax.ppermute(value, axis, [(source, source + steps) for source in range(initial, last)])


def norm_rows(inputs, gain_row, offset):
    center = inputs - jnp.mean(inputs, -1, keepdims=True)
    spread = jnp.mean(center * center, -1, keepdims=True)
    return center * lax.rsqrt(spread + EPSILON) * gain_row + offset


def place_rows(lengths, token_index):
    row_ends = jnp.cumsum(lengths)
    passed = token_index[:, None] >= row_ends[None, :]
    row_ids = jnp.sum(passed.astype(jnp.int32), 1)
    offsets = token_index - jnp.sum(jnp.where(passed, lengths[None, :], 0), 1)
    return (row_ids, offsets)


def query_chosen(query_pos):
    head_ids = jnp.arange(HEADS, dtype=jnp.int32)
    chosen = []
    for seg_width, seg_ratio in zip(WIDTHS, RATIOS):
        query_pick = query_pos % seg_width % seg_ratio
        chosen.append(query_pick[None, :] == (head_ids % seg_ratio)[:, None])
    return chosen


def pattern_allow(query_rows, query_pos, key_rows, key_pos):
    widths = jnp.array(WIDTHS, jnp.int32)[:, None]
    ratios = jnp.array(RATIOS, jnp.int32)[:, None]
    residue = jnp.arange(HEADS, dtype=jnp.int32)[None, :] % ratios
    query_mod = query_pos[None, :] % widths % ratios
    key_mod = key_pos[None, :] % widths % ratios
    query_ok = query_mod[:, None, :] == residue[:, :, None]
    key_ok = key_mod[:, None, :] == residue[:, :, None]
    common = (query_rows[:, None] == key_rows[None, :]) & (key_pos[None, :] <= query_pos[:, None])
    inside = common[None] & (
        (query_pos[None, :] // widths)[:, :, None] == (key_pos[None, :] // widths)[:, None, :]
    )
    return inside[:, None] & query_ok[:, :, :, None] & key_ok[:, :, None, :]


def block_rows(total_rows):
    step_rows = min(total_rows, 512)
    return step_rows


def split_heads(matrix):
    return matrix.reshape(matrix.shape[0], HEADS, HEAD_DIM)


def pair_terms(query_block, keys_block, query_rows, query_pos, key_rows, key_pos):
    scores = jnp.einsum(
        "qhe,khe->hqk", query_block, keys_block, preferred_element_type=jnp.float32
    ) * HEAD_DIM ** (-0.5)
    allowed = pattern_allow(query_rows, query_pos, key_rows, key_pos)
    counts = jnp.sum(allowed.astype(jnp.float32), 0)
    raised = jnp.exp(scores)
    return (raised, counts * raised, allowed)


def project_tokens(inputs, qkv_matrix, norm_gains, norm_biases):
    hidden = norm_rows(inputs, norm_gains[0], norm_biases[0]).astype(jnp.bfloat16)
    bias_row = jnp.concatenate(
        [jnp.zeros_like(norm_biases[3]), jnp.zeros_like(norm_biases[3]), norm_biases[3]]
    )
    projected = (jnp.dot(hidden, qkv_matrix, preferred_element_type=jnp.float32) + bias_row).astype(
        jnp.bfloat16
    )
    return (hidden, projected)


def attention_forward(section_in, projected, whole_keys, lengths, params, seq_index):
    out_matrix, norm_gains, norm_biases = (params[1], params[4], params[5])
    tok_rows = section_in.shape[0]
    inputs = section_in.astype(jnp.float32)
    queries = split_heads(projected[:, :D])
    query_rows, query_pos = place_rows(
        lengths, seq_index * tok_rows + jnp.arange(tok_rows, dtype=jnp.int32)
    )
    group_rows = whole_keys.shape[0]
    step_rows = block_rows(group_rows)

    def one_block(running, block_start):
        totals, pattern_sums, accumulated = running
        kv_block = lax.dynamic_slice_in_dim(whole_keys, block_start, step_rows, 0)
        key_rows, key_pos = place_rows(
            lengths, block_start + jnp.arange(step_rows, dtype=jnp.int32)
        )
        raised, weighted, allowed = pair_terms(
            queries, split_heads(kv_block[:, :D]), query_rows, query_pos, key_rows, key_pos
        )
        totals = totals + jnp.sum(weighted, -1)
        pattern_sums = pattern_sums + jnp.sum(jnp.where(allowed, raised[None], 0.0), -1)
        accumulated = accumulated + jnp.einsum(
            "hqk,khe->hqe",
            weighted.astype(jnp.bfloat16),
            split_heads(kv_block[:, D:]),
            preferred_element_type=jnp.float32,
        )
        return ((totals, pattern_sums, accumulated), None)

    start_sums = (
        jnp.zeros((HEADS, tok_rows), jnp.float32),
        jnp.zeros((len(WIDTHS), HEADS, tok_rows), jnp.float32),
        jnp.zeros((HEADS, tok_rows, HEAD_DIM), jnp.float32),
    )
    folded, unused = lax.scan(
        one_block, start_sums, jnp.arange(0, group_rows, step_rows, dtype=jnp.int32)
    )
    totals, pattern_sums, accumulated = folded
    attended = jnp.transpose(accumulated / totals[:, :, None], (1, 0, 2)).reshape(tok_rows, D)
    inner_norm = norm_rows(attended, norm_gains[1], norm_biases[1]).astype(jnp.bfloat16)
    branch = jnp.dot(inner_norm, out_matrix, preferred_element_type=jnp.float32) + norm_biases[4]
    section_out = (inputs + branch).astype(jnp.bfloat16)
    chosen = query_chosen(query_pos)
    log_terms = jnp.stack(
        [
            jnp.sum(
                jnp.where(pick_row, jnp.log(jnp.where(pick_row, pattern_sums[number], 1.0)), 0.0)
            )
            for number, pick_row in enumerate(chosen)
        ]
    )
    pick_counts = jnp.stack([jnp.sum(pick_row.astype(jnp.float32)) for pick_row in chosen])
    return (section_out, attended, totals, log_terms, pick_counts)


def feed_forward(section_in, params):
    up_matrix, down_matrix, norm_gains, norm_biases, hidden_gain, hidden_bias = (
        params[2],
        params[3],
        params[4],
        params[5],
        params[6],
        params[7],
    )
    tok_rows = section_in.shape[0]
    inputs = section_in.astype(jnp.float32)
    hidden = norm_rows(inputs, norm_gains[2], norm_biases[2]).astype(jnp.bfloat16)
    upward = jnp.dot(hidden, up_matrix, preferred_element_type=jnp.float32) + hidden_bias[0]
    inner_norm = norm_rows(
        jax.nn.gelu(upward, approximate=False), hidden_gain, hidden_bias[1]
    ).astype(jnp.bfloat16)
    branch = jnp.dot(inner_norm, down_matrix, preferred_element_type=jnp.float32) + norm_biases[5]
    section_out = (inputs + branch).astype(jnp.bfloat16)
    empty_terms = jnp.zeros((len(WIDTHS),), jnp.float32)
    return (
        section_out,
        jnp.zeros((tok_rows, D), jnp.float32),
        jnp.zeros((HEADS, tok_rows), jnp.float32),
        empty_terms,
        empty_terms,
    )


def attention_middle(
    section_in, grad_out, attended, totals, lengths, all_keys, projected, params, seq_index
):
    out_matrix, norm_gains, norm_biases = (params[1], params[4], params[5])
    scale_factor = HEAD_DIM ** (-0.5)
    tok_rows = section_in.shape[0]
    queries = split_heads(projected[:, :D])
    query_rows, query_pos = place_rows(
        lengths, seq_index * tok_rows + jnp.arange(tok_rows, dtype=jnp.int32)
    )
    inner_norm = norm_rows(attended, norm_gains[1], norm_biases[1]).astype(jnp.bfloat16)
    out_step = jnp.einsum("td,tf->df", inner_norm, grad_out, preferred_element_type=jnp.float32)
    inner_grad = jnp.einsum("tf,df->td", grad_out, out_matrix, preferred_element_type=jnp.float32)
    unused, inner_back = jax.vjp(norm_rows, attended, norm_gains[1], norm_biases[1])
    attended_grad, inner_gain_grad, inner_bias_grad = inner_back(inner_grad)
    low_attended = attended_grad.astype(jnp.bfloat16)
    head_grad = split_heads(low_attended)
    row_dots = jnp.einsum("qhe,qhe->hq", head_grad.astype(jnp.float32), split_heads(attended))
    scaled_grad = head_grad.astype(jnp.float32) / jnp.transpose(totals)[:, :, None]
    group_rows = all_keys.shape[0]
    step_rows = block_rows(group_rows)

    def grad_block(query_grad, block_start):
        kv_block = lax.dynamic_slice_in_dim(all_keys, block_start, step_rows, 0)
        keys_block = split_heads(kv_block[:, :D])
        values_block = split_heads(kv_block[:, D:])
        key_rows, key_pos = place_rows(
            lengths, block_start + jnp.arange(step_rows, dtype=jnp.int32)
        )
        raised, weighted, allowed = pair_terms(
            queries, keys_block, query_rows, query_pos, key_rows, key_pos
        )
        prob_grad = jnp.einsum(
            "qhe,khe->hqk", head_grad, values_block, preferred_element_type=jnp.float32
        )
        score_grad = (weighted / totals[:, :, None] * (prob_grad - row_dots[:, :, None])).astype(
            jnp.bfloat16
        )
        query_grad = (
            query_grad
            + jnp.einsum("hqk,khe->qhe", score_grad, keys_block, preferred_element_type=jnp.float32)
            * scale_factor
        )
        key_grad = (
            jnp.einsum("hqk,qhe->khe", score_grad, queries, preferred_element_type=jnp.float32)
            * scale_factor
        )
        value_grad = jnp.einsum(
            "hqk,qhe->khe",
            weighted.astype(jnp.bfloat16),
            scaled_grad,
            preferred_element_type=jnp.float32,
        )
        block_grad = jnp.concatenate(
            [key_grad.reshape(step_rows, D), value_grad.reshape(step_rows, D)], 1
        )
        return (query_grad, block_grad)

    query_grad, block_grads = lax.scan(
        grad_block,
        jnp.zeros((tok_rows, HEADS, HEAD_DIM), jnp.float32),
        jnp.arange(0, group_rows, step_rows, dtype=jnp.int32),
    )
    block_grads = block_grads.reshape(group_rows, 2 * D)
    return (
        query_grad.reshape(tok_rows, D),
        low_attended,
        row_dots,
        block_grads,
        out_step,
        inner_gain_grad,
        inner_bias_grad,
    )


def attention_finish(section_in, grad_out, middle, extra, params, grad_sums):
    qkv_matrix, norm_gains, norm_biases = (params[0], params[4], params[5])
    inputs = section_in.astype(jnp.float32)
    grad_float = grad_out.astype(jnp.float32)
    hidden = norm_rows(inputs, norm_gains[0], norm_biases[0]).astype(jnp.bfloat16)
    query_grad, low_attended, row_dots, block_grads, out_step, inner_gain_grad, inner_bias_grad = (
        middle
    )
    own_grads = extra[0]
    proj_grad = jnp.concatenate([query_grad, own_grads], 1).astype(jnp.bfloat16)
    qkv_step = jnp.einsum("td,tf->df", hidden, proj_grad, preferred_element_type=jnp.float32)
    value_bias_sums = jnp.sum(proj_grad[:, 2 * D :].astype(jnp.float32), 0)
    hidden_grad = jnp.einsum("tf,df->td", proj_grad, qkv_matrix, preferred_element_type=jnp.float32)
    unused_first, first_back = jax.vjp(norm_rows, inputs, norm_gains[0], norm_biases[0])
    input_grad, first_gain_grad, first_bias_grad = first_back(hidden_grad)
    qkv_sum, out_sum, up_sum, down_sum, gain_sum, bias_sum, hgain_sum, hbias_sum = grad_sums
    gain_sum = gain_sum.at[0].add(first_gain_grad).at[1].add(inner_gain_grad)
    bias_sum = (
        bias_sum.at[0]
        .add(first_bias_grad)
        .at[1]
        .add(inner_bias_grad)
        .at[3]
        .add(value_bias_sums)
        .at[4]
        .add(jnp.sum(grad_float, 0))
    )
    return (
        grad_float + input_grad,
        (
            qkv_sum + qkv_step,
            out_sum + out_step,
            up_sum,
            down_sum,
            gain_sum,
            bias_sum,
            hgain_sum,
            hbias_sum,
        ),
    )


def feed_backward(section_in, grad_out, params, grad_sums):
    up_matrix, down_matrix, norm_gains, norm_biases, hidden_gain, hidden_bias = (
        params[2],
        params[3],
        params[4],
        params[5],
        params[6],
        params[7],
    )
    inputs = section_in.astype(jnp.float32)
    grad_float = grad_out.astype(jnp.float32)
    hidden = norm_rows(inputs, norm_gains[2], norm_biases[2]).astype(jnp.bfloat16)
    upward = jnp.dot(hidden, up_matrix, preferred_element_type=jnp.float32) + hidden_bias[0]

    def inner_rows(upward_in, gain_row, bias_row):
        return norm_rows(jax.nn.gelu(upward_in, approximate=False), gain_row, bias_row)

    inner_value, inner_back = jax.vjp(inner_rows, upward, hidden_gain, hidden_bias[1])
    inner_norm = inner_value.astype(jnp.bfloat16)
    down_step = jnp.einsum("tf,td->fd", inner_norm, grad_out, preferred_element_type=jnp.float32)
    inner_grad = jnp.einsum("td,fd->tf", grad_out, down_matrix, preferred_element_type=jnp.float32)
    upward_grad, hgain_step, hbias_step = inner_back(inner_grad)
    low_upward = upward_grad.astype(jnp.bfloat16)
    up_step = jnp.einsum("td,tf->df", hidden, low_upward, preferred_element_type=jnp.float32)
    hidden_grad = jnp.einsum("tf,df->td", low_upward, up_matrix, preferred_element_type=jnp.float32)
    unused, first_back = jax.vjp(norm_rows, inputs, norm_gains[2], norm_biases[2])
    input_grad, first_gain_grad, first_bias_grad = first_back(hidden_grad)
    qkv_sum, out_sum, up_sum, down_sum, gain_sum, bias_sum, hgain_sum, hbias_sum = grad_sums
    gain_sum = gain_sum.at[2].add(first_gain_grad)
    bias_sum = bias_sum.at[2].add(first_bias_grad).at[5].add(jnp.sum(grad_float, 0))
    hbias_sum = (
        hbias_sum.at[0].add(jnp.sum(low_upward.astype(jnp.float32), 0)).at[1].add(hbias_step)
    )
    return (
        grad_float + input_grad,
        (
            qkv_sum,
            out_sum,
            up_sum + up_step,
            down_sum + down_step,
            gain_sum,
            bias_sum,
            hgain_sum + hgain_step,
            hbias_sum,
        ),
    )


def keep_slot(store, fresh, slot_id, in_range):
    previous = lax.dynamic_index_in_dim(store, slot_id, 0, False)
    return lax.dynamic_update_index_in_dim(store, jnp.where(in_range, fresh, previous), slot_id, 0)


def body(
    embeds,
    row_lengths,
    qkv_weight,
    out_weight,
    up_weight,
    down_weight,
    model_gains,
    model_biases,
    hidden_gains,
    hidden_biases,
    cotangent,
):
    section_id = lax.axis_index("section")
    seq_index = lax.axis_index("seq")
    section_count = lax.axis_size("section")
    micro_count = embeds.shape[0]
    tok_rows = embeds.shape[1]
    group_rows = tok_rows * lax.axis_size("seq")
    layer_id = section_id // 2
    attends = section_id % 2 == 0
    bias_count = model_biases.shape[1]

    def pick_layer(stacked):
        return lax.dynamic_index_in_dim(stacked, layer_id, 0, False)

    gathered = (
        lax.all_gather(pick_layer(qkv_weight), "seq", axis=0, tiled=True),
        lax.all_gather(pick_layer(out_weight), "seq", axis=0, tiled=True),
        lax.all_gather(pick_layer(up_weight), "seq", axis=0, tiled=True),
        lax.all_gather(pick_layer(down_weight), "seq", axis=0, tiled=True),
        lax.all_gather(pick_layer(model_gains), "seq", axis=1, tiled=True),
        lax.all_gather(pick_layer(model_biases), "seq", axis=1, tiled=True),
        lax.all_gather(pick_layer(hidden_gains), "seq", axis=0, tiled=True),
        lax.all_gather(pick_layer(hidden_biases), "seq", axis=1, tiled=True),
    )
    params = tuple(gathered[:4]) + tuple((vector.astype(jnp.float32) for vector in gathered[4:]))
    whole_shape = (0,)

    def make_projected(section_in):
        return project_tokens(section_in.astype(jnp.float32), params[0], params[4], params[5])[1]

    def skip_projected(section_in):
        return jnp.zeros((tok_rows, 3 * D), jnp.bfloat16)

    def run_attention(section_in, projected, whole_keys, lengths):
        return attention_forward(section_in, projected, whole_keys, lengths, params, seq_index)

    def run_feed(section_in, projected, whole_keys, lengths):
        return feed_forward(section_in, params)

    def forward_tick(running, tick_id):
        (
            incoming,
            kept_inputs,
            kept_attended,
            kept_totals,
            kept_whole,
            outputs,
            log_sums,
            pick_sums,
        ) = running
        micro_id = tick_id - section_id
        in_range = (micro_id >= 0) & (micro_id < micro_count)
        slot_id = jnp.clip(micro_id, 0, micro_count - 1)
        lengths = lax.dynamic_index_in_dim(row_lengths, slot_id, 0, False)
        section_in = jnp.where(
            section_id == 0, lax.dynamic_index_in_dim(embeds, slot_id, 0, False), incoming
        )
        projected = lax.cond(attends, make_projected, skip_projected, section_in)
        whole_keys = lax.all_gather(projected[:, D:], "seq", axis=0, tiled=True)
        section_out, attended, totals, log_terms, pick_counts = lax.cond(
            attends, run_attention, run_feed, section_in, projected, whole_keys, lengths
        )
        kept_inputs = keep_slot(kept_inputs, section_in, slot_id, in_range)
        kept_attended = keep_slot(kept_attended, attended, slot_id, in_range)
        kept_totals = keep_slot(kept_totals, totals, slot_id, in_range)
        outputs = keep_slot(outputs, section_out, slot_id, in_range)
        log_sums = log_sums + jnp.where(in_range, log_terms, 0.0)
        pick_sums = pick_sums + jnp.where(in_range, pick_counts, 0.0)
        incoming = passed_along(section_out, "section", 1)
        return (
            (
                incoming,
                kept_inputs,
                kept_attended,
                kept_totals,
                kept_whole,
                outputs,
                log_sums,
                pick_sums,
            ),
            None,
        )

    forward_start = (
        jnp.zeros((tok_rows, D), jnp.bfloat16),
        jnp.zeros((micro_count, tok_rows, D), jnp.bfloat16),
        jnp.zeros((micro_count, tok_rows, D), jnp.float32),
        jnp.zeros((micro_count, HEADS, tok_rows), jnp.float32),
        jnp.zeros((micro_count,) + whole_shape, jnp.bfloat16),
        jnp.zeros((micro_count, tok_rows, D), jnp.bfloat16),
        jnp.zeros((len(WIDTHS),), jnp.float32),
        jnp.zeros((len(WIDTHS),), jnp.float32),
    )
    ticks = jnp.arange(micro_count + section_count - 1, dtype=jnp.int32)
    forward_end, unused = lax.scan(forward_tick, forward_start, ticks)
    unused_in, kept_inputs, kept_attended, kept_totals, kept_whole, outputs, log_sums, pick_sums = (
        forward_end
    )
    block_shape = (group_rows, 2 * D)

    def middle_attention(section_in, grad_out, attended, totals, lengths, all_keys, projected):
        return attention_middle(
            section_in, grad_out, attended, totals, lengths, all_keys, projected, params, seq_index
        )

    def middle_feed(section_in, grad_out, attended, totals, lengths, all_keys, projected):
        return (
            jnp.zeros((tok_rows, D), jnp.float32),
            jnp.zeros((tok_rows, D), jnp.bfloat16),
            jnp.zeros((HEADS, tok_rows), jnp.float32),
            jnp.zeros(block_shape, jnp.float32),
            jnp.zeros((D, D), jnp.float32),
            jnp.zeros((D,), jnp.float32),
            jnp.zeros((D,), jnp.float32),
        )

    def finish_attention(section_in, grad_out, projected, middle, extra, lengths, grad_sums):
        return attention_finish(section_in, grad_out, middle, extra, params, grad_sums)

    def finish_feed(section_in, grad_out, projected, middle, extra, lengths, grad_sums):
        return feed_backward(section_in, grad_out, params, grad_sums)

    def backward_tick(running, tick_id):
        incoming, grad_sums, input_grads = running
        micro_id = micro_count - 1 - tick_id + (section_count - 1 - section_id)
        in_range = (micro_id >= 0) & (micro_id < micro_count)
        slot_id = jnp.clip(micro_id, 0, micro_count - 1)
        from_next = jnp.where(
            section_id == section_count - 1,
            lax.dynamic_index_in_dim(cotangent, slot_id, 0, False),
            incoming,
        )
        grad_out = jnp.where(in_range, from_next, jnp.zeros_like(from_next))
        section_in = lax.dynamic_index_in_dim(kept_inputs, slot_id, 0, False)
        attended = lax.dynamic_index_in_dim(kept_attended, slot_id, 0, False)
        totals = lax.dynamic_index_in_dim(kept_totals, slot_id, 0, False)
        lengths = lax.dynamic_index_in_dim(row_lengths, slot_id, 0, False)
        projected = lax.cond(attends, make_projected, skip_projected, section_in)
        all_keys = lax.all_gather(projected[:, D:], "seq", axis=0, tiled=True)
        middle = lax.cond(
            attends,
            middle_attention,
            middle_feed,
            section_in,
            grad_out,
            attended,
            totals,
            lengths,
            all_keys,
            projected,
        )
        extra = (lax.psum_scatter(middle[3], "seq", scatter_dimension=0, tiled=True),)
        section_grad, grad_sums = lax.cond(
            attends,
            finish_attention,
            finish_feed,
            section_in,
            grad_out,
            projected,
            middle,
            extra,
            lengths,
            grad_sums,
        )
        low_grad = section_grad.astype(jnp.bfloat16)
        input_grads = keep_slot(input_grads, low_grad, slot_id, in_range)
        incoming = passed_along(low_grad, "section", -1)
        return ((incoming, grad_sums, input_grads), None)

    grad_start = (
        jnp.zeros((D, 3 * D), jnp.float32),
        jnp.zeros((D, D), jnp.float32),
        jnp.zeros((D, FF), jnp.float32),
        jnp.zeros((FF, D), jnp.float32),
        jnp.zeros((3, D), jnp.float32),
        jnp.zeros((bias_count, D), jnp.float32),
        jnp.zeros((FF,), jnp.float32),
        jnp.zeros((2, FF), jnp.float32),
    )
    backward_start = (
        jnp.zeros((tok_rows, D), jnp.bfloat16),
        grad_start,
        jnp.zeros((micro_count, tok_rows, D), jnp.bfloat16),
    )
    backward_end, unused_back = lax.scan(backward_tick, backward_start, ticks)
    unused_grad, grad_sums, input_grads = backward_end
    shards = (
        lax.psum_scatter(grad_sums[0], "seq", scatter_dimension=0, tiled=True),
        lax.psum_scatter(grad_sums[1], "seq", scatter_dimension=0, tiled=True),
        lax.psum_scatter(grad_sums[2], "seq", scatter_dimension=0, tiled=True),
        lax.psum_scatter(grad_sums[3], "seq", scatter_dimension=0, tiled=True),
        lax.psum_scatter(grad_sums[4], "seq", scatter_dimension=1, tiled=True),
        lax.psum_scatter(grad_sums[5], "seq", scatter_dimension=1, tiled=True),
        lax.psum_scatter(grad_sums[6], "seq", scatter_dimension=0, tiled=True),
        lax.psum_scatter(grad_sums[7], "seq", scatter_dimension=1, tiled=True),
    )
    sources = (
        qkv_weight,
        out_weight,
        up_weight,
        down_weight,
        model_gains,
        model_biases,
        hidden_gains,
        hidden_biases,
    )
    placed = tuple(
        (
            lax.dynamic_update_index_in_dim(
                jnp.zeros(source.shape, jnp.float32), shard, layer_id, 0
            )
            for shard, source in zip(shards, sources)
        )
    )
    summed = (
        lax.psum(placed[0].astype(jnp.bfloat16), "section").astype(jnp.float32),
        lax.psum(placed[1].astype(jnp.bfloat16), "section").astype(jnp.float32),
        lax.psum(placed[2].astype(jnp.bfloat16), "section").astype(jnp.float32),
        lax.psum(placed[3].astype(jnp.bfloat16), "section").astype(jnp.float32),
        lax.psum(placed[4].astype(jnp.bfloat16), "section").astype(jnp.float32),
        lax.psum(placed[5].astype(jnp.bfloat16), "section").astype(jnp.float32),
        lax.psum(placed[6].astype(jnp.bfloat16), "section").astype(jnp.float32),
        lax.psum(placed[7].astype(jnp.bfloat16), "section").astype(jnp.float32),
    )
    layer_count = qkv_weight.shape[0]
    layer_terms = lax.dynamic_update_index_in_dim(
        jnp.zeros((layer_count, len(WIDTHS)), jnp.float32), log_sums, layer_id, 0
    )
    layer_picks = lax.dynamic_update_index_in_dim(
        jnp.zeros((layer_count, len(WIDTHS)), jnp.float32), pick_sums, layer_id, 0
    )
    log_totals, pick_totals = lax.psum((layer_terms, layer_picks), ("section", "seq"))
    pattern_means = log_totals / pick_totals
    return (
        outputs[None],
        input_grads[None],
        summed[0],
        summed[1],
        summed[2],
        summed[3],
        summed[4],
        summed[5],
        summed[6],
        summed[7],
        pattern_means,
    )


BF16 = jnp.bfloat16
F32 = jnp.float32
PAIRS = HEADS // 2
OWNERS = (0, 2, 3, 4, 5, 6)
TOKENS = 128
PAIR_LANES = 128
QUERY_STEP = 256
VEC_ROWS = 16
KERNEL_VMEM_BYTES = 64 * 1024 * 1024 - 65536
SCALE = HEAD_DIM ** (-0.5)


def mul(left, right):
    return lax.dot_general(left, right, (((1,), (0,)), ((), ())), preferred_element_type=F32)


def mul_nt(left, right):
    return lax.dot_general(left, right, (((1,), (1,)), ((), ())), preferred_element_type=F32)


def mul_tn(left, right):
    return lax.dot_general(left, right, (((0,), (0,)), ((), ())), preferred_element_type=F32)


def standardize(values):
    center = values - jnp.mean(values, -1, keepdims=True)
    rstd = lax.rsqrt(jnp.mean(center * center, -1, keepdims=True) + EPSILON)
    return (center * rstd, rstd)


def norm_back(unit, rstd, unit_grad):
    first = jnp.mean(unit_grad, -1, keepdims=True)
    second = jnp.mean(unit_grad * unit, -1, keepdims=True)
    return rstd * (unit_grad - first - unit * second)


def remote(source, target, send_sem, recv_sem, axis, peer):
    return pltpu.make_async_remote_copy(
        src_ref=source,
        dst_ref=target,
        send_sem=send_sem,
        recv_sem=recv_sem,
        device_id={axis: peer},
        device_id_type=pl.DeviceIdType.MESH,
    )


def greet(axis, peers):
    barrier = pltpu.get_barrier_semaphore()
    for peer in peers:
        pl.semaphore_signal(
            barrier, inc=1, device_id={axis: peer}, device_id_type=pl.DeviceIdType.MESH
        )
    pl.semaphore_wait(barrier, len(peers))


def seq_peers(me, count):
    return [lax.rem(me + step, count) for step in range(1, count)]


def plane_peers(me):
    return [
        me,
        me + 1 - 2 * lax.rem(me, 2),
        lax.rem(me + 2, 4),
        3 - me,
    ]


def rows_of(block, size=TOKENS):
    return pl.ds(pl.multiple_of(block * size, size), size)


def gelu_parts(values):
    below = 0.5 * (1.0 + lax.erf(values * (0.5**0.5)))
    return (values * below, below)


def share_stats(columns, send, recv, send_sem, recv_sem, peers):
    send[...] = columns.T[0:8, :]
    recv[0] = send[...]
    copies = [
        remote(send, recv.at[k], send_sem.at[k], recv_sem.at[k], "section", peers[k])
        for k in range(1, 4)
    ]
    for copy in copies:
        copy.start()
    return copies


def two_columns(first, second):
    lane = lax.broadcasted_iota(jnp.int32, (first.shape[0], PAIR_LANES), 1)
    return jnp.where(lane == 0, first, jnp.where(lane == 1, second, 0.0))


def slot_rows(k):
    return slice(k * TOKENS, (k + 1) * TOKENS)


def shaped(shape, kind):
    return jax.ShapeDtypeStruct(shape, kind)


class Named:
    def __init__(self, groups, refs):
        names = [name for group in groups for name in group]
        for name, ref in zip(names, refs, strict=True):
            setattr(self, name, ref)


GROUP_TOKENS = 8 * TOKENS
WIDE = 4 * TOKENS
SHARD = D // 8


def square(ref):
    return ref[...].reshape(D, D)


def remote_both(source, target, send_sem, recv_sem, section, seq):
    return pltpu.make_async_remote_copy(
        src_ref=source,
        dst_ref=target,
        send_sem=send_sem,
        recv_sem=recv_sem,
        device_id=(section, seq),
        device_id_type=pl.DeviceIdType.MESH,
    )


def greet_all(barrier, section, me):
    for other in range(4):
        for j in range(8):

            @pl.when((section != other) | (me != j))
            def _():
                pl.semaphore_signal(
                    barrier, inc=1, device_id=(other, j), device_id_type=pl.DeviceIdType.MESH
                )


class Place:
    def __init__(self):
        self.me = lax.axis_index("seq")
        self.section = lax.axis_index("section")
        self.peers = plane_peers(self.section)
        self.core = lax.rem(self.me, 2)
        self.chip = lax.div(self.me, 2)
        self.high = lax.div(self.chip, 2)
        self.low = lax.rem(self.chip, 2)
        self.sibling = self.me + 1 - 2 * self.core
        self.across = 2 * (2 * (1 - self.high) + self.low) + self.core
        self.next = 2 * (2 * self.high + 1 - self.low) + self.core
        self.is_owner = (self.me != 1) & (self.me != 7)
        pair = jnp.where(self.me == 0, 0, self.me - 1)
        self.my_pair = jnp.where(pair > PAIRS - 1, PAIRS - 1, pair)


class LineGather:
    def __init__(self, place, base, far_sems, near_sems, core_sems):
        self.place = place
        self.base = base
        self.far_sems = far_sems
        self.near_sems = near_sems
        self.core_sems = core_sems

    def far(self, high):
        p = self.place
        view = self.base.at[high, p.low, p.core]
        return remote(view, view, self.far_sems[0], self.far_sems[1], "seq", p.across)

    def near(self, low):
        p = self.place
        view = self.base.at[:, low, p.core]
        return remote(view, view, self.near_sems[0], self.near_sems[1], "seq", p.next)

    def cores(self, core):
        p = self.place
        view = self.base.at[:, :, core]
        return remote(view, view, self.core_sems[0], self.core_sems[1], "seq", p.sibling)

    def start(self):
        self.far(self.place.high).start()

    def pass_line(self):
        self.far(1 - self.place.high).wait_recv()
        self.near(self.place.low).start()

    def pass_core(self):
        self.near(1 - self.place.low).wait_recv()
        self.cores(self.place.core).start()

    def ready(self):
        self.cores(1 - self.place.core).wait_recv()

    def drain(self):
        self.far(self.place.high).wait_send()
        self.near(self.place.low).wait_send()
        self.cores(self.place.core).wait_send()


BOTH_VMEM = dict(model=0, hgains=0, hbiases=0)
BOTH_ANY = dict(embeds_in=0, qkv_w=0, out_w=0, up_w=0, down_w=0, cotangent_in=0)
BOTH_OUT = dict(
    sub_f_out=((4, TOKENS, D), BF16, False),
    sub_g_out=((4, TOKENS, D), BF16, False),
    all_m_out=((6, 4, SHARD, D), BF16, False),
    all_v_out=((2, 4, SHARD, PAIR_LANES), BF16, False),
    log_total=((8, PAIR_LANES), F32, True),
)
BOTH_SCRATCH = dict(
    embeds=((4, TOKENS, D), BF16),
    att=((2, TOKENS, D), BF16),
    picks=((2, GROUP_TOKENS, PAIR_LANES), BF16),
    wa=((2, 2, 2, 2, 2, SHARD, D), BF16),
    wf=((2, 2, 2, 2, 2, SHARD, D), BF16),
    qkv=((2, 3, GROUP_TOKENS, PAIR_LANES), BF16),
    pa=((2, GROUP_TOKENS, PAIR_LANES), F32),
    pt=((2, GROUP_TOKENS, PAIR_LANES), F32),
    hid=((2, WIDE, D), BF16),
    up=((2, WIDE, D), F32),
    stat=((2, WIDE, PAIR_LANES), F32),
    left=((2, WIDE, D), BF16),
    raw_up=((2, SHARD, FF), BF16),
    small_src=((2, 32, PAIR_LANES), BF16),
    small=((8, 2, 32, PAIR_LANES), BF16),
    inner=((TOKENS, D), BF16),
    vecs=((2, VEC_ROWS, D), F32),
    logs=((8, PAIR_LANES), F32),
    proj_send=((4, PAIRS, TOKENS, PAIR_LANES), BF16),
    att_send=((GROUP_TOKENS, PAIR_LANES), BF16),
    att_recv=((2, PAIRS, TOKENS, PAIR_LANES), BF16),
    columns=((WIDE, PAIR_LANES), F32),
    stat_rows=((PAIR_LANES, WIDE), F32),
    stat_send=((8, WIDE), F32),
    first_recv=((4, TOKENS, D), BF16),
    fstat_recv=((2, 4, 8, WIDE), F32),
    xs=((4, TOKENS, D), BF16),
    last_send=((4, TOKENS, D), BF16),
    last_recv=((4, TOKENS, D), BF16),
    last=((TOKENS, D), F32),
    streams=((4, TOKENS, D), BF16),
    grads=((WIDE, D), BF16),
    units=((WIDE, D), F32),
    unit_grads=((WIDE, D), F32),
    inners=((WIDE, D), BF16),
    lows=((WIDE, D), BF16),
    part_send=((4, TOKENS, D), BF16),
    part_recv=((4, TOKENS, D), BF16),
    stat_recv=((4, 8, WIDE), F32),
    do_send=((PAIRS, TOKENS, PAIR_LANES), BF16),
    do_recv=((GROUP_TOKENS, PAIR_LANES), BF16),
    key_sum=((GROUP_TOKENS, PAIR_LANES), F32),
    value_sum=((GROUP_TOKENS, PAIR_LANES), F32),
    d_send=((3, GROUP_TOKENS, PAIR_LANES), BF16),
    d_recv=((2, 4, PAIRS, TOKENS, PAIR_LANES), BF16),
    left_src=((TOKENS, D), BF16),
    right_src=((TOKENS, D), BF16),
    right=((2, WIDE, D), BF16),
    vec_rows=((2, PAIR_LANES, D), F32),
    hidden_grad=((TOKENS, D), F32),
    prod=((3, 2, 2, 2, SHARD, D), BF16),
    prod_v=((2, 2, 2, 2, SHARD, PAIR_LANES), BF16),
    pair=((6, 2, 2, SHARD, D), BF16),
    pair_v=((2, 2, 2, SHARD, PAIR_LANES), BF16),
    near=((6, 2, SHARD, D), BF16),
    near_v=((2, 2, SHARD, PAIR_LANES), BF16),
    far=((6, SHARD, D), BF16),
    far_v=((2, SHARD, PAIR_LANES), BF16),
    done=((6, SHARD, D), BF16),
    done_v=((2, SHARD, PAIR_LANES), BF16),
    line=((3, SHARD, D), BF16),
    log_line=((8, 8, PAIR_LANES), F32),
    log_plane=((4, 8, PAIR_LANES), F32),
)
BOTH_SEMS = dict(
    load_sem=(2, 3),
    embeds_sem=(4,),
    small_s=(8,),
    small_r=(8,),
    az_s=(4,),
    az_r=(4,),
    line_s=(6, 3),
    line_r=(6, 3),
    axy_s=(2, 4),
    axy_r=(2, 4),
    axs_s=(2, 4),
    axs_r=(2, 4),
    inner_s=(4,),
    inner_r=(4,),
    wide_s=(2, 4, PAIRS),
    wide_r=(2, 3, 8),
    att_s=(2, 8),
    att_r=(2, PAIRS),
    fhid_s=(2, 4),
    fhid_r=(2, 4),
    fstat_s=(2, 4),
    fstat_r=(2, 4),
    fleft_s=(4,),
    fleft_r=(4,),
    first_s=(4,),
    first_r=(4,),
    g_s=(2, 4),
    g_r=(2, 4),
    stat_s=(2, 4),
    stat_r=(2, 4),
    part_s=(2, 4),
    part_r=(2, 4),
    do_s=(2, PAIRS),
    do_r=(2, 8),
    d_s=(2, 3, 8),
    d_r=(2, 4, PAIRS),
    left_s=(2, 4),
    left_r=(2, 4),
    right_s=(2, 4),
    right_r=(2, 4),
    back_s=(2, 4),
    back_r=(2, 4),
    subf_s=(4,),
    subf_r=(4,),
    subg_s=(4,),
    subg_r=(4,),
    own_sem=(2,),
    last_s=(4,),
    last_r=(4,),
    cot_sem=(4,),
    pair_s=(8,),
    pair_r=(8,),
    near_s=(8,),
    near_r=(8,),
    far_s=(8,),
    far_r=(8,),
    all_s=(8, 4),
    all_r=(8, 4),
    log_s=(8,),
    log_r=(8,),
    log_plane_s=(4,),
    log_plane_r=(4,),
    third_sem=(4,),
    last_line_s=(4,),
    last_line_r=(4,),
)


def make_picks(lengths_ref, section, my_pair, picks_ref):
    tokens = lax.broadcasted_iota(jnp.int32, (GROUP_TOKENS, PAIR_LANES), 0)
    lane = lax.broadcasted_iota(jnp.int32, (GROUP_TOKENS, PAIR_LANES), 1)
    row_id = jnp.zeros_like(tokens)
    first = jnp.zeros_like(tokens)
    end = 0
    for row in range(lengths_ref.shape[1]):
        end = end + lengths_ref[section, row]
        passed = tokens >= end
        row_id = row_id + jnp.where(passed, 1, 0)
        first = jnp.where(passed, end, first)
    pos = (tokens - first).astype(F32)
    number = lax.shift_right_logical(lane, 2)
    row = lane - 4 * number
    ratio = jnp.zeros(lane.shape, F32)
    for i, each in enumerate(RATIOS):
        ratio = jnp.where(number == i, float(each), ratio)
    valid = ratio > 0.5
    ratio = jnp.where(valid, ratio, 1.0)

    def residue(values):
        return values - ratio * jnp.floor((values + 0.5) / ratio)

    residues = residue(pos)
    for head in range(2):
        wanted = residue(jnp.full(lane.shape, 2 * my_pair + head, jnp.int32).astype(F32))
        fits = valid & (row == row_id) & (jnp.abs(residues - wanted) < 0.5)
        picks_ref[head] = jnp.where(fits, 1.0, 0.0).astype(BF16)


def both_kernel(lengths, *refs):
    b = Named([BOTH_VMEM, BOTH_ANY, BOTH_OUT, BOTH_SCRATCH, BOTH_SEMS], refs)
    p = Place()
    me, section, peers, core = (p.me, p.section, p.peers, p.core)
    chip, high, low = (p.chip, p.high, p.low)
    out_slot = jnp.where(section == 3, 0, 1)

    barrier = pltpu.get_barrier_semaphore()
    greet_all(barrier, section, me)

    def block_from_qkv(layer):
        return pltpu.make_async_copy(
            b.qkv_w.at[layer, :, pl.ds(pl.multiple_of(lax.rem(section, 3) * D, D), D)],
            b.wa.at[layer, 0, high, low, core],
            b.load_sem.at[layer, 0],
        )

    def block_from_out(layer):
        return pltpu.make_async_copy(
            b.out_w.at[layer], b.wa.at[layer, 0, high, low, core], b.load_sem.at[layer, 0]
        )

    def load_up(layer):
        return pltpu.make_async_copy(b.up_w.at[layer], b.raw_up.at[layer], b.load_sem.at[layer, 1])

    def load_down(layer):
        return pltpu.make_async_copy(
            b.down_w.at[layer, pl.ds(pl.multiple_of(section * SHARD, SHARD), SHARD)],
            b.wf.at[layer, 1, high, low, core],
            b.load_sem.at[layer, 2],
        )

    def load_embeds(k):
        return pltpu.make_async_copy(
            b.embeds_in.at[peers[k]], b.embeds.at[k], b.embeds_sem.at[k]
        )

    for layer in range(2):

        @pl.when(section != 3)
        def _():
            block_from_qkv(layer).start()

        @pl.when(section == 3)
        def _():
            block_from_out(layer).start()

        if layer == 0:
            for k in range(4):
                load_embeds(k).start()
        load_up(layer).start()
        load_down(layer).start()

    def block_loaded(layer):
        @pl.when(section != 3)
        def _():
            block_from_qkv(layer).wait()

        @pl.when(section == 3)
        def _():
            block_from_out(layer).wait()

    def pick_up(layer):
        load_up(layer).wait()
        load_down(layer).wait()
        raw = b.raw_up[layer]
        for s in range(4):

            @pl.when(section == s)
            def _():
                b.wf[layer, 0, high, low, core] = jnp.concatenate(
                    [
                        raw[:, (4 * j + s) * SHARD : (4 * j + s + 1) * SHARD].astype(F32)
                        for j in range(8)
                    ],
                    1,
                ).astype(BF16)

    def line_gather(number, base):
        pairs = [(b.line_s.at[number, i], b.line_r.at[number, i]) for i in range(3)]
        return LineGather(p, base, *pairs)

    block = [line_gather(layer, b.wa.at[layer, 0]) for layer in range(2)]
    feed_lines = [
        [line_gather(2 + 2 * layer + which, b.wf.at[layer, which]) for which in range(2)]
        for layer in range(2)
    ]

    def first_z(step, source):
        view = b.wa.at[0, 0, lax.div(source, 2), lax.rem(source, 2), core]
        return remote(
            view,
            view,
            b.az_s.at[step],
            b.az_r.at[step],
            "seq",
            2 * lax.rem(chip + step, 4) + core,
        )

    def block_plane(layer, k):
        source = b.wa.at[layer, 0, :, :, core]
        target = b.wa.at[layer, 1, :, :, core]
        return remote(source, target, b.axy_s.at[layer, k], b.axy_r.at[layer, k], "section", peers[k])

    def block_across(layer, k, side):
        view = b.wa.at[layer, 1, :, :, side]
        return remote(view, view, b.axs_s.at[layer, k], b.axs_r.at[layer, k], "seq", p.sibling)

    for layer in range(2):
        model = b.model[layer].astype(F32)
        hidden_gain = b.hgains[layer : layer + 1, :].astype(F32)
        hidden_bias = b.hbiases[layer].astype(F32)
        lines = [model]
        for each in (hidden_gain, hidden_bias[0:1, :], hidden_bias[1:2, :]):
            for s in range(4):
                lines.append(each[:, s * SHARD : (s + 1) * SHARD])
        lines.append(jnp.zeros((11, SHARD), F32))
        packed = jnp.concatenate(lines, 0)
        packed = jnp.concatenate([packed, jnp.zeros((32, PAIR_LANES - SHARD), F32)], 1)
        b.small_src[layer] = packed.astype(BF16)
    b.small[me] = b.small_src[...]
    make_picks(lengths, section, p.my_pair, b.picks)
    b.logs[...] = jnp.zeros_like(b.logs)
    block_loaded(0)
    pl.semaphore_wait(barrier, 31)

    def small_copy(step):
        return remote(
            b.small_src,
            b.small.at[me],
            b.small_s.at[step],
            b.small_r.at[step],
            "seq",
            lax.rem(me + step, 8),
        )

    for step in range(1, 8):
        small_copy(step).start()
    for step in range(1, 4):
        first_z(step, chip).start()
    pick_up(0)
    for step in range(1, 8):
        source = lax.rem(me + 8 - step, 8)
        remote(
            b.small_src,
            b.small.at[source],
            b.small_s.at[step],
            b.small_r.at[step],
            "seq",
            source,
        ).wait_recv()
    for layer in range(2):
        pieces = []
        for j in range(8):
            small = b.small[j, layer].astype(F32)
            lines = [small[0:9]]
            for third in range(3):
                line = jnp.zeros((1, PAIR_LANES), F32)
                for s in range(4):
                    at = 9 + 4 * third + s
                    line = line + jnp.where(section == s, small[at : at + 1], 0.0)
                lines.append(line)
            lines.append(jnp.zeros((4, PAIR_LANES), F32))
            pieces.append(jnp.concatenate(lines, 0)[:, 0:SHARD])
        b.vecs[layer] = jnp.concatenate(pieces, 1)

    def owner_of(pair):
        return jnp.where(pair == 0, 0, pair + 1)

    def wide_turned(layer, k, step):
        pair = lax.rem(me + step, PAIRS)
        return (
            remote_both(
                b.proj_send.at[k, pair],
                b.qkv.at[layer, lax.rem(section, 3), rows_of(me)],
                b.wide_s.at[layer, k, pair],
                b.wide_r.at[layer, lax.rem(section, 3), me],
                peers[k],
                owner_of(pair),
            ),
            owner_of(pair),
        )

    def wide_copy(layer, k, pair):
        return remote_both(
            b.proj_send.at[k, pair],
            b.qkv.at[layer, lax.rem(section, 3), rows_of(me)],
            b.wide_s.at[layer, k, pair],
            b.wide_r.at[layer, lax.rem(section, 3), me],
            peers[k],
            OWNERS[pair],
        )

    def project(layer, arrive):
        vec = b.vecs.at[layer]

        @pl.when(section != 3)
        def _():
            bias = jnp.where(section == 2, vec[6:7, :], 0.0)
            for k in (3, 1, 2, 0) if layer == 0 else (0, 1, 2, 3):
                if k > 0:
                    arrive(k)
                part = mul(b.left[layer, slot_rows(k), :], square(b.wa.at[layer, 0])) + bias
                part = part.astype(BF16)
                for pair in range(PAIRS):
                    b.proj_send[k, pair] = part[:, pair * PAIR_LANES : (pair + 1) * PAIR_LANES]
                for step in range(PAIRS):
                    if k > 0:
                        wide_turned(layer, k, step)[0].start()
                    else:
                        owner = wide_turned(layer, k, step)[1]

                        @pl.when(me != owner)
                        def _():
                            wide_turned(layer, k, step)[0].start()

                if k == 0:

                    @pl.when(p.is_owner)
                    def _():
                        b.qkv[layer, section, rows_of(me), :] = b.proj_send[0, p.my_pair]

    def wait_projected(layer):
        @pl.when(p.is_owner)
        def _():
            for third in range(3):
                for source in range(8):

                    @pl.when((section != third) | (me != source))
                    def _():
                        remote_both(
                            b.proj_send.at[0, 0],
                            b.qkv.at[layer, third, pl.ds(source * TOKENS, TOKENS)],
                            b.wide_s.at[layer, 0, 0],
                            b.wide_r.at[layer, third, source],
                            third,
                            source,
                        ).wait_recv()

        @pl.when(section != 3)
        def _():
            for k in range(4):
                for pair, owner in enumerate(OWNERS):
                    if k > 0:
                        wide_copy(layer, k, pair).wait_send()
                    else:

                        @pl.when(me != owner)
                        def _():
                            wide_copy(layer, k, pair).wait_send()

    def back_copy(layer, target):
        return remote(
            b.att_send.at[pl.ds(target * TOKENS, TOKENS)],
            b.att_recv.at[layer, p.my_pair],
            b.att_s.at[layer, target],
            b.att_r.at[layer, p.my_pair],
            "seq",
            target,
        )

    def attend(layer):
        lane = lax.broadcasted_iota(jnp.int32, (QUERY_STEP, PAIR_LANES), 1)
        first_half = lane < HEAD_DIM
        for step in range(GROUP_TOKENS // QUERY_STEP):
            start = step * QUERY_STEP
            keys_end = start + QUERY_STEP
            rows = slice(start, keys_end)
            query = b.qkv[layer, 0, rows, :] * jnp.asarray(SCALE, BF16)
            keys = b.qkv[layer, 1, 0:keys_end, :]
            values = b.qkv[layer, 2, 0:keys_end, :]
            causal = lax.broadcasted_iota(jnp.int32, (QUERY_STEP, keys_end), 1) <= (
                start + lax.broadcasted_iota(jnp.int32, (QUERY_STEP, keys_end), 0)
            )
            sums = []
            totals = []
            logs = jnp.zeros((1, PAIR_LANES), F32)
            picked_sum = jnp.zeros((1, PAIR_LANES), F32)
            for head in range(2):
                mine = first_half if head == 0 else ~first_half
                own_query = jnp.where(mine, query, jnp.zeros_like(query))
                scores = mul_nt(own_query, keys)
                raised = jnp.where(causal, jnp.exp(scores), 0.0)
                pick_query = b.picks[head, rows, :]
                pick_keys = b.picks[head, 0:keys_end, :]
                counts = mul_nt(pick_query, pick_keys)
                weighted = (raised * counts).astype(BF16)
                sums.append(mul(weighted, values))
                pattern = mul(raised.astype(BF16), pick_keys)
                picked = pick_query.astype(F32)
                totals.append(jnp.sum(pattern * picked, -1, keepdims=True))
                chosen = picked > 0.5
                logs = logs + jnp.sum(
                    jnp.where(chosen, jnp.log(jnp.where(chosen, pattern, 1.0)), 0.0),
                    0,
                    keepdims=True,
                )
                picked_sum = picked_sum + jnp.sum(picked, 0, keepdims=True)
            b.logs[layer : layer + 1, :] += logs
            if layer == 0:
                b.logs[2:3, :] += picked_sum
            total = jnp.where(first_half, totals[0], totals[1])
            attended = jnp.where(first_half, sums[0], sums[1]) / total
            b.pa[layer, rows, :] = attended
            b.pt[layer, rows, :] = total
            b.att_send[rows, :] = attended.astype(BF16)
            for target in (2 * step, 2 * step + 1):

                @pl.when(me != target)
                def _():
                    back_copy(layer, target).start()

                @pl.when(me == target)
                def _():
                    b.att_recv[layer, p.my_pair] = b.att_send[
                        target * TOKENS : (target + 1) * TOKENS, :
                    ]

    def attention_rest(layer, inputs_ref, after):
        vec = b.vecs.at[layer]
        wait_projected(layer)
        feed_lines[layer][0].start()
        after()

        @pl.when(p.is_owner)
        def _():
            attend(layer)

        feed_lines[layer][0].pass_line()
        for k in range(1, 4):

            @pl.when(peers[k] == 3)
            def _():
                block_plane(layer, k).wait_recv()
                block_across(layer, k, core).start()

        for pair, owner in enumerate(OWNERS):

            @pl.when(me != owner)
            def _():
                remote(
                    b.att_send.at[pl.ds(0, TOKENS)],
                    b.att_recv.at[layer, pair],
                    b.att_s.at[layer, 0],
                    b.att_r.at[layer, pair],
                    "seq",
                    owner,
                ).wait_recv()

            b.att[layer, :, pair * PAIR_LANES : (pair + 1) * PAIR_LANES] = b.att_recv[layer, pair]
        inner_unit, unused = standardize(b.att[layer].astype(F32))
        inner = (inner_unit * vec[1:2, :] + vec[4:5, :]).astype(BF16)
        if layer == 0:
            b.inner[...] = inner
        for k in range(1, 4):

            @pl.when(peers[k] == 3)
            def _():
                block_across(layer, k, 1 - core).wait_recv()

        branch = mul(inner, square(b.wa.at[layer, out_slot])) + vec[7:8, :]
        b.xs[2 * layer] = (inputs_ref[...].astype(F32) + branch).astype(BF16)

    def attention_drain(layer):
        @pl.when(p.is_owner)
        def _():
            for target in range(8):

                @pl.when(me != target)
                def _():
                    back_copy(layer, target).wait_send()

    def feed(layer, resting, parting):
        vec = b.vecs.at[layer]
        inputs = b.xs[2 * layer].astype(F32)
        unit, unused = standardize(inputs)
        b.hid[layer, slot_rows(0), :] = (unit * vec[2:3, :] + vec[5:6, :]).astype(BF16)
        hidden_copies = [
            remote(
                b.hid.at[layer, pl.ds(0, TOKENS)],
                b.hid.at[layer, pl.ds(k * TOKENS, TOKENS)],
                b.fhid_s.at[layer, k],
                b.fhid_r.at[layer, k],
                "section",
                peers[k],
            )
            for k in range(1, 4)
        ]
        for copy in hidden_copies:
            copy.start()
        up_line, down_line = feed_lines[layer]
        down_line.start()
        up_line.pass_core()
        down_line.pass_line()
        up_line.ready()
        for k in range(4):
            if k > 0:
                hidden_copies[k - 1].wait_recv()
            upward = mul(b.hid[layer, slot_rows(k), :], square(b.wf.at[layer, 0])) + vec[10:11, :]
            b.up[layer, slot_rows(k), :] = upward
            values, unused = gelu_parts(upward)
            b.units[slot_rows(k), :] = values
            mean = jnp.mean(values, -1, keepdims=True)
            center = values - mean
            b.columns[slot_rows(k), :] = two_columns(
                mean, jnp.sum(center * center, -1, keepdims=True)
            )
        stat_copies = share_stats(
            b.columns[...],
            b.stat_send,
            b.fstat_recv.at[layer],
            b.fstat_s.at[layer],
            b.fstat_r.at[layer],
            peers,
        )
        down_line.pass_core()
        resting()
        for copy in stat_copies:
            copy.wait_recv()
        b.stat_rows[...] = jnp.zeros((PAIR_LANES, WIDE), F32)
        for k in range(4):
            means = [b.fstat_recv[layer, other, 0:1, slot_rows(k ^ other)] for other in range(4)]
            squares = [b.fstat_recv[layer, other, 1:2, slot_rows(k ^ other)] for other in range(4)]
            mean = (means[0] + means[1] + means[2] + means[3]) * 0.25
            spread = squares[0] + squares[1] + squares[2] + squares[3]
            for each in means:
                spread = spread + D * (each - mean) * (each - mean)
            b.stat_rows[0:1, slot_rows(k)] = mean
            b.stat_rows[1:2, slot_rows(k)] = lax.rsqrt(spread * (1.0 / FF) + EPSILON)
        b.stat[layer] = b.stat_rows[...].T
        down_line.ready()
        if layer == 1:
            parting()
            for copy in hidden_copies + stat_copies:
                copy.wait_send()
            return
        branch = None
        part_copies = []
        for k in (3, 1, 2, 0):
            both = b.stat[layer, slot_rows(k), :]
            inner = (
                (b.units[slot_rows(k), :] - both[:, 0:1]) * both[:, 1:2] * vec[9:10, :]
                + vec[11:12, :]
            ).astype(BF16)
            part = mul(inner, square(b.wf.at[layer, 1]))
            if k == 0:
                branch = part
            else:
                b.part_send[k] = part.astype(BF16)
                part_copies.append(
                    remote(
                        b.part_send.at[k],
                        b.first_recv.at[k],
                        b.first_s.at[k],
                        b.first_r.at[k],
                        "section",
                        peers[k],
                    )
                )
                part_copies[-1].start()
        parting()
        for k, copy in zip((3, 1, 2), part_copies):
            copy.wait_recv()
            branch = branch + b.first_recv[k].astype(F32)
        b.xs[2 * layer + 1] = (inputs + branch + vec[8:9, :]).astype(BF16)
        for copy in hidden_copies + stat_copies + part_copies:
            copy.wait_send()

    def sub_copies(number, forward):
        source = b.xs if forward else b.streams
        target = b.sub_f_out if forward else b.sub_g_out
        send_sem = b.subf_s if forward else b.subg_s
        recv_sem = b.subf_r if forward else b.subg_r

        def away():
            return remote(
                source.at[number],
                target.at[section],
                send_sem.at[number],
                recv_sem.at[section],
                "section",
                number,
            )

        def own():
            return pltpu.make_async_copy(
                source.at[number], target.at[section], b.own_sem.at[0 if forward else 1]
            )

        return away, own

    def send_sub(number, forward):
        @pl.when(section != number)
        def _():
            sub_copies(number, forward)[0]().start()

        @pl.when(section == number)
        def _():
            sub_copies(number, forward)[1]().start()

    def drain_sub(number, forward):
        @pl.when(section != number)
        def _():
            sub_copies(number, forward)[0]().wait_send()

        @pl.when(section == number)
        def _():
            sub_copies(number, forward)[1]().wait()

    def receive_sub(source, forward):
        target = b.sub_f_out if forward else b.sub_g_out

        @pl.when(section != source)
        def _():
            remote(
                b.streams.at[0],
                target.at[source],
                (b.subf_s if forward else b.subg_s).at[0],
                (b.subf_r if forward else b.subg_r).at[source],
                "section",
                source,
            ).wait_recv()

    for k in range(4):
        load_embeds(k).wait()

        @pl.when(section != 3)
        def _():
            unit, unused = standardize(b.embeds[k].astype(F32))
            b.left[0, slot_rows(k), :] = (
                unit * b.vecs[0, 0:1, :] + b.vecs[0, 3:4, :]
            ).astype(BF16)
    pick_up(1)
    for step in range(1, 4):
        first_z(step, lax.rem(chip + 4 - step, 4)).wait_recv()
    block[0].cores(core).start()

    @pl.when(section == 3)
    def _():
        for k in range(1, 4):
            block_plane(0, k).start()

    block[0].ready()
    project(0, lambda k: None)

    attention_rest(0, b.embeds.at[0], lambda: None)

    def resting_first():
        block_loaded(1)
        block[1].start()

    def parting_first():
        attention_drain(0)
        block[1].pass_line()

    feed(0, resting_first, parting_first)

    second = b.vecs.at[1]
    unit, unused = standardize(b.xs[1].astype(F32))
    b.left[1, slot_rows(0), :] = (unit * second[0:1, :] + second[3:4, :]).astype(BF16)

    def left_copy(k):
        return remote(
            b.left.at[1, pl.ds(0, TOKENS)],
            b.left.at[1, pl.ds(k * TOKENS, TOKENS)],
            b.fleft_s.at[k],
            b.fleft_r.at[k],
            "section",
            peers[k],
        )

    for k in (3, 1, 2):

        @pl.when(peers[k] != 3)
        def _():
            left_copy(k).start()

    block[1].pass_core()
    for k in range(1, 4):

        @pl.when(peers[k] != 3)
        def _():
            left_copy(k).wait_send()

    @pl.when(section == 3)
    def _():
        for k in range(1, 4):
            block_plane(1, k).start()

    block[1].ready()
    project(1, lambda k: left_copy(k).wait_recv())

    def inner_copy(k):
        return remote(
            b.inner,
            b.left.at[0, pl.ds(k * TOKENS, TOKENS)],
            b.inner_s.at[k],
            b.inner_r.at[k],
            "section",
            peers[k],
        )

    def after_second():
        for k in range(1, 4):

            @pl.when(peers[k] == 3)
            def _():
                inner_copy(k).start()

        @pl.when(section == 3)
        def _():
            b.left[0, slot_rows(0), :] = b.inner[...]

        send_sub(0, True)
        send_sub(1, True)

    attention_rest(1, b.xs.at[1], after_second)

    def resting_second():
        send_sub(2, True)
        for k in range(1, 4):

            @pl.when(peers[k] == 3)
            def _():
                inner_copy(k).wait_send()

        @pl.when(section == 3)
        def _():
            for k in range(1, 4):
                inner_copy(k).wait_recv()

    def parting_second():
        attention_drain(1)

    feed(1, resting_second, parting_second)

    def cotangent_load(k):
        return pltpu.make_async_copy(
            b.cotangent_in.at[peers[k]], b.grads.at[pl.ds(k * TOKENS, TOKENS)], b.cot_sem.at[k]
        )

    for k in range(4):
        cotangent_load(k).start()

    def log_copy(step):
        return remote(
            b.logs,
            b.log_line.at[me],
            b.log_s.at[step],
            b.log_r.at[step],
            "seq",
            lax.rem(me + step, 8),
        )

    def log_plane_copy(k, slot):
        return remote(
            b.log_plane.at[slot],
            b.log_plane.at[slot],
            b.log_plane_s.at[k],
            b.log_plane_r.at[k],
            "section",
            peers[k],
        )

    def start_logs():
        b.log_line[me] = b.logs[...]
        for step in range(1, 8):
            log_copy(step).start()

    def sum_logs():
        for step in range(1, 8):
            source = lax.rem(me + 8 - step, 8)
            remote(
                b.logs,
                b.log_line.at[source],
                b.log_s.at[step],
                b.log_r.at[step],
                "seq",
                source,
            ).wait_recv()
        total = b.log_line[0]
        for j in range(1, 8):
            total = total + b.log_line[j]
        b.log_plane[section] = total
        for k in range(1, 4):
            log_plane_copy(k, section).start()

    def finish_logs():
        for k in range(1, 4):
            log_plane_copy(k, peers[k]).wait_recv()
        total = b.log_plane[0]
        for other in range(1, 4):
            total = total + b.log_plane[other]
        b.log_total[...] = total
        for step in range(1, 8):
            log_copy(step).wait_send()
        for k in range(1, 4):
            log_plane_copy(k, section).wait_send()

    class Matrix:
        def __init__(self, number):
            self.number = number
            self.direct = number > 4
            self.turn = (1, 2) if number % 2 else (2, 1)
            self.j = number % 3 if number < 6 else number - 6
            if number < 6:
                self.i = number
                refs = (b.prod, b.pair, b.near, b.far, b.done, b.all_m_out)
            else:
                self.i = number - 6
                refs = (b.prod_v, b.pair_v, b.near_v, b.far_v, b.done_v, b.all_v_out)
            self.prod, self.pair, self.near, self.far, self.done, self.all = refs

        def store(self, value):
            if 3 <= self.number < 6:
                matrices[self.number - 3].sent()
            for j in range(8):
                self.prod[self.j, j % 2, j // 4, j // 2 % 2] = value[
                    j * SHARD : (j + 1) * SHARD, :
                ].astype(BF16)

        def pair_copy(self):
            n = self.number
            return remote(
                self.prod.at[self.j, 1 - core],
                self.pair.at[self.i],
                b.pair_s.at[n],
                b.pair_r.at[n],
                "seq",
                p.sibling,
            )

        def near_copy(self):
            n = self.number
            return remote(
                self.prod.at[self.j, core, :, 1 - low],
                self.near.at[self.i],
                b.near_s.at[n],
                b.near_r.at[n],
                "seq",
                p.next,
            )

        def far_copy(self):
            n = self.number
            return remote(
                self.prod.at[self.j, core, 1 - high, low],
                self.far.at[self.i],
                b.far_s.at[n],
                b.far_r.at[n],
                "seq",
                p.across,
            )

        def all_copy(self, k, slot):
            n = self.number
            return remote(
                self.done.at[self.i],
                self.all.at[self.i, slot],
                b.all_s.at[n, k],
                b.all_r.at[n, k],
                "section",
                peers[k],
            )

        def own_copy(self):
            return pltpu.make_async_copy(
                self.done.at[self.i], self.all.at[self.i, section], b.all_s.at[self.number, 0]
            )

        def step_near(self):
            self.pair_copy().wait_recv()
            i, at = (self.i, self.j)
            for h in range(2):
                for l in range(2):
                    self.prod[at, core, h, l] = (
                        self.prod[at, core, h, l].astype(F32) + self.pair[i, h, l].astype(F32)
                    ).astype(BF16)
            self.near_copy().start()

        def line_copy(self, step):
            target = lax.rem(chip + step, 4)
            return remote(
                self.prod.at[self.j, core, lax.div(target, 2), lax.rem(target, 2)],
                b.line.at[step - 1],
                b.last_line_s.at[step],
                b.last_line_r.at[step],
                "seq",
                2 * target + core,
            )

        def step_line(self):
            self.pair_copy().wait_recv()
            i, at = (self.i, self.j)
            for h in range(2):
                for l in range(2):
                    self.prod[at, core, h, l] = (
                        self.prod[at, core, h, l].astype(F32) + self.pair[i, h, l].astype(F32)
                    ).astype(BF16)
            for step in (2, 1, 3):
                self.line_copy(step).start()

        def step_line_plane(self):
            total = self.prod[self.j, core, high, low].astype(F32)
            for step in range(1, 4):
                self.line_copy(step).wait_recv()
                total = total + b.line[step - 1].astype(F32)
            self.done[self.i] = total.astype(BF16)
            for k in (3, 1, 2):
                self.all_copy(k, section).start()
            self.own_copy().start()

        def step_far(self):
            self.near_copy().wait_recv()
            i, at = (self.i, self.j)
            for h in range(2):
                self.prod[at, core, h, low] = (
                    self.prod[at, core, h, low].astype(F32) + self.near[i, h].astype(F32)
                ).astype(BF16)
            self.far_copy().start()

        def step_plane(self):
            self.far_copy().wait_recv()
            i = self.i
            self.done[i] = (
                self.prod[self.j, core, high, low].astype(F32) + self.far[i].astype(F32)
            ).astype(BF16)
            for k in (3, 1, 2) if self.direct else (1, 2):
                self.all_copy(k, section).start()
            self.own_copy().start()

        def turn_copy(self):
            n = self.number
            first, second = self.turn
            view = self.all.at[self.i, peers[first]]
            return remote(
                view, view, b.all_s.at[n, 3], b.all_r.at[n, 3], "section", peers[second]
            )

        def step_pass(self):
            first = self.turn[0]
            self.all_copy(first, peers[first]).wait_recv()
            self.turn_copy().start()

        def step_end(self):
            for k in range(1, 4):
                if self.direct or k != self.turn[0]:
                    self.all_copy(k, peers[k]).wait_recv()
                if self.direct or k != 3:
                    self.all_copy(k, section).wait_send()
                else:
                    self.turn_copy().wait_send()
            self.own_copy().wait()
            if self.number > 2:
                self.sent()

        def sent(self):
            self.pair_copy().wait_send()
            if self.number == 5:
                for step in range(1, 4):
                    self.line_copy(step).wait_send()
                return
            self.near_copy().wait_send()
            self.far_copy().wait_send()

    matrices = [Matrix(number) for number in range(8)]
    up1, down1, att1, up0, down0, att0, vec1, vec0 = matrices

    def last_copy(k):
        return remote(
            b.last_send.at[k],
            b.last_recv.at[k],
            b.last_s.at[k],
            b.last_r.at[k],
            "section",
            peers[k],
        )

    def start_last():
        for k in (3, 1, 2, 0):
            part = mul(b.inners[slot_rows(k), :], square(b.wf.at[1, 1]))
            if k == 0:
                b.last[...] = part
            else:
                b.last_send[k] = part.astype(BF16)
                last_copy(k).start()

    def finish_last():
        total = b.xs[2].astype(F32) + b.last[...] + b.vecs[1, 8:9, :]
        for k in range(1, 4):
            last_copy(k).wait_recv()
            total = total + b.last_recv[k].astype(F32)
        b.xs[3] = total.astype(BF16)
        for k in range(1, 4):
            last_copy(k).wait_send()

    def feed_phase(layer, grad_ref, x_ref, hooks):
        phase = 1 - layer
        vec = b.vecs.at[layer]
        rows = b.vec_rows.at[layer]
        up_matrix = matrices[3 * phase]
        down_matrix = matrices[3 * phase + 1]
        early, middle, parting, late = hooks
        if layer == 0:
            b.grads[slot_rows(0), :] = grad_ref[...]
        grad_copies = [] if layer == 1 else [
            remote(
                b.grads.at[pl.ds(0, TOKENS)],
                b.grads.at[pl.ds(k * TOKENS, TOKENS)],
                b.g_s.at[phase, k],
                b.g_r.at[phase, k],
                "section",
                peers[k],
            )
            for k in range(1, 4)
        ]
        if layer == 0:
            for k in (3, 1, 2):
                grad_copies[k - 1].start()
        rows[...] = jnp.zeros((PAIR_LANES, D), F32)
        early()
        for k in range(4):
            both = b.stat[layer, slot_rows(k), :]
            upward = b.up[layer, slot_rows(k), :]
            values, below = gelu_parts(upward)
            b.up[layer, slot_rows(k), :] = below + upward * (
                jnp.exp(-0.5 * upward * upward) * (0.5 / 3.141592653589793) ** 0.5
            )
            unit = (values - both[:, 0:1]) * both[:, 1:2]
            b.units[slot_rows(k), :] = unit
            b.inners[slot_rows(k), :] = (unit * vec[9:10, :] + vec[11:12, :]).astype(BF16)
        gain_sum = jnp.zeros((1, D), F32)
        bias_sum = jnp.zeros((1, D), F32)
        for k in range(4):
            if layer == 1:
                cotangent_load(k).wait()
            elif k > 0:
                if k == 3:
                    att1.step_far()
                    vec1.step_near()
                grad_copies[k - 1].wait_recv()
            unit = b.units[slot_rows(k), :]
            inner_grad = mul_nt(b.grads[slot_rows(k), :], square(b.wf.at[layer, 1]))
            gain_sum = gain_sum + jnp.sum(inner_grad * unit, 0, keepdims=True)
            bias_sum = bias_sum + jnp.sum(inner_grad, 0, keepdims=True)
            unit_grad = inner_grad * vec[9:10, :]
            b.unit_grads[slot_rows(k), :] = unit_grad
            b.columns[slot_rows(k), :] = two_columns(
                jnp.sum(unit_grad, -1, keepdims=True), jnp.sum(unit_grad * unit, -1, keepdims=True)
            )
        stat_copies = share_stats(
            b.columns[...],
            b.stat_send,
            b.stat_recv,
            b.stat_s.at[phase],
            b.stat_r.at[phase],
            peers,
        )
        rows[9:10, :] = gain_sum
        rows[11:12, :] = bias_sum
        down_matrix.store(mul_tn(b.inners[...], b.grads[...]))
        down_matrix.pair_copy().start()
        middle()
        for copy in stat_copies:
            copy.wait_recv()
        b.stat_rows[...] = jnp.zeros((PAIR_LANES, WIDE), F32)
        for k in range(4):
            for line in range(2):
                parts = [
                    b.stat_recv[other, line : line + 1, slot_rows(k ^ other)]
                    for other in range(4)
                ]
                b.stat_rows[line : line + 1, slot_rows(k)] = (
                    parts[0] + parts[1] + parts[2] + parts[3]
                ) * (1.0 / FF)
        b.columns[...] = b.stat_rows[...].T
        hidden_grad = None
        low_sum = jnp.zeros((1, D), F32)
        part_copies = []
        for k in (3, 1, 2, 0):
            rstd = b.stat[layer, slot_rows(k), :][:, 1:2]
            both = b.columns[slot_rows(k), :]
            lowered = (
                rstd
                * (
                    b.unit_grads[slot_rows(k), :]
                    - both[:, 0:1]
                    - b.units[slot_rows(k), :] * both[:, 1:2]
                )
                * b.up[layer, slot_rows(k), :]
            ).astype(BF16)
            b.lows[slot_rows(k), :] = lowered
            low_sum = low_sum + jnp.sum(lowered.astype(F32), 0, keepdims=True)
            part = mul_nt(lowered, square(b.wf.at[layer, 0]))
            if k == 0:
                hidden_grad = part
            else:
                b.part_send[k] = part.astype(BF16)
                part_copies.append(
                    remote(
                        b.part_send.at[k],
                        b.part_recv.at[k],
                        b.part_s.at[phase, k],
                        b.part_r.at[phase, k],
                        "section",
                        peers[k],
                    )
                )
                part_copies[-1].start()
        rows[10:11, :] = low_sum
        up_matrix.store(mul_tn(b.hid[layer], b.lows[...]))
        up_matrix.pair_copy().start()
        unit, rstd = standardize(x_ref[...].astype(F32))
        parting()
        for k, copy in zip((3, 1, 2), part_copies):
            copy.wait_recv()
            hidden_grad = hidden_grad + b.part_recv[k].astype(F32)
        grad = grad_ref[...].astype(F32)
        number = 2 * layer + 1
        b.streams[number] = (
            grad + norm_back(unit, rstd, hidden_grad * vec[2:3, :])
        ).astype(BF16)
        rows[2:3, :] = jnp.sum(hidden_grad * unit, 0, keepdims=True)
        rows[5:6, :] = jnp.sum(hidden_grad, 0, keepdims=True)
        rows[8:9, :] = jnp.sum(grad, 0, keepdims=True)
        for copy in grad_copies + stat_copies + part_copies:
            copy.wait_send()
        late()

    def attention_phase(layer, grad_ref, x_ref, att_ref, hooks):
        phase = 1 - layer
        vec = b.vecs.at[layer]
        rows = b.vec_rows.at[layer]
        before, inside, after, during = hooks
        grad = grad_ref[...]
        inner_unit, inner_rstd = standardize(att_ref[...].astype(F32))
        inner_grad = mul_nt(grad, square(b.wa.at[layer, out_slot]))
        att_grad = norm_back(inner_unit, inner_rstd, inner_grad * vec[1:2, :]).astype(BF16)
        for pair in range(PAIRS):
            b.do_send[pair] = att_grad[:, pair * PAIR_LANES : (pair + 1) * PAIR_LANES]

        def out_copy(pair):
            return remote(
                b.do_send.at[pair],
                b.do_recv.at[rows_of(me)],
                b.do_s.at[phase, pair],
                b.do_r.at[phase, me],
                "seq",
                OWNERS[pair],
            )

        def out_turned(step):
            pair = lax.rem(me + step, PAIRS)
            return (
                remote(
                    b.do_send.at[pair],
                    b.do_recv.at[rows_of(me)],
                    b.do_s.at[phase, pair],
                    b.do_r.at[phase, me],
                    "seq",
                    owner_of(pair),
                ),
                owner_of(pair),
            )

        for step in range(PAIRS):
            owner = out_turned(step)[1]

            @pl.when(me != owner)
            def _():
                out_turned(step)[0].start()

        @pl.when(p.is_owner)
        def _():
            b.do_recv[rows_of(me), :] = b.do_send[p.my_pair]

        def left_copy(k):
            return remote(
                b.left_src,
                b.left.at[layer, pl.ds(k * TOKENS, TOKENS)],
                b.left_s.at[phase, k],
                b.left_r.at[phase, k],
                "section",
                peers[k],
            )

        def right_copy(k):
            return remote(
                b.right_src,
                b.right.at[layer, pl.ds(k * TOKENS, TOKENS)],
                b.right_s.at[phase, k],
                b.right_r.at[phase, k],
                "section",
                peers[k],
            )

        unit, rstd = standardize(x_ref[...].astype(F32))
        b.left_src[...] = (inner_unit * vec[1:2, :] + vec[4:5, :]).astype(BF16)
        b.right_src[...] = grad
        for k in range(1, 4):

            @pl.when(peers[k] == 3)
            def _():
                right_copy(k).start()
                if layer == 1:
                    left_copy(k).start()

        if layer == 1:

            @pl.when(section == 3)
            def _():
                b.left[layer, slot_rows(0), :] = b.left_src[...]

        rows[1:2, :] = jnp.sum(inner_grad * inner_unit, 0, keepdims=True)
        rows[4:5, :] = jnp.sum(inner_grad, 0, keepdims=True)
        rows[7:8, :] = jnp.sum(grad.astype(F32), 0, keepdims=True)

        def back_copy(third, target):
            return remote_both(
                b.d_send.at[third, pl.ds(target * TOKENS, TOKENS)],
                b.d_recv.at[layer, section, p.my_pair],
                b.d_s.at[phase, third, target],
                b.d_r.at[phase, section, p.my_pair],
                third,
                target,
            )

        @pl.when(p.is_owner)
        def _():
            for source in range(8):

                @pl.when(me != source)
                def _():
                    remote(
                        b.do_send.at[0],
                        b.do_recv.at[pl.ds(source * TOKENS, TOKENS)],
                        b.do_s.at[phase, 0],
                        b.do_r.at[phase, source],
                        "seq",
                        source,
                    ).wait_recv()

        before()

        @pl.when(p.is_owner)
        def _():
            b.key_sum[...] = jnp.zeros((GROUP_TOKENS, PAIR_LANES), F32)
            b.value_sum[...] = jnp.zeros((GROUP_TOKENS, PAIR_LANES), F32)
            lane = lax.broadcasted_iota(jnp.int32, (QUERY_STEP, PAIR_LANES), 1)
            first_half = lane < HEAD_DIM
            last_step = GROUP_TOKENS // QUERY_STEP - 1
            for step in (0,) + tuple(range(last_step, 0, -1)):
                start = step * QUERY_STEP
                keys_end = start + QUERY_STEP
                block = slice(start, keys_end)
                plain_query = b.qkv[layer, 0, block, :]
                query = plain_query * jnp.asarray(SCALE, BF16)
                keys = b.qkv[layer, 1, 0:keys_end, :]
                values = b.qkv[layer, 2, 0:keys_end, :]
                causal = lax.broadcasted_iota(jnp.int32, (QUERY_STEP, keys_end), 1) <= (
                    start + lax.broadcasted_iota(jnp.int32, (QUERY_STEP, keys_end), 0)
                )
                head_grad = b.do_recv[block, :]
                inverse = 1.0 / b.pt[layer, block, :]
                head_float = head_grad.astype(F32)
                products = head_float * b.pa[layer, block, :]
                scaled = (head_float * inverse).astype(BF16)
                key_lanes = lax.broadcasted_iota(jnp.int32, (keys_end, PAIR_LANES), 1) < HEAD_DIM
                query_parts = []
                key_parts = []
                value_parts = []
                for head in range(2):
                    mine = first_half if head == 0 else ~first_half
                    own_query = jnp.where(mine, query, jnp.zeros_like(query))
                    own_grad = jnp.where(mine, head_grad, jnp.zeros_like(head_grad))
                    delta = jnp.sum(jnp.where(mine, products, 0.0), -1, keepdims=True)
                    own_inverse = jnp.max(jnp.where(mine, inverse, 0.0), -1, keepdims=True)
                    counts = mul_nt(b.picks[head, block, :], b.picks[head, 0:keys_end, :])
                    scores = mul_nt(own_query, keys)
                    weighted = jnp.where(causal, jnp.exp(scores) * counts, 0.0)
                    prob_grad = mul_nt(own_grad, values)
                    score_grad = (weighted * own_inverse * (prob_grad - delta)).astype(BF16)
                    query_parts.append(mul(score_grad, keys))
                    key_parts.append(mul_tn(score_grad, plain_query))
                    value_parts.append(mul_tn(weighted.astype(BF16), scaled))
                b.key_sum[0:keys_end, :] += jnp.where(key_lanes, key_parts[0], key_parts[1])
                b.value_sum[0:keys_end, :] += jnp.where(key_lanes, value_parts[0], value_parts[1])
                query_grad = jnp.where(first_half, query_parts[0], query_parts[1]) * SCALE
                b.d_send[0, block, :] = query_grad.astype(BF16)
                ready = [(0, step)]
                if step > 0:
                    ready = [(0, step), (1, step), (2, step)]
                if step == 1:
                    ready = [(1, 0), (2, 0)] + ready
                for third, part in ready:
                    part_rows = slice(part * QUERY_STEP, (part + 1) * QUERY_STEP)
                    if third == 1:
                        b.d_send[1, part_rows, :] = (b.key_sum[part_rows, :] * SCALE).astype(BF16)
                    if third == 2:
                        b.d_send[2, part_rows, :] = b.value_sum[part_rows, :].astype(BF16)
                    for target in (2 * part, 2 * part + 1):
                        away = (section != third) | (me != target)

                        @pl.when(away)
                        def _():
                            back_copy(third, target).start()

                        @pl.when(~away)
                        def _():
                            b.d_recv[layer, section, p.my_pair] = b.d_send[
                                third, target * TOKENS : (target + 1) * TOKENS, :
                            ]

        inside()
        after()

        def part_copy(k):
            return remote(
                b.part_send.at[k],
                b.part_recv.at[k],
                b.back_s.at[phase, k],
                b.back_r.at[phase, k],
                "section",
                peers[k],
            )

        @pl.when(section != 3)
        def _():
            for k in (3, 2, 1, 0):
                for pair, owner in enumerate(OWNERS):
                    away = me != owner if k == 0 else True

                    @pl.when(away)
                    def _():
                        remote_both(
                            b.d_send.at[0, pl.ds(0, TOKENS)],
                            b.d_recv.at[layer, peers[k], pair],
                            b.d_s.at[phase, 0, 0],
                            b.d_r.at[phase, peers[k], pair],
                            peers[k],
                            owner,
                        ).wait_recv()

                    b.right[layer, slot_rows(k), pair * PAIR_LANES : (pair + 1) * PAIR_LANES] = (
                        b.d_recv[layer, peers[k], pair]
                    )
                part = mul_nt(b.right[layer, slot_rows(k), :], square(b.wa.at[layer, 0]))
                if k == 0:
                    b.hidden_grad[...] = part
                else:
                    b.part_send[k] = part.astype(BF16)
                    part_copy(k).start()

        @pl.when(section == 3)
        def _():
            b.right[layer, slot_rows(0), :] = b.right_src[...]
            b.hidden_grad[...] = jnp.zeros((TOKENS, D), F32)
            for k in range(1, 4):
                right_copy(k).wait_recv()
                if layer == 1:
                    left_copy(k).wait_recv()

        matrix = matrices[3 * phase + 2]
        matrix.store(mul_tn(b.left[layer], b.right[layer]))
        matrix.pair_copy().start()
        value_sum = jnp.sum(b.right[layer].astype(F32), 0, keepdims=True)
        rows[6:7, :] = jnp.where(section == 2, value_sum, 0.0)
        during()
        for k in (3, 1, 2):

            @pl.when(peers[k] != 3)
            def _():
                part_copy(k).wait_recv()
                b.hidden_grad[...] += b.part_recv[k].astype(F32)

        hidden_grad = b.hidden_grad[...]
        b.streams[2 * layer] = (
            grad.astype(F32) + norm_back(unit, rstd, hidden_grad * vec[0:1, :])
        ).astype(BF16)
        rows[0:1, :] = jnp.sum(hidden_grad * unit, 0, keepdims=True)
        rows[3:4, :] = jnp.sum(hidden_grad, 0, keepdims=True)

        def drain():
            @pl.when(section != 3)
            def _():
                for k in range(1, 4):
                    part_copy(k).wait_send()

            for k in range(1, 4):

                @pl.when(peers[k] == 3)
                def _():
                    right_copy(k).wait_send()
                    if layer == 1:
                        left_copy(k).wait_send()

            for pair, owner in enumerate(OWNERS):

                @pl.when(me != owner)
                def _():
                    out_copy(pair).wait_send()

            @pl.when(p.is_owner)
            def _():
                for third in range(3):
                    for target in range(8):

                        @pl.when((section != third) | (me != target))
                        def _():
                            back_copy(third, target).wait_send()

        return drain

    def nothing():
        pass

    def middle_first():
        start_logs()

    def late_first():
        start_last()

    feed_phase(
        1,
        b.grads.at[pl.ds(0, TOKENS)],
        b.xs.at[2],
        (nothing, middle_first, down1.step_near, late_first),
    )

    def third_out(k):
        return pltpu.make_async_copy(
            b.right.at[1, pl.ds(k * TOKENS, TOKENS)], b.sub_g_out.at[peers[k]], b.third_sem.at[k]
        )

    def before_first():
        down1.step_far()

    def during_first():
        up1.step_far()
        down1.step_pass()
        finish_last()
        sum_logs()

    drain_first = attention_phase(
        1,
        b.streams.at[3],
        b.xs.at[1],
        b.att.at[1],
        (before_first, down1.step_plane, up1.step_near, during_first),
    )

    def early_second():
        vec1.store(b.vec_rows[1].T)
        vec1.pair_copy().start()
        drain_first()
        att1.step_near()

    def middle_second():
        up1.step_plane()
        down0.step_near()

    def late_second():
        att1.step_plane()
        send_sub(2, False)
        send_sub(1, False)

    def parting_second():
        down0.step_far()

    feed_phase(
        0,
        b.streams.at[2],
        b.xs.at[0],
        (early_second, middle_second, parting_second, late_second),
    )

    def before_second():
        up0.step_near()
        vec1.step_far()
        up1.step_pass()
        down0.step_plane()
        send_sub(3, True)

    def inside_second():
        up0.step_far()
        att1.step_pass()
        vec1.step_plane()
        down0.step_pass()
        @pl.when(section == 3)
        def _():
            for k in range(4):
                third_out(k).start()

        finish_logs()

    def during_second():
        att0.step_line()
        up0.step_plane()

    drain_second = attention_phase(
        0,
        b.streams.at[1],
        b.embeds.at[0],
        b.att.at[0],
        (before_second, inside_second, nothing, during_second),
    )
    vec0.store(b.vec_rows[0].T)
    vec0.pair_copy().start()
    send_sub(0, False)
    vec0.step_near()
    att0.step_line_plane()
    vec0.step_far()
    up0.step_pass()
    vec0.step_plane()
    drain_second()
    for matrix in (up1, down1, att1, vec1, down0, up0, vec0, att0):
        matrix.step_end()
    for number in range(3):
        drain_sub(number, False)

    @pl.when(section != 3)
    def _():
        for source in range(4):
            receive_sub(source, False)

    @pl.when(section == 3)
    def _():
        for k in range(4):
            third_out(k).wait()

    for number in range(4):
        drain_sub(number, True)
        receive_sub(number, True)
    for step in range(1, 8):
        small_copy(step).wait_send()
    for step in range(1, 4):
        first_z(step, chip).wait_send()
    block[0].cores(core).wait_send()
    block[1].drain()
    for layer in range(2):
        for line in feed_lines[layer]:
            line.drain()
        for k in range(1, 4):

            @pl.when(section == 3)
            def _():
                block_plane(layer, k).wait_send()

            @pl.when(peers[k] == 3)
            def _():
                block_across(layer, k, core).wait_send()


FINISH_IN = dict(all_m=0, all_v=0, sub_f=0, sub_g=0, log_total=0)
FINISH_OUT = dict(
    outputs=((1, 4, TOKENS, D), BF16, False),
    grads=((1, 4, TOKENS, D), BF16, False),
    qkv=((2, SHARD, 3 * D), F32, False),
    out=((2, SHARD, D), F32, False),
    up=((2, SHARD, FF), F32, False),
    down=((2, 4 * SHARD, D), F32, False),
    gains=((2, 3, SHARD), F32, True),
    biases=((2, 6, SHARD), F32, True),
    hgains=((2, 4 * SHARD), F32, True),
    hbiases=((2, 2, 4 * SHARD), F32, True),
    means=((2, 5), F32, True),
)
FINISH_SCRATCH = dict(
    matrix=((6, 4, SHARD, D), BF16),
    vectors=((2, 4, SHARD, PAIR_LANES), BF16),
    wide=((2, SHARD, 4 * D), F32),
    tall=((2, 4 * SHARD, D), F32),
    spread=((2, SHARD, FF), F32),
    first=((4, TOKENS, D), BF16),
    second=((4, TOKENS, D), BF16),
)
FINISH_SEMS = dict(load_sem=(9,), store_sem=(10,))


def finish_kernel(*refs):
    b = Named([FINISH_IN, FINISH_OUT, FINISH_SCRATCH, FINISH_SEMS], refs)
    loads = [
        pltpu.make_async_copy(b.all_m.at[i], b.matrix.at[i], b.load_sem.at[i]) for i in range(6)
    ] + [pltpu.make_async_copy(b.all_v, b.vectors, b.load_sem.at[6])]
    for copy in loads:
        copy.start()

    outputs_load = pltpu.make_async_copy(b.sub_f, b.first, b.load_sem.at[7])
    outputs_load.start()
    grads_load = pltpu.make_async_copy(b.sub_g, b.second, b.load_sem.at[8])
    grads_load.start()
    stores = []

    def store(source, target, number):
        copy = pltpu.make_async_copy(source, target, b.store_sem.at[number])
        copy.start()
        stores.append(copy)

    for layer in (1, 0):
        up_i = 3 * (1 - layer)
        loads[up_i].wait()
        for j in range(8):
            b.spread[layer, :, j * 4 * SHARD : (j + 1) * 4 * SHARD] = jnp.concatenate(
                [
                    b.matrix[up_i, source, :, j * SHARD : (j + 1) * SHARD].astype(F32)
                    for source in range(4)
                ],
                1,
            )
        store(b.spread.at[layer], b.up.at[layer], 4 * layer)
        loads[up_i + 1].wait()
        for source in range(4):
            b.tall[layer, source * SHARD : (source + 1) * SHARD, :] = b.matrix[
                up_i + 1, source
            ].astype(F32)
        store(b.tall.at[layer], b.down.at[layer], 4 * layer + 1)
        loads[up_i + 2].wait()
        for source in range(4):
            b.wide[layer, :, source * D : (source + 1) * D] = b.matrix[up_i + 2, source].astype(
                F32
            )
        store(b.wide.at[layer, :, pl.ds(0, 3 * D)], b.qkv.at[layer], 4 * layer + 2)
        store(b.wide.at[layer, :, pl.ds(3 * D, D)], b.out.at[layer], 4 * layer + 3)
    outputs_load.wait()
    store(b.first, b.outputs.at[0], 8)
    grads_load.wait()
    store(b.second, b.grads.at[0], 9)
    loads[6].wait()
    for layer in range(2):
        lines = []
        for source in range(4):
            tail = b.vectors[1 - layer, source].astype(F32)
            tail = jnp.concatenate([tail, jnp.zeros((PAIR_LANES - SHARD, PAIR_LANES), F32)], 0)
            lines.append(tail.T)
        model = lines[0] + lines[1] + lines[2] + lines[3]
        b.gains[layer] = model[0:3, 0:SHARD]
        b.biases[layer] = model[3:9, 0:SHARD]
        hidden = jnp.concatenate([each[9:12, 0:SHARD] for each in lines], 1)
        b.hgains[layer : layer + 1, :] = hidden[0:1, :]
        b.hbiases[layer] = hidden[1:3, :]
    lane = lax.broadcasted_iota(jnp.int32, (8, PAIR_LANES), 1)
    number = lax.shift_right_logical(lane, 2)
    sums = jnp.zeros((8, PAIR_LANES), F32)
    for i in range(5):
        part = jnp.sum(jnp.where(number == i, b.log_total[...], 0.0), -1, keepdims=True)
        sums = sums + jnp.where(lane == i, part, 0.0)
    means = sums[0:2, :] / jnp.where(lane[0:2, :] < 5, sums[2:3, :], 1.0)
    b.means[...] = means[:, 0:5]
    for copy in stores:
        copy.wait()


def run_remote(kernel, number, lengths, near, far, outs, scratch, sems):
    vmem = pl.BlockSpec(memory_space=pltpu.VMEM)
    anywhere = pl.BlockSpec(memory_space=pl.ANY)
    smem = pl.BlockSpec(memory_space=pltpu.SMEM)
    return pl.pallas_call(
        kernel,
        out_shape=[shaped(out[0], out[1]) for out in outs.values()],
        in_specs=[smem] * len(lengths) + [vmem] * len(near) + [anywhere] * len(far),
        out_specs=[vmem if out[2] else anywhere for out in outs.values()],
        scratch_shapes=[pltpu.VMEM(item[0], item[1]) for item in scratch.values()]
        + [pltpu.SemaphoreType.DMA(item) for item in sems.values()],
        compiler_params=pltpu.CompilerParams(
            collective_id=number, has_side_effects=True, vmem_limit_bytes=KERNEL_VMEM_BYTES
        ),
        cost_estimate=pl.CostEstimate(
            flops=10**10, bytes_accessed=100_000_000, transcendentals=0
        ),
    )(*lengths, *near, *far)


def run_finish(log_total, *far):
    vmem = pl.BlockSpec(memory_space=pltpu.VMEM)
    anywhere = pl.BlockSpec(memory_space=pl.ANY)
    return pl.pallas_call(
        finish_kernel,
        out_shape=[shaped(out[0], out[1]) for out in FINISH_OUT.values()],
        in_specs=[anywhere] * len(far) + [vmem],
        out_specs=[vmem if out[2] else anywhere for out in FINISH_OUT.values()],
        scratch_shapes=[pltpu.VMEM(item[0], item[1]) for item in FINISH_SCRATCH.values()]
        + [pltpu.SemaphoreType.DMA(item) for item in FINISH_SEMS.values()],
        compiler_params=pltpu.CompilerParams(vmem_limit_bytes=KERNEL_VMEM_BYTES),
    )(*far, log_total)


def quick_body(
    embeds,
    row_lengths,
    qkv_weight,
    out_weight,
    up_weight,
    down_weight,
    model_gains,
    model_biases,
    hidden_gains,
    hidden_biases,
    cotangent,
):
    both = Named(
        [BOTH_OUT],
        run_remote(
            both_kernel,
            10,
            (row_lengths,),
            (jnp.concatenate([model_gains, model_biases], 1), hidden_gains, hidden_biases),
            (embeds, qkv_weight, out_weight, up_weight, down_weight, cotangent),
            BOTH_OUT,
            BOTH_SCRATCH,
            BOTH_SEMS,
        ),
    )
    return tuple(
        run_finish(
            both.log_total,
            both.all_m_out,
            both.all_v_out,
            both.sub_f_out,
            both.sub_g_out,
        )
    )


def fits_quick(mesh):
    return mesh.shape["section"] == 4 and mesh.shape["seq"] == 8


def solution(mesh):
    return jax.shard_map(
        quick_body if fits_quick(mesh) else body,
        mesh=mesh,
        in_specs=(
            P(None, "seq", None),
            P(),
            P(None, "seq", None),
            P(None, "seq", None),
            P(None, "seq", None),
            P(None, "seq", None),
            P(None, None, "seq"),
            P(None, None, "seq"),
            P(None, "seq"),
            P(None, None, "seq"),
            P(None, "seq", None),
        ),
        out_specs=(
            P("section", None, "seq", None),
            P("section", None, "seq", None),
            P(None, "seq", None),
            P(None, "seq", None),
            P(None, "seq", None),
            P(None, "seq", None),
            P(None, None, "seq"),
            P(None, None, "seq"),
            P(None, "seq"),
            P(None, None, "seq"),
            P(),
        ),
        check_vma=False,
    )
```
